32 devices in a mesh: grp: 16 (over z, y, core), hd: 2 (over x).
Axes of the slice: x: 2, y: 2, z: 4, core: 2. Of those that a mesh axis runs over, the one named last changes fastest.
Arguments:
- tokens: bfloat16 [4096, 1536], P(('grp', 'hd')), may hold values from -6 to 6
- positions: int32 [4096], P('grp'), may hold values from -1 to 127, as said below
- attn_gain: float32 [1536], replicated, may hold values from 0.1 to 1.9
- w_query: bfloat16 [1536, 1536], P(None, 'hd'), may hold values from -0.15625 to 0.15625
- w_keyval: bfloat16 [1536, 8, 128], P(None, 'hd'), may hold values from -0.15625 to 0.15625
- w_out: bfloat16 [1536, 1536], P(None, 'grp'), may hold values from -0.15625 to 0.15625
- moe_gain: float32 [1536], replicated, may hold values from 0.1 to 1.9
- router: bfloat16 [1536, 40], replicated, may hold values from -0.15625 to 0.15625
- w_gate_up: bfloat16 [2, 1536, 1024], P('hd', 'grp'), may hold values from -0.15625 to 0.15625
- w_down: bfloat16 [2, 512, 1536], P('hd', 'grp'), may hold values from -0.25 to 0.25
- expert_ids: int32 [4096, 8], P(('grp', 'hd')), may hold values from 0 to 39, as said below
- cache_slot: int32 [4096], P('grp'), may hold values from -1 to 8191, as said below
- kv_cache: bfloat16 [8192, 8, 128], P('grp', 'hd'), may hold values from -6 to 6
Outputs:
- layer_out: bfloat16 [4096, 1536], P(('grp', 'hd'))
- cache_after: bfloat16 [8192, 8, 128], P('grp', 'hd')
The draws below stay inside these ranges and needn't reach their ends.
Inputs may be any that keep to these rules, and one draw needn't show every extreme that they name: Inside each segment the positions count up by one from 0 over consecutive tokens; a segment holds at most 128 tokens, and the one starting at token 0 holds exactly 128; padding tokens have -1. `expert_ids`: each row names 8 different experts. In each aligned block of 128 rows (the rows of one device) each expert below 2 is named by at most 32 rows, and some expert below 2 by exactly 32. A token has -1 exactly when its position is -1; other tokens have distinct slots. cache_slot // 512 is the slot's owner. The tokens of one aligned block of 256 tokens hold at most 32 slots of any one owner, and the first block holds exactly 32 slots of the last owner.
All inputs are finite; a program needn't handle non-finite values.
Results may differ from the reference program's by a relative error of at most 0.0095.
Values may be sent and summed in bfloat16 or wider, within the bound.
No kernel may reach another device: no remote copies, remote signals or barrier semaphores. Data moves between devices by JAX's collectives and lax.ppermute only.
A program may use at most 64 MiB of HBM per device.

```python
import jax
import jax.numpy as jnp
from jax import lax

D = 1536
H = 24
KV = 8
HEAD = 64
EXPERTS = 40
FFE = 512
TOPK = 8
TOK_DEV = 128
BLOCK = 256
TOKENS = 4096
SEG_MAX = 128
CAP = 32
LIVE = 2
CAPC = 32
SLOTS_DEV = 512
N_GRP = 16


def segment_layout(key):
    seg_count = TOKENS // 2 + 1
    lengths = jax.random.randint(jax.random.fold_in(key, 11), (seg_count,), 2, SEG_MAX + 1)
    lengths = lengths.at[0].set(SEG_MAX)
    padded = jax.random.randint(jax.random.fold_in(key, 12), (seg_count,), 0, 8) == 0
    padded = padded.at[0].set(False)
    seg_ends = jnp.cumsum(lengths)
    tok_index = jnp.arange(TOKENS, dtype=jnp.int32)
    seg_index = jnp.searchsorted(seg_ends, tok_index, side='right')
    seg_starts = seg_ends[seg_index] - lengths[seg_index]
    return jnp.where(padded[seg_index], -1, tok_index - seg_starts).astype(jnp.int32)


def draw_positions(key, part):
    return segment_layout(key)


def draw_cache_slot(key, part):
    positions = segment_layout(key)
    blocks_all = TOKENS // BLOCK
    halves = blocks_all // 2
    orders = jax.random.permutation(jax.random.fold_in(key, 21), jnp.broadcast_to(jnp.arange(BLOCK, dtype=jnp.int32), (blocks_all, BLOCK)), axis=1, independent=True)
    orders = orders.at[0].set((jnp.arange(BLOCK, dtype=jnp.int32) + BLOCK - CAPC) % BLOCK)
    offsets = jax.random.randint(jax.random.fold_in(key, 22), (blocks_all,), 0, halves + 1).at[0].set(halves)
    owners = orders // CAPC + offsets[:, None]
    within = jnp.arange(blocks_all, dtype=jnp.int32)[:, None] * CAPC + orders % CAPC
    shuffle = jax.random.permutation(jax.random.fold_in(key, 23), jnp.broadcast_to(jnp.arange(SLOTS_DEV, dtype=jnp.int32), (blocks_all, SLOTS_DEV)), axis=1, independent=True)
    last_row = shuffle[blocks_all - 1]
    where_top = jnp.argmax(last_row)
    last_row = last_row.at[where_top].set(last_row[0]).at[0].set(SLOTS_DEV - 1)
    shuffle = shuffle.at[blocks_all - 1].set(last_row)
    placed = shuffle[owners, within]
    slots_all = owners * SLOTS_DEV + placed
    return jnp.where(positions.reshape(blocks_all, BLOCK) >= 0, slots_all, -1).reshape(TOKENS).astype(jnp.int32)


def draw_expert_ids(key, part):
    blocks_all = TOKENS // TOK_DEV
    orders = jax.random.permutation(jax.random.fold_in(key, 31), jnp.broadcast_to(jnp.arange(TOK_DEV, dtype=jnp.int32), (blocks_all * LIVE, TOK_DEV)), axis=1, independent=True).reshape(blocks_all, LIVE, TOK_DEV)
    counts = jax.random.randint(jax.random.fold_in(key, 32), (blocks_all, LIVE), CAP // 8, CAP // 2 + 1)
    busiest = jax.random.randint(jax.random.fold_in(key, 33), (blocks_all,), 0, LIVE)
    counts = jnp.where(jnp.arange(LIVE)[None, :] == busiest[:, None], CAP, counts)
    picked = orders < counts[:, :, None]
    picked = jnp.transpose(picked, (0, 2, 1)).reshape(TOKENS, LIVE)
    jitter = jax.random.randint(jax.random.fold_in(key, 34), (TOKENS, EXPERTS), 0, 2 ** 15) * 64 + jnp.arange(EXPERTS, dtype=jnp.int32)[None, :]
    live_part = jnp.where(picked, jitter[:, :LIVE] + 2 ** 22, -1 - jnp.arange(LIVE, dtype=jnp.int32)[None, :])
    scores = jnp.concatenate([live_part, jitter[:, LIVE:]], axis=1).astype(jnp.int32)
    return lax.top_k(scores, TOPK)[1].astype(jnp.int32)


def block_levels(rng, dims, split, smallest, top_value):
    gain = 1.0
    for dim, shards_of in split:
        heights = jax.random.uniform(jax.random.fold_in(jax.random.fold_in(rng, 6), dim), (shards_of,), jnp.float32, smallest / len(split), top_value / len(split))
        gain = gain * jnp.repeat(jnp.exp(heights), dims[dim] // shards_of).reshape((-1,) + (1,) * (len(dims) - 1 - dim))
    return gain


def gaussian(stream_key, dims, spread, most, split=(), kind=jnp.bfloat16):
    level = block_levels(stream_key, dims, split, -0.22, 0.18) if split else 1.0
    drawn = jax.random.normal(stream_key, dims, jnp.float32) * spread * level
    return jnp.minimum(jnp.maximum(drawn, -most), most).astype(kind)


def setup_inputs(seed: int = 0) -> dict:
    arg_keys = jax.random.split(jax.random.key(seed), 14)
    return {
        "tokens": gaussian(arg_keys[0], (TOKENS, D), 1.0, 6.0, ((0, 32),)),
        "positions": draw_positions(jax.random.fold_in(arg_keys[13], 71), 0),
        "attn_gain": jnp.clip(1.0 + 0.18 * jax.random.normal(arg_keys[2], (D,), jnp.float32), 0.1, 1.9),
        "w_query": gaussian(arg_keys[3], (D, H * HEAD), D ** -0.5, 0.15625, ((1, 2),)),
        "w_keyval": gaussian(arg_keys[4], (D, KV, 2 * HEAD), D ** -0.5, 0.15625, ((1, 2),)),
        "w_out": gaussian(arg_keys[5], (H * HEAD, D), (H * HEAD) ** -0.5, 0.15625, ((1, 16),)),
        "moe_gain": jnp.clip(1.0 + 0.18 * jax.random.normal(arg_keys[6], (D,), jnp.float32), 0.1, 1.9),
        "router": gaussian(arg_keys[7], (D, EXPERTS), D ** -0.5, 0.15625),
        "w_gate_up": gaussian(arg_keys[8], (LIVE, D, 2 * FFE), D ** -0.5, 0.15625, ((0, 2), (1, 16))),
        "w_down": gaussian(arg_keys[9], (LIVE, FFE, D), FFE ** -0.5, 0.25, ((0, 2), (1, 16))),
        "expert_ids": draw_expert_ids(jax.random.fold_in(arg_keys[13], 71), 0),
        "cache_slot": draw_cache_slot(jax.random.fold_in(arg_keys[13], 71), 0),
        "kv_cache": gaussian(arg_keys[12], (N_GRP * SLOTS_DEV, KV, 2 * HEAD), 1.0, 6.0, ((0, 16), (1, 2))),
    }


norm_eps = 1e-05
rope_base = 10000.0

def rms_norm(row_set, norm_gain):
    floats = row_set.astype(jnp.float32)
    factor = lax.rsqrt(lax.optimization_barrier(jnp.mean(floats * floats, axis=-1, keepdims=True)) + norm_eps)
    return (floats * factor * norm_gain).astype(jnp.bfloat16)

def rotate(vectors, angle_pos):
    halves = vectors.shape[-1] // 2
    inverse_freq = rope_base ** (-2.0 * jnp.arange(halves, dtype=jnp.float32) / vectors.shape[-1])
    angles = angle_pos[:, None, None] * inverse_freq[None, None, :]
    cosine = jnp.cos(angles)
    sine_part = jnp.sin(angles)
    first_half = vectors[..., :halves]
    second_half = vectors[..., halves:]
    return jnp.concatenate([first_half * cosine - second_half * sine_part, second_half * cosine + first_half * sine_part], axis=-1)

def expert(row_set, gate_up, down_rows):
    gate_and_up = jnp.dot(row_set, gate_up, preferred_element_type=jnp.float32)
    inner_width = gate_and_up.shape[1] // 2
    hidden = (jax.nn.silu(gate_and_up[:, :inner_width]) * gate_and_up[:, inner_width:]).astype(jnp.bfloat16)
    return jnp.dot(hidden, down_rows, preferred_element_type=jnp.float32).astype(jnp.bfloat16)

def reference(tokens, positions, attn_gain, w_query, w_keyval, w_out, moe_gain, router, w_gate_up, w_down, expert_ids, cache_slot, kv_cache):
    normed = rms_norm(tokens, attn_gain)
    angle_pos = jnp.maximum(positions, 0).astype(jnp.float32)
    queries = rotate(jnp.dot(normed, w_query, preferred_element_type=jnp.float32).reshape(TOKENS, H, HEAD), angle_pos).astype(jnp.bfloat16)
    key_val = jnp.dot(normed, w_keyval.reshape(D, KV * 2 * HEAD), preferred_element_type=jnp.float32).reshape(TOKENS, KV, 2 * HEAD)
    keys_all = rotate(key_val[:, :, :HEAD], angle_pos).astype(jnp.bfloat16)
    values_all = key_val[:, :, HEAD:].astype(jnp.bfloat16)
    stored = jnp.concatenate([keys_all, values_all], axis=2)
    write_rows = jnp.where(cache_slot >= 0, cache_slot, kv_cache.shape[0]).astype(jnp.int32)
    cache_after = kv_cache.at[write_rows].set(stored, mode='drop')
    tok_index = jnp.arange(TOKENS, dtype=jnp.int32)
    lowest = tok_index - jnp.maximum(positions, 0)
    pad_keys = jnp.concatenate([jnp.zeros((SEG_MAX, KV, HEAD), keys_all.dtype), keys_all], axis=0)
    pad_vals = jnp.concatenate([jnp.zeros((SEG_MAX, KV, HEAD), values_all.dtype), values_all], axis=0)
    per_kv = H // KV
    scale_qk = HEAD ** (-0.5)

    def one_block(block_idx):
        first_row = (block_idx * SEG_MAX).astype(jnp.int32)
        query_blk = lax.dynamic_slice_in_dim(queries, first_row, SEG_MAX, 0).reshape(SEG_MAX, KV, per_kv, HEAD)
        keys_blk = lax.dynamic_slice_in_dim(pad_keys, first_row, 2 * SEG_MAX, 0)
        vals_blk = lax.dynamic_slice_in_dim(pad_vals, first_row, 2 * SEG_MAX, 0)
        low_here = lax.dynamic_slice_in_dim(lowest, first_row, SEG_MAX, 0)
        rows_here = first_row + jnp.arange(SEG_MAX, dtype=jnp.int32)
        cols_here = first_row - SEG_MAX + jnp.arange(2 * SEG_MAX, dtype=jnp.int32)
        visible = (cols_here[None, :] >= low_here[:, None]) & (cols_here[None, :] <= rows_here[:, None])
        scores = jnp.einsum('qkgd,skd->kgqs', query_blk.astype(jnp.float32), keys_blk.astype(jnp.float32)) * scale_qk
        weights_f = jnp.where(visible[None, None], jnp.exp(scores), 0.0)
        prob_bf = (weights_f / lax.optimization_barrier(jnp.sum(weights_f, axis=-1, keepdims=True))).astype(jnp.bfloat16)
        mixed_rows = jnp.einsum('kgqs,skd->qkgd', prob_bf.astype(jnp.float32), vals_blk.astype(jnp.float32))
        return mixed_rows.reshape(SEG_MAX, H * HEAD).astype(jnp.bfloat16)
    attended = lax.map(one_block, jnp.arange(TOKENS // SEG_MAX, dtype=jnp.int32)).reshape(TOKENS, H * HEAD)
    attn_proj = jnp.dot(attended, w_out, preferred_element_type=jnp.float32)
    residual = (tokens.astype(jnp.float32) + attn_proj).astype(jnp.bfloat16)
    moe_in = rms_norm(residual, moe_gain)
    logits = jnp.dot(moe_in, router, preferred_element_type=jnp.float32)
    chosen = jnp.take_along_axis(logits, expert_ids, axis=1)
    raised = jnp.exp(chosen)
    gates = raised / lax.optimization_barrier(jnp.sum(raised, axis=1, keepdims=True))
    row_bound = TOKENS // TOK_DEV * CAP
    moe_total = jnp.zeros((TOKENS, D), jnp.float32)
    for expert_idx in range(LIVE):
        match_here = expert_ids == expert_idx
        member = jnp.any(match_here, axis=1)
        weighting = lax.optimization_barrier(jnp.sum(jnp.where(match_here, gates, 0.0), axis=1))
        ranking = jnp.cumsum(member.astype(jnp.int32)) - 1
        target_rows = jnp.where(member, ranking, row_bound).astype(jnp.int32)
        packed = jnp.zeros((row_bound, D), moe_in.dtype).at[target_rows].set(moe_in, mode='drop')
        produced = expert(packed, w_gate_up[expert_idx], w_down[expert_idx])
        fetched = produced[jnp.minimum(target_rows, row_bound - 1)].astype(jnp.float32)
        moe_total = moe_total + jnp.where(member[:, None], weighting[:, None] * fetched, 0.0)
    layer_out = (residual.astype(jnp.float32) + moe_total).astype(jnp.bfloat16)
    return (layer_out, cache_after)
```

```python
import functools

import jax
import jax.numpy as jnp
import numpy as np
from jax import lax
from jax.experimental import pallas as pl
from jax.experimental.pallas import tpu as pltpu
from jax.sharding import PartitionSpec as P

norm_eps = 1e-05
rope_base = 10000.0
bf16 = jnp.bfloat16
f32 = jnp.float32
LAST_DIMS = (((1,), (1,)), ((), ()))


def ring_cycle(groups):
    rows = groups // 4
    return [2 * r for r in range(rows)] + [2 * r + 1 for r in reversed(range(rows))]


def ring_pairs(groups):
    cycle = ring_cycle(groups)
    count = len(cycle)
    pairs = []
    for place, pair in enumerate(cycle):
        pairs.append((2 * pair, 2 * cycle[(place + 1) % count]))
        pairs.append((2 * pair + 1, 2 * cycle[(place - 1) % count] + 1))
    return pairs


def sibling_pairs(groups):
    return [(g, g ^ 1) for g in range(groups)]


def ring_sources(groups):
    cycle = ring_cycle(groups)
    count = len(cycle)
    table = []
    for g in range(groups):
        core, place = g % 2, cycle.index(g // 2)

        def block(side, steps):
            pair = cycle[(place - steps if side == 0 else place + steps) % count]
            return [2 * pair + side, 2 * pair + 1 - side]

        full = (count - 1) // 2
        row = [g, g ^ 1]
        for steps in range(1, full + 1):
            row += block(core, steps)
        for steps in range(1, full + 1):
            row += block(1 - core, steps)
        row += [block(core, count // 2)[0], block(1 - core, count // 2)[0]]
        table.append(row)
    return np.array(table, np.int32)


def ring_gather(unit, groups):
    across = functools.partial(lax.ppermute, axis_name="grp", perm=ring_pairs(groups))
    beside = functools.partial(lax.ppermute, axis_name="grp", perm=sibling_pairs(groups))
    held = jnp.concatenate([unit, beside(unit)], axis=0)
    parts = [held]
    mine = []
    for _ in range((groups // 2 - 1) // 2):
        held = across(held)
        mine.append(held)
    last = across(held[: unit.shape[0]])
    return parts + mine + [beside(part) for part in mine] + [last, beside(last)]


def start_parts(meta, parts, unit_rows, pieces, sems):
    copies = []
    shard = 0
    for part in parts:
        for unit in range(part.shape[0] // unit_rows):
            source = meta[1 + shard]
            for first, rows, lanes, target, scale, offset, to_lane in pieces:
                at = pl.multiple_of(source * scale + offset, 16)
                copy = pltpu.make_async_copy(
                    part.at[pl.ds(unit * unit_rows + first, rows), lanes],
                    target.at[pl.ds(at, rows), to_lane],
                    sems.at[len(copies)],
                )
                copy.start()
                copies.append(copy)
            shard += 1
    return copies


def normalized(floats, gain):
    factor = lax.rsqrt(jnp.mean(floats * floats, axis=-1, keepdims=True) + norm_eps)
    return (floats * factor * gain).astype(bf16)


def project_kernel(
    meta, own, other, gain, cosine, sine, w_query, w_keyval, q_out, kv_out, rows, wq, wkv, sems
):
    width = 256
    steps = [(w_query, wq, q_out, c) for c in range(0, wq.shape[1], width)]
    steps += [(w_keyval, wkv, kv_out, c) for c in range(0, wkv.shape[1], width)]
    copies = []
    for index, (source, target, _, first) in enumerate(steps):
        lanes = pl.ds(first, width)
        copies.append(
            pltpu.make_async_copy(source.at[:, lanes], target.at[:, lanes], sems.at[index])
        )
        copies[-1].start()
    count = own.shape[0]
    mine = pl.multiple_of(meta[0] * count, count)
    theirs = pl.multiple_of((1 - meta[0]) * count, count)
    rows[pl.ds(mine, count), :] = normalized(own[...].astype(f32), gain[...])
    rows[pl.ds(theirs, count), :] = normalized(other[...].astype(f32), gain[...])
    cos_q, sin_q = cosine[...], sine[...]
    lane = lax.broadcasted_iota(jnp.int32, cos_q.shape, 1)
    lower = lane % 64 < 32
    cos_kv = jnp.where(lane < 64, cos_q, 1.0)
    sin_kv = jnp.where(lane < 64, sin_q, 0.0)
    for copy, (_, target, out, first) in zip(copies, steps):
        copy.wait()
        made = jnp.dot(rows[...], target[:, first : first + width], preferred_element_type=f32)
        cos, sin = (cos_q, sin_q) if out is q_out else (cos_kv, sin_kv)
        for part in range(0, width, 128):
            here = made[:, part : part + 128]
            turned = jnp.where(lower, pltpu.roll(here, 96, 1), pltpu.roll(here, 32, 1))
            out[:, first + part : first + part + 128] = (here * cos + turned * sin).astype(bf16)


def project(meta, own, other, gain, cosine, sine, w_query, flat_kv):
    block = 2 * own.shape[0]
    width = own.shape[1]
    vmem = pl.BlockSpec(memory_space=pltpu.VMEM)
    hbm = pl.BlockSpec(memory_space=pl.ANY)
    chunks = (w_query.shape[1] + flat_kv.shape[1]) // 256
    return pl.pallas_call(
        project_kernel,
        out_shape=(
            jax.ShapeDtypeStruct((block, w_query.shape[1]), bf16),
            jax.ShapeDtypeStruct((block, flat_kv.shape[1]), bf16),
        ),
        in_specs=[pl.BlockSpec(memory_space=pltpu.SMEM)] + [vmem] * 5 + [hbm] * 2,
        out_specs=(vmem, vmem),
        scratch_shapes=[
            pltpu.VMEM((block, width), bf16),
            pltpu.VMEM(w_query.shape, bf16),
            pltpu.VMEM(flat_kv.shape, bf16),
            pltpu.SemaphoreType.DMA((chunks,)),
        ],
        compiler_params=pltpu.CompilerParams(vmem_limit_bytes=32 << 20),
        cost_estimate=pl.CostEstimate(
            flops=2 * block * width * chunks * 256,
            bytes_accessed=2 * width * chunks * 256,
            transcendentals=0,
        ),
        name="project",
    )(meta, own, other, gain, cosine, sine, w_query, flat_kv)


def attend_kernel(flip, unit_rows, n_parts, meta, q, kv, seam, positions, *refs):
    parts, (out, window, mixed, w_out, sems) = refs[:n_parts], refs[n_parts:]
    count = seam.shape[0]
    all_lanes = pl.ds(0, w_out.shape[1])
    copies = start_parts(
        meta, parts, unit_rows, [(0, unit_rows, all_lanes, w_out, unit_rows, 0, all_lanes)], sems
    )
    which = (1 - meta[0]) if flip else meta[0]
    first = pl.multiple_of(which * count, count)

    @pl.when(which == 0)
    def _():
        window[:count, :] = seam[...]

    @pl.when(which != 0)
    def _():
        window[:count, :] = kv[:count, :]

    window[count:, :] = kv[pl.ds(first, count), :]
    row = lax.broadcasted_iota(jnp.int32, (count, 2 * count), 0) + count
    col = lax.broadcasted_iota(jnp.int32, (count, 2 * count), 1)
    past = jnp.maximum(positions[pl.ds(first, count), :], 0)
    visible = (col <= row) & (col >= row - past)
    head = 64
    kv_heads = kv.shape[1] // (2 * head)
    per_kv = q.shape[1] // head // kv_heads
    for kv_head in range(kv_heads):
        lanes = 2 * head * kv_head
        keys = window[:, lanes : lanes + head]
        values = window[:, lanes + head : lanes + 2 * head]
        for index in range(per_kv):
            at = (kv_head * per_kv + index) * head
            query = q[pl.ds(first, count), at : at + head]
            scores = lax.dot_general(query, keys, LAST_DIMS, preferred_element_type=f32)
            raised = jnp.where(visible, jnp.exp(scores * head ** (-0.5)), 0.0)
            probs = (raised / jnp.sum(raised, axis=-1, keepdims=True)).astype(bf16)
            made = jnp.dot(probs, values, preferred_element_type=f32)
            mixed[:, at : at + head] = made.astype(bf16)
    for copy in copies:
        copy.wait()
    out[...] = lax.dot_general(
        mixed[...], w_out[...], LAST_DIMS, preferred_element_type=f32
    ).astype(out.dtype)


def attend(flip, out_type, meta, q, kv, seam, positions, parts, unit):
    count = seam.shape[0]
    shards = sum(part.shape[0] for part in parts) // unit.shape[0]
    width = shards * unit.shape[0]
    vmem = pl.BlockSpec(memory_space=pltpu.VMEM)
    hbm = pl.BlockSpec(memory_space=pl.ANY)
    return pl.pallas_call(
        functools.partial(attend_kernel, flip, unit.shape[0], len(parts)),
        out_shape=jax.ShapeDtypeStruct((count, width), out_type),
        in_specs=[pl.BlockSpec(memory_space=pltpu.SMEM)] + [vmem] * 4 + [hbm] * len(parts),
        out_specs=vmem,
        scratch_shapes=[
            pltpu.VMEM((2 * count, kv.shape[1]), bf16),
            pltpu.VMEM((count, q.shape[1]), bf16),
            pltpu.VMEM((width, unit.shape[1]), bf16),
            pltpu.SemaphoreType.DMA((shards,)),
        ],
        compiler_params=pltpu.CompilerParams(vmem_limit_bytes=32 << 20),
        cost_estimate=pl.CostEstimate(
            flops=2 * count * width * unit.shape[1],
            bytes_accessed=2 * width * unit.shape[1],
            transcendentals=q.shape[1] // 64 * count * count * 2,
        ),
        name="attend_send" if flip else "attend_keep",
    )(meta, q, kv, seam, positions, *parts)


def route_kernel(tokens, mine, arrived, gain, router, named, place, residual, gates, rows):
    added = tokens[...].astype(f32) + (mine[...] + arrived[...].astype(f32))
    residual[...] = added.astype(bf16)
    moe_in = normalized(added.astype(bf16).astype(f32), gain[...])
    logits = jnp.dot(moe_in, router[...], preferred_element_type=f32)
    raised = jnp.where(named[...] > 0, jnp.exp(logits), 0.0)
    gates[...] = raised / jnp.sum(raised, axis=-1, keepdims=True)
    rows[...] = jnp.dot(place[...], moe_in, preferred_element_type=f32).astype(bf16)


def route(tokens, mine, arrived, gain, router, named, place):
    vmem = pl.BlockSpec(memory_space=pltpu.VMEM)
    return pl.pallas_call(
        route_kernel,
        out_shape=(
            jax.ShapeDtypeStruct(tokens.shape, bf16),
            jax.ShapeDtypeStruct(named.shape, f32),
            jax.ShapeDtypeStruct((place.shape[0], tokens.shape[1]), bf16),
        ),
        in_specs=[vmem] * 7,
        out_specs=(vmem,) * 3,
        compiler_params=pltpu.CompilerParams(vmem_limit_bytes=32 << 20),
        name="route",
    )(tokens, mine, arrived, gain, router, named, place)


def expert_kernel(unit_rows, up_rows, down_rows, n_parts, meta, own, other, *refs):
    parts = refs[:n_parts]
    own_out, other_out, rows, gate_up, down, sems = refs[n_parts:]
    width = gate_up.shape[1]
    rest = down.shape[1] - width
    half = down_rows // 2
    copies = start_parts(
        meta,
        parts,
        unit_rows,
        [
            (0, up_rows, pl.ds(0, width), gate_up, up_rows, 0, pl.ds(0, width)),
            (up_rows, down_rows, pl.ds(0, width), down, down_rows, 0, pl.ds(0, width)),
            (up_rows + down_rows, half, pl.ds(0, rest), down, down_rows, 0, pl.ds(width, rest)),
            (up_rows + down_rows, half, pl.ds(rest, rest), down, down_rows, half, pl.ds(width, rest)),
        ],
        sems,
    )
    count = own.shape[0]
    rows[:count, :] = own[...]
    rows[count:, :] = other[...]
    for copy in copies:
        copy.wait()
    both = jnp.dot(rows[...], gate_up[...], preferred_element_type=f32)
    gate, up = both[:, : width // 2], both[:, width // 2 :]
    hidden = (gate / (1.0 + jnp.exp(-gate)) * up).astype(bf16)
    made = jnp.dot(hidden, down[...], preferred_element_type=f32).astype(bf16)
    own_out[...] = made[:count, :]
    other_out[...] = made[count:, :]


def expert(meta, own, other, parts, unit, up_rows, down_rows):
    count, model = own.shape
    shards = sum(part.shape[0] for part in parts) // unit.shape[0]
    vmem = pl.BlockSpec(memory_space=pltpu.VMEM)
    hbm = pl.BlockSpec(memory_space=pl.ANY)
    return pl.pallas_call(
        functools.partial(expert_kernel, unit.shape[0], up_rows, down_rows, len(parts)),
        out_shape=(jax.ShapeDtypeStruct(own.shape, bf16),) * 2,
        in_specs=[pl.BlockSpec(memory_space=pltpu.SMEM)] + [vmem] * 2 + [hbm] * len(parts),
        out_specs=(vmem, vmem),
        scratch_shapes=[
            pltpu.VMEM((2 * count, model), bf16),
            pltpu.VMEM((shards * up_rows, unit.shape[1]), bf16),
            pltpu.VMEM((shards * down_rows, model), bf16),
            pltpu.SemaphoreType.DMA((4 * shards,)),
        ],
        compiler_params=pltpu.CompilerParams(vmem_limit_bytes=32 << 20),
        cost_estimate=pl.CostEstimate(
            flops=2 * 2 * count * unit.shape[1] * unit.shape[0] * shards,
            bytes_accessed=2 * unit.shape[1] * unit.shape[0] * shards,
            transcendentals=0,
        ),
        name="expert",
    )(meta, own, other, *parts)


def combine_kernel(meta, residual, gates, spread, own, returned, out):
    count = own.shape[0]
    lane = lax.broadcasted_iota(jnp.int32, gates.shape, 1)
    total = jnp.zeros(residual.shape, f32)
    for index, made in ((0, own), (1, returned)):
        live = meta[0] if index == 0 else 1 - meta[0]
        weight = jnp.sum(jnp.where(lane == live, gates[...], 0.0), axis=-1, keepdims=True)
        picked = jnp.dot(
            spread[:, index * count : (index + 1) * count], made[...], preferred_element_type=f32
        )
        total += weight * picked
    out[...] = (residual[...].astype(f32) + total).astype(bf16)


def combine(meta, residual, gates, spread, own, returned):
    vmem = pl.BlockSpec(memory_space=pltpu.VMEM)
    return pl.pallas_call(
        combine_kernel,
        out_shape=jax.ShapeDtypeStruct(residual.shape, bf16),
        in_specs=[pl.BlockSpec(memory_space=pltpu.SMEM)] + [vmem] * 5,
        out_specs=vmem,
        compiler_params=pltpu.CompilerParams(vmem_limit_bytes=32 << 20),
        name="combine",
    )(meta, residual, gates, spread, own, returned)


def two_lane_shards(
    tokens,
    positions,
    attn_gain,
    w_query,
    w_keyval,
    w_out,
    moe_gain,
    router,
    w_gate_up,
    w_down,
    expert_ids,
    cache_slot,
    kv_cache,
):
    groups = lax.axis_size("grp")
    lane = lax.axis_index("hd")
    tok_rows, model = tokens.shape
    block = positions.shape[0]
    seg_most = block // 2
    kv_local, head2 = w_keyval.shape[1:]
    kv_width = kv_local * head2
    q_width = w_query.shape[1]
    swap = functools.partial(lax.ppermute, axis_name="hd", perm=[(0, 1), (1, 0)])

    other_tokens = swap(tokens)

    out_rows = lax.dynamic_slice_in_dim(w_out, lane * q_width, q_width, 0)
    out_unit = out_rows.T
    up, down = w_gate_up[0], w_down[0]
    up_rows, up_width = up.shape
    down_rows = down.shape[0]
    half = down_rows // 2
    rest = down[:, up_width:]
    expert_unit = jnp.concatenate(
        [up, down[:, :up_width], jnp.concatenate([rest[:half], rest[half:]], axis=1)], axis=0
    )
    out_parts = ring_gather(out_unit, groups)
    expert_parts = ring_gather(expert_unit, groups)
    sources = jnp.asarray(ring_sources(groups))[lax.axis_index("grp")]
    meta = jnp.concatenate([lane[None].astype(jnp.int32), sources])

    angle_pos = jnp.maximum(positions, 0).astype(f32)
    quarter = head2 // 4
    inverse_freq = rope_base ** (-2.0 * jnp.arange(quarter, dtype=f32) / (2 * quarter))
    angles = angle_pos[:, None] * inverse_freq[None, :]
    cosine, sine = jnp.cos(angles), jnp.sin(angles)
    cosine = jnp.concatenate([cosine] * 4, axis=1)
    sine = jnp.concatenate([-sine, sine] * 2, axis=1)

    live_range = jnp.arange(2, dtype=jnp.int32)
    cap = tok_rows // 4
    named = jnp.any(
        expert_ids[:, :, None] == jnp.arange(router.shape[1], dtype=jnp.int32)[None, None, :], axis=1
    )
    token_range = jnp.arange(tok_rows, dtype=jnp.int32)
    earlier = (token_range[:, None] >= token_range[None, :]).astype(bf16)
    member = named[:, :2]
    ranking = jnp.dot(earlier, member.astype(bf16), preferred_element_type=f32).astype(jnp.int32) - 1
    in_order = (live_range != lane).astype(jnp.int32)
    target = jnp.where(member, in_order[None, :] * cap + ranking, -1)
    slot_range = jnp.arange(2 * cap, dtype=jnp.int32)
    place = jnp.any(target[None, :, :] == slot_range[:, None, None], axis=2).astype(bf16)
    spread = jnp.any(target[:, None, :] == slot_range[None, :, None], axis=2).astype(bf16)

    slots_dev = kv_cache.shape[0]
    capc = 2 * block // groups
    live_slot = cache_slot >= 0
    owners = jnp.where(live_slot, cache_slot // slots_dev, groups)
    owner_hit = (owners[:, None] == jnp.arange(groups, dtype=jnp.int32)[None, :]).astype(bf16)
    local_rows = jnp.arange(block, dtype=jnp.int32)
    lower_tri = (local_rows[:, None] >= local_rows[None, :]).astype(bf16)
    running = jnp.dot(lower_tri, owner_hit, preferred_element_type=f32)
    owner_rank = jnp.sum(running * owner_hit.astype(f32), axis=1).astype(jnp.int32) - 1
    send_rows = jnp.where(live_slot, owners * capc + owner_rank, -1)
    send_hit = send_rows[None, :] == jnp.arange(groups * capc, dtype=jnp.int32)[:, None]
    outgoing_slots = (
        jnp.sum(jnp.where(send_hit, (cache_slot % slots_dev + 1)[None, :], 0), axis=1) - 1
    )
    arrived_slots = lax.all_to_all(
        outgoing_slots.reshape(groups, capc), "grp", split_axis=0, concat_axis=0, tiled=True
    ).reshape(groups * capc)
    write_hit = arrived_slots[None, :] == jnp.arange(slots_dev, dtype=jnp.int32)[:, None]

    q, kv = project(
        meta,
        tokens,
        other_tokens,
        attn_gain[None],
        cosine,
        sine,
        w_query,
        w_keyval.reshape(model, kv_width),
    )
    seam = lax.ppermute(kv[block - seg_most :], "grp", [(g, g + 1) for g in range(groups - 1)])
    column = positions[:, None]
    sent = attend(True, bf16, meta, q, kv, seam, column, out_parts, out_unit)
    arrived = swap(sent)
    mine = attend(False, f32, meta, q, kv, seam, column, out_parts, out_unit)

    outgoing_cache = jnp.dot(
        send_hit.astype(bf16), kv, preferred_element_type=f32
    ).astype(bf16)
    arrived_cache = lax.all_to_all(
        outgoing_cache.reshape(groups, capc, kv_width), "grp", split_axis=0, concat_axis=0, tiled=True
    ).reshape(groups * capc, kv_width)
    written = jnp.dot(
        write_hit.astype(bf16), arrived_cache, preferred_element_type=f32
    ).astype(bf16)
    cache_after = jnp.where(
        jnp.any(write_hit, axis=1)[:, None, None], written.reshape(kv_cache.shape), kv_cache
    )

    residual, gates, rows = route(
        tokens, mine, arrived, moe_gain[None], router, named.astype(f32), place
    )
    landed = swap(rows[cap:])
    own_made, back = expert(
        meta, rows[:cap], landed, expert_parts, expert_unit, up_rows, down_rows
    )
    returned = swap(back)
    layer_out = combine(meta, residual, gates, spread, own_made, returned)
    return (layer_out, cache_after)


def passed_along(value, axis, steps):
    count = lax.axis_size(axis)
    initial, last = (max(0, -steps), min(count, count - steps))
    return lax.ppermute(value, axis, [(source, source + steps) for source in range(initial, last)])


def rms_norm(row_set, norm_gain):
    floats = row_set.astype(jnp.float32)
    factor = lax.rsqrt(jnp.mean(floats * floats, axis=-1, keepdims=True) + norm_eps)
    return (floats * factor * norm_gain).astype(jnp.bfloat16)


def rotate(vectors, angle_pos):
    halves = vectors.shape[-1] // 2
    inverse_freq = rope_base ** (-2.0 * jnp.arange(halves, dtype=jnp.float32) / vectors.shape[-1])
    angles = angle_pos[:, None, None] * inverse_freq[None, None, :]
    cosine = jnp.cos(angles)
    sine_part = jnp.sin(angles)
    first_half = vectors[..., :halves]
    second_half = vectors[..., halves:]
    return jnp.concatenate(
        [
            first_half * cosine - second_half * sine_part,
            second_half * cosine + first_half * sine_part,
        ],
        axis=-1,
    )


def expert_rows(row_set, gate_up, down_rows):
    gate_and_up = jnp.dot(row_set, gate_up, preferred_element_type=jnp.float32)
    inner_width = gate_and_up.shape[1] // 2
    hidden = (jax.nn.silu(gate_and_up[:, :inner_width]) * gate_and_up[:, inner_width:]).astype(
        jnp.bfloat16
    )
    return jnp.dot(hidden, down_rows, preferred_element_type=jnp.float32).astype(jnp.bfloat16)


def attend_rows(query_blk, keys_blk, vals_blk, visible, scale_qk):
    scores = (
        jnp.einsum("qkgd,skd->kgqs", query_blk, keys_blk, preferred_element_type=jnp.float32)
        * scale_qk
    )
    weights_f = jnp.where(visible[None, None], jnp.exp(scores), 0.0)
    prob_bf = (weights_f / jnp.sum(weights_f, axis=-1, keepdims=True)).astype(jnp.bfloat16)
    return jnp.einsum("kgqs,skd->qkgd", prob_bf, vals_blk, preferred_element_type=jnp.float32)


def shards(
    tokens,
    positions,
    attn_gain,
    w_query,
    w_keyval,
    w_out,
    moe_gain,
    router,
    w_gate_up,
    w_down,
    expert_ids,
    cache_slot,
    kv_cache,
):
    lane_count = lax.axis_size("hd")
    group_count = lax.axis_size("grp")
    tok_rows = tokens.shape[0]
    model_width = tokens.shape[1]
    block_len = positions.shape[0]
    seg_most = block_len // 2
    head_dim = w_keyval.shape[2] // 2
    kv_local = w_keyval.shape[1]
    q_local = w_query.shape[1] // head_dim
    per_kv = q_local // kv_local
    expert_cap = tok_rows // 4
    normed = rms_norm(tokens, attn_gain)
    flat_kv = w_keyval.reshape(model_width, kv_local * 2 * head_dim)
    section = lax.all_gather(normed, "hd", axis=0, tiled=True)
    projected = jnp.concatenate(
        [
            jnp.dot(section, w_query, preferred_element_type=jnp.float32),
            jnp.dot(section, flat_kv, preferred_element_type=jnp.float32),
        ],
        axis=1,
    )
    angle_pos = jnp.maximum(positions, 0).astype(jnp.float32)
    queries = rotate(
        projected[:, : q_local * head_dim].reshape(block_len, q_local, head_dim), angle_pos
    ).astype(jnp.bfloat16)
    key_val = projected[:, q_local * head_dim :].reshape(block_len, kv_local, 2 * head_dim)
    rotated = rotate(key_val[:, :, :head_dim], angle_pos).astype(jnp.bfloat16)
    stored = jnp.concatenate([rotated, key_val[:, :, head_dim:].astype(jnp.bfloat16)], axis=2)
    seam_rows = passed_along(stored[block_len - seg_most :], "grp", 1)
    window = jnp.concatenate([seam_rows, stored], axis=0)
    scale_qk = head_dim ** (-0.5)
    local_rows = jnp.arange(block_len, dtype=jnp.int32)
    lowest = local_rows - jnp.maximum(positions, 0)
    pieces_out = []
    for q_block in range(2):
        first_row = q_block * seg_most
        rows_here = first_row + jnp.arange(seg_most, dtype=jnp.int32)
        cols_here = first_row - seg_most + jnp.arange(2 * seg_most, dtype=jnp.int32)
        low_here = lowest[first_row : first_row + seg_most]
        visible = (cols_here[None, :] >= low_here[:, None]) & (
            cols_here[None, :] <= rows_here[:, None]
        )
        query_blk = queries[first_row : first_row + seg_most].reshape(
            seg_most, kv_local, per_kv, head_dim
        )
        keys_blk = window[first_row : first_row + 2 * seg_most, :, :head_dim]
        vals_blk = window[first_row : first_row + 2 * seg_most, :, head_dim:]
        mixed_rows = attend_rows(query_blk, keys_blk, vals_blk, visible, scale_qk)
        pieces_out.append(mixed_rows.reshape(seg_most, q_local * head_dim).astype(jnp.bfloat16))
    attended = jnp.concatenate(pieces_out, axis=0)
    slots_dev = kv_cache.shape[0]
    capc = 2 * block_len // group_count
    live_slot = cache_slot >= 0
    owners = jnp.where(live_slot, cache_slot // slots_dev, group_count)
    owner_hit = (owners[:, None] == jnp.arange(group_count, dtype=jnp.int32)[None, :]).astype(
        jnp.bfloat16
    )
    lower_tri = (local_rows[:, None] >= local_rows[None, :]).astype(jnp.bfloat16)
    running = jnp.dot(lower_tri, owner_hit, preferred_element_type=jnp.float32)
    owner_rank = jnp.sum(running * owner_hit.astype(jnp.float32), axis=1).astype(jnp.int32) - 1
    send_rows = jnp.where(live_slot, owners * capc + owner_rank, group_count * capc)
    outgoing_cache = (
        jnp.zeros((group_count * capc, kv_local, 2 * head_dim), jnp.bfloat16)
        .at[send_rows]
        .set(stored, mode="drop")
    )
    outgoing_slots = (
        jnp.full((group_count * capc,), -1, jnp.int32)
        .at[send_rows]
        .set(cache_slot % slots_dev, mode="drop")
    )
    arrived, arrived_slots = (
        lax.all_to_all(
            outgoing_cache.reshape(group_count, capc, kv_local, 2 * head_dim),
            "grp",
            split_axis=0,
            concat_axis=0,
            tiled=True,
        ),
        lax.all_to_all(
            outgoing_slots.reshape(group_count, capc),
            "grp",
            split_axis=0,
            concat_axis=0,
            tiled=True,
        ),
    )
    flat_slots = arrived_slots.reshape(group_count * capc)
    write_rows = jnp.where(flat_slots >= 0, flat_slots, slots_dev).astype(jnp.int32)
    cache_after = kv_cache.at[write_rows].set(
        arrived.reshape(group_count * capc, kv_local, 2 * head_dim), mode="drop"
    )
    by_token = lax.all_to_all(attended, "hd", split_axis=0, concat_axis=1, tiled=True)
    attn_proj = jnp.dot(
        by_token,
        lax.all_gather(w_out, "grp", axis=1, tiled=True),
        preferred_element_type=jnp.float32,
    )
    residual = (tokens.astype(jnp.float32) + attn_proj).astype(jnp.bfloat16)
    moe_in = rms_norm(residual, moe_gain)
    logits = jnp.dot(moe_in, router, preferred_element_type=jnp.float32)
    expert_range = jnp.arange(router.shape[1], dtype=jnp.int32)
    matches_all = expert_ids[:, :, None] == expert_range[None, None, :]
    chosen = jnp.sum(jnp.where(matches_all, logits[:, None, :], 0.0), axis=2)
    raised = jnp.exp(chosen)
    gates = raised / jnp.sum(raised, axis=1, keepdims=True)
    live_range = jnp.arange(lane_count, dtype=jnp.int32)
    matches = expert_ids[:, :, None] == live_range[None, None, :]
    member = jnp.any(matches, axis=1)
    weighting = jnp.sum(jnp.where(matches, gates[:, :, None], 0.0), axis=1)
    ranking = jnp.cumsum(member.astype(jnp.int32), axis=0) - 1
    target = jnp.where(member, live_range[None, :] * expert_cap + ranking, -1)
    slot_range = jnp.arange(lane_count * expert_cap, dtype=jnp.int32)
    slot_hits = target[None, :, :] == slot_range[:, None, None]
    placing = jnp.any(slot_hits, axis=2).astype(jnp.bfloat16)
    outgoing = (
        jnp.dot(placing, moe_in, preferred_element_type=jnp.float32)
        .astype(jnp.bfloat16)
        .reshape(lane_count, expert_cap, model_width)
    )
    gate_up_all, down_all = (
        lax.all_gather(w_gate_up, "grp", axis=1, tiled=True),
        lax.all_gather(w_down, "grp", axis=1, tiled=True),
    )
    gate_up_mat = gate_up_all[0]
    down_mat = down_all[0]
    landed = lax.all_to_all(outgoing, "hd", split_axis=0, concat_axis=0, tiled=True)
    results = expert_rows(landed.reshape(-1, model_width), gate_up_mat, down_mat).reshape(landed.shape)
    returned = lax.all_to_all(results, "hd", split_axis=0, concat_axis=0, tiled=True)
    flat_returned = returned.reshape(-1, model_width)
    fetched = flat_returned[jnp.maximum(target, 0)]
    used_weight = jnp.where(member, weighting, 0.0)
    moe_total = jnp.sum(used_weight[:, :, None] * fetched.astype(jnp.float32), axis=1)
    layer_out = (residual.astype(jnp.float32) + moe_total).astype(jnp.bfloat16)
    return (layer_out, cache_after)


def solution(mesh):
    two_lanes = mesh.shape["hd"] == 2 and mesh.shape["grp"] % 8 == 0
    return jax.shard_map(
        two_lane_shards if two_lanes else shards,
        mesh=mesh,
        in_specs=(
            P(("grp", "hd"), None),
            P("grp"),
            P(),
            P(None, "hd"),
            P(None, "hd", None),
            P(None, "grp"),
            P(),
            P(),
            P("hd", "grp", None),
            P("hd", "grp", None),
            P(("grp", "hd"), None),
            P("grp"),
            P("grp", "hd", None),
        ),
        out_specs=(P(("grp", "hd"), None), P("grp", "hd", None)),
        check_vma=False,
    )
```

```python
import functools

import jax
import jax.numpy as jnp
import numpy as np
from jax import lax
from jax.experimental import pallas as pl
from jax.experimental.pallas import tpu as pltpu
from jax.sharding import PartitionSpec as P

norm_eps = 1e-05
rope_base = 10000.0
bf16 = jnp.bfloat16
f32 = jnp.float32
LAST_DIMS = (((1,), (1,)), ((), ()))


def ring_cycle(groups):
    rows = groups // 4
    return [2 * r for r in range(rows)] + [2 * r + 1 for r in reversed(range(rows))]


def ring_pairs(groups):
    cycle = ring_cycle(groups)
    count = len(cycle)
    pairs = []
    for place, pair in enumerate(cycle):
        pairs.append((2 * pair, 2 * cycle[(place + 1) % count]))
        pairs.append((2 * pair + 1, 2 * cycle[(place - 1) % count] + 1))
    return pairs


def sibling_pairs(groups):
    return [(g, g ^ 1) for g in range(groups)]


def ring_sources(groups, me):
    count = groups // 2
    rows = count // 2
    side, pair = me % 2, me // 2
    row, col = pair // 2, pair % 2
    place = jnp.where(col == 0, row, count - 1 - row)

    def block(core, steps):
        there = (place + (2 * core - 1) * steps + count) % count
        other = jnp.where(there < rows, 2 * there, 2 * (count - 1 - there) + 1)
        return [2 * other + core, 2 * other + 1 - core]

    full = (count - 1) // 2
    listed = [me, me + 1 - 2 * side]
    for core in (side, 1 - side):
        for steps in range(1, full + 1):
            listed += block(core, steps)
    return listed + [block(side, count // 2)[0], block(1 - side, count // 2)[0]]


def ring_gather(unit, groups):
    across = functools.partial(lax.ppermute, axis_name="grp", perm=ring_pairs(groups))
    beside = functools.partial(lax.ppermute, axis_name="grp", perm=sibling_pairs(groups))
    held = jnp.concatenate([unit, beside(unit)], axis=0)
    parts = [held]
    mine = []
    for _ in range((groups // 2 - 1) // 2):
        held = across(held)
        mine.append(held)
    last = across(held[: unit.shape[0]])
    return parts + mine + [beside(part) for part in mine] + [last, beside(last)]


def start_parts(groups, parts, unit_rows, pieces, sems):
    sources = ring_sources(groups, lax.axis_index("grp"))
    copies = []
    shard = 0
    for part in parts:
        for unit in range(part.shape[0] // unit_rows):
            for first, rows, lanes, target, scale, offset, to_lane in pieces:
                at = pl.multiple_of(sources[shard] * scale + offset, 16)
                copy = pltpu.make_async_copy(
                    part.at[pl.ds(unit * unit_rows + first, rows), lanes],
                    target.at[pl.ds(at, rows), to_lane],
                    sems.at[len(copies)],
                )
                copy.start()
                copies.append(copy)
            shard += 1
    return copies


VMEM = pl.BlockSpec(memory_space=pltpu.VMEM)
ANY = pl.BlockSpec(memory_space=pl.ANY)
PARAMS = pltpu.CompilerParams(vmem_limit_bytes=40 << 20)


def cost(flops, nbytes):
    return pl.CostEstimate(flops=flops, bytes_accessed=nbytes, transcendentals=0)


def normalized(floats, gain):
    factor = lax.rsqrt(jnp.mean(floats * floats, axis=-1, keepdims=True) + norm_eps)
    return (floats * factor * gain).astype(bf16)


def fetch(pairs, sems):
    copies = []
    for index, (source, target) in enumerate(pairs):
        copies.append(pltpu.make_async_copy(source, target, sems.at[index]))
        copies[-1].start()
    return copies


def pack_kernel(up, down, w_out, expert_unit, out_unit, sems):
    width = up.shape[1]
    rest = down.shape[1] - width
    up_rows, down_rows = up.shape[0], down.shape[0]
    half = down_rows // 2
    lane = lax.axis_index("hd")
    first = pl.multiple_of(lane * out_unit.shape[1], out_unit.shape[1])
    tail = up_rows + down_rows
    copies = fetch(
        [
            (w_out.at[:, pl.ds(first, out_unit.shape[1])], out_unit),
            (up, expert_unit.at[pl.ds(0, up_rows), :]),
            (down.at[:, pl.ds(0, width)], expert_unit.at[pl.ds(up_rows, down_rows), :]),
            (down.at[pl.ds(0, half), pl.ds(width, rest)], expert_unit.at[pl.ds(tail, half), pl.ds(0, rest)]),
            (
                down.at[pl.ds(half, half), pl.ds(width, rest)],
                expert_unit.at[pl.ds(tail, half), pl.ds(rest, rest)],
            ),
        ],
        sems,
    )
    for copy in copies:
        copy.wait()


def pack(up, down, w_out_t):
    unit = (up.shape[0] + down.shape[0] + down.shape[0] // 2, up.shape[1])
    return pl.pallas_call(
        pack_kernel,
        out_shape=(
            jax.ShapeDtypeStruct(unit, bf16),
            jax.ShapeDtypeStruct((w_out_t.shape[0], w_out_t.shape[1] // 2), bf16),
        ),
        in_specs=[ANY] * 3,
        out_specs=(ANY, ANY),
        scratch_shapes=[pltpu.SemaphoreType.DMA((5,))],
        compiler_params=PARAMS,
        cost_estimate=cost(0, 4 * unit[0] * unit[1]),
        name="pack",
    )(up, down, w_out_t)


def as_column(row, eye):
    return jnp.sum(jnp.where(eye, row, 0.0), axis=1, keepdims=True)


def prepare_kernel(
    groups, slots_dev, positions, slots, ids, cosine, sine, past, named, place, spread, send, tags
):
    lane = lax.axis_index("hd")
    block = positions.shape[1]

    def iota(shape, dim):
        return lax.broadcasted_iota(jnp.int32, shape, dim)

    eye = iota((block, block), 0) == iota((block, block), 1)
    reach = as_column(jnp.maximum(positions[...], 0).astype(f32), eye)
    past[...] = jnp.broadcast_to(reach, past.shape)
    column = iota((8, 128), 1)
    exponent = (column % 32).astype(f32) * (-2.0 / 64)
    inverse_freq = jnp.exp(exponent * np.float32(np.log(rope_base)))[:1, :]
    angles = reach * inverse_freq
    cosine[...] = jnp.cos(angles)
    turned = jnp.sin(angles)
    sine[...] = jnp.where(iota(angles.shape, 1) % 64 < 32, -turned, turned)

    tokens = ids.shape[1]
    experts = named.shape[1]
    cap = place.shape[0] // 2
    expert = iota((experts, tokens), 0)
    hit = jnp.zeros((experts, tokens), f32)
    for index in range(ids.shape[0]):
        hit = jnp.where(ids[index : index + 1, :] == expert, 1.0, hit)
    small_eye = (iota((tokens, tokens), 0) == iota((tokens, tokens), 1)).astype(f32)
    named[...] = lax.dot_general(small_eye, hit, LAST_DIMS, preferred_element_type=f32)
    upto = (iota((tokens, tokens), 0) <= iota((tokens, tokens), 1)).astype(f32)
    rank = jnp.dot(hit[:8, :], upto, preferred_element_type=f32) - 1.0
    slot = iota((2 * cap, tokens), 0).astype(f32)
    placed = jnp.zeros((2 * cap, tokens), f32)
    for live in range(2):
        order = jnp.where(lane == live, 0, cap).astype(f32)
        member = hit[live : live + 1, :] > 0.0
        placed = jnp.where(member & (slot == rank[live : live + 1, :] + order), 1.0, placed)
    place[...] = placed.astype(bf16)
    spread[...] = lax.dot_general(small_eye, placed, LAST_DIMS, preferred_element_type=f32).astype(bf16)

    where = slots[...]
    owner = jnp.where(where >= 0, where // slots_dev, -1)
    owner_hit = (iota((groups, block), 0) == owner).astype(f32)
    before = (iota((block, block), 0) <= iota((block, block), 1)).astype(f32)
    running = jnp.dot(owner_hit, before, preferred_element_type=f32)
    owner_rank = jnp.sum(owner_hit * running, axis=0, keepdims=True) - 1.0
    capc = send.shape[0] // groups
    row = jnp.where(owner >= 0, owner * capc + owner_rank.astype(jnp.int32), -1)
    send[...] = (iota(send.shape, 0) == row).astype(bf16)
    inside = jnp.where(where >= 0, where % slots_dev, 0)
    high = as_column((inside // 64 + 1).astype(f32), eye)
    low = as_column((inside % 64).astype(f32), eye)
    spot = iota(tags.shape, 1)
    tags[...] = jnp.where(spot == 0, high, jnp.where(spot == 1, low, 0.0)).astype(bf16)


def prepare(groups, slots_dev, positions, slots, ids, experts):
    block, tokens = positions.shape[0], ids.shape[0]
    cap = tokens // 4
    capc = 2 * block // groups
    shapes = [
        ((block, 128), f32),
        ((block, 128), f32),
        ((block, 128), f32),
        ((tokens, experts), f32),
        ((2 * cap, tokens), bf16),
        ((tokens, 2 * cap), bf16),
        ((groups * capc, block), bf16),
        ((block, 128), bf16),
    ]
    return pl.pallas_call(
        functools.partial(prepare_kernel, groups, slots_dev),
        out_shape=tuple(jax.ShapeDtypeStruct(shape, kind) for shape, kind in shapes),
        in_specs=[VMEM] * 3,
        out_specs=(VMEM,) * len(shapes),
        compiler_params=PARAMS,
        cost_estimate=cost(0, 1 << 20),
        name="prepare",
    )(positions[None], slots[None], ids.T)


def project_kernel(
    own, other, gain, cosine, sine, w_query, w_keyval, q_out, kv_out, seam_out, raw, rows, sems
):
    count = own.shape[0]
    lane = lax.axis_index("hd")
    mine = pl.multiple_of(lane * count, count)
    theirs = pl.multiple_of((1 - lane) * count, count)
    copies = fetch([(own, raw.at[0]), (other, raw.at[1])], sems)
    cos_q, sin_q = cosine[...], sine[...]
    column = lax.broadcasted_iota(jnp.int32, cos_q.shape, 1)
    lower = column % 64 < 32
    cos_kv = jnp.where(column < 64, cos_q, 1.0)
    sin_kv = jnp.where(column < 64, sin_q, 0.0)
    for index, first in ((0, mine), (1, theirs)):
        copies[index].wait()
        rows[pl.ds(first, count), :] = normalized(raw[index].astype(f32), gain[...])
    width = 256
    for weights, out, cos, sin in ((w_keyval, kv_out, cos_kv, sin_kv), (w_query, q_out, cos_q, sin_q)):
        for first in range(0, weights.shape[1], width):
            made = jnp.dot(rows[...], weights[:, first : first + width], preferred_element_type=f32)
            for part in range(0, width, 128):
                here = made[:, part : part + 128]
                turned = jnp.where(lower, pltpu.roll(here, 96, 1), pltpu.roll(here, 32, 1))
                done = (here * cos + turned * sin).astype(bf16)
                out[:, first + part : first + part + 128] = done
                if out is kv_out:
                    seam_out[:, first + part : first + part + 128] = done[count:, :]


def project(own, other, gain, cosine, sine, w_query, flat_kv):
    count, width = own.shape
    made = w_query.shape[1] + flat_kv.shape[1]
    return pl.pallas_call(
        project_kernel,
        out_shape=(
            jax.ShapeDtypeStruct((2 * count, w_query.shape[1]), bf16),
            jax.ShapeDtypeStruct((2 * count, flat_kv.shape[1]), bf16),
            jax.ShapeDtypeStruct((count, flat_kv.shape[1]), bf16),
        ),
        in_specs=[ANY] * 2 + [VMEM] * 5,
        out_specs=(VMEM, VMEM, VMEM),
        scratch_shapes=[
            pltpu.VMEM((2, count, width), bf16),
            pltpu.VMEM((2 * count, width), bf16),
            pltpu.SemaphoreType.DMA((2,)),
        ],
        compiler_params=PARAMS,
        cost_estimate=cost(4 * count * width * made, 2 * width * made),
        name="project",
    )(own, other, gain, cosine, sine, w_query, flat_kv)


def attend_kernel(flip, groups, unit_rows, n_parts, q, kv, seam, past, *refs):
    parts, (out, window, mixed, w_out, sems, seam_sem) = refs[:n_parts], refs[n_parts:]
    count = seam.shape[0]
    all_lanes = pl.ds(0, w_out.shape[1])
    copies = start_parts(
        groups, parts, unit_rows, [(0, unit_rows, all_lanes, w_out, unit_rows, 0, all_lanes)], sems
    )
    lane = lax.axis_index("hd")
    which = (1 - lane) if flip else lane
    first = pl.multiple_of(which * count, count)

    @pl.when(which == 0)
    def _():
        copy = pltpu.make_async_copy(seam, window.at[pl.ds(0, count), :], seam_sem)
        copy.start()
        copy.wait()

    @pl.when(which != 0)
    def _():
        window[:count, :] = kv[:count, :]

    window[count:, :] = kv[pl.ds(first, count), :]
    head = 64
    kv_heads = kv.shape[1] // (2 * head)
    per_kv = q.shape[1] // head // kv_heads
    shape = (per_kv * count, 2 * count)
    row = lax.broadcasted_iota(jnp.int32, shape, 0) % count + count
    col = lax.broadcasted_iota(jnp.int32, shape, 1)
    reach = past[pl.ds(first, count), :][:, :1].astype(jnp.int32)
    reach = jnp.concatenate([reach] * per_kv, axis=0)
    visible = (col <= row) & (col >= row - reach)
    for kv_head in range(kv_heads):
        lanes = 2 * head * kv_head
        keys = window[:, lanes : lanes + head]
        values = window[:, lanes + head : lanes + 2 * head]
        at = kv_head * per_kv * head
        query = jnp.concatenate(
            [q[pl.ds(first, count), at + i * head : at + (i + 1) * head] for i in range(per_kv)], axis=0
        )
        scores = lax.dot_general(query, keys, LAST_DIMS, preferred_element_type=f32)
        raised = jnp.where(visible, jnp.exp(scores * head ** (-0.5)), 0.0)
        probs = (raised / jnp.sum(raised, axis=-1, keepdims=True)).astype(bf16)
        made = jnp.dot(probs, values, preferred_element_type=f32).astype(bf16)
        for i in range(per_kv):
            mixed[:, at + i * head : at + (i + 1) * head] = made[i * count : (i + 1) * count, :]
    for copy in copies:
        copy.wait()
    out[...] = lax.dot_general(
        mixed[...], w_out[...], LAST_DIMS, preferred_element_type=f32
    ).astype(out.dtype)


def attend(flip, out_type, groups, q, kv, seam, past, parts, unit):
    count = seam.shape[0]
    width = groups * unit.shape[0]
    return pl.pallas_call(
        functools.partial(attend_kernel, flip, groups, unit.shape[0], len(parts)),
        out_shape=jax.ShapeDtypeStruct((count, width), out_type),
        in_specs=[VMEM, VMEM, ANY, VMEM] + [ANY] * len(parts),
        out_specs=VMEM,
        scratch_shapes=[
            pltpu.VMEM((2 * count, kv.shape[1]), bf16),
            pltpu.VMEM((count, q.shape[1]), bf16),
            pltpu.VMEM((width, unit.shape[1]), bf16),
            pltpu.SemaphoreType.DMA((groups,)),
            pltpu.SemaphoreType.DMA,
        ],
        compiler_params=PARAMS,
        cost_estimate=cost(2 * count * width * unit.shape[1], 2 * width * unit.shape[1]),
        name="attend_send" if flip else "attend_keep",
    )(q, kv, seam, past, *parts)


def route_kernel(tokens, mine, arrived, gain, router, named, place, residual, gates, own, sent, got, sems):
    copies = fetch([(arrived, got)], sems)
    copies[0].wait()
    added = tokens[...].astype(f32) + (mine[...] + got[...].astype(f32))
    residual[...] = added.astype(bf16)
    moe_in = normalized(added.astype(bf16).astype(f32), gain[...])
    rows = jnp.dot(place[...], moe_in, preferred_element_type=f32).astype(bf16)
    cap = own.shape[0]
    own[...] = rows[:cap, :]
    sent[...] = rows[cap:, :]
    logits = lax.dot_general(moe_in, router[...], LAST_DIMS, preferred_element_type=f32)
    raised = jnp.where(named[...] > 0, jnp.exp(logits), 0.0)
    gates[...] = raised / jnp.sum(raised, axis=-1, keepdims=True)


def route(tokens, mine, arrived, gain, router_t, named, place):
    cap = place.shape[0] // 2
    return pl.pallas_call(
        route_kernel,
        out_shape=(
            jax.ShapeDtypeStruct(tokens.shape, bf16),
            jax.ShapeDtypeStruct(named.shape, f32),
            jax.ShapeDtypeStruct((cap, tokens.shape[1]), bf16),
            jax.ShapeDtypeStruct((cap, tokens.shape[1]), bf16),
        ),
        in_specs=[VMEM, VMEM, ANY] + [VMEM] * 4,
        out_specs=(VMEM,) * 4,
        scratch_shapes=[pltpu.VMEM(tokens.shape, bf16), pltpu.SemaphoreType.DMA((1,))],
        compiler_params=PARAMS,
        cost_estimate=cost(0, 2 << 20),
        name="route",
    )(tokens, mine, arrived, gain, router_t, named, place)


def expert_kernel(groups, unit_rows, up_rows, down_rows, n_parts, own, other, *refs):
    parts = refs[:n_parts]
    own_out, other_out, rows, gate_up, down, sems, row_sems = refs[n_parts:]
    width = gate_up.shape[1]
    rest = down.shape[1] - width
    half = down_rows // 2
    count = own.shape[0]
    arriving = fetch(
        [(own, rows.at[pl.ds(0, count), :]), (other, rows.at[pl.ds(count, count), :])], row_sems
    )
    copies = start_parts(
        groups,
        parts,
        unit_rows,
        [(0, up_rows, pl.ds(0, width), gate_up, up_rows, 0, pl.ds(0, width))],
        sems.at[0],
    )
    tail = up_rows + down_rows
    later = start_parts(
        groups,
        parts,
        unit_rows,
        [
            (up_rows, down_rows, pl.ds(0, width), down, down_rows, 0, pl.ds(0, width)),
            (tail, half, pl.ds(0, rest), down, down_rows, 0, pl.ds(width, rest)),
            (tail, half, pl.ds(rest, rest), down, down_rows, half, pl.ds(width, rest)),
        ],
        sems.at[1],
    )
    for copy in arriving + copies:
        copy.wait()
    both = jnp.dot(rows[...], gate_up[...], preferred_element_type=f32)
    gate, up = both[:, : width // 2], both[:, width // 2 :]
    hidden = (gate / (1.0 + jnp.exp(-gate)) * up).astype(bf16)
    for copy in later:
        copy.wait()
    made = jnp.dot(hidden, down[...], preferred_element_type=f32).astype(bf16)
    own_out[...] = made[:count, :]
    other_out[...] = made[count:, :]


def expert(groups, own, other, parts, unit, up_rows, down_rows):
    count, model = own.shape
    return pl.pallas_call(
        functools.partial(expert_kernel, groups, unit.shape[0], up_rows, down_rows, len(parts)),
        out_shape=(jax.ShapeDtypeStruct(own.shape, bf16),) * 2,
        in_specs=[ANY] * (2 + len(parts)),
        out_specs=(VMEM, VMEM),
        scratch_shapes=[
            pltpu.VMEM((2 * count, model), bf16),
            pltpu.VMEM((groups * up_rows, unit.shape[1]), bf16),
            pltpu.VMEM((groups * down_rows, model), bf16),
            pltpu.SemaphoreType.DMA((2, 3 * groups)),
            pltpu.SemaphoreType.DMA((2,)),
        ],
        compiler_params=PARAMS,
        cost_estimate=cost(4 * count * unit.shape[1] * unit.shape[0] * groups, 4 << 20),
        name="expert",
    )(own, other, *parts)


def combine_kernel(residual, gates, spread, own, returned, out, got, sems):
    lane = lax.axis_index("hd")
    copies = fetch([(own, got.at[0]), (returned, got.at[1])], sems)
    count = own.shape[0]
    column = lax.broadcasted_iota(jnp.int32, gates.shape, 1)
    total = jnp.zeros(residual.shape, f32)
    for index in range(2):
        live = lane if index == 0 else 1 - lane
        weight = jnp.sum(jnp.where(column == live, gates[...], 0.0), axis=-1, keepdims=True)
        copies[index].wait()
        picked = jnp.dot(
            spread[:, index * count : (index + 1) * count], got[index], preferred_element_type=f32
        )
        total += weight * picked
    out[...] = (residual[...].astype(f32) + total).astype(bf16)


def combine(residual, gates, spread, own, returned):
    return pl.pallas_call(
        combine_kernel,
        out_shape=jax.ShapeDtypeStruct(residual.shape, bf16),
        in_specs=[VMEM] * 3 + [ANY] * 2,
        out_specs=VMEM,
        scratch_shapes=[pltpu.VMEM((2,) + own.shape, bf16), pltpu.SemaphoreType.DMA((2,))],
        compiler_params=PARAMS,
        cost_estimate=cost(0, 1 << 20),
        name="combine",
    )(residual, gates, spread, own, returned)


def two_lane_shards(
    tokens,
    positions,
    attn_gain,
    w_query,
    w_keyval,
    w_out,
    moe_gain,
    router,
    w_gate_up,
    w_down,
    expert_ids,
    cache_slot,
    kv_cache,
):
    groups = lax.axis_size("grp")
    tok_rows, model = tokens.shape
    block = positions.shape[0]
    kv_local, head2 = w_keyval.shape[1:]
    kv_width = kv_local * head2
    slots_dev = kv_cache.shape[0]
    capc = 2 * block // groups
    swap = functools.partial(lax.ppermute, axis_name="hd", perm=[(0, 1), (1, 0)])

    other_tokens = swap(tokens)
    up, down = w_gate_up[0], w_down[0]
    expert_unit, out_unit = pack(up, down, w_out.T)
    out_parts = ring_gather(out_unit, groups)
    expert_parts = ring_gather(expert_unit, groups)
    cosine, sine, past, named, place, spread, send, tags = prepare(
        groups, slots_dev, positions, cache_slot, expert_ids, router.shape[1]
    )

    q, kv, tail = project(
        tokens,
        other_tokens,
        attn_gain[None],
        cosine,
        sine,
        w_query,
        w_keyval.reshape(model, kv_width),
    )
    seam = lax.ppermute(tail, "grp", [(g, g + 1) for g in range(groups - 1)])
    sent = attend(True, bf16, groups, q, kv, seam, past, out_parts, out_unit)
    arrived = swap(sent)
    mine = attend(False, f32, groups, q, kv, seam, past, out_parts, out_unit)

    outgoing = jnp.dot(
        send, jnp.concatenate([kv, tags], axis=1), preferred_element_type=f32
    ).astype(bf16)
    arrived_cache = lax.all_to_all(
        outgoing.reshape(groups, capc, kv_width + 128), "grp", split_axis=0, concat_axis=0, tiled=True
    ).reshape(groups * capc, kv_width + 128)
    numbers = arrived_cache[:, kv_width : kv_width + 2].astype(jnp.int32)
    write_rows = numbers[:, 0] * 64 + numbers[:, 1] - 64
    write_hit = write_rows[None, :] == jnp.arange(slots_dev, dtype=jnp.int32)[:, None]
    written = jnp.dot(
        write_hit.astype(bf16), arrived_cache[:, :kv_width], preferred_element_type=f32
    ).astype(bf16)
    cache_after = jnp.where(
        jnp.any(write_hit, axis=1)[:, None, None], written.reshape(kv_cache.shape), kv_cache
    )

    residual, gates, own_rows, sent_rows = route(
        tokens, mine, arrived, moe_gain[None], router.T, named, place
    )
    landed = swap(sent_rows)
    own_made, back = expert(
        groups, own_rows, landed, expert_parts, expert_unit, up.shape[0], down.shape[0]
    )
    returned = swap(back)
    layer_out = combine(residual, gates, spread, own_made, returned)
    return (layer_out, cache_after)


def passed_along(value, axis, steps):
    count = lax.axis_size(axis)
    initial, last = (max(0, -steps), min(count, count - steps))
    return lax.ppermute(value, axis, [(source, source + steps) for source in range(initial, last)])


def rms_norm(row_set, norm_gain):
    floats = row_set.astype(jnp.float32)
    factor = lax.rsqrt(jnp.mean(floats * floats, axis=-1, keepdims=True) + norm_eps)
    return (floats * factor * norm_gain).astype(jnp.bfloat16)


def rotate(vectors, angle_pos):
    halves = vectors.shape[-1] // 2
    inverse_freq = rope_base ** (-2.0 * jnp.arange(halves, dtype=jnp.float32) / vectors.shape[-1])
    angles = angle_pos[:, None, None] * inverse_freq[None, None, :]
    cosine = jnp.cos(angles)
    sine_part = jnp.sin(angles)
    first_half = vectors[..., :halves]
    second_half = vectors[..., halves:]
    return jnp.concatenate(
        [
            first_half * cosine - second_half * sine_part,
            second_half * cosine + first_half * sine_part,
        ],
        axis=-1,
    )


def expert_rows(row_set, gate_up, down_rows):
    gate_and_up = jnp.dot(row_set, gate_up, preferred_element_type=jnp.float32)
    inner_width = gate_and_up.shape[1] // 2
    hidden = (jax.nn.silu(gate_and_up[:, :inner_width]) * gate_and_up[:, inner_width:]).astype(
        jnp.bfloat16
    )
    return jnp.dot(hidden, down_rows, preferred_element_type=jnp.float32).astype(jnp.bfloat16)


def attend_rows(query_blk, keys_blk, vals_blk, visible, scale_qk):
    scores = (
        jnp.einsum("qkgd,skd->kgqs", query_blk, keys_blk, preferred_element_type=jnp.float32)
        * scale_qk
    )
    weights_f = jnp.where(visible[None, None], jnp.exp(scores), 0.0)
    prob_bf = (weights_f / jnp.sum(weights_f, axis=-1, keepdims=True)).astype(jnp.bfloat16)
    return jnp.einsum("kgqs,skd->qkgd", prob_bf, vals_blk, preferred_element_type=jnp.float32)


def shards(
    tokens,
    positions,
    attn_gain,
    w_query,
    w_keyval,
    w_out,
    moe_gain,
    router,
    w_gate_up,
    w_down,
    expert_ids,
    cache_slot,
    kv_cache,
):
    lane_count = lax.axis_size("hd")
    group_count = lax.axis_size("grp")
    tok_rows = tokens.shape[0]
    model_width = tokens.shape[1]
    block_len = positions.shape[0]
    seg_most = block_len // 2
    head_dim = w_keyval.shape[2] // 2
    kv_local = w_keyval.shape[1]
    q_local = w_query.shape[1] // head_dim
    per_kv = q_local // kv_local
    expert_cap = tok_rows // 4
    normed = rms_norm(tokens, attn_gain)
    flat_kv = w_keyval.reshape(model_width, kv_local * 2 * head_dim)
    section = lax.all_gather(normed, "hd", axis=0, tiled=True)
    projected = jnp.concatenate(
        [
            jnp.dot(section, w_query, preferred_element_type=jnp.float32),
            jnp.dot(section, flat_kv, preferred_element_type=jnp.float32),
        ],
        axis=1,
    )
    angle_pos = jnp.maximum(positions, 0).astype(jnp.float32)
    queries = rotate(
        projected[:, : q_local * head_dim].reshape(block_len, q_local, head_dim), angle_pos
    ).astype(jnp.bfloat16)
    key_val = projected[:, q_local * head_dim :].reshape(block_len, kv_local, 2 * head_dim)
    rotated = rotate(key_val[:, :, :head_dim], angle_pos).astype(jnp.bfloat16)
    stored = jnp.concatenate([rotated, key_val[:, :, head_dim:].astype(jnp.bfloat16)], axis=2)
    seam_rows = passed_along(stored[block_len - seg_most :], "grp", 1)
    window = jnp.concatenate([seam_rows, stored], axis=0)
    scale_qk = head_dim ** (-0.5)
    local_rows = jnp.arange(block_len, dtype=jnp.int32)
    lowest = local_rows - jnp.maximum(positions, 0)
    pieces_out = []
    for q_block in range(2):
        first_row = q_block * seg_most
        rows_here = first_row + jnp.arange(seg_most, dtype=jnp.int32)
        cols_here = first_row - seg_most + jnp.arange(2 * seg_most, dtype=jnp.int32)
        low_here = lowest[first_row : first_row + seg_most]
        visible = (cols_here[None, :] >= low_here[:, None]) & (
            cols_here[None, :] <= rows_here[:, None]
        )
        query_blk = queries[first_row : first_row + seg_most].reshape(
            seg_most, kv_local, per_kv, head_dim
        )
        keys_blk = window[first_row : first_row + 2 * seg_most, :, :head_dim]
        vals_blk = window[first_row : first_row + 2 * seg_most, :, head_dim:]
        mixed_rows = attend_rows(query_blk, keys_blk, vals_blk, visible, scale_qk)
        pieces_out.append(mixed_rows.reshape(seg_most, q_local * head_dim).astype(jnp.bfloat16))
    attended = jnp.concatenate(pieces_out, axis=0)
    slots_dev = kv_cache.shape[0]
    capc = 2 * block_len // group_count
    live_slot = cache_slot >= 0
    owners = jnp.where(live_slot, cache_slot // slots_dev, group_count)
    owner_hit = (owners[:, None] == jnp.arange(group_count, dtype=jnp.int32)[None, :]).astype(
        jnp.bfloat16
    )
    lower_tri = (local_rows[:, None] >= local_rows[None, :]).astype(jnp.bfloat16)
    running = jnp.dot(lower_tri, owner_hit, preferred_element_type=jnp.float32)
    owner_rank = jnp.sum(running * owner_hit.astype(jnp.float32), axis=1).astype(jnp.int32) - 1
    send_rows = jnp.where(live_slot, owners * capc + owner_rank, group_count * capc)
    outgoing_cache = (
        jnp.zeros((group_count * capc, kv_local, 2 * head_dim), jnp.bfloat16)
        .at[send_rows]
        .set(stored, mode="drop")
    )
    outgoing_slots = (
        jnp.full((group_count * capc,), -1, jnp.int32)
        .at[send_rows]
        .set(cache_slot % slots_dev, mode="drop")
    )
    arrived, arrived_slots = (
        lax.all_to_all(
            outgoing_cache.reshape(group_count, capc, kv_local, 2 * head_dim),
            "grp",
            split_axis=0,
            concat_axis=0,
            tiled=True,
        ),
        lax.all_to_all(
            outgoing_slots.reshape(group_count, capc),
            "grp",
            split_axis=0,
            concat_axis=0,
            tiled=True,
        ),
    )
    flat_slots = arrived_slots.reshape(group_count * capc)
    write_rows = jnp.where(flat_slots >= 0, flat_slots, slots_dev).astype(jnp.int32)
    cache_after = kv_cache.at[write_rows].set(
        arrived.reshape(group_count * capc, kv_local, 2 * head_dim), mode="drop"
    )
    by_token = lax.all_to_all(attended, "hd", split_axis=0, concat_axis=1, tiled=True)
    attn_proj = jnp.dot(
        by_token,
        lax.all_gather(w_out, "grp", axis=1, tiled=True),
        preferred_element_type=jnp.float32,
    )
    residual = (tokens.astype(jnp.float32) + attn_proj).astype(jnp.bfloat16)
    moe_in = rms_norm(residual, moe_gain)
    logits = jnp.dot(moe_in, router, preferred_element_type=jnp.float32)
    expert_range = jnp.arange(router.shape[1], dtype=jnp.int32)
    matches_all = expert_ids[:, :, None] == expert_range[None, None, :]
    chosen = jnp.sum(jnp.where(matches_all, logits[:, None, :], 0.0), axis=2)
    raised = jnp.exp(chosen)
    gates = raised / jnp.sum(raised, axis=1, keepdims=True)
    live_range = jnp.arange(lane_count, dtype=jnp.int32)
    matches = expert_ids[:, :, None] == live_range[None, None, :]
    member = jnp.any(matches, axis=1)
    weighting = jnp.sum(jnp.where(matches, gates[:, :, None], 0.0), axis=1)
    ranking = jnp.cumsum(member.astype(jnp.int32), axis=0) - 1
    target = jnp.where(member, live_range[None, :] * expert_cap + ranking, -1)
    slot_range = jnp.arange(lane_count * expert_cap, dtype=jnp.int32)
    slot_hits = target[None, :, :] == slot_range[:, None, None]
    placing = jnp.any(slot_hits, axis=2).astype(jnp.bfloat16)
    outgoing = (
        jnp.dot(placing, moe_in, preferred_element_type=jnp.float32)
        .astype(jnp.bfloat16)
        .reshape(lane_count, expert_cap, model_width)
    )
    gate_up_all, down_all = (
        lax.all_gather(w_gate_up, "grp", axis=1, tiled=True),
        lax.all_gather(w_down, "grp", axis=1, tiled=True),
    )
    gate_up_mat = gate_up_all[0]
    down_mat = down_all[0]
    landed = lax.all_to_all(outgoing, "hd", split_axis=0, concat_axis=0, tiled=True)
    results = expert_rows(landed.reshape(-1, model_width), gate_up_mat, down_mat).reshape(landed.shape)
    returned = lax.all_to_all(results, "hd", split_axis=0, concat_axis=0, tiled=True)
    flat_returned = returned.reshape(-1, model_width)
    fetched = flat_returned[jnp.maximum(target, 0)]
    used_weight = jnp.where(member, weighting, 0.0)
    moe_total = jnp.sum(used_weight[:, :, None] * fetched.astype(jnp.float32), axis=1)
    layer_out = (residual.astype(jnp.float32) + moe_total).astype(jnp.bfloat16)
    return (layer_out, cache_after)


def solution(mesh):
    two_lanes = mesh.shape["hd"] == 2 and mesh.shape["grp"] % 8 == 0
    return jax.shard_map(
        two_lane_shards if two_lanes else shards,
        mesh=mesh,
        in_specs=(
            P(("grp", "hd"), None),
            P("grp"),
            P(),
            P(None, "hd"),
            P(None, "hd", None),
            P(None, "grp"),
            P(),
            P(),
            P("hd", "grp", None),
            P("hd", "grp", None),
            P(("grp", "hd"), None),
            P("grp"),
            P("grp", "hd", None),
        ),
        out_specs=(P(("grp", "hd"), None), P("grp", "hd", None)),
        check_vma=False,
    )
```

```python
import functools

import jax
import jax.numpy as jnp
import numpy as np
from jax import lax
from jax.experimental import pallas as pl
from jax.experimental.pallas import tpu as pltpu
from jax.sharding import PartitionSpec as P

norm_eps = 1e-05
rope_base = 10000.0
bf16 = jnp.bfloat16
f32 = jnp.float32
LAST_DIMS = (((1,), (1,)), ((), ()))


def ring_cycle(groups):
    rows = groups // 4
    return [2 * r for r in range(rows)] + [2 * r + 1 for r in reversed(range(rows))]


def ring_pairs(groups):
    cycle = ring_cycle(groups)
    count = len(cycle)
    pairs = []
    for place, pair in enumerate(cycle):
        pairs.append((2 * pair, 2 * cycle[(place + 1) % count]))
        pairs.append((2 * pair + 1, 2 * cycle[(place - 1) % count] + 1))
    return pairs


def sibling_pairs(groups):
    return [(g, g ^ 1) for g in range(groups)]


def ring_sources(groups, me):
    count = groups // 2
    rows = count // 2
    side, pair = me % 2, me // 2
    row, col = pair // 2, pair % 2
    place = jnp.where(col == 0, row, count - 1 - row)

    def block(core, steps):
        there = (place + (2 * core - 1) * steps + count) % count
        other = jnp.where(there < rows, 2 * there, 2 * (count - 1 - there) + 1)
        return [2 * other + core, 2 * other + 1 - core]

    full = (count - 1) // 2
    listed = [me, me + 1 - 2 * side]
    for core in (side, 1 - side):
        for steps in range(1, full + 1):
            listed += block(core, steps)
    return listed + [block(side, count // 2)[0], block(1 - side, count // 2)[0]]


class Ring:
    def __init__(self, unit, groups):
        self.across = functools.partial(lax.ppermute, axis_name="grp", perm=ring_pairs(groups))
        self.beside = functools.partial(lax.ppermute, axis_name="grp", perm=sibling_pairs(groups))
        self.full = (groups // 2 - 1) // 2
        self.unit = unit
        self.mine = [jnp.concatenate([unit, self.beside(unit)], axis=0)]
        self.near = []

    def step(self):
        held = self.mine[-1]
        if len(self.mine) > self.full:
            held = held[: self.unit.shape[0]]
        self.mine.append(self.across(held))

    def pin(self, *others):
        done = lax.optimization_barrier((self.mine[-1],) + others)
        self.mine[-1] = done[0]
        return done[1:] if len(others) > 1 else done[1]

    def share(self):
        for index in range(1 + len(self.near), len(self.mine)):
            self.near.append(self.beside(self.mine[index]))

    def parts(self):
        full = self.full
        return self.mine[: full + 1] + self.near[:full] + [self.mine[full + 1], self.near[full]]


def start_parts(groups, parts, unit_rows, pieces, sems):
    sources = ring_sources(groups, lax.axis_index("grp"))
    copies = []
    shard = 0
    for part in parts:
        for unit in range(part.shape[0] // unit_rows):
            for first, rows, lanes, target, scale, offset, to_lane in pieces:
                at = pl.multiple_of(sources[shard] * scale + offset, 16)
                copy = pltpu.make_async_copy(
                    part.at[pl.ds(unit * unit_rows + first, rows), lanes],
                    target.at[pl.ds(at, rows), to_lane],
                    sems.at[len(copies)],
                )
                copy.start()
                copies.append(copy)
            shard += 1
    return copies


VMEM = pl.BlockSpec(memory_space=pltpu.VMEM)
ANY = pl.BlockSpec(memory_space=pl.ANY)
HBM = pl.BlockSpec(memory_space=pltpu.HBM)
PARAMS = pltpu.CompilerParams(vmem_limit_bytes=40 << 20)


def cost(flops, nbytes):
    return pl.CostEstimate(flops=flops, bytes_accessed=nbytes, transcendentals=0)


def normalized(floats, gain):
    factor = lax.rsqrt(jnp.mean(floats * floats, axis=-1, keepdims=True) + norm_eps)
    return (floats * factor * gain).astype(bf16)


def fetch(pairs, sems):
    copies = []
    for index, (source, target) in enumerate(pairs):
        copies.append(pltpu.make_async_copy(source, target, sems.at[index]))
        copies[-1].start()
    return copies


def pack_kernel(up, down, w_out, expert_unit, out_unit, sems):
    width = up.shape[1]
    rest = down.shape[1] - width
    up_rows, down_rows = up.shape[0], down.shape[0]
    half = down_rows // 2
    lane = lax.axis_index("hd")
    first = pl.multiple_of(lane * out_unit.shape[1], out_unit.shape[1])
    tail = up_rows + down_rows
    copies = fetch(
        [
            (w_out.at[:, pl.ds(first, out_unit.shape[1])], out_unit),
            (up, expert_unit.at[pl.ds(0, up_rows), :]),
            (down.at[:, pl.ds(0, width)], expert_unit.at[pl.ds(up_rows, down_rows), :]),
            (down.at[pl.ds(0, half), pl.ds(width, rest)], expert_unit.at[pl.ds(tail, half), pl.ds(0, rest)]),
            (
                down.at[pl.ds(half, half), pl.ds(width, rest)],
                expert_unit.at[pl.ds(tail, half), pl.ds(rest, rest)],
            ),
        ],
        sems,
    )
    for copy in copies:
        copy.wait()


def pack(up, down, w_out_t):
    unit = (up.shape[0] + down.shape[0] + down.shape[0] // 2, up.shape[1])
    return pl.pallas_call(
        pack_kernel,
        out_shape=(
            jax.ShapeDtypeStruct(unit, bf16),
            jax.ShapeDtypeStruct((w_out_t.shape[0], w_out_t.shape[1] // 2), bf16),
        ),
        in_specs=[HBM] * 3,
        out_specs=(ANY, ANY),
        scratch_shapes=[pltpu.SemaphoreType.DMA((5,))],
        compiler_params=PARAMS,
        cost_estimate=cost(0, 4 * unit[0] * unit[1]),
        name="pack",
    )(up, down, w_out_t)


def as_column(row, eye):
    return jnp.sum(jnp.where(eye, row, 0.0), axis=1, keepdims=True)


def prepare_kernel(
    groups, slots_dev, positions, slots, ids, cosine, sine, past, named, place, spread, send, tags
):
    lane = lax.axis_index("hd")
    block = positions.shape[1]

    def iota(shape, dim):
        return lax.broadcasted_iota(jnp.int32, shape, dim)

    eye = iota((block, block), 0) == iota((block, block), 1)
    reach = as_column(jnp.maximum(positions[...], 0).astype(f32), eye)
    past[...] = jnp.broadcast_to(reach, past.shape)
    column = iota((8, 128), 1)
    exponent = (column % 32).astype(f32) * (-2.0 / 64)
    inverse_freq = jnp.exp(exponent * np.float32(np.log(rope_base)))[:1, :]
    angles = reach * inverse_freq
    cosine[...] = jnp.cos(angles)
    turned = jnp.sin(angles)
    sine[...] = jnp.where(iota(angles.shape, 1) % 64 < 32, -turned, turned)

    tokens = ids.shape[1]
    experts = named.shape[1]
    cap = place.shape[0] // 2
    expert = iota((experts, tokens), 0)
    hit = jnp.zeros((experts, tokens), f32)
    for index in range(ids.shape[0]):
        hit = jnp.where(ids[index : index + 1, :] == expert, 1.0, hit)
    small_eye = (iota((tokens, tokens), 0) == iota((tokens, tokens), 1)).astype(f32)
    named[...] = lax.dot_general(small_eye, hit, LAST_DIMS, preferred_element_type=f32)
    upto = (iota((tokens, tokens), 0) <= iota((tokens, tokens), 1)).astype(f32)
    rank = jnp.dot(hit[:8, :], upto, preferred_element_type=f32) - 1.0
    slot = iota((2 * cap, tokens), 0).astype(f32)
    placed = jnp.zeros((2 * cap, tokens), f32)
    for live in range(2):
        order = jnp.where(lane == live, 0, cap).astype(f32)
        member = hit[live : live + 1, :] > 0.0
        placed = jnp.where(member & (slot == rank[live : live + 1, :] + order), 1.0, placed)
    place[...] = placed.astype(bf16)
    spread[...] = lax.dot_general(small_eye, placed, LAST_DIMS, preferred_element_type=f32).astype(bf16)

    where = slots[...]
    owner = jnp.where(where >= 0, where // slots_dev, -1)
    owner_hit = (iota((groups, block), 0) == owner).astype(f32)
    before = (iota((block, block), 0) <= iota((block, block), 1)).astype(f32)
    running = jnp.dot(owner_hit, before, preferred_element_type=f32)
    owner_rank = jnp.sum(owner_hit * running, axis=0, keepdims=True) - 1.0
    capc = send.shape[0] // groups
    row = jnp.where(owner >= 0, owner * capc + owner_rank.astype(jnp.int32), -1)
    send[...] = (iota(send.shape, 0) == row).astype(bf16)
    inside = jnp.where(where >= 0, where % slots_dev, 0)
    high = as_column((inside // 64 + 1).astype(f32), eye)
    low = as_column((inside % 64).astype(f32), eye)
    spot = iota(tags.shape, 1)
    tags[...] = jnp.where(spot == 0, high, jnp.where(spot == 1, low, 0.0)).astype(bf16)


def prepare(groups, slots_dev, positions, slots, ids, experts):
    block, tokens = positions.shape[0], ids.shape[0]
    cap = tokens // 4
    capc = 2 * block // groups
    shapes = [
        ((block, 128), f32),
        ((block, 128), f32),
        ((block, 128), f32),
        ((tokens, experts), f32),
        ((2 * cap, tokens), bf16),
        ((tokens, 2 * cap), bf16),
        ((groups * capc, block), bf16),
        ((block, 128), bf16),
    ]
    return pl.pallas_call(
        functools.partial(prepare_kernel, groups, slots_dev),
        out_shape=tuple(jax.ShapeDtypeStruct(shape, kind) for shape, kind in shapes),
        in_specs=[VMEM] * 3,
        out_specs=(VMEM,) * len(shapes),
        compiler_params=PARAMS,
        cost_estimate=cost(0, 1 << 20),
        name="prepare",
    )(positions[None], slots[None], ids.T)


def project_kernel(
    own, other, gain, cosine, sine, w_query, w_keyval, q_out, kv_out, seam_out, raw, rows, sems
):
    count = own.shape[0]
    lane = lax.axis_index("hd")
    mine = pl.multiple_of(lane * count, count)
    theirs = pl.multiple_of((1 - lane) * count, count)
    copies = fetch([(own, raw.at[0]), (other, raw.at[1])], sems)
    cos_q, sin_q = cosine[...], sine[...]
    column = lax.broadcasted_iota(jnp.int32, cos_q.shape, 1)
    lower = column % 64 < 32
    cos_kv = jnp.where(column < 64, cos_q, 1.0)
    sin_kv = jnp.where(column < 64, sin_q, 0.0)
    for index, first in ((0, mine), (1, theirs)):
        copies[index].wait()
        rows[pl.ds(first, count), :] = normalized(raw[index].astype(f32), gain[...])
    width = 256
    for weights, out, cos, sin in ((w_keyval, kv_out, cos_kv, sin_kv), (w_query, q_out, cos_q, sin_q)):
        for first in range(0, weights.shape[1], width):
            made = jnp.dot(rows[...], weights[:, first : first + width], preferred_element_type=f32)
            for part in range(0, width, 128):
                here = made[:, part : part + 128]
                turned = jnp.where(lower, pltpu.roll(here, 96, 1), pltpu.roll(here, 32, 1))
                done = (here * cos + turned * sin).astype(bf16)
                out[:, first + part : first + part + 128] = done
                if out is kv_out:
                    seam_out[:, first + part : first + part + 128] = done[count:, :]


def project(own, other, gain, cosine, sine, w_query, flat_kv):
    count, width = own.shape
    made = w_query.shape[1] + flat_kv.shape[1]
    return pl.pallas_call(
        project_kernel,
        out_shape=(
            jax.ShapeDtypeStruct((2 * count, w_query.shape[1]), bf16),
            jax.ShapeDtypeStruct((2 * count, flat_kv.shape[1]), bf16),
            jax.ShapeDtypeStruct((count, flat_kv.shape[1]), bf16),
        ),
        in_specs=[ANY] * 2 + [VMEM] * 5,
        out_specs=(VMEM, VMEM, VMEM),
        scratch_shapes=[
            pltpu.VMEM((2, count, width), bf16),
            pltpu.VMEM((2 * count, width), bf16),
            pltpu.SemaphoreType.DMA((2,)),
        ],
        compiler_params=PARAMS,
        cost_estimate=cost(4 * count * width * made, 2 * width * made),
        name="project",
    )(own, other, gain, cosine, sine, w_query, flat_kv)


def attend_kernel(q, kv, seam, past, mixed, window, sem):
    count = seam.shape[0]
    copy = pltpu.make_async_copy(seam, window.at[pl.ds(0, count), :], sem)
    copy.start()
    window[count:, :] = kv[...]
    head = 64
    kv_heads = kv.shape[1] // (2 * head)
    per_kv = q.shape[1] // head // kv_heads
    shape = (count, 2 * count)
    row = lax.broadcasted_iota(jnp.int32, shape, 0) + count
    col = lax.broadcasted_iota(jnp.int32, shape, 1)
    for half in (1, 0):
        first = half * count
        if half == 0:
            copy.wait()
        reach = past[first : first + count, :1].astype(jnp.int32)
        visible = (col <= row) & (col >= row - reach)
        for kv_head in range(kv_heads):
            lanes = 2 * head * kv_head
            keys = window[first : first + 2 * count, lanes : lanes + head]
            values = window[first : first + 2 * count, lanes + head : lanes + 2 * head]
            for index in range(per_kv):
                at = (kv_head * per_kv + index) * head
                query = q[first : first + count, at : at + head]
                scores = lax.dot_general(query, keys, LAST_DIMS, preferred_element_type=f32)
                raised = jnp.where(visible, jnp.exp(scores * head ** (-0.5)), 0.0)
                probs = (raised / jnp.sum(raised, axis=-1, keepdims=True)).astype(bf16)
                made = jnp.dot(probs, values, preferred_element_type=f32)
                mixed[first : first + count, at : at + head] = made.astype(bf16)


def attend(q, kv, seam, past):
    count = seam.shape[0]
    return pl.pallas_call(
        attend_kernel,
        out_shape=jax.ShapeDtypeStruct(q.shape, bf16),
        in_specs=[VMEM, VMEM, ANY, VMEM],
        out_specs=VMEM,
        scratch_shapes=[
            pltpu.VMEM((3 * count, kv.shape[1]), bf16),
            pltpu.SemaphoreType.DMA,
        ],
        compiler_params=PARAMS,
        cost_estimate=cost(8 * count * count * q.shape[1], 1 << 20),
        name="attend",
    )(q, kv, seam, past)


def outward_kernel(flip, groups, unit_rows, n_parts, mixed, *refs):
    parts, (out, w_out, sems) = refs[:n_parts], refs[n_parts:]
    all_lanes = pl.ds(0, w_out.shape[1])
    copies = start_parts(
        groups, parts, unit_rows, [(0, unit_rows, all_lanes, w_out, unit_rows, 0, all_lanes)], sems
    )
    count = out.shape[0]
    lane = lax.axis_index("hd")
    first = pl.multiple_of(((1 - lane) if flip else lane) * count, count)
    for copy in copies:
        copy.wait()
    out[...] = lax.dot_general(
        mixed[pl.ds(first, count), :], w_out[...], LAST_DIMS, preferred_element_type=f32
    ).astype(out.dtype)


def outward(flip, out_type, groups, mixed, parts, unit):
    count = mixed.shape[0] // 2
    width = groups * unit.shape[0]
    return pl.pallas_call(
        functools.partial(outward_kernel, flip, groups, unit.shape[0], len(parts)),
        out_shape=jax.ShapeDtypeStruct((count, width), out_type),
        in_specs=[VMEM] + [ANY] * len(parts),
        out_specs=VMEM,
        scratch_shapes=[
            pltpu.VMEM((width, unit.shape[1]), bf16),
            pltpu.SemaphoreType.DMA((groups,)),
        ],
        compiler_params=PARAMS,
        cost_estimate=cost(2 * count * width * unit.shape[1], 2 * width * unit.shape[1]),
        name="outward_send" if flip else "outward_keep",
    )(mixed, *parts)


def route_kernel(tokens, mine, arrived, gain, router, named, place, residual, gates, own, sent, got, sems):
    copies = fetch([(arrived, got)], sems)
    copies[0].wait()
    added = tokens[...].astype(f32) + (mine[...] + got[...].astype(f32))
    residual[...] = added.astype(bf16)
    moe_in = normalized(added.astype(bf16).astype(f32), gain[...])
    rows = jnp.dot(place[...], moe_in, preferred_element_type=f32).astype(bf16)
    cap = own.shape[0]
    own[...] = rows[:cap, :]
    sent[...] = rows[cap:, :]
    logits = lax.dot_general(moe_in, router[...], LAST_DIMS, preferred_element_type=f32)
    raised = jnp.where(named[...] > 0, jnp.exp(logits), 0.0)
    gates[...] = raised / jnp.sum(raised, axis=-1, keepdims=True)


def route(tokens, mine, arrived, gain, router_t, named, place):
    cap = place.shape[0] // 2
    return pl.pallas_call(
        route_kernel,
        out_shape=(
            jax.ShapeDtypeStruct(tokens.shape, bf16),
            jax.ShapeDtypeStruct(named.shape, f32),
            jax.ShapeDtypeStruct((cap, tokens.shape[1]), bf16),
            jax.ShapeDtypeStruct((cap, tokens.shape[1]), bf16),
        ),
        in_specs=[VMEM, VMEM, ANY] + [VMEM] * 4,
        out_specs=(VMEM,) * 4,
        scratch_shapes=[pltpu.VMEM(tokens.shape, bf16), pltpu.SemaphoreType.DMA((1,))],
        compiler_params=PARAMS,
        cost_estimate=cost(0, 2 << 20),
        name="route",
    )(tokens, mine, arrived, gain, router_t, named, place)


def expert_kernel(groups, unit_rows, up_rows, down_rows, n_parts, own, other, *refs):
    parts = refs[:n_parts]
    own_out, other_out, rows, gate_up, down, sems, row_sems = refs[n_parts:]
    width = gate_up.shape[1]
    rest = down.shape[1] - width
    half = down_rows // 2
    count = own.shape[0]
    arriving = fetch(
        [(own, rows.at[pl.ds(0, count), :]), (other, rows.at[pl.ds(count, count), :])], row_sems
    )
    copies = start_parts(
        groups,
        parts,
        unit_rows,
        [(0, up_rows, pl.ds(0, width), gate_up, up_rows, 0, pl.ds(0, width))],
        sems.at[0],
    )
    tail = up_rows + down_rows
    later = start_parts(
        groups,
        parts,
        unit_rows,
        [
            (up_rows, down_rows, pl.ds(0, width), down, down_rows, 0, pl.ds(0, width)),
            (tail, half, pl.ds(0, rest), down, down_rows, 0, pl.ds(width, rest)),
            (tail, half, pl.ds(rest, rest), down, down_rows, half, pl.ds(width, rest)),
        ],
        sems.at[1],
    )
    for copy in arriving + copies:
        copy.wait()
    both = jnp.dot(rows[...], gate_up[...], preferred_element_type=f32)
    gate, up = both[:, : width // 2], both[:, width // 2 :]
    hidden = (gate / (1.0 + jnp.exp(-gate)) * up).astype(bf16)
    for copy in later:
        copy.wait()
    made = jnp.dot(hidden, down[...], preferred_element_type=f32).astype(bf16)
    own_out[...] = made[:count, :]
    other_out[...] = made[count:, :]


def expert(groups, own, other, parts, unit, up_rows, down_rows):
    count, model = own.shape
    return pl.pallas_call(
        functools.partial(expert_kernel, groups, unit.shape[0], up_rows, down_rows, len(parts)),
        out_shape=(jax.ShapeDtypeStruct(own.shape, bf16),) * 2,
        in_specs=[ANY] * (2 + len(parts)),
        out_specs=(VMEM, VMEM),
        scratch_shapes=[
            pltpu.VMEM((2 * count, model), bf16),
            pltpu.VMEM((groups * up_rows, unit.shape[1]), bf16),
            pltpu.VMEM((groups * down_rows, model), bf16),
            pltpu.SemaphoreType.DMA((2, 3 * groups)),
            pltpu.SemaphoreType.DMA((2,)),
        ],
        compiler_params=PARAMS,
        cost_estimate=cost(4 * count * unit.shape[1] * unit.shape[0] * groups, 4 << 20),
        name="expert",
    )(own, other, *parts)


def combine_kernel(residual, gates, spread, own, returned, out, got, sems):
    lane = lax.axis_index("hd")
    copies = fetch([(own, got.at[0]), (returned, got.at[1])], sems)
    count = own.shape[0]
    column = lax.broadcasted_iota(jnp.int32, gates.shape, 1)
    total = jnp.zeros(residual.shape, f32)
    for index in range(2):
        live = lane if index == 0 else 1 - lane
        weight = jnp.sum(jnp.where(column == live, gates[...], 0.0), axis=-1, keepdims=True)
        copies[index].wait()
        picked = jnp.dot(
            spread[:, index * count : (index + 1) * count], got[index], preferred_element_type=f32
        )
        total += weight * picked
    out[...] = (residual[...].astype(f32) + total).astype(bf16)


def combine(residual, gates, spread, own, returned):
    return pl.pallas_call(
        combine_kernel,
        out_shape=jax.ShapeDtypeStruct(residual.shape, bf16),
        in_specs=[VMEM] * 3 + [ANY] * 2,
        out_specs=VMEM,
        scratch_shapes=[pltpu.VMEM((2,) + own.shape, bf16), pltpu.SemaphoreType.DMA((2,))],
        compiler_params=PARAMS,
        cost_estimate=cost(0, 1 << 20),
        name="combine",
    )(residual, gates, spread, own, returned)


def two_lane_shards(
    tokens,
    positions,
    attn_gain,
    w_query,
    w_keyval,
    w_out,
    moe_gain,
    router,
    w_gate_up,
    w_down,
    expert_ids,
    cache_slot,
    kv_cache,
):
    groups = lax.axis_size("grp")
    tok_rows, model = tokens.shape
    block = positions.shape[0]
    kv_local, head2 = w_keyval.shape[1:]
    kv_width = kv_local * head2
    slots_dev = kv_cache.shape[0]
    capc = 2 * block // groups
    swap = functools.partial(lax.ppermute, axis_name="hd", perm=[(0, 1), (1, 0)])

    other_tokens = swap(tokens)
    up, down = w_gate_up[0], w_down[0]
    expert_unit, out_unit = pack(up, down, w_out.T)
    out_ring = Ring(out_unit, groups)
    out_ring.step()
    expert_ring = Ring(expert_unit, groups)
    expert_ring.step()
    cosine, sine, past, named, place, spread, send, tags = prepare(
        groups, slots_dev, positions, cache_slot, expert_ids, router.shape[1]
    )
    other_tokens = out_ring.pin(other_tokens)
    out_ring.step()
    q, kv, tail = project(
        tokens,
        other_tokens,
        attn_gain[None],
        cosine,
        sine,
        w_query,
        w_keyval.reshape(model, kv_width),
    )
    q, kv = out_ring.pin(q, kv)
    seam = lax.ppermute(tail, "grp", [(g, g + 1) for g in range(groups - 1)])
    out_ring.step()
    out_ring.share()
    q, kv = expert_ring.pin(q, kv)
    expert_ring.step()
    mixed = attend(q, kv, seam, past)
    mixed = out_ring.pin(mixed)
    out_ring.step()
    out_ring.share()
    mixed = expert_ring.pin(mixed)
    expert_ring.step()
    expert_ring.share()
    out_parts = out_ring.parts()
    sent = outward(True, bf16, groups, mixed, out_parts, out_unit)
    arrived = swap(sent)
    mixed, send = lax.optimization_barrier((mixed, send, sent))[:2]
    mine = outward(False, f32, groups, mixed, out_parts, out_unit)

    outgoing = jnp.dot(
        send, jnp.concatenate([kv, tags], axis=1), preferred_element_type=f32
    ).astype(bf16)
    outgoing = expert_ring.pin(outgoing)
    expert_ring.step()
    expert_ring.share()
    arrived_cache = lax.all_to_all(
        outgoing.reshape(groups, capc, kv_width + 128), "grp", split_axis=0, concat_axis=0, tiled=True
    ).reshape(groups * capc, kv_width + 128)
    numbers = arrived_cache[:, kv_width : kv_width + 2].astype(jnp.int32)
    write_rows = numbers[:, 0] * 64 + numbers[:, 1] - 64
    write_hit = write_rows[None, :] == jnp.arange(slots_dev, dtype=jnp.int32)[:, None]
    written = jnp.dot(
        write_hit.astype(bf16), arrived_cache[:, :kv_width], preferred_element_type=f32
    ).astype(bf16)
    cache_after = jnp.where(
        jnp.any(write_hit, axis=1)[:, None, None], written.reshape(kv_cache.shape), kv_cache
    )

    residual, gates, own_rows, sent_rows = route(
        tokens, mine, arrived, moe_gain[None], router.T, named, place
    )
    landed = swap(sent_rows)
    own_made, back = expert(
        groups, own_rows, landed, expert_ring.parts(), expert_unit, up.shape[0], down.shape[0]
    )
    returned = swap(back)
    layer_out = combine(residual, gates, spread, own_made, returned)
    return (layer_out, cache_after)


def passed_along(value, axis, steps):
    count = lax.axis_size(axis)
    initial, last = (max(0, -steps), min(count, count - steps))
    return lax.ppermute(value, axis, [(source, source + steps) for source in range(initial, last)])


def rms_norm(row_set, norm_gain):
    floats = row_set.astype(jnp.float32)
    factor = lax.rsqrt(jnp.mean(floats * floats, axis=-1, keepdims=True) + norm_eps)
    return (floats * factor * norm_gain).astype(jnp.bfloat16)


def rotate(vectors, angle_pos):
    halves = vectors.shape[-1] // 2
    inverse_freq = rope_base ** (-2.0 * jnp.arange(halves, dtype=jnp.float32) / vectors.shape[-1])
    angles = angle_pos[:, None, None] * inverse_freq[None, None, :]
    cosine = jnp.cos(angles)
    sine_part = jnp.sin(angles)
    first_half = vectors[..., :halves]
    second_half = vectors[..., halves:]
    return jnp.concatenate(
        [
            first_half * cosine - second_half * sine_part,
            second_half * cosine + first_half * sine_part,
        ],
        axis=-1,
    )


def expert_rows(row_set, gate_up, down_rows):
    gate_and_up = jnp.dot(row_set, gate_up, preferred_element_type=jnp.float32)
    inner_width = gate_and_up.shape[1] // 2
    hidden = (jax.nn.silu(gate_and_up[:, :inner_width]) * gate_and_up[:, inner_width:]).astype(
        jnp.bfloat16
    )
    return jnp.dot(hidden, down_rows, preferred_element_type=jnp.float32).astype(jnp.bfloat16)


def attend_rows(query_blk, keys_blk, vals_blk, visible, scale_qk):
    scores = (
        jnp.einsum("qkgd,skd->kgqs", query_blk, keys_blk, preferred_element_type=jnp.float32)
        * scale_qk
    )
    weights_f = jnp.where(visible[None, None], jnp.exp(scores), 0.0)
    prob_bf = (weights_f / jnp.sum(weights_f, axis=-1, keepdims=True)).astype(jnp.bfloat16)
    return jnp.einsum("kgqs,skd->qkgd", prob_bf, vals_blk, preferred_element_type=jnp.float32)


def shards(
    tokens,
    positions,
    attn_gain,
    w_query,
    w_keyval,
    w_out,
    moe_gain,
    router,
    w_gate_up,
    w_down,
    expert_ids,
    cache_slot,
    kv_cache,
):
    lane_count = lax.axis_size("hd")
    group_count = lax.axis_size("grp")
    tok_rows = tokens.shape[0]
    model_width = tokens.shape[1]
    block_len = positions.shape[0]
    seg_most = block_len // 2
    head_dim = w_keyval.shape[2] // 2
    kv_local = w_keyval.shape[1]
    q_local = w_query.shape[1] // head_dim
    per_kv = q_local // kv_local
    expert_cap = tok_rows // 4
    normed = rms_norm(tokens, attn_gain)
    flat_kv = w_keyval.reshape(model_width, kv_local * 2 * head_dim)
    section = lax.all_gather(normed, "hd", axis=0, tiled=True)
    projected = jnp.concatenate(
        [
            jnp.dot(section, w_query, preferred_element_type=jnp.float32),
            jnp.dot(section, flat_kv, preferred_element_type=jnp.float32),
        ],
        axis=1,
    )
    angle_pos = jnp.maximum(positions, 0).astype(jnp.float32)
    queries = rotate(
        projected[:, : q_local * head_dim].reshape(block_len, q_local, head_dim), angle_pos
    ).astype(jnp.bfloat16)
    key_val = projected[:, q_local * head_dim :].reshape(block_len, kv_local, 2 * head_dim)
    rotated = rotate(key_val[:, :, :head_dim], angle_pos).astype(jnp.bfloat16)
    stored = jnp.concatenate([rotated, key_val[:, :, head_dim:].astype(jnp.bfloat16)], axis=2)
    seam_rows = passed_along(stored[block_len - seg_most :], "grp", 1)
    window = jnp.concatenate([seam_rows, stored], axis=0)
    scale_qk = head_dim ** (-0.5)
    local_rows = jnp.arange(block_len, dtype=jnp.int32)
    lowest = local_rows - jnp.maximum(positions, 0)
    pieces_out = []
    for q_block in range(2):
        first_row = q_block * seg_most
        rows_here = first_row + jnp.arange(seg_most, dtype=jnp.int32)
        cols_here = first_row - seg_most + jnp.arange(2 * seg_most, dtype=jnp.int32)
        low_here = lowest[first_row : first_row + seg_most]
        visible = (cols_here[None, :] >= low_here[:, None]) & (
            cols_here[None, :] <= rows_here[:, None]
        )
        query_blk = queries[first_row : first_row + seg_most].reshape(
            seg_most, kv_local, per_kv, head_dim
        )
        keys_blk = window[first_row : first_row + 2 * seg_most, :, :head_dim]
        vals_blk = window[first_row : first_row + 2 * seg_most, :, head_dim:]
        mixed_rows = attend_rows(query_blk, keys_blk, vals_blk, visible, scale_qk)
        pieces_out.append(mixed_rows.reshape(seg_most, q_local * head_dim).astype(jnp.bfloat16))
    attended = jnp.concatenate(pieces_out, axis=0)
    slots_dev = kv_cache.shape[0]
    capc = 2 * block_len // group_count
    live_slot = cache_slot >= 0
    owners = jnp.where(live_slot, cache_slot // slots_dev, group_count)
    owner_hit = (owners[:, None] == jnp.arange(group_count, dtype=jnp.int32)[None, :]).astype(
        jnp.bfloat16
    )
    lower_tri = (local_rows[:, None] >= local_rows[None, :]).astype(jnp.bfloat16)
    running = jnp.dot(lower_tri, owner_hit, preferred_element_type=jnp.float32)
    owner_rank = jnp.sum(running * owner_hit.astype(jnp.float32), axis=1).astype(jnp.int32) - 1
    send_rows = jnp.where(live_slot, owners * capc + owner_rank, group_count * capc)
    outgoing_cache = (
        jnp.zeros((group_count * capc, kv_local, 2 * head_dim), jnp.bfloat16)
        .at[send_rows]
        .set(stored, mode="drop")
    )
    outgoing_slots = (
        jnp.full((group_count * capc,), -1, jnp.int32)
        .at[send_rows]
        .set(cache_slot % slots_dev, mode="drop")
    )
    arrived, arrived_slots = (
        lax.all_to_all(
            outgoing_cache.reshape(group_count, capc, kv_local, 2 * head_dim),
            "grp",
            split_axis=0,
            concat_axis=0,
            tiled=True,
        ),
        lax.all_to_all(
            outgoing_slots.reshape(group_count, capc),
            "grp",
            split_axis=0,
            concat_axis=0,
            tiled=True,
        ),
    )
    flat_slots = arrived_slots.reshape(group_count * capc)
    write_rows = jnp.where(flat_slots >= 0, flat_slots, slots_dev).astype(jnp.int32)
    cache_after = kv_cache.at[write_rows].set(
        arrived.reshape(group_count * capc, kv_local, 2 * head_dim), mode="drop"
    )
    by_token = lax.all_to_all(attended, "hd", split_axis=0, concat_axis=1, tiled=True)
    attn_proj = jnp.dot(
        by_token,
        lax.all_gather(w_out, "grp", axis=1, tiled=True),
        preferred_element_type=jnp.float32,
    )
    residual = (tokens.astype(jnp.float32) + attn_proj).astype(jnp.bfloat16)
    moe_in = rms_norm(residual, moe_gain)
    logits = jnp.dot(moe_in, router, preferred_element_type=jnp.float32)
    expert_range = jnp.arange(router.shape[1], dtype=jnp.int32)
    matches_all = expert_ids[:, :, None] == expert_range[None, None, :]
    chosen = jnp.sum(jnp.where(matches_all, logits[:, None, :], 0.0), axis=2)
    raised = jnp.exp(chosen)
    gates = raised / jnp.sum(raised, axis=1, keepdims=True)
    live_range = jnp.arange(lane_count, dtype=jnp.int32)
    matches = expert_ids[:, :, None] == live_range[None, None, :]
    member = jnp.any(matches, axis=1)
    weighting = jnp.sum(jnp.where(matches, gates[:, :, None], 0.0), axis=1)
    ranking = jnp.cumsum(member.astype(jnp.int32), axis=0) - 1
    target = jnp.where(member, live_range[None, :] * expert_cap + ranking, -1)
    slot_range = jnp.arange(lane_count * expert_cap, dtype=jnp.int32)
    slot_hits = target[None, :, :] == slot_range[:, None, None]
    placing = jnp.any(slot_hits, axis=2).astype(jnp.bfloat16)
    outgoing = (
        jnp.dot(placing, moe_in, preferred_element_type=jnp.float32)
        .astype(jnp.bfloat16)
        .reshape(lane_count, expert_cap, model_width)
    )
    gate_up_all, down_all = (
        lax.all_gather(w_gate_up, "grp", axis=1, tiled=True),
        lax.all_gather(w_down, "grp", axis=1, tiled=True),
    )
    gate_up_mat = gate_up_all[0]
    down_mat = down_all[0]
    landed = lax.all_to_all(outgoing, "hd", split_axis=0, concat_axis=0, tiled=True)
    results = expert_rows(landed.reshape(-1, model_width), gate_up_mat, down_mat).reshape(landed.shape)
    returned = lax.all_to_all(results, "hd", split_axis=0, concat_axis=0, tiled=True)
    flat_returned = returned.reshape(-1, model_width)
    fetched = flat_returned[jnp.maximum(target, 0)]
    used_weight = jnp.where(member, weighting, 0.0)
    moe_total = jnp.sum(used_weight[:, :, None] * fetched.astype(jnp.float32), axis=1)
    layer_out = (residual.astype(jnp.float32) + moe_total).astype(jnp.bfloat16)
    return (layer_out, cache_after)


def solution(mesh):
    two_lanes = mesh.shape["hd"] == 2 and mesh.shape["grp"] % 8 == 0
    return jax.shard_map(
        two_lane_shards if two_lanes else shards,
        mesh=mesh,
        in_specs=(
            P(("grp", "hd"), None),
            P("grp"),
            P(),
            P(None, "hd"),
            P(None, "hd", None),
            P(None, "grp"),
            P(),
            P(),
            P("hd", "grp", None),
            P("hd", "grp", None),
            P(("grp", "hd"), None),
            P("grp"),
            P("grp", "hd", None),
        ),
        out_specs=(P(("grp", "hd"), None), P("grp", "hd", None)),
        check_vma=False,
    )
```

```python
import functools

import jax
import jax.numpy as jnp
import numpy as np
from jax import lax
from jax.experimental import pallas as pl
from jax.experimental.pallas import tpu as pltpu
from jax.sharding import PartitionSpec as P

norm_eps = 1e-05
rope_base = 10000.0
bf16 = jnp.bfloat16
f32 = jnp.float32
LAST_DIMS = (((1,), (1,)), ((), ()))


def ring_cycle(groups):
    rows = groups // 4
    return [2 * r for r in range(rows)] + [2 * r + 1 for r in reversed(range(rows))]


def ring_pairs(groups):
    cycle = ring_cycle(groups)
    count = len(cycle)
    pairs = []
    for place, pair in enumerate(cycle):
        pairs.append((2 * pair, 2 * cycle[(place + 1) % count]))
        pairs.append((2 * pair + 1, 2 * cycle[(place - 1) % count] + 1))
    return pairs


def sibling_pairs(groups):
    return [(g, g ^ 1) for g in range(groups)]


def ring_sources(groups, me):
    count = groups // 2
    rows = count // 2
    side, pair = me % 2, me // 2
    row, col = pair // 2, pair % 2
    place = jnp.where(col == 0, row, count - 1 - row)

    def block(core, steps):
        there = (place + (2 * core - 1) * steps + count) % count
        other = jnp.where(there < rows, 2 * there, 2 * (count - 1 - there) + 1)
        return [2 * other + core, 2 * other + 1 - core]

    full = (count - 1) // 2
    listed = [me, me + 1 - 2 * side]
    for core in (side, 1 - side):
        for steps in range(1, full + 1):
            listed += block(core, steps)
    return listed + [block(side, count // 2)[0], block(1 - side, count // 2)[0]]


class Ring:
    def __init__(self, pair, groups):
        self.across = functools.partial(lax.ppermute, axis_name="grp", perm=ring_pairs(groups))
        self.beside = functools.partial(lax.ppermute, axis_name="grp", perm=sibling_pairs(groups))
        self.full = (groups // 2 - 1) // 2
        self.unit_rows = pair.shape[0] // 2
        self.mine = [pair]
        self.near = []

    def step(self):
        held = self.mine[-1]
        if len(self.mine) > self.full:
            held = held[: self.unit_rows]
        self.mine.append(self.across(held))

    def pin(self, *others):
        done = lax.optimization_barrier((self.mine[-1],) + others)
        self.mine[-1] = done[0]
        return done[1:] if len(others) > 1 else done[1]

    def share(self):
        for index in range(1 + len(self.near), len(self.mine)):
            self.near.append(self.beside(self.mine[index]))

    def parts(self):
        full = self.full
        return self.mine[: full + 1] + self.near[:full] + [self.mine[full + 1], self.near[full]]


def place_parts(groups, parts, unit_rows, pieces):
    sources = ring_sources(groups, lax.axis_index("grp"))
    shard = 0
    for part in parts:
        for unit in range(part.shape[0] // unit_rows):
            for first, rows, target, lane in pieces:
                at = pl.multiple_of(sources[shard] * rows, rows)
                start = unit * unit_rows + first
                target[pl.ds(at, rows), lane : lane + part.shape[1]] = part[start : start + rows, :]
            shard += 1


VMEM = pl.BlockSpec(memory_space=pltpu.VMEM)
ANY = pl.BlockSpec(memory_space=pl.ANY)
HBM = pl.BlockSpec(memory_space=pltpu.HBM)
PARAMS = pltpu.CompilerParams(vmem_limit_bytes=40 << 20)


def cost(flops, nbytes):
    return pl.CostEstimate(flops=flops, bytes_accessed=nbytes, transcendentals=0)


def normalized(floats, gain):
    factor = lax.rsqrt(jnp.mean(floats * floats, axis=-1, keepdims=True) + norm_eps)
    return (floats * factor * gain).astype(bf16)


def fetch(pairs, sems):
    copies = []
    for index, (source, target) in enumerate(pairs):
        copies.append(pltpu.make_async_copy(source, target, sems.at[index]))
        copies[-1].start()
    return copies


def pack_kernel(*refs):
    sources, (expert_pair, out_pair, sems) = refs[:6], refs[6:]
    width = expert_pair.shape[1]
    lane = lax.axis_index("hd")
    first = pl.multiple_of(lane * out_pair.shape[1], out_pair.shape[1])
    pairs = []
    row = 0
    for index in range(2):
        up, down, w_out = sources[3 * index : 3 * index + 3]
        count = w_out.shape[0]
        pairs.append(
            (w_out.at[:, pl.ds(first, out_pair.shape[1])], out_pair.at[pl.ds(index * count, count), :])
        )
        for source in (up, down):
            for at in range(0, source.shape[1], width):
                pairs.append(
                    (source.at[:, pl.ds(at, width)], expert_pair.at[pl.ds(row, source.shape[0]), :])
                )
                row += source.shape[0]
    for copy in fetch(pairs, sems):
        copy.wait()


def pack(own, beside):
    up, down, w_out_t = own
    width = up.shape[1] // 2
    pieces = [up.shape[1] // width, down.shape[1] // width]
    unit_rows = pieces[0] * up.shape[0] + pieces[1] * down.shape[0]
    return pl.pallas_call(
        pack_kernel,
        out_shape=(
            jax.ShapeDtypeStruct((2 * unit_rows, width), bf16),
            jax.ShapeDtypeStruct((2 * w_out_t.shape[0], w_out_t.shape[1] // 2), bf16),
        ),
        in_specs=[ANY] * 6,
        out_specs=(ANY, ANY),
        scratch_shapes=[pltpu.SemaphoreType.DMA((2 + 2 * sum(pieces),))],
        compiler_params=PARAMS,
        cost_estimate=cost(0, 0),
        name="pack",
    )(*own, *beside)


def as_column(row, eye):
    return jnp.sum(jnp.where(eye, row, 0.0), axis=1, keepdims=True)


def prepare_kernel(
    groups, slots_dev, positions, slots, ids, cosine, sine, past, named, place, spread, send, tags
):
    lane = lax.axis_index("hd")
    block = positions.shape[1]

    def iota(shape, dim):
        return lax.broadcasted_iota(jnp.int32, shape, dim)

    eye = iota((block, block), 0) == iota((block, block), 1)
    reach = as_column(jnp.maximum(positions[...], 0).astype(f32), eye)
    past[...] = jnp.broadcast_to(reach, past.shape)
    column = iota((8, 128), 1)
    exponent = (column % 32).astype(f32) * (-2.0 / 64)
    inverse_freq = jnp.exp(exponent * np.float32(np.log(rope_base)))[:1, :]
    angles = reach * inverse_freq
    cosine[...] = jnp.cos(angles)
    turned = jnp.sin(angles)
    sine[...] = jnp.where(iota(angles.shape, 1) % 64 < 32, -turned, turned)

    tokens = ids.shape[1]
    experts = named.shape[1]
    cap = place.shape[0] // 2
    expert = iota((experts, tokens), 0)
    hit = jnp.zeros((experts, tokens), f32)
    for index in range(ids.shape[0]):
        hit = jnp.where(ids[index : index + 1, :] == expert, 1.0, hit)
    small_eye = (iota((tokens, tokens), 0) == iota((tokens, tokens), 1)).astype(f32)
    named[...] = lax.dot_general(small_eye, hit, LAST_DIMS, preferred_element_type=f32)
    upto = (iota((tokens, tokens), 0) <= iota((tokens, tokens), 1)).astype(f32)
    rank = jnp.dot(hit[:8, :], upto, preferred_element_type=f32) - 1.0
    slot = iota((2 * cap, tokens), 0).astype(f32)
    placed = jnp.zeros((2 * cap, tokens), f32)
    for live in range(2):
        order = jnp.where(lane == live, 0, cap).astype(f32)
        member = hit[live : live + 1, :] > 0.0
        placed = jnp.where(member & (slot == rank[live : live + 1, :] + order), 1.0, placed)
    place[...] = placed.astype(bf16)
    spread[...] = lax.dot_general(small_eye, placed, LAST_DIMS, preferred_element_type=f32).astype(bf16)

    where = slots[...]
    owner = jnp.where(where >= 0, where // slots_dev, -1)
    owner_hit = (iota((groups, block), 0) == owner).astype(f32)
    before = (iota((block, block), 0) <= iota((block, block), 1)).astype(f32)
    running = jnp.dot(owner_hit, before, preferred_element_type=f32)
    owner_rank = jnp.sum(owner_hit * running, axis=0, keepdims=True) - 1.0
    capc = send.shape[0] // groups
    row = jnp.where(owner >= 0, owner * capc + owner_rank.astype(jnp.int32), -1)
    send[...] = (iota(send.shape, 0) == row).astype(bf16)
    inside = jnp.where(where >= 0, where % slots_dev, 0)
    high = as_column((inside // 64 + 1).astype(f32), eye)
    low = as_column((inside % 64).astype(f32), eye)
    spot = iota(tags.shape, 1)
    tags[...] = jnp.where(spot == 0, high, jnp.where(spot == 1, low, 0.0)).astype(bf16)


def prepare(groups, slots_dev, positions, slots, ids, experts):
    block, tokens = positions.shape[0], ids.shape[0]
    cap = tokens // 4
    capc = 2 * block // groups
    shapes = [
        ((block, 128), f32),
        ((block, 128), f32),
        ((block, 128), f32),
        ((tokens, experts), f32),
        ((2 * cap, tokens), bf16),
        ((tokens, 2 * cap), bf16),
        ((groups * capc, block), bf16),
        ((block, 128), bf16),
    ]
    return pl.pallas_call(
        functools.partial(prepare_kernel, groups, slots_dev),
        out_shape=tuple(jax.ShapeDtypeStruct(shape, kind) for shape, kind in shapes),
        in_specs=[VMEM] * 3,
        out_specs=(VMEM,) * len(shapes),
        compiler_params=PARAMS,
        cost_estimate=cost(0, 1 << 20),
        name="prepare",
    )(positions[None], slots[None], ids.T)


def project_kernel(
    own, other, gain, cosine, sine, w_query, w_keyval, q_out, kv_out, seam_out, raw, rows, sems
):
    count = own.shape[0]
    lane = lax.axis_index("hd")
    mine = pl.multiple_of(lane * count, count)
    theirs = pl.multiple_of((1 - lane) * count, count)
    copies = fetch([(own, raw.at[0]), (other, raw.at[1])], sems)
    cos_q, sin_q = cosine[...], sine[...]
    column = lax.broadcasted_iota(jnp.int32, cos_q.shape, 1)
    lower = column % 64 < 32
    cos_kv = jnp.where(column < 64, cos_q, 1.0)
    sin_kv = jnp.where(column < 64, sin_q, 0.0)
    for index, first in ((0, mine), (1, theirs)):
        copies[index].wait()
        rows[pl.ds(first, count), :] = normalized(raw[index].astype(f32), gain[...])
    width = 256
    for weights, out, cos, sin in ((w_keyval, kv_out, cos_kv, sin_kv), (w_query, q_out, cos_q, sin_q)):
        for first in range(0, weights.shape[1], width):
            made = jnp.dot(rows[...], weights[:, first : first + width], preferred_element_type=f32)
            for part in range(0, width, 128):
                here = made[:, part : part + 128]
                turned = jnp.where(lower, pltpu.roll(here, 96, 1), pltpu.roll(here, 32, 1))
                done = (here * cos + turned * sin).astype(bf16)
                out[:, first + part : first + part + 128] = done
                if out is kv_out:
                    seam_out[:, first + part : first + part + 128] = done[count:, :]


def project(own, other, gain, cosine, sine, w_query, flat_kv):
    count, width = own.shape
    made = w_query.shape[1] + flat_kv.shape[1]
    return pl.pallas_call(
        project_kernel,
        out_shape=(
            jax.ShapeDtypeStruct((2 * count, w_query.shape[1]), bf16),
            jax.ShapeDtypeStruct((2 * count, flat_kv.shape[1]), bf16),
            jax.ShapeDtypeStruct((count, flat_kv.shape[1]), bf16),
        ),
        in_specs=[ANY] * 2 + [VMEM] * 5,
        out_specs=(VMEM, VMEM, VMEM),
        scratch_shapes=[
            pltpu.VMEM((2, count, width), bf16),
            pltpu.VMEM((2 * count, width), bf16),
            pltpu.SemaphoreType.DMA((2,)),
        ],
        compiler_params=PARAMS,
        cost_estimate=cost(4 * count * width * made, 2 * width * made),
        name="project",
    )(own, other, gain, cosine, sine, w_query, flat_kv)


def attend_kernel(q, kv, seam, past, mixed, window, sem):
    count = seam.shape[0]
    copy = pltpu.make_async_copy(seam, window.at[pl.ds(0, count), :], sem)
    copy.start()
    window[count:, :] = kv[...]
    head = 64
    kv_heads = kv.shape[1] // (2 * head)
    per_kv = q.shape[1] // head // kv_heads
    shape = (count, 2 * count)
    row = lax.broadcasted_iota(jnp.int32, shape, 0) + count
    col = lax.broadcasted_iota(jnp.int32, shape, 1)
    for half in (1, 0):
        first = half * count
        if half == 0:
            copy.wait()
        reach = past[first : first + count, :1].astype(jnp.int32)
        visible = (col <= row) & (col >= row - reach)
        for kv_head in range(kv_heads):
            lanes = 2 * head * kv_head
            keys = window[first : first + 2 * count, lanes : lanes + head]
            values = window[first : first + 2 * count, lanes + head : lanes + 2 * head]
            for index in range(per_kv):
                at = (kv_head * per_kv + index) * head
                query = q[first : first + count, at : at + head]
                scores = lax.dot_general(query, keys, LAST_DIMS, preferred_element_type=f32)
                raised = jnp.where(visible, jnp.exp(scores * head ** (-0.5)), 0.0)
                probs = (raised / jnp.sum(raised, axis=-1, keepdims=True)).astype(bf16)
                made = jnp.dot(probs, values, preferred_element_type=f32)
                mixed[first : first + count, at : at + head] = made.astype(bf16)


def attend(q, kv, seam, past):
    count = seam.shape[0]
    return pl.pallas_call(
        attend_kernel,
        out_shape=jax.ShapeDtypeStruct(q.shape, bf16),
        in_specs=[VMEM, VMEM, ANY, VMEM],
        out_specs=VMEM,
        scratch_shapes=[
            pltpu.VMEM((3 * count, kv.shape[1]), bf16),
            pltpu.SemaphoreType.DMA,
        ],
        compiler_params=PARAMS,
        cost_estimate=cost(8 * count * count * q.shape[1], 1 << 20),
        name="attend",
    )(q, kv, seam, past)


def outward_kernel(flip, groups, unit_rows, n_parts, mixed, *refs):
    parts, (out, w_out) = refs[:n_parts], refs[n_parts:]
    place_parts(groups, parts, unit_rows, [(0, unit_rows, w_out, 0)])
    count = out.shape[0]
    lane = lax.axis_index("hd")
    first = pl.multiple_of(((1 - lane) if flip else lane) * count, count)
    out[...] = lax.dot_general(
        mixed[pl.ds(first, count), :], w_out[...], LAST_DIMS, preferred_element_type=f32
    ).astype(out.dtype)


def outward(flip, out_type, groups, mixed, parts, unit_rows):
    count = mixed.shape[0] // 2
    width = groups * unit_rows
    depth = parts[0].shape[1]
    return pl.pallas_call(
        functools.partial(outward_kernel, flip, groups, unit_rows, len(parts)),
        out_shape=jax.ShapeDtypeStruct((count, width), out_type),
        in_specs=[VMEM] * (1 + len(parts)),
        out_specs=VMEM,
        scratch_shapes=[pltpu.VMEM((width, depth), bf16)],
        compiler_params=PARAMS,
        cost_estimate=cost(2 * count * width * depth, 2 * width * depth),
        name="outward_send" if flip else "outward_keep",
    )(mixed, *parts)


def route_kernel(tokens, mine, arrived, gain, router, named, place, residual, gates, own, sent, got, sems):
    copies = fetch([(arrived, got)], sems)
    copies[0].wait()
    added = tokens[...].astype(f32) + (mine[...] + got[...].astype(f32))
    residual[...] = added.astype(bf16)
    moe_in = normalized(added.astype(bf16).astype(f32), gain[...])
    rows = jnp.dot(place[...], moe_in, preferred_element_type=f32).astype(bf16)
    cap = own.shape[0]
    own[...] = rows[:cap, :]
    sent[...] = rows[cap:, :]
    logits = lax.dot_general(moe_in, router[...], LAST_DIMS, preferred_element_type=f32)
    raised = jnp.where(named[...] > 0, jnp.exp(logits), 0.0)
    gates[...] = raised / jnp.sum(raised, axis=-1, keepdims=True)


def route(tokens, mine, arrived, gain, router_t, named, place):
    cap = place.shape[0] // 2
    return pl.pallas_call(
        route_kernel,
        out_shape=(
            jax.ShapeDtypeStruct(tokens.shape, bf16),
            jax.ShapeDtypeStruct(named.shape, f32),
            jax.ShapeDtypeStruct((cap, tokens.shape[1]), bf16),
            jax.ShapeDtypeStruct((cap, tokens.shape[1]), bf16),
        ),
        in_specs=[VMEM, VMEM, ANY] + [VMEM] * 4,
        out_specs=(VMEM,) * 4,
        scratch_shapes=[pltpu.VMEM(tokens.shape, bf16), pltpu.SemaphoreType.DMA((1,))],
        compiler_params=PARAMS,
        cost_estimate=cost(0, 2 << 20),
        name="route",
    )(tokens, mine, arrived, gain, router_t, named, place)


def expert_kernel(groups, up_rows, down_rows, n_parts, own, other, *refs):
    parts = refs[:n_parts]
    own_out, other_out, rows, gate_up, down = refs[n_parts:]
    width = parts[0].shape[1]
    count = own.shape[0]
    rows[:count, :] = own[...]
    rows[count:, :] = other[...]
    pieces = [(i * up_rows, up_rows, gate_up, i * width) for i in range(2)]
    pieces += [
        (2 * up_rows + i * down_rows, down_rows, down, i * width) for i in range(down.shape[1] // width)
    ]
    unit_rows = pieces[-1][0] + down_rows
    place_parts(groups, parts, unit_rows, pieces)
    both = jnp.dot(rows[...], gate_up[...], preferred_element_type=f32)
    gate, up = both[:, :width], both[:, width:]
    hidden = (gate / (1.0 + jnp.exp(-gate)) * up).astype(bf16)
    made = jnp.dot(hidden, down[...], preferred_element_type=f32).astype(bf16)
    own_out[...] = made[:count, :]
    other_out[...] = made[count:, :]


def expert(groups, own, other, parts, up_rows, down_rows):
    count, model = own.shape
    width = parts[0].shape[1]
    return pl.pallas_call(
        functools.partial(expert_kernel, groups, up_rows, down_rows, len(parts)),
        out_shape=(jax.ShapeDtypeStruct(own.shape, bf16),) * 2,
        in_specs=[VMEM] * (2 + len(parts)),
        out_specs=(VMEM, VMEM),
        scratch_shapes=[
            pltpu.VMEM((2 * count, model), bf16),
            pltpu.VMEM((groups * up_rows, 2 * width), bf16),
            pltpu.VMEM((groups * down_rows, model), bf16),
        ],
        compiler_params=PARAMS,
        cost_estimate=cost(4 * count * width * 9 * down_rows * groups, 4 << 20),
        name="expert",
    )(own, other, *parts)


def combine_kernel(residual, gates, spread, own, returned, out):
    lane = lax.axis_index("hd")
    count = own.shape[0]
    column = lax.broadcasted_iota(jnp.int32, gates.shape, 1)
    total = jnp.zeros(residual.shape, f32)
    for index, made in ((0, own), (1, returned)):
        live = lane if index == 0 else 1 - lane
        weight = jnp.sum(jnp.where(column == live, gates[...], 0.0), axis=-1, keepdims=True)
        picked = jnp.dot(
            spread[:, index * count : (index + 1) * count], made[...], preferred_element_type=f32
        )
        total += weight * picked
    out[...] = (residual[...].astype(f32) + total).astype(bf16)


def combine(residual, gates, spread, own, returned):
    return pl.pallas_call(
        combine_kernel,
        out_shape=jax.ShapeDtypeStruct(residual.shape, bf16),
        in_specs=[VMEM] * 5,
        out_specs=VMEM,
        compiler_params=PARAMS,
        cost_estimate=cost(0, 1 << 20),
        name="combine",
    )(residual, gates, spread, own, returned)


def bundle_kernel(send, kv, tags, out):
    groups, rows, _ = out.shape
    heads = kv.shape[1] // 128
    capc = send.shape[0] // groups
    packed = jnp.dot(send[...], kv[...], preferred_element_type=f32).astype(bf16)
    tagged = jnp.dot(send[...], tags[...], preferred_element_type=f32)
    one = (lax.broadcasted_iota(jnp.int32, (16, 128), 0) == lax.broadcasted_iota(jnp.int32, (16, 128), 1))
    for owner in range(groups):
        mine = slice(owner * capc, (owner + 1) * capc)
        for head in range(heads):
            out[owner, head * capc : (head + 1) * capc, :] = packed[mine, head * 128 : (head + 1) * 128]
        wide = jnp.concatenate([tagged[mine, :], jnp.zeros((128 - capc, 128), f32)], axis=0)
        out[owner, heads * capc :, :] = lax.dot_general(
            one.astype(f32), wide, LAST_DIMS, preferred_element_type=f32
        ).astype(bf16)


def bundle(groups, send, kv, tags):
    rows = send.shape[0] // groups * (kv.shape[1] // 128) + 16
    return pl.pallas_call(
        bundle_kernel,
        out_shape=jax.ShapeDtypeStruct((groups, rows, 128), bf16),
        in_specs=[VMEM] * 3,
        out_specs=VMEM,
        compiler_params=PARAMS,
        cost_estimate=cost(0, 1 << 20),
        name="bundle",
    )(send, kv, tags)


def write_kernel(arrived, cache, out, rows):
    groups, size, _ = arrived.shape
    slots, heads, _ = cache.shape
    capc = (size - 16) // heads
    high, low = [], []
    for source in range(groups):
        for head in range(heads):
            rows[source * capc : (source + 1) * capc, head * 128 : (head + 1) * 128] = arrived[
                source, head * capc : (head + 1) * capc, :
            ]
        numbers = arrived[source, heads * capc :, :].astype(f32)
        high.append(numbers[0:1, :capc])
        low.append(numbers[1:2, :capc])
    slot = jnp.concatenate(high, axis=1) * 64.0 + jnp.concatenate(low, axis=1) - 64.0
    hit = (lax.broadcasted_iota(jnp.int32, (slots, slot.shape[1]), 0).astype(f32) == slot).astype(f32)
    known = jnp.max(hit, axis=1, keepdims=True) > 0.0
    made = jnp.dot(hit.astype(bf16), rows[...], preferred_element_type=f32)
    for head in range(heads):
        here = made[:, head * 128 : (head + 1) * 128]
        out[:, head, :] = jnp.where(known, here, cache[:, head, :].astype(f32)).astype(bf16)


def write(arrived, cache):
    slots, heads, lanes = cache.shape
    capc = (arrived.shape[1] - 16) // heads
    return pl.pallas_call(
        write_kernel,
        out_shape=jax.ShapeDtypeStruct(cache.shape, bf16),
        in_specs=[VMEM] * 2,
        out_specs=VMEM,
        scratch_shapes=[pltpu.VMEM((arrived.shape[0] * capc, heads * lanes), bf16)],
        compiler_params=PARAMS,
        cost_estimate=cost(0, 1 << 20),
        name="write",
    )(arrived, cache)


def two_lane_shards(
    tokens,
    positions,
    attn_gain,
    w_query,
    w_keyval,
    w_out,
    moe_gain,
    router,
    w_gate_up,
    w_down,
    expert_ids,
    cache_slot,
    kv_cache,
):
    groups = lax.axis_size("grp")
    tok_rows, model = tokens.shape
    block = positions.shape[0]
    kv_local, head2 = w_keyval.shape[1:]
    kv_width = kv_local * head2
    slots_dev = kv_cache.shape[0]
    swap = functools.partial(lax.ppermute, axis_name="hd", perm=[(0, 1), (1, 0)])

    other_tokens = swap(tokens)
    up, down = w_gate_up[0], w_down[0]
    own = (up, down, w_out.T)
    expert_pair, out_pair = pack(
        own, [lax.ppermute(part, "grp", sibling_pairs(groups)) for part in own]
    )
    out_ring = Ring(out_pair, groups)
    out_ring.step()
    expert_ring = Ring(expert_pair, groups)
    expert_ring.step()
    cosine, sine, past, named, place, spread, send, tags = prepare(
        groups, slots_dev, positions, cache_slot, expert_ids, router.shape[1]
    )
    other_tokens = out_ring.pin(other_tokens)
    out_ring.step()
    other_tokens = out_ring.pin(other_tokens)
    out_ring.step()
    q, kv, tail = project(
        tokens,
        other_tokens,
        attn_gain[None],
        cosine,
        sine,
        w_query,
        w_keyval.reshape(model, kv_width),
    )
    seam = lax.ppermute(tail, "grp", [(g, g + 1) for g in range(groups - 1)])
    seam = out_ring.pin(seam)
    out_ring.step()
    out_ring.share()
    seam = expert_ring.pin(seam)
    expert_ring.step()
    mixed = attend(q, kv, seam, past)
    out_parts = out_ring.parts()
    sent = outward(True, bf16, groups, mixed, out_parts, out_ring.unit_rows)
    arrived = swap(sent)
    mine = outward(False, f32, groups, mixed, out_parts, out_ring.unit_rows)
    outgoing = bundle(groups, send, kv, tags)
    mine = expert_ring.pin(mine)
    expert_ring.step()
    mine, arrived = expert_ring.pin(mine, arrived)
    expert_ring.step()
    expert_ring.share()

    residual, gates, own_rows, sent_rows = route(
        tokens, mine, arrived, moe_gain[None], router.T, named, place
    )
    landed = swap(sent_rows)
    outgoing = lax.optimization_barrier((outgoing, sent_rows))[0]
    arrived_cache = lax.all_to_all(outgoing, "grp", split_axis=0, concat_axis=0, tiled=True)
    own_made, back = expert(
        groups, own_rows, landed, expert_ring.parts(), up.shape[0], down.shape[0]
    )
    returned = swap(back)
    layer_out = combine(residual, gates, spread, own_made, returned)
    cache_after = write(arrived_cache, kv_cache)
    return (layer_out, cache_after)


def passed_along(value, axis, steps):
    count = lax.axis_size(axis)
    initial, last = (max(0, -steps), min(count, count - steps))
    return lax.ppermute(value, axis, [(source, source + steps) for source in range(initial, last)])


def rms_norm(row_set, norm_gain):
    floats = row_set.astype(jnp.float32)
    factor = lax.rsqrt(jnp.mean(floats * floats, axis=-1, keepdims=True) + norm_eps)
    return (floats * factor * norm_gain).astype(jnp.bfloat16)


def rotate(vectors, angle_pos):
    halves = vectors.shape[-1] // 2
    inverse_freq = rope_base ** (-2.0 * jnp.arange(halves, dtype=jnp.float32) / vectors.shape[-1])
    angles = angle_pos[:, None, None] * inverse_freq[None, None, :]
    cosine = jnp.cos(angles)
    sine_part = jnp.sin(angles)
    first_half = vectors[..., :halves]
    second_half = vectors[..., halves:]
    return jnp.concatenate(
        [
            first_half * cosine - second_half * sine_part,
            second_half * cosine + first_half * sine_part,
        ],
        axis=-1,
    )


def expert_rows(row_set, gate_up, down_rows):
    gate_and_up = jnp.dot(row_set, gate_up, preferred_element_type=jnp.float32)
    inner_width = gate_and_up.shape[1] // 2
    hidden = (jax.nn.silu(gate_and_up[:, :inner_width]) * gate_and_up[:, inner_width:]).astype(
        jnp.bfloat16
    )
    return jnp.dot(hidden, down_rows, preferred_element_type=jnp.float32).astype(jnp.bfloat16)


def attend_rows(query_blk, keys_blk, vals_blk, visible, scale_qk):
    scores = (
        jnp.einsum("qkgd,skd->kgqs", query_blk, keys_blk, preferred_element_type=jnp.float32)
        * scale_qk
    )
    weights_f = jnp.where(visible[None, None], jnp.exp(scores), 0.0)
    prob_bf = (weights_f / jnp.sum(weights_f, axis=-1, keepdims=True)).astype(jnp.bfloat16)
    return jnp.einsum("kgqs,skd->qkgd", prob_bf, vals_blk, preferred_element_type=jnp.float32)


def shards(
    tokens,
    positions,
    attn_gain,
    w_query,
    w_keyval,
    w_out,
    moe_gain,
    router,
    w_gate_up,
    w_down,
    expert_ids,
    cache_slot,
    kv_cache,
):
    lane_count = lax.axis_size("hd")
    group_count = lax.axis_size("grp")
    tok_rows = tokens.shape[0]
    model_width = tokens.shape[1]
    block_len = positions.shape[0]
    seg_most = block_len // 2
    head_dim = w_keyval.shape[2] // 2
    kv_local = w_keyval.shape[1]
    q_local = w_query.shape[1] // head_dim
    per_kv = q_local // kv_local
    expert_cap = tok_rows // 4
    normed = rms_norm(tokens, attn_gain)
    flat_kv = w_keyval.reshape(model_width, kv_local * 2 * head_dim)
    section = lax.all_gather(normed, "hd", axis=0, tiled=True)
    projected = jnp.concatenate(
        [
            jnp.dot(section, w_query, preferred_element_type=jnp.float32),
            jnp.dot(section, flat_kv, preferred_element_type=jnp.float32),
        ],
        axis=1,
    )
    angle_pos = jnp.maximum(positions, 0).astype(jnp.float32)
    queries = rotate(
        projected[:, : q_local * head_dim].reshape(block_len, q_local, head_dim), angle_pos
    ).astype(jnp.bfloat16)
    key_val = projected[:, q_local * head_dim :].reshape(block_len, kv_local, 2 * head_dim)
    rotated = rotate(key_val[:, :, :head_dim], angle_pos).astype(jnp.bfloat16)
    stored = jnp.concatenate([rotated, key_val[:, :, head_dim:].astype(jnp.bfloat16)], axis=2)
    seam_rows = passed_along(stored[block_len - seg_most :], "grp", 1)
    window = jnp.concatenate([seam_rows, stored], axis=0)
    scale_qk = head_dim ** (-0.5)
    local_rows = jnp.arange(block_len, dtype=jnp.int32)
    lowest = local_rows - jnp.maximum(positions, 0)
    pieces_out = []
    for q_block in range(2):
        first_row = q_block * seg_most
        rows_here = first_row + jnp.arange(seg_most, dtype=jnp.int32)
        cols_here = first_row - seg_most + jnp.arange(2 * seg_most, dtype=jnp.int32)
        low_here = lowest[first_row : first_row + seg_most]
        visible = (cols_here[None, :] >= low_here[:, None]) & (
            cols_here[None, :] <= rows_here[:, None]
        )
        query_blk = queries[first_row : first_row + seg_most].reshape(
            seg_most, kv_local, per_kv, head_dim
        )
        keys_blk = window[first_row : first_row + 2 * seg_most, :, :head_dim]
        vals_blk = window[first_row : first_row + 2 * seg_most, :, head_dim:]
        mixed_rows = attend_rows(query_blk, keys_blk, vals_blk, visible, scale_qk)
        pieces_out.append(mixed_rows.reshape(seg_most, q_local * head_dim).astype(jnp.bfloat16))
    attended = jnp.concatenate(pieces_out, axis=0)
    slots_dev = kv_cache.shape[0]
    capc = 2 * block_len // group_count
    live_slot = cache_slot >= 0
    owners = jnp.where(live_slot, cache_slot // slots_dev, group_count)
    owner_hit = (owners[:, None] == jnp.arange(group_count, dtype=jnp.int32)[None, :]).astype(
        jnp.bfloat16
    )
    lower_tri = (local_rows[:, None] >= local_rows[None, :]).astype(jnp.bfloat16)
    running = jnp.dot(lower_tri, owner_hit, preferred_element_type=jnp.float32)
    owner_rank = jnp.sum(running * owner_hit.astype(jnp.float32), axis=1).astype(jnp.int32) - 1
    send_rows = jnp.where(live_slot, owners * capc + owner_rank, group_count * capc)
    outgoing_cache = (
        jnp.zeros((group_count * capc, kv_local, 2 * head_dim), jnp.bfloat16)
        .at[send_rows]
        .set(stored, mode="drop")
    )
    outgoing_slots = (
        jnp.full((group_count * capc,), -1, jnp.int32)
        .at[send_rows]
        .set(cache_slot % slots_dev, mode="drop")
    )
    arrived, arrived_slots = (
        lax.all_to_all(
            outgoing_cache.reshape(group_count, capc, kv_local, 2 * head_dim),
            "grp",
            split_axis=0,
            concat_axis=0,
            tiled=True,
        ),
        lax.all_to_all(
            outgoing_slots.reshape(group_count, capc),
            "grp",
            split_axis=0,
            concat_axis=0,
            tiled=True,
        ),
    )
    flat_slots = arrived_slots.reshape(group_count * capc)
    write_rows = jnp.where(flat_slots >= 0, flat_slots, slots_dev).astype(jnp.int32)
    cache_after = kv_cache.at[write_rows].set(
        arrived.reshape(group_count * capc, kv_local, 2 * head_dim), mode="drop"
    )
    by_token = lax.all_to_all(attended, "hd", split_axis=0, concat_axis=1, tiled=True)
    attn_proj = jnp.dot(
        by_token,
        lax.all_gather(w_out, "grp", axis=1, tiled=True),
        preferred_element_type=jnp.float32,
    )
    residual = (tokens.astype(jnp.float32) + attn_proj).astype(jnp.bfloat16)
    moe_in = rms_norm(residual, moe_gain)
    logits = jnp.dot(moe_in, router, preferred_element_type=jnp.float32)
    expert_range = jnp.arange(router.shape[1], dtype=jnp.int32)
    matches_all = expert_ids[:, :, None] == expert_range[None, None, :]
    chosen = jnp.sum(jnp.where(matches_all, logits[:, None, :], 0.0), axis=2)
    raised = jnp.exp(chosen)
    gates = raised / jnp.sum(raised, axis=1, keepdims=True)
    live_range = jnp.arange(lane_count, dtype=jnp.int32)
    matches = expert_ids[:, :, None] == live_range[None, None, :]
    member = jnp.any(matches, axis=1)
    weighting = jnp.sum(jnp.where(matches, gates[:, :, None], 0.0), axis=1)
    ranking = jnp.cumsum(member.astype(jnp.int32), axis=0) - 1
    target = jnp.where(member, live_range[None, :] * expert_cap + ranking, -1)
    slot_range = jnp.arange(lane_count * expert_cap, dtype=jnp.int32)
    slot_hits = target[None, :, :] == slot_range[:, None, None]
    placing = jnp.any(slot_hits, axis=2).astype(jnp.bfloat16)
    outgoing = (
        jnp.dot(placing, moe_in, preferred_element_type=jnp.float32)
        .astype(jnp.bfloat16)
        .reshape(lane_count, expert_cap, model_width)
    )
    gate_up_all, down_all = (
        lax.all_gather(w_gate_up, "grp", axis=1, tiled=True),
        lax.all_gather(w_down, "grp", axis=1, tiled=True),
    )
    gate_up_mat = gate_up_all[0]
    down_mat = down_all[0]
    landed = lax.all_to_all(outgoing, "hd", split_axis=0, concat_axis=0, tiled=True)
    results = expert_rows(landed.reshape(-1, model_width), gate_up_mat, down_mat).reshape(landed.shape)
    returned = lax.all_to_all(results, "hd", split_axis=0, concat_axis=0, tiled=True)
    flat_returned = returned.reshape(-1, model_width)
    fetched = flat_returned[jnp.maximum(target, 0)]
    used_weight = jnp.where(member, weighting, 0.0)
    moe_total = jnp.sum(used_weight[:, :, None] * fetched.astype(jnp.float32), axis=1)
    layer_out = (residual.astype(jnp.float32) + moe_total).astype(jnp.bfloat16)
    return (layer_out, cache_after)


def solution(mesh):
    two_lanes = mesh.shape["hd"] == 2 and mesh.shape["grp"] % 8 == 0
    return jax.shard_map(
        two_lane_shards if two_lanes else shards,
        mesh=mesh,
        in_specs=(
            P(("grp", "hd"), None),
            P("grp"),
            P(),
            P(None, "hd"),
            P(None, "hd", None),
            P(None, "grp"),
            P(),
            P(),
            P("hd", "grp", None),
            P("hd", "grp", None),
            P(("grp", "hd"), None),
            P("grp"),
            P("grp", "hd", None),
        ),
        out_specs=(P(("grp", "hd"), None), P("grp", "hd", None)),
        check_vma=False,
    )
```

```python
import functools

import jax
import jax.numpy as jnp
import numpy as np
from jax import lax
from jax.experimental import pallas as pl
from jax.experimental.pallas import tpu as pltpu
from jax.sharding import PartitionSpec as P

norm_eps = 1e-05
rope_base = 10000.0
bf16 = jnp.bfloat16
f32 = jnp.float32
LAST_DIMS = (((1,), (1,)), ((), ()))


def ring_cycle(groups):
    rows = groups // 4
    return [2 * r for r in range(rows)] + [2 * r + 1 for r in reversed(range(rows))]


def ring_pairs(groups):
    cycle = ring_cycle(groups)
    count = len(cycle)
    pairs = []
    for place, pair in enumerate(cycle):
        pairs.append((2 * pair, 2 * cycle[(place + 1) % count]))
        pairs.append((2 * pair + 1, 2 * cycle[(place - 1) % count] + 1))
    return pairs


def sibling_pairs(groups):
    return [(g, g ^ 1) for g in range(groups)]


def ring_sources(groups, me):
    count = groups // 2
    rows = count // 2
    side, pair = me % 2, me // 2
    row, col = pair // 2, pair % 2
    place = jnp.where(col == 0, row, count - 1 - row)

    def block(core, steps):
        there = (place + (2 * core - 1) * steps + count) % count
        other = jnp.where(there < rows, 2 * there, 2 * (count - 1 - there) + 1)
        return [2 * other + core, 2 * other + 1 - core]

    full = (count - 1) // 2
    listed = [me, me + 1 - 2 * side]
    for core in (side, 1 - side):
        for steps in range(1, full + 1):
            listed += block(core, steps)
    return listed + [block(side, count // 2)[0], block(1 - side, count // 2)[0]]


class Ring:
    def __init__(self, pair, groups):
        self.across = functools.partial(lax.ppermute, axis_name="grp", perm=ring_pairs(groups))
        self.beside = functools.partial(lax.ppermute, axis_name="grp", perm=sibling_pairs(groups))
        self.full = (groups // 2 - 1) // 2
        self.unit_rows = pair.shape[0] // 2
        self.mine = [pair]
        self.near = []

    def step(self):
        held = self.mine[-1]
        if len(self.mine) > self.full:
            held = held[: self.unit_rows]
        self.mine.append(self.across(held))

    def pin(self, *others):
        done = lax.optimization_barrier((self.mine[-1],) + others)
        self.mine[-1] = done[0]
        return done[1:] if len(others) > 1 else done[1]

    def share(self):
        for index in range(1 + len(self.near), len(self.mine)):
            self.near.append(self.beside(self.mine[index]))

    def parts(self):
        full = self.full
        return self.mine[: full + 1] + self.near[:full] + [self.mine[full + 1], self.near[full]]


def place_parts(groups, parts, unit_rows, pieces):
    sources = ring_sources(groups, lax.axis_index("grp"))
    shard = 0
    for part in parts:
        for unit in range(part.shape[0] // unit_rows):
            for first, rows, target, lane in pieces:
                at = pl.multiple_of(sources[shard] * rows, rows)
                start = unit * unit_rows + first
                target[pl.ds(at, rows), lane : lane + part.shape[1]] = part[start : start + rows, :]
            shard += 1


VMEM = pl.BlockSpec(memory_space=pltpu.VMEM)
ANY = pl.BlockSpec(memory_space=pl.ANY)
HBM = pl.BlockSpec(memory_space=pltpu.HBM)
PARAMS = pltpu.CompilerParams(vmem_limit_bytes=40 << 20)


LITTLE = pl.CostEstimate(flops=1, bytes_accessed=1, transcendentals=0)


def normalized(floats, gain):
    factor = lax.rsqrt(jnp.mean(floats * floats, axis=-1, keepdims=True) + norm_eps)
    return (floats * factor * gain).astype(bf16)


def fetch(pairs, sems):
    copies = []
    for index, (source, target) in enumerate(pairs):
        copies.append(pltpu.make_async_copy(source, target, sems.at[index]))
        copies[-1].start()
    return copies


def pack_kernel(*refs):
    sources, (expert_pair, out_pair, sems) = refs[:6], refs[6:]
    width = expert_pair.shape[1]
    lane = lax.axis_index("hd")
    first = pl.multiple_of(lane * out_pair.shape[1], out_pair.shape[1])
    pairs = []
    row = 0
    for index in range(2):
        up, down, w_out = sources[3 * index : 3 * index + 3]
        count = w_out.shape[0]
        pairs.append(
            (w_out.at[:, pl.ds(first, out_pair.shape[1])], out_pair.at[pl.ds(index * count, count), :])
        )
        for source in (up, down):
            for at in range(0, source.shape[1], width):
                pairs.append(
                    (source.at[:, pl.ds(at, width)], expert_pair.at[pl.ds(row, source.shape[0]), :])
                )
                row += source.shape[0]
    for copy in fetch(pairs, sems):
        copy.wait()


def pack(own, beside):
    own = [pltpu.with_memory_space_constraint(part, pltpu.HBM) for part in own]
    up, down, w_out_t = own
    width = up.shape[1] // 2
    pieces = [up.shape[1] // width, down.shape[1] // width]
    unit_rows = pieces[0] * up.shape[0] + pieces[1] * down.shape[0]
    return pl.pallas_call(
        pack_kernel,
        out_shape=(
            jax.ShapeDtypeStruct((2 * unit_rows, width), bf16),
            jax.ShapeDtypeStruct((2 * w_out_t.shape[0], w_out_t.shape[1] // 2), bf16),
        ),
        in_specs=[ANY] * 6,
        out_specs=(ANY, ANY),
        scratch_shapes=[pltpu.SemaphoreType.DMA((2 + 2 * sum(pieces),))],
        compiler_params=PARAMS,
        cost_estimate=LITTLE,
        name="pack",
    )(*own, *beside)


def as_column(row, eye):
    return jnp.sum(jnp.where(eye, row, 0.0), axis=1, keepdims=True)


def prepare_kernel(
    groups, slots_dev, positions, slots, ids, cosine, sine, past, named, place, spread, send, tags
):
    lane = lax.axis_index("hd")
    block = positions.shape[1]

    def iota(shape, dim):
        return lax.broadcasted_iota(jnp.int32, shape, dim)

    eye = iota((block, block), 0) == iota((block, block), 1)
    reach = as_column(jnp.maximum(positions[...], 0).astype(f32), eye)
    past[...] = jnp.broadcast_to(reach, past.shape)
    column = iota((8, 128), 1)
    exponent = (column % 32).astype(f32) * (-2.0 / 64)
    inverse_freq = jnp.exp(exponent * np.float32(np.log(rope_base)))[:1, :]
    angles = reach * inverse_freq
    cosine[...] = jnp.cos(angles)
    turned = jnp.sin(angles)
    sine[...] = jnp.where(iota(angles.shape, 1) % 64 < 32, -turned, turned)

    tokens = ids.shape[1]
    experts = named.shape[1]
    cap = place.shape[0] // 2
    expert = iota((experts, tokens), 0)
    hit = jnp.zeros((experts, tokens), f32)
    for index in range(ids.shape[0]):
        hit = jnp.where(ids[index : index + 1, :] == expert, 1.0, hit)
    small_eye = (iota((tokens, tokens), 0) == iota((tokens, tokens), 1)).astype(f32)
    named[...] = lax.dot_general(small_eye, hit, LAST_DIMS, preferred_element_type=f32)
    upto = (iota((tokens, tokens), 0) <= iota((tokens, tokens), 1)).astype(f32)
    rank = jnp.dot(hit[:8, :], upto, preferred_element_type=f32) - 1.0
    slot = iota((2 * cap, tokens), 0).astype(f32)
    placed = jnp.zeros((2 * cap, tokens), f32)
    for live in range(2):
        order = jnp.where(lane == live, 0, cap).astype(f32)
        member = hit[live : live + 1, :] > 0.0
        placed = jnp.where(member & (slot == rank[live : live + 1, :] + order), 1.0, placed)
    place[...] = placed.astype(bf16)
    spread[...] = lax.dot_general(small_eye, placed, LAST_DIMS, preferred_element_type=f32).astype(bf16)

    where = slots[...]
    owner = jnp.where(where >= 0, where // slots_dev, -1)
    owner_hit = (iota((groups, block), 0) == owner).astype(f32)
    before = (iota((block, block), 0) <= iota((block, block), 1)).astype(f32)
    running = jnp.dot(owner_hit, before, preferred_element_type=f32)
    owner_rank = jnp.sum(owner_hit * running, axis=0, keepdims=True) - 1.0
    capc = send.shape[0] // groups
    row = jnp.where(owner >= 0, owner * capc + owner_rank.astype(jnp.int32), -1)
    send[...] = (iota(send.shape, 0) == row).astype(bf16)
    inside = jnp.where(where >= 0, where % slots_dev, 0)
    high = as_column((inside // 64 + 1).astype(f32), eye)
    low = as_column((inside % 64).astype(f32), eye)
    spot = iota(tags.shape, 1)
    tags[...] = jnp.where(spot == 0, high, jnp.where(spot == 1, low, 0.0)).astype(bf16)


def prepare(groups, slots_dev, positions, slots, ids, experts):
    block, tokens = positions.shape[0], ids.shape[0]
    cap = tokens // 4
    capc = 2 * block // groups
    shapes = [
        ((block, 128), f32),
        ((block, 128), f32),
        ((block, 128), f32),
        ((tokens, experts), f32),
        ((2 * cap, tokens), bf16),
        ((tokens, 2 * cap), bf16),
        ((groups * capc, block), bf16),
        ((block, 128), bf16),
    ]
    return pl.pallas_call(
        functools.partial(prepare_kernel, groups, slots_dev),
        out_shape=tuple(jax.ShapeDtypeStruct(shape, kind) for shape, kind in shapes),
        in_specs=[VMEM] * 3,
        out_specs=(VMEM,) * len(shapes),
        compiler_params=PARAMS,
        cost_estimate=LITTLE,
        name="prepare",
    )(positions[None], slots[None], ids.T)


def project_kernel(
    own, other, gain, cosine, sine, w_query, w_keyval, q_out, kv_out, seam_out, raw, rows, sems
):
    count = own.shape[0]
    lane = lax.axis_index("hd")
    mine = pl.multiple_of(lane * count, count)
    theirs = pl.multiple_of((1 - lane) * count, count)
    copies = fetch([(own, raw.at[0]), (other, raw.at[1])], sems)
    cos_q, sin_q = cosine[...], sine[...]
    column = lax.broadcasted_iota(jnp.int32, cos_q.shape, 1)
    lower = column % 64 < 32
    cos_kv = jnp.where(column < 64, cos_q, 1.0)
    sin_kv = jnp.where(column < 64, sin_q, 0.0)
    for index, first in ((0, mine), (1, theirs)):
        copies[index].wait()
        rows[pl.ds(first, count), :] = normalized(raw[index].astype(f32), gain[...])
    width = 256
    for weights, out, cos, sin in ((w_keyval, kv_out, cos_kv, sin_kv), (w_query, q_out, cos_q, sin_q)):
        for first in range(0, weights.shape[1], width):
            made = jnp.dot(rows[...], weights[:, first : first + width], preferred_element_type=f32)
            for part in range(0, width, 128):
                here = made[:, part : part + 128]
                turned = jnp.where(lower, pltpu.roll(here, 96, 1), pltpu.roll(here, 32, 1))
                done = (here * cos + turned * sin).astype(bf16)
                out[:, first + part : first + part + 128] = done
                if out is kv_out:
                    seam_out[:, first + part : first + part + 128] = done[count:, :]


def project(own, other, gain, cosine, sine, w_query, flat_kv):
    count, width = own.shape
    made = w_query.shape[1] + flat_kv.shape[1]
    return pl.pallas_call(
        project_kernel,
        out_shape=(
            jax.ShapeDtypeStruct((2 * count, w_query.shape[1]), bf16),
            jax.ShapeDtypeStruct((2 * count, flat_kv.shape[1]), bf16),
            jax.ShapeDtypeStruct((count, flat_kv.shape[1]), bf16),
        ),
        in_specs=[ANY] * 2 + [VMEM] * 5,
        out_specs=(VMEM, VMEM, VMEM),
        scratch_shapes=[
            pltpu.VMEM((2, count, width), bf16),
            pltpu.VMEM((2 * count, width), bf16),
            pltpu.SemaphoreType.DMA((2,)),
        ],
        compiler_params=PARAMS,
        cost_estimate=LITTLE,
        name="project",
    )(own, other, gain, cosine, sine, w_query, flat_kv)


def attend_kernel(q, kv, seam, past, mixed, window, sem):
    count = seam.shape[0]
    copy = pltpu.make_async_copy(seam, window.at[pl.ds(0, count), :], sem)
    copy.start()
    window[count:, :] = kv[...]
    head = 64
    kv_heads = kv.shape[1] // (2 * head)
    per_kv = q.shape[1] // head // kv_heads
    shape = (count, 2 * count)
    row = lax.broadcasted_iota(jnp.int32, shape, 0) + count
    col = lax.broadcasted_iota(jnp.int32, shape, 1)
    for half in (1, 0):
        first = half * count
        if half == 0:
            copy.wait()
        reach = past[first : first + count, :1].astype(jnp.int32)
        visible = (col <= row) & (col >= row - reach)
        for kv_head in range(kv_heads):
            lanes = 2 * head * kv_head
            keys = window[first : first + 2 * count, lanes : lanes + head]
            values = window[first : first + 2 * count, lanes + head : lanes + 2 * head]
            for index in range(per_kv):
                at = (kv_head * per_kv + index) * head
                query = q[first : first + count, at : at + head]
                scores = lax.dot_general(query, keys, LAST_DIMS, preferred_element_type=f32)
                raised = jnp.where(visible, jnp.exp(scores * head ** (-0.5)), 0.0)
                probs = (raised / jnp.sum(raised, axis=-1, keepdims=True)).astype(bf16)
                made = jnp.dot(probs, values, preferred_element_type=f32)
                mixed[first : first + count, at : at + head] = made.astype(bf16)


def attend(q, kv, seam, past):
    count = seam.shape[0]
    return pl.pallas_call(
        attend_kernel,
        out_shape=jax.ShapeDtypeStruct(q.shape, bf16),
        in_specs=[VMEM, VMEM, ANY, VMEM],
        out_specs=VMEM,
        scratch_shapes=[
            pltpu.VMEM((3 * count, kv.shape[1]), bf16),
            pltpu.SemaphoreType.DMA,
        ],
        compiler_params=PARAMS,
        cost_estimate=LITTLE,
        name="attend",
    )(q, kv, seam, past)


def outward_kernel(flip, groups, unit_rows, n_parts, mixed, *refs):
    parts, (out, w_out) = refs[:n_parts], refs[n_parts:]
    place_parts(groups, parts, unit_rows, [(0, unit_rows, w_out, 0)])
    count = out.shape[0]
    lane = lax.axis_index("hd")
    first = pl.multiple_of(((1 - lane) if flip else lane) * count, count)
    out[...] = lax.dot_general(
        mixed[pl.ds(first, count), :], w_out[...], LAST_DIMS, preferred_element_type=f32
    ).astype(out.dtype)


def outward(flip, out_type, groups, mixed, parts, unit_rows):
    count = mixed.shape[0] // 2
    width = groups * unit_rows
    depth = parts[0].shape[1]
    return pl.pallas_call(
        functools.partial(outward_kernel, flip, groups, unit_rows, len(parts)),
        out_shape=jax.ShapeDtypeStruct((count, width), out_type),
        in_specs=[VMEM] * (1 + len(parts)),
        out_specs=VMEM,
        scratch_shapes=[pltpu.VMEM((width, depth), bf16)],
        compiler_params=PARAMS,
        cost_estimate=LITTLE,
        name="outward_send" if flip else "outward_keep",
    )(mixed, *parts)


def route_kernel(tokens, mine, arrived, gain, place, residual, moe_in, sent):
    added = (tokens[...].astype(f32) + (mine[...] + arrived[...].astype(f32))).astype(bf16)
    residual[...] = added
    moe_in[...] = normalized(added.astype(f32), gain[...])
    cap = sent.shape[0]
    rows = jnp.dot(place[cap:, :], moe_in[...], preferred_element_type=f32)
    sent[...] = rows.astype(bf16)


def route(tokens, mine, arrived, gain, place):
    cap = place.shape[0] // 2
    return pl.pallas_call(
        route_kernel,
        out_shape=(
            jax.ShapeDtypeStruct(tokens.shape, bf16),
            jax.ShapeDtypeStruct(tokens.shape, bf16),
            jax.ShapeDtypeStruct((cap, tokens.shape[1]), bf16),
        ),
        in_specs=[VMEM] * 5,
        out_specs=(VMEM,) * 3,
        compiler_params=PARAMS,
        cost_estimate=LITTLE,
        name="route",
    )(tokens, mine, arrived, gain, place)


def gate_kernel(moe_in, router, named, place, gates, own):
    cap = own.shape[0]
    own[...] = jnp.dot(place[:cap, :], moe_in[...], preferred_element_type=f32).astype(bf16)
    logits = lax.dot_general(moe_in[...], router[...], LAST_DIMS, preferred_element_type=f32)
    raised = jnp.where(named[...] > 0, jnp.exp(logits), 0.0)
    gates[...] = raised / jnp.sum(raised, axis=-1, keepdims=True)


def gate(moe_in, router_t, named, place):
    cap = place.shape[0] // 2
    return pl.pallas_call(
        gate_kernel,
        out_shape=(
            jax.ShapeDtypeStruct(named.shape, f32),
            jax.ShapeDtypeStruct((cap, moe_in.shape[1]), bf16),
        ),
        in_specs=[VMEM] * 4,
        out_specs=(VMEM,) * 2,
        compiler_params=PARAMS,
        cost_estimate=LITTLE,
        name="gate",
    )(moe_in, router_t, named, place)


def expert_kernel(groups, up_rows, down_rows, n_parts, own, other, *refs):
    parts = refs[:n_parts]
    own_out, other_out, rows, gate_up, down = refs[n_parts:]
    width = parts[0].shape[1]
    count = own.shape[0]
    rows[:count, :] = own[...]
    rows[count:, :] = other[...]
    pieces = [(i * up_rows, up_rows, gate_up, i * width) for i in range(2)]
    pieces += [
        (2 * up_rows + i * down_rows, down_rows, down, i * width) for i in range(down.shape[1] // width)
    ]
    unit_rows = pieces[-1][0] + down_rows
    place_parts(groups, parts, unit_rows, pieces)
    both = jnp.dot(rows[...], gate_up[...], preferred_element_type=f32)
    gate, up = both[:, :width], both[:, width:]
    hidden = (gate / (1.0 + jnp.exp(-gate)) * up).astype(bf16)
    made = jnp.dot(hidden, down[...], preferred_element_type=f32).astype(bf16)
    own_out[...] = made[:count, :]
    other_out[...] = made[count:, :]


def expert(groups, own, other, parts, up_rows, down_rows):
    count, model = own.shape
    width = parts[0].shape[1]
    return pl.pallas_call(
        functools.partial(expert_kernel, groups, up_rows, down_rows, len(parts)),
        out_shape=(jax.ShapeDtypeStruct(own.shape, bf16),) * 2,
        in_specs=[VMEM] * (2 + len(parts)),
        out_specs=(VMEM, VMEM),
        scratch_shapes=[
            pltpu.VMEM((2 * count, model), bf16),
            pltpu.VMEM((groups * up_rows, 2 * width), bf16),
            pltpu.VMEM((groups * down_rows, model), bf16),
        ],
        compiler_params=PARAMS,
        cost_estimate=LITTLE,
        name="expert",
    )(own, other, *parts)


def combine_kernel(residual, gates, spread, own, returned, out):
    lane = lax.axis_index("hd")
    count = own.shape[0]
    column = lax.broadcasted_iota(jnp.int32, gates.shape, 1)
    total = jnp.zeros(residual.shape, f32)
    for index, made in ((0, own), (1, returned)):
        live = lane if index == 0 else 1 - lane
        weight = jnp.sum(jnp.where(column == live, gates[...], 0.0), axis=-1, keepdims=True)
        picked = jnp.dot(
            spread[:, index * count : (index + 1) * count], made[...], preferred_element_type=f32
        )
        total += weight * picked
    out[...] = (residual[...].astype(f32) + total).astype(bf16)


def combine(residual, gates, spread, own, returned):
    return pl.pallas_call(
        combine_kernel,
        out_shape=jax.ShapeDtypeStruct(residual.shape, bf16),
        in_specs=[VMEM] * 5,
        out_specs=VMEM,
        compiler_params=PARAMS,
        cost_estimate=LITTLE,
        name="combine",
    )(residual, gates, spread, own, returned)


def bundle_kernel(send, kv, tags, out):
    groups, rows, _ = out.shape
    heads = kv.shape[1] // 128
    capc = send.shape[0] // groups
    packed = jnp.dot(send[...], kv[...], preferred_element_type=f32).astype(bf16)
    tagged = jnp.dot(send[...], tags[...], preferred_element_type=f32)
    one = (lax.broadcasted_iota(jnp.int32, (16, 128), 0) == lax.broadcasted_iota(jnp.int32, (16, 128), 1))
    for owner in range(groups):
        mine = slice(owner * capc, (owner + 1) * capc)
        for head in range(heads):
            out[owner, head * capc : (head + 1) * capc, :] = packed[mine, head * 128 : (head + 1) * 128]
        wide = jnp.concatenate([tagged[mine, :], jnp.zeros((128 - capc, 128), f32)], axis=0)
        out[owner, heads * capc :, :] = lax.dot_general(
            one.astype(f32), wide, LAST_DIMS, preferred_element_type=f32
        ).astype(bf16)


def bundle(groups, send, kv, tags):
    rows = send.shape[0] // groups * (kv.shape[1] // 128) + 16
    return pl.pallas_call(
        bundle_kernel,
        out_shape=jax.ShapeDtypeStruct((groups, rows, 128), bf16),
        in_specs=[VMEM] * 3,
        out_specs=VMEM,
        compiler_params=PARAMS,
        cost_estimate=LITTLE,
        name="bundle",
    )(send, kv, tags)


def write_kernel(arrived, cache, out, rows):
    groups, size, _ = arrived.shape
    slots, heads, _ = cache.shape
    capc = (size - 16) // heads
    high, low = [], []
    for source in range(groups):
        for head in range(heads):
            rows[source * capc : (source + 1) * capc, head * 128 : (head + 1) * 128] = arrived[
                source, head * capc : (head + 1) * capc, :
            ]
        numbers = arrived[source, heads * capc :, :].astype(f32)
        high.append(numbers[0:1, :capc])
        low.append(numbers[1:2, :capc])
    slot = jnp.concatenate(high, axis=1) * 64.0 + jnp.concatenate(low, axis=1) - 64.0
    hit = (lax.broadcasted_iota(jnp.int32, (slots, slot.shape[1]), 0).astype(f32) == slot).astype(f32)
    known = jnp.max(hit, axis=1, keepdims=True) > 0.0
    made = jnp.dot(hit.astype(bf16), rows[...], preferred_element_type=f32)
    for head in range(heads):
        here = made[:, head * 128 : (head + 1) * 128]
        out[:, head, :] = jnp.where(known, here, cache[:, head, :].astype(f32)).astype(bf16)


def write(arrived, cache):
    slots, heads, lanes = cache.shape
    capc = (arrived.shape[1] - 16) // heads
    return pl.pallas_call(
        write_kernel,
        out_shape=jax.ShapeDtypeStruct(cache.shape, bf16),
        in_specs=[VMEM] * 2,
        out_specs=VMEM,
        scratch_shapes=[pltpu.VMEM((arrived.shape[0] * capc, heads * lanes), bf16)],
        compiler_params=PARAMS,
        cost_estimate=LITTLE,
        name="write",
    )(arrived, cache)


def two_lane_shards(
    tokens,
    positions,
    attn_gain,
    w_query,
    w_keyval,
    w_out,
    moe_gain,
    router,
    w_gate_up,
    w_down,
    expert_ids,
    cache_slot,
    kv_cache,
):
    groups = lax.axis_size("grp")
    tok_rows, model = tokens.shape
    block = positions.shape[0]
    kv_local, head2 = w_keyval.shape[1:]
    kv_width = kv_local * head2
    slots_dev = kv_cache.shape[0]
    swap = functools.partial(lax.ppermute, axis_name="hd", perm=[(0, 1), (1, 0)])

    together = lax.optimization_barrier

    other_tokens = swap(tokens)
    own = (w_gate_up[0], w_down[0], w_out.T)
    up_rows, down_rows = own[0].shape[0], own[1].shape[0]
    beside = [lax.ppermute(part, "grp", sibling_pairs(groups)) for part in own]
    flat_kv = w_keyval.reshape(model, kv_width)
    cosine, sine, past, named, place, spread, send, tags = prepare(
        groups, slots_dev, positions, cache_slot, expert_ids, router.shape[1]
    )
    beside, cosine, flat_kv = together((beside, cosine, flat_kv))
    expert_pair, out_pair = pack(own, beside)
    out_ring = Ring(out_pair, groups)
    out_ring.step()
    expert_ring = Ring(expert_pair, groups)
    expert_ring.step()
    other_tokens = out_ring.pin(other_tokens)
    out_ring.step()

    q, kv, tail = project(
        tokens, other_tokens, attn_gain[None], cosine, sine, w_query, flat_kv
    )
    seam = lax.ppermute(tail, "grp", [(g, g + 1) for g in range(groups - 1)])
    outgoing = bundle(groups, send, kv, tags)
    outgoing = out_ring.pin(outgoing)
    out_ring.step()
    seam, q = together((seam, q, outgoing))[:2]
    seam = expert_ring.pin(seam)
    expert_ring.step()
    seam = out_ring.pin(seam)
    out_ring.step()
    mixed = attend(q, kv, seam, past)
    mixed = out_ring.pin(mixed)
    out_ring.mine[-1] = expert_ring.pin(out_ring.mine[-1])
    out_ring.share()
    expert_ring.step()
    sent = outward(True, bf16, groups, mixed, out_ring.parts(), out_ring.unit_rows)
    arrived = swap(sent)
    mixed = together((mixed, sent))[0]
    mine = outward(False, f32, groups, mixed, out_ring.parts(), out_ring.unit_rows)
    gain, router_t = together((moe_gain[None], router.T, mine))[:2]
    mine = expert_ring.pin(mine)
    expert_ring.share()
    expert_ring.step()

    residual, moe_in, sent_rows = route(tokens, mine, arrived, gain, place)
    landed = swap(sent_rows)
    gates, own_rows = gate(moe_in, router_t, named, place)
    outgoing = together((outgoing, own_rows))[0]
    landed = expert_ring.pin(landed)
    expert_ring.share()
    arrived_cache = lax.all_to_all(outgoing, "grp", split_axis=0, concat_axis=0, tiled=True)
    own_made, back = expert(
        groups, own_rows, landed, expert_ring.parts(), up_rows, down_rows
    )
    returned = swap(back)
    cache_after = write(arrived_cache, kv_cache)
    layer_out = combine(residual, gates, spread, own_made, returned)
    return (layer_out, cache_after)


def passed_along(value, axis, steps):
    count = lax.axis_size(axis)
    initial, last = (max(0, -steps), min(count, count - steps))
    return lax.ppermute(value, axis, [(source, source + steps) for source in range(initial, last)])


def rms_norm(row_set, norm_gain):
    floats = row_set.astype(jnp.float32)
    factor = lax.rsqrt(jnp.mean(floats * floats, axis=-1, keepdims=True) + norm_eps)
    return (floats * factor * norm_gain).astype(jnp.bfloat16)


def rotate(vectors, angle_pos):
    halves = vectors.shape[-1] // 2
    inverse_freq = rope_base ** (-2.0 * jnp.arange(halves, dtype=jnp.float32) / vectors.shape[-1])
    angles = angle_pos[:, None, None] * inverse_freq[None, None, :]
    cosine = jnp.cos(angles)
    sine_part = jnp.sin(angles)
    first_half = vectors[..., :halves]
    second_half = vectors[..., halves:]
    return jnp.concatenate(
        [
            first_half * cosine - second_half * sine_part,
            second_half * cosine + first_half * sine_part,
        ],
        axis=-1,
    )


def expert_rows(row_set, gate_up, down_rows):
    gate_and_up = jnp.dot(row_set, gate_up, preferred_element_type=jnp.float32)
    inner_width = gate_and_up.shape[1] // 2
    hidden = (jax.nn.silu(gate_and_up[:, :inner_width]) * gate_and_up[:, inner_width:]).astype(
        jnp.bfloat16
    )
    return jnp.dot(hidden, down_rows, preferred_element_type=jnp.float32).astype(jnp.bfloat16)


def attend_rows(query_blk, keys_blk, vals_blk, visible, scale_qk):
    scores = (
        jnp.einsum("qkgd,skd->kgqs", query_blk, keys_blk, preferred_element_type=jnp.float32)
        * scale_qk
    )
    weights_f = jnp.where(visible[None, None], jnp.exp(scores), 0.0)
    prob_bf = (weights_f / jnp.sum(weights_f, axis=-1, keepdims=True)).astype(jnp.bfloat16)
    return jnp.einsum("kgqs,skd->qkgd", prob_bf, vals_blk, preferred_element_type=jnp.float32)


def shards(
    tokens,
    positions,
    attn_gain,
    w_query,
    w_keyval,
    w_out,
    moe_gain,
    router,
    w_gate_up,
    w_down,
    expert_ids,
    cache_slot,
    kv_cache,
):
    lane_count = lax.axis_size("hd")
    group_count = lax.axis_size("grp")
    tok_rows = tokens.shape[0]
    model_width = tokens.shape[1]
    block_len = positions.shape[0]
    seg_most = block_len // 2
    head_dim = w_keyval.shape[2] // 2
    kv_local = w_keyval.shape[1]
    q_local = w_query.shape[1] // head_dim
    per_kv = q_local // kv_local
    expert_cap = tok_rows // 4
    normed = rms_norm(tokens, attn_gain)
    flat_kv = w_keyval.reshape(model_width, kv_local * 2 * head_dim)
    section = lax.all_gather(normed, "hd", axis=0, tiled=True)
    projected = jnp.concatenate(
        [
            jnp.dot(section, w_query, preferred_element_type=jnp.float32),
            jnp.dot(section, flat_kv, preferred_element_type=jnp.float32),
        ],
        axis=1,
    )
    angle_pos = jnp.maximum(positions, 0).astype(jnp.float32)
    queries = rotate(
        projected[:, : q_local * head_dim].reshape(block_len, q_local, head_dim), angle_pos
    ).astype(jnp.bfloat16)
    key_val = projected[:, q_local * head_dim :].reshape(block_len, kv_local, 2 * head_dim)
    rotated = rotate(key_val[:, :, :head_dim], angle_pos).astype(jnp.bfloat16)
    stored = jnp.concatenate([rotated, key_val[:, :, head_dim:].astype(jnp.bfloat16)], axis=2)
    seam_rows = passed_along(stored[block_len - seg_most :], "grp", 1)
    window = jnp.concatenate([seam_rows, stored], axis=0)
    scale_qk = head_dim ** (-0.5)
    local_rows = jnp.arange(block_len, dtype=jnp.int32)
    lowest = local_rows - jnp.maximum(positions, 0)
    pieces_out = []
    for q_block in range(2):
        first_row = q_block * seg_most
        rows_here = first_row + jnp.arange(seg_most, dtype=jnp.int32)
        cols_here = first_row - seg_most + jnp.arange(2 * seg_most, dtype=jnp.int32)
        low_here = lowest[first_row : first_row + seg_most]
        visible = (cols_here[None, :] >= low_here[:, None]) & (
            cols_here[None, :] <= rows_here[:, None]
        )
        query_blk = queries[first_row : first_row + seg_most].reshape(
            seg_most, kv_local, per_kv, head_dim
        )
        keys_blk = window[first_row : first_row + 2 * seg_most, :, :head_dim]
        vals_blk = window[first_row : first_row + 2 * seg_most, :, head_dim:]
        mixed_rows = attend_rows(query_blk, keys_blk, vals_blk, visible, scale_qk)
        pieces_out.append(mixed_rows.reshape(seg_most, q_local * head_dim).astype(jnp.bfloat16))
    attended = jnp.concatenate(pieces_out, axis=0)
    slots_dev = kv_cache.shape[0]
    capc = 2 * block_len // group_count
    live_slot = cache_slot >= 0
    owners = jnp.where(live_slot, cache_slot // slots_dev, group_count)
    owner_hit = (owners[:, None] == jnp.arange(group_count, dtype=jnp.int32)[None, :]).astype(
        jnp.bfloat16
    )
    lower_tri = (local_rows[:, None] >= local_rows[None, :]).astype(jnp.bfloat16)
    running = jnp.dot(lower_tri, owner_hit, preferred_element_type=jnp.float32)
    owner_rank = jnp.sum(running * owner_hit.astype(jnp.float32), axis=1).astype(jnp.int32) - 1
    send_rows = jnp.where(live_slot, owners * capc + owner_rank, group_count * capc)
    outgoing_cache = (
        jnp.zeros((group_count * capc, kv_local, 2 * head_dim), jnp.bfloat16)
        .at[send_rows]
        .set(stored, mode="drop")
    )
    outgoing_slots = (
        jnp.full((group_count * capc,), -1, jnp.int32)
        .at[send_rows]
        .set(cache_slot % slots_dev, mode="drop")
    )
    arrived, arrived_slots = (
        lax.all_to_all(
            outgoing_cache.reshape(group_count, capc, kv_local, 2 * head_dim),
            "grp",
            split_axis=0,
            concat_axis=0,
            tiled=True,
        ),
        lax.all_to_all(
            outgoing_slots.reshape(group_count, capc),
            "grp",
            split_axis=0,
            concat_axis=0,
            tiled=True,
        ),
    )
    flat_slots = arrived_slots.reshape(group_count * capc)
    write_rows = jnp.where(flat_slots >= 0, flat_slots, slots_dev).astype(jnp.int32)
    cache_after = kv_cache.at[write_rows].set(
        arrived.reshape(group_count * capc, kv_local, 2 * head_dim), mode="drop"
    )
    by_token = lax.all_to_all(attended, "hd", split_axis=0, concat_axis=1, tiled=True)
    attn_proj = jnp.dot(
        by_token,
        lax.all_gather(w_out, "grp", axis=1, tiled=True),
        preferred_element_type=jnp.float32,
    )
    residual = (tokens.astype(jnp.float32) + attn_proj).astype(jnp.bfloat16)
    moe_in = rms_norm(residual, moe_gain)
    logits = jnp.dot(moe_in, router, preferred_element_type=jnp.float32)
    expert_range = jnp.arange(router.shape[1], dtype=jnp.int32)
    matches_all = expert_ids[:, :, None] == expert_range[None, None, :]
    chosen = jnp.sum(jnp.where(matches_all, logits[:, None, :], 0.0), axis=2)
    raised = jnp.exp(chosen)
    gates = raised / jnp.sum(raised, axis=1, keepdims=True)
    live_range = jnp.arange(lane_count, dtype=jnp.int32)
    matches = expert_ids[:, :, None] == live_range[None, None, :]
    member = jnp.any(matches, axis=1)
    weighting = jnp.sum(jnp.where(matches, gates[:, :, None], 0.0), axis=1)
    ranking = jnp.cumsum(member.astype(jnp.int32), axis=0) - 1
    target = jnp.where(member, live_range[None, :] * expert_cap + ranking, -1)
    slot_range = jnp.arange(lane_count * expert_cap, dtype=jnp.int32)
    slot_hits = target[None, :, :] == slot_range[:, None, None]
    placing = jnp.any(slot_hits, axis=2).astype(jnp.bfloat16)
    outgoing = (
        jnp.dot(placing, moe_in, preferred_element_type=jnp.float32)
        .astype(jnp.bfloat16)
        .reshape(lane_count, expert_cap, model_width)
    )
    gate_up_all, down_all = (
        lax.all_gather(w_gate_up, "grp", axis=1, tiled=True),
        lax.all_gather(w_down, "grp", axis=1, tiled=True),
    )
    gate_up_mat = gate_up_all[0]
    down_mat = down_all[0]
    landed = lax.all_to_all(outgoing, "hd", split_axis=0, concat_axis=0, tiled=True)
    results = expert_rows(landed.reshape(-1, model_width), gate_up_mat, down_mat).reshape(landed.shape)
    returned = lax.all_to_all(results, "hd", split_axis=0, concat_axis=0, tiled=True)
    flat_returned = returned.reshape(-1, model_width)
    fetched = flat_returned[jnp.maximum(target, 0)]
    used_weight = jnp.where(member, weighting, 0.0)
    moe_total = jnp.sum(used_weight[:, :, None] * fetched.astype(jnp.float32), axis=1)
    layer_out = (residual.astype(jnp.float32) + moe_total).astype(jnp.bfloat16)
    return (layer_out, cache_after)


def solution(mesh):
    two_lanes = mesh.shape["hd"] == 2 and mesh.shape["grp"] % 8 == 0
    return jax.shard_map(
        two_lane_shards if two_lanes else shards,
        mesh=mesh,
        in_specs=(
            P(("grp", "hd"), None),
            P("grp"),
            P(),
            P(None, "hd"),
            P(None, "hd", None),
            P(None, "grp"),
            P(),
            P(),
            P("hd", "grp", None),
            P("hd", "grp", None),
            P(("grp", "hd"), None),
            P("grp"),
            P("grp", "hd", None),
        ),
        out_specs=(P(("grp", "hd"), None), P("grp", "hd", None)),
        check_vma=False,
    )
```

```python
import functools

import jax
import jax.numpy as jnp
import numpy as np
from jax import lax
from jax.experimental import pallas as pl
from jax.experimental.pallas import tpu as pltpu
from jax.sharding import PartitionSpec as P

norm_eps = 1e-05
rope_base = 10000.0
bf16 = jnp.bfloat16
f32 = jnp.float32
LAST_DIMS = (((1,), (1,)), ((), ()))


def ring_cycle(groups):
    rows = groups // 4
    return [2 * r for r in range(rows)] + [2 * r + 1 for r in reversed(range(rows))]


def ring_pairs(groups):
    cycle = ring_cycle(groups)
    count = len(cycle)
    pairs = []
    for place, pair in enumerate(cycle):
        pairs.append((2 * pair, 2 * cycle[(place + 1) % count]))
        pairs.append((2 * pair + 1, 2 * cycle[(place - 1) % count] + 1))
    return pairs


def sibling_pairs(groups):
    return [(g, g ^ 1) for g in range(groups)]


def ring_sources(groups, me):
    count = groups // 2
    rows = count // 2
    side, pair = me % 2, me // 2
    row, col = pair // 2, pair % 2
    place = jnp.where(col == 0, row, count - 1 - row)

    def block(core, steps):
        there = (place + (2 * core - 1) * steps + count) % count
        other = jnp.where(there < rows, 2 * there, 2 * (count - 1 - there) + 1)
        return [2 * other + core, 2 * other + 1 - core]

    full = (count - 1) // 2
    listed = [me, me + 1 - 2 * side]
    for core in (side, 1 - side):
        for steps in range(1, full + 1):
            listed += block(core, steps)
    return listed + [block(side, count // 2)[0], block(1 - side, count // 2)[0]]


class Ring:
    def __init__(self, pair, groups):
        self.across = functools.partial(lax.ppermute, axis_name="grp", perm=ring_pairs(groups))
        self.beside = functools.partial(lax.ppermute, axis_name="grp", perm=sibling_pairs(groups))
        self.full = (groups // 2 - 1) // 2
        self.unit_rows = pair.shape[0] // 2
        self.mine = [pair]
        self.near = []

    def step(self):
        held = self.mine[-1]
        if len(self.mine) > self.full:
            held = held[: self.unit_rows]
        self.mine.append(self.across(held))

    def pin(self, *others):
        done = lax.optimization_barrier((self.mine[-1],) + others)
        self.mine[-1] = done[0]
        return done[1:] if len(others) > 1 else done[1]

    def share(self):
        for index in range(1 + len(self.near), len(self.mine)):
            self.near.append(self.beside(self.mine[index]))

    def parts(self):
        full = self.full
        return self.mine[: full + 1] + self.near[:full] + [self.mine[full + 1], self.near[full]]


def place_parts(groups, parts, unit_rows, pieces):
    sources = ring_sources(groups, lax.axis_index("grp"))
    shard = 0
    for part in parts:
        for unit in range(part.shape[0] // unit_rows):
            for first, rows, target, lane in pieces:
                at = pl.multiple_of(sources[shard] * rows, rows)
                start = unit * unit_rows + first
                target[pl.ds(at, rows), lane : lane + part.shape[1]] = part[start : start + rows, :]
            shard += 1


VMEM = pl.BlockSpec(memory_space=pltpu.VMEM)
ANY = pl.BlockSpec(memory_space=pl.ANY)
HBM = pl.BlockSpec(memory_space=pltpu.HBM)
PARAMS = pltpu.CompilerParams(vmem_limit_bytes=40 << 20)


LITTLE = pl.CostEstimate(flops=1, bytes_accessed=1, transcendentals=0)


def normalized(floats, gain):
    factor = lax.rsqrt(jnp.mean(floats * floats, axis=-1, keepdims=True) + norm_eps)
    return (floats * factor * gain).astype(bf16)


def fetch(pairs, sems):
    copies = []
    for index, (source, target) in enumerate(pairs):
        copies.append(pltpu.make_async_copy(source, target, sems.at[index]))
        copies[-1].start()
    return copies


def pack_kernel(*refs):
    sources, (expert_pair, out_pair, sems) = refs[:6], refs[6:]
    width = expert_pair.shape[1]
    lane = lax.axis_index("hd")
    first = pl.multiple_of(lane * out_pair.shape[1], out_pair.shape[1])
    pairs = []
    row = 0
    for index in range(2):
        up, down, w_out = sources[3 * index : 3 * index + 3]
        count = w_out.shape[0]
        pairs.append(
            (w_out.at[:, pl.ds(first, out_pair.shape[1])], out_pair.at[pl.ds(index * count, count), :])
        )
        for source in (up, down):
            for at in range(0, source.shape[1], width):
                pairs.append(
                    (source.at[:, pl.ds(at, width)], expert_pair.at[pl.ds(row, source.shape[0]), :])
                )
                row += source.shape[0]
    for copy in fetch(pairs, sems):
        copy.wait()


def pack(own, beside):
    own = [pltpu.with_memory_space_constraint(part, pltpu.HBM) for part in own]
    up, down, w_out_t = own
    width = up.shape[1] // 2
    pieces = [up.shape[1] // width, down.shape[1] // width]
    unit_rows = pieces[0] * up.shape[0] + pieces[1] * down.shape[0]
    return pl.pallas_call(
        pack_kernel,
        out_shape=(
            jax.ShapeDtypeStruct((2 * unit_rows, width), bf16),
            jax.ShapeDtypeStruct((2 * w_out_t.shape[0], w_out_t.shape[1] // 2), bf16),
        ),
        in_specs=[ANY] * 6,
        out_specs=(ANY, ANY),
        scratch_shapes=[pltpu.SemaphoreType.DMA((2 + 2 * sum(pieces),))],
        compiler_params=PARAMS,
        cost_estimate=LITTLE,
        name="pack",
    )(*own, *beside)


def as_column(row, eye):
    return jnp.sum(jnp.where(eye, row, 0.0), axis=1, keepdims=True)


def prepare_kernel(groups, slots_dev, *refs):
    sources, (cosine, sine, past, named, place, spread, send, tags, gain, late_gain, router) = (
        refs[:6],
        refs[6:17],
    )
    positions, slots, ids, sems = refs[17:]
    copies = fetch(list(zip(sources, (positions, slots, ids, gain, late_gain, router))), sems)
    for copy in copies:
        copy.wait()
    lane = lax.axis_index("hd")
    block = positions.shape[1]

    def iota(shape, dim):
        return lax.broadcasted_iota(jnp.int32, shape, dim)

    eye = iota((block, block), 0) == iota((block, block), 1)
    reach = as_column(jnp.maximum(positions[...], 0).astype(f32), eye)
    past[...] = jnp.broadcast_to(reach, past.shape)
    column = iota((8, 128), 1)
    exponent = (column % 32).astype(f32) * (-2.0 / 64)
    inverse_freq = jnp.exp(exponent * np.float32(np.log(rope_base)))[:1, :]
    angles = reach * inverse_freq
    cosine[...] = jnp.cos(angles)
    turned = jnp.sin(angles)
    sine[...] = jnp.where(iota(angles.shape, 1) % 64 < 32, -turned, turned)

    tokens = ids.shape[1]
    experts = named.shape[1]
    cap = place.shape[0] // 2
    expert = iota((experts, tokens), 0)
    hit = jnp.zeros((experts, tokens), f32)
    for index in range(ids.shape[0]):
        hit = jnp.where(ids[index : index + 1, :] == expert, 1.0, hit)
    small_eye = (iota((tokens, tokens), 0) == iota((tokens, tokens), 1)).astype(f32)
    named[...] = lax.dot_general(small_eye, hit, LAST_DIMS, preferred_element_type=f32)
    upto = (iota((tokens, tokens), 0) <= iota((tokens, tokens), 1)).astype(f32)
    rank = jnp.dot(hit[:8, :], upto, preferred_element_type=f32) - 1.0
    slot = iota((2 * cap, tokens), 0).astype(f32)
    placed = jnp.zeros((2 * cap, tokens), f32)
    for live in range(2):
        order = jnp.where(lane == live, 0, cap).astype(f32)
        member = hit[live : live + 1, :] > 0.0
        placed = jnp.where(member & (slot == rank[live : live + 1, :] + order), 1.0, placed)
    place[...] = placed.astype(bf16)
    spread[...] = lax.dot_general(small_eye, placed, LAST_DIMS, preferred_element_type=f32).astype(bf16)

    where = slots[...]
    owner = jnp.where(where >= 0, where // slots_dev, -1)
    owner_hit = (iota((groups, block), 0) == owner).astype(f32)
    before = (iota((block, block), 0) <= iota((block, block), 1)).astype(f32)
    running = jnp.dot(owner_hit, before, preferred_element_type=f32)
    owner_rank = jnp.sum(owner_hit * running, axis=0, keepdims=True) - 1.0
    capc = send.shape[0] // groups
    row = jnp.where(owner >= 0, owner * capc + owner_rank.astype(jnp.int32), -1)
    send[...] = (iota(send.shape, 0) == row).astype(bf16)
    inside = jnp.where(where >= 0, where % slots_dev, 0)
    high = as_column((inside // 64 + 1).astype(f32), eye)
    low = as_column((inside % 64).astype(f32), eye)
    spot = iota(tags.shape, 1)
    tags[...] = jnp.where(spot == 0, high, jnp.where(spot == 1, low, 0.0)).astype(bf16)


def prepare(groups, slots_dev, positions, slots, ids, gain, late_gain, router):
    block, tokens = positions.shape[0], ids.shape[0]
    model, experts = router.shape
    cap = tokens // 4
    capc = 2 * block // groups
    shapes = [
        ((block, 128), f32),
        ((block, 128), f32),
        ((block, 128), f32),
        ((tokens, experts), f32),
        ((2 * cap, tokens), bf16),
        ((tokens, 2 * cap), bf16),
        ((groups * capc, block), bf16),
        ((block, 128), bf16),
        ((1, model), f32),
        ((1, model), f32),
        ((experts, model), bf16),
    ]
    sources = (positions[None], slots[None], ids.T, gain[None], late_gain[None], router.T)
    return pl.pallas_call(
        functools.partial(prepare_kernel, groups, slots_dev),
        out_shape=tuple(jax.ShapeDtypeStruct(shape, kind) for shape, kind in shapes),
        in_specs=[ANY] * 6,
        out_specs=(VMEM,) * len(shapes),
        scratch_shapes=[
            pltpu.VMEM((1, block), jnp.int32),
            pltpu.VMEM((1, block), jnp.int32),
            pltpu.VMEM(ids.shape[::-1], jnp.int32),
            pltpu.SemaphoreType.DMA((6,)),
        ],
        compiler_params=PARAMS,
        cost_estimate=LITTLE,
        name="prepare",
    )(*[pltpu.with_memory_space_constraint(source, pltpu.HBM) for source in sources])


def project_kernel(
    own, other, gain, cosine, sine, w_query, w_keyval, q_out, kv_out, seam_out, raw, rows, sems
):
    count = own.shape[0]
    lane = lax.axis_index("hd")
    mine = pl.multiple_of(lane * count, count)
    theirs = pl.multiple_of((1 - lane) * count, count)
    copies = fetch([(own, raw.at[0]), (other, raw.at[1])], sems)
    cos_q, sin_q = cosine[...], sine[...]
    column = lax.broadcasted_iota(jnp.int32, cos_q.shape, 1)
    lower = column % 64 < 32
    cos_kv = jnp.where(column < 64, cos_q, 1.0)
    sin_kv = jnp.where(column < 64, sin_q, 0.0)
    for index, first in ((0, mine), (1, theirs)):
        copies[index].wait()
        rows[pl.ds(first, count), :] = normalized(raw[index].astype(f32), gain[...])
    width = 256
    for weights, out, cos, sin in ((w_keyval, kv_out, cos_kv, sin_kv), (w_query, q_out, cos_q, sin_q)):
        for first in range(0, weights.shape[1], width):
            made = jnp.dot(rows[...], weights[:, first : first + width], preferred_element_type=f32)
            for part in range(0, width, 128):
                here = made[:, part : part + 128]
                turned = jnp.where(lower, pltpu.roll(here, 96, 1), pltpu.roll(here, 32, 1))
                done = (here * cos + turned * sin).astype(bf16)
                out[:, first + part : first + part + 128] = done
                if out is kv_out:
                    seam_out[:, first + part : first + part + 128] = done[count:, :]


def project(own, other, gain, cosine, sine, w_query, flat_kv):
    count, width = own.shape
    made = w_query.shape[1] + flat_kv.shape[1]
    return pl.pallas_call(
        project_kernel,
        out_shape=(
            jax.ShapeDtypeStruct((2 * count, w_query.shape[1]), bf16),
            jax.ShapeDtypeStruct((2 * count, flat_kv.shape[1]), bf16),
            jax.ShapeDtypeStruct((count, flat_kv.shape[1]), bf16),
        ),
        in_specs=[ANY] * 2 + [VMEM] * 5,
        out_specs=(VMEM, VMEM, VMEM),
        scratch_shapes=[
            pltpu.VMEM((2, count, width), bf16),
            pltpu.VMEM((2 * count, width), bf16),
            pltpu.SemaphoreType.DMA((2,)),
        ],
        compiler_params=PARAMS,
        cost_estimate=LITTLE,
        name="project",
    )(own, other, gain, cosine, sine, w_query, flat_kv)


def attend_kernel(q, kv, seam, past, mixed, window, sem):
    count = seam.shape[0]
    copy = pltpu.make_async_copy(seam, window.at[pl.ds(0, count), :], sem)
    copy.start()
    window[count:, :] = kv[...]
    head = 64
    kv_heads = kv.shape[1] // (2 * head)
    per_kv = q.shape[1] // head // kv_heads
    shape = (count, 2 * count)
    row = lax.broadcasted_iota(jnp.int32, shape, 0) + count
    col = lax.broadcasted_iota(jnp.int32, shape, 1)
    for half in (1, 0):
        first = half * count
        if half == 0:
            copy.wait()
        reach = past[first : first + count, :1].astype(jnp.int32)
        visible = (col <= row) & (col >= row - reach)
        for kv_head in range(kv_heads):
            lanes = 2 * head * kv_head
            keys = window[first : first + 2 * count, lanes : lanes + head]
            values = window[first : first + 2 * count, lanes + head : lanes + 2 * head]
            for index in range(per_kv):
                at = (kv_head * per_kv + index) * head
                query = q[first : first + count, at : at + head]
                scores = lax.dot_general(query, keys, LAST_DIMS, preferred_element_type=f32)
                raised = jnp.where(visible, jnp.exp(scores * head ** (-0.5)), 0.0)
                probs = (raised / jnp.sum(raised, axis=-1, keepdims=True)).astype(bf16)
                made = jnp.dot(probs, values, preferred_element_type=f32)
                mixed[first : first + count, at : at + head] = made.astype(bf16)


def attend(q, kv, seam, past):
    count = seam.shape[0]
    return pl.pallas_call(
        attend_kernel,
        out_shape=jax.ShapeDtypeStruct(q.shape, bf16),
        in_specs=[VMEM, VMEM, ANY, VMEM],
        out_specs=VMEM,
        scratch_shapes=[
            pltpu.VMEM((3 * count, kv.shape[1]), bf16),
            pltpu.SemaphoreType.DMA,
        ],
        compiler_params=PARAMS,
        cost_estimate=LITTLE,
        name="attend",
    )(q, kv, seam, past)


def outward_kernel(flip, groups, unit_rows, n_parts, mixed, *refs):
    parts, (out, w_out) = refs[:n_parts], refs[n_parts:]
    place_parts(groups, parts, unit_rows, [(0, unit_rows, w_out, 0)])
    count = out.shape[0]
    lane = lax.axis_index("hd")
    first = pl.multiple_of(((1 - lane) if flip else lane) * count, count)
    out[...] = lax.dot_general(
        mixed[pl.ds(first, count), :], w_out[...], LAST_DIMS, preferred_element_type=f32
    ).astype(out.dtype)


def outward(flip, out_type, groups, mixed, parts, unit_rows):
    count = mixed.shape[0] // 2
    width = groups * unit_rows
    depth = parts[0].shape[1]
    return pl.pallas_call(
        functools.partial(outward_kernel, flip, groups, unit_rows, len(parts)),
        out_shape=jax.ShapeDtypeStruct((count, width), out_type),
        in_specs=[VMEM] * (1 + len(parts)),
        out_specs=VMEM,
        scratch_shapes=[pltpu.VMEM((width, depth), bf16)],
        compiler_params=PARAMS,
        cost_estimate=LITTLE,
        name="outward_send" if flip else "outward_keep",
    )(mixed, *parts)


def route_kernel(tokens, mine, arrived, gain, place, residual, moe_in, sent):
    added = (tokens[...].astype(f32) + (mine[...] + arrived[...].astype(f32))).astype(bf16)
    residual[...] = added
    moe_in[...] = normalized(added.astype(f32), gain[...])
    cap = sent.shape[0]
    rows = jnp.dot(place[cap:, :], moe_in[...], preferred_element_type=f32)
    sent[...] = rows.astype(bf16)


def route(tokens, mine, arrived, gain, place):
    cap = place.shape[0] // 2
    return pl.pallas_call(
        route_kernel,
        out_shape=(
            jax.ShapeDtypeStruct(tokens.shape, bf16),
            jax.ShapeDtypeStruct(tokens.shape, bf16),
            jax.ShapeDtypeStruct((cap, tokens.shape[1]), bf16),
        ),
        in_specs=[VMEM] * 5,
        out_specs=(VMEM,) * 3,
        compiler_params=PARAMS,
        cost_estimate=LITTLE,
        name="route",
    )(tokens, mine, arrived, gain, place)


def gate_kernel(moe_in, router, named, place, gates, own):
    cap = own.shape[0]
    own[...] = jnp.dot(place[:cap, :], moe_in[...], preferred_element_type=f32).astype(bf16)
    logits = lax.dot_general(moe_in[...], router[...], LAST_DIMS, preferred_element_type=f32)
    raised = jnp.where(named[...] > 0, jnp.exp(logits), 0.0)
    gates[...] = raised / jnp.sum(raised, axis=-1, keepdims=True)


def gate(moe_in, router_t, named, place):
    cap = place.shape[0] // 2
    return pl.pallas_call(
        gate_kernel,
        out_shape=(
            jax.ShapeDtypeStruct(named.shape, f32),
            jax.ShapeDtypeStruct((cap, moe_in.shape[1]), bf16),
        ),
        in_specs=[VMEM] * 4,
        out_specs=(VMEM,) * 2,
        compiler_params=PARAMS,
        cost_estimate=LITTLE,
        name="gate",
    )(moe_in, router_t, named, place)


def expert_kernel(groups, up_rows, down_rows, n_parts, own, other, *refs):
    parts = refs[:n_parts]
    own_out, other_out, rows, gate_up, down = refs[n_parts:]
    width = parts[0].shape[1]
    count = own.shape[0]
    rows[:count, :] = own[...]
    rows[count:, :] = other[...]
    pieces = [(i * up_rows, up_rows, gate_up, i * width) for i in range(2)]
    pieces += [
        (2 * up_rows + i * down_rows, down_rows, down, i * width) for i in range(down.shape[1] // width)
    ]
    unit_rows = pieces[-1][0] + down_rows
    place_parts(groups, parts, unit_rows, pieces)
    both = jnp.dot(rows[...], gate_up[...], preferred_element_type=f32)
    gate, up = both[:, :width], both[:, width:]
    hidden = (gate / (1.0 + jnp.exp(-gate)) * up).astype(bf16)
    made = jnp.dot(hidden, down[...], preferred_element_type=f32).astype(bf16)
    own_out[...] = made[:count, :]
    other_out[...] = made[count:, :]


def expert(groups, own, other, parts, up_rows, down_rows):
    count, model = own.shape
    width = parts[0].shape[1]
    return pl.pallas_call(
        functools.partial(expert_kernel, groups, up_rows, down_rows, len(parts)),
        out_shape=(jax.ShapeDtypeStruct(own.shape, bf16),) * 2,
        in_specs=[VMEM] * (2 + len(parts)),
        out_specs=(VMEM, VMEM),
        scratch_shapes=[
            pltpu.VMEM((2 * count, model), bf16),
            pltpu.VMEM((groups * up_rows, 2 * width), bf16),
            pltpu.VMEM((groups * down_rows, model), bf16),
        ],
        compiler_params=PARAMS,
        cost_estimate=LITTLE,
        name="expert",
    )(own, other, *parts)


def combine_kernel(residual, gates, spread, own, returned, out):
    lane = lax.axis_index("hd")
    count = own.shape[0]
    column = lax.broadcasted_iota(jnp.int32, gates.shape, 1)
    total = jnp.zeros(residual.shape, f32)
    for index, made in ((0, own), (1, returned)):
        live = lane if index == 0 else 1 - lane
        weight = jnp.sum(jnp.where(column == live, gates[...], 0.0), axis=-1, keepdims=True)
        picked = jnp.dot(
            spread[:, index * count : (index + 1) * count], made[...], preferred_element_type=f32
        )
        total += weight * picked
    out[...] = (residual[...].astype(f32) + total).astype(bf16)


def combine(residual, gates, spread, own, returned):
    return pl.pallas_call(
        combine_kernel,
        out_shape=jax.ShapeDtypeStruct(residual.shape, bf16),
        in_specs=[VMEM] * 5,
        out_specs=VMEM,
        compiler_params=PARAMS,
        cost_estimate=LITTLE,
        name="combine",
    )(residual, gates, spread, own, returned)


def bundle_kernel(send, kv, tags, out):
    groups, rows, _ = out.shape
    heads = kv.shape[1] // 128
    capc = send.shape[0] // groups
    packed = jnp.dot(send[...], kv[...], preferred_element_type=f32).astype(bf16)
    tagged = jnp.dot(send[...], tags[...], preferred_element_type=f32)
    one = (lax.broadcasted_iota(jnp.int32, (16, 128), 0) == lax.broadcasted_iota(jnp.int32, (16, 128), 1))
    for owner in range(groups):
        mine = slice(owner * capc, (owner + 1) * capc)
        for head in range(heads):
            out[owner, head * capc : (head + 1) * capc, :] = packed[mine, head * 128 : (head + 1) * 128]
        wide = jnp.concatenate([tagged[mine, :], jnp.zeros((128 - capc, 128), f32)], axis=0)
        out[owner, heads * capc :, :] = lax.dot_general(
            one.astype(f32), wide, LAST_DIMS, preferred_element_type=f32
        ).astype(bf16)


def bundle(groups, send, kv, tags):
    rows = send.shape[0] // groups * (kv.shape[1] // 128) + 16
    return pl.pallas_call(
        bundle_kernel,
        out_shape=jax.ShapeDtypeStruct((groups, rows, 128), bf16),
        in_specs=[VMEM] * 3,
        out_specs=VMEM,
        compiler_params=PARAMS,
        cost_estimate=LITTLE,
        name="bundle",
    )(send, kv, tags)


def write_kernel(arrived, cache, out, rows):
    groups, size, _ = arrived.shape
    slots, heads, _ = cache.shape
    capc = (size - 16) // heads
    high, low = [], []
    for source in range(groups):
        for head in range(heads):
            rows[source * capc : (source + 1) * capc, head * 128 : (head + 1) * 128] = arrived[
                source, head * capc : (head + 1) * capc, :
            ]
        numbers = arrived[source, heads * capc :, :].astype(f32)
        high.append(numbers[0:1, :capc])
        low.append(numbers[1:2, :capc])
    slot = jnp.concatenate(high, axis=1) * 64.0 + jnp.concatenate(low, axis=1) - 64.0
    hit = (lax.broadcasted_iota(jnp.int32, (slots, slot.shape[1]), 0).astype(f32) == slot).astype(f32)
    known = jnp.max(hit, axis=1, keepdims=True) > 0.0
    made = jnp.dot(hit.astype(bf16), rows[...], preferred_element_type=f32)
    for head in range(heads):
        here = made[:, head * 128 : (head + 1) * 128]
        out[:, head, :] = jnp.where(known, here, cache[:, head, :].astype(f32)).astype(bf16)


def write(arrived, cache):
    slots, heads, lanes = cache.shape
    capc = (arrived.shape[1] - 16) // heads
    return pl.pallas_call(
        write_kernel,
        out_shape=jax.ShapeDtypeStruct(cache.shape, bf16),
        in_specs=[VMEM] * 2,
        out_specs=VMEM,
        scratch_shapes=[pltpu.VMEM((arrived.shape[0] * capc, heads * lanes), bf16)],
        compiler_params=PARAMS,
        cost_estimate=LITTLE,
        name="write",
    )(arrived, cache)


def two_lane_shards(
    tokens,
    positions,
    attn_gain,
    w_query,
    w_keyval,
    w_out,
    moe_gain,
    router,
    w_gate_up,
    w_down,
    expert_ids,
    cache_slot,
    kv_cache,
):
    groups = lax.axis_size("grp")
    tok_rows, model = tokens.shape
    block = positions.shape[0]
    kv_local, head2 = w_keyval.shape[1:]
    kv_width = kv_local * head2
    slots_dev = kv_cache.shape[0]
    swap = functools.partial(lax.ppermute, axis_name="hd", perm=[(0, 1), (1, 0)])

    together = lax.optimization_barrier

    other_tokens = swap(tokens)
    own = (w_gate_up[0], w_down[0], w_out.T)
    up_rows, down_rows = own[0].shape[0], own[1].shape[0]
    beside = [lax.ppermute(part, "grp", sibling_pairs(groups)) for part in own]
    flat_kv = w_keyval.reshape(model, kv_width)
    beside, flat_kv = together((beside, flat_kv))
    expert_pair, out_pair = pack(own, beside)
    out_ring = Ring(out_pair, groups)
    out_ring.step()
    expert_ring = Ring(expert_pair, groups)
    expert_ring.step()
    positions = together((positions, out_pair))[0]
    cosine, sine, past, named, place, spread, send, tags, gain, late_gain, router_t = prepare(
        groups, slots_dev, positions, cache_slot, expert_ids, attn_gain, moe_gain, router
    )
    other_tokens, cosine = out_ring.pin(other_tokens, cosine)
    out_ring.step()

    q, kv, tail = project(tokens, other_tokens, gain, cosine, sine, w_query, flat_kv)
    seam = lax.ppermute(tail, "grp", [(g, g + 1) for g in range(groups - 1)])
    outgoing = bundle(groups, send, kv, tags)
    outgoing = out_ring.pin(outgoing)
    out_ring.step()
    seam, q = together((seam, q, outgoing))[:2]
    seam = expert_ring.pin(seam)
    expert_ring.step()
    mixed = attend(q, kv, seam, past)
    mixed = out_ring.pin(mixed)
    out_ring.step()
    out_ring.mine[-1] = expert_ring.pin(out_ring.mine[-1])
    out_ring.share()
    expert_ring.step()
    sent = outward(True, bf16, groups, mixed, out_ring.parts(), out_ring.unit_rows)
    arrived = swap(sent)
    mixed = together((mixed, sent))[0]
    mine = outward(False, f32, groups, mixed, out_ring.parts(), out_ring.unit_rows)
    outgoing, mine = together((outgoing, mine))
    arrived_cache = lax.all_to_all(outgoing, "grp", split_axis=0, concat_axis=0, tiled=True)

    residual, moe_in, sent_rows = route(tokens, mine, arrived, late_gain, place)
    landed = swap(sent_rows)
    gates, own_rows = gate(moe_in, router_t, named, place)
    landed, own_rows = expert_ring.pin(landed, own_rows)
    expert_ring.share()
    expert_ring.step()
    expert_ring.share()
    own_made, back = expert(
        groups, own_rows, landed, expert_ring.parts(), up_rows, down_rows
    )
    returned = swap(back)
    arrived_cache = together((arrived_cache, back))[0]
    cache_after = write(arrived_cache, kv_cache)
    returned, cache_after = together((returned, cache_after))
    layer_out = combine(residual, gates, spread, own_made, returned)
    return (layer_out, cache_after)


def passed_along(value, axis, steps):
    count = lax.axis_size(axis)
    initial, last = (max(0, -steps), min(count, count - steps))
    return lax.ppermute(value, axis, [(source, source + steps) for source in range(initial, last)])


def rms_norm(row_set, norm_gain):
    floats = row_set.astype(jnp.float32)
    factor = lax.rsqrt(jnp.mean(floats * floats, axis=-1, keepdims=True) + norm_eps)
    return (floats * factor * norm_gain).astype(jnp.bfloat16)


def rotate(vectors, angle_pos):
    halves = vectors.shape[-1] // 2
    inverse_freq = rope_base ** (-2.0 * jnp.arange(halves, dtype=jnp.float32) / vectors.shape[-1])
    angles = angle_pos[:, None, None] * inverse_freq[None, None, :]
    cosine = jnp.cos(angles)
    sine_part = jnp.sin(angles)
    first_half = vectors[..., :halves]
    second_half = vectors[..., halves:]
    return jnp.concatenate(
        [
            first_half * cosine - second_half * sine_part,
            second_half * cosine + first_half * sine_part,
        ],
        axis=-1,
    )


def expert_rows(row_set, gate_up, down_rows):
    gate_and_up = jnp.dot(row_set, gate_up, preferred_element_type=jnp.float32)
    inner_width = gate_and_up.shape[1] // 2
    hidden = (jax.nn.silu(gate_and_up[:, :inner_width]) * gate_and_up[:, inner_width:]).astype(
        jnp.bfloat16
    )
    return jnp.dot(hidden, down_rows, preferred_element_type=jnp.float32).astype(jnp.bfloat16)


def attend_rows(query_blk, keys_blk, vals_blk, visible, scale_qk):
    scores = (
        jnp.einsum("qkgd,skd->kgqs", query_blk, keys_blk, preferred_element_type=jnp.float32)
        * scale_qk
    )
    weights_f = jnp.where(visible[None, None], jnp.exp(scores), 0.0)
    prob_bf = (weights_f / jnp.sum(weights_f, axis=-1, keepdims=True)).astype(jnp.bfloat16)
    return jnp.einsum("kgqs,skd->qkgd", prob_bf, vals_blk, preferred_element_type=jnp.float32)


def shards(
    tokens,
    positions,
    attn_gain,
    w_query,
    w_keyval,
    w_out,
    moe_gain,
    router,
    w_gate_up,
    w_down,
    expert_ids,
    cache_slot,
    kv_cache,
):
    lane_count = lax.axis_size("hd")
    group_count = lax.axis_size("grp")
    tok_rows = tokens.shape[0]
    model_width = tokens.shape[1]
    block_len = positions.shape[0]
    seg_most = block_len // 2
    head_dim = w_keyval.shape[2] // 2
    kv_local = w_keyval.shape[1]
    q_local = w_query.shape[1] // head_dim
    per_kv = q_local // kv_local
    expert_cap = tok_rows // 4
    normed = rms_norm(tokens, attn_gain)
    flat_kv = w_keyval.reshape(model_width, kv_local * 2 * head_dim)
    section = lax.all_gather(normed, "hd", axis=0, tiled=True)
    projected = jnp.concatenate(
        [
            jnp.dot(section, w_query, preferred_element_type=jnp.float32),
            jnp.dot(section, flat_kv, preferred_element_type=jnp.float32),
        ],
        axis=1,
    )
    angle_pos = jnp.maximum(positions, 0).astype(jnp.float32)
    queries = rotate(
        projected[:, : q_local * head_dim].reshape(block_len, q_local, head_dim), angle_pos
    ).astype(jnp.bfloat16)
    key_val = projected[:, q_local * head_dim :].reshape(block_len, kv_local, 2 * head_dim)
    rotated = rotate(key_val[:, :, :head_dim], angle_pos).astype(jnp.bfloat16)
    stored = jnp.concatenate([rotated, key_val[:, :, head_dim:].astype(jnp.bfloat16)], axis=2)
    seam_rows = passed_along(stored[block_len - seg_most :], "grp", 1)
    window = jnp.concatenate([seam_rows, stored], axis=0)
    scale_qk = head_dim ** (-0.5)
    local_rows = jnp.arange(block_len, dtype=jnp.int32)
    lowest = local_rows - jnp.maximum(positions, 0)
    pieces_out = []
    for q_block in range(2):
        first_row = q_block * seg_most
        rows_here = first_row + jnp.arange(seg_most, dtype=jnp.int32)
        cols_here = first_row - seg_most + jnp.arange(2 * seg_most, dtype=jnp.int32)
        low_here = lowest[first_row : first_row + seg_most]
        visible = (cols_here[None, :] >= low_here[:, None]) & (
            cols_here[None, :] <= rows_here[:, None]
        )
        query_blk = queries[first_row : first_row + seg_most].reshape(
            seg_most, kv_local, per_kv, head_dim
        )
        keys_blk = window[first_row : first_row + 2 * seg_most, :, :head_dim]
        vals_blk = window[first_row : first_row + 2 * seg_most, :, head_dim:]
        mixed_rows = attend_rows(query_blk, keys_blk, vals_blk, visible, scale_qk)
        pieces_out.append(mixed_rows.reshape(seg_most, q_local * head_dim).astype(jnp.bfloat16))
    attended = jnp.concatenate(pieces_out, axis=0)
    slots_dev = kv_cache.shape[0]
    capc = 2 * block_len // group_count
    live_slot = cache_slot >= 0
    owners = jnp.where(live_slot, cache_slot // slots_dev, group_count)
    owner_hit = (owners[:, None] == jnp.arange(group_count, dtype=jnp.int32)[None, :]).astype(
        jnp.bfloat16
    )
    lower_tri = (local_rows[:, None] >= local_rows[None, :]).astype(jnp.bfloat16)
    running = jnp.dot(lower_tri, owner_hit, preferred_element_type=jnp.float32)
    owner_rank = jnp.sum(running * owner_hit.astype(jnp.float32), axis=1).astype(jnp.int32) - 1
    send_rows = jnp.where(live_slot, owners * capc + owner_rank, group_count * capc)
    outgoing_cache = (
        jnp.zeros((group_count * capc, kv_local, 2 * head_dim), jnp.bfloat16)
        .at[send_rows]
        .set(stored, mode="drop")
    )
    outgoing_slots = (
        jnp.full((group_count * capc,), -1, jnp.int32)
        .at[send_rows]
        .set(cache_slot % slots_dev, mode="drop")
    )
    arrived, arrived_slots = (
        lax.all_to_all(
            outgoing_cache.reshape(group_count, capc, kv_local, 2 * head_dim),
            "grp",
            split_axis=0,
            concat_axis=0,
            tiled=True,
        ),
        lax.all_to_all(
            outgoing_slots.reshape(group_count, capc),
            "grp",
            split_axis=0,
            concat_axis=0,
            tiled=True,
        ),
    )
    flat_slots = arrived_slots.reshape(group_count * capc)
    write_rows = jnp.where(flat_slots >= 0, flat_slots, slots_dev).astype(jnp.int32)
    cache_after = kv_cache.at[write_rows].set(
        arrived.reshape(group_count * capc, kv_local, 2 * head_dim), mode="drop"
    )
    by_token = lax.all_to_all(attended, "hd", split_axis=0, concat_axis=1, tiled=True)
    attn_proj = jnp.dot(
        by_token,
        lax.all_gather(w_out, "grp", axis=1, tiled=True),
        preferred_element_type=jnp.float32,
    )
    residual = (tokens.astype(jnp.float32) + attn_proj).astype(jnp.bfloat16)
    moe_in = rms_norm(residual, moe_gain)
    logits = jnp.dot(moe_in, router, preferred_element_type=jnp.float32)
    expert_range = jnp.arange(router.shape[1], dtype=jnp.int32)
    matches_all = expert_ids[:, :, None] == expert_range[None, None, :]
    chosen = jnp.sum(jnp.where(matches_all, logits[:, None, :], 0.0), axis=2)
    raised = jnp.exp(chosen)
    gates = raised / jnp.sum(raised, axis=1, keepdims=True)
    live_range = jnp.arange(lane_count, dtype=jnp.int32)
    matches = expert_ids[:, :, None] == live_range[None, None, :]
    member = jnp.any(matches, axis=1)
    weighting = jnp.sum(jnp.where(matches, gates[:, :, None], 0.0), axis=1)
    ranking = jnp.cumsum(member.astype(jnp.int32), axis=0) - 1
    target = jnp.where(member, live_range[None, :] * expert_cap + ranking, -1)
    slot_range = jnp.arange(lane_count * expert_cap, dtype=jnp.int32)
    slot_hits = target[None, :, :] == slot_range[:, None, None]
    placing = jnp.any(slot_hits, axis=2).astype(jnp.bfloat16)
    outgoing = (
        jnp.dot(placing, moe_in, preferred_element_type=jnp.float32)
        .astype(jnp.bfloat16)
        .reshape(lane_count, expert_cap, model_width)
    )
    gate_up_all, down_all = (
        lax.all_gather(w_gate_up, "grp", axis=1, tiled=True),
        lax.all_gather(w_down, "grp", axis=1, tiled=True),
    )
    gate_up_mat = gate_up_all[0]
    down_mat = down_all[0]
    landed = lax.all_to_all(outgoing, "hd", split_axis=0, concat_axis=0, tiled=True)
    results = expert_rows(landed.reshape(-1, model_width), gate_up_mat, down_mat).reshape(landed.shape)
    returned = lax.all_to_all(results, "hd", split_axis=0, concat_axis=0, tiled=True)
    flat_returned = returned.reshape(-1, model_width)
    fetched = flat_returned[jnp.maximum(target, 0)]
    used_weight = jnp.where(member, weighting, 0.0)
    moe_total = jnp.sum(used_weight[:, :, None] * fetched.astype(jnp.float32), axis=1)
    layer_out = (residual.astype(jnp.float32) + moe_total).astype(jnp.bfloat16)
    return (layer_out, cache_after)


def solution(mesh):
    two_lanes = mesh.shape["hd"] == 2 and mesh.shape["grp"] % 8 == 0
    return jax.shard_map(
        two_lane_shards if two_lanes else shards,
        mesh=mesh,
        in_specs=(
            P(("grp", "hd"), None),
            P("grp"),
            P(),
            P(None, "hd"),
            P(None, "hd", None),
            P(None, "grp"),
            P(),
            P(),
            P("hd", "grp", None),
            P("hd", "grp", None),
            P(("grp", "hd"), None),
            P("grp"),
            P("grp", "hd", None),
        ),
        out_specs=(P(("grp", "hd"), None), P("grp", "hd", None)),
        check_vma=False,
    )
```

```python
import functools

import jax
import jax.numpy as jnp
import numpy as np
from jax import lax
from jax.experimental import pallas as pl
from jax.experimental.pallas import tpu as pltpu
from jax.sharding import PartitionSpec as P

norm_eps = 1e-05
rope_base = 10000.0
bf16 = jnp.bfloat16
f32 = jnp.float32
LAST_DIMS = (((1,), (1,)), ((), ()))


def ring_cycle(groups):
    rows = groups // 4
    return [2 * r for r in range(rows)] + [2 * r + 1 for r in reversed(range(rows))]


def ring_pairs(groups):
    cycle = ring_cycle(groups)
    count = len(cycle)
    pairs = []
    for place, pair in enumerate(cycle):
        pairs.append((2 * pair, 2 * cycle[(place + 1) % count]))
        pairs.append((2 * pair + 1, 2 * cycle[(place - 1) % count] + 1))
    return pairs


def sibling_pairs(groups):
    return [(g, g ^ 1) for g in range(groups)]


def ring_sources(groups, me):
    count = groups // 2
    rows = count // 2
    side, pair = me % 2, me // 2
    row, col = pair // 2, pair % 2
    place = jnp.where(col == 0, row, count - 1 - row)

    def block(core, steps):
        there = (place + (2 * core - 1) * steps + count) % count
        other = jnp.where(there < rows, 2 * there, 2 * (count - 1 - there) + 1)
        return [2 * other + core, 2 * other + 1 - core]

    full = (count - 1) // 2
    listed = [me, me + 1 - 2 * side]
    for core in (side, 1 - side):
        for steps in range(1, full + 1):
            listed += block(core, steps)
    return listed + [block(side, count // 2)[0], block(1 - side, count // 2)[0]]


class Ring:
    def __init__(self, pair, groups):
        self.across = functools.partial(lax.ppermute, axis_name="grp", perm=ring_pairs(groups))
        self.beside = functools.partial(lax.ppermute, axis_name="grp", perm=sibling_pairs(groups))
        self.full = (groups // 2 - 1) // 2
        self.unit_rows = pair.shape[0] // 2
        self.mine = [pair]
        self.near = []

    def step(self):
        held = self.mine[-1]
        if len(self.mine) > self.full:
            held = held[: self.unit_rows]
        self.mine.append(self.across(held))

    def pin(self, *others):
        done = lax.optimization_barrier((self.mine[-1],) + others)
        self.mine[-1] = done[0]
        return done[1:] if len(others) > 1 else done[1]

    def share(self):
        for index in range(1 + len(self.near), len(self.mine)):
            self.near.append(self.beside(self.mine[index]))

    def parts(self):
        full = self.full
        return self.mine[: full + 1] + self.near[:full] + [self.mine[full + 1], self.near[full]]


def place_parts(groups, parts, unit_rows, pieces):
    sources = ring_sources(groups, lax.axis_index("grp"))
    shard = 0
    for part in parts:
        for unit in range(part.shape[0] // unit_rows):
            for first, rows, target, lane in pieces:
                at = pl.multiple_of(sources[shard] * rows, rows)
                start = unit * unit_rows + first
                target[pl.ds(at, rows), lane : lane + part.shape[1]] = part[start : start + rows, :]
            shard += 1


VMEM = pl.BlockSpec(memory_space=pltpu.VMEM)
ANY = pl.BlockSpec(memory_space=pl.ANY)
HBM = pl.BlockSpec(memory_space=pltpu.HBM)
PARAMS = pltpu.CompilerParams(vmem_limit_bytes=40 << 20)


LITTLE = pl.CostEstimate(flops=1, bytes_accessed=1, transcendentals=0)


def takes(us):
    return pl.CostEstimate(flops=int(us * 1.15e9), bytes_accessed=1, transcendentals=0)


def reads(nbytes):
    return pl.CostEstimate(flops=1, bytes_accessed=nbytes, transcendentals=0)


def normalized(floats, gain):
    factor = lax.rsqrt(jnp.mean(floats * floats, axis=-1, keepdims=True) + norm_eps)
    return (floats * factor * gain).astype(bf16)


def fetch(pairs, sems):
    copies = []
    for index, (source, target) in enumerate(pairs):
        copies.append(pltpu.make_async_copy(source, target, sems.at[index]))
        copies[-1].start()
    return copies


def pack_kernel(*refs):
    sources, (expert_pair, out_pair, sems) = refs[:6], refs[6:]
    width = expert_pair.shape[1]
    lane = lax.axis_index("hd")
    first = pl.multiple_of(lane * out_pair.shape[1], out_pair.shape[1])
    pairs = []
    row = 0
    for index in range(2):
        up, down, w_out = sources[3 * index : 3 * index + 3]
        count = w_out.shape[0]
        pairs.append(
            (w_out.at[:, pl.ds(first, out_pair.shape[1])], out_pair.at[pl.ds(index * count, count), :])
        )
        for source in (up, down):
            for at in range(0, source.shape[1], width):
                pairs.append(
                    (source.at[:, pl.ds(at, width)], expert_pair.at[pl.ds(row, source.shape[0]), :])
                )
                row += source.shape[0]
    for copy in fetch(pairs, sems):
        copy.wait()


def pack(own, beside):
    own = [pltpu.with_memory_space_constraint(part, pltpu.HBM) for part in own]
    up, down, w_out_t = own
    width = up.shape[1] // 2
    pieces = [up.shape[1] // width, down.shape[1] // width]
    unit_rows = pieces[0] * up.shape[0] + pieces[1] * down.shape[0]
    return pl.pallas_call(
        pack_kernel,
        out_shape=(
            jax.ShapeDtypeStruct((2 * unit_rows, width), bf16),
            jax.ShapeDtypeStruct((2 * w_out_t.shape[0], w_out_t.shape[1] // 2), bf16),
        ),
        in_specs=[ANY] * 6,
        out_specs=(ANY, ANY),
        scratch_shapes=[pltpu.SemaphoreType.DMA((2 + 2 * sum(pieces),))],
        compiler_params=PARAMS,
        cost_estimate=LITTLE,
        name="pack",
    )(*own, *beside)


def as_column(row, eye):
    return jnp.sum(jnp.where(eye, row, 0.0), axis=1, keepdims=True)


def prepare_kernel(groups, slots_dev, *refs):
    sources, (cosine, sine, past, named, place, spread, send, tags, gain, late_gain, router) = (
        refs[:6],
        refs[6:17],
    )
    positions, slots, ids, flat_gains, flat_late, sems = refs[17:]
    copies = fetch(list(zip(sources, (positions, slots, ids, flat_gains, flat_late, router))), sems)
    for copy in copies:
        copy.wait()
    gain[...] = flat_gains[...].reshape(gain.shape)
    late_gain[...] = flat_late[...].reshape(late_gain.shape)
    lane = lax.axis_index("hd")
    block = positions.shape[1]

    def iota(shape, dim):
        return lax.broadcasted_iota(jnp.int32, shape, dim)

    eye = iota((block, block), 0) == iota((block, block), 1)
    reach = as_column(jnp.maximum(positions[...], 0).astype(f32), eye)
    past[...] = jnp.broadcast_to(reach, past.shape)
    column = iota((8, 128), 1)
    exponent = (column % 32).astype(f32) * (-2.0 / 64)
    inverse_freq = jnp.exp(exponent * np.float32(np.log(rope_base)))[:1, :]
    angles = reach * inverse_freq
    cosine[...] = jnp.cos(angles)
    turned = jnp.sin(angles)
    sine[...] = jnp.where(iota(angles.shape, 1) % 64 < 32, -turned, turned)

    tokens = ids.shape[1]
    experts = named.shape[1]
    cap = place.shape[0] // 2
    expert = iota((experts, tokens), 0)
    hit = jnp.zeros((experts, tokens), f32)
    for index in range(ids.shape[0]):
        hit = jnp.where(ids[index : index + 1, :] == expert, 1.0, hit)
    small_eye = (iota((tokens, tokens), 0) == iota((tokens, tokens), 1)).astype(f32)
    named[...] = lax.dot_general(small_eye, hit, LAST_DIMS, preferred_element_type=f32)
    upto = (iota((tokens, tokens), 0) <= iota((tokens, tokens), 1)).astype(f32)
    rank = jnp.dot(hit[:8, :], upto, preferred_element_type=f32) - 1.0
    slot = iota((2 * cap, tokens), 0).astype(f32)
    placed = jnp.zeros((2 * cap, tokens), f32)
    for live in range(2):
        order = jnp.where(lane == live, 0, cap).astype(f32)
        member = hit[live : live + 1, :] > 0.0
        placed = jnp.where(member & (slot == rank[live : live + 1, :] + order), 1.0, placed)
    place[...] = placed.astype(bf16)
    spread[...] = lax.dot_general(small_eye, placed, LAST_DIMS, preferred_element_type=f32).astype(bf16)

    where = slots[...]
    owner = jnp.where(where >= 0, where // slots_dev, -1)
    owner_hit = (iota((groups, block), 0) == owner).astype(f32)
    before = (iota((block, block), 0) <= iota((block, block), 1)).astype(f32)
    running = jnp.dot(owner_hit, before, preferred_element_type=f32)
    owner_rank = jnp.sum(owner_hit * running, axis=0, keepdims=True) - 1.0
    capc = send.shape[0] // groups
    row = jnp.where(owner >= 0, owner * capc + owner_rank.astype(jnp.int32), -1)
    send[...] = (iota(send.shape, 0) == row).astype(bf16)
    inside = jnp.where(where >= 0, where % slots_dev, 0)
    high = as_column((inside // 64 + 1).astype(f32), eye)
    low = as_column((inside % 64).astype(f32), eye)
    spot = iota(tags.shape, 1)
    tags[...] = jnp.where(spot == 0, high, jnp.where(spot == 1, low, 0.0)).astype(bf16)


def prepare(groups, slots_dev, positions, slots, ids, gain, late_gain, router):
    block, tokens = positions.shape[0], ids.shape[0]
    model, experts = router.shape
    cap = tokens // 4
    capc = 2 * block // groups
    shapes = [
        ((block, 128), f32),
        ((block, 128), f32),
        ((block, 128), f32),
        ((tokens, experts), f32),
        ((2 * cap, tokens), bf16),
        ((tokens, 2 * cap), bf16),
        ((groups * capc, block), bf16),
        ((block, 128), bf16),
        ((1, model), f32),
        ((1, model), f32),
        ((experts, model), bf16),
    ]
    sources = (positions[None], slots[None], ids.T, gain, late_gain, router.T)
    return pl.pallas_call(
        functools.partial(prepare_kernel, groups, slots_dev),
        out_shape=tuple(jax.ShapeDtypeStruct(shape, kind) for shape, kind in shapes),
        in_specs=[ANY] * 6,
        out_specs=(VMEM,) * len(shapes),
        scratch_shapes=[
            pltpu.VMEM((1, block), jnp.int32),
            pltpu.VMEM((1, block), jnp.int32),
            pltpu.VMEM(ids.shape[::-1], jnp.int32),
            pltpu.VMEM((model,), f32),
            pltpu.VMEM((model,), f32),
            pltpu.SemaphoreType.DMA((6,)),
        ],
        compiler_params=PARAMS,
        cost_estimate=LITTLE,
        name="prepare",
    )(*[pltpu.with_memory_space_constraint(source, pltpu.HBM) for source in sources])


def project_kernel(
    own, other, gain, cosine, sine, w_query, w_keyval, q_out, kv_out, seam_out, raw, rows, sems
):
    count = own.shape[0]
    lane = lax.axis_index("hd")
    mine = pl.multiple_of(lane * count, count)
    theirs = pl.multiple_of((1 - lane) * count, count)
    copies = fetch([(own, raw.at[0]), (other, raw.at[1])], sems)
    cos_q, sin_q = cosine[...], sine[...]
    column = lax.broadcasted_iota(jnp.int32, cos_q.shape, 1)
    lower = column % 64 < 32
    cos_kv = jnp.where(column < 64, cos_q, 1.0)
    sin_kv = jnp.where(column < 64, sin_q, 0.0)
    for index, first in ((0, mine), (1, theirs)):
        copies[index].wait()
        rows[pl.ds(first, count), :] = normalized(raw[index].astype(f32), gain[...])
    width = 256
    for weights, out, cos, sin in ((w_keyval, kv_out, cos_kv, sin_kv), (w_query, q_out, cos_q, sin_q)):
        for first in range(0, weights.shape[1], width):
            made = jnp.dot(rows[...], weights[:, first : first + width], preferred_element_type=f32)
            for part in range(0, width, 128):
                here = made[:, part : part + 128]
                turned = jnp.where(lower, pltpu.roll(here, 96, 1), pltpu.roll(here, 32, 1))
                done = (here * cos + turned * sin).astype(bf16)
                out[:, first + part : first + part + 128] = done
                if out is kv_out:
                    seam_out[:, first + part : first + part + 128] = done[count:, :]


def project(own, other, gain, cosine, sine, w_query, flat_kv):
    count, width = own.shape
    made = w_query.shape[1] + flat_kv.shape[1]
    return pl.pallas_call(
        project_kernel,
        out_shape=(
            jax.ShapeDtypeStruct((2 * count, w_query.shape[1]), bf16),
            jax.ShapeDtypeStruct((2 * count, flat_kv.shape[1]), bf16),
            jax.ShapeDtypeStruct((count, flat_kv.shape[1]), bf16),
        ),
        in_specs=[ANY] * 2 + [VMEM] * 5,
        out_specs=(VMEM, VMEM, VMEM),
        scratch_shapes=[
            pltpu.VMEM((2, count, width), bf16),
            pltpu.VMEM((2 * count, width), bf16),
            pltpu.SemaphoreType.DMA((2,)),
        ],
        compiler_params=PARAMS,
        cost_estimate=takes(6),
        name="project",
    )(own, other, gain, cosine, sine, w_query, flat_kv)


def attend_kernel(q, kv, seam, past, mixed, window, sem):
    count = seam.shape[0]
    copy = pltpu.make_async_copy(seam, window.at[pl.ds(0, count), :], sem)
    copy.start()
    window[count:, :] = kv[...]
    head = 64
    kv_heads = kv.shape[1] // (2 * head)
    per_kv = q.shape[1] // head // kv_heads
    shape = (count, 2 * count)
    row = lax.broadcasted_iota(jnp.int32, shape, 0) + count
    col = lax.broadcasted_iota(jnp.int32, shape, 1)
    for half in (1, 0):
        first = half * count
        if half == 0:
            copy.wait()
        reach = past[first : first + count, :1].astype(jnp.int32)
        visible = (col <= row) & (col >= row - reach)
        for kv_head in range(kv_heads):
            lanes = 2 * head * kv_head
            keys = window[first : first + 2 * count, lanes : lanes + head]
            values = window[first : first + 2 * count, lanes + head : lanes + 2 * head]
            for index in range(per_kv):
                at = (kv_head * per_kv + index) * head
                query = q[first : first + count, at : at + head]
                scores = lax.dot_general(query, keys, LAST_DIMS, preferred_element_type=f32)
                raised = jnp.where(visible, jnp.exp(scores * head ** (-0.5)), 0.0)
                probs = (raised / jnp.sum(raised, axis=-1, keepdims=True)).astype(bf16)
                made = jnp.dot(probs, values, preferred_element_type=f32)
                mixed[first : first + count, at : at + head] = made.astype(bf16)


def attend(q, kv, seam, past):
    count = seam.shape[0]
    return pl.pallas_call(
        attend_kernel,
        out_shape=jax.ShapeDtypeStruct(q.shape, bf16),
        in_specs=[VMEM, VMEM, ANY, VMEM],
        out_specs=VMEM,
        scratch_shapes=[
            pltpu.VMEM((3 * count, kv.shape[1]), bf16),
            pltpu.SemaphoreType.DMA,
        ],
        compiler_params=PARAMS,
        cost_estimate=takes(4),
        name="attend",
    )(q, kv, seam, past)


def outward_kernel(flip, groups, unit_rows, n_parts, mixed, *refs):
    parts, (out, w_out) = refs[:n_parts], refs[n_parts:]
    place_parts(groups, parts, unit_rows, [(0, unit_rows, w_out, 0)])
    count = out.shape[0]
    lane = lax.axis_index("hd")
    first = pl.multiple_of(((1 - lane) if flip else lane) * count, count)
    out[...] = lax.dot_general(
        mixed[pl.ds(first, count), :], w_out[...], LAST_DIMS, preferred_element_type=f32
    ).astype(out.dtype)


def outward(flip, out_type, groups, mixed, parts, unit_rows):
    count = mixed.shape[0] // 2
    width = groups * unit_rows
    depth = parts[0].shape[1]
    return pl.pallas_call(
        functools.partial(outward_kernel, flip, groups, unit_rows, len(parts)),
        out_shape=jax.ShapeDtypeStruct((count, width), out_type),
        in_specs=[VMEM] * (1 + len(parts)),
        out_specs=VMEM,
        scratch_shapes=[pltpu.VMEM((width, depth), bf16)],
        compiler_params=PARAMS,
        cost_estimate=reads(2 * width * depth),
        name="outward_send" if flip else "outward_keep",
    )(mixed, *parts)


def route_kernel(tokens, mine, arrived, gain, place, residual, moe_in, sent):
    added = (tokens[...].astype(f32) + (mine[...] + arrived[...].astype(f32))).astype(bf16)
    residual[...] = added
    moe_in[...] = normalized(added.astype(f32), gain[...])
    cap = sent.shape[0]
    rows = jnp.dot(place[cap:, :], moe_in[...], preferred_element_type=f32)
    sent[...] = rows.astype(bf16)


def route(tokens, mine, arrived, gain, place):
    cap = place.shape[0] // 2
    return pl.pallas_call(
        route_kernel,
        out_shape=(
            jax.ShapeDtypeStruct(tokens.shape, bf16),
            jax.ShapeDtypeStruct(tokens.shape, bf16),
            jax.ShapeDtypeStruct((cap, tokens.shape[1]), bf16),
        ),
        in_specs=[VMEM] * 5,
        out_specs=(VMEM,) * 3,
        compiler_params=PARAMS,
        cost_estimate=reads(10 * tokens.shape[0] * tokens.shape[1]),
        name="route",
    )(tokens, mine, arrived, gain, place)


def gate_kernel(moe_in, router, named, place, gates, own):
    cap = own.shape[0]
    own[...] = jnp.dot(place[:cap, :], moe_in[...], preferred_element_type=f32).astype(bf16)
    logits = lax.dot_general(moe_in[...], router[...], LAST_DIMS, preferred_element_type=f32)
    raised = jnp.where(named[...] > 0, jnp.exp(logits), 0.0)
    gates[...] = raised / jnp.sum(raised, axis=-1, keepdims=True)


def gate(moe_in, router_t, named, place):
    cap = place.shape[0] // 2
    return pl.pallas_call(
        gate_kernel,
        out_shape=(
            jax.ShapeDtypeStruct(named.shape, f32),
            jax.ShapeDtypeStruct((cap, moe_in.shape[1]), bf16),
        ),
        in_specs=[VMEM] * 4,
        out_specs=(VMEM,) * 2,
        compiler_params=PARAMS,
        cost_estimate=reads(1 << 20),
        name="gate",
    )(moe_in, router_t, named, place)


def expert_kernel(groups, up_rows, down_rows, n_parts, own, other, *refs):
    parts = refs[:n_parts]
    own_out, other_out, rows, gate_up, down = refs[n_parts:]
    width = parts[0].shape[1]
    count = own.shape[0]
    rows[:count, :] = own[...]
    rows[count:, :] = other[...]
    pieces = [(i * up_rows, up_rows, gate_up, i * width) for i in range(2)]
    pieces += [
        (2 * up_rows + i * down_rows, down_rows, down, i * width) for i in range(down.shape[1] // width)
    ]
    unit_rows = pieces[-1][0] + down_rows
    place_parts(groups, parts, unit_rows, pieces)
    both = jnp.dot(rows[...], gate_up[...], preferred_element_type=f32)
    gate, up = both[:, :width], both[:, width:]
    hidden = (gate / (1.0 + jnp.exp(-gate)) * up).astype(bf16)
    made = jnp.dot(hidden, down[...], preferred_element_type=f32).astype(bf16)
    own_out[...] = made[:count, :]
    other_out[...] = made[count:, :]


def expert(groups, own, other, parts, up_rows, down_rows):
    count, model = own.shape
    width = parts[0].shape[1]
    return pl.pallas_call(
        functools.partial(expert_kernel, groups, up_rows, down_rows, len(parts)),
        out_shape=(jax.ShapeDtypeStruct(own.shape, bf16),) * 2,
        in_specs=[VMEM] * (2 + len(parts)),
        out_specs=(VMEM, VMEM),
        scratch_shapes=[
            pltpu.VMEM((2 * count, model), bf16),
            pltpu.VMEM((groups * up_rows, 2 * width), bf16),
            pltpu.VMEM((groups * down_rows, model), bf16),
        ],
        compiler_params=PARAMS,
        cost_estimate=reads(2 * groups * 2 * (up_rows * 2 * width + down_rows * model)),
        name="expert",
    )(own, other, *parts)


def combine_kernel(residual, gates, spread, own, returned, out):
    lane = lax.axis_index("hd")
    count = own.shape[0]
    column = lax.broadcasted_iota(jnp.int32, gates.shape, 1)
    total = jnp.zeros(residual.shape, f32)
    for index, made in ((0, own), (1, returned)):
        live = lane if index == 0 else 1 - lane
        weight = jnp.sum(jnp.where(column == live, gates[...], 0.0), axis=-1, keepdims=True)
        picked = jnp.dot(
            spread[:, index * count : (index + 1) * count], made[...], preferred_element_type=f32
        )
        total += weight * picked
    out[...] = (residual[...].astype(f32) + total).astype(bf16)


def combine(residual, gates, spread, own, returned):
    return pl.pallas_call(
        combine_kernel,
        out_shape=jax.ShapeDtypeStruct(residual.shape, bf16),
        in_specs=[VMEM] * 5,
        out_specs=VMEM,
        compiler_params=PARAMS,
        cost_estimate=reads(6 * residual.shape[0] * residual.shape[1]),
        name="combine",
    )(residual, gates, spread, own, returned)


def bundle_kernel(send, kv, tags, out):
    groups, rows, _ = out.shape
    heads = kv.shape[1] // 128
    capc = send.shape[0] // groups
    packed = jnp.dot(send[...], kv[...], preferred_element_type=f32).astype(bf16)
    tagged = jnp.dot(send[...], tags[...], preferred_element_type=f32)
    one = (lax.broadcasted_iota(jnp.int32, (16, 128), 0) == lax.broadcasted_iota(jnp.int32, (16, 128), 1))
    for owner in range(groups):
        mine = slice(owner * capc, (owner + 1) * capc)
        for head in range(heads):
            out[owner, head * capc : (head + 1) * capc, :] = packed[mine, head * 128 : (head + 1) * 128]
        wide = jnp.concatenate([tagged[mine, :], jnp.zeros((128 - capc, 128), f32)], axis=0)
        out[owner, heads * capc :, :] = lax.dot_general(
            one.astype(f32), wide, LAST_DIMS, preferred_element_type=f32
        ).astype(bf16)


def bundle(groups, send, kv, tags):
    rows = send.shape[0] // groups * (kv.shape[1] // 128) + 16
    return pl.pallas_call(
        bundle_kernel,
        out_shape=jax.ShapeDtypeStruct((groups, rows, 128), bf16),
        in_specs=[VMEM] * 3,
        out_specs=VMEM,
        compiler_params=PARAMS,
        cost_estimate=takes(2),
        name="bundle",
    )(send, kv, tags)


def write_kernel(arrived, cache, out, rows):
    groups, size, _ = arrived.shape
    slots, heads, _ = cache.shape
    capc = (size - 16) // heads
    high, low = [], []
    for source in range(groups):
        for head in range(heads):
            rows[source * capc : (source + 1) * capc, head * 128 : (head + 1) * 128] = arrived[
                source, head * capc : (head + 1) * capc, :
            ]
        numbers = arrived[source, heads * capc :, :].astype(f32)
        high.append(numbers[0:1, :capc])
        low.append(numbers[1:2, :capc])
    slot = jnp.concatenate(high, axis=1) * 64.0 + jnp.concatenate(low, axis=1) - 64.0
    hit = (lax.broadcasted_iota(jnp.int32, (slots, slot.shape[1]), 0).astype(f32) == slot).astype(f32)
    known = jnp.max(hit, axis=1, keepdims=True) > 0.0
    made = jnp.dot(hit.astype(bf16), rows[...], preferred_element_type=f32)
    for head in range(heads):
        here = made[:, head * 128 : (head + 1) * 128]
        out[:, head, :] = jnp.where(known, here, cache[:, head, :].astype(f32)).astype(bf16)


def write(arrived, cache):
    slots, heads, lanes = cache.shape
    capc = (arrived.shape[1] - 16) // heads
    return pl.pallas_call(
        write_kernel,
        out_shape=jax.ShapeDtypeStruct(cache.shape, bf16),
        in_specs=[VMEM] * 2,
        out_specs=VMEM,
        scratch_shapes=[pltpu.VMEM((arrived.shape[0] * capc, heads * lanes), bf16)],
        compiler_params=PARAMS,
        cost_estimate=reads(1 << 21),
        name="write",
    )(arrived, cache)


def two_lane_shards(
    tokens,
    positions,
    attn_gain,
    w_query,
    w_keyval,
    w_out,
    moe_gain,
    router,
    w_gate_up,
    w_down,
    expert_ids,
    cache_slot,
    kv_cache,
):
    groups = lax.axis_size("grp")
    tok_rows, model = tokens.shape
    block = positions.shape[0]
    kv_local, head2 = w_keyval.shape[1:]
    kv_width = kv_local * head2
    slots_dev = kv_cache.shape[0]
    swap = functools.partial(lax.ppermute, axis_name="hd", perm=[(0, 1), (1, 0)])

    together = lax.optimization_barrier

    other_tokens = swap(tokens)
    own = (w_gate_up[0], w_down[0], w_out.T)
    up_rows, down_rows = own[0].shape[0], own[1].shape[0]
    beside = [lax.ppermute(part, "grp", sibling_pairs(groups)) for part in own]
    flat_kv = w_keyval.reshape(model, kv_width)
    cosine, sine, past, named, place, spread, send, tags, gain, late_gain, router_t = prepare(
        groups, slots_dev, positions, cache_slot, expert_ids, attn_gain, moe_gain, router
    )
    beside, cosine, flat_kv = together((beside, cosine, flat_kv))
    expert_pair, out_pair = pack(own, beside)
    out_ring = Ring(out_pair, groups)
    out_ring.step()
    expert_ring = Ring(expert_pair, groups)
    expert_ring.step()
    other_tokens = out_ring.pin(other_tokens)
    out_ring.step()

    q, kv, tail = project(tokens, other_tokens, gain, cosine, sine, w_query, flat_kv)
    seam = lax.ppermute(tail, "grp", [(g, g + 1) for g in range(groups - 1)])
    kv_now = expert_ring.pin(kv)
    expert_ring.step()
    outgoing = bundle(groups, send, kv_now, tags)
    seam, outgoing = out_ring.pin(seam, outgoing)
    out_ring.step()
    mixed = attend(q, kv, seam, past)
    mixed = out_ring.pin(mixed)
    out_ring.step()
    out_ring.mine[-1] = expert_ring.pin(out_ring.mine[-1])
    out_ring.share()
    expert_ring.step()
    sent = outward(True, bf16, groups, mixed, out_ring.parts(), out_ring.unit_rows)
    arrived = swap(sent)
    mixed = together((mixed, sent))[0]
    mine = outward(False, f32, groups, mixed, out_ring.parts(), out_ring.unit_rows)
    mine = expert_ring.pin(mine)
    expert_ring.share()
    expert_ring.step()
    outgoing, mine = together((outgoing, mine))
    arrived_cache = lax.all_to_all(outgoing, "grp", split_axis=0, concat_axis=0, tiled=True)

    residual, moe_in, sent_rows = route(tokens, mine, arrived, late_gain, place)
    landed = swap(sent_rows)
    gates, own_rows = gate(moe_in, router_t, named, place)
    own_rows = expert_ring.pin(own_rows)
    expert_ring.share()
    own_made, back = expert(
        groups, own_rows, landed, expert_ring.parts(), up_rows, down_rows
    )
    returned = swap(back)
    arrived_cache = together((arrived_cache, back))[0]
    cache_after = write(arrived_cache, kv_cache)
    returned, cache_after = together((returned, cache_after))
    layer_out = combine(residual, gates, spread, own_made, returned)
    return (layer_out, cache_after)


def passed_along(value, axis, steps):
    count = lax.axis_size(axis)
    initial, last = (max(0, -steps), min(count, count - steps))
    return lax.ppermute(value, axis, [(source, source + steps) for source in range(initial, last)])


def rms_norm(row_set, norm_gain):
    floats = row_set.astype(jnp.float32)
    factor = lax.rsqrt(jnp.mean(floats * floats, axis=-1, keepdims=True) + norm_eps)
    return (floats * factor * norm_gain).astype(jnp.bfloat16)


def rotate(vectors, angle_pos):
    halves = vectors.shape[-1] // 2
    inverse_freq = rope_base ** (-2.0 * jnp.arange(halves, dtype=jnp.float32) / vectors.shape[-1])
    angles = angle_pos[:, None, None] * inverse_freq[None, None, :]
    cosine = jnp.cos(angles)
    sine_part = jnp.sin(angles)
    first_half = vectors[..., :halves]
    second_half = vectors[..., halves:]
    return jnp.concatenate(
        [
            first_half * cosine - second_half * sine_part,
            second_half * cosine + first_half * sine_part,
        ],
        axis=-1,
    )


def expert_rows(row_set, gate_up, down_rows):
    gate_and_up = jnp.dot(row_set, gate_up, preferred_element_type=jnp.float32)
    inner_width = gate_and_up.shape[1] // 2
    hidden = (jax.nn.silu(gate_and_up[:, :inner_width]) * gate_and_up[:, inner_width:]).astype(
        jnp.bfloat16
    )
    return jnp.dot(hidden, down_rows, preferred_element_type=jnp.float32).astype(jnp.bfloat16)


def attend_rows(query_blk, keys_blk, vals_blk, visible, scale_qk):
    scores = (
        jnp.einsum("qkgd,skd->kgqs", query_blk, keys_blk, preferred_element_type=jnp.float32)
        * scale_qk
    )
    weights_f = jnp.where(visible[None, None], jnp.exp(scores), 0.0)
    prob_bf = (weights_f / jnp.sum(weights_f, axis=-1, keepdims=True)).astype(jnp.bfloat16)
    return jnp.einsum("kgqs,skd->qkgd", prob_bf, vals_blk, preferred_element_type=jnp.float32)


def shards(
    tokens,
    positions,
    attn_gain,
    w_query,
    w_keyval,
    w_out,
    moe_gain,
    router,
    w_gate_up,
    w_down,
    expert_ids,
    cache_slot,
    kv_cache,
):
    lane_count = lax.axis_size("hd")
    group_count = lax.axis_size("grp")
    tok_rows = tokens.shape[0]
    model_width = tokens.shape[1]
    block_len = positions.shape[0]
    seg_most = block_len // 2
    head_dim = w_keyval.shape[2] // 2
    kv_local = w_keyval.shape[1]
    q_local = w_query.shape[1] // head_dim
    per_kv = q_local // kv_local
    expert_cap = tok_rows // 4
    normed = rms_norm(tokens, attn_gain)
    flat_kv = w_keyval.reshape(model_width, kv_local * 2 * head_dim)
    section = lax.all_gather(normed, "hd", axis=0, tiled=True)
    projected = jnp.concatenate(
        [
            jnp.dot(section, w_query, preferred_element_type=jnp.float32),
            jnp.dot(section, flat_kv, preferred_element_type=jnp.float32),
        ],
        axis=1,
    )
    angle_pos = jnp.maximum(positions, 0).astype(jnp.float32)
    queries = rotate(
        projected[:, : q_local * head_dim].reshape(block_len, q_local, head_dim), angle_pos
    ).astype(jnp.bfloat16)
    key_val = projected[:, q_local * head_dim :].reshape(block_len, kv_local, 2 * head_dim)
    rotated = rotate(key_val[:, :, :head_dim], angle_pos).astype(jnp.bfloat16)
    stored = jnp.concatenate([rotated, key_val[:, :, head_dim:].astype(jnp.bfloat16)], axis=2)
    seam_rows = passed_along(stored[block_len - seg_most :], "grp", 1)
    window = jnp.concatenate([seam_rows, stored], axis=0)
    scale_qk = head_dim ** (-0.5)
    local_rows = jnp.arange(block_len, dtype=jnp.int32)
    lowest = local_rows - jnp.maximum(positions, 0)
    pieces_out = []
    for q_block in range(2):
        first_row = q_block * seg_most
        rows_here = first_row + jnp.arange(seg_most, dtype=jnp.int32)
        cols_here = first_row - seg_most + jnp.arange(2 * seg_most, dtype=jnp.int32)
        low_here = lowest[first_row : first_row + seg_most]
        visible = (cols_here[None, :] >= low_here[:, None]) & (
            cols_here[None, :] <= rows_here[:, None]
        )
        query_blk = queries[first_row : first_row + seg_most].reshape(
            seg_most, kv_local, per_kv, head_dim
        )
        keys_blk = window[first_row : first_row + 2 * seg_most, :, :head_dim]
        vals_blk = window[first_row : first_row + 2 * seg_most, :, head_dim:]
        mixed_rows = attend_rows(query_blk, keys_blk, vals_blk, visible, scale_qk)
        pieces_out.append(mixed_rows.reshape(seg_most, q_local * head_dim).astype(jnp.bfloat16))
    attended = jnp.concatenate(pieces_out, axis=0)
    slots_dev = kv_cache.shape[0]
    capc = 2 * block_len // group_count
    live_slot = cache_slot >= 0
    owners = jnp.where(live_slot, cache_slot // slots_dev, group_count)
    owner_hit = (owners[:, None] == jnp.arange(group_count, dtype=jnp.int32)[None, :]).astype(
        jnp.bfloat16
    )
    lower_tri = (local_rows[:, None] >= local_rows[None, :]).astype(jnp.bfloat16)
    running = jnp.dot(lower_tri, owner_hit, preferred_element_type=jnp.float32)
    owner_rank = jnp.sum(running * owner_hit.astype(jnp.float32), axis=1).astype(jnp.int32) - 1
    send_rows = jnp.where(live_slot, owners * capc + owner_rank, group_count * capc)
    outgoing_cache = (
        jnp.zeros((group_count * capc, kv_local, 2 * head_dim), jnp.bfloat16)
        .at[send_rows]
        .set(stored, mode="drop")
    )
    outgoing_slots = (
        jnp.full((group_count * capc,), -1, jnp.int32)
        .at[send_rows]
        .set(cache_slot % slots_dev, mode="drop")
    )
    arrived, arrived_slots = (
        lax.all_to_all(
            outgoing_cache.reshape(group_count, capc, kv_local, 2 * head_dim),
            "grp",
            split_axis=0,
            concat_axis=0,
            tiled=True,
        ),
        lax.all_to_all(
            outgoing_slots.reshape(group_count, capc),
            "grp",
            split_axis=0,
            concat_axis=0,
            tiled=True,
        ),
    )
    flat_slots = arrived_slots.reshape(group_count * capc)
    write_rows = jnp.where(flat_slots >= 0, flat_slots, slots_dev).astype(jnp.int32)
    cache_after = kv_cache.at[write_rows].set(
        arrived.reshape(group_count * capc, kv_local, 2 * head_dim), mode="drop"
    )
    by_token = lax.all_to_all(attended, "hd", split_axis=0, concat_axis=1, tiled=True)
    attn_proj = jnp.dot(
        by_token,
        lax.all_gather(w_out, "grp", axis=1, tiled=True),
        preferred_element_type=jnp.float32,
    )
    residual = (tokens.astype(jnp.float32) + attn_proj).astype(jnp.bfloat16)
    moe_in = rms_norm(residual, moe_gain)
    logits = jnp.dot(moe_in, router, preferred_element_type=jnp.float32)
    expert_range = jnp.arange(router.shape[1], dtype=jnp.int32)
    matches_all = expert_ids[:, :, None] == expert_range[None, None, :]
    chosen = jnp.sum(jnp.where(matches_all, logits[:, None, :], 0.0), axis=2)
    raised = jnp.exp(chosen)
    gates = raised / jnp.sum(raised, axis=1, keepdims=True)
    live_range = jnp.arange(lane_count, dtype=jnp.int32)
    matches = expert_ids[:, :, None] == live_range[None, None, :]
    member = jnp.any(matches, axis=1)
    weighting = jnp.sum(jnp.where(matches, gates[:, :, None], 0.0), axis=1)
    ranking = jnp.cumsum(member.astype(jnp.int32), axis=0) - 1
    target = jnp.where(member, live_range[None, :] * expert_cap + ranking, -1)
    slot_range = jnp.arange(lane_count * expert_cap, dtype=jnp.int32)
    slot_hits = target[None, :, :] == slot_range[:, None, None]
    placing = jnp.any(slot_hits, axis=2).astype(jnp.bfloat16)
    outgoing = (
        jnp.dot(placing, moe_in, preferred_element_type=jnp.float32)
        .astype(jnp.bfloat16)
        .reshape(lane_count, expert_cap, model_width)
    )
    gate_up_all, down_all = (
        lax.all_gather(w_gate_up, "grp", axis=1, tiled=True),
        lax.all_gather(w_down, "grp", axis=1, tiled=True),
    )
    gate_up_mat = gate_up_all[0]
    down_mat = down_all[0]
    landed = lax.all_to_all(outgoing, "hd", split_axis=0, concat_axis=0, tiled=True)
    results = expert_rows(landed.reshape(-1, model_width), gate_up_mat, down_mat).reshape(landed.shape)
    returned = lax.all_to_all(results, "hd", split_axis=0, concat_axis=0, tiled=True)
    flat_returned = returned.reshape(-1, model_width)
    fetched = flat_returned[jnp.maximum(target, 0)]
    used_weight = jnp.where(member, weighting, 0.0)
    moe_total = jnp.sum(used_weight[:, :, None] * fetched.astype(jnp.float32), axis=1)
    layer_out = (residual.astype(jnp.float32) + moe_total).astype(jnp.bfloat16)
    return (layer_out, cache_after)


def solution(mesh):
    two_lanes = mesh.shape["hd"] == 2 and mesh.shape["grp"] % 8 == 0
    return jax.shard_map(
        two_lane_shards if two_lanes else shards,
        mesh=mesh,
        in_specs=(
            P(("grp", "hd"), None),
            P("grp"),
            P(),
            P(None, "hd"),
            P(None, "hd", None),
            P(None, "grp"),
            P(),
            P(),
            P("hd", "grp", None),
            P("hd", "grp", None),
            P(("grp", "hd"), None),
            P("grp"),
            P("grp", "hd", None),
        ),
        out_specs=(P(("grp", "hd"), None), P("grp", "hd", None)),
        check_vma=False,
    )
```

```python
import functools

import jax
import jax.numpy as jnp
import numpy as np
from jax import lax
from jax.experimental import pallas as pl
from jax.experimental.pallas import tpu as pltpu
from jax.sharding import PartitionSpec as P

norm_eps = 1e-05
rope_base = 10000.0
bf16 = jnp.bfloat16
f32 = jnp.float32
LAST_DIMS = (((1,), (1,)), ((), ()))


def ring_cycle(groups):
    rows = groups // 4
    return [2 * r for r in range(rows)] + [2 * r + 1 for r in reversed(range(rows))]


def ring_pairs(groups):
    cycle = ring_cycle(groups)
    count = len(cycle)
    pairs = []
    for place, pair in enumerate(cycle):
        pairs.append((2 * pair, 2 * cycle[(place + 1) % count]))
        pairs.append((2 * pair + 1, 2 * cycle[(place - 1) % count] + 1))
    return pairs


def sibling_pairs(groups):
    return [(g, g ^ 1) for g in range(groups)]


def ring_sources(groups, me):
    count = groups // 2
    rows = count // 2
    side, pair = me % 2, me // 2
    row, col = pair // 2, pair % 2
    place = jnp.where(col == 0, row, count - 1 - row)

    def block(core, steps):
        there = (place + (2 * core - 1) * steps + count) % count
        other = jnp.where(there < rows, 2 * there, 2 * (count - 1 - there) + 1)
        return [2 * other + core, 2 * other + 1 - core]

    full = (count - 1) // 2
    listed = [me, me + 1 - 2 * side]
    for core in (side, 1 - side):
        for steps in range(1, full + 1):
            listed += block(core, steps)
    return listed + [block(side, count // 2)[0], block(1 - side, count // 2)[0]]


class Ring:
    def __init__(self, pair, groups):
        self.across = functools.partial(lax.ppermute, axis_name="grp", perm=ring_pairs(groups))
        self.beside = functools.partial(lax.ppermute, axis_name="grp", perm=sibling_pairs(groups))
        self.full = (groups // 2 - 1) // 2
        self.unit_rows = pair.shape[0] // 2
        self.mine = [pair]
        self.near = []

    def step(self):
        held = self.mine[-1]
        if len(self.mine) > self.full:
            held = held[: self.unit_rows]
        self.mine.append(self.across(held))

    def pin(self, *others):
        done = lax.optimization_barrier((self.mine[-1],) + others)
        self.mine[-1] = done[0]
        return done[1:] if len(others) > 1 else done[1]

    def share(self):
        for index in range(1 + len(self.near), len(self.mine)):
            self.near.append(self.beside(self.mine[index]))

    def parts(self):
        full = self.full
        return self.mine[: full + 1] + self.near[:full] + [self.mine[full + 1], self.near[full]]


def place_parts(groups, parts, unit_rows, pieces):
    sources = ring_sources(groups, lax.axis_index("grp"))
    shard = 0
    for part in parts:
        for unit in range(part.shape[0] // unit_rows):
            for first, rows, target, lane in pieces:
                at = pl.multiple_of(sources[shard] * rows, rows)
                start = unit * unit_rows + first
                target[pl.ds(at, rows), lane : lane + part.shape[1]] = part[start : start + rows, :]
            shard += 1


VMEM = pl.BlockSpec(memory_space=pltpu.VMEM)
ANY = pl.BlockSpec(memory_space=pl.ANY)
HBM = pl.BlockSpec(memory_space=pltpu.HBM)
PARAMS = pltpu.CompilerParams(vmem_limit_bytes=16 << 20)


LITTLE = pl.CostEstimate(flops=1, bytes_accessed=1, transcendentals=0)


def takes(us):
    return pl.CostEstimate(flops=int(us * 1.15e9), bytes_accessed=1, transcendentals=0)


def reads(nbytes):
    return pl.CostEstimate(flops=1, bytes_accessed=nbytes, transcendentals=0)


def normalized(floats, gain):
    factor = lax.rsqrt(jnp.mean(floats * floats, axis=-1, keepdims=True) + norm_eps)
    return (floats * factor * gain).astype(bf16)


def fetch(pairs, sems):
    copies = []
    for index, (source, target) in enumerate(pairs):
        copies.append(pltpu.make_async_copy(source, target, sems.at[index]))
        copies[-1].start()
    return copies


def pack_kernel(*refs):
    sources, (expert_pair, out_pair, sems) = refs[:6], refs[6:]
    width = expert_pair.shape[1]
    lane = lax.axis_index("hd")
    first = pl.multiple_of(lane * out_pair.shape[1], out_pair.shape[1])
    pairs = []
    row = 0
    for index in range(2):
        up, down, w_out = sources[3 * index : 3 * index + 3]
        count = w_out.shape[0]
        pairs.append(
            (w_out.at[:, pl.ds(first, out_pair.shape[1])], out_pair.at[pl.ds(index * count, count), :])
        )
        for source in (up, down):
            for at in range(0, source.shape[1], width):
                pairs.append(
                    (source.at[:, pl.ds(at, width)], expert_pair.at[pl.ds(row, source.shape[0]), :])
                )
                row += source.shape[0]
    for copy in fetch(pairs, sems):
        copy.wait()


def pack(own, beside):
    own = [pltpu.with_memory_space_constraint(part, pltpu.HBM) for part in own]
    up, down, w_out_t = own
    width = up.shape[1] // 2
    pieces = [up.shape[1] // width, down.shape[1] // width]
    unit_rows = pieces[0] * up.shape[0] + pieces[1] * down.shape[0]
    return pl.pallas_call(
        pack_kernel,
        out_shape=(
            jax.ShapeDtypeStruct((2 * unit_rows, width), bf16),
            jax.ShapeDtypeStruct((2 * w_out_t.shape[0], w_out_t.shape[1] // 2), bf16),
        ),
        in_specs=[ANY] * 6,
        out_specs=(ANY, ANY),
        scratch_shapes=[pltpu.SemaphoreType.DMA((2 + 2 * sum(pieces),))],
        compiler_params=PARAMS,
        cost_estimate=LITTLE,
        name="pack",
    )(*own, *beside)


def as_column(row, eye):
    return jnp.sum(jnp.where(eye, row, 0.0), axis=1, keepdims=True)


def prepare_kernel(groups, slots_dev, *refs):
    sources, (cosine, sine, past, named, place, spread, send, tags, gain, late_gain, router) = (
        refs[:6],
        refs[6:17],
    )
    positions, slots, ids, flat_gains, flat_late, sems = refs[17:]
    copies = fetch(list(zip(sources, (positions, slots, ids, flat_gains, flat_late, router))), sems)
    for copy in copies:
        copy.wait()
    gain[...] = flat_gains[...].reshape(gain.shape)
    late_gain[...] = flat_late[...].reshape(late_gain.shape)
    lane = lax.axis_index("hd")
    block = positions.shape[1]

    def iota(shape, dim):
        return lax.broadcasted_iota(jnp.int32, shape, dim)

    eye = iota((block, block), 0) == iota((block, block), 1)
    reach = as_column(jnp.maximum(positions[...], 0).astype(f32), eye)
    past[...] = jnp.broadcast_to(reach, past.shape)
    column = iota((8, 128), 1)
    exponent = (column % 32).astype(f32) * (-2.0 / 64)
    inverse_freq = jnp.exp(exponent * np.float32(np.log(rope_base)))[:1, :]
    angles = reach * inverse_freq
    cosine[...] = jnp.cos(angles)
    turned = jnp.sin(angles)
    sine[...] = jnp.where(iota(angles.shape, 1) % 64 < 32, -turned, turned)

    tokens = ids.shape[1]
    experts = named.shape[1]
    cap = place.shape[0] // 2
    expert = iota((experts, tokens), 0)
    hit = jnp.zeros((experts, tokens), f32)
    for index in range(ids.shape[0]):
        hit = jnp.where(ids[index : index + 1, :] == expert, 1.0, hit)
    small_eye = (iota((tokens, tokens), 0) == iota((tokens, tokens), 1)).astype(f32)
    named[...] = lax.dot_general(small_eye, hit, LAST_DIMS, preferred_element_type=f32)
    upto = (iota((tokens, tokens), 0) <= iota((tokens, tokens), 1)).astype(f32)
    rank = jnp.dot(hit[:8, :], upto, preferred_element_type=f32) - 1.0
    slot = iota((2 * cap, tokens), 0).astype(f32)
    placed = jnp.zeros((2 * cap, tokens), f32)
    for live in range(2):
        order = jnp.where(lane == live, 0, cap).astype(f32)
        member = hit[live : live + 1, :] > 0.0
        placed = jnp.where(member & (slot == rank[live : live + 1, :] + order), 1.0, placed)
    place[...] = placed.astype(bf16)
    spread[...] = lax.dot_general(small_eye, placed, LAST_DIMS, preferred_element_type=f32).astype(bf16)

    where = slots[...]
    owner = jnp.where(where >= 0, where // slots_dev, -1)
    owner_hit = (iota((groups, block), 0) == owner).astype(f32)
    before = (iota((block, block), 0) <= iota((block, block), 1)).astype(f32)
    running = jnp.dot(owner_hit, before, preferred_element_type=f32)
    owner_rank = jnp.sum(owner_hit * running, axis=0, keepdims=True) - 1.0
    capc = send.shape[0] // groups
    row = jnp.where(owner >= 0, owner * capc + owner_rank.astype(jnp.int32), -1)
    send[...] = (iota(send.shape, 0) == row).astype(bf16)
    inside = jnp.where(where >= 0, where % slots_dev, 0)
    high = as_column((inside // 64 + 1).astype(f32), eye)
    low = as_column((inside % 64).astype(f32), eye)
    spot = iota(tags.shape, 1)
    tags[...] = jnp.where(spot == 0, high, jnp.where(spot == 1, low, 0.0)).astype(bf16)


def prepare(groups, slots_dev, positions, slots, ids, gain, late_gain, router):
    block, tokens = positions.shape[0], ids.shape[0]
    model, experts = router.shape
    cap = tokens // 4
    capc = 2 * block // groups
    shapes = [
        ((block, 128), f32),
        ((block, 128), f32),
        ((block, 128), f32),
        ((tokens, experts), f32),
        ((2 * cap, tokens), bf16),
        ((tokens, 2 * cap), bf16),
        ((groups * capc, block), bf16),
        ((block, 128), bf16),
        ((1, model), f32),
        ((1, model), f32),
        ((experts, model), bf16),
    ]
    sources = (positions[None], slots[None], ids.T, gain, late_gain, router.T)
    return pl.pallas_call(
        functools.partial(prepare_kernel, groups, slots_dev),
        out_shape=tuple(jax.ShapeDtypeStruct(shape, kind) for shape, kind in shapes),
        in_specs=[ANY] * 6,
        out_specs=(VMEM,) * len(shapes),
        scratch_shapes=[
            pltpu.VMEM((1, block), jnp.int32),
            pltpu.VMEM((1, block), jnp.int32),
            pltpu.VMEM(ids.shape[::-1], jnp.int32),
            pltpu.VMEM((model,), f32),
            pltpu.VMEM((model,), f32),
            pltpu.SemaphoreType.DMA((6,)),
        ],
        compiler_params=PARAMS,
        cost_estimate=LITTLE,
        name="prepare",
    )(*[pltpu.with_memory_space_constraint(source, pltpu.HBM) for source in sources])


def project_kernel(
    own, other, gain, cosine, sine, w_query, w_keyval, q_out, kv_out, seam_out, raw, rows, sems
):
    count = own.shape[0]
    lane = lax.axis_index("hd")
    mine = pl.multiple_of(lane * count, count)
    theirs = pl.multiple_of((1 - lane) * count, count)
    copies = fetch([(own, raw.at[0]), (other, raw.at[1])], sems)
    cos_q, sin_q = cosine[...], sine[...]
    column = lax.broadcasted_iota(jnp.int32, cos_q.shape, 1)
    lower = column % 64 < 32
    cos_kv = jnp.where(column < 64, cos_q, 1.0)
    sin_kv = jnp.where(column < 64, sin_q, 0.0)
    for index, first in ((0, mine), (1, theirs)):
        copies[index].wait()
        rows[pl.ds(first, count), :] = normalized(raw[index].astype(f32), gain[...])
    width = 256
    for weights, out, cos, sin in ((w_keyval, kv_out, cos_kv, sin_kv), (w_query, q_out, cos_q, sin_q)):
        for first in range(0, weights.shape[1], width):
            made = jnp.dot(rows[...], weights[:, first : first + width], preferred_element_type=f32)
            for part in range(0, width, 128):
                here = made[:, part : part + 128]
                turned = jnp.where(lower, pltpu.roll(here, 96, 1), pltpu.roll(here, 32, 1))
                done = (here * cos + turned * sin).astype(bf16)
                out[:, first + part : first + part + 128] = done
                if out is kv_out:
                    seam_out[:, first + part : first + part + 128] = done[count:, :]


def project(own, other, gain, cosine, sine, w_query, flat_kv):
    count, width = own.shape
    made = w_query.shape[1] + flat_kv.shape[1]
    return pl.pallas_call(
        project_kernel,
        out_shape=(
            jax.ShapeDtypeStruct((2 * count, w_query.shape[1]), bf16),
            jax.ShapeDtypeStruct((2 * count, flat_kv.shape[1]), bf16),
            jax.ShapeDtypeStruct((count, flat_kv.shape[1]), bf16),
        ),
        in_specs=[ANY] * 2 + [VMEM] * 5,
        out_specs=(VMEM, VMEM, VMEM),
        scratch_shapes=[
            pltpu.VMEM((2, count, width), bf16),
            pltpu.VMEM((2 * count, width), bf16),
            pltpu.SemaphoreType.DMA((2,)),
        ],
        compiler_params=PARAMS,
        cost_estimate=takes(8),
        name="project",
    )(own, other, gain, cosine, sine, w_query, flat_kv)


def attend_kernel(q, kv, seam, past, mixed, window, sem):
    count = seam.shape[0]
    copy = pltpu.make_async_copy(seam, window.at[pl.ds(0, count), :], sem)
    copy.start()
    window[count:, :] = kv[...]
    head = 64
    kv_heads = kv.shape[1] // (2 * head)
    per_kv = q.shape[1] // head // kv_heads
    shape = (count, 2 * count)
    row = lax.broadcasted_iota(jnp.int32, shape, 0) + count
    col = lax.broadcasted_iota(jnp.int32, shape, 1)
    for half in (1, 0):
        first = half * count
        if half == 0:
            copy.wait()
        reach = past[first : first + count, :1].astype(jnp.int32)
        visible = (col <= row) & (col >= row - reach)
        for kv_head in range(kv_heads):
            lanes = 2 * head * kv_head
            keys = window[first : first + 2 * count, lanes : lanes + head]
            values = window[first : first + 2 * count, lanes + head : lanes + 2 * head]
            for index in range(per_kv):
                at = (kv_head * per_kv + index) * head
                query = q[first : first + count, at : at + head]
                scores = lax.dot_general(query, keys, LAST_DIMS, preferred_element_type=f32)
                raised = jnp.where(visible, jnp.exp(scores * head ** (-0.5)), 0.0)
                probs = (raised / jnp.sum(raised, axis=-1, keepdims=True)).astype(bf16)
                made = jnp.dot(probs, values, preferred_element_type=f32)
                mixed[first : first + count, at : at + head] = made.astype(bf16)


def attend(q, kv, seam, past):
    count = seam.shape[0]
    return pl.pallas_call(
        attend_kernel,
        out_shape=jax.ShapeDtypeStruct(q.shape, bf16),
        in_specs=[VMEM, VMEM, ANY, VMEM],
        out_specs=VMEM,
        scratch_shapes=[
            pltpu.VMEM((3 * count, kv.shape[1]), bf16),
            pltpu.SemaphoreType.DMA,
        ],
        compiler_params=PARAMS,
        cost_estimate=takes(4),
        name="attend",
    )(q, kv, seam, past)


def outward_kernel(flip, groups, unit_rows, n_parts, mixed, *refs):
    parts, (out, w_out) = refs[:n_parts], refs[n_parts:]
    place_parts(groups, parts, unit_rows, [(0, unit_rows, w_out, 0)])
    count = out.shape[0]
    lane = lax.axis_index("hd")
    first = pl.multiple_of(((1 - lane) if flip else lane) * count, count)
    out[...] = lax.dot_general(
        mixed[pl.ds(first, count), :], w_out[...], LAST_DIMS, preferred_element_type=f32
    ).astype(out.dtype)


def outward(flip, out_type, groups, mixed, parts, unit_rows):
    count = mixed.shape[0] // 2
    width = groups * unit_rows
    depth = parts[0].shape[1]
    return pl.pallas_call(
        functools.partial(outward_kernel, flip, groups, unit_rows, len(parts)),
        out_shape=jax.ShapeDtypeStruct((count, width), out_type),
        in_specs=[VMEM] * (1 + len(parts)),
        out_specs=VMEM,
        scratch_shapes=[pltpu.VMEM((width, depth), bf16)],
        compiler_params=PARAMS,
        cost_estimate=reads(2 * width * depth),
        name="outward_send" if flip else "outward_keep",
    )(mixed, *parts)


def route_kernel(tokens, mine, arrived, gain, place, residual, moe_in, sent):
    added = (tokens[...].astype(f32) + (mine[...] + arrived[...].astype(f32))).astype(bf16)
    residual[...] = added
    moe_in[...] = normalized(added.astype(f32), gain[...])
    cap = sent.shape[0]
    rows = jnp.dot(place[cap:, :], moe_in[...], preferred_element_type=f32)
    sent[...] = rows.astype(bf16)


def route(tokens, mine, arrived, gain, place):
    cap = place.shape[0] // 2
    return pl.pallas_call(
        route_kernel,
        out_shape=(
            jax.ShapeDtypeStruct(tokens.shape, bf16),
            jax.ShapeDtypeStruct(tokens.shape, bf16),
            jax.ShapeDtypeStruct((cap, tokens.shape[1]), bf16),
        ),
        in_specs=[VMEM] * 5,
        out_specs=(VMEM,) * 3,
        compiler_params=PARAMS,
        cost_estimate=reads(10 * tokens.shape[0] * tokens.shape[1]),
        name="route",
    )(tokens, mine, arrived, gain, place)


def gate_kernel(moe_in, router, named, place, gates, own):
    cap = own.shape[0]
    own[...] = jnp.dot(place[:cap, :], moe_in[...], preferred_element_type=f32).astype(bf16)
    logits = lax.dot_general(moe_in[...], router[...], LAST_DIMS, preferred_element_type=f32)
    raised = jnp.where(named[...] > 0, jnp.exp(logits), 0.0)
    gates[...] = raised / jnp.sum(raised, axis=-1, keepdims=True)


def gate(moe_in, router_t, named, place):
    cap = place.shape[0] // 2
    return pl.pallas_call(
        gate_kernel,
        out_shape=(
            jax.ShapeDtypeStruct(named.shape, f32),
            jax.ShapeDtypeStruct((cap, moe_in.shape[1]), bf16),
        ),
        in_specs=[VMEM] * 4,
        out_specs=(VMEM,) * 2,
        compiler_params=PARAMS,
        cost_estimate=reads(1 << 20),
        name="gate",
    )(moe_in, router_t, named, place)


def expert_kernel(groups, up_rows, down_rows, n_parts, own, other, *refs):
    parts = refs[:n_parts]
    own_out, other_out, rows, gate_up, down = refs[n_parts:]
    width = parts[0].shape[1]
    count = own.shape[0]
    rows[:count, :] = own[...]
    rows[count:, :] = other[...]
    pieces = [(i * up_rows, up_rows, gate_up, i * width) for i in range(2)]
    pieces += [
        (2 * up_rows + i * down_rows, down_rows, down, i * width) for i in range(down.shape[1] // width)
    ]
    unit_rows = pieces[-1][0] + down_rows
    place_parts(groups, parts, unit_rows, pieces)
    both = jnp.dot(rows[...], gate_up[...], preferred_element_type=f32)
    gate, up = both[:, :width], both[:, width:]
    hidden = (gate / (1.0 + jnp.exp(-gate)) * up).astype(bf16)
    made = jnp.dot(hidden, down[...], preferred_element_type=f32).astype(bf16)
    own_out[...] = made[:count, :]
    other_out[...] = made[count:, :]


def expert(groups, own, other, parts, up_rows, down_rows):
    count, model = own.shape
    width = parts[0].shape[1]
    return pl.pallas_call(
        functools.partial(expert_kernel, groups, up_rows, down_rows, len(parts)),
        out_shape=(jax.ShapeDtypeStruct(own.shape, bf16),) * 2,
        in_specs=[VMEM] * (2 + len(parts)),
        out_specs=(VMEM, VMEM),
        scratch_shapes=[
            pltpu.VMEM((2 * count, model), bf16),
            pltpu.VMEM((groups * up_rows, 2 * width), bf16),
            pltpu.VMEM((groups * down_rows, model), bf16),
        ],
        compiler_params=PARAMS,
        cost_estimate=reads(2 * groups * 2 * (up_rows * 2 * width + down_rows * model)),
        name="expert",
    )(own, other, *parts)


def combine_kernel(residual, gates, spread, own, returned, out):
    lane = lax.axis_index("hd")
    count = own.shape[0]
    column = lax.broadcasted_iota(jnp.int32, gates.shape, 1)
    total = jnp.zeros(residual.shape, f32)
    for index, made in ((0, own), (1, returned)):
        live = lane if index == 0 else 1 - lane
        weight = jnp.sum(jnp.where(column == live, gates[...], 0.0), axis=-1, keepdims=True)
        picked = jnp.dot(
            spread[:, index * count : (index + 1) * count], made[...], preferred_element_type=f32
        )
        total += weight * picked
    out[...] = (residual[...].astype(f32) + total).astype(bf16)


def combine(residual, gates, spread, own, returned):
    return pl.pallas_call(
        combine_kernel,
        out_shape=jax.ShapeDtypeStruct(residual.shape, bf16),
        in_specs=[VMEM] * 5,
        out_specs=VMEM,
        compiler_params=PARAMS,
        cost_estimate=reads(6 * residual.shape[0] * residual.shape[1]),
        name="combine",
    )(residual, gates, spread, own, returned)


def bundle_kernel(send, kv, tags, out):
    groups, rows, _ = out.shape
    heads = kv.shape[1] // 128
    capc = send.shape[0] // groups
    packed = jnp.dot(send[...], kv[...], preferred_element_type=f32).astype(bf16)
    tagged = jnp.dot(send[...], tags[...], preferred_element_type=f32)
    one = (lax.broadcasted_iota(jnp.int32, (16, 128), 0) == lax.broadcasted_iota(jnp.int32, (16, 128), 1))
    for owner in range(groups):
        mine = slice(owner * capc, (owner + 1) * capc)
        for head in range(heads):
            out[owner, head * capc : (head + 1) * capc, :] = packed[mine, head * 128 : (head + 1) * 128]
        wide = jnp.concatenate([tagged[mine, :], jnp.zeros((128 - capc, 128), f32)], axis=0)
        out[owner, heads * capc :, :] = lax.dot_general(
            one.astype(f32), wide, LAST_DIMS, preferred_element_type=f32
        ).astype(bf16)


def bundle(groups, send, kv, tags):
    rows = send.shape[0] // groups * (kv.shape[1] // 128) + 16
    return pl.pallas_call(
        bundle_kernel,
        out_shape=jax.ShapeDtypeStruct((groups, rows, 128), bf16),
        in_specs=[VMEM] * 3,
        out_specs=VMEM,
        compiler_params=PARAMS,
        cost_estimate=takes(2),
        name="bundle",
    )(send, kv, tags)


def write_kernel(arrived, cache, out, rows):
    groups, size, _ = arrived.shape
    slots, heads, _ = cache.shape
    capc = (size - 16) // heads
    high, low = [], []
    for source in range(groups):
        for head in range(heads):
            rows[source * capc : (source + 1) * capc, head * 128 : (head + 1) * 128] = arrived[
                source, head * capc : (head + 1) * capc, :
            ]
        numbers = arrived[source, heads * capc :, :].astype(f32)
        high.append(numbers[0:1, :capc])
        low.append(numbers[1:2, :capc])
    slot = jnp.concatenate(high, axis=1) * 64.0 + jnp.concatenate(low, axis=1) - 64.0
    hit = (lax.broadcasted_iota(jnp.int32, (slots, slot.shape[1]), 0).astype(f32) == slot).astype(f32)
    known = jnp.max(hit, axis=1, keepdims=True) > 0.0
    made = jnp.dot(hit.astype(bf16), rows[...], preferred_element_type=f32)
    for head in range(heads):
        here = made[:, head * 128 : (head + 1) * 128]
        out[:, head, :] = jnp.where(known, here, cache[:, head, :].astype(f32)).astype(bf16)


def write(arrived, cache):
    slots, heads, lanes = cache.shape
    capc = (arrived.shape[1] - 16) // heads
    return pl.pallas_call(
        write_kernel,
        out_shape=jax.ShapeDtypeStruct(cache.shape, bf16),
        in_specs=[VMEM] * 2,
        out_specs=VMEM,
        scratch_shapes=[pltpu.VMEM((arrived.shape[0] * capc, heads * lanes), bf16)],
        compiler_params=PARAMS,
        cost_estimate=reads(1 << 21),
        name="write",
    )(arrived, cache)


def two_lane_shards(
    tokens,
    positions,
    attn_gain,
    w_query,
    w_keyval,
    w_out,
    moe_gain,
    router,
    w_gate_up,
    w_down,
    expert_ids,
    cache_slot,
    kv_cache,
):
    groups = lax.axis_size("grp")
    tok_rows, model = tokens.shape
    block = positions.shape[0]
    kv_local, head2 = w_keyval.shape[1:]
    kv_width = kv_local * head2
    slots_dev = kv_cache.shape[0]
    swap = functools.partial(lax.ppermute, axis_name="hd", perm=[(0, 1), (1, 0)])

    together = lax.optimization_barrier

    other_tokens = swap(tokens)
    own = (w_gate_up[0], w_down[0], w_out.T)
    up_rows, down_rows = own[0].shape[0], own[1].shape[0]
    beside = [lax.ppermute(part, "grp", sibling_pairs(groups)) for part in own]
    expert_pair, out_pair = pack(own, beside)
    out_ring = Ring(out_pair, groups)
    out_ring.step()
    expert_ring = Ring(expert_pair, groups)
    expert_ring.step()
    w_keyval, positions = together((w_keyval, positions, out_pair))[:2]
    flat_kv = w_keyval.reshape(model, kv_width)
    cosine, sine, past, named, place, spread, send, tags, gain, late_gain, router_t = prepare(
        groups, slots_dev, positions, cache_slot, expert_ids, attn_gain, moe_gain, router
    )
    other_tokens, cosine, flat_kv = out_ring.pin(other_tokens, cosine, flat_kv)
    out_ring.step()

    q, kv, tail = project(tokens, other_tokens, gain, cosine, sine, w_query, flat_kv)
    seam = lax.ppermute(tail, "grp", [(g, g + 1) for g in range(groups - 1)])
    kv_now = expert_ring.pin(kv)
    expert_ring.step()
    outgoing = bundle(groups, send, kv_now, tags)
    seam, outgoing = out_ring.pin(seam, outgoing)
    out_ring.step()
    mixed = attend(q, kv, seam, past)
    outgoing, mixed = together((outgoing, mixed))
    arrived_cache = lax.all_to_all(outgoing, "grp", split_axis=0, concat_axis=0, tiled=True)
    mixed = out_ring.pin(mixed)
    out_ring.step()
    out_ring.mine[-1] = expert_ring.pin(out_ring.mine[-1])
    out_ring.share()
    expert_ring.step()
    sent = outward(True, bf16, groups, mixed, out_ring.parts(), out_ring.unit_rows)
    arrived = swap(sent)
    mixed = together((mixed, sent))[0]
    mine = outward(False, f32, groups, mixed, out_ring.parts(), out_ring.unit_rows)
    mine = expert_ring.pin(mine)
    expert_ring.share()
    expert_ring.step()

    residual, moe_in, sent_rows = route(tokens, mine, arrived, late_gain, place)
    landed = swap(sent_rows)
    gates, own_rows = gate(moe_in, router_t, named, place)
    own_rows = expert_ring.pin(own_rows)
    expert_ring.share()
    own_made, back = expert(
        groups, own_rows, landed, expert_ring.parts(), up_rows, down_rows
    )
    returned = swap(back)
    arrived_cache = together((arrived_cache, back))[0]
    cache_after = write(arrived_cache, kv_cache)
    returned, cache_after = together((returned, cache_after))
    layer_out = combine(residual, gates, spread, own_made, returned)
    return (layer_out, cache_after)


def passed_along(value, axis, steps):
    count = lax.axis_size(axis)
    initial, last = (max(0, -steps), min(count, count - steps))
    return lax.ppermute(value, axis, [(source, source + steps) for source in range(initial, last)])


def rms_norm(row_set, norm_gain):
    floats = row_set.astype(jnp.float32)
    factor = lax.rsqrt(jnp.mean(floats * floats, axis=-1, keepdims=True) + norm_eps)
    return (floats * factor * norm_gain).astype(jnp.bfloat16)


def rotate(vectors, angle_pos):
    halves = vectors.shape[-1] // 2
    inverse_freq = rope_base ** (-2.0 * jnp.arange(halves, dtype=jnp.float32) / vectors.shape[-1])
    angles = angle_pos[:, None, None] * inverse_freq[None, None, :]
    cosine = jnp.cos(angles)
    sine_part = jnp.sin(angles)
    first_half = vectors[..., :halves]
    second_half = vectors[..., halves:]
    return jnp.concatenate(
        [
            first_half * cosine - second_half * sine_part,
            second_half * cosine + first_half * sine_part,
        ],
        axis=-1,
    )


def expert_rows(row_set, gate_up, down_rows):
    gate_and_up = jnp.dot(row_set, gate_up, preferred_element_type=jnp.float32)
    inner_width = gate_and_up.shape[1] // 2
    hidden = (jax.nn.silu(gate_and_up[:, :inner_width]) * gate_and_up[:, inner_width:]).astype(
        jnp.bfloat16
    )
    return jnp.dot(hidden, down_rows, preferred_element_type=jnp.float32).astype(jnp.bfloat16)


def attend_rows(query_blk, keys_blk, vals_blk, visible, scale_qk):
    scores = (
        jnp.einsum("qkgd,skd->kgqs", query_blk, keys_blk, preferred_element_type=jnp.float32)
        * scale_qk
    )
    weights_f = jnp.where(visible[None, None], jnp.exp(scores), 0.0)
    prob_bf = (weights_f / jnp.sum(weights_f, axis=-1, keepdims=True)).astype(jnp.bfloat16)
    return jnp.einsum("kgqs,skd->qkgd", prob_bf, vals_blk, preferred_element_type=jnp.float32)


def shards(
    tokens,
    positions,
    attn_gain,
    w_query,
    w_keyval,
    w_out,
    moe_gain,
    router,
    w_gate_up,
    w_down,
    expert_ids,
    cache_slot,
    kv_cache,
):
    lane_count = lax.axis_size("hd")
    group_count = lax.axis_size("grp")
    tok_rows = tokens.shape[0]
    model_width = tokens.shape[1]
    block_len = positions.shape[0]
    seg_most = block_len // 2
    head_dim = w_keyval.shape[2] // 2
    kv_local = w_keyval.shape[1]
    q_local = w_query.shape[1] // head_dim
    per_kv = q_local // kv_local
    expert_cap = tok_rows // 4
    normed = rms_norm(tokens, attn_gain)
    flat_kv = w_keyval.reshape(model_width, kv_local * 2 * head_dim)
    section = lax.all_gather(normed, "hd", axis=0, tiled=True)
    projected = jnp.concatenate(
        [
            jnp.dot(section, w_query, preferred_element_type=jnp.float32),
            jnp.dot(section, flat_kv, preferred_element_type=jnp.float32),
        ],
        axis=1,
    )
    angle_pos = jnp.maximum(positions, 0).astype(jnp.float32)
    queries = rotate(
        projected[:, : q_local * head_dim].reshape(block_len, q_local, head_dim), angle_pos
    ).astype(jnp.bfloat16)
    key_val = projected[:, q_local * head_dim :].reshape(block_len, kv_local, 2 * head_dim)
    rotated = rotate(key_val[:, :, :head_dim], angle_pos).astype(jnp.bfloat16)
    stored = jnp.concatenate([rotated, key_val[:, :, head_dim:].astype(jnp.bfloat16)], axis=2)
    seam_rows = passed_along(stored[block_len - seg_most :], "grp", 1)
    window = jnp.concatenate([seam_rows, stored], axis=0)
    scale_qk = head_dim ** (-0.5)
    local_rows = jnp.arange(block_len, dtype=jnp.int32)
    lowest = local_rows - jnp.maximum(positions, 0)
    pieces_out = []
    for q_block in range(2):
        first_row = q_block * seg_most
        rows_here = first_row + jnp.arange(seg_most, dtype=jnp.int32)
        cols_here = first_row - seg_most + jnp.arange(2 * seg_most, dtype=jnp.int32)
        low_here = lowest[first_row : first_row + seg_most]
        visible = (cols_here[None, :] >= low_here[:, None]) & (
            cols_here[None, :] <= rows_here[:, None]
        )
        query_blk = queries[first_row : first_row + seg_most].reshape(
            seg_most, kv_local, per_kv, head_dim
        )
        keys_blk = window[first_row : first_row + 2 * seg_most, :, :head_dim]
        vals_blk = window[first_row : first_row + 2 * seg_most, :, head_dim:]
        mixed_rows = attend_rows(query_blk, keys_blk, vals_blk, visible, scale_qk)
        pieces_out.append(mixed_rows.reshape(seg_most, q_local * head_dim).astype(jnp.bfloat16))
    attended = jnp.concatenate(pieces_out, axis=0)
    slots_dev = kv_cache.shape[0]
    capc = 2 * block_len // group_count
    live_slot = cache_slot >= 0
    owners = jnp.where(live_slot, cache_slot // slots_dev, group_count)
    owner_hit = (owners[:, None] == jnp.arange(group_count, dtype=jnp.int32)[None, :]).astype(
        jnp.bfloat16
    )
    lower_tri = (local_rows[:, None] >= local_rows[None, :]).astype(jnp.bfloat16)
    running = jnp.dot(lower_tri, owner_hit, preferred_element_type=jnp.float32)
    owner_rank = jnp.sum(running * owner_hit.astype(jnp.float32), axis=1).astype(jnp.int32) - 1
    send_rows = jnp.where(live_slot, owners * capc + owner_rank, group_count * capc)
    outgoing_cache = (
        jnp.zeros((group_count * capc, kv_local, 2 * head_dim), jnp.bfloat16)
        .at[send_rows]
        .set(stored, mode="drop")
    )
    outgoing_slots = (
        jnp.full((group_count * capc,), -1, jnp.int32)
        .at[send_rows]
        .set(cache_slot % slots_dev, mode="drop")
    )
    arrived, arrived_slots = (
        lax.all_to_all(
            outgoing_cache.reshape(group_count, capc, kv_local, 2 * head_dim),
            "grp",
            split_axis=0,
            concat_axis=0,
            tiled=True,
        ),
        lax.all_to_all(
            outgoing_slots.reshape(group_count, capc),
            "grp",
            split_axis=0,
            concat_axis=0,
            tiled=True,
        ),
    )
    flat_slots = arrived_slots.reshape(group_count * capc)
    write_rows = jnp.where(flat_slots >= 0, flat_slots, slots_dev).astype(jnp.int32)
    cache_after = kv_cache.at[write_rows].set(
        arrived.reshape(group_count * capc, kv_local, 2 * head_dim), mode="drop"
    )
    by_token = lax.all_to_all(attended, "hd", split_axis=0, concat_axis=1, tiled=True)
    attn_proj = jnp.dot(
        by_token,
        lax.all_gather(w_out, "grp", axis=1, tiled=True),
        preferred_element_type=jnp.float32,
    )
    residual = (tokens.astype(jnp.float32) + attn_proj).astype(jnp.bfloat16)
    moe_in = rms_norm(residual, moe_gain)
    logits = jnp.dot(moe_in, router, preferred_element_type=jnp.float32)
    expert_range = jnp.arange(router.shape[1], dtype=jnp.int32)
    matches_all = expert_ids[:, :, None] == expert_range[None, None, :]
    chosen = jnp.sum(jnp.where(matches_all, logits[:, None, :], 0.0), axis=2)
    raised = jnp.exp(chosen)
    gates = raised / jnp.sum(raised, axis=1, keepdims=True)
    live_range = jnp.arange(lane_count, dtype=jnp.int32)
    matches = expert_ids[:, :, None] == live_range[None, None, :]
    member = jnp.any(matches, axis=1)
    weighting = jnp.sum(jnp.where(matches, gates[:, :, None], 0.0), axis=1)
    ranking = jnp.cumsum(member.astype(jnp.int32), axis=0) - 1
    target = jnp.where(member, live_range[None, :] * expert_cap + ranking, -1)
    slot_range = jnp.arange(lane_count * expert_cap, dtype=jnp.int32)
    slot_hits = target[None, :, :] == slot_range[:, None, None]
    placing = jnp.any(slot_hits, axis=2).astype(jnp.bfloat16)
    outgoing = (
        jnp.dot(placing, moe_in, preferred_element_type=jnp.float32)
        .astype(jnp.bfloat16)
        .reshape(lane_count, expert_cap, model_width)
    )
    gate_up_all, down_all = (
        lax.all_gather(w_gate_up, "grp", axis=1, tiled=True),
        lax.all_gather(w_down, "grp", axis=1, tiled=True),
    )
    gate_up_mat = gate_up_all[0]
    down_mat = down_all[0]
    landed = lax.all_to_all(outgoing, "hd", split_axis=0, concat_axis=0, tiled=True)
    results = expert_rows(landed.reshape(-1, model_width), gate_up_mat, down_mat).reshape(landed.shape)
    returned = lax.all_to_all(results, "hd", split_axis=0, concat_axis=0, tiled=True)
    flat_returned = returned.reshape(-1, model_width)
    fetched = flat_returned[jnp.maximum(target, 0)]
    used_weight = jnp.where(member, weighting, 0.0)
    moe_total = jnp.sum(used_weight[:, :, None] * fetched.astype(jnp.float32), axis=1)
    layer_out = (residual.astype(jnp.float32) + moe_total).astype(jnp.bfloat16)
    return (layer_out, cache_after)


def solution(mesh):
    two_lanes = mesh.shape["hd"] == 2 and mesh.shape["grp"] % 8 == 0
    return jax.shard_map(
        two_lane_shards if two_lanes else shards,
        mesh=mesh,
        in_specs=(
            P(("grp", "hd"), None),
            P("grp"),
            P(),
            P(None, "hd"),
            P(None, "hd", None),
            P(None, "grp"),
            P(),
            P(),
            P("hd", "grp", None),
            P("hd", "grp", None),
            P(("grp", "hd"), None),
            P("grp"),
            P("grp", "hd", None),
        ),
        out_specs=(P(("grp", "hd"), None), P("grp", "hd", None)),
        check_vma=False,
    )
```

```python
import functools

import jax
import jax.numpy as jnp
import numpy as np
from jax import lax
from jax.experimental import pallas as pl
from jax.experimental.pallas import tpu as pltpu
from jax.sharding import PartitionSpec as P

norm_eps = 1e-05
rope_base = 10000.0
bf16 = jnp.bfloat16
f32 = jnp.float32
LAST_DIMS = (((1,), (1,)), ((), ()))


def ring_cycle(groups):
    rows = groups // 4
    return [2 * r for r in range(rows)] + [2 * r + 1 for r in reversed(range(rows))]


def ring_pairs(groups):
    cycle = ring_cycle(groups)
    count = len(cycle)
    pairs = []
    for place, pair in enumerate(cycle):
        pairs.append((2 * pair, 2 * cycle[(place + 1) % count]))
        pairs.append((2 * pair + 1, 2 * cycle[(place - 1) % count] + 1))
    return pairs


def sibling_pairs(groups):
    return [(g, g ^ 1) for g in range(groups)]


def ring_sources(groups, me):
    count = groups // 2
    rows = count // 2
    side, pair = me % 2, me // 2
    row, col = pair // 2, pair % 2
    place = jnp.where(col == 0, row, count - 1 - row)

    def block(core, steps):
        there = (place + (2 * core - 1) * steps + count) % count
        other = jnp.where(there < rows, 2 * there, 2 * (count - 1 - there) + 1)
        return [2 * other + core, 2 * other + 1 - core]

    full = (count - 1) // 2
    listed = [me, me + 1 - 2 * side]
    for core in (side, 1 - side):
        for steps in range(1, full + 1):
            listed += block(core, steps)
    return listed + [block(side, count // 2)[0], block(1 - side, count // 2)[0]]


class Ring:
    def __init__(self, pair, groups):
        self.across = functools.partial(lax.ppermute, axis_name="grp", perm=ring_pairs(groups))
        self.beside = functools.partial(lax.ppermute, axis_name="grp", perm=sibling_pairs(groups))
        self.full = (groups // 2 - 1) // 2
        self.unit_rows = pair.shape[0] // 2
        self.mine = [pair]
        self.near = []

    def step(self):
        held = self.mine[-1]
        if len(self.mine) > self.full:
            held = held[: self.unit_rows]
        self.mine.append(self.across(held))

    def pin(self, *others):
        done = lax.optimization_barrier((self.mine[-1],) + others)
        self.mine[-1] = done[0]
        return done[1:] if len(others) > 1 else done[1]

    def share(self, upto=None):
        for index in range(1 + len(self.near), 1 + (upto or len(self.mine) - 1)):
            self.near.append(self.beside(self.mine[index]))

    def parts(self):
        full = self.full
        return self.mine[: full + 1] + self.near[:full] + [self.mine[full + 1], self.near[full]]


def place_parts(groups, parts, unit_rows, pieces):
    sources = ring_sources(groups, lax.axis_index("grp"))
    shard = 0
    for part in parts:
        for unit in range(part.shape[0] // unit_rows):
            for first, rows, target, lane in pieces:
                at = pl.multiple_of(sources[shard] * rows, rows)
                start = unit * unit_rows + first
                target[pl.ds(at, rows), lane : lane + part.shape[1]] = part[start : start + rows, :]
            shard += 1


VMEM = pl.BlockSpec(memory_space=pltpu.VMEM)
ANY = pl.BlockSpec(memory_space=pl.ANY)
HBM = pl.BlockSpec(memory_space=pltpu.HBM)
PARAMS = pltpu.CompilerParams(vmem_limit_bytes=16 << 20)


LITTLE = pl.CostEstimate(flops=1, bytes_accessed=1, transcendentals=0)


def takes(us, nbytes=1):
    return pl.CostEstimate(flops=int(us * 1.15e9), bytes_accessed=nbytes, transcendentals=0)


def reads(nbytes):
    return pl.CostEstimate(flops=1, bytes_accessed=nbytes, transcendentals=0)


def normalized(floats, gain):
    factor = lax.rsqrt(jnp.mean(floats * floats, axis=-1, keepdims=True) + norm_eps)
    return (floats * factor * gain).astype(bf16)


def fetch(pairs, sems):
    copies = []
    for index, (source, target) in enumerate(pairs):
        copies.append(pltpu.make_async_copy(source, target, sems.at[index]))
        copies[-1].start()
    return copies


def pack_kernel(*refs):
    sources, (expert_pair, out_pair, sems) = refs[:6], refs[6:]
    width = expert_pair.shape[1]
    lane = lax.axis_index("hd")
    first = pl.multiple_of(lane * out_pair.shape[1], out_pair.shape[1])
    pairs = []
    row = 0
    for index in range(2):
        up, down, w_out = sources[3 * index : 3 * index + 3]
        count = w_out.shape[0]
        pairs.append(
            (w_out.at[:, pl.ds(first, out_pair.shape[1])], out_pair.at[pl.ds(index * count, count), :])
        )
        for source in (up, down):
            for at in range(0, source.shape[1], width):
                pairs.append(
                    (source.at[:, pl.ds(at, width)], expert_pair.at[pl.ds(row, source.shape[0]), :])
                )
                row += source.shape[0]
    for copy in fetch(pairs, sems):
        copy.wait()


def pack(own, beside):
    own = [pltpu.with_memory_space_constraint(part, pltpu.HBM) for part in own]
    up, down, w_out_t = own
    width = up.shape[1] // 2
    pieces = [up.shape[1] // width, down.shape[1] // width]
    unit_rows = pieces[0] * up.shape[0] + pieces[1] * down.shape[0]
    return pl.pallas_call(
        pack_kernel,
        out_shape=(
            jax.ShapeDtypeStruct((2 * unit_rows, width), bf16),
            jax.ShapeDtypeStruct((2 * w_out_t.shape[0], w_out_t.shape[1] // 2), bf16),
        ),
        in_specs=[ANY] * 6,
        out_specs=(ANY, ANY),
        scratch_shapes=[pltpu.SemaphoreType.DMA((2 + 2 * sum(pieces),))],
        compiler_params=PARAMS,
        cost_estimate=LITTLE,
        name="pack",
    )(*own, *beside)


def as_column(row, eye):
    return jnp.sum(jnp.where(eye, row, 0.0), axis=1, keepdims=True)


def named_experts(ids, experts):
    tokens = ids.shape[1]
    expert = lax.broadcasted_iota(jnp.int32, (experts, tokens), 0)
    hit = jnp.zeros((experts, tokens), f32)
    for index in range(ids.shape[0]):
        hit = jnp.where(ids[index : index + 1, :] == expert, 1.0, hit)
    return hit


def prepare_kernel(groups, slots_dev, *refs):
    sources, (cosine, sine, past, place, spread, send, tags, gain, late_gain) = refs[:5], refs[5:14]
    positions, slots, ids, flat_gains, flat_late, sems = refs[14:]
    copies = fetch(list(zip(sources, (positions, slots, ids, flat_gains, flat_late))), sems)
    for copy in copies:
        copy.wait()
    gain[...] = flat_gains[...].reshape(gain.shape)
    late_gain[...] = flat_late[...].reshape(late_gain.shape)
    lane = lax.axis_index("hd")
    block = positions.shape[1]

    def iota(shape, dim):
        return lax.broadcasted_iota(jnp.int32, shape, dim)

    eye = iota((block, block), 0) == iota((block, block), 1)
    reach = as_column(jnp.maximum(positions[...], 0).astype(f32), eye)
    past[...] = jnp.broadcast_to(reach, past.shape)
    column = iota((8, 128), 1)
    exponent = (column % 32).astype(f32) * (-2.0 / 64)
    inverse_freq = jnp.exp(exponent * np.float32(np.log(rope_base)))[:1, :]
    angles = reach * inverse_freq
    cosine[...] = jnp.cos(angles)
    turned = jnp.sin(angles)
    sine[...] = jnp.where(iota(angles.shape, 1) % 64 < 32, -turned, turned)

    tokens = ids.shape[1]
    cap = place.shape[0] // 2
    hit = named_experts(ids, 8)
    small_eye = (iota((tokens, tokens), 0) == iota((tokens, tokens), 1)).astype(f32)
    upto = (iota((tokens, tokens), 0) <= iota((tokens, tokens), 1)).astype(f32)
    rank = jnp.dot(hit, upto, preferred_element_type=f32) - 1.0
    slot = iota((2 * cap, tokens), 0).astype(f32)
    placed = jnp.zeros((2 * cap, tokens), f32)
    for live in range(2):
        order = jnp.where(lane == live, 0, cap).astype(f32)
        member = hit[live : live + 1, :] > 0.0
        placed = jnp.where(member & (slot == rank[live : live + 1, :] + order), 1.0, placed)
    place[...] = placed.astype(bf16)
    spread[...] = lax.dot_general(small_eye, placed, LAST_DIMS, preferred_element_type=f32).astype(bf16)

    where = slots[...]
    owner = jnp.where(where >= 0, where // slots_dev, -1)
    owner_hit = (iota((groups, block), 0) == owner).astype(f32)
    before = (iota((block, block), 0) <= iota((block, block), 1)).astype(f32)
    running = jnp.dot(owner_hit, before, preferred_element_type=f32)
    owner_rank = jnp.sum(owner_hit * running, axis=0, keepdims=True) - 1.0
    capc = send.shape[0] // groups
    row = jnp.where(owner >= 0, owner * capc + owner_rank.astype(jnp.int32), -1)
    send[...] = (iota(send.shape, 0) == row).astype(bf16)
    inside = jnp.where(where >= 0, where % slots_dev, 0)
    high = as_column((inside // 64 + 1).astype(f32), eye)
    low = as_column((inside % 64).astype(f32), eye)
    spot = iota(tags.shape, 1)
    tags[...] = jnp.where(spot == 0, high, jnp.where(spot == 1, low, 0.0)).astype(bf16)


def prepare(groups, slots_dev, positions, slots, ids, gain, late_gain):
    block, tokens = positions.shape[0], ids.shape[0]
    model = gain.shape[0]
    cap = tokens // 4
    capc = 2 * block // groups
    shapes = [
        ((block, 128), f32),
        ((block, 128), f32),
        ((block, 128), f32),
        ((2 * cap, tokens), bf16),
        ((tokens, 2 * cap), bf16),
        ((groups * capc, block), bf16),
        ((block, 128), bf16),
        ((1, model), f32),
        ((1, model), f32),
    ]
    sources = (positions[None], slots[None], ids.T, gain, late_gain)
    return pl.pallas_call(
        functools.partial(prepare_kernel, groups, slots_dev),
        out_shape=tuple(jax.ShapeDtypeStruct(shape, kind) for shape, kind in shapes),
        in_specs=[ANY] * 5,
        out_specs=(VMEM,) * len(shapes),
        scratch_shapes=[
            pltpu.VMEM((1, block), jnp.int32),
            pltpu.VMEM((1, block), jnp.int32),
            pltpu.VMEM(ids.shape[::-1], jnp.int32),
            pltpu.VMEM((model,), f32),
            pltpu.VMEM((model,), f32),
            pltpu.SemaphoreType.DMA((5,)),
        ],
        compiler_params=PARAMS,
        cost_estimate=LITTLE,
        name="prepare",
    )(*[pltpu.with_memory_space_constraint(source, pltpu.HBM) for source in sources])


def project_kernel(
    own, other, gain, cosine, sine, w_query, w_keyval, q_out, kv_out, seam_out, raw, rows, sems
):
    count = own.shape[0]
    lane = lax.axis_index("hd")
    mine = pl.multiple_of(lane * count, count)
    theirs = pl.multiple_of((1 - lane) * count, count)
    copies = fetch([(own, raw.at[0]), (other, raw.at[1])], sems)
    cos_q, sin_q = cosine[...], sine[...]
    column = lax.broadcasted_iota(jnp.int32, cos_q.shape, 1)
    lower = column % 64 < 32
    cos_kv = jnp.where(column < 64, cos_q, 1.0)
    sin_kv = jnp.where(column < 64, sin_q, 0.0)
    for index, first in ((0, mine), (1, theirs)):
        copies[index].wait()
        rows[pl.ds(first, count), :] = normalized(raw[index].astype(f32), gain[...])
    width = 256
    for weights, out, cos, sin in ((w_keyval, kv_out, cos_kv, sin_kv), (w_query, q_out, cos_q, sin_q)):
        for first in range(0, weights.shape[1], width):
            made = jnp.dot(rows[...], weights[:, first : first + width], preferred_element_type=f32)
            for part in range(0, width, 128):
                here = made[:, part : part + 128]
                turned = jnp.where(lower, pltpu.roll(here, 96, 1), pltpu.roll(here, 32, 1))
                done = (here * cos + turned * sin).astype(bf16)
                out[:, first + part : first + part + 128] = done
                if out is kv_out:
                    seam_out[:, first + part : first + part + 128] = done[count:, :]


def project(own, other, gain, cosine, sine, w_query, flat_kv):
    count, width = own.shape
    made = w_query.shape[1] + flat_kv.shape[1]
    return pl.pallas_call(
        project_kernel,
        out_shape=(
            jax.ShapeDtypeStruct((2 * count, w_query.shape[1]), bf16),
            jax.ShapeDtypeStruct((2 * count, flat_kv.shape[1]), bf16),
            jax.ShapeDtypeStruct((count, flat_kv.shape[1]), bf16),
        ),
        in_specs=[ANY] * 2 + [VMEM] * 5,
        out_specs=(VMEM, VMEM, VMEM),
        scratch_shapes=[
            pltpu.VMEM((2, count, width), bf16),
            pltpu.VMEM((2 * count, width), bf16),
            pltpu.SemaphoreType.DMA((2,)),
        ],
        compiler_params=PARAMS,
        cost_estimate=takes(8),
        name="project",
    )(own, other, gain, cosine, sine, w_query, flat_kv)


def attend_kernel(q, kv, seam, past, mixed, window, sem):
    count = seam.shape[0]
    copy = pltpu.make_async_copy(seam, window.at[pl.ds(0, count), :], sem)
    copy.start()
    window[count:, :] = kv[...]
    head = 64
    kv_heads = kv.shape[1] // (2 * head)
    per_kv = q.shape[1] // head // kv_heads
    shape = (count, 2 * count)
    row = lax.broadcasted_iota(jnp.int32, shape, 0) + count
    col = lax.broadcasted_iota(jnp.int32, shape, 1)
    for half in (1, 0):
        first = half * count
        if half == 0:
            copy.wait()
        reach = past[first : first + count, :1].astype(jnp.int32)
        visible = (col <= row) & (col >= row - reach)
        for kv_head in range(kv_heads):
            lanes = 2 * head * kv_head
            keys = window[first : first + 2 * count, lanes : lanes + head]
            values = window[first : first + 2 * count, lanes + head : lanes + 2 * head]
            for index in range(per_kv):
                at = (kv_head * per_kv + index) * head
                query = q[first : first + count, at : at + head]
                scores = lax.dot_general(query, keys, LAST_DIMS, preferred_element_type=f32)
                raised = jnp.where(visible, jnp.exp(scores * head ** (-0.5)), 0.0)
                probs = (raised / jnp.sum(raised, axis=-1, keepdims=True)).astype(bf16)
                made = jnp.dot(probs, values, preferred_element_type=f32)
                mixed[first : first + count, at : at + head] = made.astype(bf16)


def attend(q, kv, seam, past):
    count = seam.shape[0]
    return pl.pallas_call(
        attend_kernel,
        out_shape=jax.ShapeDtypeStruct(q.shape, bf16),
        in_specs=[VMEM, VMEM, ANY, VMEM],
        out_specs=VMEM,
        scratch_shapes=[
            pltpu.VMEM((3 * count, kv.shape[1]), bf16),
            pltpu.SemaphoreType.DMA,
        ],
        compiler_params=PARAMS,
        cost_estimate=takes(4),
        name="attend",
    )(q, kv, seam, past)


def outward_kernel(flip, groups, unit_rows, n_parts, mixed, *refs):
    parts, (out, w_out) = refs[:n_parts], refs[n_parts:]
    place_parts(groups, parts, unit_rows, [(0, unit_rows, w_out, 0)])
    count = out.shape[0]
    lane = lax.axis_index("hd")
    first = pl.multiple_of(((1 - lane) if flip else lane) * count, count)
    out[...] = lax.dot_general(
        mixed[pl.ds(first, count), :], w_out[...], LAST_DIMS, preferred_element_type=f32
    ).astype(out.dtype)


def outward(flip, out_type, groups, mixed, parts, unit_rows):
    count = mixed.shape[0] // 2
    width = groups * unit_rows
    depth = parts[0].shape[1]
    return pl.pallas_call(
        functools.partial(outward_kernel, flip, groups, unit_rows, len(parts)),
        out_shape=jax.ShapeDtypeStruct((count, width), out_type),
        in_specs=[VMEM] * (1 + len(parts)),
        out_specs=VMEM,
        scratch_shapes=[pltpu.VMEM((width, depth), bf16)],
        compiler_params=PARAMS,
        cost_estimate=reads(2 * width * depth),
        name="outward_send" if flip else "outward_keep",
    )(mixed, *parts)


def route_kernel(tokens, mine, arrived, gain, place, residual, moe_in, sent):
    added = (tokens[...].astype(f32) + (mine[...] + arrived[...].astype(f32))).astype(bf16)
    residual[...] = added
    moe_in[...] = normalized(added.astype(f32), gain[...])
    cap = sent.shape[0]
    rows = jnp.dot(place[cap:, :], moe_in[...], preferred_element_type=f32)
    sent[...] = rows.astype(bf16)


def route(tokens, mine, arrived, gain, place):
    cap = place.shape[0] // 2
    return pl.pallas_call(
        route_kernel,
        out_shape=(
            jax.ShapeDtypeStruct(tokens.shape, bf16),
            jax.ShapeDtypeStruct(tokens.shape, bf16),
            jax.ShapeDtypeStruct((cap, tokens.shape[1]), bf16),
        ),
        in_specs=[VMEM] * 5,
        out_specs=(VMEM,) * 3,
        compiler_params=PARAMS,
        cost_estimate=takes(2, 10 * tokens.shape[0] * tokens.shape[1]),
        name="route",
    )(tokens, mine, arrived, gain, place)


def gate_kernel(moe_in, router, ids, place, gates, own):
    cap = own.shape[0]
    own[...] = jnp.dot(place[:cap, :], moe_in[...], preferred_element_type=f32).astype(bf16)
    hit = named_experts(ids, router.shape[0])
    tokens = ids.shape[1]
    row = lax.broadcasted_iota(jnp.int32, (tokens, tokens), 0)
    eye = (row == lax.broadcasted_iota(jnp.int32, (tokens, tokens), 1)).astype(f32)
    named = lax.dot_general(eye, hit, LAST_DIMS, preferred_element_type=f32)
    logits = lax.dot_general(moe_in[...], router[...], LAST_DIMS, preferred_element_type=f32)
    raised = jnp.where(named > 0, jnp.exp(logits), 0.0)
    gates[...] = raised / jnp.sum(raised, axis=-1, keepdims=True)


def gate(moe_in, router_t, ids_t, place):
    cap = place.shape[0] // 2
    return pl.pallas_call(
        gate_kernel,
        out_shape=(
            jax.ShapeDtypeStruct((moe_in.shape[0], router_t.shape[0]), f32),
            jax.ShapeDtypeStruct((cap, moe_in.shape[1]), bf16),
        ),
        in_specs=[VMEM] * 4,
        out_specs=(VMEM,) * 2,
        compiler_params=PARAMS,
        cost_estimate=LITTLE,
        name="gate",
    )(moe_in, router_t, ids_t, place)


def expert_kernel(groups, up_rows, down_rows, n_parts, own, other, *refs):
    parts = refs[:n_parts]
    own_out, other_out, rows, gate_up, down = refs[n_parts:]
    width = parts[0].shape[1]
    count = own.shape[0]
    rows[:count, :] = own[...]
    rows[count:, :] = other[...]
    pieces = [(i * up_rows, up_rows, gate_up, i * width) for i in range(2)]
    pieces += [
        (2 * up_rows + i * down_rows, down_rows, down, i * width) for i in range(down.shape[1] // width)
    ]
    unit_rows = pieces[-1][0] + down_rows
    place_parts(groups, parts, unit_rows, pieces)
    both = jnp.dot(rows[...], gate_up[...], preferred_element_type=f32)
    gate, up = both[:, :width], both[:, width:]
    hidden = (gate / (1.0 + jnp.exp(-gate)) * up).astype(bf16)
    made = jnp.dot(hidden, down[...], preferred_element_type=f32).astype(bf16)
    own_out[...] = made[:count, :]
    other_out[...] = made[count:, :]


def expert(groups, own, other, parts, up_rows, down_rows):
    count, model = own.shape
    width = parts[0].shape[1]
    return pl.pallas_call(
        functools.partial(expert_kernel, groups, up_rows, down_rows, len(parts)),
        out_shape=(jax.ShapeDtypeStruct(own.shape, bf16),) * 2,
        in_specs=[VMEM] * (2 + len(parts)),
        out_specs=(VMEM, VMEM),
        scratch_shapes=[
            pltpu.VMEM((2 * count, model), bf16),
            pltpu.VMEM((groups * up_rows, 2 * width), bf16),
            pltpu.VMEM((groups * down_rows, model), bf16),
        ],
        compiler_params=PARAMS,
        cost_estimate=reads(2 * groups * 2 * (up_rows * 2 * width + down_rows * model)),
        name="expert",
    )(own, other, *parts)


def combine_kernel(residual, gates, spread, own, returned, out):
    lane = lax.axis_index("hd")
    count = own.shape[0]
    column = lax.broadcasted_iota(jnp.int32, gates.shape, 1)
    total = jnp.zeros(residual.shape, f32)
    for index, made in ((0, own), (1, returned)):
        live = lane if index == 0 else 1 - lane
        weight = jnp.sum(jnp.where(column == live, gates[...], 0.0), axis=-1, keepdims=True)
        picked = jnp.dot(
            spread[:, index * count : (index + 1) * count], made[...], preferred_element_type=f32
        )
        total += weight * picked
    out[...] = (residual[...].astype(f32) + total).astype(bf16)


def combine(residual, gates, spread, own, returned):
    return pl.pallas_call(
        combine_kernel,
        out_shape=jax.ShapeDtypeStruct(residual.shape, bf16),
        in_specs=[VMEM] * 5,
        out_specs=VMEM,
        compiler_params=PARAMS,
        cost_estimate=reads(6 * residual.shape[0] * residual.shape[1]),
        name="combine",
    )(residual, gates, spread, own, returned)


def bundle_kernel(send, kv, tags, out):
    groups, rows, _ = out.shape
    heads = kv.shape[1] // 128
    capc = send.shape[0] // groups
    packed = jnp.dot(send[...], kv[...], preferred_element_type=f32).astype(bf16)
    tagged = jnp.dot(send[...], tags[...], preferred_element_type=f32)
    one = (lax.broadcasted_iota(jnp.int32, (16, 128), 0) == lax.broadcasted_iota(jnp.int32, (16, 128), 1))
    for owner in range(groups):
        mine = slice(owner * capc, (owner + 1) * capc)
        for head in range(heads):
            out[owner, head * capc : (head + 1) * capc, :] = packed[mine, head * 128 : (head + 1) * 128]
        wide = jnp.concatenate([tagged[mine, :], jnp.zeros((128 - capc, 128), f32)], axis=0)
        out[owner, heads * capc :, :] = lax.dot_general(
            one.astype(f32), wide, LAST_DIMS, preferred_element_type=f32
        ).astype(bf16)


def bundle(groups, send, kv, tags):
    rows = send.shape[0] // groups * (kv.shape[1] // 128) + 16
    return pl.pallas_call(
        bundle_kernel,
        out_shape=jax.ShapeDtypeStruct((groups, rows, 128), bf16),
        in_specs=[VMEM] * 3,
        out_specs=VMEM,
        compiler_params=PARAMS,
        cost_estimate=takes(2),
        name="bundle",
    )(send, kv, tags)


def write_kernel(arrived, cache, out, rows):
    groups, size, _ = arrived.shape
    slots, heads, _ = cache.shape
    capc = (size - 16) // heads
    high, low = [], []
    for source in range(groups):
        for head in range(heads):
            rows[source * capc : (source + 1) * capc, head * 128 : (head + 1) * 128] = arrived[
                source, head * capc : (head + 1) * capc, :
            ]
        numbers = arrived[source, heads * capc :, :].astype(f32)
        high.append(numbers[0:1, :capc])
        low.append(numbers[1:2, :capc])
    slot = jnp.concatenate(high, axis=1) * 64.0 + jnp.concatenate(low, axis=1) - 64.0
    hit = (lax.broadcasted_iota(jnp.int32, (slots, slot.shape[1]), 0).astype(f32) == slot).astype(f32)
    known = jnp.max(hit, axis=1, keepdims=True) > 0.0
    made = jnp.dot(hit.astype(bf16), rows[...], preferred_element_type=f32)
    for head in range(heads):
        here = made[:, head * 128 : (head + 1) * 128]
        out[:, head, :] = jnp.where(known, here, cache[:, head, :].astype(f32)).astype(bf16)


def write(arrived, cache):
    slots, heads, lanes = cache.shape
    capc = (arrived.shape[1] - 16) // heads
    return pl.pallas_call(
        write_kernel,
        out_shape=jax.ShapeDtypeStruct(cache.shape, bf16),
        in_specs=[VMEM] * 2,
        out_specs=VMEM,
        scratch_shapes=[pltpu.VMEM((arrived.shape[0] * capc, heads * lanes), bf16)],
        compiler_params=PARAMS,
        cost_estimate=reads(1 << 21),
        name="write",
    )(arrived, cache)


def two_lane_shards(
    tokens,
    positions,
    attn_gain,
    w_query,
    w_keyval,
    w_out,
    moe_gain,
    router,
    w_gate_up,
    w_down,
    expert_ids,
    cache_slot,
    kv_cache,
):
    groups = lax.axis_size("grp")
    tok_rows, model = tokens.shape
    block = positions.shape[0]
    kv_local, head2 = w_keyval.shape[1:]
    kv_width = kv_local * head2
    slots_dev = kv_cache.shape[0]
    swap = functools.partial(lax.ppermute, axis_name="hd", perm=[(0, 1), (1, 0)])

    together = lax.optimization_barrier

    other_tokens = swap(tokens)
    own = (w_gate_up[0], w_down[0], w_out.T)
    up_rows, down_rows = own[0].shape[0], own[1].shape[0]
    beside = [lax.ppermute(part, "grp", sibling_pairs(groups)) for part in own]
    expert_pair, out_pair = pack(own, beside)
    out_ring = Ring(out_pair, groups)
    out_ring.step()
    expert_ring = Ring(expert_pair, groups)
    expert_ring.step()
    w_keyval, positions = together((w_keyval, positions, out_pair))[:2]
    flat_kv = w_keyval.reshape(model, kv_width)
    cosine, sine, past, place, spread, send, tags, gain, late_gain = prepare(
        groups, slots_dev, positions, cache_slot, expert_ids, attn_gain, moe_gain
    )
    other_tokens, cosine, flat_kv = out_ring.pin(other_tokens, cosine, flat_kv)
    out_ring.step()

    q, kv, tail = project(tokens, other_tokens, gain, cosine, sine, w_query, flat_kv)
    seam = lax.ppermute(tail, "grp", [(g, g + 1) for g in range(groups - 1)])
    kv_now = out_ring.pin(kv)
    out_ring.step()
    kv_now = expert_ring.pin(kv_now)
    expert_ring.step()
    outgoing = bundle(groups, send, kv_now, tags)
    seam, outgoing = together((seam, outgoing))
    out_ring.share(2)
    mixed = attend(q, kv, seam, past)
    mixed, out_ring.near = together((mixed, out_ring.near))
    mixed = out_ring.pin(mixed)
    out_ring.step()
    out_ring.share(3)
    mixed, out_ring.near = together((mixed, out_ring.near))
    mixed = out_ring.pin(mixed)
    out_ring.share()
    sent = outward(True, bf16, groups, mixed, out_ring.parts(), out_ring.unit_rows)
    arrived = swap(sent)
    mixed, outgoing = together((mixed, outgoing, sent))[:2]
    mine = outward(False, f32, groups, mixed, out_ring.parts(), out_ring.unit_rows)
    arrived_cache = lax.all_to_all(outgoing, "grp", split_axis=0, concat_axis=0, tiled=True)
    mine = expert_ring.pin(mine)
    expert_ring.share()
    expert_ring.step()

    residual, moe_in, sent_rows = route(tokens, mine, arrived, late_gain, place)
    landed = swap(sent_rows)
    moe_in = expert_ring.pin(moe_in)
    expert_ring.share()
    expert_ring.step()
    gates, own_rows = gate(moe_in, router.T, expert_ids.T, place)
    landed, own_rows = expert_ring.pin(landed, own_rows)
    expert_ring.share()
    own_made, back = expert(
        groups, own_rows, landed, expert_ring.parts(), up_rows, down_rows
    )
    returned = swap(back)
    arrived_cache = together((arrived_cache, back))[0]
    cache_after = write(arrived_cache, kv_cache)
    returned, cache_after = together((returned, cache_after))
    layer_out = combine(residual, gates, spread, own_made, returned)
    return (layer_out, cache_after)


def passed_along(value, axis, steps):
    count = lax.axis_size(axis)
    initial, last = (max(0, -steps), min(count, count - steps))
    return lax.ppermute(value, axis, [(source, source + steps) for source in range(initial, last)])


def rms_norm(row_set, norm_gain):
    floats = row_set.astype(jnp.float32)
    factor = lax.rsqrt(jnp.mean(floats * floats, axis=-1, keepdims=True) + norm_eps)
    return (floats * factor * norm_gain).astype(jnp.bfloat16)


def rotate(vectors, angle_pos):
    halves = vectors.shape[-1] // 2
    inverse_freq = rope_base ** (-2.0 * jnp.arange(halves, dtype=jnp.float32) / vectors.shape[-1])
    angles = angle_pos[:, None, None] * inverse_freq[None, None, :]
    cosine = jnp.cos(angles)
    sine_part = jnp.sin(angles)
    first_half = vectors[..., :halves]
    second_half = vectors[..., halves:]
    return jnp.concatenate(
        [
            first_half * cosine - second_half * sine_part,
            second_half * cosine + first_half * sine_part,
        ],
        axis=-1,
    )


def expert_rows(row_set, gate_up, down_rows):
    gate_and_up = jnp.dot(row_set, gate_up, preferred_element_type=jnp.float32)
    inner_width = gate_and_up.shape[1] // 2
    hidden = (jax.nn.silu(gate_and_up[:, :inner_width]) * gate_and_up[:, inner_width:]).astype(
        jnp.bfloat16
    )
    return jnp.dot(hidden, down_rows, preferred_element_type=jnp.float32).astype(jnp.bfloat16)


def attend_rows(query_blk, keys_blk, vals_blk, visible, scale_qk):
    scores = (
        jnp.einsum("qkgd,skd->kgqs", query_blk, keys_blk, preferred_element_type=jnp.float32)
        * scale_qk
    )
    weights_f = jnp.where(visible[None, None], jnp.exp(scores), 0.0)
    prob_bf = (weights_f / jnp.sum(weights_f, axis=-1, keepdims=True)).astype(jnp.bfloat16)
    return jnp.einsum("kgqs,skd->qkgd", prob_bf, vals_blk, preferred_element_type=jnp.float32)


def shards(
    tokens,
    positions,
    attn_gain,
    w_query,
    w_keyval,
    w_out,
    moe_gain,
    router,
    w_gate_up,
    w_down,
    expert_ids,
    cache_slot,
    kv_cache,
):
    lane_count = lax.axis_size("hd")
    group_count = lax.axis_size("grp")
    tok_rows = tokens.shape[0]
    model_width = tokens.shape[1]
    block_len = positions.shape[0]
    seg_most = block_len // 2
    head_dim = w_keyval.shape[2] // 2
    kv_local = w_keyval.shape[1]
    q_local = w_query.shape[1] // head_dim
    per_kv = q_local // kv_local
    expert_cap = tok_rows // 4
    normed = rms_norm(tokens, attn_gain)
    flat_kv = w_keyval.reshape(model_width, kv_local * 2 * head_dim)
    section = lax.all_gather(normed, "hd", axis=0, tiled=True)
    projected = jnp.concatenate(
        [
            jnp.dot(section, w_query, preferred_element_type=jnp.float32),
            jnp.dot(section, flat_kv, preferred_element_type=jnp.float32),
        ],
        axis=1,
    )
    angle_pos = jnp.maximum(positions, 0).astype(jnp.float32)
    queries = rotate(
        projected[:, : q_local * head_dim].reshape(block_len, q_local, head_dim), angle_pos
    ).astype(jnp.bfloat16)
    key_val = projected[:, q_local * head_dim :].reshape(block_len, kv_local, 2 * head_dim)
    rotated = rotate(key_val[:, :, :head_dim], angle_pos).astype(jnp.bfloat16)
    stored = jnp.concatenate([rotated, key_val[:, :, head_dim:].astype(jnp.bfloat16)], axis=2)
    seam_rows = passed_along(stored[block_len - seg_most :], "grp", 1)
    window = jnp.concatenate([seam_rows, stored], axis=0)
    scale_qk = head_dim ** (-0.5)
    local_rows = jnp.arange(block_len, dtype=jnp.int32)
    lowest = local_rows - jnp.maximum(positions, 0)
    pieces_out = []
    for q_block in range(2):
        first_row = q_block * seg_most
        rows_here = first_row + jnp.arange(seg_most, dtype=jnp.int32)
        cols_here = first_row - seg_most + jnp.arange(2 * seg_most, dtype=jnp.int32)
        low_here = lowest[first_row : first_row + seg_most]
        visible = (cols_here[None, :] >= low_here[:, None]) & (
            cols_here[None, :] <= rows_here[:, None]
        )
        query_blk = queries[first_row : first_row + seg_most].reshape(
            seg_most, kv_local, per_kv, head_dim
        )
        keys_blk = window[first_row : first_row + 2 * seg_most, :, :head_dim]
        vals_blk = window[first_row : first_row + 2 * seg_most, :, head_dim:]
        mixed_rows = attend_rows(query_blk, keys_blk, vals_blk, visible, scale_qk)
        pieces_out.append(mixed_rows.reshape(seg_most, q_local * head_dim).astype(jnp.bfloat16))
    attended = jnp.concatenate(pieces_out, axis=0)
    slots_dev = kv_cache.shape[0]
    capc = 2 * block_len // group_count
    live_slot = cache_slot >= 0
    owners = jnp.where(live_slot, cache_slot // slots_dev, group_count)
    owner_hit = (owners[:, None] == jnp.arange(group_count, dtype=jnp.int32)[None, :]).astype(
        jnp.bfloat16
    )
    lower_tri = (local_rows[:, None] >= local_rows[None, :]).astype(jnp.bfloat16)
    running = jnp.dot(lower_tri, owner_hit, preferred_element_type=jnp.float32)
    owner_rank = jnp.sum(running * owner_hit.astype(jnp.float32), axis=1).astype(jnp.int32) - 1
    send_rows = jnp.where(live_slot, owners * capc + owner_rank, group_count * capc)
    outgoing_cache = (
        jnp.zeros((group_count * capc, kv_local, 2 * head_dim), jnp.bfloat16)
        .at[send_rows]
        .set(stored, mode="drop")
    )
    outgoing_slots = (
        jnp.full((group_count * capc,), -1, jnp.int32)
        .at[send_rows]
        .set(cache_slot % slots_dev, mode="drop")
    )
    arrived, arrived_slots = (
        lax.all_to_all(
            outgoing_cache.reshape(group_count, capc, kv_local, 2 * head_dim),
            "grp",
            split_axis=0,
            concat_axis=0,
            tiled=True,
        ),
        lax.all_to_all(
            outgoing_slots.reshape(group_count, capc),
            "grp",
            split_axis=0,
            concat_axis=0,
            tiled=True,
        ),
    )
    flat_slots = arrived_slots.reshape(group_count * capc)
    write_rows = jnp.where(flat_slots >= 0, flat_slots, slots_dev).astype(jnp.int32)
    cache_after = kv_cache.at[write_rows].set(
        arrived.reshape(group_count * capc, kv_local, 2 * head_dim), mode="drop"
    )
    by_token = lax.all_to_all(attended, "hd", split_axis=0, concat_axis=1, tiled=True)
    attn_proj = jnp.dot(
        by_token,
        lax.all_gather(w_out, "grp", axis=1, tiled=True),
        preferred_element_type=jnp.float32,
    )
    residual = (tokens.astype(jnp.float32) + attn_proj).astype(jnp.bfloat16)
    moe_in = rms_norm(residual, moe_gain)
    logits = jnp.dot(moe_in, router, preferred_element_type=jnp.float32)
    expert_range = jnp.arange(router.shape[1], dtype=jnp.int32)
    matches_all = expert_ids[:, :, None] == expert_range[None, None, :]
    chosen = jnp.sum(jnp.where(matches_all, logits[:, None, :], 0.0), axis=2)
    raised = jnp.exp(chosen)
    gates = raised / jnp.sum(raised, axis=1, keepdims=True)
    live_range = jnp.arange(lane_count, dtype=jnp.int32)
    matches = expert_ids[:, :, None] == live_range[None, None, :]
    member = jnp.any(matches, axis=1)
    weighting = jnp.sum(jnp.where(matches, gates[:, :, None], 0.0), axis=1)
    ranking = jnp.cumsum(member.astype(jnp.int32), axis=0) - 1
    target = jnp.where(member, live_range[None, :] * expert_cap + ranking, -1)
    slot_range = jnp.arange(lane_count * expert_cap, dtype=jnp.int32)
    slot_hits = target[None, :, :] == slot_range[:, None, None]
    placing = jnp.any(slot_hits, axis=2).astype(jnp.bfloat16)
    outgoing = (
        jnp.dot(placing, moe_in, preferred_element_type=jnp.float32)
        .astype(jnp.bfloat16)
        .reshape(lane_count, expert_cap, model_width)
    )
    gate_up_all, down_all = (
        lax.all_gather(w_gate_up, "grp", axis=1, tiled=True),
        lax.all_gather(w_down, "grp", axis=1, tiled=True),
    )
    gate_up_mat = gate_up_all[0]
    down_mat = down_all[0]
    landed = lax.all_to_all(outgoing, "hd", split_axis=0, concat_axis=0, tiled=True)
    results = expert_rows(landed.reshape(-1, model_width), gate_up_mat, down_mat).reshape(landed.shape)
    returned = lax.all_to_all(results, "hd", split_axis=0, concat_axis=0, tiled=True)
    flat_returned = returned.reshape(-1, model_width)
    fetched = flat_returned[jnp.maximum(target, 0)]
    used_weight = jnp.where(member, weighting, 0.0)
    moe_total = jnp.sum(used_weight[:, :, None] * fetched.astype(jnp.float32), axis=1)
    layer_out = (residual.astype(jnp.float32) + moe_total).astype(jnp.bfloat16)
    return (layer_out, cache_after)


def solution(mesh):
    two_lanes = mesh.shape["hd"] == 2 and mesh.shape["grp"] % 8 == 0
    return jax.shard_map(
        two_lane_shards if two_lanes else shards,
        mesh=mesh,
        in_specs=(
            P(("grp", "hd"), None),
            P("grp"),
            P(),
            P(None, "hd"),
            P(None, "hd", None),
            P(None, "grp"),
            P(),
            P(),
            P("hd", "grp", None),
            P("hd", "grp", None),
            P(("grp", "hd"), None),
            P("grp"),
            P("grp", "hd", None),
        ),
        out_specs=(P(("grp", "hd"), None), P("grp", "hd", None)),
        check_vma=False,
    )
```

```python
import functools

import jax
import jax.numpy as jnp
import numpy as np
from jax import lax
from jax.experimental import pallas as pl
from jax.experimental.pallas import tpu as pltpu
from jax.sharding import PartitionSpec as P

norm_eps = 1e-05
rope_base = 10000.0
bf16 = jnp.bfloat16
f32 = jnp.float32
LAST_DIMS = (((1,), (1,)), ((), ()))


def ring_cycle(groups):
    rows = groups // 4
    return [2 * r for r in range(rows)] + [2 * r + 1 for r in reversed(range(rows))]


def ring_pairs(groups):
    cycle = ring_cycle(groups)
    count = len(cycle)
    pairs = []
    for place, pair in enumerate(cycle):
        pairs.append((2 * pair, 2 * cycle[(place + 1) % count]))
        pairs.append((2 * pair + 1, 2 * cycle[(place - 1) % count] + 1))
    return pairs


def sibling_pairs(groups):
    return [(g, g ^ 1) for g in range(groups)]


def ring_sources(groups, me):
    count = groups // 2
    rows = count // 2
    side, pair = me % 2, me // 2
    row, col = pair // 2, pair % 2
    place = jnp.where(col == 0, row, count - 1 - row)

    def block(core, steps):
        there = (place + (2 * core - 1) * steps + count) % count
        other = jnp.where(there < rows, 2 * there, 2 * (count - 1 - there) + 1)
        return [2 * other + core, 2 * other + 1 - core]

    full = (count - 1) // 2
    listed = [me, me + 1 - 2 * side]
    for core in (side, 1 - side):
        for steps in range(1, full + 1):
            listed += block(core, steps)
    return listed + [block(side, count // 2)[0], block(1 - side, count // 2)[0]]


class Ring:
    def __init__(self, pair, groups):
        self.across = functools.partial(lax.ppermute, axis_name="grp", perm=ring_pairs(groups))
        self.beside = functools.partial(lax.ppermute, axis_name="grp", perm=sibling_pairs(groups))
        self.full = (groups // 2 - 1) // 2
        self.unit_rows = pair.shape[0] // 2
        self.mine = [pair]
        self.near = []

    def step(self):
        held = self.mine[-1]
        if len(self.mine) > self.full:
            held = held[: self.unit_rows]
        self.mine.append(self.across(held))

    def pin(self, *others):
        done = lax.optimization_barrier((self.mine[-1],) + others)
        self.mine[-1] = done[0]
        return done[1:] if len(others) > 1 else done[1]

    def share(self, upto=None):
        for index in range(1 + len(self.near), 1 + (upto or len(self.mine) - 1)):
            self.near.append(self.beside(self.mine[index]))

    def parts(self):
        full = self.full
        return self.mine[: full + 1] + self.near[:full] + [self.mine[full + 1], self.near[full]]


def place_parts(groups, parts, unit_rows, pieces):
    sources = ring_sources(groups, lax.axis_index("grp"))
    shard = 0
    for part in parts:
        for unit in range(part.shape[0] // unit_rows):
            for first, rows, target, lane in pieces:
                at = pl.multiple_of(sources[shard] * rows, rows)
                start = unit * unit_rows + first
                target[pl.ds(at, rows), lane : lane + part.shape[1]] = part[start : start + rows, :]
            shard += 1


VMEM = pl.BlockSpec(memory_space=pltpu.VMEM)
ANY = pl.BlockSpec(memory_space=pl.ANY)
HBM = pl.BlockSpec(memory_space=pltpu.HBM)
PARAMS = pltpu.CompilerParams(vmem_limit_bytes=16 << 20)


LITTLE = pl.CostEstimate(flops=1, bytes_accessed=1, transcendentals=0)


def takes(us):
    return pl.CostEstimate(
        flops=int(us * 1.15e9), bytes_accessed=int(us * 8e6), transcendentals=0
    )


def reads(nbytes):
    return pl.CostEstimate(flops=1, bytes_accessed=nbytes, transcendentals=0)


def normalized(floats, gain):
    factor = lax.rsqrt(jnp.mean(floats * floats, axis=-1, keepdims=True) + norm_eps)
    return (floats * factor * gain).astype(bf16)


def fetch(pairs, sems):
    copies = []
    for index, (source, target) in enumerate(pairs):
        copies.append(pltpu.make_async_copy(source, target, sems.at[index]))
        copies[-1].start()
    return copies


def pack_kernel(*refs):
    sources, (expert_pair, out_pair, sems) = refs[:6], refs[6:]
    width = expert_pair.shape[1]
    lane = lax.axis_index("hd")
    first = pl.multiple_of(lane * out_pair.shape[1], out_pair.shape[1])
    pairs = []
    row = 0
    for index in range(2):
        up, down, w_out = sources[3 * index : 3 * index + 3]
        count = w_out.shape[0]
        pairs.append(
            (w_out.at[:, pl.ds(first, out_pair.shape[1])], out_pair.at[pl.ds(index * count, count), :])
        )
        for source in (up, down):
            for at in range(0, source.shape[1], width):
                pairs.append(
                    (source.at[:, pl.ds(at, width)], expert_pair.at[pl.ds(row, source.shape[0]), :])
                )
                row += source.shape[0]
    for copy in fetch(pairs, sems):
        copy.wait()


def pack(own, beside):
    own = [pltpu.with_memory_space_constraint(part, pltpu.HBM) for part in own]
    up, down, w_out_t = own
    width = up.shape[1] // 2
    pieces = [up.shape[1] // width, down.shape[1] // width]
    unit_rows = pieces[0] * up.shape[0] + pieces[1] * down.shape[0]
    return pl.pallas_call(
        pack_kernel,
        out_shape=(
            jax.ShapeDtypeStruct((2 * unit_rows, width), bf16),
            jax.ShapeDtypeStruct((2 * w_out_t.shape[0], w_out_t.shape[1] // 2), bf16),
        ),
        in_specs=[ANY] * 6,
        out_specs=(ANY, ANY),
        scratch_shapes=[pltpu.SemaphoreType.DMA((2 + 2 * sum(pieces),))],
        compiler_params=PARAMS,
        cost_estimate=LITTLE,
        name="pack",
    )(*own, *beside)


def as_column(row, eye):
    return jnp.sum(jnp.where(eye, row, 0.0), axis=1, keepdims=True)


def named_experts(ids, experts):
    tokens = ids.shape[1]
    expert = lax.broadcasted_iota(jnp.int32, (experts, tokens), 0)
    hit = jnp.zeros((experts, tokens), f32)
    for index in range(ids.shape[0]):
        hit = jnp.where(ids[index : index + 1, :] == expert, 1.0, hit)
    return hit


def prepare_kernel(groups, slots_dev, *refs):
    sources, (cosine, sine, past, place, send, tags, gain) = refs[:4], refs[4:11]
    positions, slots, ids, flat_gain, sems = refs[11:]
    copies = fetch(list(zip(sources, (positions, slots, ids, flat_gain))), sems)
    for copy in copies:
        copy.wait()
    gain[...] = flat_gain[...].reshape(gain.shape)
    lane = lax.axis_index("hd")
    block = positions.shape[1]

    def iota(shape, dim):
        return lax.broadcasted_iota(jnp.int32, shape, dim)

    eye = iota((block, block), 0) == iota((block, block), 1)
    reach = as_column(jnp.maximum(positions[...], 0).astype(f32), eye)
    past[...] = jnp.broadcast_to(reach, past.shape)
    column = iota((8, 128), 1)
    exponent = (column % 32).astype(f32) * (-2.0 / 64)
    inverse_freq = jnp.exp(exponent * np.float32(np.log(rope_base)))[:1, :]
    angles = reach * inverse_freq
    cosine[...] = jnp.cos(angles)
    turned = jnp.sin(angles)
    sine[...] = jnp.where(iota(angles.shape, 1) % 64 < 32, -turned, turned)

    tokens = ids.shape[1]
    cap = place.shape[0] // 2
    hit = named_experts(ids, 8)
    upto = (iota((tokens, tokens), 0) <= iota((tokens, tokens), 1)).astype(f32)
    rank = jnp.dot(hit, upto, preferred_element_type=f32) - 1.0
    slot = iota((2 * cap, tokens), 0).astype(f32)
    placed = jnp.zeros((2 * cap, tokens), f32)
    for live in range(2):
        order = jnp.where(lane == live, 0, cap).astype(f32)
        member = hit[live : live + 1, :] > 0.0
        placed = jnp.where(member & (slot == rank[live : live + 1, :] + order), 1.0, placed)
    place[...] = placed.astype(bf16)

    where = slots[...]
    owner = jnp.where(where >= 0, where // slots_dev, -1)
    owner_hit = (iota((groups, block), 0) == owner).astype(f32)
    before = (iota((block, block), 0) <= iota((block, block), 1)).astype(f32)
    running = jnp.dot(owner_hit, before, preferred_element_type=f32)
    owner_rank = jnp.sum(owner_hit * running, axis=0, keepdims=True) - 1.0
    capc = send.shape[0] // groups
    row = jnp.where(owner >= 0, owner * capc + owner_rank.astype(jnp.int32), -1)
    send[...] = (iota(send.shape, 0) == row).astype(bf16)
    inside = jnp.where(where >= 0, where % slots_dev, 0)
    high = as_column((inside // 64 + 1).astype(f32), eye)
    low = as_column((inside % 64).astype(f32), eye)
    spot = iota(tags.shape, 1)
    tags[...] = jnp.where(spot == 0, high, jnp.where(spot == 1, low, 0.0)).astype(bf16)


def prepare(groups, slots_dev, positions, slots, ids, gain):
    block, tokens = positions.shape[0], ids.shape[0]
    model = gain.shape[0]
    cap = tokens // 4
    capc = 2 * block // groups
    shapes = [
        ((block, 128), f32),
        ((block, 128), f32),
        ((block, 128), f32),
        ((2 * cap, tokens), bf16),
        ((groups * capc, block), bf16),
        ((block, 128), bf16),
        ((1, model), f32),
    ]
    sources = (positions[None], slots[None], ids.T, gain)
    return pl.pallas_call(
        functools.partial(prepare_kernel, groups, slots_dev),
        out_shape=tuple(jax.ShapeDtypeStruct(shape, kind) for shape, kind in shapes),
        in_specs=[ANY] * 4,
        out_specs=(VMEM,) * len(shapes),
        scratch_shapes=[
            pltpu.VMEM((1, block), jnp.int32),
            pltpu.VMEM((1, block), jnp.int32),
            pltpu.VMEM(ids.shape[::-1], jnp.int32),
            pltpu.VMEM((model,), f32),
            pltpu.SemaphoreType.DMA((4,)),
        ],
        compiler_params=PARAMS,
        cost_estimate=LITTLE,
        name="prepare",
    )(*[pltpu.with_memory_space_constraint(source, pltpu.HBM) for source in sources])


def project_kernel(
    own, other, gain, cosine, sine, w_query, w_keyval, q_out, kv_out, seam_out, raw, rows, sems
):
    count = own.shape[0]
    lane = lax.axis_index("hd")
    mine = pl.multiple_of(lane * count, count)
    theirs = pl.multiple_of((1 - lane) * count, count)
    copies = fetch([(own, raw.at[0]), (other, raw.at[1])], sems)
    cos_q, sin_q = cosine[...], sine[...]
    column = lax.broadcasted_iota(jnp.int32, cos_q.shape, 1)
    lower = column % 64 < 32
    cos_kv = jnp.where(column < 64, cos_q, 1.0)
    sin_kv = jnp.where(column < 64, sin_q, 0.0)
    for index, first in ((0, mine), (1, theirs)):
        copies[index].wait()
        rows[pl.ds(first, count), :] = normalized(raw[index].astype(f32), gain[...])
    width = 256
    for weights, out, cos, sin in ((w_keyval, kv_out, cos_kv, sin_kv), (w_query, q_out, cos_q, sin_q)):
        for first in range(0, weights.shape[1], width):
            made = jnp.dot(rows[...], weights[:, first : first + width], preferred_element_type=f32)
            for part in range(0, width, 128):
                here = made[:, part : part + 128]
                turned = jnp.where(lower, pltpu.roll(here, 96, 1), pltpu.roll(here, 32, 1))
                done = (here * cos + turned * sin).astype(bf16)
                out[:, first + part : first + part + 128] = done
                if out is kv_out:
                    seam_out[:, first + part : first + part + 128] = done[count:, :]


def project(own, other, gain, cosine, sine, w_query, flat_kv):
    count, width = own.shape
    made = w_query.shape[1] + flat_kv.shape[1]
    return pl.pallas_call(
        project_kernel,
        out_shape=(
            jax.ShapeDtypeStruct((2 * count, w_query.shape[1]), bf16),
            jax.ShapeDtypeStruct((2 * count, flat_kv.shape[1]), bf16),
            jax.ShapeDtypeStruct((count, flat_kv.shape[1]), bf16),
        ),
        in_specs=[ANY] * 2 + [VMEM] * 5,
        out_specs=(VMEM, VMEM, VMEM),
        scratch_shapes=[
            pltpu.VMEM((2, count, width), bf16),
            pltpu.VMEM((2 * count, width), bf16),
            pltpu.SemaphoreType.DMA((2,)),
        ],
        compiler_params=PARAMS,
        cost_estimate=takes(8),
        name="project",
    )(own, other, gain, cosine, sine, w_query, flat_kv)


def attend_kernel(q, kv, seam, past, mixed, window, sem):
    count = seam.shape[0]
    copy = pltpu.make_async_copy(seam, window.at[pl.ds(0, count), :], sem)
    copy.start()
    window[count:, :] = kv[...]
    head = 64
    kv_heads = kv.shape[1] // (2 * head)
    per_kv = q.shape[1] // head // kv_heads
    shape = (count, 2 * count)
    row = lax.broadcasted_iota(jnp.int32, shape, 0) + count
    col = lax.broadcasted_iota(jnp.int32, shape, 1)
    for half in (1, 0):
        first = half * count
        if half == 0:
            copy.wait()
        reach = past[first : first + count, :1].astype(jnp.int32)
        visible = (col <= row) & (col >= row - reach)
        for kv_head in range(kv_heads):
            lanes = 2 * head * kv_head
            keys = window[first : first + 2 * count, lanes : lanes + head]
            values = window[first : first + 2 * count, lanes + head : lanes + 2 * head]
            for index in range(per_kv):
                at = (kv_head * per_kv + index) * head
                query = q[first : first + count, at : at + head]
                scores = lax.dot_general(query, keys, LAST_DIMS, preferred_element_type=f32)
                raised = jnp.where(visible, jnp.exp(scores * head ** (-0.5)), 0.0)
                probs = (raised / jnp.sum(raised, axis=-1, keepdims=True)).astype(bf16)
                made = jnp.dot(probs, values, preferred_element_type=f32)
                mixed[first : first + count, at : at + head] = made.astype(bf16)


def attend(q, kv, seam, past):
    count = seam.shape[0]
    return pl.pallas_call(
        attend_kernel,
        out_shape=jax.ShapeDtypeStruct(q.shape, bf16),
        in_specs=[VMEM, VMEM, ANY, VMEM],
        out_specs=VMEM,
        scratch_shapes=[
            pltpu.VMEM((3 * count, kv.shape[1]), bf16),
            pltpu.SemaphoreType.DMA,
        ],
        compiler_params=PARAMS,
        cost_estimate=takes(4),
        name="attend",
    )(q, kv, seam, past)


def outward_rows(flip, groups, unit_rows, mixed, parts, w_out):
    place_parts(groups, parts, unit_rows, [(0, unit_rows, w_out, 0)])
    count = mixed.shape[0] // 2
    lane = lax.axis_index("hd")
    first = pl.multiple_of(((1 - lane) if flip else lane) * count, count)
    return lax.dot_general(
        mixed[pl.ds(first, count), :], w_out[...], LAST_DIMS, preferred_element_type=f32
    )


def send_kernel(groups, unit_rows, n_parts, mixed, *refs):
    parts, (out, w_out) = refs[:n_parts], refs[n_parts:]
    out[...] = outward_rows(True, groups, unit_rows, mixed, parts, w_out).astype(bf16)


def keep_kernel(groups, unit_rows, n_parts, mixed, tokens, flat_gain, *refs):
    parts, (out, gain, w_out) = refs[:n_parts], refs[n_parts:]
    gain[...] = flat_gain[...].reshape(gain.shape)
    made = outward_rows(False, groups, unit_rows, mixed, parts, w_out)
    out[...] = tokens[...].astype(f32) + made


def outward_send(groups, mixed, parts, unit_rows):
    count = mixed.shape[0] // 2
    width, depth = groups * unit_rows, parts[0].shape[1]
    return pl.pallas_call(
        functools.partial(send_kernel, groups, unit_rows, len(parts)),
        out_shape=jax.ShapeDtypeStruct((count, width), bf16),
        in_specs=[VMEM] * (1 + len(parts)),
        out_specs=VMEM,
        scratch_shapes=[pltpu.VMEM((width, depth), bf16)],
        compiler_params=PARAMS,
        cost_estimate=reads(2 * width * depth),
        name="outward_send",
    )(mixed, *parts)


def outward_keep(groups, mixed, tokens, gain, parts, unit_rows):
    width, depth = groups * unit_rows, parts[0].shape[1]
    return pl.pallas_call(
        functools.partial(keep_kernel, groups, unit_rows, len(parts)),
        out_shape=(
            jax.ShapeDtypeStruct(tokens.shape, f32),
            jax.ShapeDtypeStruct((1, width), f32),
        ),
        in_specs=[VMEM] * (3 + len(parts)),
        out_specs=(VMEM, VMEM),
        scratch_shapes=[pltpu.VMEM((width, depth), bf16)],
        compiler_params=PARAMS,
        cost_estimate=reads(2 * width * depth),
        name="outward_keep",
    )(mixed, tokens, gain, *parts)


def route_kernel(mine, arrived, gain, place, residual, moe_in, sent):
    added = (mine[...] + arrived[...].astype(f32)).astype(bf16)
    residual[...] = added
    moe_in[...] = normalized(added.astype(f32), gain[...])
    cap = sent.shape[0]
    rows = jnp.dot(place[cap:, :], moe_in[...], preferred_element_type=f32)
    sent[...] = rows.astype(bf16)


def route(mine, arrived, gain, place):
    cap = place.shape[0] // 2
    return pl.pallas_call(
        route_kernel,
        out_shape=(
            jax.ShapeDtypeStruct(mine.shape, bf16),
            jax.ShapeDtypeStruct(mine.shape, bf16),
            jax.ShapeDtypeStruct((cap, mine.shape[1]), bf16),
        ),
        in_specs=[VMEM] * 4,
        out_specs=(VMEM,) * 3,
        compiler_params=PARAMS,
        cost_estimate=takes(2),
        name="route",
    )(mine, arrived, gain, place)


def gate_kernel(moe_in, router, ids, place, gates, own, spread):
    cap = own.shape[0]
    own[...] = jnp.dot(place[:cap, :], moe_in[...], preferred_element_type=f32).astype(bf16)
    hit = named_experts(ids, router.shape[0])
    tokens = ids.shape[1]
    row = lax.broadcasted_iota(jnp.int32, (tokens, tokens), 0)
    eye = (row == lax.broadcasted_iota(jnp.int32, (tokens, tokens), 1)).astype(f32)
    named = lax.dot_general(eye, hit, LAST_DIMS, preferred_element_type=f32)
    spread[...] = lax.dot_general(
        eye.astype(bf16), place[...], LAST_DIMS, preferred_element_type=f32
    ).astype(bf16)
    logits = lax.dot_general(moe_in[...], router[...], LAST_DIMS, preferred_element_type=f32)
    raised = jnp.where(named > 0, jnp.exp(logits), 0.0)
    gates[...] = raised / jnp.sum(raised, axis=-1, keepdims=True)


def gate(moe_in, router_t, ids_t, place):
    cap = place.shape[0] // 2
    return pl.pallas_call(
        gate_kernel,
        out_shape=(
            jax.ShapeDtypeStruct((moe_in.shape[0], router_t.shape[0]), f32),
            jax.ShapeDtypeStruct((cap, moe_in.shape[1]), bf16),
            jax.ShapeDtypeStruct(place.shape[::-1], bf16),
        ),
        in_specs=[VMEM] * 4,
        out_specs=(VMEM,) * 3,
        compiler_params=PARAMS,
        cost_estimate=LITTLE,
        name="gate",
    )(moe_in, router_t, ids_t, place)


def expert_kernel(groups, up_rows, down_rows, n_parts, own, other, *refs):
    parts = refs[:n_parts]
    own_out, other_out, rows, gate_up, down = refs[n_parts:]
    width = parts[0].shape[1]
    count = own.shape[0]
    rows[:count, :] = own[...]
    rows[count:, :] = other[...]
    pieces = [(i * up_rows, up_rows, gate_up, i * width) for i in range(2)]
    pieces += [
        (2 * up_rows + i * down_rows, down_rows, down, i * width) for i in range(down.shape[1] // width)
    ]
    unit_rows = pieces[-1][0] + down_rows
    place_parts(groups, parts, unit_rows, pieces)
    both = jnp.dot(rows[...], gate_up[...], preferred_element_type=f32)
    gate, up = both[:, :width], both[:, width:]
    hidden = (gate / (1.0 + jnp.exp(-gate)) * up).astype(bf16)
    made = jnp.dot(hidden, down[...], preferred_element_type=f32).astype(bf16)
    own_out[...] = made[:count, :]
    other_out[...] = made[count:, :]


def expert(groups, own, other, parts, up_rows, down_rows):
    count, model = own.shape
    width = parts[0].shape[1]
    return pl.pallas_call(
        functools.partial(expert_kernel, groups, up_rows, down_rows, len(parts)),
        out_shape=(jax.ShapeDtypeStruct(own.shape, bf16),) * 2,
        in_specs=[VMEM] * (2 + len(parts)),
        out_specs=(VMEM, VMEM),
        scratch_shapes=[
            pltpu.VMEM((2 * count, model), bf16),
            pltpu.VMEM((groups * up_rows, 2 * width), bf16),
            pltpu.VMEM((groups * down_rows, model), bf16),
        ],
        compiler_params=PARAMS,
        cost_estimate=reads(2 * groups * 2 * (up_rows * 2 * width + down_rows * model)),
        name="expert",
    )(own, other, *parts)


def combine_kernel(residual, gates, spread, own, returned, out):
    lane = lax.axis_index("hd")
    count = own.shape[0]
    column = lax.broadcasted_iota(jnp.int32, gates.shape, 1)
    total = jnp.zeros(residual.shape, f32)
    for index, made in ((0, own), (1, returned)):
        live = lane if index == 0 else 1 - lane
        weight = jnp.sum(jnp.where(column == live, gates[...], 0.0), axis=-1, keepdims=True)
        picked = jnp.dot(
            spread[:, index * count : (index + 1) * count], made[...], preferred_element_type=f32
        )
        total += weight * picked
    out[...] = (residual[...].astype(f32) + total).astype(bf16)


def combine(residual, gates, spread, own, returned):
    return pl.pallas_call(
        combine_kernel,
        out_shape=jax.ShapeDtypeStruct(residual.shape, bf16),
        in_specs=[VMEM] * 5,
        out_specs=VMEM,
        compiler_params=PARAMS,
        cost_estimate=reads(6 * residual.shape[0] * residual.shape[1]),
        name="combine",
    )(residual, gates, spread, own, returned)


def bundle_kernel(send, kv, tags, out):
    groups, rows, _ = out.shape
    heads = kv.shape[1] // 128
    capc = send.shape[0] // groups
    packed = jnp.dot(send[...], kv[...], preferred_element_type=f32).astype(bf16)
    tagged = jnp.dot(send[...], tags[...], preferred_element_type=f32)
    one = (lax.broadcasted_iota(jnp.int32, (16, 128), 0) == lax.broadcasted_iota(jnp.int32, (16, 128), 1))
    for owner in range(groups):
        mine = slice(owner * capc, (owner + 1) * capc)
        for head in range(heads):
            out[owner, head * capc : (head + 1) * capc, :] = packed[mine, head * 128 : (head + 1) * 128]
        wide = jnp.concatenate([tagged[mine, :], jnp.zeros((128 - capc, 128), f32)], axis=0)
        out[owner, heads * capc :, :] = lax.dot_general(
            one.astype(f32), wide, LAST_DIMS, preferred_element_type=f32
        ).astype(bf16)


def bundle(groups, send, kv, tags):
    rows = send.shape[0] // groups * (kv.shape[1] // 128) + 16
    return pl.pallas_call(
        bundle_kernel,
        out_shape=jax.ShapeDtypeStruct((groups, rows, 128), bf16),
        in_specs=[VMEM] * 3,
        out_specs=VMEM,
        compiler_params=PARAMS,
        cost_estimate=LITTLE,
        name="bundle",
    )(send, kv, tags)


def write_kernel(heads, arrived, cache, out, rows, wide, known):
    groups, size, _ = arrived.shape
    slots = cache.shape[0] // heads
    capc = (size - 16) // heads
    high, low = [], []
    for source in range(groups):
        for head in range(heads):
            rows[source * capc : (source + 1) * capc, head * 128 : (head + 1) * 128] = arrived[
                source, head * capc : (head + 1) * capc, :
            ]
        numbers = arrived[source, heads * capc :, :].astype(f32)
        high.append(numbers[0:1, :capc])
        low.append(numbers[1:2, :capc])
    slot = jnp.concatenate(high, axis=1) * 64.0 + jnp.concatenate(low, axis=1) - 64.0
    row = lax.broadcasted_iota(jnp.int32, (slots, slot.shape[1]), 0).astype(f32)
    hit = (row == slot).astype(bf16)
    made = jnp.dot(hit, rows[...], preferred_element_type=f32)
    found = jnp.dot(hit, jnp.ones((slot.shape[1], 128), bf16), preferred_element_type=f32)
    for head in range(heads):
        wide[pl.ds(head, slots, heads), :] = made[:, head * 128 : (head + 1) * 128]
        known[pl.ds(head, slots, heads), :] = found
    old = cache[...].astype(f32)
    out[...] = jnp.where(known[...] > 0.0, wide[...], old).astype(bf16)


def write(arrived, cache):
    slots, heads, lanes = cache.shape
    capc = (arrived.shape[1] - 16) // heads
    flat = (slots * heads, lanes)
    written = pl.pallas_call(
        functools.partial(write_kernel, heads),
        out_shape=jax.ShapeDtypeStruct(flat, bf16),
        in_specs=[VMEM] * 2,
        out_specs=VMEM,
        scratch_shapes=[
            pltpu.VMEM((arrived.shape[0] * capc, heads * lanes), bf16),
            pltpu.VMEM(flat, f32),
            pltpu.VMEM(flat, f32),
        ],
        compiler_params=PARAMS,
        cost_estimate=reads(1 << 21),
        name="write",
    )(arrived, cache.reshape(flat))
    return written.reshape(cache.shape)


def two_lane_shards(
    tokens,
    positions,
    attn_gain,
    w_query,
    w_keyval,
    w_out,
    moe_gain,
    router,
    w_gate_up,
    w_down,
    expert_ids,
    cache_slot,
    kv_cache,
):
    groups = lax.axis_size("grp")
    tok_rows, model = tokens.shape
    block = positions.shape[0]
    kv_local, head2 = w_keyval.shape[1:]
    kv_width = kv_local * head2
    slots_dev = kv_cache.shape[0]
    swap = functools.partial(lax.ppermute, axis_name="hd", perm=[(0, 1), (1, 0)])

    together = lax.optimization_barrier

    other_tokens = swap(tokens)
    own = (w_gate_up[0], w_down[0], w_out.T)
    up_rows, down_rows = own[0].shape[0], own[1].shape[0]
    beside = [lax.ppermute(part, "grp", sibling_pairs(groups)) for part in own]
    expert_pair, out_pair = pack(own, beside)
    out_ring = Ring(out_pair, groups)
    out_ring.step()
    expert_ring = Ring(expert_pair, groups)
    expert_ring.step()
    w_keyval, positions = together((w_keyval, positions, out_pair))[:2]
    flat_kv = w_keyval.reshape(model, kv_width)
    cosine, sine, past, place, send, tags, gain = prepare(
        groups, slots_dev, positions, cache_slot, expert_ids, attn_gain
    )
    other_tokens, cosine, flat_kv = out_ring.pin(other_tokens, cosine, flat_kv)
    out_ring.step()

    q, kv, tail = project(tokens, other_tokens, gain, cosine, sine, w_query, flat_kv)
    seam = lax.ppermute(tail, "grp", [(g, g + 1) for g in range(groups - 1)])
    seam, q = out_ring.pin(seam, q)
    out_ring.step()
    q = expert_ring.pin(q)
    expert_ring.step()
    out_ring.share(2)
    mixed = attend(q, kv, seam, past)
    mixed, out_ring.near = together((mixed, out_ring.near))
    mixed = out_ring.pin(mixed)
    out_ring.step()
    out_ring.share(3)
    mixed, out_ring.near = together((mixed, out_ring.near))
    mixed = out_ring.pin(mixed)
    out_ring.share()
    sent = outward_send(groups, mixed, out_ring.parts(), out_ring.unit_rows)
    arrived = swap(sent)
    mixed = together((mixed, sent))[0]
    mine, late_gain = outward_keep(
        groups, mixed, tokens, moe_gain, out_ring.parts(), out_ring.unit_rows
    )
    kv, mine = together((kv, mine))
    outgoing = bundle(groups, send, kv, tags)
    arrived_cache = lax.all_to_all(outgoing, "grp", split_axis=0, concat_axis=0, tiled=True)
    mine = expert_ring.pin(mine)
    expert_ring.share()
    expert_ring.step()

    residual, moe_in, sent_rows = route(mine, arrived, late_gain, place)
    landed = swap(sent_rows)
    moe_in = expert_ring.pin(moe_in)
    expert_ring.share()
    expert_ring.step()
    gates, own_rows, spread = gate(moe_in, router.T, expert_ids.T, place)
    landed, own_rows = expert_ring.pin(landed, own_rows)
    expert_ring.share()
    own_made, back = expert(
        groups, own_rows, landed, expert_ring.parts(), up_rows, down_rows
    )
    returned = swap(back)
    arrived_cache = together((arrived_cache, back))[0]
    cache_after = write(arrived_cache, kv_cache)
    returned, cache_after = together((returned, cache_after))
    layer_out = combine(residual, gates, spread, own_made, returned)
    return (layer_out, cache_after)


def passed_along(value, axis, steps):
    count = lax.axis_size(axis)
    initial, last = (max(0, -steps), min(count, count - steps))
    return lax.ppermute(value, axis, [(source, source + steps) for source in range(initial, last)])


def rms_norm(row_set, norm_gain):
    floats = row_set.astype(jnp.float32)
    factor = lax.rsqrt(jnp.mean(floats * floats, axis=-1, keepdims=True) + norm_eps)
    return (floats * factor * norm_gain).astype(jnp.bfloat16)


def rotate(vectors, angle_pos):
    halves = vectors.shape[-1] // 2
    inverse_freq = rope_base ** (-2.0 * jnp.arange(halves, dtype=jnp.float32) / vectors.shape[-1])
    angles = angle_pos[:, None, None] * inverse_freq[None, None, :]
    cosine = jnp.cos(angles)
    sine_part = jnp.sin(angles)
    first_half = vectors[..., :halves]
    second_half = vectors[..., halves:]
    return jnp.concatenate(
        [
            first_half * cosine - second_half * sine_part,
            second_half * cosine + first_half * sine_part,
        ],
        axis=-1,
    )


def expert_rows(row_set, gate_up, down_rows):
    gate_and_up = jnp.dot(row_set, gate_up, preferred_element_type=jnp.float32)
    inner_width = gate_and_up.shape[1] // 2
    hidden = (jax.nn.silu(gate_and_up[:, :inner_width]) * gate_and_up[:, inner_width:]).astype(
        jnp.bfloat16
    )
    return jnp.dot(hidden, down_rows, preferred_element_type=jnp.float32).astype(jnp.bfloat16)


def attend_rows(query_blk, keys_blk, vals_blk, visible, scale_qk):
    scores = (
        jnp.einsum("qkgd,skd->kgqs", query_blk, keys_blk, preferred_element_type=jnp.float32)
        * scale_qk
    )
    weights_f = jnp.where(visible[None, None], jnp.exp(scores), 0.0)
    prob_bf = (weights_f / jnp.sum(weights_f, axis=-1, keepdims=True)).astype(jnp.bfloat16)
    return jnp.einsum("kgqs,skd->qkgd", prob_bf, vals_blk, preferred_element_type=jnp.float32)


def shards(
    tokens,
    positions,
    attn_gain,
    w_query,
    w_keyval,
    w_out,
    moe_gain,
    router,
    w_gate_up,
    w_down,
    expert_ids,
    cache_slot,
    kv_cache,
):
    lane_count = lax.axis_size("hd")
    group_count = lax.axis_size("grp")
    tok_rows = tokens.shape[0]
    model_width = tokens.shape[1]
    block_len = positions.shape[0]
    seg_most = block_len // 2
    head_dim = w_keyval.shape[2] // 2
    kv_local = w_keyval.shape[1]
    q_local = w_query.shape[1] // head_dim
    per_kv = q_local // kv_local
    expert_cap = tok_rows // 4
    normed = rms_norm(tokens, attn_gain)
    flat_kv = w_keyval.reshape(model_width, kv_local * 2 * head_dim)
    section = lax.all_gather(normed, "hd", axis=0, tiled=True)
    projected = jnp.concatenate(
        [
            jnp.dot(section, w_query, preferred_element_type=jnp.float32),
            jnp.dot(section, flat_kv, preferred_element_type=jnp.float32),
        ],
        axis=1,
    )
    angle_pos = jnp.maximum(positions, 0).astype(jnp.float32)
    queries = rotate(
        projected[:, : q_local * head_dim].reshape(block_len, q_local, head_dim), angle_pos
    ).astype(jnp.bfloat16)
    key_val = projected[:, q_local * head_dim :].reshape(block_len, kv_local, 2 * head_dim)
    rotated = rotate(key_val[:, :, :head_dim], angle_pos).astype(jnp.bfloat16)
    stored = jnp.concatenate([rotated, key_val[:, :, head_dim:].astype(jnp.bfloat16)], axis=2)
    seam_rows = passed_along(stored[block_len - seg_most :], "grp", 1)
    window = jnp.concatenate([seam_rows, stored], axis=0)
    scale_qk = head_dim ** (-0.5)
    local_rows = jnp.arange(block_len, dtype=jnp.int32)
    lowest = local_rows - jnp.maximum(positions, 0)
    pieces_out = []
    for q_block in range(2):
        first_row = q_block * seg_most
        rows_here = first_row + jnp.arange(seg_most, dtype=jnp.int32)
        cols_here = first_row - seg_most + jnp.arange(2 * seg_most, dtype=jnp.int32)
        low_here = lowest[first_row : first_row + seg_most]
        visible = (cols_here[None, :] >= low_here[:, None]) & (
            cols_here[None, :] <= rows_here[:, None]
        )
        query_blk = queries[first_row : first_row + seg_most].reshape(
            seg_most, kv_local, per_kv, head_dim
        )
        keys_blk = window[first_row : first_row + 2 * seg_most, :, :head_dim]
        vals_blk = window[first_row : first_row + 2 * seg_most, :, head_dim:]
        mixed_rows = attend_rows(query_blk, keys_blk, vals_blk, visible, scale_qk)
        pieces_out.append(mixed_rows.reshape(seg_most, q_local * head_dim).astype(jnp.bfloat16))
    attended = jnp.concatenate(pieces_out, axis=0)
    slots_dev = kv_cache.shape[0]
    capc = 2 * block_len // group_count
    live_slot = cache_slot >= 0
    owners = jnp.where(live_slot, cache_slot // slots_dev, group_count)
    owner_hit = (owners[:, None] == jnp.arange(group_count, dtype=jnp.int32)[None, :]).astype(
        jnp.bfloat16
    )
    lower_tri = (local_rows[:, None] >= local_rows[None, :]).astype(jnp.bfloat16)
    running = jnp.dot(lower_tri, owner_hit, preferred_element_type=jnp.float32)
    owner_rank = jnp.sum(running * owner_hit.astype(jnp.float32), axis=1).astype(jnp.int32) - 1
    send_rows = jnp.where(live_slot, owners * capc + owner_rank, group_count * capc)
    outgoing_cache = (
        jnp.zeros((group_count * capc, kv_local, 2 * head_dim), jnp.bfloat16)
        .at[send_rows]
        .set(stored, mode="drop")
    )
    outgoing_slots = (
        jnp.full((group_count * capc,), -1, jnp.int32)
        .at[send_rows]
        .set(cache_slot % slots_dev, mode="drop")
    )
    arrived, arrived_slots = (
        lax.all_to_all(
            outgoing_cache.reshape(group_count, capc, kv_local, 2 * head_dim),
            "grp",
            split_axis=0,
            concat_axis=0,
            tiled=True,
        ),
        lax.all_to_all(
            outgoing_slots.reshape(group_count, capc),
            "grp",
            split_axis=0,
            concat_axis=0,
            tiled=True,
        ),
    )
    flat_slots = arrived_slots.reshape(group_count * capc)
    write_rows = jnp.where(flat_slots >= 0, flat_slots, slots_dev).astype(jnp.int32)
    cache_after = kv_cache.at[write_rows].set(
        arrived.reshape(group_count * capc, kv_local, 2 * head_dim), mode="drop"
    )
    by_token = lax.all_to_all(attended, "hd", split_axis=0, concat_axis=1, tiled=True)
    attn_proj = jnp.dot(
        by_token,
        lax.all_gather(w_out, "grp", axis=1, tiled=True),
        preferred_element_type=jnp.float32,
    )
    residual = (tokens.astype(jnp.float32) + attn_proj).astype(jnp.bfloat16)
    moe_in = rms_norm(residual, moe_gain)
    logits = jnp.dot(moe_in, router, preferred_element_type=jnp.float32)
    expert_range = jnp.arange(router.shape[1], dtype=jnp.int32)
    matches_all = expert_ids[:, :, None] == expert_range[None, None, :]
    chosen = jnp.sum(jnp.where(matches_all, logits[:, None, :], 0.0), axis=2)
    raised = jnp.exp(chosen)
    gates = raised / jnp.sum(raised, axis=1, keepdims=True)
    live_range = jnp.arange(lane_count, dtype=jnp.int32)
    matches = expert_ids[:, :, None] == live_range[None, None, :]
    member = jnp.any(matches, axis=1)
    weighting = jnp.sum(jnp.where(matches, gates[:, :, None], 0.0), axis=1)
    ranking = jnp.cumsum(member.astype(jnp.int32), axis=0) - 1
    target = jnp.where(member, live_range[None, :] * expert_cap + ranking, -1)
    slot_range = jnp.arange(lane_count * expert_cap, dtype=jnp.int32)
    slot_hits = target[None, :, :] == slot_range[:, None, None]
    placing = jnp.any(slot_hits, axis=2).astype(jnp.bfloat16)
    outgoing = (
        jnp.dot(placing, moe_in, preferred_element_type=jnp.float32)
        .astype(jnp.bfloat16)
        .reshape(lane_count, expert_cap, model_width)
    )
    gate_up_all, down_all = (
        lax.all_gather(w_gate_up, "grp", axis=1, tiled=True),
        lax.all_gather(w_down, "grp", axis=1, tiled=True),
    )
    gate_up_mat = gate_up_all[0]
    down_mat = down_all[0]
    landed = lax.all_to_all(outgoing, "hd", split_axis=0, concat_axis=0, tiled=True)
    results = expert_rows(landed.reshape(-1, model_width), gate_up_mat, down_mat).reshape(landed.shape)
    returned = lax.all_to_all(results, "hd", split_axis=0, concat_axis=0, tiled=True)
    flat_returned = returned.reshape(-1, model_width)
    fetched = flat_returned[jnp.maximum(target, 0)]
    used_weight = jnp.where(member, weighting, 0.0)
    moe_total = jnp.sum(used_weight[:, :, None] * fetched.astype(jnp.float32), axis=1)
    layer_out = (residual.astype(jnp.float32) + moe_total).astype(jnp.bfloat16)
    return (layer_out, cache_after)


def solution(mesh):
    two_lanes = mesh.shape["hd"] == 2 and mesh.shape["grp"] % 8 == 0
    return jax.shard_map(
        two_lane_shards if two_lanes else shards,
        mesh=mesh,
        in_specs=(
            P(("grp", "hd"), None),
            P("grp"),
            P(),
            P(None, "hd"),
            P(None, "hd", None),
            P(None, "grp"),
            P(),
            P(),
            P("hd", "grp", None),
            P("hd", "grp", None),
            P(("grp", "hd"), None),
            P("grp"),
            P("grp", "hd", None),
        ),
        out_specs=(P(("grp", "hd"), None), P("grp", "hd", None)),
        check_vma=False,
    )
```

```python
import functools

import jax
import jax.numpy as jnp
import numpy as np
from jax import lax
from jax.experimental import pallas as pl
from jax.experimental.pallas import tpu as pltpu
from jax.sharding import PartitionSpec as P

norm_eps = 1e-05
rope_base = 10000.0
bf16 = jnp.bfloat16
f32 = jnp.float32
LAST_DIMS = (((1,), (1,)), ((), ()))


def ring_cycle(groups):
    rows = groups // 4
    return [2 * r for r in range(rows)] + [2 * r + 1 for r in reversed(range(rows))]


def ring_pairs(groups):
    cycle = ring_cycle(groups)
    count = len(cycle)
    pairs = []
    for place, pair in enumerate(cycle):
        pairs.append((2 * pair, 2 * cycle[(place + 1) % count]))
        pairs.append((2 * pair + 1, 2 * cycle[(place - 1) % count] + 1))
    return pairs


def sibling_pairs(groups):
    return [(g, g ^ 1) for g in range(groups)]


def ring_sources(groups, me):
    count = groups // 2
    rows = count // 2
    side, pair = me % 2, me // 2
    row, col = pair // 2, pair % 2
    place = jnp.where(col == 0, row, count - 1 - row)

    def block(core, steps):
        there = (place + (2 * core - 1) * steps + count) % count
        other = jnp.where(there < rows, 2 * there, 2 * (count - 1 - there) + 1)
        return [2 * other + core, 2 * other + 1 - core]

    full = (count - 1) // 2
    listed = [me, me + 1 - 2 * side]
    for core in (side, 1 - side):
        for steps in range(1, full + 1):
            listed += block(core, steps)
    return listed + [block(side, count // 2)[0], block(1 - side, count // 2)[0]]


class Ring:
    def __init__(self, pair, groups):
        self.across = functools.partial(lax.ppermute, axis_name="grp", perm=ring_pairs(groups))
        self.beside = functools.partial(lax.ppermute, axis_name="grp", perm=sibling_pairs(groups))
        self.full = (groups // 2 - 1) // 2
        self.unit_rows = pair.shape[0] // 2
        self.mine = [pair]
        self.near = []

    def step(self):
        held = self.mine[-1]
        if len(self.mine) > self.full:
            held = held[: self.unit_rows]
        self.mine.append(self.across(held))

    def pin(self, *others):
        done = lax.optimization_barrier((self.mine[-1],) + others)
        self.mine[-1] = done[0]
        return done[1:] if len(others) > 1 else done[1]

    def share(self, upto=None):
        for index in range(1 + len(self.near), 1 + (upto or len(self.mine) - 1)):
            self.near.append(self.beside(self.mine[index]))

    def parts(self):
        full = self.full
        return self.mine[: full + 1] + self.near[:full] + [self.mine[full + 1], self.near[full]]


def place_parts(groups, parts, unit_rows, pieces):
    sources = ring_sources(groups, lax.axis_index("grp"))
    shard = 0
    for part in parts:
        for unit in range(part.shape[0] // unit_rows):
            for first, rows, target, lane in pieces:
                at = pl.multiple_of(sources[shard] * rows, rows)
                start = unit * unit_rows + first
                target[pl.ds(at, rows), lane : lane + part.shape[1]] = part[start : start + rows, :]
            shard += 1


VMEM = pl.BlockSpec(memory_space=pltpu.VMEM)
ANY = pl.BlockSpec(memory_space=pl.ANY)
HBM = pl.BlockSpec(memory_space=pltpu.HBM)
PARAMS = pltpu.CompilerParams(vmem_limit_bytes=16 << 20)


LITTLE = pl.CostEstimate(flops=1, bytes_accessed=1, transcendentals=0)


def takes(us):
    return pl.CostEstimate(
        flops=int(us * 1.15e9), bytes_accessed=int(us * 8e6), transcendentals=0
    )


def reads(nbytes):
    return pl.CostEstimate(flops=1, bytes_accessed=nbytes, transcendentals=0)


def normalized(floats, gain):
    factor = lax.rsqrt(jnp.mean(floats * floats, axis=-1, keepdims=True) + norm_eps)
    return (floats * factor * gain).astype(bf16)


def fetch(pairs, sems):
    copies = []
    for index, (source, target) in enumerate(pairs):
        copies.append(pltpu.make_async_copy(source, target, sems.at[index]))
        copies[-1].start()
    return copies


def pack_kernel(*refs):
    sources, (expert_pair, out_pair, sems) = refs[:6], refs[6:]
    width = expert_pair.shape[1]
    lane = lax.axis_index("hd")
    first = pl.multiple_of(lane * out_pair.shape[1], out_pair.shape[1])
    pairs = []
    row = 0
    for index in range(2):
        up, down, w_out = sources[3 * index : 3 * index + 3]
        count = w_out.shape[0]
        pairs.append(
            (w_out.at[:, pl.ds(first, out_pair.shape[1])], out_pair.at[pl.ds(index * count, count), :])
        )
        for source in (up, down):
            for at in range(0, source.shape[1], width):
                pairs.append(
                    (source.at[:, pl.ds(at, width)], expert_pair.at[pl.ds(row, source.shape[0]), :])
                )
                row += source.shape[0]
    for copy in fetch(pairs, sems):
        copy.wait()


def pack(own, beside):
    own = [pltpu.with_memory_space_constraint(part, pltpu.HBM) for part in own]
    up, down, w_out_t = own
    width = up.shape[1] // 2
    pieces = [up.shape[1] // width, down.shape[1] // width]
    unit_rows = pieces[0] * up.shape[0] + pieces[1] * down.shape[0]
    return pl.pallas_call(
        pack_kernel,
        out_shape=(
            jax.ShapeDtypeStruct((2 * unit_rows, width), bf16),
            jax.ShapeDtypeStruct((2 * w_out_t.shape[0], w_out_t.shape[1] // 2), bf16),
        ),
        in_specs=[ANY] * 6,
        out_specs=(ANY, ANY),
        scratch_shapes=[pltpu.SemaphoreType.DMA((2 + 2 * sum(pieces),))],
        compiler_params=PARAMS,
        cost_estimate=LITTLE,
        name="pack",
    )(*own, *beside)


def as_column(row, eye):
    return jnp.sum(jnp.where(eye, row, 0.0), axis=1, keepdims=True)


def named_experts(ids, experts):
    tokens = ids.shape[1]
    expert = lax.broadcasted_iota(jnp.int32, (experts, tokens), 0)
    hit = jnp.zeros((experts, tokens), f32)
    for index in range(ids.shape[0]):
        hit = jnp.where(ids[index : index + 1, :] == expert, 1.0, hit)
    return hit


def prepare_kernel(groups, slots_dev, *refs):
    sources, (cosine, sine, past, place, send, tags, gain) = refs[:4], refs[4:11]
    positions, slots, ids, flat_gain, sems = refs[11:]
    copies = fetch(list(zip(sources, (positions, slots, ids, flat_gain))), sems)
    for copy in copies:
        copy.wait()
    gain[...] = flat_gain[...].reshape(gain.shape)
    lane = lax.axis_index("hd")
    block = positions.shape[1]

    def iota(shape, dim):
        return lax.broadcasted_iota(jnp.int32, shape, dim)

    eye = iota((block, block), 0) == iota((block, block), 1)
    reach = as_column(jnp.maximum(positions[...], 0).astype(f32), eye)
    past[...] = jnp.broadcast_to(reach, past.shape)
    column = iota((8, 128), 1)
    exponent = (column % 32).astype(f32) * (-2.0 / 64)
    inverse_freq = jnp.exp(exponent * np.float32(np.log(rope_base)))[:1, :]
    angles = reach * inverse_freq
    cosine[...] = jnp.cos(angles)
    turned = jnp.sin(angles)
    sine[...] = jnp.where(iota(angles.shape, 1) % 64 < 32, -turned, turned)

    tokens = ids.shape[1]
    cap = place.shape[0] // 2
    hit = named_experts(ids, 8)
    upto = (iota((tokens, tokens), 0) <= iota((tokens, tokens), 1)).astype(f32)
    rank = jnp.dot(hit, upto, preferred_element_type=f32) - 1.0
    slot = iota((2 * cap, tokens), 0).astype(f32)
    placed = jnp.zeros((2 * cap, tokens), f32)
    for live in range(2):
        order = jnp.where(lane == live, 0, cap).astype(f32)
        member = hit[live : live + 1, :] > 0.0
        placed = jnp.where(member & (slot == rank[live : live + 1, :] + order), 1.0, placed)
    place[...] = placed.astype(bf16)

    where = slots[...]
    owner = jnp.where(where >= 0, where // slots_dev, -1)
    owner_hit = (iota((groups, block), 0) == owner).astype(f32)
    before = (iota((block, block), 0) <= iota((block, block), 1)).astype(f32)
    running = jnp.dot(owner_hit, before, preferred_element_type=f32)
    owner_rank = jnp.sum(owner_hit * running, axis=0, keepdims=True) - 1.0
    capc = send.shape[0] // groups
    row = jnp.where(owner >= 0, owner * capc + owner_rank.astype(jnp.int32), -1)
    send[...] = (iota(send.shape, 0) == row).astype(bf16)
    inside = jnp.where(where >= 0, where % slots_dev, 0)
    high = as_column((inside // 64 + 1).astype(f32), eye)
    low = as_column((inside % 64).astype(f32), eye)
    spot = iota(tags.shape, 1)
    tags[...] = jnp.where(spot == 0, high, jnp.where(spot == 1, low, 0.0)).astype(bf16)


def prepare(groups, slots_dev, positions, slots, ids, gain):
    block, tokens = positions.shape[0], ids.shape[0]
    model = gain.shape[0]
    cap = tokens // 4
    capc = 2 * block // groups
    shapes = [
        ((block, 128), f32),
        ((block, 128), f32),
        ((block, 128), f32),
        ((2 * cap, tokens), bf16),
        ((groups * capc, block), bf16),
        ((block, 128), bf16),
        ((1, model), f32),
    ]
    sources = (positions[None], slots[None], ids.T, gain)
    return pl.pallas_call(
        functools.partial(prepare_kernel, groups, slots_dev),
        out_shape=tuple(jax.ShapeDtypeStruct(shape, kind) for shape, kind in shapes),
        in_specs=[ANY] * 4,
        out_specs=(VMEM,) * len(shapes),
        scratch_shapes=[
            pltpu.VMEM((1, block), jnp.int32),
            pltpu.VMEM((1, block), jnp.int32),
            pltpu.VMEM(ids.shape[::-1], jnp.int32),
            pltpu.VMEM((model,), f32),
            pltpu.SemaphoreType.DMA((4,)),
        ],
        compiler_params=PARAMS,
        cost_estimate=LITTLE,
        name="prepare",
    )(*[pltpu.with_memory_space_constraint(source, pltpu.HBM) for source in sources])


def project_kernel(
    own, other, gain, cosine, sine, w_query, w_keyval, q_out, kv_out, seam_out, raw, rows, sems
):
    count = own.shape[0]
    lane = lax.axis_index("hd")
    mine = pl.multiple_of(lane * count, count)
    theirs = pl.multiple_of((1 - lane) * count, count)
    copies = fetch([(own, raw.at[0]), (other, raw.at[1])], sems)
    cos_q, sin_q = cosine[...], sine[...]
    column = lax.broadcasted_iota(jnp.int32, cos_q.shape, 1)
    lower = column % 64 < 32
    cos_kv = jnp.where(column < 64, cos_q, 1.0)
    sin_kv = jnp.where(column < 64, sin_q, 0.0)
    for index, first in ((0, mine), (1, theirs)):
        copies[index].wait()
        rows[pl.ds(first, count), :] = normalized(raw[index].astype(f32), gain[...])
    width = 256
    for weights, out, cos, sin in ((w_keyval, kv_out, cos_kv, sin_kv), (w_query, q_out, cos_q, sin_q)):
        for first in range(0, weights.shape[1], width):
            made = jnp.dot(rows[...], weights[:, first : first + width], preferred_element_type=f32)
            for part in range(0, width, 128):
                here = made[:, part : part + 128]
                turned = jnp.where(lower, pltpu.roll(here, 96, 1), pltpu.roll(here, 32, 1))
                done = (here * cos + turned * sin).astype(bf16)
                out[:, first + part : first + part + 128] = done
                if out is kv_out:
                    seam_out[:, first + part : first + part + 128] = done[count:, :]


def project(own, other, gain, cosine, sine, w_query, flat_kv):
    count, width = own.shape
    made = w_query.shape[1] + flat_kv.shape[1]
    return pl.pallas_call(
        project_kernel,
        out_shape=(
            jax.ShapeDtypeStruct((2 * count, w_query.shape[1]), bf16),
            jax.ShapeDtypeStruct((2 * count, flat_kv.shape[1]), bf16),
            jax.ShapeDtypeStruct((count, flat_kv.shape[1]), bf16),
        ),
        in_specs=[ANY] * 2 + [VMEM] * 5,
        out_specs=(VMEM, VMEM, VMEM),
        scratch_shapes=[
            pltpu.VMEM((2, count, width), bf16),
            pltpu.VMEM((2 * count, width), bf16),
            pltpu.SemaphoreType.DMA((2,)),
        ],
        compiler_params=PARAMS,
        cost_estimate=takes(8),
        name="project",
    )(own, other, gain, cosine, sine, w_query, flat_kv)


def attend_rows_kernel(first, q, kv, seam, past, mixed, window, sem):
    count = q.shape[0] // 2
    if first == 0:
        copy = pltpu.make_async_copy(seam, window.at[pl.ds(0, count), :], sem)
        copy.start()
        window[count:, :] = kv[:count, :]
        copy.wait()
        keyed = window
    else:
        keyed = kv
    head = 64
    kv_heads = kv.shape[1] // (2 * head)
    per_kv = q.shape[1] // head // kv_heads
    shape = (count, 2 * count)
    row = lax.broadcasted_iota(jnp.int32, shape, 0) + count
    col = lax.broadcasted_iota(jnp.int32, shape, 1)
    reach = past[first : first + count, :1].astype(jnp.int32)
    visible = (col <= row) & (col >= row - reach)
    for kv_head in range(kv_heads):
        lanes = 2 * head * kv_head
        keys = keyed[:, lanes : lanes + head]
        values = keyed[:, lanes + head : lanes + 2 * head]
        for index in range(per_kv):
            at = (kv_head * per_kv + index) * head
            query = q[first : first + count, at : at + head]
            scores = lax.dot_general(query, keys, LAST_DIMS, preferred_element_type=f32)
            raised = jnp.where(visible, jnp.exp(scores * head ** (-0.5)), 0.0)
            probs = (raised / jnp.sum(raised, axis=-1, keepdims=True)).astype(bf16)
            made = jnp.dot(probs, values, preferred_element_type=f32)
            mixed[:, at : at + head] = made.astype(bf16)


def attend_late(q, kv, past):
    def kernel(q, kv, past, mixed):
        attend_rows_kernel(q.shape[0] // 2, q, kv, None, past, mixed, None, None)

    return pl.pallas_call(
        kernel,
        out_shape=jax.ShapeDtypeStruct((q.shape[0] // 2, q.shape[1]), bf16),
        in_specs=[VMEM] * 3,
        out_specs=VMEM,
        compiler_params=PARAMS,
        cost_estimate=takes(2),
        name="attend_late",
    )(q, kv, past)


def attend_early(q, kv, seam, past):
    return pl.pallas_call(
        functools.partial(attend_rows_kernel, 0),
        out_shape=jax.ShapeDtypeStruct((q.shape[0] // 2, q.shape[1]), bf16),
        in_specs=[VMEM, VMEM, ANY, VMEM],
        out_specs=VMEM,
        scratch_shapes=[pltpu.VMEM(kv.shape, bf16), pltpu.SemaphoreType.DMA],
        compiler_params=PARAMS,
        cost_estimate=takes(2),
        name="attend_early",
    )(q, kv, seam, past)


def outward_rows(flip, groups, unit_rows, early, late, parts, w_out, rows):
    place_parts(groups, parts, unit_rows, [(0, unit_rows, w_out, 0)])
    lane = lax.axis_index("hd")
    which = (1 - lane) if flip else lane

    @pl.when(which == 0)
    def _():
        rows[...] = early[...]

    @pl.when(which != 0)
    def _():
        rows[...] = late[...]

    return lax.dot_general(rows[...], w_out[...], LAST_DIMS, preferred_element_type=f32)


def send_kernel(groups, unit_rows, n_parts, early, late, *refs):
    parts, (out, w_out, rows) = refs[:n_parts], refs[n_parts:]
    out[...] = outward_rows(True, groups, unit_rows, early, late, parts, w_out, rows).astype(bf16)


def keep_kernel(groups, unit_rows, n_parts, early, late, tokens, flat_gain, *refs):
    parts, (out, gain, w_out, rows) = refs[:n_parts], refs[n_parts:]
    gain[...] = flat_gain[...].reshape(gain.shape)
    made = outward_rows(False, groups, unit_rows, early, late, parts, w_out, rows)
    out[...] = tokens[...].astype(f32) + made


def outward_send(groups, early, late, parts, unit_rows):
    width, depth = groups * unit_rows, parts[0].shape[1]
    return pl.pallas_call(
        functools.partial(send_kernel, groups, unit_rows, len(parts)),
        out_shape=jax.ShapeDtypeStruct((early.shape[0], width), bf16),
        in_specs=[VMEM] * (2 + len(parts)),
        out_specs=VMEM,
        scratch_shapes=[pltpu.VMEM((width, depth), bf16), pltpu.VMEM(early.shape, bf16)],
        compiler_params=PARAMS,
        cost_estimate=reads(2 * width * depth),
        name="outward_send",
    )(early, late, *parts)


def outward_keep(groups, early, late, tokens, gain, parts, unit_rows):
    width, depth = groups * unit_rows, parts[0].shape[1]
    return pl.pallas_call(
        functools.partial(keep_kernel, groups, unit_rows, len(parts)),
        out_shape=(
            jax.ShapeDtypeStruct(tokens.shape, f32),
            jax.ShapeDtypeStruct((1, width), f32),
        ),
        in_specs=[VMEM] * (4 + len(parts)),
        out_specs=(VMEM, VMEM),
        scratch_shapes=[pltpu.VMEM((width, depth), bf16), pltpu.VMEM(early.shape, bf16)],
        compiler_params=PARAMS,
        cost_estimate=reads(2 * width * depth),
        name="outward_keep",
    )(early, late, tokens, gain, *parts)


def route_kernel(mine, arrived, gain, place, residual, moe_in, sent):
    added = (mine[...] + arrived[...].astype(f32)).astype(bf16)
    residual[...] = added
    moe_in[...] = normalized(added.astype(f32), gain[...])
    cap = sent.shape[0]
    rows = jnp.dot(place[cap:, :], moe_in[...], preferred_element_type=f32)
    sent[...] = rows.astype(bf16)


def route(mine, arrived, gain, place):
    cap = place.shape[0] // 2
    return pl.pallas_call(
        route_kernel,
        out_shape=(
            jax.ShapeDtypeStruct(mine.shape, bf16),
            jax.ShapeDtypeStruct(mine.shape, bf16),
            jax.ShapeDtypeStruct((cap, mine.shape[1]), bf16),
        ),
        in_specs=[VMEM] * 4,
        out_specs=(VMEM,) * 3,
        compiler_params=PARAMS,
        cost_estimate=takes(2),
        name="route",
    )(mine, arrived, gain, place)


def gate_kernel(moe_in, router, ids, place, gates, own, spread):
    cap = own.shape[0]
    own[...] = jnp.dot(place[:cap, :], moe_in[...], preferred_element_type=f32).astype(bf16)
    hit = named_experts(ids, router.shape[0])
    tokens = ids.shape[1]
    row = lax.broadcasted_iota(jnp.int32, (tokens, tokens), 0)
    eye = (row == lax.broadcasted_iota(jnp.int32, (tokens, tokens), 1)).astype(f32)
    named = lax.dot_general(eye, hit, LAST_DIMS, preferred_element_type=f32)
    spread[...] = lax.dot_general(
        eye.astype(bf16), place[...], LAST_DIMS, preferred_element_type=f32
    ).astype(bf16)
    logits = lax.dot_general(moe_in[...], router[...], LAST_DIMS, preferred_element_type=f32)
    raised = jnp.where(named > 0, jnp.exp(logits), 0.0)
    gates[...] = raised / jnp.sum(raised, axis=-1, keepdims=True)


def gate(moe_in, router_t, ids_t, place):
    cap = place.shape[0] // 2
    return pl.pallas_call(
        gate_kernel,
        out_shape=(
            jax.ShapeDtypeStruct((moe_in.shape[0], router_t.shape[0]), f32),
            jax.ShapeDtypeStruct((cap, moe_in.shape[1]), bf16),
            jax.ShapeDtypeStruct(place.shape[::-1], bf16),
        ),
        in_specs=[VMEM] * 4,
        out_specs=(VMEM,) * 3,
        compiler_params=PARAMS,
        cost_estimate=LITTLE,
        name="gate",
    )(moe_in, router_t, ids_t, place)


def expert_kernel(groups, up_rows, down_rows, n_parts, own, other, *refs):
    parts = refs[:n_parts]
    own_out, other_out, rows, gate_up, down = refs[n_parts:]
    width = parts[0].shape[1]
    count = own.shape[0]
    rows[:count, :] = own[...]
    rows[count:, :] = other[...]
    pieces = [(i * up_rows, up_rows, gate_up, i * width) for i in range(2)]
    pieces += [
        (2 * up_rows + i * down_rows, down_rows, down, i * width) for i in range(down.shape[1] // width)
    ]
    unit_rows = pieces[-1][0] + down_rows
    place_parts(groups, parts, unit_rows, pieces)
    both = jnp.dot(rows[...], gate_up[...], preferred_element_type=f32)
    gate, up = both[:, :width], both[:, width:]
    hidden = (gate / (1.0 + jnp.exp(-gate)) * up).astype(bf16)
    made = jnp.dot(hidden, down[...], preferred_element_type=f32).astype(bf16)
    own_out[...] = made[:count, :]
    other_out[...] = made[count:, :]


def expert(groups, own, other, parts, up_rows, down_rows):
    count, model = own.shape
    width = parts[0].shape[1]
    return pl.pallas_call(
        functools.partial(expert_kernel, groups, up_rows, down_rows, len(parts)),
        out_shape=(jax.ShapeDtypeStruct(own.shape, bf16),) * 2,
        in_specs=[VMEM] * (2 + len(parts)),
        out_specs=(VMEM, VMEM),
        scratch_shapes=[
            pltpu.VMEM((2 * count, model), bf16),
            pltpu.VMEM((groups * up_rows, 2 * width), bf16),
            pltpu.VMEM((groups * down_rows, model), bf16),
        ],
        compiler_params=PARAMS,
        cost_estimate=reads(2 * groups * 2 * (up_rows * 2 * width + down_rows * model)),
        name="expert",
    )(own, other, *parts)


def combine_kernel(residual, gates, spread, own, returned, out):
    lane = lax.axis_index("hd")
    count = own.shape[0]
    column = lax.broadcasted_iota(jnp.int32, gates.shape, 1)
    total = jnp.zeros(residual.shape, f32)
    for index, made in ((0, own), (1, returned)):
        live = lane if index == 0 else 1 - lane
        weight = jnp.sum(jnp.where(column == live, gates[...], 0.0), axis=-1, keepdims=True)
        picked = jnp.dot(
            spread[:, index * count : (index + 1) * count], made[...], preferred_element_type=f32
        )
        total += weight * picked
    out[...] = (residual[...].astype(f32) + total).astype(bf16)


def combine(residual, gates, spread, own, returned):
    return pl.pallas_call(
        combine_kernel,
        out_shape=jax.ShapeDtypeStruct(residual.shape, bf16),
        in_specs=[VMEM] * 5,
        out_specs=VMEM,
        compiler_params=PARAMS,
        cost_estimate=reads(6 * residual.shape[0] * residual.shape[1]),
        name="combine",
    )(residual, gates, spread, own, returned)


def bundle_kernel(send, kv, tags, out):
    groups, rows, _ = out.shape
    heads = kv.shape[1] // 128
    capc = send.shape[0] // groups
    packed = jnp.dot(send[...], kv[...], preferred_element_type=f32).astype(bf16)
    tagged = jnp.dot(send[...], tags[...], preferred_element_type=f32)
    one = (lax.broadcasted_iota(jnp.int32, (16, 128), 0) == lax.broadcasted_iota(jnp.int32, (16, 128), 1))
    for owner in range(groups):
        mine = slice(owner * capc, (owner + 1) * capc)
        for head in range(heads):
            out[owner, head * capc : (head + 1) * capc, :] = packed[mine, head * 128 : (head + 1) * 128]
        wide = jnp.concatenate([tagged[mine, :], jnp.zeros((128 - capc, 128), f32)], axis=0)
        out[owner, heads * capc :, :] = lax.dot_general(
            one.astype(f32), wide, LAST_DIMS, preferred_element_type=f32
        ).astype(bf16)


def bundle(groups, send, kv, tags):
    rows = send.shape[0] // groups * (kv.shape[1] // 128) + 16
    return pl.pallas_call(
        bundle_kernel,
        out_shape=jax.ShapeDtypeStruct((groups, rows, 128), bf16),
        in_specs=[VMEM] * 3,
        out_specs=VMEM,
        compiler_params=PARAMS,
        cost_estimate=LITTLE,
        name="bundle",
    )(send, kv, tags)


def write_kernel(heads, arrived, cache, out, rows, wide, known):
    groups, size, _ = arrived.shape
    slots = cache.shape[0] // heads
    capc = (size - 16) // heads
    high, low = [], []
    for source in range(groups):
        for head in range(heads):
            rows[source * capc : (source + 1) * capc, head * 128 : (head + 1) * 128] = arrived[
                source, head * capc : (head + 1) * capc, :
            ]
        numbers = arrived[source, heads * capc :, :].astype(f32)
        high.append(numbers[0:1, :capc])
        low.append(numbers[1:2, :capc])
    slot = jnp.concatenate(high, axis=1) * 64.0 + jnp.concatenate(low, axis=1) - 64.0
    row = lax.broadcasted_iota(jnp.int32, (slots, slot.shape[1]), 0).astype(f32)
    hit = (row == slot).astype(bf16)
    made = jnp.dot(hit, rows[...], preferred_element_type=f32)
    found = jnp.dot(hit, jnp.ones((slot.shape[1], 128), bf16), preferred_element_type=f32)
    for head in range(heads):
        wide[pl.ds(head, slots, heads), :] = made[:, head * 128 : (head + 1) * 128]
        known[pl.ds(head, slots, heads), :] = found
    old = cache[...].astype(f32)
    out[...] = jnp.where(known[...] > 0.0, wide[...], old).astype(bf16)


def write(arrived, cache):
    slots, heads, lanes = cache.shape
    capc = (arrived.shape[1] - 16) // heads
    flat = (slots * heads, lanes)
    written = pl.pallas_call(
        functools.partial(write_kernel, heads),
        out_shape=jax.ShapeDtypeStruct(flat, bf16),
        in_specs=[VMEM] * 2,
        out_specs=VMEM,
        scratch_shapes=[
            pltpu.VMEM((arrived.shape[0] * capc, heads * lanes), bf16),
            pltpu.VMEM(flat, f32),
            pltpu.VMEM(flat, f32),
        ],
        compiler_params=PARAMS,
        cost_estimate=reads(1 << 21),
        name="write",
    )(arrived, cache.reshape(flat))
    return written.reshape(cache.shape)


def two_lane_shards(
    tokens,
    positions,
    attn_gain,
    w_query,
    w_keyval,
    w_out,
    moe_gain,
    router,
    w_gate_up,
    w_down,
    expert_ids,
    cache_slot,
    kv_cache,
):
    groups = lax.axis_size("grp")
    tok_rows, model = tokens.shape
    block = positions.shape[0]
    kv_local, head2 = w_keyval.shape[1:]
    kv_width = kv_local * head2
    slots_dev = kv_cache.shape[0]
    swap = functools.partial(lax.ppermute, axis_name="hd", perm=[(0, 1), (1, 0)])

    together = lax.optimization_barrier

    other_tokens = swap(tokens)
    own = (w_gate_up[0], w_down[0], w_out.T)
    up_rows, down_rows = own[0].shape[0], own[1].shape[0]
    beside = [lax.ppermute(part, "grp", sibling_pairs(groups)) for part in own]
    expert_pair, out_pair = pack(own, beside)
    out_ring = Ring(out_pair, groups)
    out_ring.step()
    expert_ring = Ring(expert_pair, groups)
    expert_ring.step()
    w_keyval, positions = together((w_keyval, positions, out_pair))[:2]
    flat_kv = w_keyval.reshape(model, kv_width)
    cosine, sine, past, place, send, tags, gain = prepare(
        groups, slots_dev, positions, cache_slot, expert_ids, attn_gain
    )
    other_tokens, cosine, flat_kv = out_ring.pin(other_tokens, cosine, flat_kv)
    out_ring.step()

    q, kv, tail = project(tokens, other_tokens, gain, cosine, sine, w_query, flat_kv)
    seam = lax.ppermute(tail, "grp", [(g, g + 1) for g in range(groups - 1)])
    q = out_ring.pin(q)
    out_ring.step()
    out_ring.share(2)
    late = attend_late(q, kv, past)
    seam, late = together((seam, late))
    seam = expert_ring.pin(seam)
    expert_ring.step()
    early = attend_early(q, kv, seam, past)
    early, out_ring.near = together((early, out_ring.near))
    early = out_ring.pin(early)
    out_ring.step()
    out_ring.share(3)
    early, kv, out_ring.near = together((early, kv, out_ring.near))
    outgoing = bundle(groups, send, kv, tags)
    arrived_cache = lax.all_to_all(outgoing, "grp", split_axis=0, concat_axis=0, tiled=True)
    early, outgoing = together((early, outgoing))
    early = out_ring.pin(early)
    early = expert_ring.pin(early)
    expert_ring.step()
    out_ring.share()
    sent = outward_send(groups, early, late, out_ring.parts(), out_ring.unit_rows)
    arrived = swap(sent)
    early = together((early, sent))[0]
    mine, late_gain = outward_keep(
        groups, early, late, tokens, moe_gain, out_ring.parts(), out_ring.unit_rows
    )
    mine = expert_ring.pin(mine)
    expert_ring.share()
    expert_ring.step()
    arrived, mine = expert_ring.pin(arrived, mine)
    expert_ring.share()

    residual, moe_in, sent_rows = route(mine, arrived, late_gain, place)
    landed = swap(sent_rows)
    gates, own_rows, spread = gate(moe_in, router.T, expert_ids.T, place)
    landed, own_rows = together((landed, own_rows))
    own_made, back = expert(
        groups, own_rows, landed, expert_ring.parts(), up_rows, down_rows
    )
    returned = swap(back)
    layer_out = combine(residual, gates, spread, own_made, returned)
    layer_out, arrived_cache = together((layer_out, arrived_cache))
    cache_after = write(arrived_cache, kv_cache)
    return (layer_out, cache_after)


def passed_along(value, axis, steps):
    count = lax.axis_size(axis)
    initial, last = (max(0, -steps), min(count, count - steps))
    return lax.ppermute(value, axis, [(source, source + steps) for source in range(initial, last)])


def rms_norm(row_set, norm_gain):
    floats = row_set.astype(jnp.float32)
    factor = lax.rsqrt(jnp.mean(floats * floats, axis=-1, keepdims=True) + norm_eps)
    return (floats * factor * norm_gain).astype(jnp.bfloat16)


def rotate(vectors, angle_pos):
    halves = vectors.shape[-1] // 2
    inverse_freq = rope_base ** (-2.0 * jnp.arange(halves, dtype=jnp.float32) / vectors.shape[-1])
    angles = angle_pos[:, None, None] * inverse_freq[None, None, :]
    cosine = jnp.cos(angles)
    sine_part = jnp.sin(angles)
    first_half = vectors[..., :halves]
    second_half = vectors[..., halves:]
    return jnp.concatenate(
        [
            first_half * cosine - second_half * sine_part,
            second_half * cosine + first_half * sine_part,
        ],
        axis=-1,
    )


def expert_rows(row_set, gate_up, down_rows):
    gate_and_up = jnp.dot(row_set, gate_up, preferred_element_type=jnp.float32)
    inner_width = gate_and_up.shape[1] // 2
    hidden = (jax.nn.silu(gate_and_up[:, :inner_width]) * gate_and_up[:, inner_width:]).astype(
        jnp.bfloat16
    )
    return jnp.dot(hidden, down_rows, preferred_element_type=jnp.float32).astype(jnp.bfloat16)


def attend_rows(query_blk, keys_blk, vals_blk, visible, scale_qk):
    scores = (
        jnp.einsum("qkgd,skd->kgqs", query_blk, keys_blk, preferred_element_type=jnp.float32)
        * scale_qk
    )
    weights_f = jnp.where(visible[None, None], jnp.exp(scores), 0.0)
    prob_bf = (weights_f / jnp.sum(weights_f, axis=-1, keepdims=True)).astype(jnp.bfloat16)
    return jnp.einsum("kgqs,skd->qkgd", prob_bf, vals_blk, preferred_element_type=jnp.float32)


def shards(
    tokens,
    positions,
    attn_gain,
    w_query,
    w_keyval,
    w_out,
    moe_gain,
    router,
    w_gate_up,
    w_down,
    expert_ids,
    cache_slot,
    kv_cache,
):
    lane_count = lax.axis_size("hd")
    group_count = lax.axis_size("grp")
    tok_rows = tokens.shape[0]
    model_width = tokens.shape[1]
    block_len = positions.shape[0]
    seg_most = block_len // 2
    head_dim = w_keyval.shape[2] // 2
    kv_local = w_keyval.shape[1]
    q_local = w_query.shape[1] // head_dim
    per_kv = q_local // kv_local
    expert_cap = tok_rows // 4
    normed = rms_norm(tokens, attn_gain)
    flat_kv = w_keyval.reshape(model_width, kv_local * 2 * head_dim)
    section = lax.all_gather(normed, "hd", axis=0, tiled=True)
    projected = jnp.concatenate(
        [
            jnp.dot(section, w_query, preferred_element_type=jnp.float32),
            jnp.dot(section, flat_kv, preferred_element_type=jnp.float32),
        ],
        axis=1,
    )
    angle_pos = jnp.maximum(positions, 0).astype(jnp.float32)
    queries = rotate(
        projected[:, : q_local * head_dim].reshape(block_len, q_local, head_dim), angle_pos
    ).astype(jnp.bfloat16)
    key_val = projected[:, q_local * head_dim :].reshape(block_len, kv_local, 2 * head_dim)
    rotated = rotate(key_val[:, :, :head_dim], angle_pos).astype(jnp.bfloat16)
    stored = jnp.concatenate([rotated, key_val[:, :, head_dim:].astype(jnp.bfloat16)], axis=2)
    seam_rows = passed_along(stored[block_len - seg_most :], "grp", 1)
    window = jnp.concatenate([seam_rows, stored], axis=0)
    scale_qk = head_dim ** (-0.5)
    local_rows = jnp.arange(block_len, dtype=jnp.int32)
    lowest = local_rows - jnp.maximum(positions, 0)
    pieces_out = []
    for q_block in range(2):
        first_row = q_block * seg_most
        rows_here = first_row + jnp.arange(seg_most, dtype=jnp.int32)
        cols_here = first_row - seg_most + jnp.arange(2 * seg_most, dtype=jnp.int32)
        low_here = lowest[first_row : first_row + seg_most]
        visible = (cols_here[None, :] >= low_here[:, None]) & (
            cols_here[None, :] <= rows_here[:, None]
        )
        query_blk = queries[first_row : first_row + seg_most].reshape(
            seg_most, kv_local, per_kv, head_dim
        )
        keys_blk = window[first_row : first_row + 2 * seg_most, :, :head_dim]
        vals_blk = window[first_row : first_row + 2 * seg_most, :, head_dim:]
        mixed_rows = attend_rows(query_blk, keys_blk, vals_blk, visible, scale_qk)
        pieces_out.append(mixed_rows.reshape(seg_most, q_local * head_dim).astype(jnp.bfloat16))
    attended = jnp.concatenate(pieces_out, axis=0)
    slots_dev = kv_cache.shape[0]
    capc = 2 * block_len // group_count
    live_slot = cache_slot >= 0
    owners = jnp.where(live_slot, cache_slot // slots_dev, group_count)
    owner_hit = (owners[:, None] == jnp.arange(group_count, dtype=jnp.int32)[None, :]).astype(
        jnp.bfloat16
    )
    lower_tri = (local_rows[:, None] >= local_rows[None, :]).astype(jnp.bfloat16)
    running = jnp.dot(lower_tri, owner_hit, preferred_element_type=jnp.float32)
    owner_rank = jnp.sum(running * owner_hit.astype(jnp.float32), axis=1).astype(jnp.int32) - 1
    send_rows = jnp.where(live_slot, owners * capc + owner_rank, group_count * capc)
    outgoing_cache = (
        jnp.zeros((group_count * capc, kv_local, 2 * head_dim), jnp.bfloat16)
        .at[send_rows]
        .set(stored, mode="drop")
    )
    outgoing_slots = (
        jnp.full((group_count * capc,), -1, jnp.int32)
        .at[send_rows]
        .set(cache_slot % slots_dev, mode="drop")
    )
    arrived, arrived_slots = (
        lax.all_to_all(
            outgoing_cache.reshape(group_count, capc, kv_local, 2 * head_dim),
            "grp",
            split_axis=0,
            concat_axis=0,
            tiled=True,
        ),
        lax.all_to_all(
            outgoing_slots.reshape(group_count, capc),
            "grp",
            split_axis=0,
            concat_axis=0,
            tiled=True,
        ),
    )
    flat_slots = arrived_slots.reshape(group_count * capc)
    write_rows = jnp.where(flat_slots >= 0, flat_slots, slots_dev).astype(jnp.int32)
    cache_after = kv_cache.at[write_rows].set(
        arrived.reshape(group_count * capc, kv_local, 2 * head_dim), mode="drop"
    )
    by_token = lax.all_to_all(attended, "hd", split_axis=0, concat_axis=1, tiled=True)
    attn_proj = jnp.dot(
        by_token,
        lax.all_gather(w_out, "grp", axis=1, tiled=True),
        preferred_element_type=jnp.float32,
    )
    residual = (tokens.astype(jnp.float32) + attn_proj).astype(jnp.bfloat16)
    moe_in = rms_norm(residual, moe_gain)
    logits = jnp.dot(moe_in, router, preferred_element_type=jnp.float32)
    expert_range = jnp.arange(router.shape[1], dtype=jnp.int32)
    matches_all = expert_ids[:, :, None] == expert_range[None, None, :]
    chosen = jnp.sum(jnp.where(matches_all, logits[:, None, :], 0.0), axis=2)
    raised = jnp.exp(chosen)
    gates = raised / jnp.sum(raised, axis=1, keepdims=True)
    live_range = jnp.arange(lane_count, dtype=jnp.int32)
    matches = expert_ids[:, :, None] == live_range[None, None, :]
    member = jnp.any(matches, axis=1)
    weighting = jnp.sum(jnp.where(matches, gates[:, :, None], 0.0), axis=1)
    ranking = jnp.cumsum(member.astype(jnp.int32), axis=0) - 1
    target = jnp.where(member, live_range[None, :] * expert_cap + ranking, -1)
    slot_range = jnp.arange(lane_count * expert_cap, dtype=jnp.int32)
    slot_hits = target[None, :, :] == slot_range[:, None, None]
    placing = jnp.any(slot_hits, axis=2).astype(jnp.bfloat16)
    outgoing = (
        jnp.dot(placing, moe_in, preferred_element_type=jnp.float32)
        .astype(jnp.bfloat16)
        .reshape(lane_count, expert_cap, model_width)
    )
    gate_up_all, down_all = (
        lax.all_gather(w_gate_up, "grp", axis=1, tiled=True),
        lax.all_gather(w_down, "grp", axis=1, tiled=True),
    )
    gate_up_mat = gate_up_all[0]
    down_mat = down_all[0]
    landed = lax.all_to_all(outgoing, "hd", split_axis=0, concat_axis=0, tiled=True)
    results = expert_rows(landed.reshape(-1, model_width), gate_up_mat, down_mat).reshape(landed.shape)
    returned = lax.all_to_all(results, "hd", split_axis=0, concat_axis=0, tiled=True)
    flat_returned = returned.reshape(-1, model_width)
    fetched = flat_returned[jnp.maximum(target, 0)]
    used_weight = jnp.where(member, weighting, 0.0)
    moe_total = jnp.sum(used_weight[:, :, None] * fetched.astype(jnp.float32), axis=1)
    layer_out = (residual.astype(jnp.float32) + moe_total).astype(jnp.bfloat16)
    return (layer_out, cache_after)


def solution(mesh):
    two_lanes = mesh.shape["hd"] == 2 and mesh.shape["grp"] % 8 == 0
    return jax.shard_map(
        two_lane_shards if two_lanes else shards,
        mesh=mesh,
        in_specs=(
            P(("grp", "hd"), None),
            P("grp"),
            P(),
            P(None, "hd"),
            P(None, "hd", None),
            P(None, "grp"),
            P(),
            P(),
            P("hd", "grp", None),
            P("hd", "grp", None),
            P(("grp", "hd"), None),
            P("grp"),
            P("grp", "hd", None),
        ),
        out_specs=(P(("grp", "hd"), None), P("grp", "hd", None)),
        check_vma=False,
    )
```

```python
import functools

import jax
import jax.numpy as jnp
import numpy as np
from jax import lax
from jax.experimental import pallas as pl
from jax.experimental.pallas import tpu as pltpu
from jax.sharding import PartitionSpec as P

norm_eps = 1e-05
rope_base = 10000.0
bf16 = jnp.bfloat16
f32 = jnp.float32
LAST_DIMS = (((1,), (1,)), ((), ()))


def ring_cycle(groups):
    rows = groups // 4
    return [2 * r for r in range(rows)] + [2 * r + 1 for r in reversed(range(rows))]


def ring_pairs(groups):
    cycle = ring_cycle(groups)
    count = len(cycle)
    pairs = []
    for place, pair in enumerate(cycle):
        pairs.append((2 * pair, 2 * cycle[(place + 1) % count]))
        pairs.append((2 * pair + 1, 2 * cycle[(place - 1) % count] + 1))
    return pairs


def sibling_pairs(groups):
    return [(g, g ^ 1) for g in range(groups)]


def ring_sources(groups, me):
    count = groups // 2
    rows = count // 2
    side, pair = me % 2, me // 2
    row, col = pair // 2, pair % 2
    place = jnp.where(col == 0, row, count - 1 - row)

    def block(core, steps):
        there = (place + (2 * core - 1) * steps + count) % count
        other = jnp.where(there < rows, 2 * there, 2 * (count - 1 - there) + 1)
        return [2 * other + core, 2 * other + 1 - core]

    full = (count - 1) // 2
    listed = [me, me + 1 - 2 * side]
    for core in (side, 1 - side):
        for steps in range(1, full + 1):
            listed += block(core, steps)
    return listed + [block(side, count // 2)[0], block(1 - side, count // 2)[0]]


class Ring:
    def __init__(self, pair, groups):
        self.across = functools.partial(lax.ppermute, axis_name="grp", perm=ring_pairs(groups))
        self.beside = functools.partial(lax.ppermute, axis_name="grp", perm=sibling_pairs(groups))
        self.full = (groups // 2 - 1) // 2
        self.unit_rows = pair.shape[0] // 2
        self.mine = [pair]
        self.near = []

    def step(self):
        held = self.mine[-1]
        if len(self.mine) > self.full:
            held = held[: self.unit_rows]
        self.mine.append(self.across(held))

    def pin(self, *others):
        done = lax.optimization_barrier((self.mine[-1],) + others)
        self.mine[-1] = done[0]
        return done[1:] if len(others) > 1 else done[1]

    def share(self, upto=None):
        for index in range(1 + len(self.near), 1 + (upto or len(self.mine) - 1)):
            self.near.append(self.beside(self.mine[index]))

    def parts(self):
        full = self.full
        return self.mine[: full + 1] + self.near[:full] + [self.mine[full + 1], self.near[full]]


def place_parts(groups, parts, unit_rows, pieces):
    sources = ring_sources(groups, lax.axis_index("grp"))
    shard = 0
    for part in parts:
        for unit in range(part.shape[0] // unit_rows):
            for first, rows, target, lane in pieces:
                at = pl.multiple_of(sources[shard] * rows, rows)
                start = unit * unit_rows + first
                target[pl.ds(at, rows), lane : lane + part.shape[1]] = part[start : start + rows, :]
            shard += 1


VMEM = pl.BlockSpec(memory_space=pltpu.VMEM)
ANY = pl.BlockSpec(memory_space=pl.ANY)
HBM = pl.BlockSpec(memory_space=pltpu.HBM)
PARAMS = pltpu.CompilerParams(vmem_limit_bytes=16 << 20)


LITTLE = pl.CostEstimate(flops=1, bytes_accessed=1, transcendentals=0)


def takes(us):
    return pl.CostEstimate(
        flops=int(us * 1.15e9), bytes_accessed=int(us * 8e6), transcendentals=0
    )


def reads(nbytes):
    return pl.CostEstimate(flops=1, bytes_accessed=nbytes, transcendentals=0)


def normalized(floats, gain):
    factor = lax.rsqrt(jnp.mean(floats * floats, axis=-1, keepdims=True) + norm_eps)
    return (floats * factor * gain).astype(bf16)


def fetch(pairs, sems):
    copies = []
    for index, (source, target) in enumerate(pairs):
        copies.append(pltpu.make_async_copy(source, target, sems.at[index]))
        copies[-1].start()
    return copies


def pack_kernel(*refs):
    sources, (expert_pair, out_pair, sems) = refs[:6], refs[6:]
    width = expert_pair.shape[1]
    lane = lax.axis_index("hd")
    first = pl.multiple_of(lane * out_pair.shape[1], out_pair.shape[1])
    pairs = []
    row = 0
    for index in range(2):
        up, down, w_out = sources[3 * index : 3 * index + 3]
        count = w_out.shape[0]
        pairs.append(
            (w_out.at[:, pl.ds(first, out_pair.shape[1])], out_pair.at[pl.ds(index * count, count), :])
        )
        for source in (up, down):
            for at in range(0, source.shape[1], width):
                pairs.append(
                    (source.at[:, pl.ds(at, width)], expert_pair.at[pl.ds(row, source.shape[0]), :])
                )
                row += source.shape[0]
    for copy in fetch(pairs, sems):
        copy.wait()


def pack(own, beside):
    own = [pltpu.with_memory_space_constraint(part, pltpu.HBM) for part in own]
    up, down, w_out_t = own
    width = up.shape[1] // 2
    pieces = [up.shape[1] // width, down.shape[1] // width]
    unit_rows = pieces[0] * up.shape[0] + pieces[1] * down.shape[0]
    return pl.pallas_call(
        pack_kernel,
        out_shape=(
            jax.ShapeDtypeStruct((2 * unit_rows, width), bf16),
            jax.ShapeDtypeStruct((2 * w_out_t.shape[0], w_out_t.shape[1] // 2), bf16),
        ),
        in_specs=[ANY] * 6,
        out_specs=(ANY, ANY),
        scratch_shapes=[pltpu.SemaphoreType.DMA((2 + 2 * sum(pieces),))],
        compiler_params=PARAMS,
        cost_estimate=LITTLE,
        name="pack",
    )(*own, *beside)


def as_column(row, eye):
    return jnp.sum(jnp.where(eye, row, 0.0), axis=1, keepdims=True)


def named_experts(ids, experts):
    tokens = ids.shape[1]
    expert = lax.broadcasted_iota(jnp.int32, (experts, tokens), 0)
    hit = jnp.zeros((experts, tokens), f32)
    for index in range(ids.shape[0]):
        hit = jnp.where(ids[index : index + 1, :] == expert, 1.0, hit)
    return hit


def prepare_kernel(groups, slots_dev, *refs):
    sources, (cosine, sine, past, place, send, tags, gain) = refs[:4], refs[4:11]
    positions, slots, ids, flat_gain, sems = refs[11:]
    copies = fetch(list(zip(sources, (positions, slots, ids, flat_gain))), sems)
    for copy in copies:
        copy.wait()
    gain[...] = flat_gain[...].reshape(gain.shape)
    lane = lax.axis_index("hd")
    block = positions.shape[1]

    def iota(shape, dim):
        return lax.broadcasted_iota(jnp.int32, shape, dim)

    eye = iota((block, block), 0) == iota((block, block), 1)
    reach = as_column(jnp.maximum(positions[...], 0).astype(f32), eye)
    past[...] = jnp.broadcast_to(reach, past.shape)
    column = iota((8, 128), 1)
    exponent = (column % 32).astype(f32) * (-2.0 / 64)
    inverse_freq = jnp.exp(exponent * np.float32(np.log(rope_base)))[:1, :]
    angles = reach * inverse_freq
    cosine[...] = jnp.cos(angles)
    turned = jnp.sin(angles)
    sine[...] = jnp.where(iota(angles.shape, 1) % 64 < 32, -turned, turned)

    tokens = ids.shape[1]
    cap = place.shape[0] // 2
    hit = named_experts(ids, 8)
    upto = (iota((tokens, tokens), 0) <= iota((tokens, tokens), 1)).astype(f32)
    rank = jnp.dot(hit, upto, preferred_element_type=f32) - 1.0
    slot = iota((2 * cap, tokens), 0).astype(f32)
    placed = jnp.zeros((2 * cap, tokens), f32)
    for live in range(2):
        order = jnp.where(lane == live, 0, cap).astype(f32)
        member = hit[live : live + 1, :] > 0.0
        placed = jnp.where(member & (slot == rank[live : live + 1, :] + order), 1.0, placed)
    place[...] = placed.astype(bf16)

    where = slots[...]
    owner = jnp.where(where >= 0, where // slots_dev, -1)
    owner_hit = (iota((groups, block), 0) == owner).astype(f32)
    before = (iota((block, block), 0) <= iota((block, block), 1)).astype(f32)
    running = jnp.dot(owner_hit, before, preferred_element_type=f32)
    owner_rank = jnp.sum(owner_hit * running, axis=0, keepdims=True) - 1.0
    capc = send.shape[0] // groups
    row = jnp.where(owner >= 0, owner * capc + owner_rank.astype(jnp.int32), -1)
    send[...] = (iota(send.shape, 0) == row).astype(bf16)
    inside = jnp.where(where >= 0, where % slots_dev, 0)
    high = as_column((inside // 64 + 1).astype(f32), eye)
    low = as_column((inside % 64).astype(f32), eye)
    spot = iota(tags.shape, 1)
    tags[...] = jnp.where(spot == 0, high, jnp.where(spot == 1, low, 0.0)).astype(bf16)


def prepare(groups, slots_dev, positions, slots, ids, gain):
    block, tokens = positions.shape[0], ids.shape[0]
    model = gain.shape[0]
    cap = tokens // 4
    capc = 2 * block // groups
    shapes = [
        ((block, 128), f32),
        ((block, 128), f32),
        ((block, 128), f32),
        ((2 * cap, tokens), bf16),
        ((groups * capc, block), bf16),
        ((block, 128), bf16),
        ((1, model), f32),
    ]
    sources = (positions[None], slots[None], ids.T, gain)
    return pl.pallas_call(
        functools.partial(prepare_kernel, groups, slots_dev),
        out_shape=tuple(jax.ShapeDtypeStruct(shape, kind) for shape, kind in shapes),
        in_specs=[ANY] * 4,
        out_specs=(VMEM,) * len(shapes),
        scratch_shapes=[
            pltpu.VMEM((1, block), jnp.int32),
            pltpu.VMEM((1, block), jnp.int32),
            pltpu.VMEM(ids.shape[::-1], jnp.int32),
            pltpu.VMEM((model,), f32),
            pltpu.SemaphoreType.DMA((4,)),
        ],
        compiler_params=PARAMS,
        cost_estimate=LITTLE,
        name="prepare",
    )(*[pltpu.with_memory_space_constraint(source, pltpu.HBM) for source in sources])


def project_kernel(
    own, other, gain, cosine, sine, w_query, w_keyval, q_out, kv_out, seam_out, raw, rows, sems
):
    count = own.shape[0]
    lane = lax.axis_index("hd")
    mine = pl.multiple_of(lane * count, count)
    theirs = pl.multiple_of((1 - lane) * count, count)
    copies = fetch([(own, raw.at[0]), (other, raw.at[1])], sems)
    cos_q, sin_q = cosine[...], sine[...]
    column = lax.broadcasted_iota(jnp.int32, cos_q.shape, 1)
    lower = column % 64 < 32
    cos_kv = jnp.where(column < 64, cos_q, 1.0)
    sin_kv = jnp.where(column < 64, sin_q, 0.0)
    for index, first in ((0, mine), (1, theirs)):
        copies[index].wait()
        rows[pl.ds(first, count), :] = normalized(raw[index].astype(f32), gain[...])
    width = 256
    for weights, out, cos, sin in ((w_keyval, kv_out, cos_kv, sin_kv), (w_query, q_out, cos_q, sin_q)):
        for first in range(0, weights.shape[1], width):
            made = jnp.dot(rows[...], weights[:, first : first + width], preferred_element_type=f32)
            for part in range(0, width, 128):
                here = made[:, part : part + 128]
                turned = jnp.where(lower, pltpu.roll(here, 96, 1), pltpu.roll(here, 32, 1))
                done = (here * cos + turned * sin).astype(bf16)
                out[:, first + part : first + part + 128] = done
                if out is kv_out:
                    seam_out[:, first + part : first + part + 128] = done[count:, :]


def project(own, other, gain, cosine, sine, w_query, flat_kv):
    count, width = own.shape
    made = w_query.shape[1] + flat_kv.shape[1]
    return pl.pallas_call(
        project_kernel,
        out_shape=(
            jax.ShapeDtypeStruct((2 * count, w_query.shape[1]), bf16),
            jax.ShapeDtypeStruct((2 * count, flat_kv.shape[1]), bf16),
            jax.ShapeDtypeStruct((count, flat_kv.shape[1]), bf16),
        ),
        in_specs=[ANY] * 2 + [VMEM] * 5,
        out_specs=(VMEM, VMEM, VMEM),
        scratch_shapes=[
            pltpu.VMEM((2, count, width), bf16),
            pltpu.VMEM((2 * count, width), bf16),
            pltpu.SemaphoreType.DMA((2,)),
        ],
        compiler_params=PARAMS,
        cost_estimate=takes(8),
        name="project",
    )(own, other, gain, cosine, sine, w_query, flat_kv)


def attend_rows_kernel(first, q, kv, seam, past, mixed, window, sem):
    count = q.shape[0] // 2
    if first == 0:
        copy = pltpu.make_async_copy(seam, window.at[pl.ds(0, count), :], sem)
        copy.start()
        window[count:, :] = kv[:count, :]
        copy.wait()
        keyed = window
    else:
        keyed = kv
    head = 64
    kv_heads = kv.shape[1] // (2 * head)
    per_kv = q.shape[1] // head // kv_heads
    shape = (count, 2 * count)
    row = lax.broadcasted_iota(jnp.int32, shape, 0) + count
    col = lax.broadcasted_iota(jnp.int32, shape, 1)
    reach = past[first : first + count, :1].astype(jnp.int32)
    visible = (col <= row) & (col >= row - reach)
    for kv_head in range(kv_heads):
        lanes = 2 * head * kv_head
        keys = keyed[:, lanes : lanes + head]
        values = keyed[:, lanes + head : lanes + 2 * head]
        for index in range(per_kv):
            at = (kv_head * per_kv + index) * head
            query = q[first : first + count, at : at + head]
            scores = lax.dot_general(query, keys, LAST_DIMS, preferred_element_type=f32)
            raised = jnp.where(visible, jnp.exp(scores * head ** (-0.5)), 0.0)
            probs = (raised / jnp.sum(raised, axis=-1, keepdims=True)).astype(bf16)
            made = jnp.dot(probs, values, preferred_element_type=f32)
            mixed[:, at : at + head] = made.astype(bf16)


def attend_late(q, kv, past):
    def kernel(q, kv, past, mixed):
        attend_rows_kernel(q.shape[0] // 2, q, kv, None, past, mixed, None, None)

    return pl.pallas_call(
        kernel,
        out_shape=jax.ShapeDtypeStruct((q.shape[0] // 2, q.shape[1]), bf16),
        in_specs=[VMEM] * 3,
        out_specs=VMEM,
        compiler_params=PARAMS,
        cost_estimate=takes(2),
        name="attend_late",
    )(q, kv, past)


def attend_early(q, kv, seam, past):
    return pl.pallas_call(
        functools.partial(attend_rows_kernel, 0),
        out_shape=jax.ShapeDtypeStruct((q.shape[0] // 2, q.shape[1]), bf16),
        in_specs=[VMEM, VMEM, ANY, VMEM],
        out_specs=VMEM,
        scratch_shapes=[pltpu.VMEM(kv.shape, bf16), pltpu.SemaphoreType.DMA],
        compiler_params=PARAMS,
        cost_estimate=takes(2),
        name="attend_early",
    )(q, kv, seam, past)


def outward_rows(flip, groups, unit_rows, early, late, parts, w_out, rows):
    place_parts(groups, parts, unit_rows, [(0, unit_rows, w_out, 0)])
    lane = lax.axis_index("hd")
    which = (1 - lane) if flip else lane

    @pl.when(which == 0)
    def _():
        rows[...] = early[...]

    @pl.when(which != 0)
    def _():
        rows[...] = late[...]

    return lax.dot_general(rows[...], w_out[...], LAST_DIMS, preferred_element_type=f32)


def send_kernel(groups, unit_rows, n_parts, early, late, *refs):
    parts, (out, w_out, rows) = refs[:n_parts], refs[n_parts:]
    out[...] = outward_rows(True, groups, unit_rows, early, late, parts, w_out, rows).astype(bf16)


def keep_kernel(groups, unit_rows, n_parts, early, late, tokens, flat_gain, *refs):
    parts, (out, gain, w_out, rows, total, sem) = refs[:n_parts], refs[n_parts:]
    gain[...] = flat_gain[...].reshape(gain.shape)
    made = outward_rows(False, groups, unit_rows, early, late, parts, w_out, rows)
    total[...] = tokens[...].astype(f32) + made
    copy = pltpu.make_async_copy(total, out, sem)
    copy.start()
    copy.wait()


def outward_send(groups, early, late, parts, unit_rows):
    width, depth = groups * unit_rows, parts[0].shape[1]
    return pl.pallas_call(
        functools.partial(send_kernel, groups, unit_rows, len(parts)),
        out_shape=jax.ShapeDtypeStruct((early.shape[0], width), bf16),
        in_specs=[VMEM] * (2 + len(parts)),
        out_specs=VMEM,
        scratch_shapes=[pltpu.VMEM((width, depth), bf16), pltpu.VMEM(early.shape, bf16)],
        compiler_params=PARAMS,
        cost_estimate=reads(2 * width * depth),
        name="outward_send",
    )(early, late, *parts)


def outward_keep(groups, early, late, tokens, gain, parts, unit_rows):
    width, depth = groups * unit_rows, parts[0].shape[1]
    return pl.pallas_call(
        functools.partial(keep_kernel, groups, unit_rows, len(parts)),
        out_shape=(
            pltpu.HBM(tokens.shape, f32),
            jax.ShapeDtypeStruct((1, width), f32),
        ),
        in_specs=[VMEM] * (4 + len(parts)),
        out_specs=(HBM, VMEM),
        scratch_shapes=[
            pltpu.VMEM((width, depth), bf16),
            pltpu.VMEM(early.shape, bf16),
            pltpu.VMEM(tokens.shape, f32),
            pltpu.SemaphoreType.DMA,
        ],
        compiler_params=PARAMS,
        cost_estimate=reads(2 * width * depth),
        name="outward_keep",
    )(early, late, tokens, gain, *parts)


def route_kernel(mine, arrived, gain, place, residual, moe_in, sent, kept, got, sems):
    for copy in fetch([(mine, kept), (arrived, got)], sems):
        copy.wait()
    added = (kept[...] + got[...].astype(f32)).astype(bf16)
    residual[...] = added
    moe_in[...] = normalized(added.astype(f32), gain[...])
    cap = sent.shape[0]
    rows = jnp.dot(place[cap:, :], moe_in[...], preferred_element_type=f32)
    sent[...] = rows.astype(bf16)


def route(mine, arrived, gain, place):
    cap = place.shape[0] // 2
    return pl.pallas_call(
        route_kernel,
        out_shape=(
            jax.ShapeDtypeStruct(mine.shape, bf16),
            jax.ShapeDtypeStruct(mine.shape, bf16),
            jax.ShapeDtypeStruct((cap, mine.shape[1]), bf16),
        ),
        in_specs=[HBM, ANY, VMEM, VMEM],
        out_specs=(VMEM,) * 3,
        scratch_shapes=[
            pltpu.VMEM(mine.shape, f32),
            pltpu.VMEM(mine.shape, bf16),
            pltpu.SemaphoreType.DMA((2,)),
        ],
        compiler_params=PARAMS,
        cost_estimate=takes(2),
        name="route",
    )(pltpu.with_memory_space_constraint(mine, pltpu.HBM), arrived, gain, place)


def gate_kernel(moe_in, router, ids, place, gates, own, spread):
    cap = own.shape[0]
    own[...] = jnp.dot(place[:cap, :], moe_in[...], preferred_element_type=f32).astype(bf16)
    hit = named_experts(ids, router.shape[0])
    tokens = ids.shape[1]
    row = lax.broadcasted_iota(jnp.int32, (tokens, tokens), 0)
    eye = (row == lax.broadcasted_iota(jnp.int32, (tokens, tokens), 1)).astype(f32)
    named = lax.dot_general(eye, hit, LAST_DIMS, preferred_element_type=f32)
    spread[...] = lax.dot_general(
        eye.astype(bf16), place[...], LAST_DIMS, preferred_element_type=f32
    ).astype(bf16)
    logits = lax.dot_general(moe_in[...], router[...], LAST_DIMS, preferred_element_type=f32)
    raised = jnp.where(named > 0, jnp.exp(logits), 0.0)
    gates[...] = raised / jnp.sum(raised, axis=-1, keepdims=True)


def gate(moe_in, router_t, ids_t, place):
    cap = place.shape[0] // 2
    return pl.pallas_call(
        gate_kernel,
        out_shape=(
            jax.ShapeDtypeStruct((moe_in.shape[0], router_t.shape[0]), f32),
            jax.ShapeDtypeStruct((cap, moe_in.shape[1]), bf16),
            jax.ShapeDtypeStruct(place.shape[::-1], bf16),
        ),
        in_specs=[VMEM] * 4,
        out_specs=(VMEM,) * 3,
        compiler_params=PARAMS,
        cost_estimate=LITTLE,
        name="gate",
    )(moe_in, router_t, ids_t, place)


def expert_kernel(groups, up_rows, down_rows, n_parts, own, other, *refs):
    parts = refs[:n_parts]
    own_out, other_out, rows, gate_up, down = refs[n_parts:]
    width = parts[0].shape[1]
    count = own.shape[0]
    rows[:count, :] = own[...]
    rows[count:, :] = other[...]
    pieces = [(i * up_rows, up_rows, gate_up, i * width) for i in range(2)]
    pieces += [
        (2 * up_rows + i * down_rows, down_rows, down, i * width) for i in range(down.shape[1] // width)
    ]
    unit_rows = pieces[-1][0] + down_rows
    place_parts(groups, parts, unit_rows, pieces)
    both = jnp.dot(rows[...], gate_up[...], preferred_element_type=f32)
    gate, up = both[:, :width], both[:, width:]
    hidden = (gate / (1.0 + jnp.exp(-gate)) * up).astype(bf16)
    made = jnp.dot(hidden, down[...], preferred_element_type=f32).astype(bf16)
    own_out[...] = made[:count, :]
    other_out[...] = made[count:, :]


def expert(groups, own, other, parts, up_rows, down_rows):
    count, model = own.shape
    width = parts[0].shape[1]
    return pl.pallas_call(
        functools.partial(expert_kernel, groups, up_rows, down_rows, len(parts)),
        out_shape=(jax.ShapeDtypeStruct(own.shape, bf16),) * 2,
        in_specs=[VMEM] * (2 + len(parts)),
        out_specs=(VMEM, VMEM),
        scratch_shapes=[
            pltpu.VMEM((2 * count, model), bf16),
            pltpu.VMEM((groups * up_rows, 2 * width), bf16),
            pltpu.VMEM((groups * down_rows, model), bf16),
        ],
        compiler_params=PARAMS,
        cost_estimate=takes(1.2),
        name="expert",
    )(own, other, *parts)


def combine_kernel(residual, gates, spread, own, returned, out):
    lane = lax.axis_index("hd")
    count = own.shape[0]
    column = lax.broadcasted_iota(jnp.int32, gates.shape, 1)
    total = jnp.zeros(residual.shape, f32)
    for index, made in ((0, own), (1, returned)):
        live = lane if index == 0 else 1 - lane
        weight = jnp.sum(jnp.where(column == live, gates[...], 0.0), axis=-1, keepdims=True)
        picked = jnp.dot(
            spread[:, index * count : (index + 1) * count], made[...], preferred_element_type=f32
        )
        total += weight * picked
    out[...] = (residual[...].astype(f32) + total).astype(bf16)


def combine(residual, gates, spread, own, returned):
    return pl.pallas_call(
        combine_kernel,
        out_shape=jax.ShapeDtypeStruct(residual.shape, bf16),
        in_specs=[VMEM] * 5,
        out_specs=VMEM,
        compiler_params=PARAMS,
        cost_estimate=reads(6 * residual.shape[0] * residual.shape[1]),
        name="combine",
    )(residual, gates, spread, own, returned)


def bundle_kernel(send, kv, tags, out):
    groups, rows, _ = out.shape
    heads = kv.shape[1] // 128
    capc = send.shape[0] // groups
    packed = jnp.dot(send[...], kv[...], preferred_element_type=f32).astype(bf16)
    tagged = jnp.dot(send[...], tags[...], preferred_element_type=f32)
    one = (lax.broadcasted_iota(jnp.int32, (16, 128), 0) == lax.broadcasted_iota(jnp.int32, (16, 128), 1))
    for owner in range(groups):
        mine = slice(owner * capc, (owner + 1) * capc)
        for head in range(heads):
            out[owner, head * capc : (head + 1) * capc, :] = packed[mine, head * 128 : (head + 1) * 128]
        wide = jnp.concatenate([tagged[mine, :], jnp.zeros((128 - capc, 128), f32)], axis=0)
        out[owner, heads * capc :, :] = lax.dot_general(
            one.astype(f32), wide, LAST_DIMS, preferred_element_type=f32
        ).astype(bf16)


def bundle(groups, send, kv, tags):
    rows = send.shape[0] // groups * (kv.shape[1] // 128) + 16
    return pl.pallas_call(
        bundle_kernel,
        out_shape=jax.ShapeDtypeStruct((groups, rows, 128), bf16),
        in_specs=[VMEM] * 3,
        out_specs=VMEM,
        compiler_params=PARAMS,
        cost_estimate=LITTLE,
        name="bundle",
    )(send, kv, tags)


def write_kernel(heads, arrived, cache, out, rows, wide, known):
    groups, size, _ = arrived.shape
    slots = cache.shape[0] // heads
    capc = (size - 16) // heads
    high, low = [], []
    for source in range(groups):
        for head in range(heads):
            rows[source * capc : (source + 1) * capc, head * 128 : (head + 1) * 128] = arrived[
                source, head * capc : (head + 1) * capc, :
            ]
        numbers = arrived[source, heads * capc :, :].astype(f32)
        high.append(numbers[0:1, :capc])
        low.append(numbers[1:2, :capc])
    slot = jnp.concatenate(high, axis=1) * 64.0 + jnp.concatenate(low, axis=1) - 64.0
    row = lax.broadcasted_iota(jnp.int32, (slots, slot.shape[1]), 0).astype(f32)
    hit = (row == slot).astype(bf16)
    made = jnp.dot(hit, rows[...], preferred_element_type=f32)
    found = jnp.dot(hit, jnp.ones((slot.shape[1], 128), bf16), preferred_element_type=f32)
    for head in range(heads):
        wide[pl.ds(head, slots, heads), :] = made[:, head * 128 : (head + 1) * 128]
        known[pl.ds(head, slots, heads), :] = found
    old = cache[...].astype(f32)
    out[...] = jnp.where(known[...] > 0.0, wide[...], old).astype(bf16)


def write(arrived, cache):
    slots, heads, lanes = cache.shape
    capc = (arrived.shape[1] - 16) // heads
    flat = (slots * heads, lanes)
    written = pl.pallas_call(
        functools.partial(write_kernel, heads),
        out_shape=jax.ShapeDtypeStruct(flat, bf16),
        in_specs=[VMEM] * 2,
        out_specs=VMEM,
        scratch_shapes=[
            pltpu.VMEM((arrived.shape[0] * capc, heads * lanes), bf16),
            pltpu.VMEM(flat, f32),
            pltpu.VMEM(flat, f32),
        ],
        compiler_params=PARAMS,
        cost_estimate=reads(1 << 21),
        name="write",
    )(arrived, cache.reshape(flat))
    return written.reshape(cache.shape)


def two_lane_shards(
    tokens,
    positions,
    attn_gain,
    w_query,
    w_keyval,
    w_out,
    moe_gain,
    router,
    w_gate_up,
    w_down,
    expert_ids,
    cache_slot,
    kv_cache,
):
    groups = lax.axis_size("grp")
    tok_rows, model = tokens.shape
    block = positions.shape[0]
    kv_local, head2 = w_keyval.shape[1:]
    kv_width = kv_local * head2
    slots_dev = kv_cache.shape[0]
    swap = functools.partial(lax.ppermute, axis_name="hd", perm=[(0, 1), (1, 0)])

    together = lax.optimization_barrier

    other_tokens = swap(tokens)
    own = (w_gate_up[0], w_down[0], w_out.T)
    up_rows, down_rows = own[0].shape[0], own[1].shape[0]
    beside = [lax.ppermute(part, "grp", sibling_pairs(groups)) for part in own]
    expert_pair, out_pair = pack(own, beside)
    out_ring = Ring(out_pair, groups)
    out_ring.step()
    expert_ring = Ring(expert_pair, groups)
    expert_ring.step()
    w_keyval, positions = together((w_keyval, positions, out_pair))[:2]
    flat_kv = w_keyval.reshape(model, kv_width)
    cosine, sine, past, place, send, tags, gain = prepare(
        groups, slots_dev, positions, cache_slot, expert_ids, attn_gain
    )
    other_tokens, cosine, flat_kv = out_ring.pin(other_tokens, cosine, flat_kv)
    out_ring.step()

    q, kv, tail = project(tokens, other_tokens, gain, cosine, sine, w_query, flat_kv)
    seam = lax.ppermute(tail, "grp", [(g, g + 1) for g in range(groups - 1)])
    q = out_ring.pin(q)
    out_ring.step()
    out_ring.share(2)
    late = attend_late(q, kv, past)
    seam, late = together((seam, late))
    seam = expert_ring.pin(seam)
    expert_ring.step()
    early = attend_early(q, kv, seam, past)
    early, out_ring.near = together((early, out_ring.near))
    early = out_ring.pin(early)
    out_ring.step()
    out_ring.share(3)
    early, out_ring.near = together((early, out_ring.near))
    early = out_ring.pin(early)
    early = expert_ring.pin(early)
    expert_ring.step()
    out_ring.share()
    sent = outward_send(groups, early, late, out_ring.parts(), out_ring.unit_rows)
    arrived = swap(sent)
    early = together((early, sent))[0]
    mine, late_gain = outward_keep(
        groups, early, late, tokens, moe_gain, out_ring.parts(), out_ring.unit_rows
    )
    kv, late_gain = expert_ring.pin(kv, late_gain)
    expert_ring.share()
    expert_ring.step()
    outgoing = bundle(groups, send, kv, tags)
    arrived_cache = lax.all_to_all(outgoing, "grp", split_axis=0, concat_axis=0, tiled=True)
    arrived, late_gain, outgoing = expert_ring.pin(arrived, late_gain, outgoing)
    expert_ring.share()

    residual, moe_in, sent_rows = route(mine, arrived, late_gain, place)
    landed = swap(sent_rows)
    gates, own_rows, spread = gate(moe_in, router.T, expert_ids.T, place)
    landed, own_rows = together((landed, own_rows))
    own_made, back = expert(
        groups, own_rows, landed, expert_ring.parts(), up_rows, down_rows
    )
    returned = swap(back)
    layer_out = combine(residual, gates, spread, own_made, returned)
    layer_out, arrived_cache = together((layer_out, arrived_cache))
    cache_after = write(arrived_cache, kv_cache)
    return (layer_out, cache_after)


def passed_along(value, axis, steps):
    count = lax.axis_size(axis)
    initial, last = (max(0, -steps), min(count, count - steps))
    return lax.ppermute(value, axis, [(source, source + steps) for source in range(initial, last)])


def rms_norm(row_set, norm_gain):
    floats = row_set.astype(jnp.float32)
    factor = lax.rsqrt(jnp.mean(floats * floats, axis=-1, keepdims=True) + norm_eps)
    return (floats * factor * norm_gain).astype(jnp.bfloat16)


def rotate(vectors, angle_pos):
    halves = vectors.shape[-1] // 2
    inverse_freq = rope_base ** (-2.0 * jnp.arange(halves, dtype=jnp.float32) / vectors.shape[-1])
    angles = angle_pos[:, None, None] * inverse_freq[None, None, :]
    cosine = jnp.cos(angles)
    sine_part = jnp.sin(angles)
    first_half = vectors[..., :halves]
    second_half = vectors[..., halves:]
    return jnp.concatenate(
        [
            first_half * cosine - second_half * sine_part,
            second_half * cosine + first_half * sine_part,
        ],
        axis=-1,
    )


def expert_rows(row_set, gate_up, down_rows):
    gate_and_up = jnp.dot(row_set, gate_up, preferred_element_type=jnp.float32)
    inner_width = gate_and_up.shape[1] // 2
    hidden = (jax.nn.silu(gate_and_up[:, :inner_width]) * gate_and_up[:, inner_width:]).astype(
        jnp.bfloat16
    )
    return jnp.dot(hidden, down_rows, preferred_element_type=jnp.float32).astype(jnp.bfloat16)


def attend_rows(query_blk, keys_blk, vals_blk, visible, scale_qk):
    scores = (
        jnp.einsum("qkgd,skd->kgqs", query_blk, keys_blk, preferred_element_type=jnp.float32)
        * scale_qk
    )
    weights_f = jnp.where(visible[None, None], jnp.exp(scores), 0.0)
    prob_bf = (weights_f / jnp.sum(weights_f, axis=-1, keepdims=True)).astype(jnp.bfloat16)
    return jnp.einsum("kgqs,skd->qkgd", prob_bf, vals_blk, preferred_element_type=jnp.float32)


def shards(
    tokens,
    positions,
    attn_gain,
    w_query,
    w_keyval,
    w_out,
    moe_gain,
    router,
    w_gate_up,
    w_down,
    expert_ids,
    cache_slot,
    kv_cache,
):
    lane_count = lax.axis_size("hd")
    group_count = lax.axis_size("grp")
    tok_rows = tokens.shape[0]
    model_width = tokens.shape[1]
    block_len = positions.shape[0]
    seg_most = block_len // 2
    head_dim = w_keyval.shape[2] // 2
    kv_local = w_keyval.shape[1]
    q_local = w_query.shape[1] // head_dim
    per_kv = q_local // kv_local
    expert_cap = tok_rows // 4
    normed = rms_norm(tokens, attn_gain)
    flat_kv = w_keyval.reshape(model_width, kv_local * 2 * head_dim)
    section = lax.all_gather(normed, "hd", axis=0, tiled=True)
    projected = jnp.concatenate(
        [
            jnp.dot(section, w_query, preferred_element_type=jnp.float32),
            jnp.dot(section, flat_kv, preferred_element_type=jnp.float32),
        ],
        axis=1,
    )
    angle_pos = jnp.maximum(positions, 0).astype(jnp.float32)
    queries = rotate(
        projected[:, : q_local * head_dim].reshape(block_len, q_local, head_dim), angle_pos
    ).astype(jnp.bfloat16)
    key_val = projected[:, q_local * head_dim :].reshape(block_len, kv_local, 2 * head_dim)
    rotated = rotate(key_val[:, :, :head_dim], angle_pos).astype(jnp.bfloat16)
    stored = jnp.concatenate([rotated, key_val[:, :, head_dim:].astype(jnp.bfloat16)], axis=2)
    seam_rows = passed_along(stored[block_len - seg_most :], "grp", 1)
    window = jnp.concatenate([seam_rows, stored], axis=0)
    scale_qk = head_dim ** (-0.5)
    local_rows = jnp.arange(block_len, dtype=jnp.int32)
    lowest = local_rows - jnp.maximum(positions, 0)
    pieces_out = []
    for q_block in range(2):
        first_row = q_block * seg_most
        rows_here = first_row + jnp.arange(seg_most, dtype=jnp.int32)
        cols_here = first_row - seg_most + jnp.arange(2 * seg_most, dtype=jnp.int32)
        low_here = lowest[first_row : first_row + seg_most]
        visible = (cols_here[None, :] >= low_here[:, None]) & (
            cols_here[None, :] <= rows_here[:, None]
        )
        query_blk = queries[first_row : first_row + seg_most].reshape(
            seg_most, kv_local, per_kv, head_dim
        )
        keys_blk = window[first_row : first_row + 2 * seg_most, :, :head_dim]
        vals_blk = window[first_row : first_row + 2 * seg_most, :, head_dim:]
        mixed_rows = attend_rows(query_blk, keys_blk, vals_blk, visible, scale_qk)
        pieces_out.append(mixed_rows.reshape(seg_most, q_local * head_dim).astype(jnp.bfloat16))
    attended = jnp.concatenate(pieces_out, axis=0)
    slots_dev = kv_cache.shape[0]
    capc = 2 * block_len // group_count
    live_slot = cache_slot >= 0
    owners = jnp.where(live_slot, cache_slot // slots_dev, group_count)
    owner_hit = (owners[:, None] == jnp.arange(group_count, dtype=jnp.int32)[None, :]).astype(
        jnp.bfloat16
    )
    lower_tri = (local_rows[:, None] >= local_rows[None, :]).astype(jnp.bfloat16)
    running = jnp.dot(lower_tri, owner_hit, preferred_element_type=jnp.float32)
    owner_rank = jnp.sum(running * owner_hit.astype(jnp.float32), axis=1).astype(jnp.int32) - 1
    send_rows = jnp.where(live_slot, owners * capc + owner_rank, group_count * capc)
    outgoing_cache = (
        jnp.zeros((group_count * capc, kv_local, 2 * head_dim), jnp.bfloat16)
        .at[send_rows]
        .set(stored, mode="drop")
    )
    outgoing_slots = (
        jnp.full((group_count * capc,), -1, jnp.int32)
        .at[send_rows]
        .set(cache_slot % slots_dev, mode="drop")
    )
    arrived, arrived_slots = (
        lax.all_to_all(
            outgoing_cache.reshape(group_count, capc, kv_local, 2 * head_dim),
            "grp",
            split_axis=0,
            concat_axis=0,
            tiled=True,
        ),
        lax.all_to_all(
            outgoing_slots.reshape(group_count, capc),
            "grp",
            split_axis=0,
            concat_axis=0,
            tiled=True,
        ),
    )
    flat_slots = arrived_slots.reshape(group_count * capc)
    write_rows = jnp.where(flat_slots >= 0, flat_slots, slots_dev).astype(jnp.int32)
    cache_after = kv_cache.at[write_rows].set(
        arrived.reshape(group_count * capc, kv_local, 2 * head_dim), mode="drop"
    )
    by_token = lax.all_to_all(attended, "hd", split_axis=0, concat_axis=1, tiled=True)
    attn_proj = jnp.dot(
        by_token,
        lax.all_gather(w_out, "grp", axis=1, tiled=True),
        preferred_element_type=jnp.float32,
    )
    residual = (tokens.astype(jnp.float32) + attn_proj).astype(jnp.bfloat16)
    moe_in = rms_norm(residual, moe_gain)
    logits = jnp.dot(moe_in, router, preferred_element_type=jnp.float32)
    expert_range = jnp.arange(router.shape[1], dtype=jnp.int32)
    matches_all = expert_ids[:, :, None] == expert_range[None, None, :]
    chosen = jnp.sum(jnp.where(matches_all, logits[:, None, :], 0.0), axis=2)
    raised = jnp.exp(chosen)
    gates = raised / jnp.sum(raised, axis=1, keepdims=True)
    live_range = jnp.arange(lane_count, dtype=jnp.int32)
    matches = expert_ids[:, :, None] == live_range[None, None, :]
    member = jnp.any(matches, axis=1)
    weighting = jnp.sum(jnp.where(matches, gates[:, :, None], 0.0), axis=1)
    ranking = jnp.cumsum(member.astype(jnp.int32), axis=0) - 1
    target = jnp.where(member, live_range[None, :] * expert_cap + ranking, -1)
    slot_range = jnp.arange(lane_count * expert_cap, dtype=jnp.int32)
    slot_hits = target[None, :, :] == slot_range[:, None, None]
    placing = jnp.any(slot_hits, axis=2).astype(jnp.bfloat16)
    outgoing = (
        jnp.dot(placing, moe_in, preferred_element_type=jnp.float32)
        .astype(jnp.bfloat16)
        .reshape(lane_count, expert_cap, model_width)
    )
    gate_up_all, down_all = (
        lax.all_gather(w_gate_up, "grp", axis=1, tiled=True),
        lax.all_gather(w_down, "grp", axis=1, tiled=True),
    )
    gate_up_mat = gate_up_all[0]
    down_mat = down_all[0]
    landed = lax.all_to_all(outgoing, "hd", split_axis=0, concat_axis=0, tiled=True)
    results = expert_rows(landed.reshape(-1, model_width), gate_up_mat, down_mat).reshape(landed.shape)
    returned = lax.all_to_all(results, "hd", split_axis=0, concat_axis=0, tiled=True)
    flat_returned = returned.reshape(-1, model_width)
    fetched = flat_returned[jnp.maximum(target, 0)]
    used_weight = jnp.where(member, weighting, 0.0)
    moe_total = jnp.sum(used_weight[:, :, None] * fetched.astype(jnp.float32), axis=1)
    layer_out = (residual.astype(jnp.float32) + moe_total).astype(jnp.bfloat16)
    return (layer_out, cache_after)


def solution(mesh):
    two_lanes = mesh.shape["hd"] == 2 and mesh.shape["grp"] % 8 == 0
    return jax.shard_map(
        two_lane_shards if two_lanes else shards,
        mesh=mesh,
        in_specs=(
            P(("grp", "hd"), None),
            P("grp"),
            P(),
            P(None, "hd"),
            P(None, "hd", None),
            P(None, "grp"),
            P(),
            P(),
            P("hd", "grp", None),
            P("hd", "grp", None),
            P(("grp", "hd"), None),
            P("grp"),
            P("grp", "hd", None),
        ),
        out_specs=(P(("grp", "hd"), None), P("grp", "hd", None)),
        check_vma=False,
    )
```

```python
import functools

import jax
import jax.numpy as jnp
import numpy as np
from jax import lax
from jax.experimental import pallas as pl
from jax.experimental.pallas import tpu as pltpu
from jax.sharding import PartitionSpec as P

norm_eps = 1e-05
rope_base = 10000.0
bf16 = jnp.bfloat16
f32 = jnp.float32
LAST_DIMS = (((1,), (1,)), ((), ()))


def ring_cycle(groups):
    rows = groups // 4
    return [2 * r for r in range(rows)] + [2 * r + 1 for r in reversed(range(rows))]


def ring_pairs(groups):
    cycle = ring_cycle(groups)
    count = len(cycle)
    pairs = []
    for place, pair in enumerate(cycle):
        pairs.append((2 * pair, 2 * cycle[(place + 1) % count]))
        pairs.append((2 * pair + 1, 2 * cycle[(place - 1) % count] + 1))
    return pairs


def sibling_pairs(groups):
    return [(g, g ^ 1) for g in range(groups)]


def ring_sources(groups, me):
    count = groups // 2
    rows = count // 2
    side, pair = me % 2, me // 2
    row, col = pair // 2, pair % 2
    place = jnp.where(col == 0, row, count - 1 - row)

    def block(core, steps):
        there = (place + (2 * core - 1) * steps + count) % count
        other = jnp.where(there < rows, 2 * there, 2 * (count - 1 - there) + 1)
        return [2 * other + core, 2 * other + 1 - core]

    full = (count - 1) // 2
    listed = [me, me + 1 - 2 * side]
    for core in (side, 1 - side):
        for steps in range(1, full + 1):
            listed += block(core, steps)
    return listed + [block(side, count // 2)[0], block(1 - side, count // 2)[0]]


class Ring:
    def __init__(self, pair, groups):
        self.across = functools.partial(lax.ppermute, axis_name="grp", perm=ring_pairs(groups))
        self.beside = functools.partial(lax.ppermute, axis_name="grp", perm=sibling_pairs(groups))
        self.full = (groups // 2 - 1) // 2
        self.unit_rows = pair.shape[0] // 2
        self.mine = [pair]
        self.near = []

    def step(self):
        held = self.mine[-1]
        if len(self.mine) > self.full:
            held = held[: self.unit_rows]
        self.mine.append(self.across(held))

    def pin(self, *others):
        done = lax.optimization_barrier((self.mine[-1],) + others)
        self.mine[-1] = done[0]
        return done[1:] if len(others) > 1 else done[1]

    def share(self, upto=None):
        for index in range(1 + len(self.near), 1 + (upto or len(self.mine) - 1)):
            self.near.append(self.beside(self.mine[index]))

    def parts(self):
        full = self.full
        return self.mine[: full + 1] + self.near[:full] + [self.mine[full + 1], self.near[full]]


def place_parts(groups, parts, unit_rows, pieces):
    sources = ring_sources(groups, lax.axis_index("grp"))
    shard = 0
    for part in parts:
        for unit in range(part.shape[0] // unit_rows):
            for first, rows, target, lane in pieces:
                at = pl.multiple_of(sources[shard] * rows, rows)
                start = unit * unit_rows + first
                target[pl.ds(at, rows), lane : lane + part.shape[1]] = part[start : start + rows, :]
            shard += 1


VMEM = pl.BlockSpec(memory_space=pltpu.VMEM)
ANY = pl.BlockSpec(memory_space=pl.ANY)
HBM = pl.BlockSpec(memory_space=pltpu.HBM)
PARAMS = pltpu.CompilerParams(vmem_limit_bytes=16 << 20)


LITTLE = pl.CostEstimate(flops=1, bytes_accessed=1, transcendentals=0)


def takes(us):
    return pl.CostEstimate(
        flops=int(us * 1.15e9), bytes_accessed=int(us * 8e6), transcendentals=0
    )


def reads(nbytes):
    return pl.CostEstimate(flops=1, bytes_accessed=nbytes, transcendentals=0)


def normalized(floats, gain):
    factor = lax.rsqrt(jnp.mean(floats * floats, axis=-1, keepdims=True) + norm_eps)
    return (floats * factor * gain).astype(bf16)


def fetch(pairs, sems):
    copies = []
    for index, (source, target) in enumerate(pairs):
        copies.append(pltpu.make_async_copy(source, target, sems.at[index]))
        copies[-1].start()
    return copies


def pack_kernel(*refs):
    sources, (expert_pair, out_pair, sems) = refs[:6], refs[6:]
    width = expert_pair.shape[1]
    lane = lax.axis_index("hd")
    first = pl.multiple_of(lane * out_pair.shape[1], out_pair.shape[1])
    pairs = []
    row = 0
    for index in range(2):
        up, down, w_out = sources[3 * index : 3 * index + 3]
        count = w_out.shape[0]
        pairs.append(
            (w_out.at[:, pl.ds(first, out_pair.shape[1])], out_pair.at[pl.ds(index * count, count), :])
        )
        for source in (up, down):
            for at in range(0, source.shape[1], width):
                pairs.append(
                    (source.at[:, pl.ds(at, width)], expert_pair.at[pl.ds(row, source.shape[0]), :])
                )
                row += source.shape[0]
    for copy in fetch(pairs, sems):
        copy.wait()


def pack(own, beside):
    own = [pltpu.with_memory_space_constraint(part, pltpu.HBM) for part in own]
    up, down, w_out_t = own
    width = up.shape[1] // 2
    pieces = [up.shape[1] // width, down.shape[1] // width]
    unit_rows = pieces[0] * up.shape[0] + pieces[1] * down.shape[0]
    return pl.pallas_call(
        pack_kernel,
        out_shape=(
            jax.ShapeDtypeStruct((2 * unit_rows, width), bf16),
            jax.ShapeDtypeStruct((2 * w_out_t.shape[0], w_out_t.shape[1] // 2), bf16),
        ),
        in_specs=[ANY] * 6,
        out_specs=(ANY, ANY),
        scratch_shapes=[pltpu.SemaphoreType.DMA((2 + 2 * sum(pieces),))],
        compiler_params=PARAMS,
        cost_estimate=LITTLE,
        name="pack",
    )(*own, *beside)


def as_column(row, eye):
    return jnp.sum(jnp.where(eye, row, 0.0), axis=1, keepdims=True)


def named_experts(ids, experts):
    tokens = ids.shape[1]
    expert = lax.broadcasted_iota(jnp.int32, (experts, tokens), 0)
    hit = jnp.zeros((experts, tokens), f32)
    for index in range(ids.shape[0]):
        hit = jnp.where(ids[index : index + 1, :] == expert, 1.0, hit)
    return hit


def prepare_kernel(groups, slots_dev, *refs):
    sources, (cosine, sine, past, place, send, tags, gain) = refs[:4], refs[4:11]
    positions, slots, ids, flat_gain, sems = refs[11:]
    copies = fetch(list(zip(sources, (positions, slots, ids, flat_gain))), sems)
    for copy in copies:
        copy.wait()
    gain[...] = flat_gain[...].reshape(gain.shape)
    lane = lax.axis_index("hd")
    block = positions.shape[1]

    def iota(shape, dim):
        return lax.broadcasted_iota(jnp.int32, shape, dim)

    eye = iota((block, block), 0) == iota((block, block), 1)
    reach = as_column(jnp.maximum(positions[...], 0).astype(f32), eye)
    past[...] = jnp.broadcast_to(reach, past.shape)
    column = iota((8, 128), 1)
    exponent = (column % 32).astype(f32) * (-2.0 / 64)
    inverse_freq = jnp.exp(exponent * np.float32(np.log(rope_base)))[:1, :]
    angles = reach * inverse_freq
    cosine[...] = jnp.cos(angles)
    turned = jnp.sin(angles)
    sine[...] = jnp.where(iota(angles.shape, 1) % 64 < 32, -turned, turned)

    tokens = ids.shape[1]
    cap = place.shape[0] // 2
    hit = named_experts(ids, 8)
    upto = (iota((tokens, tokens), 0) <= iota((tokens, tokens), 1)).astype(f32)
    rank = jnp.dot(hit, upto, preferred_element_type=f32) - 1.0
    slot = iota((2 * cap, tokens), 0).astype(f32)
    placed = jnp.zeros((2 * cap, tokens), f32)
    for live in range(2):
        order = jnp.where(lane == live, 0, cap).astype(f32)
        member = hit[live : live + 1, :] > 0.0
        placed = jnp.where(member & (slot == rank[live : live + 1, :] + order), 1.0, placed)
    place[...] = placed.astype(bf16)

    where = slots[...]
    owner = jnp.where(where >= 0, where // slots_dev, -1)
    owner_hit = (iota((groups, block), 0) == owner).astype(f32)
    before = (iota((block, block), 0) <= iota((block, block), 1)).astype(f32)
    running = jnp.dot(owner_hit, before, preferred_element_type=f32)
    owner_rank = jnp.sum(owner_hit * running, axis=0, keepdims=True) - 1.0
    capc = send.shape[0] // groups
    row = jnp.where(owner >= 0, owner * capc + owner_rank.astype(jnp.int32), -1)
    send[...] = (iota(send.shape, 0) == row).astype(bf16)
    inside = jnp.where(where >= 0, where % slots_dev, 0)
    high = as_column((inside // 64 + 1).astype(f32), eye)
    low = as_column((inside % 64).astype(f32), eye)
    spot = iota(tags.shape, 1)
    tags[...] = jnp.where(spot == 0, high, jnp.where(spot == 1, low, 0.0)).astype(bf16)


def prepare(groups, slots_dev, positions, slots, ids, gain):
    block, tokens = positions.shape[0], ids.shape[0]
    model = gain.shape[0]
    cap = tokens // 4
    capc = 2 * block // groups
    shapes = [
        ((block, 128), f32),
        ((block, 128), f32),
        ((block, 128), f32),
        ((2 * cap, tokens), bf16),
        ((groups * capc, block), bf16),
        ((block, 128), bf16),
        ((1, model), f32),
    ]
    sources = (positions[None], slots[None], ids.T, gain)
    return pl.pallas_call(
        functools.partial(prepare_kernel, groups, slots_dev),
        out_shape=tuple(jax.ShapeDtypeStruct(shape, kind) for shape, kind in shapes),
        in_specs=[ANY] * 4,
        out_specs=(VMEM,) * len(shapes),
        scratch_shapes=[
            pltpu.VMEM((1, block), jnp.int32),
            pltpu.VMEM((1, block), jnp.int32),
            pltpu.VMEM(ids.shape[::-1], jnp.int32),
            pltpu.VMEM((model,), f32),
            pltpu.SemaphoreType.DMA((4,)),
        ],
        compiler_params=PARAMS,
        cost_estimate=LITTLE,
        name="prepare",
    )(*[pltpu.with_memory_space_constraint(source, pltpu.HBM) for source in sources])


def project_kernel(
    own, other, gain, cosine, sine, w_query, w_keyval, q_out, kv_out, seam_out, raw, rows, sems
):
    count = own.shape[0]
    lane = lax.axis_index("hd")
    mine = pl.multiple_of(lane * count, count)
    theirs = pl.multiple_of((1 - lane) * count, count)
    copies = fetch([(own, raw.at[0]), (other, raw.at[1])], sems)
    cos_q, sin_q = cosine[...], sine[...]
    column = lax.broadcasted_iota(jnp.int32, cos_q.shape, 1)
    lower = column % 64 < 32
    cos_kv = jnp.where(column < 64, cos_q, 1.0)
    sin_kv = jnp.where(column < 64, sin_q, 0.0)
    for index, first in ((0, mine), (1, theirs)):
        copies[index].wait()
        rows[pl.ds(first, count), :] = normalized(raw[index].astype(f32), gain[...])
    width = 256
    for weights, out, cos, sin in ((w_keyval, kv_out, cos_kv, sin_kv), (w_query, q_out, cos_q, sin_q)):
        for first in range(0, weights.shape[1], width):
            made = jnp.dot(rows[...], weights[:, first : first + width], preferred_element_type=f32)
            for part in range(0, width, 128):
                here = made[:, part : part + 128]
                turned = jnp.where(lower, pltpu.roll(here, 96, 1), pltpu.roll(here, 32, 1))
                done = (here * cos + turned * sin).astype(bf16)
                out[:, first + part : first + part + 128] = done
                if out is kv_out:
                    seam_out[:, first + part : first + part + 128] = done[count:, :]


def project(own, other, gain, cosine, sine, w_query, flat_kv):
    count, width = own.shape
    made = w_query.shape[1] + flat_kv.shape[1]
    return pl.pallas_call(
        project_kernel,
        out_shape=(
            jax.ShapeDtypeStruct((2 * count, w_query.shape[1]), bf16),
            jax.ShapeDtypeStruct((2 * count, flat_kv.shape[1]), bf16),
            jax.ShapeDtypeStruct((count, flat_kv.shape[1]), bf16),
        ),
        in_specs=[ANY] * 2 + [VMEM] * 5,
        out_specs=(VMEM, VMEM, VMEM),
        scratch_shapes=[
            pltpu.VMEM((2, count, width), bf16),
            pltpu.VMEM((2 * count, width), bf16),
            pltpu.SemaphoreType.DMA((2,)),
        ],
        compiler_params=PARAMS,
        cost_estimate=takes(8),
        name="project",
    )(own, other, gain, cosine, sine, w_query, flat_kv)


def attend_rows_kernel(first, q, kv, seam, past, mixed, window, sem):
    count = q.shape[0] // 2
    if first == 0:
        copy = pltpu.make_async_copy(seam, window.at[pl.ds(0, count), :], sem)
        copy.start()
        window[count:, :] = kv[:count, :]
        copy.wait()
        keyed = window
    else:
        keyed = kv
    head = 64
    kv_heads = kv.shape[1] // (2 * head)
    per_kv = q.shape[1] // head // kv_heads
    shape = (count, 2 * count)
    row = lax.broadcasted_iota(jnp.int32, shape, 0) + count
    col = lax.broadcasted_iota(jnp.int32, shape, 1)
    reach = past[first : first + count, :1].astype(jnp.int32)
    visible = (col <= row) & (col >= row - reach)
    for kv_head in range(kv_heads):
        lanes = 2 * head * kv_head
        keys = keyed[:, lanes : lanes + head]
        values = keyed[:, lanes + head : lanes + 2 * head]
        for index in range(per_kv):
            at = (kv_head * per_kv + index) * head
            query = q[first : first + count, at : at + head]
            scores = lax.dot_general(query, keys, LAST_DIMS, preferred_element_type=f32)
            raised = jnp.where(visible, jnp.exp(scores * head ** (-0.5)), 0.0)
            probs = (raised / jnp.sum(raised, axis=-1, keepdims=True)).astype(bf16)
            made = jnp.dot(probs, values, preferred_element_type=f32)
            mixed[:, at : at + head] = made.astype(bf16)


def attend_late(q, kv, past):
    def kernel(q, kv, past, mixed):
        attend_rows_kernel(q.shape[0] // 2, q, kv, None, past, mixed, None, None)

    return pl.pallas_call(
        kernel,
        out_shape=jax.ShapeDtypeStruct((q.shape[0] // 2, q.shape[1]), bf16),
        in_specs=[VMEM] * 3,
        out_specs=VMEM,
        compiler_params=PARAMS,
        cost_estimate=takes(2),
        name="attend_late",
    )(q, kv, past)


def attend_early(q, kv, seam, past):
    return pl.pallas_call(
        functools.partial(attend_rows_kernel, 0),
        out_shape=jax.ShapeDtypeStruct((q.shape[0] // 2, q.shape[1]), bf16),
        in_specs=[VMEM, VMEM, ANY, VMEM],
        out_specs=VMEM,
        scratch_shapes=[pltpu.VMEM(kv.shape, bf16), pltpu.SemaphoreType.DMA],
        compiler_params=PARAMS,
        cost_estimate=takes(2),
        name="attend_early",
    )(q, kv, seam, past)


def outward_rows(flip, groups, unit_rows, early, late, parts, w_out, rows):
    place_parts(groups, parts, unit_rows, [(0, unit_rows, w_out, 0)])
    lane = lax.axis_index("hd")
    which = (1 - lane) if flip else lane

    @pl.when(which == 0)
    def _():
        rows[...] = early[...]

    @pl.when(which != 0)
    def _():
        rows[...] = late[...]

    return lax.dot_general(rows[...], w_out[...], LAST_DIMS, preferred_element_type=f32)


def send_kernel(groups, unit_rows, n_parts, early, late, *refs):
    parts, (out, w_out, rows) = refs[:n_parts], refs[n_parts:]
    out[...] = outward_rows(True, groups, unit_rows, early, late, parts, w_out, rows).astype(bf16)


def keep_kernel(groups, unit_rows, n_parts, early, late, tokens, flat_gain, *refs):
    parts, (out, gain, w_out, rows, total, sem) = refs[:n_parts], refs[n_parts:]
    gain[...] = flat_gain[...].reshape(gain.shape)
    made = outward_rows(False, groups, unit_rows, early, late, parts, w_out, rows)
    total[...] = tokens[...].astype(f32) + made
    copy = pltpu.make_async_copy(total, out, sem)
    copy.start()
    copy.wait()


def outward_send(groups, early, late, parts, unit_rows):
    width, depth = groups * unit_rows, parts[0].shape[1]
    return pl.pallas_call(
        functools.partial(send_kernel, groups, unit_rows, len(parts)),
        out_shape=jax.ShapeDtypeStruct((early.shape[0], width), bf16),
        in_specs=[VMEM] * (2 + len(parts)),
        out_specs=VMEM,
        scratch_shapes=[pltpu.VMEM((width, depth), bf16), pltpu.VMEM(early.shape, bf16)],
        compiler_params=PARAMS,
        cost_estimate=reads(2 * width * depth),
        name="outward_send",
    )(early, late, *parts)


def outward_keep(groups, early, late, tokens, gain, parts, unit_rows):
    width, depth = groups * unit_rows, parts[0].shape[1]
    return pl.pallas_call(
        functools.partial(keep_kernel, groups, unit_rows, len(parts)),
        out_shape=(
            pltpu.HBM(tokens.shape, f32),
            jax.ShapeDtypeStruct((1, width), f32),
        ),
        in_specs=[VMEM] * (4 + len(parts)),
        out_specs=(HBM, VMEM),
        scratch_shapes=[
            pltpu.VMEM((width, depth), bf16),
            pltpu.VMEM(early.shape, bf16),
            pltpu.VMEM(tokens.shape, f32),
            pltpu.SemaphoreType.DMA,
        ],
        compiler_params=PARAMS,
        cost_estimate=reads(2 * width * depth),
        name="outward_keep",
    )(early, late, tokens, gain, *parts)


def route_kernel(mine, arrived, gain, place, residual, moe_in, sent, kept, got, sems):
    for copy in fetch([(mine, kept), (arrived, got)], sems):
        copy.wait()
    added = (kept[...] + got[...].astype(f32)).astype(bf16)
    residual[...] = added
    moe_in[...] = normalized(added.astype(f32), gain[...])
    cap = sent.shape[0]
    rows = jnp.dot(place[cap:, :], moe_in[...], preferred_element_type=f32)
    sent[...] = rows.astype(bf16)


def route(mine, arrived, gain, place):
    cap = place.shape[0] // 2
    return pl.pallas_call(
        route_kernel,
        out_shape=(
            jax.ShapeDtypeStruct(mine.shape, bf16),
            jax.ShapeDtypeStruct(mine.shape, bf16),
            jax.ShapeDtypeStruct((cap, mine.shape[1]), bf16),
        ),
        in_specs=[HBM, ANY, VMEM, VMEM],
        out_specs=(VMEM,) * 3,
        scratch_shapes=[
            pltpu.VMEM(mine.shape, f32),
            pltpu.VMEM(mine.shape, bf16),
            pltpu.SemaphoreType.DMA((2,)),
        ],
        compiler_params=PARAMS,
        cost_estimate=takes(2),
        name="route",
    )(pltpu.with_memory_space_constraint(mine, pltpu.HBM), arrived, gain, place)


def gate_kernel(moe_in, router, ids, place, gates, own, spread):
    cap = own.shape[0]
    own[...] = jnp.dot(place[:cap, :], moe_in[...], preferred_element_type=f32).astype(bf16)
    hit = named_experts(ids, router.shape[0])
    tokens = ids.shape[1]
    row = lax.broadcasted_iota(jnp.int32, (tokens, tokens), 0)
    eye = (row == lax.broadcasted_iota(jnp.int32, (tokens, tokens), 1)).astype(f32)
    named = lax.dot_general(eye, hit, LAST_DIMS, preferred_element_type=f32)
    spread[...] = lax.dot_general(
        eye.astype(bf16), place[...], LAST_DIMS, preferred_element_type=f32
    ).astype(bf16)
    logits = lax.dot_general(moe_in[...], router[...], LAST_DIMS, preferred_element_type=f32)
    raised = jnp.where(named > 0, jnp.exp(logits), 0.0)
    gates[...] = raised / jnp.sum(raised, axis=-1, keepdims=True)


def gate(moe_in, router_t, ids_t, place):
    cap = place.shape[0] // 2
    return pl.pallas_call(
        gate_kernel,
        out_shape=(
            jax.ShapeDtypeStruct((moe_in.shape[0], router_t.shape[0]), f32),
            jax.ShapeDtypeStruct((cap, moe_in.shape[1]), bf16),
            jax.ShapeDtypeStruct(place.shape[::-1], bf16),
        ),
        in_specs=[VMEM] * 4,
        out_specs=(VMEM,) * 3,
        compiler_params=PARAMS,
        cost_estimate=LITTLE,
        name="gate",
    )(moe_in, router_t, ids_t, place)


def expert_kernel(groups, up_rows, down_rows, n_parts, own, other, *refs):
    parts = refs[:n_parts]
    own_out, other_out, rows, gate_up, down = refs[n_parts:]
    width = parts[0].shape[1]
    count = own.shape[0]
    rows[:count, :] = own[...]
    rows[count:, :] = other[...]
    pieces = [(i * up_rows, up_rows, gate_up, i * width) for i in range(2)]
    pieces += [
        (2 * up_rows + i * down_rows, down_rows, down, i * width) for i in range(down.shape[1] // width)
    ]
    unit_rows = pieces[-1][0] + down_rows
    place_parts(groups, parts, unit_rows, pieces)
    both = jnp.dot(rows[...], gate_up[...], preferred_element_type=f32)
    gate, up = both[:, :width], both[:, width:]
    hidden = (gate / (1.0 + jnp.exp(-gate)) * up).astype(bf16)
    made = jnp.dot(hidden, down[...], preferred_element_type=f32).astype(bf16)
    own_out[...] = made[:count, :]
    other_out[...] = made[count:, :]


def expert(groups, own, other, parts, up_rows, down_rows):
    count, model = own.shape
    width = parts[0].shape[1]
    return pl.pallas_call(
        functools.partial(expert_kernel, groups, up_rows, down_rows, len(parts)),
        out_shape=(jax.ShapeDtypeStruct(own.shape, bf16),) * 2,
        in_specs=[VMEM] * (2 + len(parts)),
        out_specs=(VMEM, VMEM),
        scratch_shapes=[
            pltpu.VMEM((2 * count, model), bf16),
            pltpu.VMEM((groups * up_rows, 2 * width), bf16),
            pltpu.VMEM((groups * down_rows, model), bf16),
        ],
        compiler_params=PARAMS,
        cost_estimate=takes(4.2),
        name="expert",
    )(own, other, *parts)


def combine_kernel(residual, gates, spread, own, returned, out):
    lane = lax.axis_index("hd")
    count = own.shape[0]
    column = lax.broadcasted_iota(jnp.int32, gates.shape, 1)
    total = jnp.zeros(residual.shape, f32)
    for index, made in ((0, own), (1, returned)):
        live = lane if index == 0 else 1 - lane
        weight = jnp.sum(jnp.where(column == live, gates[...], 0.0), axis=-1, keepdims=True)
        picked = jnp.dot(
            spread[:, index * count : (index + 1) * count], made[...], preferred_element_type=f32
        )
        total += weight * picked
    out[...] = (residual[...].astype(f32) + total).astype(bf16)


def combine(residual, gates, spread, own, returned):
    return pl.pallas_call(
        combine_kernel,
        out_shape=jax.ShapeDtypeStruct(residual.shape, bf16),
        in_specs=[VMEM] * 5,
        out_specs=VMEM,
        compiler_params=PARAMS,
        cost_estimate=reads(6 * residual.shape[0] * residual.shape[1]),
        name="combine",
    )(residual, gates, spread, own, returned)


def bundle_kernel(send, kv, tags, out):
    groups, rows, _ = out.shape
    heads = kv.shape[1] // 128
    capc = send.shape[0] // groups
    packed = jnp.dot(send[...], kv[...], preferred_element_type=f32).astype(bf16)
    tagged = jnp.dot(send[...], tags[...], preferred_element_type=f32)
    one = (lax.broadcasted_iota(jnp.int32, (16, 128), 0) == lax.broadcasted_iota(jnp.int32, (16, 128), 1))
    for owner in range(groups):
        mine = slice(owner * capc, (owner + 1) * capc)
        for head in range(heads):
            out[owner, head * capc : (head + 1) * capc, :] = packed[mine, head * 128 : (head + 1) * 128]
        wide = jnp.concatenate([tagged[mine, :], jnp.zeros((128 - capc, 128), f32)], axis=0)
        out[owner, heads * capc :, :] = lax.dot_general(
            one.astype(f32), wide, LAST_DIMS, preferred_element_type=f32
        ).astype(bf16)


def bundle(groups, send, kv, tags):
    rows = send.shape[0] // groups * (kv.shape[1] // 128) + 16
    return pl.pallas_call(
        bundle_kernel,
        out_shape=jax.ShapeDtypeStruct((groups, rows, 128), bf16),
        in_specs=[VMEM] * 3,
        out_specs=VMEM,
        compiler_params=PARAMS,
        cost_estimate=LITTLE,
        name="bundle",
    )(send, kv, tags)


def write_kernel(heads, arrived, cache, out, rows, wide, known):
    groups, size, _ = arrived.shape
    slots = cache.shape[0] // heads
    capc = (size - 16) // heads
    high, low = [], []
    for source in range(groups):
        for head in range(heads):
            rows[source * capc : (source + 1) * capc, head * 128 : (head + 1) * 128] = arrived[
                source, head * capc : (head + 1) * capc, :
            ]
        numbers = arrived[source, heads * capc :, :].astype(f32)
        high.append(numbers[0:1, :capc])
        low.append(numbers[1:2, :capc])
    slot = jnp.concatenate(high, axis=1) * 64.0 + jnp.concatenate(low, axis=1) - 64.0
    row = lax.broadcasted_iota(jnp.int32, (slots, slot.shape[1]), 0).astype(f32)
    hit = (row == slot).astype(bf16)
    made = jnp.dot(hit, rows[...], preferred_element_type=f32)
    found = jnp.dot(hit, jnp.ones((slot.shape[1], 128), bf16), preferred_element_type=f32)
    for head in range(heads):
        wide[pl.ds(head, slots, heads), :] = made[:, head * 128 : (head + 1) * 128]
        known[pl.ds(head, slots, heads), :] = found
    old = cache[...].astype(f32)
    out[...] = jnp.where(known[...] > 0.0, wide[...], old).astype(bf16)


def write(arrived, cache):
    slots, heads, lanes = cache.shape
    capc = (arrived.shape[1] - 16) // heads
    flat = (slots * heads, lanes)
    written = pl.pallas_call(
        functools.partial(write_kernel, heads),
        out_shape=jax.ShapeDtypeStruct(flat, bf16),
        in_specs=[VMEM] * 2,
        out_specs=VMEM,
        scratch_shapes=[
            pltpu.VMEM((arrived.shape[0] * capc, heads * lanes), bf16),
            pltpu.VMEM(flat, f32),
            pltpu.VMEM(flat, f32),
        ],
        compiler_params=PARAMS,
        cost_estimate=reads(1 << 21),
        name="write",
    )(arrived, cache.reshape(flat))
    return written.reshape(cache.shape)


def two_lane_shards(
    tokens,
    positions,
    attn_gain,
    w_query,
    w_keyval,
    w_out,
    moe_gain,
    router,
    w_gate_up,
    w_down,
    expert_ids,
    cache_slot,
    kv_cache,
):
    groups = lax.axis_size("grp")
    tok_rows, model = tokens.shape
    block = positions.shape[0]
    kv_local, head2 = w_keyval.shape[1:]
    kv_width = kv_local * head2
    slots_dev = kv_cache.shape[0]
    swap = functools.partial(lax.ppermute, axis_name="hd", perm=[(0, 1), (1, 0)])

    together = lax.optimization_barrier

    other_tokens = swap(tokens)
    own = (w_gate_up[0], w_down[0], w_out.T)
    up_rows, down_rows = own[0].shape[0], own[1].shape[0]
    beside = [lax.ppermute(part, "grp", sibling_pairs(groups)) for part in own]
    expert_pair, out_pair = pack(own, beside)
    out_ring = Ring(out_pair, groups)
    out_ring.step()
    expert_ring = Ring(expert_pair, groups)
    expert_ring.step()
    w_keyval, positions = together((w_keyval, positions, out_pair))[:2]
    flat_kv = w_keyval.reshape(model, kv_width)
    cosine, sine, past, place, send, tags, gain = prepare(
        groups, slots_dev, positions, cache_slot, expert_ids, attn_gain
    )
    other_tokens, cosine, flat_kv = out_ring.pin(other_tokens, cosine, flat_kv)
    out_ring.step()

    q, kv, tail = project(tokens, other_tokens, gain, cosine, sine, w_query, flat_kv)
    seam = lax.ppermute(tail, "grp", [(g, g + 1) for g in range(groups - 1)])
    q = out_ring.pin(q)
    out_ring.step()
    out_ring.share(2)
    late = attend_late(q, kv, past)
    seam, late = together((seam, late))
    seam = expert_ring.pin(seam)
    expert_ring.step()
    early = attend_early(q, kv, seam, past)
    early, out_ring.near = together((early, out_ring.near))
    early = out_ring.pin(early)
    out_ring.step()
    out_ring.share(3)
    early, out_ring.near = together((early, out_ring.near))
    early = out_ring.pin(early)
    early = expert_ring.pin(early)
    expert_ring.step()
    out_ring.share()
    sent = outward_send(groups, early, late, out_ring.parts(), out_ring.unit_rows)
    arrived = swap(sent)
    early = together((early, sent))[0]
    mine, late_gain = outward_keep(
        groups, early, late, tokens, moe_gain, out_ring.parts(), out_ring.unit_rows
    )
    kv, late_gain = expert_ring.pin(kv, late_gain)
    expert_ring.share()
    expert_ring.step()
    outgoing = bundle(groups, send, kv, tags)
    arrived_cache = lax.all_to_all(outgoing, "grp", split_axis=0, concat_axis=0, tiled=True)
    arrived, late_gain, outgoing = expert_ring.pin(arrived, late_gain, outgoing)
    expert_ring.share()

    residual, moe_in, sent_rows = route(mine, arrived, late_gain, place)
    landed = swap(sent_rows)
    gates, own_rows, spread = gate(moe_in, router.T, expert_ids.T, place)
    landed, own_rows = together((landed, own_rows))
    own_made, back = expert(
        groups, own_rows, landed, expert_ring.parts(), up_rows, down_rows
    )
    returned = swap(back)
    layer_out = combine(residual, gates, spread, own_made, returned)
    layer_out, arrived_cache = together((layer_out, arrived_cache))
    cache_after = write(arrived_cache, kv_cache)
    return (layer_out, cache_after)


def passed_along(value, axis, steps):
    count = lax.axis_size(axis)
    initial, last = (max(0, -steps), min(count, count - steps))
    return lax.ppermute(value, axis, [(source, source + steps) for source in range(initial, last)])


def rms_norm(row_set, norm_gain):
    floats = row_set.astype(jnp.float32)
    factor = lax.rsqrt(jnp.mean(floats * floats, axis=-1, keepdims=True) + norm_eps)
    return (floats * factor * norm_gain).astype(jnp.bfloat16)


def rotate(vectors, angle_pos):
    halves = vectors.shape[-1] // 2
    inverse_freq = rope_base ** (-2.0 * jnp.arange(halves, dtype=jnp.float32) / vectors.shape[-1])
    angles = angle_pos[:, None, None] * inverse_freq[None, None, :]
    cosine = jnp.cos(angles)
    sine_part = jnp.sin(angles)
    first_half = vectors[..., :halves]
    second_half = vectors[..., halves:]
    return jnp.concatenate(
        [
            first_half * cosine - second_half * sine_part,
            second_half * cosine + first_half * sine_part,
        ],
        axis=-1,
    )


def expert_rows(row_set, gate_up, down_rows):
    gate_and_up = jnp.dot(row_set, gate_up, preferred_element_type=jnp.float32)
    inner_width = gate_and_up.shape[1] // 2
    hidden = (jax.nn.silu(gate_and_up[:, :inner_width]) * gate_and_up[:, inner_width:]).astype(
        jnp.bfloat16
    )
    return jnp.dot(hidden, down_rows, preferred_element_type=jnp.float32).astype(jnp.bfloat16)


def attend_rows(query_blk, keys_blk, vals_blk, visible, scale_qk):
    scores = (
        jnp.einsum("qkgd,skd->kgqs", query_blk, keys_blk, preferred_element_type=jnp.float32)
        * scale_qk
    )
    weights_f = jnp.where(visible[None, None], jnp.exp(scores), 0.0)
    prob_bf = (weights_f / jnp.sum(weights_f, axis=-1, keepdims=True)).astype(jnp.bfloat16)
    return jnp.einsum("kgqs,skd->qkgd", prob_bf, vals_blk, preferred_element_type=jnp.float32)


def shards(
    tokens,
    positions,
    attn_gain,
    w_query,
    w_keyval,
    w_out,
    moe_gain,
    router,
    w_gate_up,
    w_down,
    expert_ids,
    cache_slot,
    kv_cache,
):
    lane_count = lax.axis_size("hd")
    group_count = lax.axis_size("grp")
    tok_rows = tokens.shape[0]
    model_width = tokens.shape[1]
    block_len = positions.shape[0]
    seg_most = block_len // 2
    head_dim = w_keyval.shape[2] // 2
    kv_local = w_keyval.shape[1]
    q_local = w_query.shape[1] // head_dim
    per_kv = q_local // kv_local
    expert_cap = tok_rows // 4
    normed = rms_norm(tokens, attn_gain)
    flat_kv = w_keyval.reshape(model_width, kv_local * 2 * head_dim)
    section = lax.all_gather(normed, "hd", axis=0, tiled=True)
    projected = jnp.concatenate(
        [
            jnp.dot(section, w_query, preferred_element_type=jnp.float32),
            jnp.dot(section, flat_kv, preferred_element_type=jnp.float32),
        ],
        axis=1,
    )
    angle_pos = jnp.maximum(positions, 0).astype(jnp.float32)
    queries = rotate(
        projected[:, : q_local * head_dim].reshape(block_len, q_local, head_dim), angle_pos
    ).astype(jnp.bfloat16)
    key_val = projected[:, q_local * head_dim :].reshape(block_len, kv_local, 2 * head_dim)
    rotated = rotate(key_val[:, :, :head_dim], angle_pos).astype(jnp.bfloat16)
    stored = jnp.concatenate([rotated, key_val[:, :, head_dim:].astype(jnp.bfloat16)], axis=2)
    seam_rows = passed_along(stored[block_len - seg_most :], "grp", 1)
    window = jnp.concatenate([seam_rows, stored], axis=0)
    scale_qk = head_dim ** (-0.5)
    local_rows = jnp.arange(block_len, dtype=jnp.int32)
    lowest = local_rows - jnp.maximum(positions, 0)
    pieces_out = []
    for q_block in range(2):
        first_row = q_block * seg_most
        rows_here = first_row + jnp.arange(seg_most, dtype=jnp.int32)
        cols_here = first_row - seg_most + jnp.arange(2 * seg_most, dtype=jnp.int32)
        low_here = lowest[first_row : first_row + seg_most]
        visible = (cols_here[None, :] >= low_here[:, None]) & (
            cols_here[None, :] <= rows_here[:, None]
        )
        query_blk = queries[first_row : first_row + seg_most].reshape(
            seg_most, kv_local, per_kv, head_dim
        )
        keys_blk = window[first_row : first_row + 2 * seg_most, :, :head_dim]
        vals_blk = window[first_row : first_row + 2 * seg_most, :, head_dim:]
        mixed_rows = attend_rows(query_blk, keys_blk, vals_blk, visible, scale_qk)
        pieces_out.append(mixed_rows.reshape(seg_most, q_local * head_dim).astype(jnp.bfloat16))
    attended = jnp.concatenate(pieces_out, axis=0)
    slots_dev = kv_cache.shape[0]
    capc = 2 * block_len // group_count
    live_slot = cache_slot >= 0
    owners = jnp.where(live_slot, cache_slot // slots_dev, group_count)
    owner_hit = (owners[:, None] == jnp.arange(group_count, dtype=jnp.int32)[None, :]).astype(
        jnp.bfloat16
    )
    lower_tri = (local_rows[:, None] >= local_rows[None, :]).astype(jnp.bfloat16)
    running = jnp.dot(lower_tri, owner_hit, preferred_element_type=jnp.float32)
    owner_rank = jnp.sum(running * owner_hit.astype(jnp.float32), axis=1).astype(jnp.int32) - 1
    send_rows = jnp.where(live_slot, owners * capc + owner_rank, group_count * capc)
    outgoing_cache = (
        jnp.zeros((group_count * capc, kv_local, 2 * head_dim), jnp.bfloat16)
        .at[send_rows]
        .set(stored, mode="drop")
    )
    outgoing_slots = (
        jnp.full((group_count * capc,), -1, jnp.int32)
        .at[send_rows]
        .set(cache_slot % slots_dev, mode="drop")
    )
    arrived, arrived_slots = (
        lax.all_to_all(
            outgoing_cache.reshape(group_count, capc, kv_local, 2 * head_dim),
            "grp",
            split_axis=0,
            concat_axis=0,
            tiled=True,
        ),
        lax.all_to_all(
            outgoing_slots.reshape(group_count, capc),
            "grp",
            split_axis=0,
            concat_axis=0,
            tiled=True,
        ),
    )
    flat_slots = arrived_slots.reshape(group_count * capc)
    write_rows = jnp.where(flat_slots >= 0, flat_slots, slots_dev).astype(jnp.int32)
    cache_after = kv_cache.at[write_rows].set(
        arrived.reshape(group_count * capc, kv_local, 2 * head_dim), mode="drop"
    )
    by_token = lax.all_to_all(attended, "hd", split_axis=0, concat_axis=1, tiled=True)
    attn_proj = jnp.dot(
        by_token,
        lax.all_gather(w_out, "grp", axis=1, tiled=True),
        preferred_element_type=jnp.float32,
    )
    residual = (tokens.astype(jnp.float32) + attn_proj).astype(jnp.bfloat16)
    moe_in = rms_norm(residual, moe_gain)
    logits = jnp.dot(moe_in, router, preferred_element_type=jnp.float32)
    expert_range = jnp.arange(router.shape[1], dtype=jnp.int32)
    matches_all = expert_ids[:, :, None] == expert_range[None, None, :]
    chosen = jnp.sum(jnp.where(matches_all, logits[:, None, :], 0.0), axis=2)
    raised = jnp.exp(chosen)
    gates = raised / jnp.sum(raised, axis=1, keepdims=True)
    live_range = jnp.arange(lane_count, dtype=jnp.int32)
    matches = expert_ids[:, :, None] == live_range[None, None, :]
    member = jnp.any(matches, axis=1)
    weighting = jnp.sum(jnp.where(matches, gates[:, :, None], 0.0), axis=1)
    ranking = jnp.cumsum(member.astype(jnp.int32), axis=0) - 1
    target = jnp.where(member, live_range[None, :] * expert_cap + ranking, -1)
    slot_range = jnp.arange(lane_count * expert_cap, dtype=jnp.int32)
    slot_hits = target[None, :, :] == slot_range[:, None, None]
    placing = jnp.any(slot_hits, axis=2).astype(jnp.bfloat16)
    outgoing = (
        jnp.dot(placing, moe_in, preferred_element_type=jnp.float32)
        .astype(jnp.bfloat16)
        .reshape(lane_count, expert_cap, model_width)
    )
    gate_up_all, down_all = (
        lax.all_gather(w_gate_up, "grp", axis=1, tiled=True),
        lax.all_gather(w_down, "grp", axis=1, tiled=True),
    )
    gate_up_mat = gate_up_all[0]
    down_mat = down_all[0]
    landed = lax.all_to_all(outgoing, "hd", split_axis=0, concat_axis=0, tiled=True)
    results = expert_rows(landed.reshape(-1, model_width), gate_up_mat, down_mat).reshape(landed.shape)
    returned = lax.all_to_all(results, "hd", split_axis=0, concat_axis=0, tiled=True)
    flat_returned = returned.reshape(-1, model_width)
    fetched = flat_returned[jnp.maximum(target, 0)]
    used_weight = jnp.where(member, weighting, 0.0)
    moe_total = jnp.sum(used_weight[:, :, None] * fetched.astype(jnp.float32), axis=1)
    layer_out = (residual.astype(jnp.float32) + moe_total).astype(jnp.bfloat16)
    return (layer_out, cache_after)


def solution(mesh):
    two_lanes = mesh.shape["hd"] == 2 and mesh.shape["grp"] % 8 == 0
    return jax.shard_map(
        two_lane_shards if two_lanes else shards,
        mesh=mesh,
        in_specs=(
            P(("grp", "hd"), None),
            P("grp"),
            P(),
            P(None, "hd"),
            P(None, "hd", None),
            P(None, "grp"),
            P(),
            P(),
            P("hd", "grp", None),
            P("hd", "grp", None),
            P(("grp", "hd"), None),
            P("grp"),
            P("grp", "hd", None),
        ),
        out_specs=(P(("grp", "hd"), None), P("grp", "hd", None)),
        check_vma=False,
    )
```

```python
import functools

import jax
import jax.numpy as jnp
import numpy as np
from jax import lax
from jax.experimental import pallas as pl
from jax.experimental.pallas import tpu as pltpu
from jax.sharding import PartitionSpec as P

norm_eps = 1e-05
rope_base = 10000.0
bf16 = jnp.bfloat16
f32 = jnp.float32
LAST_DIMS = (((1,), (1,)), ((), ()))


def ring_cycle(groups):
    rows = groups // 4
    return [2 * r for r in range(rows)] + [2 * r + 1 for r in reversed(range(rows))]


def ring_pairs(groups):
    cycle = ring_cycle(groups)
    count = len(cycle)
    pairs = []
    for place, pair in enumerate(cycle):
        pairs.append((2 * pair, 2 * cycle[(place + 1) % count]))
        pairs.append((2 * pair + 1, 2 * cycle[(place - 1) % count] + 1))
    return pairs


def sibling_pairs(groups):
    return [(g, g ^ 1) for g in range(groups)]


def ring_sources(groups, me):
    count = groups // 2
    rows = count // 2
    side, pair = me % 2, me // 2
    row, col = pair // 2, pair % 2
    place = jnp.where(col == 0, row, count - 1 - row)

    def block(core, steps):
        there = (place + (2 * core - 1) * steps + count) % count
        other = jnp.where(there < rows, 2 * there, 2 * (count - 1 - there) + 1)
        return [2 * other + core, 2 * other + 1 - core]

    full = (count - 1) // 2
    listed = [me, me + 1 - 2 * side]
    for core in (side, 1 - side):
        for steps in range(1, full + 1):
            listed += block(core, steps)
    return listed + [block(side, count // 2)[0], block(1 - side, count // 2)[0]]


class Ring:
    def __init__(self, pair, groups):
        self.across = functools.partial(lax.ppermute, axis_name="grp", perm=ring_pairs(groups))
        self.beside = functools.partial(lax.ppermute, axis_name="grp", perm=sibling_pairs(groups))
        self.full = (groups // 2 - 1) // 2
        self.unit_rows = pair.shape[0] // 2
        self.mine = [pair]
        self.near = []

    def step(self):
        held = self.mine[-1]
        if len(self.mine) > self.full:
            held = held[: self.unit_rows]
        self.mine.append(self.across(held))

    def pin(self, *others):
        done = lax.optimization_barrier((self.mine[-1],) + others)
        self.mine[-1] = done[0]
        return done[1:] if len(others) > 1 else done[1]

    def share(self, upto=None):
        for index in range(1 + len(self.near), 1 + (upto or len(self.mine) - 1)):
            self.near.append(self.beside(self.mine[index]))

    def parts(self):
        full = self.full
        return self.mine[: full + 1] + self.near[:full] + [self.mine[full + 1], self.near[full]]


def place_parts(groups, parts, unit_rows, pieces):
    sources = ring_sources(groups, lax.axis_index("grp"))
    shard = 0
    for part in parts:
        for unit in range(part.shape[0] // unit_rows):
            for first, rows, target, lane in pieces:
                at = pl.multiple_of(sources[shard] * rows, rows)
                start = unit * unit_rows + first
                target[pl.ds(at, rows), lane : lane + part.shape[1]] = part[start : start + rows, :]
            shard += 1


VMEM = pl.BlockSpec(memory_space=pltpu.VMEM)
ANY = pl.BlockSpec(memory_space=pl.ANY)
HBM = pl.BlockSpec(memory_space=pltpu.HBM)
PARAMS = pltpu.CompilerParams(vmem_limit_bytes=16 << 20)


LITTLE = pl.CostEstimate(flops=1, bytes_accessed=1, transcendentals=0)


def takes(us):
    return pl.CostEstimate(
        flops=int(us * 1.15e9), bytes_accessed=int(us * 8e6), transcendentals=0
    )


def reads(nbytes):
    return pl.CostEstimate(flops=1, bytes_accessed=nbytes, transcendentals=0)


def normalized(floats, gain):
    factor = lax.rsqrt(jnp.mean(floats * floats, axis=-1, keepdims=True) + norm_eps)
    return (floats * factor * gain).astype(bf16)


def fetch(pairs, sems):
    copies = []
    for index, (source, target) in enumerate(pairs):
        copies.append(pltpu.make_async_copy(source, target, sems.at[index]))
        copies[-1].start()
    return copies


def pack_kernel(*refs):
    sources, (expert_pair, out_pair, sems) = refs[:6], refs[6:]
    width = expert_pair.shape[1]
    lane = lax.axis_index("hd")
    first = pl.multiple_of(lane * out_pair.shape[1], out_pair.shape[1])
    pairs = []
    row = 0
    for index in range(2):
        up, down, w_out = sources[3 * index : 3 * index + 3]
        count = w_out.shape[0]
        pairs.append(
            (w_out.at[:, pl.ds(first, out_pair.shape[1])], out_pair.at[pl.ds(index * count, count), :])
        )
        for source in (up, down):
            for at in range(0, source.shape[1], width):
                pairs.append(
                    (source.at[:, pl.ds(at, width)], expert_pair.at[pl.ds(row, source.shape[0]), :])
                )
                row += source.shape[0]
    for copy in fetch(pairs, sems):
        copy.wait()


def pack(own, beside):
    own = [pltpu.with_memory_space_constraint(part, pltpu.HBM) for part in own]
    up, down, w_out_t = own
    width = up.shape[1] // 2
    pieces = [up.shape[1] // width, down.shape[1] // width]
    unit_rows = pieces[0] * up.shape[0] + pieces[1] * down.shape[0]
    return pl.pallas_call(
        pack_kernel,
        out_shape=(
            jax.ShapeDtypeStruct((2 * unit_rows, width), bf16),
            jax.ShapeDtypeStruct((2 * w_out_t.shape[0], w_out_t.shape[1] // 2), bf16),
        ),
        in_specs=[ANY] * 6,
        out_specs=(ANY, ANY),
        scratch_shapes=[pltpu.SemaphoreType.DMA((2 + 2 * sum(pieces),))],
        compiler_params=PARAMS,
        cost_estimate=LITTLE,
        name="pack",
    )(*own, *beside)


def as_column(row, eye):
    return jnp.sum(jnp.where(eye, row, 0.0), axis=1, keepdims=True)


def named_experts(ids, experts):
    tokens = ids.shape[1]
    expert = lax.broadcasted_iota(jnp.int32, (experts, tokens), 0)
    hit = jnp.zeros((experts, tokens), f32)
    for index in range(ids.shape[0]):
        hit = jnp.where(ids[index : index + 1, :] == expert, 1.0, hit)
    return hit


def prepare_kernel(groups, slots_dev, *refs):
    sources, (cosine, sine, past, place, send, tags, gain) = refs[:4], refs[4:11]
    positions, slots, ids, flat_gain, sems = refs[11:]
    copies = fetch(list(zip(sources, (positions, slots, ids, flat_gain))), sems)
    for copy in copies:
        copy.wait()
    gain[...] = flat_gain[...].reshape(gain.shape)
    lane = lax.axis_index("hd")
    block = positions.shape[1]

    def iota(shape, dim):
        return lax.broadcasted_iota(jnp.int32, shape, dim)

    eye = iota((block, block), 0) == iota((block, block), 1)
    reach = as_column(jnp.maximum(positions[...], 0).astype(f32), eye)
    past[...] = jnp.broadcast_to(reach, past.shape)
    column = iota((8, 128), 1)
    exponent = (column % 32).astype(f32) * (-2.0 / 64)
    inverse_freq = jnp.exp(exponent * np.float32(np.log(rope_base)))[:1, :]
    angles = reach * inverse_freq
    cosine[...] = jnp.cos(angles)
    turned = jnp.sin(angles)
    sine[...] = jnp.where(iota(angles.shape, 1) % 64 < 32, -turned, turned)

    tokens = ids.shape[1]
    cap = place.shape[0] // 2
    hit = named_experts(ids, 8)
    upto = (iota((tokens, tokens), 0) <= iota((tokens, tokens), 1)).astype(f32)
    rank = jnp.dot(hit, upto, preferred_element_type=f32) - 1.0
    slot = iota((2 * cap, tokens), 0).astype(f32)
    placed = jnp.zeros((2 * cap, tokens), f32)
    for live in range(2):
        order = jnp.where(lane == live, 0, cap).astype(f32)
        member = hit[live : live + 1, :] > 0.0
        placed = jnp.where(member & (slot == rank[live : live + 1, :] + order), 1.0, placed)
    place[...] = placed.astype(bf16)

    where = slots[...]
    owner = jnp.where(where >= 0, where // slots_dev, -1)
    owner_hit = (iota((groups, block), 0) == owner).astype(f32)
    before = (iota((block, block), 0) <= iota((block, block), 1)).astype(f32)
    running = jnp.dot(owner_hit, before, preferred_element_type=f32)
    owner_rank = jnp.sum(owner_hit * running, axis=0, keepdims=True) - 1.0
    capc = send.shape[0] // groups
    row = jnp.where(owner >= 0, owner * capc + owner_rank.astype(jnp.int32), -1)
    send[...] = (iota(send.shape, 0) == row).astype(bf16)
    inside = jnp.where(where >= 0, where % slots_dev, 0)
    high = as_column((inside // 64 + 1).astype(f32), eye)
    low = as_column((inside % 64).astype(f32), eye)
    spot = iota(tags.shape, 1)
    tags[...] = jnp.where(spot == 0, high, jnp.where(spot == 1, low, 0.0)).astype(bf16)


def prepare(groups, slots_dev, positions, slots, ids, gain):
    block, tokens = positions.shape[0], ids.shape[0]
    model = gain.shape[0]
    cap = tokens // 4
    capc = 2 * block // groups
    shapes = [
        ((block, 128), f32),
        ((block, 128), f32),
        ((block, 128), f32),
        ((2 * cap, tokens), bf16),
        ((groups * capc, block), bf16),
        ((block, 128), bf16),
        ((1, model), f32),
    ]
    sources = (positions[None], slots[None], ids.T, gain)
    return pl.pallas_call(
        functools.partial(prepare_kernel, groups, slots_dev),
        out_shape=tuple(jax.ShapeDtypeStruct(shape, kind) for shape, kind in shapes),
        in_specs=[ANY] * 4,
        out_specs=(VMEM,) * len(shapes),
        scratch_shapes=[
            pltpu.VMEM((1, block), jnp.int32),
            pltpu.VMEM((1, block), jnp.int32),
            pltpu.VMEM(ids.shape[::-1], jnp.int32),
            pltpu.VMEM((model,), f32),
            pltpu.SemaphoreType.DMA((4,)),
        ],
        compiler_params=PARAMS,
        cost_estimate=LITTLE,
        name="prepare",
    )(*[pltpu.with_memory_space_constraint(source, pltpu.HBM) for source in sources])


def project_kernel(
    own, other, gain, cosine, sine, w_query, w_keyval, q_out, kv_out, seam_out, raw, rows, sems
):
    count = own.shape[0]
    lane = lax.axis_index("hd")
    mine = pl.multiple_of(lane * count, count)
    theirs = pl.multiple_of((1 - lane) * count, count)
    copies = fetch([(own, raw.at[0]), (other, raw.at[1])], sems)
    cos_q, sin_q = cosine[...], sine[...]
    column = lax.broadcasted_iota(jnp.int32, cos_q.shape, 1)
    lower = column % 64 < 32
    cos_kv = jnp.where(column < 64, cos_q, 1.0)
    sin_kv = jnp.where(column < 64, sin_q, 0.0)
    for index, first in ((0, mine), (1, theirs)):
        copies[index].wait()
        rows[pl.ds(first, count), :] = normalized(raw[index].astype(f32), gain[...])
    width = 256
    for weights, out, cos, sin in ((w_keyval, kv_out, cos_kv, sin_kv), (w_query, q_out, cos_q, sin_q)):
        for first in range(0, weights.shape[1], width):
            made = jnp.dot(rows[...], weights[:, first : first + width], preferred_element_type=f32)
            for part in range(0, width, 128):
                here = made[:, part : part + 128]
                turned = jnp.where(lower, pltpu.roll(here, 96, 1), pltpu.roll(here, 32, 1))
                done = (here * cos + turned * sin).astype(bf16)
                out[:, first + part : first + part + 128] = done
                if out is kv_out:
                    seam_out[:, first + part : first + part + 128] = done[count:, :]


def project(own, other, gain, cosine, sine, w_query, flat_kv):
    count, width = own.shape
    made = w_query.shape[1] + flat_kv.shape[1]
    return pl.pallas_call(
        project_kernel,
        out_shape=(
            jax.ShapeDtypeStruct((2 * count, w_query.shape[1]), bf16),
            jax.ShapeDtypeStruct((2 * count, flat_kv.shape[1]), bf16),
            jax.ShapeDtypeStruct((count, flat_kv.shape[1]), bf16),
        ),
        in_specs=[ANY] * 2 + [VMEM] * 5,
        out_specs=(VMEM, VMEM, VMEM),
        scratch_shapes=[
            pltpu.VMEM((2, count, width), bf16),
            pltpu.VMEM((2 * count, width), bf16),
            pltpu.SemaphoreType.DMA((2,)),
        ],
        compiler_params=PARAMS,
        cost_estimate=takes(8),
        name="project",
    )(own, other, gain, cosine, sine, w_query, flat_kv)


def attend_rows_kernel(first, q, kv, seam, past, mixed, window, sem):
    count = q.shape[0] // 2
    if first == 0:
        copy = pltpu.make_async_copy(seam, window.at[pl.ds(0, count), :], sem)
        copy.start()
        window[count:, :] = kv[:count, :]
        copy.wait()
        keyed = window
    else:
        keyed = kv
    head = 64
    kv_heads = kv.shape[1] // (2 * head)
    per_kv = q.shape[1] // head // kv_heads
    shape = (count, 2 * count)
    row = lax.broadcasted_iota(jnp.int32, shape, 0) + count
    col = lax.broadcasted_iota(jnp.int32, shape, 1)
    reach = past[first : first + count, :1].astype(jnp.int32)
    visible = (col <= row) & (col >= row - reach)
    for kv_head in range(kv_heads):
        lanes = 2 * head * kv_head
        keys = keyed[:, lanes : lanes + head]
        values = keyed[:, lanes + head : lanes + 2 * head]
        for index in range(per_kv):
            at = (kv_head * per_kv + index) * head
            query = q[first : first + count, at : at + head]
            scores = lax.dot_general(query, keys, LAST_DIMS, preferred_element_type=f32)
            raised = jnp.where(visible, jnp.exp(scores * head ** (-0.5)), 0.0)
            probs = (raised / jnp.sum(raised, axis=-1, keepdims=True)).astype(bf16)
            made = jnp.dot(probs, values, preferred_element_type=f32)
            mixed[:, at : at + head] = made.astype(bf16)


def attend_late(q, kv, past):
    def kernel(q, kv, past, mixed):
        attend_rows_kernel(q.shape[0] // 2, q, kv, None, past, mixed, None, None)

    return pl.pallas_call(
        kernel,
        out_shape=jax.ShapeDtypeStruct((q.shape[0] // 2, q.shape[1]), bf16),
        in_specs=[VMEM] * 3,
        out_specs=VMEM,
        compiler_params=PARAMS,
        cost_estimate=takes(2),
        name="attend_late",
    )(q, kv, past)


def attend_early(q, kv, seam, past):
    return pl.pallas_call(
        functools.partial(attend_rows_kernel, 0),
        out_shape=jax.ShapeDtypeStruct((q.shape[0] // 2, q.shape[1]), bf16),
        in_specs=[VMEM, VMEM, ANY, VMEM],
        out_specs=VMEM,
        scratch_shapes=[pltpu.VMEM(kv.shape, bf16), pltpu.SemaphoreType.DMA],
        compiler_params=PARAMS,
        cost_estimate=takes(2),
        name="attend_early",
    )(q, kv, seam, past)


def outward_rows(flip, groups, unit_rows, early, late, parts, w_out, rows):
    place_parts(groups, parts, unit_rows, [(0, unit_rows, w_out, 0)])
    lane = lax.axis_index("hd")
    which = (1 - lane) if flip else lane

    @pl.when(which == 0)
    def _():
        rows[...] = early[...]

    @pl.when(which != 0)
    def _():
        rows[...] = late[...]

    return lax.dot_general(rows[...], w_out[...], LAST_DIMS, preferred_element_type=f32)


def send_kernel(groups, unit_rows, n_parts, early, late, *refs):
    parts, (out, w_out, rows) = refs[:n_parts], refs[n_parts:]
    out[...] = outward_rows(True, groups, unit_rows, early, late, parts, w_out, rows).astype(bf16)


def keep_kernel(groups, unit_rows, n_parts, early, late, tokens, flat_gain, *refs):
    parts, (out, gain, w_out, rows) = refs[:n_parts], refs[n_parts:]
    gain[...] = flat_gain[...].reshape(gain.shape)
    made = outward_rows(False, groups, unit_rows, early, late, parts, w_out, rows)
    out[...] = tokens[...].astype(f32) + made


def outward_send(groups, early, late, parts, unit_rows):
    width, depth = groups * unit_rows, parts[0].shape[1]
    return pl.pallas_call(
        functools.partial(send_kernel, groups, unit_rows, len(parts)),
        out_shape=jax.ShapeDtypeStruct((early.shape[0], width), bf16),
        in_specs=[VMEM] * (2 + len(parts)),
        out_specs=VMEM,
        scratch_shapes=[pltpu.VMEM((width, depth), bf16), pltpu.VMEM(early.shape, bf16)],
        compiler_params=PARAMS,
        cost_estimate=reads(2 * width * depth),
        name="outward_send",
    )(early, late, *parts)


def outward_keep(groups, early, late, tokens, gain, parts, unit_rows):
    width, depth = groups * unit_rows, parts[0].shape[1]
    return pl.pallas_call(
        functools.partial(keep_kernel, groups, unit_rows, len(parts)),
        out_shape=(
            jax.ShapeDtypeStruct(tokens.shape, f32),
            jax.ShapeDtypeStruct((1, width), f32),
        ),
        in_specs=[VMEM] * (4 + len(parts)),
        out_specs=(VMEM, VMEM),
        scratch_shapes=[
            pltpu.VMEM((width, depth), bf16),
            pltpu.VMEM(early.shape, bf16),
        ],
        compiler_params=PARAMS,
        cost_estimate=reads(2 * width * depth),
        name="outward_keep",
    )(early, late, tokens, gain, *parts)


def route_kernel(mine, arrived, gain, place, residual, moe_in, sent):
    added = (mine[...] + arrived[...].astype(f32)).astype(bf16)
    residual[...] = added
    moe_in[...] = normalized(added.astype(f32), gain[...])
    cap = sent.shape[0]
    rows = jnp.dot(place[cap:, :], moe_in[...], preferred_element_type=f32)
    sent[...] = rows.astype(bf16)


def route(mine, arrived, gain, place):
    cap = place.shape[0] // 2
    return pl.pallas_call(
        route_kernel,
        out_shape=(
            jax.ShapeDtypeStruct(mine.shape, bf16),
            jax.ShapeDtypeStruct(mine.shape, bf16),
            jax.ShapeDtypeStruct((cap, mine.shape[1]), bf16),
        ),
        in_specs=[VMEM] * 4,
        out_specs=(VMEM,) * 3,
        compiler_params=PARAMS,
        cost_estimate=reads(10 * mine.shape[0] * mine.shape[1]),
        name="route",
    )(mine, arrived, gain, place)


def gate_kernel(moe_in, router, ids, place, gates, own, spread):
    cap = own.shape[0]
    own[...] = jnp.dot(place[:cap, :], moe_in[...], preferred_element_type=f32).astype(bf16)
    hit = named_experts(ids, router.shape[0])
    tokens = ids.shape[1]
    row = lax.broadcasted_iota(jnp.int32, (tokens, tokens), 0)
    eye = (row == lax.broadcasted_iota(jnp.int32, (tokens, tokens), 1)).astype(f32)
    named = lax.dot_general(eye, hit, LAST_DIMS, preferred_element_type=f32)
    spread[...] = lax.dot_general(
        eye.astype(bf16), place[...], LAST_DIMS, preferred_element_type=f32
    ).astype(bf16)
    logits = lax.dot_general(moe_in[...], router[...], LAST_DIMS, preferred_element_type=f32)
    raised = jnp.where(named > 0, jnp.exp(logits), 0.0)
    gates[...] = raised / jnp.sum(raised, axis=-1, keepdims=True)


def gate(moe_in, router_t, ids_t, place):
    cap = place.shape[0] // 2
    return pl.pallas_call(
        gate_kernel,
        out_shape=(
            jax.ShapeDtypeStruct((moe_in.shape[0], router_t.shape[0]), f32),
            jax.ShapeDtypeStruct((cap, moe_in.shape[1]), bf16),
            jax.ShapeDtypeStruct(place.shape[::-1], bf16),
        ),
        in_specs=[VMEM] * 4,
        out_specs=(VMEM,) * 3,
        compiler_params=PARAMS,
        cost_estimate=LITTLE,
        name="gate",
    )(moe_in, router_t, ids_t, place)


def expert_kernel(groups, up_rows, down_rows, n_parts, own, other, *refs):
    parts = refs[:n_parts]
    own_out, other_out, rows, gate_up, down = refs[n_parts:]
    width = parts[0].shape[1]
    count = own.shape[0]
    rows[:count, :] = own[...]
    rows[count:, :] = other[...]
    pieces = [(i * up_rows, up_rows, gate_up, i * width) for i in range(2)]
    pieces += [
        (2 * up_rows + i * down_rows, down_rows, down, i * width) for i in range(down.shape[1] // width)
    ]
    unit_rows = pieces[-1][0] + down_rows
    place_parts(groups, parts, unit_rows, pieces)
    both = jnp.dot(rows[...], gate_up[...], preferred_element_type=f32)
    gate, up = both[:, :width], both[:, width:]
    hidden = (gate / (1.0 + jnp.exp(-gate)) * up).astype(bf16)
    made = jnp.dot(hidden, down[...], preferred_element_type=f32).astype(bf16)
    own_out[...] = made[:count, :]
    other_out[...] = made[count:, :]


def expert(groups, own, other, parts, up_rows, down_rows):
    count, model = own.shape
    width = parts[0].shape[1]
    return pl.pallas_call(
        functools.partial(expert_kernel, groups, up_rows, down_rows, len(parts)),
        out_shape=(jax.ShapeDtypeStruct(own.shape, bf16),) * 2,
        in_specs=[VMEM] * (2 + len(parts)),
        out_specs=(VMEM, VMEM),
        scratch_shapes=[
            pltpu.VMEM((2 * count, model), bf16),
            pltpu.VMEM((groups * up_rows, 2 * width), bf16),
            pltpu.VMEM((groups * down_rows, model), bf16),
        ],
        compiler_params=PARAMS,
        cost_estimate=takes(5.2),
        name="expert",
    )(own, other, *parts)


def combine_kernel(residual, gates, spread, own, returned, out):
    lane = lax.axis_index("hd")
    count = own.shape[0]
    column = lax.broadcasted_iota(jnp.int32, gates.shape, 1)
    total = jnp.zeros(residual.shape, f32)
    for index, made in ((0, own), (1, returned)):
        live = lane if index == 0 else 1 - lane
        weight = jnp.sum(jnp.where(column == live, gates[...], 0.0), axis=-1, keepdims=True)
        picked = jnp.dot(
            spread[:, index * count : (index + 1) * count], made[...], preferred_element_type=f32
        )
        total += weight * picked
    out[...] = (residual[...].astype(f32) + total).astype(bf16)


def combine(residual, gates, spread, own, returned):
    return pl.pallas_call(
        combine_kernel,
        out_shape=jax.ShapeDtypeStruct(residual.shape, bf16),
        in_specs=[VMEM] * 5,
        out_specs=VMEM,
        compiler_params=PARAMS,
        cost_estimate=reads(6 * residual.shape[0] * residual.shape[1]),
        name="combine",
    )(residual, gates, spread, own, returned)


def bundle_kernel(send, kv, tags, result, out, sem):
    groups, rows, _ = out.shape
    heads = kv.shape[1] // 128
    capc = send.shape[0] // groups
    packed = jnp.dot(send[...], kv[...], preferred_element_type=f32).astype(bf16)
    tagged = jnp.dot(send[...], tags[...], preferred_element_type=f32)
    one = (lax.broadcasted_iota(jnp.int32, (16, 128), 0) == lax.broadcasted_iota(jnp.int32, (16, 128), 1))
    for owner in range(groups):
        mine = slice(owner * capc, (owner + 1) * capc)
        for head in range(heads):
            out[owner, head * capc : (head + 1) * capc, :] = packed[mine, head * 128 : (head + 1) * 128]
        wide = jnp.concatenate([tagged[mine, :], jnp.zeros((128 - capc, 128), f32)], axis=0)
        out[owner, heads * capc :, :] = lax.dot_general(
            one.astype(f32), wide, LAST_DIMS, preferred_element_type=f32
        ).astype(bf16)
    copy = pltpu.make_async_copy(out, result, sem)
    copy.start()
    copy.wait()


def bundle(groups, send, kv, tags):
    rows = send.shape[0] // groups * (kv.shape[1] // 128) + 16
    return pl.pallas_call(
        bundle_kernel,
        out_shape=pltpu.HBM((groups, rows, 128), bf16),
        in_specs=[VMEM] * 3,
        out_specs=HBM,
        scratch_shapes=[pltpu.VMEM((groups, rows, 128), bf16), pltpu.SemaphoreType.DMA],
        compiler_params=PARAMS,
        cost_estimate=LITTLE,
        name="bundle",
    )(send, kv, tags)


def write_kernel(heads, arrived, cache, out, rows, wide, known):
    groups, size, _ = arrived.shape
    slots = cache.shape[0] // heads
    capc = (size - 16) // heads
    high, low = [], []
    for source in range(groups):
        for head in range(heads):
            rows[source * capc : (source + 1) * capc, head * 128 : (head + 1) * 128] = arrived[
                source, head * capc : (head + 1) * capc, :
            ]
        numbers = arrived[source, heads * capc :, :].astype(f32)
        high.append(numbers[0:1, :capc])
        low.append(numbers[1:2, :capc])
    slot = jnp.concatenate(high, axis=1) * 64.0 + jnp.concatenate(low, axis=1) - 64.0
    row = lax.broadcasted_iota(jnp.int32, (slots, slot.shape[1]), 0).astype(f32)
    hit = (row == slot).astype(bf16)
    made = jnp.dot(hit, rows[...], preferred_element_type=f32)
    found = jnp.dot(hit, jnp.ones((slot.shape[1], 128), bf16), preferred_element_type=f32)
    for head in range(heads):
        wide[pl.ds(head, slots, heads), :] = made[:, head * 128 : (head + 1) * 128]
        known[pl.ds(head, slots, heads), :] = found
    old = cache[...].astype(f32)
    out[...] = jnp.where(known[...] > 0.0, wide[...], old).astype(bf16)


def write(arrived, cache):
    slots, heads, lanes = cache.shape
    capc = (arrived.shape[1] - 16) // heads
    flat = (slots * heads, lanes)
    written = pl.pallas_call(
        functools.partial(write_kernel, heads),
        out_shape=jax.ShapeDtypeStruct(flat, bf16),
        in_specs=[VMEM] * 2,
        out_specs=VMEM,
        scratch_shapes=[
            pltpu.VMEM((arrived.shape[0] * capc, heads * lanes), bf16),
            pltpu.VMEM(flat, f32),
            pltpu.VMEM(flat, f32),
        ],
        compiler_params=PARAMS,
        cost_estimate=reads(1 << 21),
        name="write",
    )(arrived, cache.reshape(flat))
    return written.reshape(cache.shape)


def two_lane_shards(
    tokens,
    positions,
    attn_gain,
    w_query,
    w_keyval,
    w_out,
    moe_gain,
    router,
    w_gate_up,
    w_down,
    expert_ids,
    cache_slot,
    kv_cache,
):
    groups = lax.axis_size("grp")
    tok_rows, model = tokens.shape
    block = positions.shape[0]
    kv_local, head2 = w_keyval.shape[1:]
    kv_width = kv_local * head2
    slots_dev = kv_cache.shape[0]
    swap = functools.partial(lax.ppermute, axis_name="hd", perm=[(0, 1), (1, 0)])

    together = lax.optimization_barrier

    other_tokens = swap(tokens)
    own = (w_gate_up[0], w_down[0], w_out.T)
    up_rows, down_rows = own[0].shape[0], own[1].shape[0]
    beside = [lax.ppermute(part, "grp", sibling_pairs(groups)) for part in own]
    expert_pair, out_pair = pack(own, beside)
    out_ring = Ring(out_pair, groups)
    out_ring.step()
    expert_ring = Ring(expert_pair, groups)
    expert_ring.step()
    w_keyval, positions = together((w_keyval, positions, out_pair))[:2]
    flat_kv = w_keyval.reshape(model, kv_width)
    cosine, sine, past, place, send, tags, gain = prepare(
        groups, slots_dev, positions, cache_slot, expert_ids, attn_gain
    )
    other_tokens, cosine, flat_kv = out_ring.pin(other_tokens, cosine, flat_kv)
    out_ring.step()

    q, kv, tail = project(tokens, other_tokens, gain, cosine, sine, w_query, flat_kv)
    seam = lax.ppermute(tail, "grp", [(g, g + 1) for g in range(groups - 1)])
    q = out_ring.pin(q)
    out_ring.step()
    out_ring.share(2)
    late = attend_late(q, kv, past)
    seam, late = together((seam, late))
    seam = expert_ring.pin(seam)
    expert_ring.step()
    early = attend_early(q, kv, seam, past)
    early, out_ring.near = together((early, out_ring.near))
    early = out_ring.pin(early)
    out_ring.step()
    out_ring.share(3)
    early, kv, out_ring.near = together((early, kv, out_ring.near))
    outgoing = bundle(groups, send, kv, tags)
    early, outgoing = together((early, outgoing))
    early = out_ring.pin(early)
    early = expert_ring.pin(early)
    expert_ring.step()
    out_ring.share()
    sent = outward_send(groups, early, late, out_ring.parts(), out_ring.unit_rows)
    arrived = swap(sent)
    early = together((early, sent))[0]
    mine, late_gain = outward_keep(
        groups, early, late, tokens, moe_gain, out_ring.parts(), out_ring.unit_rows
    )
    late_gain = expert_ring.pin(late_gain)
    expert_ring.share()
    expert_ring.step()
    outgoing = together((outgoing, sent))[0]
    arrived_cache = lax.all_to_all(outgoing, "grp", split_axis=0, concat_axis=0, tiled=True)

    residual, moe_in, sent_rows = route(mine, arrived, late_gain, place)
    landed = swap(sent_rows)
    gates, own_rows, spread = gate(moe_in, router.T, expert_ids.T, place)
    landed, own_rows = expert_ring.pin(landed, own_rows)
    expert_ring.share()
    own_made, back = expert(
        groups, own_rows, landed, expert_ring.parts(), up_rows, down_rows
    )
    returned = swap(back)
    layer_out = combine(residual, gates, spread, own_made, returned)
    layer_out, arrived_cache = together((layer_out, arrived_cache))
    cache_after = write(arrived_cache, kv_cache)
    return (layer_out, cache_after)


def passed_along(value, axis, steps):
    count = lax.axis_size(axis)
    initial, last = (max(0, -steps), min(count, count - steps))
    return lax.ppermute(value, axis, [(source, source + steps) for source in range(initial, last)])


def rms_norm(row_set, norm_gain):
    floats = row_set.astype(jnp.float32)
    factor = lax.rsqrt(jnp.mean(floats * floats, axis=-1, keepdims=True) + norm_eps)
    return (floats * factor * norm_gain).astype(jnp.bfloat16)


def rotate(vectors, angle_pos):
    halves = vectors.shape[-1] // 2
    inverse_freq = rope_base ** (-2.0 * jnp.arange(halves, dtype=jnp.float32) / vectors.shape[-1])
    angles = angle_pos[:, None, None] * inverse_freq[None, None, :]
    cosine = jnp.cos(angles)
    sine_part = jnp.sin(angles)
    first_half = vectors[..., :halves]
    second_half = vectors[..., halves:]
    return jnp.concatenate(
        [
            first_half * cosine - second_half * sine_part,
            second_half * cosine + first_half * sine_part,
        ],
        axis=-1,
    )


def expert_rows(row_set, gate_up, down_rows):
    gate_and_up = jnp.dot(row_set, gate_up, preferred_element_type=jnp.float32)
    inner_width = gate_and_up.shape[1] // 2
    hidden = (jax.nn.silu(gate_and_up[:, :inner_width]) * gate_and_up[:, inner_width:]).astype(
        jnp.bfloat16
    )
    return jnp.dot(hidden, down_rows, preferred_element_type=jnp.float32).astype(jnp.bfloat16)


def attend_rows(query_blk, keys_blk, vals_blk, visible, scale_qk):
    scores = (
        jnp.einsum("qkgd,skd->kgqs", query_blk, keys_blk, preferred_element_type=jnp.float32)
        * scale_qk
    )
    weights_f = jnp.where(visible[None, None], jnp.exp(scores), 0.0)
    prob_bf = (weights_f / jnp.sum(weights_f, axis=-1, keepdims=True)).astype(jnp.bfloat16)
    return jnp.einsum("kgqs,skd->qkgd", prob_bf, vals_blk, preferred_element_type=jnp.float32)


def shards(
    tokens,
    positions,
    attn_gain,
    w_query,
    w_keyval,
    w_out,
    moe_gain,
    router,
    w_gate_up,
    w_down,
    expert_ids,
    cache_slot,
    kv_cache,
):
    lane_count = lax.axis_size("hd")
    group_count = lax.axis_size("grp")
    tok_rows = tokens.shape[0]
    model_width = tokens.shape[1]
    block_len = positions.shape[0]
    seg_most = block_len // 2
    head_dim = w_keyval.shape[2] // 2
    kv_local = w_keyval.shape[1]
    q_local = w_query.shape[1] // head_dim
    per_kv = q_local // kv_local
    expert_cap = tok_rows // 4
    normed = rms_norm(tokens, attn_gain)
    flat_kv = w_keyval.reshape(model_width, kv_local * 2 * head_dim)
    section = lax.all_gather(normed, "hd", axis=0, tiled=True)
    projected = jnp.concatenate(
        [
            jnp.dot(section, w_query, preferred_element_type=jnp.float32),
            jnp.dot(section, flat_kv, preferred_element_type=jnp.float32),
        ],
        axis=1,
    )
    angle_pos = jnp.maximum(positions, 0).astype(jnp.float32)
    queries = rotate(
        projected[:, : q_local * head_dim].reshape(block_len, q_local, head_dim), angle_pos
    ).astype(jnp.bfloat16)
    key_val = projected[:, q_local * head_dim :].reshape(block_len, kv_local, 2 * head_dim)
    rotated = rotate(key_val[:, :, :head_dim], angle_pos).astype(jnp.bfloat16)
    stored = jnp.concatenate([rotated, key_val[:, :, head_dim:].astype(jnp.bfloat16)], axis=2)
    seam_rows = passed_along(stored[block_len - seg_most :], "grp", 1)
    window = jnp.concatenate([seam_rows, stored], axis=0)
    scale_qk = head_dim ** (-0.5)
    local_rows = jnp.arange(block_len, dtype=jnp.int32)
    lowest = local_rows - jnp.maximum(positions, 0)
    pieces_out = []
    for q_block in range(2):
        first_row = q_block * seg_most
        rows_here = first_row + jnp.arange(seg_most, dtype=jnp.int32)
        cols_here = first_row - seg_most + jnp.arange(2 * seg_most, dtype=jnp.int32)
        low_here = lowest[first_row : first_row + seg_most]
        visible = (cols_here[None, :] >= low_here[:, None]) & (
            cols_here[None, :] <= rows_here[:, None]
        )
        query_blk = queries[first_row : first_row + seg_most].reshape(
            seg_most, kv_local, per_kv, head_dim
        )
        keys_blk = window[first_row : first_row + 2 * seg_most, :, :head_dim]
        vals_blk = window[first_row : first_row + 2 * seg_most, :, head_dim:]
        mixed_rows = attend_rows(query_blk, keys_blk, vals_blk, visible, scale_qk)
        pieces_out.append(mixed_rows.reshape(seg_most, q_local * head_dim).astype(jnp.bfloat16))
    attended = jnp.concatenate(pieces_out, axis=0)
    slots_dev = kv_cache.shape[0]
    capc = 2 * block_len // group_count
    live_slot = cache_slot >= 0
    owners = jnp.where(live_slot, cache_slot // slots_dev, group_count)
    owner_hit = (owners[:, None] == jnp.arange(group_count, dtype=jnp.int32)[None, :]).astype(
        jnp.bfloat16
    )
    lower_tri = (local_rows[:, None] >= local_rows[None, :]).astype(jnp.bfloat16)
    running = jnp.dot(lower_tri, owner_hit, preferred_element_type=jnp.float32)
    owner_rank = jnp.sum(running * owner_hit.astype(jnp.float32), axis=1).astype(jnp.int32) - 1
    send_rows = jnp.where(live_slot, owners * capc + owner_rank, group_count * capc)
    outgoing_cache = (
        jnp.zeros((group_count * capc, kv_local, 2 * head_dim), jnp.bfloat16)
        .at[send_rows]
        .set(stored, mode="drop")
    )
    outgoing_slots = (
        jnp.full((group_count * capc,), -1, jnp.int32)
        .at[send_rows]
        .set(cache_slot % slots_dev, mode="drop")
    )
    arrived, arrived_slots = (
        lax.all_to_all(
            outgoing_cache.reshape(group_count, capc, kv_local, 2 * head_dim),
            "grp",
            split_axis=0,
            concat_axis=0,
            tiled=True,
        ),
        lax.all_to_all(
            outgoing_slots.reshape(group_count, capc),
            "grp",
            split_axis=0,
            concat_axis=0,
            tiled=True,
        ),
    )
    flat_slots = arrived_slots.reshape(group_count * capc)
    write_rows = jnp.where(flat_slots >= 0, flat_slots, slots_dev).astype(jnp.int32)
    cache_after = kv_cache.at[write_rows].set(
        arrived.reshape(group_count * capc, kv_local, 2 * head_dim), mode="drop"
    )
    by_token = lax.all_to_all(attended, "hd", split_axis=0, concat_axis=1, tiled=True)
    attn_proj = jnp.dot(
        by_token,
        lax.all_gather(w_out, "grp", axis=1, tiled=True),
        preferred_element_type=jnp.float32,
    )
    residual = (tokens.astype(jnp.float32) + attn_proj).astype(jnp.bfloat16)
    moe_in = rms_norm(residual, moe_gain)
    logits = jnp.dot(moe_in, router, preferred_element_type=jnp.float32)
    expert_range = jnp.arange(router.shape[1], dtype=jnp.int32)
    matches_all = expert_ids[:, :, None] == expert_range[None, None, :]
    chosen = jnp.sum(jnp.where(matches_all, logits[:, None, :], 0.0), axis=2)
    raised = jnp.exp(chosen)
    gates = raised / jnp.sum(raised, axis=1, keepdims=True)
    live_range = jnp.arange(lane_count, dtype=jnp.int32)
    matches = expert_ids[:, :, None] == live_range[None, None, :]
    member = jnp.any(matches, axis=1)
    weighting = jnp.sum(jnp.where(matches, gates[:, :, None], 0.0), axis=1)
    ranking = jnp.cumsum(member.astype(jnp.int32), axis=0) - 1
    target = jnp.where(member, live_range[None, :] * expert_cap + ranking, -1)
    slot_range = jnp.arange(lane_count * expert_cap, dtype=jnp.int32)
    slot_hits = target[None, :, :] == slot_range[:, None, None]
    placing = jnp.any(slot_hits, axis=2).astype(jnp.bfloat16)
    outgoing = (
        jnp.dot(placing, moe_in, preferred_element_type=jnp.float32)
        .astype(jnp.bfloat16)
        .reshape(lane_count, expert_cap, model_width)
    )
    gate_up_all, down_all = (
        lax.all_gather(w_gate_up, "grp", axis=1, tiled=True),
        lax.all_gather(w_down, "grp", axis=1, tiled=True),
    )
    gate_up_mat = gate_up_all[0]
    down_mat = down_all[0]
    landed = lax.all_to_all(outgoing, "hd", split_axis=0, concat_axis=0, tiled=True)
    results = expert_rows(landed.reshape(-1, model_width), gate_up_mat, down_mat).reshape(landed.shape)
    returned = lax.all_to_all(results, "hd", split_axis=0, concat_axis=0, tiled=True)
    flat_returned = returned.reshape(-1, model_width)
    fetched = flat_returned[jnp.maximum(target, 0)]
    used_weight = jnp.where(member, weighting, 0.0)
    moe_total = jnp.sum(used_weight[:, :, None] * fetched.astype(jnp.float32), axis=1)
    layer_out = (residual.astype(jnp.float32) + moe_total).astype(jnp.bfloat16)
    return (layer_out, cache_after)


def solution(mesh):
    two_lanes = mesh.shape["hd"] == 2 and mesh.shape["grp"] % 8 == 0
    return jax.shard_map(
        two_lane_shards if two_lanes else shards,
        mesh=mesh,
        in_specs=(
            P(("grp", "hd"), None),
            P("grp"),
            P(),
            P(None, "hd"),
            P(None, "hd", None),
            P(None, "grp"),
            P(),
            P(),
            P("hd", "grp", None),
            P("hd", "grp", None),
            P(("grp", "hd"), None),
            P("grp"),
            P("grp", "hd", None),
        ),
        out_specs=(P(("grp", "hd"), None), P("grp", "hd", None)),
        check_vma=False,
    )
```

```python
import functools

import jax
import jax.numpy as jnp
import numpy as np
from jax import lax
from jax.experimental import pallas as pl
from jax.experimental.pallas import tpu as pltpu
from jax.sharding import PartitionSpec as P

norm_eps = 1e-05
rope_base = 10000.0
bf16 = jnp.bfloat16
f32 = jnp.float32
LAST_DIMS = (((1,), (1,)), ((), ()))


def ring_cycle(groups):
    rows = groups // 4
    return [2 * r for r in range(rows)] + [2 * r + 1 for r in reversed(range(rows))]


def ring_pairs(groups):
    cycle = ring_cycle(groups)
    count = len(cycle)
    pairs = []
    for place, pair in enumerate(cycle):
        pairs.append((2 * pair, 2 * cycle[(place + 1) % count]))
        pairs.append((2 * pair + 1, 2 * cycle[(place - 1) % count] + 1))
    return pairs


def sibling_pairs(groups):
    return [(g, g ^ 1) for g in range(groups)]


def ring_sources(groups, me):
    count = groups // 2
    rows = count // 2
    side, pair = me % 2, me // 2
    row, col = pair // 2, pair % 2
    place = jnp.where(col == 0, row, count - 1 - row)

    def block(core, steps):
        there = (place + (2 * core - 1) * steps + count) % count
        other = jnp.where(there < rows, 2 * there, 2 * (count - 1 - there) + 1)
        return [2 * other + core, 2 * other + 1 - core]

    full = (count - 1) // 2
    listed = [me, me + 1 - 2 * side]
    for core in (side, 1 - side):
        for steps in range(1, full + 1):
            listed += block(core, steps)
    return listed + [block(side, count // 2)[0], block(1 - side, count // 2)[0]]


class Ring:
    def __init__(self, pair, groups):
        self.across = functools.partial(lax.ppermute, axis_name="grp", perm=ring_pairs(groups))
        self.beside = functools.partial(lax.ppermute, axis_name="grp", perm=sibling_pairs(groups))
        self.full = (groups // 2 - 1) // 2
        self.unit_rows = pair.shape[0] // 2
        self.mine = [pair]
        self.near = []

    def step(self):
        held = self.mine[-1]
        if len(self.mine) > self.full:
            held = held[: self.unit_rows]
        self.mine.append(self.across(held))

    def pin(self, *others):
        done = lax.optimization_barrier((self.mine[-1],) + others)
        self.mine[-1] = done[0]
        return done[1:] if len(others) > 1 else done[1]

    def share(self, upto=None):
        for index in range(1 + len(self.near), 1 + (upto or len(self.mine) - 1)):
            self.near.append(self.beside(self.mine[index]))

    def parts(self):
        full = self.full
        return self.mine[: full + 1] + self.near[:full] + [self.mine[full + 1], self.near[full]]

    def split(self):
        full = self.full
        listed = [(part, 2 * index) for index, part in enumerate(self.parts()[:-1])]
        listed.append((self.near[full], 4 * full + 3))
        late = (full, 2 * full, 2 * full + 1, 2 * full + 2)
        return (
            [pair for index, pair in enumerate(listed) if index not in late],
            [listed[index] for index in late],
        )


def place_parts(groups, parts, unit_rows, pieces, shards=None):
    sources = ring_sources(groups, lax.axis_index("grp"))
    shard = 0
    for index, part in enumerate(parts):
        shard = shards[index] if shards else shard
        for unit in range(part.shape[0] // unit_rows):
            for first, rows, target, lane in pieces:
                at = pl.multiple_of(sources[shard] * rows, rows)
                start = unit * unit_rows + first
                target[pl.ds(at, rows), lane : lane + part.shape[1]] = part[start : start + rows, :]
            shard += 1


VMEM = pl.BlockSpec(memory_space=pltpu.VMEM)
ANY = pl.BlockSpec(memory_space=pl.ANY)
HBM = pl.BlockSpec(memory_space=pltpu.HBM)
PARAMS = pltpu.CompilerParams(vmem_limit_bytes=16 << 20)


LITTLE = pl.CostEstimate(flops=1, bytes_accessed=1, transcendentals=0)


def takes(us):
    return pl.CostEstimate(
        flops=int(us * 1.15e9), bytes_accessed=int(us * 8e6), transcendentals=0
    )


def reads(nbytes):
    return pl.CostEstimate(flops=1, bytes_accessed=nbytes, transcendentals=0)


def normalized(floats, gain):
    factor = lax.rsqrt(jnp.mean(floats * floats, axis=-1, keepdims=True) + norm_eps)
    return (floats * factor * gain).astype(bf16)


def fetch(pairs, sems):
    copies = []
    for index, (source, target) in enumerate(pairs):
        copies.append(pltpu.make_async_copy(source, target, sems.at[index]))
        copies[-1].start()
    return copies


def pack_kernel(*refs):
    sources, (expert_pair, out_pair, sems) = refs[:6], refs[6:]
    width = expert_pair.shape[1]
    lane = lax.axis_index("hd")
    first = pl.multiple_of(lane * out_pair.shape[1], out_pair.shape[1])
    pairs = []
    row = 0
    for index in range(2):
        up, down, w_out = sources[3 * index : 3 * index + 3]
        count = w_out.shape[0]
        pairs.append(
            (w_out.at[:, pl.ds(first, out_pair.shape[1])], out_pair.at[pl.ds(index * count, count), :])
        )
        for source in (up, down):
            for at in range(0, source.shape[1], width):
                pairs.append(
                    (source.at[:, pl.ds(at, width)], expert_pair.at[pl.ds(row, source.shape[0]), :])
                )
                row += source.shape[0]
    for copy in fetch(pairs, sems):
        copy.wait()


def pack(own, beside):
    own = [pltpu.with_memory_space_constraint(part, pltpu.HBM) for part in own]
    up, down, w_out_t = own
    width = up.shape[1] // 2
    pieces = [up.shape[1] // width, down.shape[1] // width]
    unit_rows = pieces[0] * up.shape[0] + pieces[1] * down.shape[0]
    return pl.pallas_call(
        pack_kernel,
        out_shape=(
            jax.ShapeDtypeStruct((2 * unit_rows, width), bf16),
            jax.ShapeDtypeStruct((2 * w_out_t.shape[0], w_out_t.shape[1] // 2), bf16),
        ),
        in_specs=[ANY] * 6,
        out_specs=(ANY, ANY),
        scratch_shapes=[pltpu.SemaphoreType.DMA((2 + 2 * sum(pieces),))],
        compiler_params=PARAMS,
        cost_estimate=LITTLE,
        name="pack",
    )(*own, *beside)


def as_column(row, eye):
    return jnp.sum(jnp.where(eye, row, 0.0), axis=1, keepdims=True)


def named_experts(ids, experts):
    tokens = ids.shape[1]
    expert = lax.broadcasted_iota(jnp.int32, (experts, tokens), 0)
    hit = jnp.zeros((experts, tokens), f32)
    for index in range(ids.shape[0]):
        hit = jnp.where(ids[index : index + 1, :] == expert, 1.0, hit)
    return hit


def prepare_kernel(groups, slots_dev, *refs):
    sources, (cosine, sine, past, place, send, tags, gain) = refs[:4], refs[4:11]
    positions, slots, ids, flat_gain, sems = refs[11:]
    copies = fetch(list(zip(sources, (positions, slots, ids, flat_gain))), sems)
    for copy in copies:
        copy.wait()
    gain[...] = flat_gain[...].reshape(gain.shape)
    lane = lax.axis_index("hd")
    block = positions.shape[1]

    def iota(shape, dim):
        return lax.broadcasted_iota(jnp.int32, shape, dim)

    eye = iota((block, block), 0) == iota((block, block), 1)
    reach = as_column(jnp.maximum(positions[...], 0).astype(f32), eye)
    past[...] = jnp.broadcast_to(reach, past.shape)
    column = iota((8, 128), 1)
    exponent = (column % 32).astype(f32) * (-2.0 / 64)
    inverse_freq = jnp.exp(exponent * np.float32(np.log(rope_base)))[:1, :]
    angles = reach * inverse_freq
    cosine[...] = jnp.cos(angles)
    turned = jnp.sin(angles)
    sine[...] = jnp.where(iota(angles.shape, 1) % 64 < 32, -turned, turned)

    tokens = ids.shape[1]
    cap = place.shape[0] // 2
    hit = named_experts(ids, 8)
    upto = (iota((tokens, tokens), 0) <= iota((tokens, tokens), 1)).astype(f32)
    rank = jnp.dot(hit, upto, preferred_element_type=f32) - 1.0
    slot = iota((2 * cap, tokens), 0).astype(f32)
    placed = jnp.zeros((2 * cap, tokens), f32)
    for live in range(2):
        order = jnp.where(lane == live, 0, cap).astype(f32)
        member = hit[live : live + 1, :] > 0.0
        placed = jnp.where(member & (slot == rank[live : live + 1, :] + order), 1.0, placed)
    place[...] = placed.astype(bf16)

    where = slots[...]
    owner = jnp.where(where >= 0, where // slots_dev, -1)
    owner_hit = (iota((groups, block), 0) == owner).astype(f32)
    before = (iota((block, block), 0) <= iota((block, block), 1)).astype(f32)
    running = jnp.dot(owner_hit, before, preferred_element_type=f32)
    owner_rank = jnp.sum(owner_hit * running, axis=0, keepdims=True) - 1.0
    capc = send.shape[0] // groups
    row = jnp.where(owner >= 0, owner * capc + owner_rank.astype(jnp.int32), -1)
    send[...] = (iota(send.shape, 0) == row).astype(bf16)
    inside = jnp.where(where >= 0, where % slots_dev, 0)
    high = as_column((inside // 64 + 1).astype(f32), eye)
    low = as_column((inside % 64).astype(f32), eye)
    spot = iota(tags.shape, 1)
    tags[...] = jnp.where(spot == 0, high, jnp.where(spot == 1, low, 0.0)).astype(bf16)


def prepare(groups, slots_dev, positions, slots, ids, gain):
    block, tokens = positions.shape[0], ids.shape[0]
    model = gain.shape[0]
    cap = tokens // 4
    capc = 2 * block // groups
    shapes = [
        ((block, 128), f32),
        ((block, 128), f32),
        ((block, 128), f32),
        ((2 * cap, tokens), bf16),
        ((groups * capc, block), bf16),
        ((block, 128), bf16),
        ((1, model), f32),
    ]
    sources = (positions[None], slots[None], ids.T, gain)
    return pl.pallas_call(
        functools.partial(prepare_kernel, groups, slots_dev),
        out_shape=tuple(jax.ShapeDtypeStruct(shape, kind) for shape, kind in shapes),
        in_specs=[ANY] * 4,
        out_specs=(VMEM,) * len(shapes),
        scratch_shapes=[
            pltpu.VMEM((1, block), jnp.int32),
            pltpu.VMEM((1, block), jnp.int32),
            pltpu.VMEM(ids.shape[::-1], jnp.int32),
            pltpu.VMEM((model,), f32),
            pltpu.SemaphoreType.DMA((4,)),
        ],
        compiler_params=PARAMS,
        cost_estimate=LITTLE,
        name="prepare",
    )(*[pltpu.with_memory_space_constraint(source, pltpu.HBM) for source in sources])


def project_kernel(
    own, other, gain, cosine, sine, w_query, w_keyval, q_out, kv_out, seam_out, raw, rows, sems
):
    count = own.shape[0]
    lane = lax.axis_index("hd")
    mine = pl.multiple_of(lane * count, count)
    theirs = pl.multiple_of((1 - lane) * count, count)
    copies = fetch([(own, raw.at[0]), (other, raw.at[1])], sems)
    cos_q, sin_q = cosine[...], sine[...]
    column = lax.broadcasted_iota(jnp.int32, cos_q.shape, 1)
    lower = column % 64 < 32
    cos_kv = jnp.where(column < 64, cos_q, 1.0)
    sin_kv = jnp.where(column < 64, sin_q, 0.0)
    for index, first in ((0, mine), (1, theirs)):
        copies[index].wait()
        rows[pl.ds(first, count), :] = normalized(raw[index].astype(f32), gain[...])
    width = 256
    for weights, out, cos, sin in ((w_keyval, kv_out, cos_kv, sin_kv), (w_query, q_out, cos_q, sin_q)):
        for first in range(0, weights.shape[1], width):
            made = jnp.dot(rows[...], weights[:, first : first + width], preferred_element_type=f32)
            for part in range(0, width, 128):
                here = made[:, part : part + 128]
                turned = jnp.where(lower, pltpu.roll(here, 96, 1), pltpu.roll(here, 32, 1))
                done = (here * cos + turned * sin).astype(bf16)
                out[:, first + part : first + part + 128] = done
                if out is kv_out:
                    seam_out[:, first + part : first + part + 128] = done[count:, :]


def project(own, other, gain, cosine, sine, w_query, flat_kv):
    count, width = own.shape
    made = w_query.shape[1] + flat_kv.shape[1]
    return pl.pallas_call(
        project_kernel,
        out_shape=(
            jax.ShapeDtypeStruct((2 * count, w_query.shape[1]), bf16),
            jax.ShapeDtypeStruct((2 * count, flat_kv.shape[1]), bf16),
            jax.ShapeDtypeStruct((count, flat_kv.shape[1]), bf16),
        ),
        in_specs=[ANY] * 2 + [VMEM] * 5,
        out_specs=(VMEM, VMEM, VMEM),
        scratch_shapes=[
            pltpu.VMEM((2, count, width), bf16),
            pltpu.VMEM((2 * count, width), bf16),
            pltpu.SemaphoreType.DMA((2,)),
        ],
        compiler_params=PARAMS,
        cost_estimate=takes(8),
        name="project",
    )(own, other, gain, cosine, sine, w_query, flat_kv)


def attend_rows_kernel(first, q, kv, seam, past, mixed, window, sem):
    count = q.shape[0] // 2
    if first == 0:
        copy = pltpu.make_async_copy(seam, window.at[pl.ds(0, count), :], sem)
        copy.start()
        window[count:, :] = kv[:count, :]
        copy.wait()
        keyed = window
    else:
        keyed = kv
    head = 64
    kv_heads = kv.shape[1] // (2 * head)
    per_kv = q.shape[1] // head // kv_heads
    shape = (count, 2 * count)
    row = lax.broadcasted_iota(jnp.int32, shape, 0) + count
    col = lax.broadcasted_iota(jnp.int32, shape, 1)
    reach = past[first : first + count, :1].astype(jnp.int32)
    visible = (col <= row) & (col >= row - reach)
    for kv_head in range(kv_heads):
        lanes = 2 * head * kv_head
        keys = keyed[:, lanes : lanes + head]
        values = keyed[:, lanes + head : lanes + 2 * head]
        for index in range(per_kv):
            at = (kv_head * per_kv + index) * head
            query = q[first : first + count, at : at + head]
            scores = lax.dot_general(query, keys, LAST_DIMS, preferred_element_type=f32)
            raised = jnp.where(visible, jnp.exp(scores * head ** (-0.5)), 0.0)
            probs = (raised / jnp.sum(raised, axis=-1, keepdims=True)).astype(bf16)
            made = jnp.dot(probs, values, preferred_element_type=f32)
            mixed[:, at : at + head] = made.astype(bf16)


def attend_late(q, kv, past):
    def kernel(q, kv, past, mixed):
        attend_rows_kernel(q.shape[0] // 2, q, kv, None, past, mixed, None, None)

    return pl.pallas_call(
        kernel,
        out_shape=jax.ShapeDtypeStruct((q.shape[0] // 2, q.shape[1]), bf16),
        in_specs=[VMEM] * 3,
        out_specs=VMEM,
        compiler_params=PARAMS,
        cost_estimate=takes(2),
        name="attend_late",
    )(q, kv, past)


def attend_early(q, kv, seam, past):
    return pl.pallas_call(
        functools.partial(attend_rows_kernel, 0),
        out_shape=jax.ShapeDtypeStruct((q.shape[0] // 2, q.shape[1]), bf16),
        in_specs=[VMEM, VMEM, ANY, VMEM],
        out_specs=VMEM,
        scratch_shapes=[pltpu.VMEM(kv.shape, bf16), pltpu.SemaphoreType.DMA],
        compiler_params=PARAMS,
        cost_estimate=takes(2),
        name="attend_early",
    )(q, kv, seam, past)


def outward_rows(flip, groups, unit_rows, early, late, parts, w_out, rows):
    place_parts(groups, parts, unit_rows, [(0, unit_rows, w_out, 0)])
    lane = lax.axis_index("hd")
    which = (1 - lane) if flip else lane

    @pl.when(which == 0)
    def _():
        rows[...] = early[...]

    @pl.when(which != 0)
    def _():
        rows[...] = late[...]

    return lax.dot_general(rows[...], w_out[...], LAST_DIMS, preferred_element_type=f32)


def send_kernel(groups, unit_rows, n_parts, early, late, *refs):
    parts, (out, w_out, rows) = refs[:n_parts], refs[n_parts:]
    out[...] = outward_rows(True, groups, unit_rows, early, late, parts, w_out, rows).astype(bf16)


def keep_kernel(groups, unit_rows, n_parts, early, late, tokens, flat_gain, *refs):
    parts, (out, gain, w_out, rows) = refs[:n_parts], refs[n_parts:]
    gain[...] = flat_gain[...].reshape(gain.shape)
    made = outward_rows(False, groups, unit_rows, early, late, parts, w_out, rows)
    out[...] = tokens[...].astype(f32) + made


def outward_send(groups, early, late, parts, unit_rows):
    width, depth = groups * unit_rows, parts[0].shape[1]
    return pl.pallas_call(
        functools.partial(send_kernel, groups, unit_rows, len(parts)),
        out_shape=jax.ShapeDtypeStruct((early.shape[0], width), bf16),
        in_specs=[VMEM] * (2 + len(parts)),
        out_specs=VMEM,
        scratch_shapes=[pltpu.VMEM((width, depth), bf16), pltpu.VMEM(early.shape, bf16)],
        compiler_params=PARAMS,
        cost_estimate=reads(2 * width * depth),
        name="outward_send",
    )(early, late, *parts)


def outward_keep(groups, early, late, tokens, gain, parts, unit_rows):
    width, depth = groups * unit_rows, parts[0].shape[1]
    return pl.pallas_call(
        functools.partial(keep_kernel, groups, unit_rows, len(parts)),
        out_shape=(
            jax.ShapeDtypeStruct(tokens.shape, f32),
            jax.ShapeDtypeStruct((1, width), f32),
        ),
        in_specs=[VMEM] * (4 + len(parts)),
        out_specs=(VMEM, VMEM),
        scratch_shapes=[
            pltpu.VMEM((width, depth), bf16),
            pltpu.VMEM(early.shape, bf16),
        ],
        compiler_params=PARAMS,
        cost_estimate=reads(2 * width * depth),
        name="outward_keep",
    )(early, late, tokens, gain, *parts)


def route_kernel(mine, arrived, gain, place, residual, moe_in, sent):
    added = (mine[...] + arrived[...].astype(f32)).astype(bf16)
    residual[...] = added
    moe_in[...] = normalized(added.astype(f32), gain[...])
    cap = sent.shape[0]
    rows = jnp.dot(place[cap:, :], moe_in[...], preferred_element_type=f32)
    sent[...] = rows.astype(bf16)


def route(mine, arrived, gain, place):
    cap = place.shape[0] // 2
    return pl.pallas_call(
        route_kernel,
        out_shape=(
            jax.ShapeDtypeStruct(mine.shape, bf16),
            jax.ShapeDtypeStruct(mine.shape, bf16),
            jax.ShapeDtypeStruct((cap, mine.shape[1]), bf16),
        ),
        in_specs=[VMEM] * 4,
        out_specs=(VMEM,) * 3,
        compiler_params=PARAMS,
        cost_estimate=reads(10 * mine.shape[0] * mine.shape[1]),
        name="route",
    )(mine, arrived, gain, place)


def gate_kernel(moe_in, router, ids, place, gates, own, spread):
    cap = own.shape[0]
    own[...] = jnp.dot(place[:cap, :], moe_in[...], preferred_element_type=f32).astype(bf16)
    hit = named_experts(ids, router.shape[0])
    tokens = ids.shape[1]
    row = lax.broadcasted_iota(jnp.int32, (tokens, tokens), 0)
    eye = (row == lax.broadcasted_iota(jnp.int32, (tokens, tokens), 1)).astype(f32)
    named = lax.dot_general(eye, hit, LAST_DIMS, preferred_element_type=f32)
    spread[...] = lax.dot_general(
        eye.astype(bf16), place[...], LAST_DIMS, preferred_element_type=f32
    ).astype(bf16)
    logits = lax.dot_general(moe_in[...], router[...], LAST_DIMS, preferred_element_type=f32)
    raised = jnp.where(named > 0, jnp.exp(logits), 0.0)
    gates[...] = raised / jnp.sum(raised, axis=-1, keepdims=True)


def gate(moe_in, router_t, ids_t, place):
    cap = place.shape[0] // 2
    return pl.pallas_call(
        gate_kernel,
        out_shape=(
            jax.ShapeDtypeStruct((moe_in.shape[0], router_t.shape[0]), f32),
            jax.ShapeDtypeStruct((cap, moe_in.shape[1]), bf16),
            jax.ShapeDtypeStruct(place.shape[::-1], bf16),
        ),
        in_specs=[VMEM] * 4,
        out_specs=(VMEM,) * 3,
        compiler_params=PARAMS,
        cost_estimate=LITTLE,
        name="gate",
    )(moe_in, router_t, ids_t, place)


def expert_pieces(gate_up, down, up_rows, down_rows, width):
    pieces = [(i * up_rows, up_rows, gate_up, i * width) for i in range(2)]
    pieces += [
        (2 * up_rows + i * down_rows, down_rows, down, i * width) for i in range(down.shape[1] // width)
    ]
    return pieces, pieces[-1][0] + down_rows


def stage_kernel(groups, up_rows, down_rows, shards, *refs):
    parts, (gate_up, down) = refs[: len(shards)], refs[len(shards) :]
    pieces, unit_rows = expert_pieces(gate_up, down, up_rows, down_rows, parts[0].shape[1])
    place_parts(groups, parts, unit_rows, pieces, shards)


def stage(groups, early, up_rows, down_rows, model):
    width = early[0][0].shape[1]
    return pl.pallas_call(
        functools.partial(stage_kernel, groups, up_rows, down_rows, [shard for _, shard in early]),
        out_shape=(
            jax.ShapeDtypeStruct((groups * up_rows, 2 * width), bf16),
            jax.ShapeDtypeStruct((groups * down_rows, model), bf16),
        ),
        in_specs=[VMEM] * len(early),
        out_specs=(VMEM, VMEM),
        compiler_params=PARAMS,
        cost_estimate=reads(2 * groups * 2 * (up_rows * 2 * width + down_rows * model)),
        name="stage",
    )(*[part for part, _ in early])


def expert_kernel(groups, up_rows, down_rows, shards, own, other, gate_up_in, down_in, *refs):
    parts = refs[: len(shards)]
    own_out, other_out, gate_up, down, rows = refs[len(shards) :]
    width = parts[0].shape[1]
    count = own.shape[0]
    rows[:count, :] = own[...]
    rows[count:, :] = other[...]
    pieces, unit_rows = expert_pieces(gate_up, down, up_rows, down_rows, width)
    place_parts(groups, parts, unit_rows, pieces, shards)
    both = jnp.dot(rows[...], gate_up[...], preferred_element_type=f32)
    gate, up = both[:, :width], both[:, width:]
    hidden = (gate / (1.0 + jnp.exp(-gate)) * up).astype(bf16)
    made = jnp.dot(hidden, down[...], preferred_element_type=f32).astype(bf16)
    own_out[...] = made[:count, :]
    other_out[...] = made[count:, :]


def expert(groups, own, other, staged, late, up_rows, down_rows):
    count, model = own.shape
    width = late[0][0].shape[1]
    return pl.pallas_call(
        functools.partial(expert_kernel, groups, up_rows, down_rows, [shard for _, shard in late]),
        out_shape=(jax.ShapeDtypeStruct(own.shape, bf16),) * 2
        + tuple(jax.ShapeDtypeStruct(part.shape, bf16) for part in staged),
        in_specs=[VMEM] * (4 + len(late)),
        out_specs=(VMEM,) * 4,
        scratch_shapes=[pltpu.VMEM((2 * count, model), bf16)],
        input_output_aliases={2: 2, 3: 3},
        compiler_params=PARAMS,
        cost_estimate=takes(6.2),
        name="expert",
    )(own, other, *staged, *[part for part, _ in late])[:2]


def combine_kernel(residual, gates, spread, own, returned, out):
    lane = lax.axis_index("hd")
    count = own.shape[0]
    column = lax.broadcasted_iota(jnp.int32, gates.shape, 1)
    total = jnp.zeros(residual.shape, f32)
    for index, made in ((0, own), (1, returned)):
        live = lane if index == 0 else 1 - lane
        weight = jnp.sum(jnp.where(column == live, gates[...], 0.0), axis=-1, keepdims=True)
        picked = jnp.dot(
            spread[:, index * count : (index + 1) * count], made[...], preferred_element_type=f32
        )
        total += weight * picked
    out[...] = (residual[...].astype(f32) + total).astype(bf16)


def combine(residual, gates, spread, own, returned):
    return pl.pallas_call(
        combine_kernel,
        out_shape=jax.ShapeDtypeStruct(residual.shape, bf16),
        in_specs=[VMEM] * 5,
        out_specs=VMEM,
        compiler_params=PARAMS,
        cost_estimate=reads(6 * residual.shape[0] * residual.shape[1]),
        name="combine",
    )(residual, gates, spread, own, returned)


def bundle_kernel(send, kv, tags, result, out, sem):
    groups, rows, _ = out.shape
    heads = kv.shape[1] // 128
    capc = send.shape[0] // groups
    packed = jnp.dot(send[...], kv[...], preferred_element_type=f32).astype(bf16)
    tagged = jnp.dot(send[...], tags[...], preferred_element_type=f32)
    one = (lax.broadcasted_iota(jnp.int32, (16, 128), 0) == lax.broadcasted_iota(jnp.int32, (16, 128), 1))
    for owner in range(groups):
        mine = slice(owner * capc, (owner + 1) * capc)
        for head in range(heads):
            out[owner, head * capc : (head + 1) * capc, :] = packed[mine, head * 128 : (head + 1) * 128]
        wide = jnp.concatenate([tagged[mine, :], jnp.zeros((128 - capc, 128), f32)], axis=0)
        out[owner, heads * capc :, :] = lax.dot_general(
            one.astype(f32), wide, LAST_DIMS, preferred_element_type=f32
        ).astype(bf16)
    copy = pltpu.make_async_copy(out, result, sem)
    copy.start()
    copy.wait()


def bundle(groups, send, kv, tags):
    rows = send.shape[0] // groups * (kv.shape[1] // 128) + 16
    return pl.pallas_call(
        bundle_kernel,
        out_shape=pltpu.HBM((groups, rows, 128), bf16),
        in_specs=[VMEM] * 3,
        out_specs=HBM,
        scratch_shapes=[pltpu.VMEM((groups, rows, 128), bf16), pltpu.SemaphoreType.DMA],
        compiler_params=PARAMS,
        cost_estimate=LITTLE,
        name="bundle",
    )(send, kv, tags)


def write_kernel(heads, arrived, cache, out, rows, wide, known):
    groups, size, _ = arrived.shape
    slots = cache.shape[0] // heads
    capc = (size - 16) // heads
    high, low = [], []
    for source in range(groups):
        for head in range(heads):
            rows[source * capc : (source + 1) * capc, head * 128 : (head + 1) * 128] = arrived[
                source, head * capc : (head + 1) * capc, :
            ]
        numbers = arrived[source, heads * capc :, :].astype(f32)
        high.append(numbers[0:1, :capc])
        low.append(numbers[1:2, :capc])
    slot = jnp.concatenate(high, axis=1) * 64.0 + jnp.concatenate(low, axis=1) - 64.0
    row = lax.broadcasted_iota(jnp.int32, (slots, slot.shape[1]), 0).astype(f32)
    hit = (row == slot).astype(bf16)
    made = jnp.dot(hit, rows[...], preferred_element_type=f32)
    found = jnp.dot(hit, jnp.ones((slot.shape[1], 128), bf16), preferred_element_type=f32)
    for head in range(heads):
        wide[pl.ds(head, slots, heads), :] = made[:, head * 128 : (head + 1) * 128]
        known[pl.ds(head, slots, heads), :] = found
    old = cache[...].astype(f32)
    out[...] = jnp.where(known[...] > 0.0, wide[...], old).astype(bf16)


def write(arrived, cache):
    slots, heads, lanes = cache.shape
    capc = (arrived.shape[1] - 16) // heads
    flat = (slots * heads, lanes)
    written = pl.pallas_call(
        functools.partial(write_kernel, heads),
        out_shape=jax.ShapeDtypeStruct(flat, bf16),
        in_specs=[VMEM] * 2,
        out_specs=VMEM,
        scratch_shapes=[
            pltpu.VMEM((arrived.shape[0] * capc, heads * lanes), bf16),
            pltpu.VMEM(flat, f32),
            pltpu.VMEM(flat, f32),
        ],
        compiler_params=PARAMS,
        cost_estimate=reads(1 << 21),
        name="write",
    )(arrived, cache.reshape(flat))
    return written.reshape(cache.shape)


def two_lane_shards(
    tokens,
    positions,
    attn_gain,
    w_query,
    w_keyval,
    w_out,
    moe_gain,
    router,
    w_gate_up,
    w_down,
    expert_ids,
    cache_slot,
    kv_cache,
):
    groups = lax.axis_size("grp")
    tok_rows, model = tokens.shape
    block = positions.shape[0]
    kv_local, head2 = w_keyval.shape[1:]
    kv_width = kv_local * head2
    slots_dev = kv_cache.shape[0]
    swap = functools.partial(lax.ppermute, axis_name="hd", perm=[(0, 1), (1, 0)])

    together = lax.optimization_barrier

    other_tokens = swap(tokens)
    own = (w_gate_up[0], w_down[0], w_out.T)
    up_rows, down_rows = own[0].shape[0], own[1].shape[0]
    beside = [lax.ppermute(part, "grp", sibling_pairs(groups)) for part in own]
    expert_pair, out_pair = pack(own, beside)
    out_ring = Ring(out_pair, groups)
    out_ring.step()
    expert_ring = Ring(expert_pair, groups)
    expert_ring.step()
    w_keyval, positions = together((w_keyval, positions, out_pair))[:2]
    flat_kv = w_keyval.reshape(model, kv_width)
    cosine, sine, past, place, send, tags, gain = prepare(
        groups, slots_dev, positions, cache_slot, expert_ids, attn_gain
    )
    other_tokens, cosine, flat_kv = out_ring.pin(other_tokens, cosine, flat_kv)
    out_ring.step()

    q, kv, tail = project(tokens, other_tokens, gain, cosine, sine, w_query, flat_kv)
    seam = lax.ppermute(tail, "grp", [(g, g + 1) for g in range(groups - 1)])
    q = out_ring.pin(q)
    out_ring.step()
    out_ring.share(2)
    late = attend_late(q, kv, past)
    seam, late = together((seam, late))
    seam = expert_ring.pin(seam)
    expert_ring.step()
    early = attend_early(q, kv, seam, past)
    early, out_ring.near = together((early, out_ring.near))
    early = out_ring.pin(early)
    out_ring.step()
    out_ring.share(3)
    early, kv, out_ring.near = together((early, kv, out_ring.near))
    outgoing = bundle(groups, send, kv, tags)
    early, outgoing = together((early, outgoing))
    early = out_ring.pin(early)
    early = expert_ring.pin(early)
    expert_ring.step()
    out_ring.share()
    sent = outward_send(groups, early, late, out_ring.parts(), out_ring.unit_rows)
    arrived = swap(sent)
    early = together((early, sent))[0]
    mine, late_gain = outward_keep(
        groups, early, late, tokens, moe_gain, out_ring.parts(), out_ring.unit_rows
    )
    late_gain = expert_ring.pin(late_gain)
    expert_ring.share()
    expert_ring.step()
    outgoing = together((outgoing, sent))[0]
    arrived_cache = lax.all_to_all(outgoing, "grp", split_axis=0, concat_axis=0, tiled=True)
    arrived, late_gain = expert_ring.pin(arrived, late_gain)
    expert_ring.share()

    residual, moe_in, sent_rows = route(mine, arrived, late_gain, place)
    landed = swap(sent_rows)
    gates, own_rows, spread = gate(moe_in, router.T, expert_ids.T, place)
    parts_early, parts_late = expert_ring.split()
    first, own_rows = together((parts_early[0][0], own_rows))
    parts_early[0] = (first, parts_early[0][1])
    staged = stage(groups, parts_early, up_rows, down_rows, model)
    landed, staged = together((landed, staged))
    own_made, back = expert(groups, own_rows, landed, staged, parts_late, up_rows, down_rows)
    returned = swap(back)
    layer_out = combine(residual, gates, spread, own_made, returned)
    layer_out, arrived_cache = together((layer_out, arrived_cache))
    cache_after = write(arrived_cache, kv_cache)
    return (layer_out, cache_after)


def passed_along(value, axis, steps):
    count = lax.axis_size(axis)
    initial, last = (max(0, -steps), min(count, count - steps))
    return lax.ppermute(value, axis, [(source, source + steps) for source in range(initial, last)])


def rms_norm(row_set, norm_gain):
    floats = row_set.astype(jnp.float32)
    factor = lax.rsqrt(jnp.mean(floats * floats, axis=-1, keepdims=True) + norm_eps)
    return (floats * factor * norm_gain).astype(jnp.bfloat16)


def rotate(vectors, angle_pos):
    halves = vectors.shape[-1] // 2
    inverse_freq = rope_base ** (-2.0 * jnp.arange(halves, dtype=jnp.float32) / vectors.shape[-1])
    angles = angle_pos[:, None, None] * inverse_freq[None, None, :]
    cosine = jnp.cos(angles)
    sine_part = jnp.sin(angles)
    first_half = vectors[..., :halves]
    second_half = vectors[..., halves:]
    return jnp.concatenate(
        [
            first_half * cosine - second_half * sine_part,
            second_half * cosine + first_half * sine_part,
        ],
        axis=-1,
    )


def expert_rows(row_set, gate_up, down_rows):
    gate_and_up = jnp.dot(row_set, gate_up, preferred_element_type=jnp.float32)
    inner_width = gate_and_up.shape[1] // 2
    hidden = (jax.nn.silu(gate_and_up[:, :inner_width]) * gate_and_up[:, inner_width:]).astype(
        jnp.bfloat16
    )
    return jnp.dot(hidden, down_rows, preferred_element_type=jnp.float32).astype(jnp.bfloat16)


def attend_rows(query_blk, keys_blk, vals_blk, visible, scale_qk):
    scores = (
        jnp.einsum("qkgd,skd->kgqs", query_blk, keys_blk, preferred_element_type=jnp.float32)
        * scale_qk
    )
    weights_f = jnp.where(visible[None, None], jnp.exp(scores), 0.0)
    prob_bf = (weights_f / jnp.sum(weights_f, axis=-1, keepdims=True)).astype(jnp.bfloat16)
    return jnp.einsum("kgqs,skd->qkgd", prob_bf, vals_blk, preferred_element_type=jnp.float32)


def shards(
    tokens,
    positions,
    attn_gain,
    w_query,
    w_keyval,
    w_out,
    moe_gain,
    router,
    w_gate_up,
    w_down,
    expert_ids,
    cache_slot,
    kv_cache,
):
    lane_count = lax.axis_size("hd")
    group_count = lax.axis_size("grp")
    tok_rows = tokens.shape[0]
    model_width = tokens.shape[1]
    block_len = positions.shape[0]
    seg_most = block_len // 2
    head_dim = w_keyval.shape[2] // 2
    kv_local = w_keyval.shape[1]
    q_local = w_query.shape[1] // head_dim
    per_kv = q_local // kv_local
    expert_cap = tok_rows // 4
    normed = rms_norm(tokens, attn_gain)
    flat_kv = w_keyval.reshape(model_width, kv_local * 2 * head_dim)
    section = lax.all_gather(normed, "hd", axis=0, tiled=True)
    projected = jnp.concatenate(
        [
            jnp.dot(section, w_query, preferred_element_type=jnp.float32),
            jnp.dot(section, flat_kv, preferred_element_type=jnp.float32),
        ],
        axis=1,
    )
    angle_pos = jnp.maximum(positions, 0).astype(jnp.float32)
    queries = rotate(
        projected[:, : q_local * head_dim].reshape(block_len, q_local, head_dim), angle_pos
    ).astype(jnp.bfloat16)
    key_val = projected[:, q_local * head_dim :].reshape(block_len, kv_local, 2 * head_dim)
    rotated = rotate(key_val[:, :, :head_dim], angle_pos).astype(jnp.bfloat16)
    stored = jnp.concatenate([rotated, key_val[:, :, head_dim:].astype(jnp.bfloat16)], axis=2)
    seam_rows = passed_along(stored[block_len - seg_most :], "grp", 1)
    window = jnp.concatenate([seam_rows, stored], axis=0)
    scale_qk = head_dim ** (-0.5)
    local_rows = jnp.arange(block_len, dtype=jnp.int32)
    lowest = local_rows - jnp.maximum(positions, 0)
    pieces_out = []
    for q_block in range(2):
        first_row = q_block * seg_most
        rows_here = first_row + jnp.arange(seg_most, dtype=jnp.int32)
        cols_here = first_row - seg_most + jnp.arange(2 * seg_most, dtype=jnp.int32)
        low_here = lowest[first_row : first_row + seg_most]
        visible = (cols_here[None, :] >= low_here[:, None]) & (
            cols_here[None, :] <= rows_here[:, None]
        )
        query_blk = queries[first_row : first_row + seg_most].reshape(
            seg_most, kv_local, per_kv, head_dim
        )
        keys_blk = window[first_row : first_row + 2 * seg_most, :, :head_dim]
        vals_blk = window[first_row : first_row + 2 * seg_most, :, head_dim:]
        mixed_rows = attend_rows(query_blk, keys_blk, vals_blk, visible, scale_qk)
        pieces_out.append(mixed_rows.reshape(seg_most, q_local * head_dim).astype(jnp.bfloat16))
    attended = jnp.concatenate(pieces_out, axis=0)
    slots_dev = kv_cache.shape[0]
    capc = 2 * block_len // group_count
    live_slot = cache_slot >= 0
    owners = jnp.where(live_slot, cache_slot // slots_dev, group_count)
    owner_hit = (owners[:, None] == jnp.arange(group_count, dtype=jnp.int32)[None, :]).astype(
        jnp.bfloat16
    )
    lower_tri = (local_rows[:, None] >= local_rows[None, :]).astype(jnp.bfloat16)
    running = jnp.dot(lower_tri, owner_hit, preferred_element_type=jnp.float32)
    owner_rank = jnp.sum(running * owner_hit.astype(jnp.float32), axis=1).astype(jnp.int32) - 1
    send_rows = jnp.where(live_slot, owners * capc + owner_rank, group_count * capc)
    outgoing_cache = (
        jnp.zeros((group_count * capc, kv_local, 2 * head_dim), jnp.bfloat16)
        .at[send_rows]
        .set(stored, mode="drop")
    )
    outgoing_slots = (
        jnp.full((group_count * capc,), -1, jnp.int32)
        .at[send_rows]
        .set(cache_slot % slots_dev, mode="drop")
    )
    arrived, arrived_slots = (
        lax.all_to_all(
            outgoing_cache.reshape(group_count, capc, kv_local, 2 * head_dim),
            "grp",
            split_axis=0,
            concat_axis=0,
            tiled=True,
        ),
        lax.all_to_all(
            outgoing_slots.reshape(group_count, capc),
            "grp",
            split_axis=0,
            concat_axis=0,
            tiled=True,
        ),
    )
    flat_slots = arrived_slots.reshape(group_count * capc)
    write_rows = jnp.where(flat_slots >= 0, flat_slots, slots_dev).astype(jnp.int32)
    cache_after = kv_cache.at[write_rows].set(
        arrived.reshape(group_count * capc, kv_local, 2 * head_dim), mode="drop"
    )
    by_token = lax.all_to_all(attended, "hd", split_axis=0, concat_axis=1, tiled=True)
    attn_proj = jnp.dot(
        by_token,
        lax.all_gather(w_out, "grp", axis=1, tiled=True),
        preferred_element_type=jnp.float32,
    )
    residual = (tokens.astype(jnp.float32) + attn_proj).astype(jnp.bfloat16)
    moe_in = rms_norm(residual, moe_gain)
    logits = jnp.dot(moe_in, router, preferred_element_type=jnp.float32)
    expert_range = jnp.arange(router.shape[1], dtype=jnp.int32)
    matches_all = expert_ids[:, :, None] == expert_range[None, None, :]
    chosen = jnp.sum(jnp.where(matches_all, logits[:, None, :], 0.0), axis=2)
    raised = jnp.exp(chosen)
    gates = raised / jnp.sum(raised, axis=1, keepdims=True)
    live_range = jnp.arange(lane_count, dtype=jnp.int32)
    matches = expert_ids[:, :, None] == live_range[None, None, :]
    member = jnp.any(matches, axis=1)
    weighting = jnp.sum(jnp.where(matches, gates[:, :, None], 0.0), axis=1)
    ranking = jnp.cumsum(member.astype(jnp.int32), axis=0) - 1
    target = jnp.where(member, live_range[None, :] * expert_cap + ranking, -1)
    slot_range = jnp.arange(lane_count * expert_cap, dtype=jnp.int32)
    slot_hits = target[None, :, :] == slot_range[:, None, None]
    placing = jnp.any(slot_hits, axis=2).astype(jnp.bfloat16)
    outgoing = (
        jnp.dot(placing, moe_in, preferred_element_type=jnp.float32)
        .astype(jnp.bfloat16)
        .reshape(lane_count, expert_cap, model_width)
    )
    gate_up_all, down_all = (
        lax.all_gather(w_gate_up, "grp", axis=1, tiled=True),
        lax.all_gather(w_down, "grp", axis=1, tiled=True),
    )
    gate_up_mat = gate_up_all[0]
    down_mat = down_all[0]
    landed = lax.all_to_all(outgoing, "hd", split_axis=0, concat_axis=0, tiled=True)
    results = expert_rows(landed.reshape(-1, model_width), gate_up_mat, down_mat).reshape(landed.shape)
    returned = lax.all_to_all(results, "hd", split_axis=0, concat_axis=0, tiled=True)
    flat_returned = returned.reshape(-1, model_width)
    fetched = flat_returned[jnp.maximum(target, 0)]
    used_weight = jnp.where(member, weighting, 0.0)
    moe_total = jnp.sum(used_weight[:, :, None] * fetched.astype(jnp.float32), axis=1)
    layer_out = (residual.astype(jnp.float32) + moe_total).astype(jnp.bfloat16)
    return (layer_out, cache_after)


def solution(mesh):
    two_lanes = mesh.shape["hd"] == 2 and mesh.shape["grp"] % 8 == 0
    return jax.shard_map(
        two_lane_shards if two_lanes else shards,
        mesh=mesh,
        in_specs=(
            P(("grp", "hd"), None),
            P("grp"),
            P(),
            P(None, "hd"),
            P(None, "hd", None),
            P(None, "grp"),
            P(),
            P(),
            P("hd", "grp", None),
            P("hd", "grp", None),
            P(("grp", "hd"), None),
            P("grp"),
            P("grp", "hd", None),
        ),
        out_specs=(P(("grp", "hd"), None), P("grp", "hd", None)),
        check_vma=False,
    )
```

```python
import functools

import jax
import jax.numpy as jnp
import numpy as np
from jax import lax
from jax.experimental import pallas as pl
from jax.experimental.pallas import tpu as pltpu
from jax.sharding import PartitionSpec as P

norm_eps = 1e-05
rope_base = 10000.0
bf16 = jnp.bfloat16
f32 = jnp.float32
LAST_DIMS = (((1,), (1,)), ((), ()))


def ring_cycle(groups):
    rows = groups // 4
    return [2 * r for r in range(rows)] + [2 * r + 1 for r in reversed(range(rows))]


def ring_pairs(groups):
    cycle = ring_cycle(groups)
    count = len(cycle)
    pairs = []
    for place, pair in enumerate(cycle):
        pairs.append((2 * pair, 2 * cycle[(place + 1) % count]))
        pairs.append((2 * pair + 1, 2 * cycle[(place - 1) % count] + 1))
    return pairs


def sibling_pairs(groups):
    return [(g, g ^ 1) for g in range(groups)]


def ring_sources(groups, me):
    count = groups // 2
    rows = count // 2
    side, pair = me % 2, me // 2
    row, col = pair // 2, pair % 2
    place = jnp.where(col == 0, row, count - 1 - row)

    def block(core, steps):
        there = (place + (2 * core - 1) * steps + count) % count
        other = jnp.where(there < rows, 2 * there, 2 * (count - 1 - there) + 1)
        return [2 * other + core, 2 * other + 1 - core]

    full = (count - 1) // 2
    listed = [me, me + 1 - 2 * side]
    for core in (side, 1 - side):
        for steps in range(1, full + 1):
            listed += block(core, steps)
    return listed + [block(side, count // 2)[0], block(1 - side, count // 2)[0]]


class Ring:
    def __init__(self, pair, groups):
        self.across = functools.partial(lax.ppermute, axis_name="grp", perm=ring_pairs(groups))
        self.beside = functools.partial(lax.ppermute, axis_name="grp", perm=sibling_pairs(groups))
        self.full = (groups // 2 - 1) // 2
        self.unit_rows = pair.shape[0] // 2
        self.mine = [pair]
        self.near = []

    def step(self):
        held = self.mine[-1]
        if len(self.mine) > self.full:
            held = held[: self.unit_rows]
        self.mine.append(self.across(held))

    def pin(self, *others):
        done = lax.optimization_barrier((self.mine[-1],) + others)
        self.mine[-1] = done[0]
        return done[1:] if len(others) > 1 else done[1]

    def share(self, upto=None):
        for index in range(1 + len(self.near), 1 + (upto or len(self.mine) - 1)):
            self.near.append(self.beside(self.mine[index]))

    def parts(self):
        full = self.full
        return self.mine[: full + 1] + self.near[:full] + [self.mine[full + 1], self.near[full]]

    def split(self):
        full = self.full
        listed = [(part, 2 * index) for index, part in enumerate(self.parts()[:-1])]
        listed.append((self.near[full], 4 * full + 3))
        late = (full, 2 * full, 2 * full + 1, 2 * full + 2)
        return (
            [pair for index, pair in enumerate(listed) if index not in late],
            [listed[index] for index in late],
        )


def place_parts(groups, parts, unit_rows, pieces, shards=None):
    sources = ring_sources(groups, lax.axis_index("grp"))
    shard = 0
    for index, part in enumerate(parts):
        shard = shards[index] if shards else shard
        for unit in range(part.shape[0] // unit_rows):
            for first, rows, target, lane in pieces:
                at = pl.multiple_of(sources[shard] * rows, rows)
                start = unit * unit_rows + first
                target[pl.ds(at, rows), lane : lane + part.shape[1]] = part[start : start + rows, :]
            shard += 1


VMEM = pl.BlockSpec(memory_space=pltpu.VMEM)
ANY = pl.BlockSpec(memory_space=pl.ANY)
HBM = pl.BlockSpec(memory_space=pltpu.HBM)
PARAMS = pltpu.CompilerParams(vmem_limit_bytes=16 << 20)


LITTLE = pl.CostEstimate(flops=1, bytes_accessed=1, transcendentals=0)


def takes(us):
    return pl.CostEstimate(
        flops=int(us * 1.15e9), bytes_accessed=int(us * 8e6), transcendentals=0
    )


def reads(nbytes):
    return pl.CostEstimate(flops=1, bytes_accessed=nbytes, transcendentals=0)


def normalized(floats, gain):
    factor = lax.rsqrt(jnp.mean(floats * floats, axis=-1, keepdims=True) + norm_eps)
    return (floats * factor * gain).astype(bf16)


def fetch(pairs, sems):
    copies = []
    for index, (source, target) in enumerate(pairs):
        copies.append(pltpu.make_async_copy(source, target, sems.at[index]))
        copies[-1].start()
    return copies


def pack_kernel(*refs):
    sources, (expert_pair, out_pair, sems) = refs[:6], refs[6:]
    width = expert_pair.shape[1]
    lane = lax.axis_index("hd")
    first = pl.multiple_of(lane * out_pair.shape[1], out_pair.shape[1])
    pairs = []
    row = 0
    for index in range(2):
        up, down, w_out = sources[3 * index : 3 * index + 3]
        count = w_out.shape[0]
        pairs.append(
            (w_out.at[:, pl.ds(first, out_pair.shape[1])], out_pair.at[pl.ds(index * count, count), :])
        )
        for source in (up, down):
            for at in range(0, source.shape[1], width):
                pairs.append(
                    (source.at[:, pl.ds(at, width)], expert_pair.at[pl.ds(row, source.shape[0]), :])
                )
                row += source.shape[0]
    for copy in fetch(pairs, sems):
        copy.wait()


def pack(own, beside):
    own = [pltpu.with_memory_space_constraint(part, pltpu.HBM) for part in own]
    up, down, w_out_t = own
    width = up.shape[1] // 2
    pieces = [up.shape[1] // width, down.shape[1] // width]
    unit_rows = pieces[0] * up.shape[0] + pieces[1] * down.shape[0]
    return pl.pallas_call(
        pack_kernel,
        out_shape=(
            jax.ShapeDtypeStruct((2 * unit_rows, width), bf16),
            jax.ShapeDtypeStruct((2 * w_out_t.shape[0], w_out_t.shape[1] // 2), bf16),
        ),
        in_specs=[ANY] * 6,
        out_specs=(ANY, ANY),
        scratch_shapes=[pltpu.SemaphoreType.DMA((2 + 2 * sum(pieces),))],
        compiler_params=PARAMS,
        cost_estimate=LITTLE,
        name="pack",
    )(*own, *beside)


def as_column(row, eye):
    return jnp.sum(jnp.where(eye, row, 0.0), axis=1, keepdims=True)


def named_experts(ids, experts):
    tokens = ids.shape[1]
    expert = lax.broadcasted_iota(jnp.int32, (experts, tokens), 0)
    hit = jnp.zeros((experts, tokens), f32)
    for index in range(ids.shape[0]):
        hit = jnp.where(ids[index : index + 1, :] == expert, 1.0, hit)
    return hit


def prepare_kernel(groups, slots_dev, *refs):
    sources, (cosine, sine, past, place, send, tags, gain) = refs[:4], refs[4:11]
    positions, slots, ids, flat_gain, sems = refs[11:]
    copies = fetch(list(zip(sources, (positions, slots, ids, flat_gain))), sems)
    for copy in copies:
        copy.wait()
    gain[...] = flat_gain[...].reshape(gain.shape)
    lane = lax.axis_index("hd")
    block = positions.shape[1]

    def iota(shape, dim):
        return lax.broadcasted_iota(jnp.int32, shape, dim)

    eye = iota((block, block), 0) == iota((block, block), 1)
    reach = as_column(jnp.maximum(positions[...], 0).astype(f32), eye)
    past[...] = jnp.broadcast_to(reach, past.shape)
    column = iota((8, 128), 1)
    exponent = (column % 32).astype(f32) * (-2.0 / 64)
    inverse_freq = jnp.exp(exponent * np.float32(np.log(rope_base)))[:1, :]
    angles = reach * inverse_freq
    cosine[...] = jnp.cos(angles)
    turned = jnp.sin(angles)
    sine[...] = jnp.where(iota(angles.shape, 1) % 64 < 32, -turned, turned)

    tokens = ids.shape[1]
    cap = place.shape[0] // 2
    hit = named_experts(ids, 8)
    upto = (iota((tokens, tokens), 0) <= iota((tokens, tokens), 1)).astype(f32)
    rank = jnp.dot(hit, upto, preferred_element_type=f32) - 1.0
    slot = iota((2 * cap, tokens), 0).astype(f32)
    placed = jnp.zeros((2 * cap, tokens), f32)
    for live in range(2):
        order = jnp.where(lane == live, 0, cap).astype(f32)
        member = hit[live : live + 1, :] > 0.0
        placed = jnp.where(member & (slot == rank[live : live + 1, :] + order), 1.0, placed)
    place[...] = placed.astype(bf16)

    where = slots[...]
    owner = jnp.where(where >= 0, where // slots_dev, -1)
    owner_hit = (iota((groups, block), 0) == owner).astype(f32)
    before = (iota((block, block), 0) <= iota((block, block), 1)).astype(f32)
    running = jnp.dot(owner_hit, before, preferred_element_type=f32)
    owner_rank = jnp.sum(owner_hit * running, axis=0, keepdims=True) - 1.0
    capc = send.shape[0] // groups
    row = jnp.where(owner >= 0, owner * capc + owner_rank.astype(jnp.int32), -1)
    send[...] = (iota(send.shape, 0) == row).astype(bf16)
    inside = jnp.where(where >= 0, where % slots_dev, 0)
    high = as_column((inside // 64 + 1).astype(f32), eye)
    low = as_column((inside % 64).astype(f32), eye)
    spot = iota(tags.shape, 1)
    tags[...] = jnp.where(spot == 0, high, jnp.where(spot == 1, low, 0.0)).astype(bf16)


def prepare(groups, slots_dev, positions, slots, ids, gain):
    block, tokens = positions.shape[0], ids.shape[0]
    model = gain.shape[0]
    cap = tokens // 4
    capc = 2 * block // groups
    shapes = [
        ((block, 128), f32),
        ((block, 128), f32),
        ((block, 128), f32),
        ((2 * cap, tokens), bf16),
        ((groups * capc, block), bf16),
        ((block, 128), bf16),
        ((1, model), f32),
    ]
    sources = (positions[None], slots[None], ids.T, gain)
    return pl.pallas_call(
        functools.partial(prepare_kernel, groups, slots_dev),
        out_shape=tuple(jax.ShapeDtypeStruct(shape, kind) for shape, kind in shapes),
        in_specs=[ANY] * 4,
        out_specs=(VMEM,) * len(shapes),
        scratch_shapes=[
            pltpu.VMEM((1, block), jnp.int32),
            pltpu.VMEM((1, block), jnp.int32),
            pltpu.VMEM(ids.shape[::-1], jnp.int32),
            pltpu.VMEM((model,), f32),
            pltpu.SemaphoreType.DMA((4,)),
        ],
        compiler_params=PARAMS,
        cost_estimate=LITTLE,
        name="prepare",
    )(*[pltpu.with_memory_space_constraint(source, pltpu.HBM) for source in sources])


def project_kernel(
    own, other, gain, cosine, sine, w_query, w_keyval, q_out, kv_out, seam_out, raw, rows, sems
):
    count = own.shape[0]
    lane = lax.axis_index("hd")
    mine = pl.multiple_of(lane * count, count)
    theirs = pl.multiple_of((1 - lane) * count, count)
    copies = fetch([(own, raw.at[0]), (other, raw.at[1])], sems)
    cos_q, sin_q = cosine[...], sine[...]
    column = lax.broadcasted_iota(jnp.int32, cos_q.shape, 1)
    lower = column % 64 < 32
    cos_kv = jnp.where(column < 64, cos_q, 1.0)
    sin_kv = jnp.where(column < 64, sin_q, 0.0)
    for index, first in ((0, mine), (1, theirs)):
        copies[index].wait()
        rows[pl.ds(first, count), :] = normalized(raw[index].astype(f32), gain[...])
    width = 256
    for weights, out, cos, sin in ((w_keyval, kv_out, cos_kv, sin_kv), (w_query, q_out, cos_q, sin_q)):
        for first in range(0, weights.shape[1], width):
            made = jnp.dot(rows[...], weights[:, first : first + width], preferred_element_type=f32)
            for part in range(0, width, 128):
                here = made[:, part : part + 128]
                turned = jnp.where(lower, pltpu.roll(here, 96, 1), pltpu.roll(here, 32, 1))
                done = (here * cos + turned * sin).astype(bf16)
                out[:, first + part : first + part + 128] = done
                if out is kv_out:
                    seam_out[:, first + part : first + part + 128] = done[count:, :]


def project(own, other, gain, cosine, sine, w_query, flat_kv):
    count, width = own.shape
    made = w_query.shape[1] + flat_kv.shape[1]
    return pl.pallas_call(
        project_kernel,
        out_shape=(
            jax.ShapeDtypeStruct((2 * count, w_query.shape[1]), bf16),
            jax.ShapeDtypeStruct((2 * count, flat_kv.shape[1]), bf16),
            jax.ShapeDtypeStruct((count, flat_kv.shape[1]), bf16),
        ),
        in_specs=[ANY] * 2 + [VMEM] * 5,
        out_specs=(VMEM, VMEM, VMEM),
        scratch_shapes=[
            pltpu.VMEM((2, count, width), bf16),
            pltpu.VMEM((2 * count, width), bf16),
            pltpu.SemaphoreType.DMA((2,)),
        ],
        compiler_params=PARAMS,
        cost_estimate=takes(8),
        name="project",
    )(own, other, gain, cosine, sine, w_query, flat_kv)


def attend_rows_kernel(first, q, kv, seam, past, mixed, window, sem):
    count = q.shape[0] // 2
    if first == 0:
        copy = pltpu.make_async_copy(seam, window.at[pl.ds(0, count), :], sem)
        copy.start()
        window[count:, :] = kv[:count, :]
        copy.wait()
        keyed = window
    else:
        keyed = kv
    head = 64
    kv_heads = kv.shape[1] // (2 * head)
    per_kv = q.shape[1] // head // kv_heads
    shape = (count, 2 * count)
    row = lax.broadcasted_iota(jnp.int32, shape, 0) + count
    col = lax.broadcasted_iota(jnp.int32, shape, 1)
    reach = past[first : first + count, :1].astype(jnp.int32)
    visible = (col <= row) & (col >= row - reach)
    for kv_head in range(kv_heads):
        lanes = 2 * head * kv_head
        keys = keyed[:, lanes : lanes + head]
        values = keyed[:, lanes + head : lanes + 2 * head]
        for index in range(per_kv):
            at = (kv_head * per_kv + index) * head
            query = q[first : first + count, at : at + head]
            scores = lax.dot_general(query, keys, LAST_DIMS, preferred_element_type=f32)
            raised = jnp.where(visible, jnp.exp(scores * head ** (-0.5)), 0.0)
            probs = (raised / jnp.sum(raised, axis=-1, keepdims=True)).astype(bf16)
            made = jnp.dot(probs, values, preferred_element_type=f32)
            mixed[:, at : at + head] = made.astype(bf16)


def attend_late(q, kv, past):
    def kernel(q, kv, past, mixed):
        attend_rows_kernel(q.shape[0] // 2, q, kv, None, past, mixed, None, None)

    return pl.pallas_call(
        kernel,
        out_shape=jax.ShapeDtypeStruct((q.shape[0] // 2, q.shape[1]), bf16),
        in_specs=[VMEM] * 3,
        out_specs=VMEM,
        compiler_params=PARAMS,
        cost_estimate=takes(2),
        name="attend_late",
    )(q, kv, past)


def attend_early(q, kv, seam, past):
    return pl.pallas_call(
        functools.partial(attend_rows_kernel, 0),
        out_shape=jax.ShapeDtypeStruct((q.shape[0] // 2, q.shape[1]), bf16),
        in_specs=[VMEM, VMEM, ANY, VMEM],
        out_specs=VMEM,
        scratch_shapes=[pltpu.VMEM(kv.shape, bf16), pltpu.SemaphoreType.DMA],
        compiler_params=PARAMS,
        cost_estimate=takes(2),
        name="attend_early",
    )(q, kv, seam, past)


def outward_rows(flip, groups, unit_rows, early, late, parts, w_out, rows):
    place_parts(groups, parts, unit_rows, [(0, unit_rows, w_out, 0)])
    lane = lax.axis_index("hd")
    which = (1 - lane) if flip else lane

    @pl.when(which == 0)
    def _():
        rows[...] = early[...]

    @pl.when(which != 0)
    def _():
        rows[...] = late[...]

    return lax.dot_general(rows[...], w_out[...], LAST_DIMS, preferred_element_type=f32)


def send_kernel(groups, unit_rows, n_parts, early, late, *refs):
    parts, (out, w_out, rows) = refs[:n_parts], refs[n_parts:]
    out[...] = outward_rows(True, groups, unit_rows, early, late, parts, w_out, rows).astype(bf16)


def keep_kernel(groups, unit_rows, n_parts, early, late, tokens, flat_gain, *refs):
    parts, (out, gain, w_out, rows) = refs[:n_parts], refs[n_parts:]
    gain[...] = flat_gain[...].reshape(gain.shape)
    made = outward_rows(False, groups, unit_rows, early, late, parts, w_out, rows)
    out[...] = tokens[...].astype(f32) + made


def outward_send(groups, early, late, parts, unit_rows):
    width, depth = groups * unit_rows, parts[0].shape[1]
    return pl.pallas_call(
        functools.partial(send_kernel, groups, unit_rows, len(parts)),
        out_shape=jax.ShapeDtypeStruct((early.shape[0], width), bf16),
        in_specs=[VMEM] * (2 + len(parts)),
        out_specs=VMEM,
        scratch_shapes=[pltpu.VMEM((width, depth), bf16), pltpu.VMEM(early.shape, bf16)],
        compiler_params=PARAMS,
        cost_estimate=reads(2 * width * depth),
        name="outward_send",
    )(early, late, *parts)


def outward_keep(groups, early, late, tokens, gain, parts, unit_rows):
    width, depth = groups * unit_rows, parts[0].shape[1]
    return pl.pallas_call(
        functools.partial(keep_kernel, groups, unit_rows, len(parts)),
        out_shape=(
            jax.ShapeDtypeStruct(tokens.shape, f32),
            jax.ShapeDtypeStruct((1, width), f32),
        ),
        in_specs=[VMEM] * (4 + len(parts)),
        out_specs=(VMEM, VMEM),
        scratch_shapes=[
            pltpu.VMEM((width, depth), bf16),
            pltpu.VMEM(early.shape, bf16),
        ],
        compiler_params=PARAMS,
        cost_estimate=reads(2 * width * depth),
        name="outward_keep",
    )(early, late, tokens, gain, *parts)


def route_kernel(mine, arrived, gain, place, residual, moe_in, sent):
    added = (mine[...] + arrived[...].astype(f32)).astype(bf16)
    residual[...] = added
    moe_in[...] = normalized(added.astype(f32), gain[...])
    cap = sent.shape[0]
    rows = jnp.dot(place[cap:, :], moe_in[...], preferred_element_type=f32)
    sent[...] = rows.astype(bf16)


def route(mine, arrived, gain, place):
    cap = place.shape[0] // 2
    return pl.pallas_call(
        route_kernel,
        out_shape=(
            jax.ShapeDtypeStruct(mine.shape, bf16),
            jax.ShapeDtypeStruct(mine.shape, bf16),
            jax.ShapeDtypeStruct((cap, mine.shape[1]), bf16),
        ),
        in_specs=[VMEM] * 4,
        out_specs=(VMEM,) * 3,
        compiler_params=PARAMS,
        cost_estimate=reads(10 * mine.shape[0] * mine.shape[1]),
        name="route",
    )(mine, arrived, gain, place)


def expert_pieces(gate_up, down, up_rows, down_rows, width):
    pieces = [(i * up_rows, up_rows, gate_up, i * width) for i in range(2)]
    pieces += [
        (2 * up_rows + i * down_rows, down_rows, down, i * width) for i in range(down.shape[1] // width)
    ]
    return pieces, pieces[-1][0] + down_rows


def gate_kernel(groups, up_rows, down_rows, shards, moe_in, router_in, ids_in, place, *refs):
    parts, (gates, own, spread, gate_up, down, router, ids, sems, part_sems) = (
        refs[: len(shards)],
        refs[len(shards) :],
    )
    small = fetch([(router_in, router), (ids_in, ids)], sems)
    width = parts[0].shape[1]
    pieces, unit_rows = expert_pieces(gate_up, down, up_rows, down_rows, width)
    sources = ring_sources(groups, lax.axis_index("grp"))
    pairs = []
    for part, shard in zip(parts, shards):
        for unit in range(part.shape[0] // unit_rows):
            for first, rows, target, lane in pieces:
                at = pl.multiple_of(sources[shard + unit] * rows, rows)
                pairs.append(
                    (
                        part.at[pl.ds(unit * unit_rows + first, rows), :],
                        target.at[pl.ds(at, rows), pl.ds(lane, width)],
                    )
                )
    copies = fetch(pairs, part_sems)
    cap = own.shape[0]
    own[...] = jnp.dot(place[:cap, :], moe_in[...], preferred_element_type=f32).astype(bf16)
    tokens = ids.shape[1]
    row = lax.broadcasted_iota(jnp.int32, (tokens, tokens), 0)
    eye = (row == lax.broadcasted_iota(jnp.int32, (tokens, tokens), 1)).astype(f32)
    spread[...] = lax.dot_general(
        eye.astype(bf16), place[...], LAST_DIMS, preferred_element_type=f32
    ).astype(bf16)
    for copy in small:
        copy.wait()
    hit = named_experts(ids, router.shape[0])
    named = lax.dot_general(eye, hit, LAST_DIMS, preferred_element_type=f32)
    logits = lax.dot_general(moe_in[...], router[...], LAST_DIMS, preferred_element_type=f32)
    raised = jnp.where(named > 0, jnp.exp(logits), 0.0)
    gates[...] = raised / jnp.sum(raised, axis=-1, keepdims=True)
    for copy in copies:
        copy.wait()


def gate(groups, moe_in, router_t, ids_t, place, early, up_rows, down_rows):
    cap = place.shape[0] // 2
    tokens, model = moe_in.shape
    width = early[0][0].shape[1]
    units = 2 * len(early)
    far = [pltpu.with_memory_space_constraint(part, pltpu.HBM) for part in (router_t, ids_t)]
    return pl.pallas_call(
        functools.partial(gate_kernel, groups, up_rows, down_rows, [shard for _, shard in early]),
        out_shape=(
            jax.ShapeDtypeStruct((tokens, router_t.shape[0]), f32),
            jax.ShapeDtypeStruct((cap, model), bf16),
            jax.ShapeDtypeStruct(place.shape[::-1], bf16),
            jax.ShapeDtypeStruct((groups * up_rows, 2 * width), bf16),
            jax.ShapeDtypeStruct((groups * down_rows, model), bf16),
        ),
        in_specs=[VMEM, ANY, ANY, VMEM] + [ANY] * len(early),
        out_specs=(VMEM,) * 5,
        scratch_shapes=[
            pltpu.VMEM(router_t.shape, bf16),
            pltpu.VMEM(ids_t.shape, jnp.int32),
            pltpu.SemaphoreType.DMA((2,)),
            pltpu.SemaphoreType.DMA((units * (2 + model // width),)),
        ],
        compiler_params=PARAMS,
        cost_estimate=LITTLE,
        name="gate",
    )(moe_in, *far, place, *[part for part, _ in early])


def expert_kernel(groups, up_rows, down_rows, shards, own, other, gate_up_in, down_in, *refs):
    parts = refs[: len(shards)]
    own_out, other_out, gate_up, down, rows = refs[len(shards) :]
    width = parts[0].shape[1]
    count = own.shape[0]
    rows[:count, :] = own[...]
    rows[count:, :] = other[...]
    pieces, unit_rows = expert_pieces(gate_up, down, up_rows, down_rows, width)
    place_parts(groups, parts, unit_rows, pieces, shards)
    both = jnp.dot(rows[...], gate_up[...], preferred_element_type=f32)
    gate, up = both[:, :width], both[:, width:]
    hidden = (gate / (1.0 + jnp.exp(-gate)) * up).astype(bf16)
    made = jnp.dot(hidden, down[...], preferred_element_type=f32).astype(bf16)
    own_out[...] = made[:count, :]
    other_out[...] = made[count:, :]


def expert(groups, own, other, staged, late, up_rows, down_rows):
    count, model = own.shape
    width = late[0][0].shape[1]
    return pl.pallas_call(
        functools.partial(expert_kernel, groups, up_rows, down_rows, [shard for _, shard in late]),
        out_shape=(jax.ShapeDtypeStruct(own.shape, bf16),) * 2
        + tuple(jax.ShapeDtypeStruct(part.shape, bf16) for part in staged),
        in_specs=[VMEM] * (4 + len(late)),
        out_specs=(VMEM,) * 4,
        scratch_shapes=[pltpu.VMEM((2 * count, model), bf16)],
        input_output_aliases={2: 2, 3: 3},
        compiler_params=PARAMS,
        cost_estimate=takes(6.2),
        name="expert",
    )(own, other, *staged, *[part for part, _ in late])[:2]


def combine_kernel(residual, gates, spread, own, returned, out):
    lane = lax.axis_index("hd")
    count = own.shape[0]
    column = lax.broadcasted_iota(jnp.int32, gates.shape, 1)
    total = jnp.zeros(residual.shape, f32)
    for index, made in ((0, own), (1, returned)):
        live = lane if index == 0 else 1 - lane
        weight = jnp.sum(jnp.where(column == live, gates[...], 0.0), axis=-1, keepdims=True)
        picked = jnp.dot(
            spread[:, index * count : (index + 1) * count], made[...], preferred_element_type=f32
        )
        total += weight * picked
    out[...] = (residual[...].astype(f32) + total).astype(bf16)


def combine(residual, gates, spread, own, returned):
    return pl.pallas_call(
        combine_kernel,
        out_shape=jax.ShapeDtypeStruct(residual.shape, bf16),
        in_specs=[VMEM] * 5,
        out_specs=VMEM,
        compiler_params=PARAMS,
        cost_estimate=reads(6 * residual.shape[0] * residual.shape[1]),
        name="combine",
    )(residual, gates, spread, own, returned)


def bundle_kernel(send, kv, tags, result, out, sem):
    groups, rows, _ = out.shape
    heads = kv.shape[1] // 128
    capc = send.shape[0] // groups
    packed = jnp.dot(send[...], kv[...], preferred_element_type=f32).astype(bf16)
    tagged = jnp.dot(send[...], tags[...], preferred_element_type=f32)
    one = (lax.broadcasted_iota(jnp.int32, (16, 128), 0) == lax.broadcasted_iota(jnp.int32, (16, 128), 1))
    for owner in range(groups):
        mine = slice(owner * capc, (owner + 1) * capc)
        for head in range(heads):
            out[owner, head * capc : (head + 1) * capc, :] = packed[mine, head * 128 : (head + 1) * 128]
        wide = jnp.concatenate([tagged[mine, :], jnp.zeros((128 - capc, 128), f32)], axis=0)
        out[owner, heads * capc :, :] = lax.dot_general(
            one.astype(f32), wide, LAST_DIMS, preferred_element_type=f32
        ).astype(bf16)
    copy = pltpu.make_async_copy(out, result, sem)
    copy.start()
    copy.wait()


def bundle(groups, send, kv, tags):
    rows = send.shape[0] // groups * (kv.shape[1] // 128) + 16
    return pl.pallas_call(
        bundle_kernel,
        out_shape=pltpu.HBM((groups, rows, 128), bf16),
        in_specs=[VMEM] * 3,
        out_specs=HBM,
        scratch_shapes=[pltpu.VMEM((groups, rows, 128), bf16), pltpu.SemaphoreType.DMA],
        compiler_params=PARAMS,
        cost_estimate=LITTLE,
        name="bundle",
    )(send, kv, tags)


def write_kernel(heads, arrived, cache, out, rows, wide, known):
    groups, size, _ = arrived.shape
    slots = cache.shape[0] // heads
    capc = (size - 16) // heads
    high, low = [], []
    for source in range(groups):
        for head in range(heads):
            rows[source * capc : (source + 1) * capc, head * 128 : (head + 1) * 128] = arrived[
                source, head * capc : (head + 1) * capc, :
            ]
        numbers = arrived[source, heads * capc :, :].astype(f32)
        high.append(numbers[0:1, :capc])
        low.append(numbers[1:2, :capc])
    slot = jnp.concatenate(high, axis=1) * 64.0 + jnp.concatenate(low, axis=1) - 64.0
    row = lax.broadcasted_iota(jnp.int32, (slots, slot.shape[1]), 0).astype(f32)
    hit = (row == slot).astype(bf16)
    made = jnp.dot(hit, rows[...], preferred_element_type=f32)
    found = jnp.dot(hit, jnp.ones((slot.shape[1], 128), bf16), preferred_element_type=f32)
    for head in range(heads):
        wide[pl.ds(head, slots, heads), :] = made[:, head * 128 : (head + 1) * 128]
        known[pl.ds(head, slots, heads), :] = found
    old = cache[...].astype(f32)
    out[...] = jnp.where(known[...] > 0.0, wide[...], old).astype(bf16)


def write(arrived, cache):
    slots, heads, lanes = cache.shape
    capc = (arrived.shape[1] - 16) // heads
    flat = (slots * heads, lanes)
    written = pl.pallas_call(
        functools.partial(write_kernel, heads),
        out_shape=jax.ShapeDtypeStruct(flat, bf16),
        in_specs=[VMEM] * 2,
        out_specs=VMEM,
        scratch_shapes=[
            pltpu.VMEM((arrived.shape[0] * capc, heads * lanes), bf16),
            pltpu.VMEM(flat, f32),
            pltpu.VMEM(flat, f32),
        ],
        compiler_params=PARAMS,
        cost_estimate=reads(1 << 21),
        name="write",
    )(arrived, cache.reshape(flat))
    return written.reshape(cache.shape)


def two_lane_shards(
    tokens,
    positions,
    attn_gain,
    w_query,
    w_keyval,
    w_out,
    moe_gain,
    router,
    w_gate_up,
    w_down,
    expert_ids,
    cache_slot,
    kv_cache,
):
    groups = lax.axis_size("grp")
    tok_rows, model = tokens.shape
    block = positions.shape[0]
    kv_local, head2 = w_keyval.shape[1:]
    kv_width = kv_local * head2
    slots_dev = kv_cache.shape[0]
    swap = functools.partial(lax.ppermute, axis_name="hd", perm=[(0, 1), (1, 0)])

    together = lax.optimization_barrier

    other_tokens = swap(tokens)
    own = (w_gate_up[0], w_down[0], w_out.T)
    up_rows, down_rows = own[0].shape[0], own[1].shape[0]
    beside = [lax.ppermute(part, "grp", sibling_pairs(groups)) for part in own]
    expert_pair, out_pair = pack(own, beside)
    out_ring = Ring(out_pair, groups)
    out_ring.step()
    expert_ring = Ring(expert_pair, groups)
    expert_ring.step()
    w_keyval, positions = together((w_keyval, positions, out_pair))[:2]
    flat_kv = w_keyval.reshape(model, kv_width)
    cosine, sine, past, place, send, tags, gain = prepare(
        groups, slots_dev, positions, cache_slot, expert_ids, attn_gain
    )
    other_tokens, cosine, flat_kv = out_ring.pin(other_tokens, cosine, flat_kv)
    out_ring.step()

    q, kv, tail = project(tokens, other_tokens, gain, cosine, sine, w_query, flat_kv)
    seam = lax.ppermute(tail, "grp", [(g, g + 1) for g in range(groups - 1)])
    q = out_ring.pin(q)
    out_ring.step()
    out_ring.share(2)
    late = attend_late(q, kv, past)
    seam, late = together((seam, late))
    seam = expert_ring.pin(seam)
    expert_ring.step()
    early = attend_early(q, kv, seam, past)
    early, out_ring.near = together((early, out_ring.near))
    early = out_ring.pin(early)
    out_ring.step()
    out_ring.share(3)
    early, kv, out_ring.near = together((early, kv, out_ring.near))
    outgoing = bundle(groups, send, kv, tags)
    early, outgoing = together((early, outgoing))
    early = out_ring.pin(early)
    early = expert_ring.pin(early)
    expert_ring.step()
    out_ring.share()
    sent = outward_send(groups, early, late, out_ring.parts(), out_ring.unit_rows)
    arrived = swap(sent)
    early = together((early, sent))[0]
    mine, late_gain = outward_keep(
        groups, early, late, tokens, moe_gain, out_ring.parts(), out_ring.unit_rows
    )
    late_gain = expert_ring.pin(late_gain)
    expert_ring.share()
    expert_ring.step()
    outgoing = together((outgoing, sent))[0]
    arrived_cache = lax.all_to_all(outgoing, "grp", split_axis=0, concat_axis=0, tiled=True)
    arrived, late_gain = expert_ring.pin(arrived, late_gain)
    expert_ring.share()

    residual, moe_in, sent_rows = route(mine, arrived, late_gain, place)
    landed = swap(sent_rows)
    parts_early, parts_late = expert_ring.split()
    gates, own_rows, spread, *staged = gate(
        groups, moe_in, router.T, expert_ids.T, place, parts_early, up_rows, down_rows
    )
    landed, own_rows = together((landed, own_rows))
    own_made, back = expert(groups, own_rows, landed, staged, parts_late, up_rows, down_rows)
    returned = swap(back)
    layer_out = combine(residual, gates, spread, own_made, returned)
    layer_out, arrived_cache = together((layer_out, arrived_cache))
    cache_after = write(arrived_cache, kv_cache)
    return (layer_out, cache_after)


def passed_along(value, axis, steps):
    count = lax.axis_size(axis)
    initial, last = (max(0, -steps), min(count, count - steps))
    return lax.ppermute(value, axis, [(source, source + steps) for source in range(initial, last)])


def rms_norm(row_set, norm_gain):
    floats = row_set.astype(jnp.float32)
    factor = lax.rsqrt(jnp.mean(floats * floats, axis=-1, keepdims=True) + norm_eps)
    return (floats * factor * norm_gain).astype(jnp.bfloat16)


def rotate(vectors, angle_pos):
    halves = vectors.shape[-1] // 2
    inverse_freq = rope_base ** (-2.0 * jnp.arange(halves, dtype=jnp.float32) / vectors.shape[-1])
    angles = angle_pos[:, None, None] * inverse_freq[None, None, :]
    cosine = jnp.cos(angles)
    sine_part = jnp.sin(angles)
    first_half = vectors[..., :halves]
    second_half = vectors[..., halves:]
    return jnp.concatenate(
        [
            first_half * cosine - second_half * sine_part,
            second_half * cosine + first_half * sine_part,
        ],
        axis=-1,
    )


def expert_rows(row_set, gate_up, down_rows):
    gate_and_up = jnp.dot(row_set, gate_up, preferred_element_type=jnp.float32)
    inner_width = gate_and_up.shape[1] // 2
    hidden = (jax.nn.silu(gate_and_up[:, :inner_width]) * gate_and_up[:, inner_width:]).astype(
        jnp.bfloat16
    )
    return jnp.dot(hidden, down_rows, preferred_element_type=jnp.float32).astype(jnp.bfloat16)


def attend_rows(query_blk, keys_blk, vals_blk, visible, scale_qk):
    scores = (
        jnp.einsum("qkgd,skd->kgqs", query_blk, keys_blk, preferred_element_type=jnp.float32)
        * scale_qk
    )
    weights_f = jnp.where(visible[None, None], jnp.exp(scores), 0.0)
    prob_bf = (weights_f / jnp.sum(weights_f, axis=-1, keepdims=True)).astype(jnp.bfloat16)
    return jnp.einsum("kgqs,skd->qkgd", prob_bf, vals_blk, preferred_element_type=jnp.float32)


def shards(
    tokens,
    positions,
    attn_gain,
    w_query,
    w_keyval,
    w_out,
    moe_gain,
    router,
    w_gate_up,
    w_down,
    expert_ids,
    cache_slot,
    kv_cache,
):
    lane_count = lax.axis_size("hd")
    group_count = lax.axis_size("grp")
    tok_rows = tokens.shape[0]
    model_width = tokens.shape[1]
    block_len = positions.shape[0]
    seg_most = block_len // 2
    head_dim = w_keyval.shape[2] // 2
    kv_local = w_keyval.shape[1]
    q_local = w_query.shape[1] // head_dim
    per_kv = q_local // kv_local
    expert_cap = tok_rows // 4
    normed = rms_norm(tokens, attn_gain)
    flat_kv = w_keyval.reshape(model_width, kv_local * 2 * head_dim)
    section = lax.all_gather(normed, "hd", axis=0, tiled=True)
    projected = jnp.concatenate(
        [
            jnp.dot(section, w_query, preferred_element_type=jnp.float32),
            jnp.dot(section, flat_kv, preferred_element_type=jnp.float32),
        ],
        axis=1,
    )
    angle_pos = jnp.maximum(positions, 0).astype(jnp.float32)
    queries = rotate(
        projected[:, : q_local * head_dim].reshape(block_len, q_local, head_dim), angle_pos
    ).astype(jnp.bfloat16)
    key_val = projected[:, q_local * head_dim :].reshape(block_len, kv_local, 2 * head_dim)
    rotated = rotate(key_val[:, :, :head_dim], angle_pos).astype(jnp.bfloat16)
    stored = jnp.concatenate([rotated, key_val[:, :, head_dim:].astype(jnp.bfloat16)], axis=2)
    seam_rows = passed_along(stored[block_len - seg_most :], "grp", 1)
    window = jnp.concatenate([seam_rows, stored], axis=0)
    scale_qk = head_dim ** (-0.5)
    local_rows = jnp.arange(block_len, dtype=jnp.int32)
    lowest = local_rows - jnp.maximum(positions, 0)
    pieces_out = []
    for q_block in range(2):
        first_row = q_block * seg_most
        rows_here = first_row + jnp.arange(seg_most, dtype=jnp.int32)
        cols_here = first_row - seg_most + jnp.arange(2 * seg_most, dtype=jnp.int32)
        low_here = lowest[first_row : first_row + seg_most]
        visible = (cols_here[None, :] >= low_here[:, None]) & (
            cols_here[None, :] <= rows_here[:, None]
        )
        query_blk = queries[first_row : first_row + seg_most].reshape(
            seg_most, kv_local, per_kv, head_dim
        )
        keys_blk = window[first_row : first_row + 2 * seg_most, :, :head_dim]
        vals_blk = window[first_row : first_row + 2 * seg_most, :, head_dim:]
        mixed_rows = attend_rows(query_blk, keys_blk, vals_blk, visible, scale_qk)
        pieces_out.append(mixed_rows.reshape(seg_most, q_local * head_dim).astype(jnp.bfloat16))
    attended = jnp.concatenate(pieces_out, axis=0)
    slots_dev = kv_cache.shape[0]
    capc = 2 * block_len // group_count
    live_slot = cache_slot >= 0
    owners = jnp.where(live_slot, cache_slot // slots_dev, group_count)
    owner_hit = (owners[:, None] == jnp.arange(group_count, dtype=jnp.int32)[None, :]).astype(
        jnp.bfloat16
    )
    lower_tri = (local_rows[:, None] >= local_rows[None, :]).astype(jnp.bfloat16)
    running = jnp.dot(lower_tri, owner_hit, preferred_element_type=jnp.float32)
    owner_rank = jnp.sum(running * owner_hit.astype(jnp.float32), axis=1).astype(jnp.int32) - 1
    send_rows = jnp.where(live_slot, owners * capc + owner_rank, group_count * capc)
    outgoing_cache = (
        jnp.zeros((group_count * capc, kv_local, 2 * head_dim), jnp.bfloat16)
        .at[send_rows]
        .set(stored, mode="drop")
    )
    outgoing_slots = (
        jnp.full((group_count * capc,), -1, jnp.int32)
        .at[send_rows]
        .set(cache_slot % slots_dev, mode="drop")
    )
    arrived, arrived_slots = (
        lax.all_to_all(
            outgoing_cache.reshape(group_count, capc, kv_local, 2 * head_dim),
            "grp",
            split_axis=0,
            concat_axis=0,
            tiled=True,
        ),
        lax.all_to_all(
            outgoing_slots.reshape(group_count, capc),
            "grp",
            split_axis=0,
            concat_axis=0,
            tiled=True,
        ),
    )
    flat_slots = arrived_slots.reshape(group_count * capc)
    write_rows = jnp.where(flat_slots >= 0, flat_slots, slots_dev).astype(jnp.int32)
    cache_after = kv_cache.at[write_rows].set(
        arrived.reshape(group_count * capc, kv_local, 2 * head_dim), mode="drop"
    )
    by_token = lax.all_to_all(attended, "hd", split_axis=0, concat_axis=1, tiled=True)
    attn_proj = jnp.dot(
        by_token,
        lax.all_gather(w_out, "grp", axis=1, tiled=True),
        preferred_element_type=jnp.float32,
    )
    residual = (tokens.astype(jnp.float32) + attn_proj).astype(jnp.bfloat16)
    moe_in = rms_norm(residual, moe_gain)
    logits = jnp.dot(moe_in, router, preferred_element_type=jnp.float32)
    expert_range = jnp.arange(router.shape[1], dtype=jnp.int32)
    matches_all = expert_ids[:, :, None] == expert_range[None, None, :]
    chosen = jnp.sum(jnp.where(matches_all, logits[:, None, :], 0.0), axis=2)
    raised = jnp.exp(chosen)
    gates = raised / jnp.sum(raised, axis=1, keepdims=True)
    live_range = jnp.arange(lane_count, dtype=jnp.int32)
    matches = expert_ids[:, :, None] == live_range[None, None, :]
    member = jnp.any(matches, axis=1)
    weighting = jnp.sum(jnp.where(matches, gates[:, :, None], 0.0), axis=1)
    ranking = jnp.cumsum(member.astype(jnp.int32), axis=0) - 1
    target = jnp.where(member, live_range[None, :] * expert_cap + ranking, -1)
    slot_range = jnp.arange(lane_count * expert_cap, dtype=jnp.int32)
    slot_hits = target[None, :, :] == slot_range[:, None, None]
    placing = jnp.any(slot_hits, axis=2).astype(jnp.bfloat16)
    outgoing = (
        jnp.dot(placing, moe_in, preferred_element_type=jnp.float32)
        .astype(jnp.bfloat16)
        .reshape(lane_count, expert_cap, model_width)
    )
    gate_up_all, down_all = (
        lax.all_gather(w_gate_up, "grp", axis=1, tiled=True),
        lax.all_gather(w_down, "grp", axis=1, tiled=True),
    )
    gate_up_mat = gate_up_all[0]
    down_mat = down_all[0]
    landed = lax.all_to_all(outgoing, "hd", split_axis=0, concat_axis=0, tiled=True)
    results = expert_rows(landed.reshape(-1, model_width), gate_up_mat, down_mat).reshape(landed.shape)
    returned = lax.all_to_all(results, "hd", split_axis=0, concat_axis=0, tiled=True)
    flat_returned = returned.reshape(-1, model_width)
    fetched = flat_returned[jnp.maximum(target, 0)]
    used_weight = jnp.where(member, weighting, 0.0)
    moe_total = jnp.sum(used_weight[:, :, None] * fetched.astype(jnp.float32), axis=1)
    layer_out = (residual.astype(jnp.float32) + moe_total).astype(jnp.bfloat16)
    return (layer_out, cache_after)


def solution(mesh):
    two_lanes = mesh.shape["hd"] == 2 and mesh.shape["grp"] % 8 == 0
    return jax.shard_map(
        two_lane_shards if two_lanes else shards,
        mesh=mesh,
        in_specs=(
            P(("grp", "hd"), None),
            P("grp"),
            P(),
            P(None, "hd"),
            P(None, "hd", None),
            P(None, "grp"),
            P(),
            P(),
            P("hd", "grp", None),
            P("hd", "grp", None),
            P(("grp", "hd"), None),
            P("grp"),
            P("grp", "hd", None),
        ),
        out_specs=(P(("grp", "hd"), None), P("grp", "hd", None)),
        check_vma=False,
    )
```

```python
import functools

import jax
import jax.numpy as jnp
import numpy as np
from jax import lax
from jax.experimental import pallas as pl
from jax.experimental.pallas import tpu as pltpu
from jax.sharding import PartitionSpec as P

norm_eps = 1e-05
rope_base = 10000.0
bf16 = jnp.bfloat16
f32 = jnp.float32
LAST_DIMS = (((1,), (1,)), ((), ()))


def ring_cycle(groups):
    rows = groups // 4
    return [2 * r for r in range(rows)] + [2 * r + 1 for r in reversed(range(rows))]


def ring_pairs(groups):
    cycle = ring_cycle(groups)
    count = len(cycle)
    pairs = []
    for place, pair in enumerate(cycle):
        pairs.append((2 * pair, 2 * cycle[(place + 1) % count]))
        pairs.append((2 * pair + 1, 2 * cycle[(place - 1) % count] + 1))
    return pairs


def sibling_pairs(groups):
    return [(g, g ^ 1) for g in range(groups)]


def ring_sources(groups, me):
    count = groups // 2
    rows = count // 2
    side, pair = me % 2, me // 2
    row, col = pair // 2, pair % 2
    place = jnp.where(col == 0, row, count - 1 - row)

    def block(core, steps):
        there = (place + (2 * core - 1) * steps + count) % count
        other = jnp.where(there < rows, 2 * there, 2 * (count - 1 - there) + 1)
        return [2 * other + core, 2 * other + 1 - core]

    full = (count - 1) // 2
    listed = [me, me + 1 - 2 * side]
    for core in (side, 1 - side):
        for steps in range(1, full + 1):
            listed += block(core, steps)
    return listed + [block(side, count // 2)[0], block(1 - side, count // 2)[0]]


def cut_kernel(whole, out, sem):
    copy = pltpu.make_async_copy(whole.at[pl.ds(0, out.shape[0]), :], out, sem)
    copy.start()
    copy.wait()


def cut(whole, rows):
    return pl.pallas_call(
        cut_kernel,
        out_shape=jax.ShapeDtypeStruct((rows, whole.shape[1]), whole.dtype),
        in_specs=[pl.BlockSpec(memory_space=pl.ANY)],
        out_specs=pl.BlockSpec(memory_space=pl.ANY),
        scratch_shapes=[pltpu.SemaphoreType.DMA],
        cost_estimate=pl.CostEstimate(flops=1, bytes_accessed=1, transcendentals=0),
        name="cut",
    )(whole)


class Ring:
    def __init__(self, pair, groups):
        self.across = functools.partial(lax.ppermute, axis_name="grp", perm=ring_pairs(groups))
        self.beside = functools.partial(lax.ppermute, axis_name="grp", perm=sibling_pairs(groups))
        self.full = (groups // 2 - 1) // 2
        self.unit_rows = pair.shape[0] // 2
        self.mine = [pair]
        self.near = []

    def step(self):
        held = self.mine[-1]
        if len(self.mine) > self.full:
            held = cut(held, self.unit_rows)
        self.mine.append(self.across(held))

    def pin(self, *others):
        done = lax.optimization_barrier((self.mine[-1],) + others)
        self.mine[-1] = done[0]
        return done[1:] if len(others) > 1 else done[1]

    def share(self, upto=None):
        for index in range(1 + len(self.near), 1 + (upto or len(self.mine) - 1)):
            self.near.append(self.beside(self.mine[index]))

    def parts(self):
        full = self.full
        return self.mine[: full + 1] + self.near[:full] + [self.mine[full + 1], self.near[full]]

    def split(self):
        full = self.full
        listed = [(part, 2 * index) for index, part in enumerate(self.parts()[:-1])]
        listed.append((self.near[full], 4 * full + 3))
        late = (full, 2 * full, 2 * full + 1, 2 * full + 2)
        return (
            [pair for index, pair in enumerate(listed) if index not in late],
            [listed[index] for index in late],
        )


def place_parts(groups, parts, unit_rows, pieces, shards=None):
    sources = ring_sources(groups, lax.axis_index("grp"))
    shard = 0
    for index, part in enumerate(parts):
        shard = shards[index] if shards else shard
        for unit in range(part.shape[0] // unit_rows):
            for first, rows, target, lane in pieces:
                at = pl.multiple_of(sources[shard] * rows, rows)
                start = unit * unit_rows + first
                target[pl.ds(at, rows), lane : lane + part.shape[1]] = part[start : start + rows, :]
            shard += 1


VMEM = pl.BlockSpec(memory_space=pltpu.VMEM)
ANY = pl.BlockSpec(memory_space=pl.ANY)
HBM = pl.BlockSpec(memory_space=pltpu.HBM)
PARAMS = pltpu.CompilerParams(vmem_limit_bytes=16 << 20)


LITTLE = pl.CostEstimate(flops=1, bytes_accessed=1, transcendentals=0)


def takes(us):
    return pl.CostEstimate(
        flops=int(us * 1.15e9), bytes_accessed=int(us * 8e6), transcendentals=0
    )


def reads(nbytes):
    return pl.CostEstimate(flops=1, bytes_accessed=nbytes, transcendentals=0)


def normalized(floats, gain):
    factor = lax.rsqrt(jnp.mean(floats * floats, axis=-1, keepdims=True) + norm_eps)
    return (floats * factor * gain).astype(bf16)


def fetch(pairs, sems):
    copies = []
    for index, (source, target) in enumerate(pairs):
        copies.append(pltpu.make_async_copy(source, target, sems.at[index]))
        copies[-1].start()
    return copies


def pack_kernel(*refs):
    sources, (expert_pair, out_pair, sems) = refs[:6], refs[6:]
    width = expert_pair.shape[1]
    lane = lax.axis_index("hd")
    first = pl.multiple_of(lane * out_pair.shape[1], out_pair.shape[1])
    pairs = []
    row = 0
    for index in range(2):
        up, down, w_out = sources[3 * index : 3 * index + 3]
        count = w_out.shape[0]
        pairs.append(
            (w_out.at[:, pl.ds(first, out_pair.shape[1])], out_pair.at[pl.ds(index * count, count), :])
        )
        for source in (up, down):
            for at in range(0, source.shape[1], width):
                pairs.append(
                    (source.at[:, pl.ds(at, width)], expert_pair.at[pl.ds(row, source.shape[0]), :])
                )
                row += source.shape[0]
    for copy in fetch(pairs, sems):
        copy.wait()


def pack(own, beside):
    own = [pltpu.with_memory_space_constraint(part, pltpu.HBM) for part in own]
    up, down, w_out_t = own
    width = up.shape[1] // 2
    pieces = [up.shape[1] // width, down.shape[1] // width]
    unit_rows = pieces[0] * up.shape[0] + pieces[1] * down.shape[0]
    return pl.pallas_call(
        pack_kernel,
        out_shape=(
            jax.ShapeDtypeStruct((2 * unit_rows, width), bf16),
            jax.ShapeDtypeStruct((2 * w_out_t.shape[0], w_out_t.shape[1] // 2), bf16),
        ),
        in_specs=[ANY] * 6,
        out_specs=(ANY, ANY),
        scratch_shapes=[pltpu.SemaphoreType.DMA((2 + 2 * sum(pieces),))],
        compiler_params=PARAMS,
        cost_estimate=LITTLE,
        name="pack",
    )(*own, *beside)


def as_column(row, eye):
    return jnp.sum(jnp.where(eye, row, 0.0), axis=1, keepdims=True)


def named_experts(ids, experts):
    tokens = ids.shape[1]
    expert = lax.broadcasted_iota(jnp.int32, (experts, tokens), 0)
    hit = jnp.zeros((experts, tokens), f32)
    for index in range(ids.shape[0]):
        hit = jnp.where(ids[index : index + 1, :] == expert, 1.0, hit)
    return hit


def prepare_kernel(groups, slots_dev, *refs):
    sources, (cosine, sine, past, place, send, tags, gain) = refs[:4], refs[4:11]
    positions, slots, ids, flat_gain, sems = refs[11:]
    copies = fetch(list(zip(sources, (positions, slots, ids, flat_gain))), sems)
    for copy in copies:
        copy.wait()
    gain[...] = flat_gain[...].reshape(gain.shape)
    lane = lax.axis_index("hd")
    block = positions.shape[1]

    def iota(shape, dim):
        return lax.broadcasted_iota(jnp.int32, shape, dim)

    eye = iota((block, block), 0) == iota((block, block), 1)
    reach = as_column(jnp.maximum(positions[...], 0).astype(f32), eye)
    past[...] = jnp.broadcast_to(reach, past.shape)
    column = iota((8, 128), 1)
    exponent = (column % 32).astype(f32) * (-2.0 / 64)
    inverse_freq = jnp.exp(exponent * np.float32(np.log(rope_base)))[:1, :]
    angles = reach * inverse_freq
    cosine[...] = jnp.cos(angles)
    turned = jnp.sin(angles)
    sine[...] = jnp.where(iota(angles.shape, 1) % 64 < 32, -turned, turned)

    tokens = ids.shape[1]
    cap = place.shape[0] // 2
    hit = named_experts(ids, 8)
    upto = (iota((tokens, tokens), 0) <= iota((tokens, tokens), 1)).astype(f32)
    rank = jnp.dot(hit, upto, preferred_element_type=f32) - 1.0
    slot = iota((2 * cap, tokens), 0).astype(f32)
    placed = jnp.zeros((2 * cap, tokens), f32)
    for live in range(2):
        order = jnp.where(lane == live, 0, cap).astype(f32)
        member = hit[live : live + 1, :] > 0.0
        placed = jnp.where(member & (slot == rank[live : live + 1, :] + order), 1.0, placed)
    place[...] = placed.astype(bf16)

    where = slots[...]
    owner = jnp.where(where >= 0, where // slots_dev, -1)
    owner_hit = (iota((groups, block), 0) == owner).astype(f32)
    before = (iota((block, block), 0) <= iota((block, block), 1)).astype(f32)
    running = jnp.dot(owner_hit, before, preferred_element_type=f32)
    owner_rank = jnp.sum(owner_hit * running, axis=0, keepdims=True) - 1.0
    capc = send.shape[0] // groups
    row = jnp.where(owner >= 0, owner * capc + owner_rank.astype(jnp.int32), -1)
    send[...] = (iota(send.shape, 0) == row).astype(bf16)
    inside = jnp.where(where >= 0, where % slots_dev, 0)
    high = as_column((inside // 64 + 1).astype(f32), eye)
    low = as_column((inside % 64).astype(f32), eye)
    spot = iota(tags.shape, 1)
    tags[...] = jnp.where(spot == 0, high, jnp.where(spot == 1, low, 0.0)).astype(bf16)


def prepare(groups, slots_dev, positions, slots, ids, gain):
    block, tokens = positions.shape[0], ids.shape[0]
    model = gain.shape[0]
    cap = tokens // 4
    capc = 2 * block // groups
    shapes = [
        ((block, 128), f32),
        ((block, 128), f32),
        ((block, 128), f32),
        ((2 * cap, tokens), bf16),
        ((groups * capc, block), bf16),
        ((block, 128), bf16),
        ((1, model), f32),
    ]
    sources = (positions[None], slots[None], ids.T, gain)
    return pl.pallas_call(
        functools.partial(prepare_kernel, groups, slots_dev),
        out_shape=tuple(jax.ShapeDtypeStruct(shape, kind) for shape, kind in shapes),
        in_specs=[ANY] * 4,
        out_specs=(VMEM,) * len(shapes),
        scratch_shapes=[
            pltpu.VMEM((1, block), jnp.int32),
            pltpu.VMEM((1, block), jnp.int32),
            pltpu.VMEM(ids.shape[::-1], jnp.int32),
            pltpu.VMEM((model,), f32),
            pltpu.SemaphoreType.DMA((4,)),
        ],
        compiler_params=PARAMS,
        cost_estimate=LITTLE,
        name="prepare",
    )(*[pltpu.with_memory_space_constraint(source, pltpu.HBM) for source in sources])


def project_kernel(
    own, other, gain, cosine, sine, w_query, w_keyval, q_out, kv_out, seam_out, raw, rows, sems
):
    count = own.shape[0]
    lane = lax.axis_index("hd")
    mine = pl.multiple_of(lane * count, count)
    theirs = pl.multiple_of((1 - lane) * count, count)
    copies = fetch([(own, raw.at[0]), (other, raw.at[1])], sems)
    cos_q, sin_q = cosine[...], sine[...]
    column = lax.broadcasted_iota(jnp.int32, cos_q.shape, 1)
    lower = column % 64 < 32
    cos_kv = jnp.where(column < 64, cos_q, 1.0)
    sin_kv = jnp.where(column < 64, sin_q, 0.0)
    for index, first in ((0, mine), (1, theirs)):
        copies[index].wait()
        rows[pl.ds(first, count), :] = normalized(raw[index].astype(f32), gain[...])
    width = 256
    for weights, out, cos, sin in ((w_keyval, kv_out, cos_kv, sin_kv), (w_query, q_out, cos_q, sin_q)):
        for first in range(0, weights.shape[1], width):
            made = jnp.dot(rows[...], weights[:, first : first + width], preferred_element_type=f32)
            for part in range(0, width, 128):
                here = made[:, part : part + 128]
                turned = jnp.where(lower, pltpu.roll(here, 96, 1), pltpu.roll(here, 32, 1))
                done = (here * cos + turned * sin).astype(bf16)
                out[:, first + part : first + part + 128] = done
                if out is kv_out:
                    seam_out[:, first + part : first + part + 128] = done[count:, :]


def project(own, other, gain, cosine, sine, w_query, flat_kv):
    count, width = own.shape
    made = w_query.shape[1] + flat_kv.shape[1]
    return pl.pallas_call(
        project_kernel,
        out_shape=(
            jax.ShapeDtypeStruct((2 * count, w_query.shape[1]), bf16),
            jax.ShapeDtypeStruct((2 * count, flat_kv.shape[1]), bf16),
            jax.ShapeDtypeStruct((count, flat_kv.shape[1]), bf16),
        ),
        in_specs=[ANY] * 2 + [VMEM] * 5,
        out_specs=(VMEM, VMEM, VMEM),
        scratch_shapes=[
            pltpu.VMEM((2, count, width), bf16),
            pltpu.VMEM((2 * count, width), bf16),
            pltpu.SemaphoreType.DMA((2,)),
        ],
        compiler_params=PARAMS,
        cost_estimate=takes(8),
        name="project",
    )(own, other, gain, cosine, sine, w_query, flat_kv)


def attend_rows_kernel(first, q, kv, seam, past, mixed, window, sem):
    count = q.shape[0] // 2
    if first == 0:
        copy = pltpu.make_async_copy(seam, window.at[pl.ds(0, count), :], sem)
        copy.start()
        window[count:, :] = kv[:count, :]
        copy.wait()
        keyed = window
    else:
        keyed = kv
    head = 64
    kv_heads = kv.shape[1] // (2 * head)
    per_kv = q.shape[1] // head // kv_heads
    shape = (count, 2 * count)
    row = lax.broadcasted_iota(jnp.int32, shape, 0) + count
    col = lax.broadcasted_iota(jnp.int32, shape, 1)
    reach = past[first : first + count, :1].astype(jnp.int32)
    visible = (col <= row) & (col >= row - reach)
    for kv_head in range(kv_heads):
        lanes = 2 * head * kv_head
        keys = keyed[:, lanes : lanes + head]
        values = keyed[:, lanes + head : lanes + 2 * head]
        for index in range(per_kv):
            at = (kv_head * per_kv + index) * head
            query = q[first : first + count, at : at + head]
            scores = lax.dot_general(query, keys, LAST_DIMS, preferred_element_type=f32)
            raised = jnp.where(visible, jnp.exp(scores * head ** (-0.5)), 0.0)
            probs = (raised / jnp.sum(raised, axis=-1, keepdims=True)).astype(bf16)
            made = jnp.dot(probs, values, preferred_element_type=f32)
            mixed[:, at : at + head] = made.astype(bf16)


def attend_late(q, kv, past):
    def kernel(q, kv, past, mixed):
        attend_rows_kernel(q.shape[0] // 2, q, kv, None, past, mixed, None, None)

    return pl.pallas_call(
        kernel,
        out_shape=jax.ShapeDtypeStruct((q.shape[0] // 2, q.shape[1]), bf16),
        in_specs=[VMEM] * 3,
        out_specs=VMEM,
        compiler_params=PARAMS,
        cost_estimate=takes(2),
        name="attend_late",
    )(q, kv, past)


def attend_early(q, kv, seam, past):
    return pl.pallas_call(
        functools.partial(attend_rows_kernel, 0),
        out_shape=jax.ShapeDtypeStruct((q.shape[0] // 2, q.shape[1]), bf16),
        in_specs=[VMEM, VMEM, ANY, VMEM],
        out_specs=VMEM,
        scratch_shapes=[pltpu.VMEM(kv.shape, bf16), pltpu.SemaphoreType.DMA],
        compiler_params=PARAMS,
        cost_estimate=takes(2),
        name="attend_early",
    )(q, kv, seam, past)


def outward_rows(flip, groups, unit_rows, early, late, parts, w_out, rows):
    place_parts(groups, parts, unit_rows, [(0, unit_rows, w_out, 0)])
    lane = lax.axis_index("hd")
    which = (1 - lane) if flip else lane

    @pl.when(which == 0)
    def _():
        rows[...] = early[...]

    @pl.when(which != 0)
    def _():
        rows[...] = late[...]

    return lax.dot_general(rows[...], w_out[...], LAST_DIMS, preferred_element_type=f32)


def send_kernel(groups, unit_rows, n_parts, early, late, *refs):
    parts, (out, w_out, rows) = refs[:n_parts], refs[n_parts:]
    out[...] = outward_rows(True, groups, unit_rows, early, late, parts, w_out, rows).astype(bf16)


def keep_kernel(groups, unit_rows, n_parts, early, late, tokens, flat_gain, *refs):
    parts, (out, gain, w_out, rows) = refs[:n_parts], refs[n_parts:]
    gain[...] = flat_gain[...].reshape(gain.shape)
    made = outward_rows(False, groups, unit_rows, early, late, parts, w_out, rows)
    out[...] = tokens[...].astype(f32) + made


def outward_send(groups, early, late, parts, unit_rows):
    width, depth = groups * unit_rows, parts[0].shape[1]
    return pl.pallas_call(
        functools.partial(send_kernel, groups, unit_rows, len(parts)),
        out_shape=jax.ShapeDtypeStruct((early.shape[0], width), bf16),
        in_specs=[VMEM] * (2 + len(parts)),
        out_specs=VMEM,
        scratch_shapes=[pltpu.VMEM((width, depth), bf16), pltpu.VMEM(early.shape, bf16)],
        compiler_params=PARAMS,
        cost_estimate=reads(2 * width * depth),
        name="outward_send",
    )(early, late, *parts)


def outward_keep(groups, early, late, tokens, gain, parts, unit_rows):
    width, depth = groups * unit_rows, parts[0].shape[1]
    return pl.pallas_call(
        functools.partial(keep_kernel, groups, unit_rows, len(parts)),
        out_shape=(
            jax.ShapeDtypeStruct(tokens.shape, f32),
            jax.ShapeDtypeStruct((1, width), f32),
        ),
        in_specs=[VMEM] * (4 + len(parts)),
        out_specs=(VMEM, VMEM),
        scratch_shapes=[
            pltpu.VMEM((width, depth), bf16),
            pltpu.VMEM(early.shape, bf16),
        ],
        compiler_params=PARAMS,
        cost_estimate=reads(2 * width * depth),
        name="outward_keep",
    )(early, late, tokens, gain, *parts)


def route_kernel(mine, arrived, gain, place, residual, moe_in, sent):
    added = (mine[...] + arrived[...].astype(f32)).astype(bf16)
    residual[...] = added
    moe_in[...] = normalized(added.astype(f32), gain[...])
    cap = sent.shape[0]
    rows = jnp.dot(place[cap:, :], moe_in[...], preferred_element_type=f32)
    sent[...] = rows.astype(bf16)


def route(mine, arrived, gain, place):
    cap = place.shape[0] // 2
    return pl.pallas_call(
        route_kernel,
        out_shape=(
            jax.ShapeDtypeStruct(mine.shape, bf16),
            jax.ShapeDtypeStruct(mine.shape, bf16),
            jax.ShapeDtypeStruct((cap, mine.shape[1]), bf16),
        ),
        in_specs=[VMEM] * 4,
        out_specs=(VMEM,) * 3,
        compiler_params=PARAMS,
        cost_estimate=reads(16 << 20),
        name="route",
    )(mine, arrived, gain, place)


def expert_pieces(gate_up, down, up_rows, down_rows, width):
    pieces = [(i * up_rows, up_rows, gate_up, i * width) for i in range(2)]
    pieces += [
        (2 * up_rows + i * down_rows, down_rows, down, i * width) for i in range(down.shape[1] // width)
    ]
    return pieces, pieces[-1][0] + down_rows


def gate_kernel(groups, up_rows, down_rows, shards, moe_in, router_in, ids_in, place, *refs):
    parts, (gates, own, spread, gate_up, down, router, ids, sems, part_sems) = (
        refs[: len(shards)],
        refs[len(shards) :],
    )
    small = fetch([(router_in, router), (ids_in, ids)], sems)
    width = parts[0].shape[1]
    pieces, unit_rows = expert_pieces(gate_up, down, up_rows, down_rows, width)
    copies = fetch(part_copies(groups, parts, shards, unit_rows, pieces), part_sems)
    cap = own.shape[0]
    own[...] = jnp.dot(place[:cap, :], moe_in[...], preferred_element_type=f32).astype(bf16)
    tokens = ids.shape[1]
    row = lax.broadcasted_iota(jnp.int32, (tokens, tokens), 0)
    eye = (row == lax.broadcasted_iota(jnp.int32, (tokens, tokens), 1)).astype(f32)
    spread[...] = lax.dot_general(
        eye.astype(bf16), place[...], LAST_DIMS, preferred_element_type=f32
    ).astype(bf16)
    for copy in small:
        copy.wait()
    hit = named_experts(ids, router.shape[0])
    named = lax.dot_general(eye, hit, LAST_DIMS, preferred_element_type=f32)
    logits = lax.dot_general(moe_in[...], router[...], LAST_DIMS, preferred_element_type=f32)
    raised = jnp.where(named > 0, jnp.exp(logits), 0.0)
    gates[...] = raised / jnp.sum(raised, axis=-1, keepdims=True)
    for copy in copies:
        copy.wait()


def gate(groups, moe_in, router_t, ids_t, place, early, up_rows, down_rows):
    cap = place.shape[0] // 2
    tokens, model = moe_in.shape
    width = early[0][0].shape[1]
    units = 2 * len(early)
    far = [pltpu.with_memory_space_constraint(part, pltpu.HBM) for part in (router_t, ids_t)]
    return pl.pallas_call(
        functools.partial(gate_kernel, groups, up_rows, down_rows, [shard for _, shard in early]),
        out_shape=(
            jax.ShapeDtypeStruct((tokens, router_t.shape[0]), f32),
            jax.ShapeDtypeStruct((cap, model), bf16),
            jax.ShapeDtypeStruct(place.shape[::-1], bf16),
            jax.ShapeDtypeStruct((groups * up_rows, 2 * width), bf16),
            jax.ShapeDtypeStruct((groups * down_rows, model), bf16),
        ),
        in_specs=[VMEM, ANY, ANY, VMEM] + [ANY] * len(early),
        out_specs=(VMEM,) * 5,
        scratch_shapes=[
            pltpu.VMEM(router_t.shape, bf16),
            pltpu.VMEM(ids_t.shape, jnp.int32),
            pltpu.SemaphoreType.DMA((2,)),
            pltpu.SemaphoreType.DMA((units * (2 + model // width),)),
        ],
        compiler_params=PARAMS,
        cost_estimate=LITTLE,
        name="gate",
    )(moe_in, *far, place, *[part for part, _ in early])


def part_copies(groups, parts, shards, unit_rows, pieces):
    sources = ring_sources(groups, lax.axis_index("grp"))
    pairs = []
    for part, shard in zip(parts, shards):
        for unit in range(part.shape[0] // unit_rows):
            for first, rows, target, lane in pieces:
                at = pl.multiple_of(sources[shard + unit] * rows, rows)
                pairs.append(
                    (
                        part.at[pl.ds(unit * unit_rows + first, rows), :],
                        target.at[pl.ds(at, rows), pl.ds(lane, part.shape[1])],
                    )
                )
    return pairs


def expert_kernel(groups, up_rows, down_rows, shards, own, other, gate_up_in, down_in, *refs):
    parts = refs[: len(shards)]
    own_out, other_out, gate_up, down, rows, sems, down_sems = refs[len(shards) :]
    width = parts[0].shape[1]
    pieces, unit_rows = expert_pieces(gate_up, down, up_rows, down_rows, width)
    ups = fetch(part_copies(groups, parts, shards, unit_rows, pieces[:2]), sems)
    downs = fetch(part_copies(groups, parts, shards, unit_rows, pieces[2:]), down_sems)
    count = own.shape[0]
    rows[:count, :] = own[...]
    rows[count:, :] = other[...]
    for copy in ups:
        copy.wait()
    both = jnp.dot(rows[...], gate_up[...], preferred_element_type=f32)
    gate, up = both[:, :width], both[:, width:]
    hidden = (gate / (1.0 + jnp.exp(-gate)) * up).astype(bf16)
    for copy in downs:
        copy.wait()
    made = jnp.dot(hidden, down[...], preferred_element_type=f32).astype(bf16)
    own_out[...] = made[:count, :]
    other_out[...] = made[count:, :]


def expert(groups, own, other, staged, late, up_rows, down_rows):
    count, model = own.shape
    width = late[0][0].shape[1]
    units = sum(part.shape[0] for part, _ in late) // (2 * up_rows + model // width * down_rows)
    return pl.pallas_call(
        functools.partial(expert_kernel, groups, up_rows, down_rows, [shard for _, shard in late]),
        out_shape=(jax.ShapeDtypeStruct(own.shape, bf16),) * 2
        + tuple(jax.ShapeDtypeStruct(part.shape, bf16) for part in staged),
        in_specs=[VMEM] * 4 + [ANY] * len(late),
        out_specs=(VMEM,) * 4,
        scratch_shapes=[
            pltpu.VMEM((2 * count, model), bf16),
            pltpu.SemaphoreType.DMA((2 * units,)),
            pltpu.SemaphoreType.DMA((model // width * units,)),
        ],
        input_output_aliases={2: 2, 3: 3},
        compiler_params=PARAMS,
        cost_estimate=pl.CostEstimate(flops=int(6.2 * 1.15e9), bytes_accessed=1, transcendentals=0),
        name="expert",
    )(own, other, *staged, *[part for part, _ in late])[:2]


def combine_kernel(residual, gates, spread, own, returned, out):
    lane = lax.axis_index("hd")
    count = own.shape[0]
    column = lax.broadcasted_iota(jnp.int32, gates.shape, 1)
    total = jnp.zeros(residual.shape, f32)
    for index, made in ((0, own), (1, returned)):
        live = lane if index == 0 else 1 - lane
        weight = jnp.sum(jnp.where(column == live, gates[...], 0.0), axis=-1, keepdims=True)
        picked = jnp.dot(
            spread[:, index * count : (index + 1) * count], made[...], preferred_element_type=f32
        )
        total += weight * picked
    out[...] = (residual[...].astype(f32) + total).astype(bf16)


def combine(residual, gates, spread, own, returned):
    return pl.pallas_call(
        combine_kernel,
        out_shape=jax.ShapeDtypeStruct(residual.shape, bf16),
        in_specs=[VMEM] * 5,
        out_specs=VMEM,
        compiler_params=PARAMS,
        cost_estimate=reads(6 * residual.shape[0] * residual.shape[1]),
        name="combine",
    )(residual, gates, spread, own, returned)


def bundle_kernel(send, kv, tags, result, out, sem):
    groups, rows, _ = out.shape
    heads = kv.shape[1] // 128
    capc = send.shape[0] // groups
    packed = jnp.dot(send[...], kv[...], preferred_element_type=f32).astype(bf16)
    tagged = jnp.dot(send[...], tags[...], preferred_element_type=f32)
    one = (lax.broadcasted_iota(jnp.int32, (16, 128), 0) == lax.broadcasted_iota(jnp.int32, (16, 128), 1))
    for owner in range(groups):
        mine = slice(owner * capc, (owner + 1) * capc)
        for head in range(heads):
            out[owner, head * capc : (head + 1) * capc, :] = packed[mine, head * 128 : (head + 1) * 128]
        wide = jnp.concatenate([tagged[mine, :], jnp.zeros((128 - capc, 128), f32)], axis=0)
        out[owner, heads * capc :, :] = lax.dot_general(
            one.astype(f32), wide, LAST_DIMS, preferred_element_type=f32
        ).astype(bf16)
    copy = pltpu.make_async_copy(out, result, sem)
    copy.start()
    copy.wait()


def bundle(groups, send, kv, tags):
    rows = send.shape[0] // groups * (kv.shape[1] // 128) + 16
    return pl.pallas_call(
        bundle_kernel,
        out_shape=pltpu.HBM((groups, rows, 128), bf16),
        in_specs=[VMEM] * 3,
        out_specs=HBM,
        scratch_shapes=[pltpu.VMEM((groups, rows, 128), bf16), pltpu.SemaphoreType.DMA],
        compiler_params=PARAMS,
        cost_estimate=LITTLE,
        name="bundle",
    )(send, kv, tags)


def write_kernel(heads, arrived, cache, out, rows, wide, known):
    groups, size, _ = arrived.shape
    slots = cache.shape[0] // heads
    capc = (size - 16) // heads
    high, low = [], []
    for source in range(groups):
        for head in range(heads):
            rows[source * capc : (source + 1) * capc, head * 128 : (head + 1) * 128] = arrived[
                source, head * capc : (head + 1) * capc, :
            ]
        numbers = arrived[source, heads * capc :, :].astype(f32)
        high.append(numbers[0:1, :capc])
        low.append(numbers[1:2, :capc])
    slot = jnp.concatenate(high, axis=1) * 64.0 + jnp.concatenate(low, axis=1) - 64.0
    row = lax.broadcasted_iota(jnp.int32, (slots, slot.shape[1]), 0).astype(f32)
    hit = (row == slot).astype(bf16)
    made = jnp.dot(hit, rows[...], preferred_element_type=f32)
    found = jnp.dot(hit, jnp.ones((slot.shape[1], 128), bf16), preferred_element_type=f32)
    for head in range(heads):
        wide[pl.ds(head, slots, heads), :] = made[:, head * 128 : (head + 1) * 128]
        known[pl.ds(head, slots, heads), :] = found
    old = cache[...].astype(f32)
    out[...] = jnp.where(known[...] > 0.0, wide[...], old).astype(bf16)


def write(arrived, cache):
    slots, heads, lanes = cache.shape
    capc = (arrived.shape[1] - 16) // heads
    flat = (slots * heads, lanes)
    written = pl.pallas_call(
        functools.partial(write_kernel, heads),
        out_shape=jax.ShapeDtypeStruct(flat, bf16),
        in_specs=[VMEM] * 2,
        out_specs=VMEM,
        scratch_shapes=[
            pltpu.VMEM((arrived.shape[0] * capc, heads * lanes), bf16),
            pltpu.VMEM(flat, f32),
            pltpu.VMEM(flat, f32),
        ],
        compiler_params=PARAMS,
        cost_estimate=reads(1 << 21),
        name="write",
    )(arrived, cache.reshape(flat))
    return written.reshape(cache.shape)


def two_lane_shards(
    tokens,
    positions,
    attn_gain,
    w_query,
    w_keyval,
    w_out,
    moe_gain,
    router,
    w_gate_up,
    w_down,
    expert_ids,
    cache_slot,
    kv_cache,
):
    groups = lax.axis_size("grp")
    tok_rows, model = tokens.shape
    block = positions.shape[0]
    kv_local, head2 = w_keyval.shape[1:]
    kv_width = kv_local * head2
    slots_dev = kv_cache.shape[0]
    swap = functools.partial(lax.ppermute, axis_name="hd", perm=[(0, 1), (1, 0)])

    together = lax.optimization_barrier

    other_tokens = swap(tokens)
    own = (w_gate_up[0], w_down[0], w_out.T)
    up_rows, down_rows = own[0].shape[0], own[1].shape[0]
    beside = [lax.ppermute(part, "grp", sibling_pairs(groups)) for part in own]
    expert_pair, out_pair = pack(own, beside)
    out_ring = Ring(out_pair, groups)
    out_ring.step()
    expert_ring = Ring(expert_pair, groups)
    expert_ring.step()
    w_keyval, positions = together((w_keyval, positions, out_pair))[:2]
    flat_kv = w_keyval.reshape(model, kv_width)
    cosine, sine, past, place, send, tags, gain = prepare(
        groups, slots_dev, positions, cache_slot, expert_ids, attn_gain
    )
    cosine, flat_kv = out_ring.pin(cosine, flat_kv)
    out_ring.step()

    q, kv, tail = project(tokens, other_tokens, gain, cosine, sine, w_query, flat_kv)
    seam = lax.ppermute(tail, "grp", [(g, g + 1) for g in range(groups - 1)])
    q = out_ring.pin(q)
    out_ring.step()
    out_ring.share(2)
    late = attend_late(q, kv, past)
    seam, late = together((seam, late))
    seam = expert_ring.pin(seam)
    expert_ring.step()
    early = attend_early(q, kv, seam, past)
    early, out_ring.near = together((early, out_ring.near))
    early = out_ring.pin(early)
    out_ring.step()
    out_ring.share(3)
    early, kv, out_ring.near = together((early, kv, out_ring.near))
    outgoing = bundle(groups, send, kv, tags)
    early, outgoing = together((early, outgoing))
    early = out_ring.pin(early)
    early = expert_ring.pin(early)
    expert_ring.step()
    out_ring.share()
    sent = outward_send(groups, early, late, out_ring.parts(), out_ring.unit_rows)
    arrived = swap(sent)
    early = together((early, sent))[0]
    mine, late_gain = outward_keep(
        groups, early, late, tokens, moe_gain, out_ring.parts(), out_ring.unit_rows
    )
    late_gain = expert_ring.pin(late_gain)
    expert_ring.share()
    expert_ring.step()
    outgoing = together((outgoing, sent))[0]
    arrived_cache = lax.all_to_all(outgoing, "grp", split_axis=0, concat_axis=0, tiled=True)
    arrived, late_gain = expert_ring.pin(arrived, late_gain)
    expert_ring.share()

    residual, moe_in, sent_rows = route(mine, arrived, late_gain, place)
    landed = swap(sent_rows)
    parts_early, parts_late = expert_ring.split()
    gates, own_rows, spread, *staged = gate(
        groups, moe_in, router.T, expert_ids.T, place, parts_early, up_rows, down_rows
    )
    landed, own_rows = together((landed, own_rows))
    own_made, back = expert(groups, own_rows, landed, staged, parts_late, up_rows, down_rows)
    returned = swap(back)
    layer_out = combine(residual, gates, spread, own_made, returned)
    layer_out, arrived_cache = together((layer_out, arrived_cache))
    cache_after = write(arrived_cache, kv_cache)
    return (layer_out, cache_after)


def passed_along(value, axis, steps):
    count = lax.axis_size(axis)
    initial, last = (max(0, -steps), min(count, count - steps))
    return lax.ppermute(value, axis, [(source, source + steps) for source in range(initial, last)])


def rms_norm(row_set, norm_gain):
    floats = row_set.astype(jnp.float32)
    factor = lax.rsqrt(jnp.mean(floats * floats, axis=-1, keepdims=True) + norm_eps)
    return (floats * factor * norm_gain).astype(jnp.bfloat16)


def rotate(vectors, angle_pos):
    halves = vectors.shape[-1] // 2
    inverse_freq = rope_base ** (-2.0 * jnp.arange(halves, dtype=jnp.float32) / vectors.shape[-1])
    angles = angle_pos[:, None, None] * inverse_freq[None, None, :]
    cosine = jnp.cos(angles)
    sine_part = jnp.sin(angles)
    first_half = vectors[..., :halves]
    second_half = vectors[..., halves:]
    return jnp.concatenate(
        [
            first_half * cosine - second_half * sine_part,
            second_half * cosine + first_half * sine_part,
        ],
        axis=-1,
    )


def expert_rows(row_set, gate_up, down_rows):
    gate_and_up = jnp.dot(row_set, gate_up, preferred_element_type=jnp.float32)
    inner_width = gate_and_up.shape[1] // 2
    hidden = (jax.nn.silu(gate_and_up[:, :inner_width]) * gate_and_up[:, inner_width:]).astype(
        jnp.bfloat16
    )
    return jnp.dot(hidden, down_rows, preferred_element_type=jnp.float32).astype(jnp.bfloat16)


def attend_rows(query_blk, keys_blk, vals_blk, visible, scale_qk):
    scores = (
        jnp.einsum("qkgd,skd->kgqs", query_blk, keys_blk, preferred_element_type=jnp.float32)
        * scale_qk
    )
    weights_f = jnp.where(visible[None, None], jnp.exp(scores), 0.0)
    prob_bf = (weights_f / jnp.sum(weights_f, axis=-1, keepdims=True)).astype(jnp.bfloat16)
    return jnp.einsum("kgqs,skd->qkgd", prob_bf, vals_blk, preferred_element_type=jnp.float32)


def shards(
    tokens,
    positions,
    attn_gain,
    w_query,
    w_keyval,
    w_out,
    moe_gain,
    router,
    w_gate_up,
    w_down,
    expert_ids,
    cache_slot,
    kv_cache,
):
    lane_count = lax.axis_size("hd")
    group_count = lax.axis_size("grp")
    tok_rows = tokens.shape[0]
    model_width = tokens.shape[1]
    block_len = positions.shape[0]
    seg_most = block_len // 2
    head_dim = w_keyval.shape[2] // 2
    kv_local = w_keyval.shape[1]
    q_local = w_query.shape[1] // head_dim
    per_kv = q_local // kv_local
    expert_cap = tok_rows // 4
    normed = rms_norm(tokens, attn_gain)
    flat_kv = w_keyval.reshape(model_width, kv_local * 2 * head_dim)
    section = lax.all_gather(normed, "hd", axis=0, tiled=True)
    projected = jnp.concatenate(
        [
            jnp.dot(section, w_query, preferred_element_type=jnp.float32),
            jnp.dot(section, flat_kv, preferred_element_type=jnp.float32),
        ],
        axis=1,
    )
    angle_pos = jnp.maximum(positions, 0).astype(jnp.float32)
    queries = rotate(
        projected[:, : q_local * head_dim].reshape(block_len, q_local, head_dim), angle_pos
    ).astype(jnp.bfloat16)
    key_val = projected[:, q_local * head_dim :].reshape(block_len, kv_local, 2 * head_dim)
    rotated = rotate(key_val[:, :, :head_dim], angle_pos).astype(jnp.bfloat16)
    stored = jnp.concatenate([rotated, key_val[:, :, head_dim:].astype(jnp.bfloat16)], axis=2)
    seam_rows = passed_along(stored[block_len - seg_most :], "grp", 1)
    window = jnp.concatenate([seam_rows, stored], axis=0)
    scale_qk = head_dim ** (-0.5)
    local_rows = jnp.arange(block_len, dtype=jnp.int32)
    lowest = local_rows - jnp.maximum(positions, 0)
    pieces_out = []
    for q_block in range(2):
        first_row = q_block * seg_most
        rows_here = first_row + jnp.arange(seg_most, dtype=jnp.int32)
        cols_here = first_row - seg_most + jnp.arange(2 * seg_most, dtype=jnp.int32)
        low_here = lowest[first_row : first_row + seg_most]
        visible = (cols_here[None, :] >= low_here[:, None]) & (
            cols_here[None, :] <= rows_here[:, None]
        )
        query_blk = queries[first_row : first_row + seg_most].reshape(
            seg_most, kv_local, per_kv, head_dim
        )
        keys_blk = window[first_row : first_row + 2 * seg_most, :, :head_dim]
        vals_blk = window[first_row : first_row + 2 * seg_most, :, head_dim:]
        mixed_rows = attend_rows(query_blk, keys_blk, vals_blk, visible, scale_qk)
        pieces_out.append(mixed_rows.reshape(seg_most, q_local * head_dim).astype(jnp.bfloat16))
    attended = jnp.concatenate(pieces_out, axis=0)
    slots_dev = kv_cache.shape[0]
    capc = 2 * block_len // group_count
    live_slot = cache_slot >= 0
    owners = jnp.where(live_slot, cache_slot // slots_dev, group_count)
    owner_hit = (owners[:, None] == jnp.arange(group_count, dtype=jnp.int32)[None, :]).astype(
        jnp.bfloat16
    )
    lower_tri = (local_rows[:, None] >= local_rows[None, :]).astype(jnp.bfloat16)
    running = jnp.dot(lower_tri, owner_hit, preferred_element_type=jnp.float32)
    owner_rank = jnp.sum(running * owner_hit.astype(jnp.float32), axis=1).astype(jnp.int32) - 1
    send_rows = jnp.where(live_slot, owners * capc + owner_rank, group_count * capc)
    outgoing_cache = (
        jnp.zeros((group_count * capc, kv_local, 2 * head_dim), jnp.bfloat16)
        .at[send_rows]
        .set(stored, mode="drop")
    )
    outgoing_slots = (
        jnp.full((group_count * capc,), -1, jnp.int32)
        .at[send_rows]
        .set(cache_slot % slots_dev, mode="drop")
    )
    arrived, arrived_slots = (
        lax.all_to_all(
            outgoing_cache.reshape(group_count, capc, kv_local, 2 * head_dim),
            "grp",
            split_axis=0,
            concat_axis=0,
            tiled=True,
        ),
        lax.all_to_all(
            outgoing_slots.reshape(group_count, capc),
            "grp",
            split_axis=0,
            concat_axis=0,
            tiled=True,
        ),
    )
    flat_slots = arrived_slots.reshape(group_count * capc)
    write_rows = jnp.where(flat_slots >= 0, flat_slots, slots_dev).astype(jnp.int32)
    cache_after = kv_cache.at[write_rows].set(
        arrived.reshape(group_count * capc, kv_local, 2 * head_dim), mode="drop"
    )
    by_token = lax.all_to_all(attended, "hd", split_axis=0, concat_axis=1, tiled=True)
    attn_proj = jnp.dot(
        by_token,
        lax.all_gather(w_out, "grp", axis=1, tiled=True),
        preferred_element_type=jnp.float32,
    )
    residual = (tokens.astype(jnp.float32) + attn_proj).astype(jnp.bfloat16)
    moe_in = rms_norm(residual, moe_gain)
    logits = jnp.dot(moe_in, router, preferred_element_type=jnp.float32)
    expert_range = jnp.arange(router.shape[1], dtype=jnp.int32)
    matches_all = expert_ids[:, :, None] == expert_range[None, None, :]
    chosen = jnp.sum(jnp.where(matches_all, logits[:, None, :], 0.0), axis=2)
    raised = jnp.exp(chosen)
    gates = raised / jnp.sum(raised, axis=1, keepdims=True)
    live_range = jnp.arange(lane_count, dtype=jnp.int32)
    matches = expert_ids[:, :, None] == live_range[None, None, :]
    member = jnp.any(matches, axis=1)
    weighting = jnp.sum(jnp.where(matches, gates[:, :, None], 0.0), axis=1)
    ranking = jnp.cumsum(member.astype(jnp.int32), axis=0) - 1
    target = jnp.where(member, live_range[None, :] * expert_cap + ranking, -1)
    slot_range = jnp.arange(lane_count * expert_cap, dtype=jnp.int32)
    slot_hits = target[None, :, :] == slot_range[:, None, None]
    placing = jnp.any(slot_hits, axis=2).astype(jnp.bfloat16)
    outgoing = (
        jnp.dot(placing, moe_in, preferred_element_type=jnp.float32)
        .astype(jnp.bfloat16)
        .reshape(lane_count, expert_cap, model_width)
    )
    gate_up_all, down_all = (
        lax.all_gather(w_gate_up, "grp", axis=1, tiled=True),
        lax.all_gather(w_down, "grp", axis=1, tiled=True),
    )
    gate_up_mat = gate_up_all[0]
    down_mat = down_all[0]
    landed = lax.all_to_all(outgoing, "hd", split_axis=0, concat_axis=0, tiled=True)
    results = expert_rows(landed.reshape(-1, model_width), gate_up_mat, down_mat).reshape(landed.shape)
    returned = lax.all_to_all(results, "hd", split_axis=0, concat_axis=0, tiled=True)
    flat_returned = returned.reshape(-1, model_width)
    fetched = flat_returned[jnp.maximum(target, 0)]
    used_weight = jnp.where(member, weighting, 0.0)
    moe_total = jnp.sum(used_weight[:, :, None] * fetched.astype(jnp.float32), axis=1)
    layer_out = (residual.astype(jnp.float32) + moe_total).astype(jnp.bfloat16)
    return (layer_out, cache_after)


def solution(mesh):
    two_lanes = mesh.shape["hd"] == 2 and mesh.shape["grp"] % 8 == 0
    return jax.shard_map(
        two_lane_shards if two_lanes else shards,
        mesh=mesh,
        in_specs=(
            P(("grp", "hd"), None),
            P("grp"),
            P(),
            P(None, "hd"),
            P(None, "hd", None),
            P(None, "grp"),
            P(),
            P(),
            P("hd", "grp", None),
            P("hd", "grp", None),
            P(("grp", "hd"), None),
            P("grp"),
            P("grp", "hd", None),
        ),
        out_specs=(P(("grp", "hd"), None), P("grp", "hd", None)),
        check_vma=False,
    )
```

```python
import functools

import jax
import jax.numpy as jnp
import numpy as np
from jax import lax
from jax.experimental import pallas as pl
from jax.experimental.pallas import tpu as pltpu
from jax.sharding import PartitionSpec as P

norm_eps = 1e-05
rope_base = 10000.0
bf16 = jnp.bfloat16
f32 = jnp.float32
LAST_DIMS = (((1,), (1,)), ((), ()))


def ring_cycle(groups):
    rows = groups // 4
    return [2 * r for r in range(rows)] + [2 * r + 1 for r in reversed(range(rows))]


def ring_pairs(groups):
    cycle = ring_cycle(groups)
    count = len(cycle)
    pairs = []
    for place, pair in enumerate(cycle):
        pairs.append((2 * pair, 2 * cycle[(place + 1) % count]))
        pairs.append((2 * pair + 1, 2 * cycle[(place - 1) % count] + 1))
    return pairs


def sibling_pairs(groups):
    return [(g, g ^ 1) for g in range(groups)]


def ring_sources(groups, me):
    count = groups // 2
    rows = count // 2
    side, pair = me % 2, me // 2
    row, col = pair // 2, pair % 2
    place = jnp.where(col == 0, row, count - 1 - row)

    def block(core, steps):
        there = (place + (2 * core - 1) * steps + count) % count
        other = jnp.where(there < rows, 2 * there, 2 * (count - 1 - there) + 1)
        return [2 * other + core, 2 * other + 1 - core]

    full = (count - 1) // 2
    listed = [me, me + 1 - 2 * side]
    for core in (side, 1 - side):
        for steps in range(1, full + 1):
            listed += block(core, steps)
    return listed + [block(side, count // 2)[0], block(1 - side, count // 2)[0]]


def cut_kernel(whole, out, sem):
    copy = pltpu.make_async_copy(whole.at[pl.ds(0, out.shape[0]), :], out, sem)
    copy.start()
    copy.wait()


def cut(whole, rows):
    return pl.pallas_call(
        cut_kernel,
        out_shape=jax.ShapeDtypeStruct((rows, whole.shape[1]), whole.dtype),
        in_specs=[pl.BlockSpec(memory_space=pl.ANY)],
        out_specs=pl.BlockSpec(memory_space=pltpu.VMEM),
        scratch_shapes=[pltpu.SemaphoreType.DMA],
        cost_estimate=pl.CostEstimate(flops=1, bytes_accessed=1 << 22, transcendentals=0),
        name="cut",
    )(whole)


class Ring:
    def __init__(self, pair, groups, first):
        self.first = first
        self.across = functools.partial(lax.ppermute, axis_name="grp", perm=ring_pairs(groups))
        self.beside = functools.partial(lax.ppermute, axis_name="grp", perm=sibling_pairs(groups))
        self.full = (groups // 2 - 1) // 2
        self.unit_rows = pair.shape[0] // 2
        self.mine = [pair]
        self.near = []

    def step(self):
        held = self.mine[-1]
        if len(self.mine) > self.full:
            held = self.first(held, self.unit_rows)
        self.mine.append(self.across(held))

    def pin(self, *others):
        done = lax.optimization_barrier((self.mine[-1],) + others)
        self.mine[-1] = done[0]
        return done[1:] if len(others) > 1 else done[1]

    def share(self, upto=None):
        for index in range(1 + len(self.near), 1 + (upto or len(self.mine) - 1)):
            self.near.append(self.beside(self.mine[index]))

    def parts(self):
        full = self.full
        return self.mine[: full + 1] + self.near[:full] + [self.mine[full + 1], self.near[full]]

    def split(self):
        full = self.full
        listed = [(part, 2 * index) for index, part in enumerate(self.parts()[:-1])]
        listed.append((self.near[full], 4 * full + 3))
        late = (full, 2 * full, 2 * full + 1, 2 * full + 2)
        return (
            [pair for index, pair in enumerate(listed) if index not in late],
            [listed[index] for index in late],
        )


def place_parts(groups, parts, unit_rows, pieces, shards=None):
    sources = ring_sources(groups, lax.axis_index("grp"))
    shard = 0
    for index, part in enumerate(parts):
        shard = shards[index] if shards else shard
        for unit in range(part.shape[0] // unit_rows):
            for first, rows, target, lane in pieces:
                at = pl.multiple_of(sources[shard] * rows, rows)
                start = unit * unit_rows + first
                target[pl.ds(at, rows), lane : lane + part.shape[1]] = part[start : start + rows, :]
            shard += 1


VMEM = pl.BlockSpec(memory_space=pltpu.VMEM)
ANY = pl.BlockSpec(memory_space=pl.ANY)
HBM = pl.BlockSpec(memory_space=pltpu.HBM)
PARAMS = pltpu.CompilerParams(vmem_limit_bytes=16 << 20)


LITTLE = pl.CostEstimate(flops=1, bytes_accessed=1, transcendentals=0)


def takes(us):
    return pl.CostEstimate(
        flops=int(us * 1.15e9), bytes_accessed=int(us * 8e6), transcendentals=0
    )


def reads(nbytes):
    return pl.CostEstimate(flops=1, bytes_accessed=nbytes, transcendentals=0)


def normalized(floats, gain):
    factor = lax.rsqrt(jnp.mean(floats * floats, axis=-1, keepdims=True) + norm_eps)
    return (floats * factor * gain).astype(bf16)


def fetch(pairs, sems):
    copies = []
    for index, (source, target) in enumerate(pairs):
        copies.append(pltpu.make_async_copy(source, target, sems.at[index]))
        copies[-1].start()
    return copies


def pack_kernel(*refs):
    sources, (expert_pair, out_pair, sems) = refs[:6], refs[6:]
    width = expert_pair.shape[1]
    lane = lax.axis_index("hd")
    first = pl.multiple_of(lane * out_pair.shape[1], out_pair.shape[1])
    pairs = []
    row = 0
    for index in range(2):
        up, down, w_out = sources[3 * index : 3 * index + 3]
        count = w_out.shape[0]
        pairs.append(
            (w_out.at[:, pl.ds(first, out_pair.shape[1])], out_pair.at[pl.ds(index * count, count), :])
        )
        for source in (up, down):
            for at in range(0, source.shape[1], width):
                pairs.append(
                    (source.at[:, pl.ds(at, width)], expert_pair.at[pl.ds(row, source.shape[0]), :])
                )
                row += source.shape[0]
    for copy in fetch(pairs, sems):
        copy.wait()


def pack(own, beside):
    own = [pltpu.with_memory_space_constraint(part, pltpu.HBM) for part in own]
    up, down, w_out_t = own
    width = up.shape[1] // 2
    pieces = [up.shape[1] // width, down.shape[1] // width]
    unit_rows = pieces[0] * up.shape[0] + pieces[1] * down.shape[0]
    return pl.pallas_call(
        pack_kernel,
        out_shape=(
            jax.ShapeDtypeStruct((2 * unit_rows, width), bf16),
            jax.ShapeDtypeStruct((2 * w_out_t.shape[0], w_out_t.shape[1] // 2), bf16),
        ),
        in_specs=[ANY] * 6,
        out_specs=(ANY, ANY),
        scratch_shapes=[pltpu.SemaphoreType.DMA((2 + 2 * sum(pieces),))],
        compiler_params=PARAMS,
        cost_estimate=LITTLE,
        name="pack",
    )(*own, *beside)


def as_column(row, eye):
    return jnp.sum(jnp.where(eye, row, 0.0), axis=1, keepdims=True)


def named_experts(ids, experts):
    tokens = ids.shape[1]
    expert = lax.broadcasted_iota(jnp.int32, (experts, tokens), 0)
    hit = jnp.zeros((experts, tokens), f32)
    for index in range(ids.shape[0]):
        hit = jnp.where(ids[index : index + 1, :] == expert, 1.0, hit)
    return hit


def prepare_kernel(groups, slots_dev, *refs):
    sources, (cosine, sine, past, place, send, tags, gain) = refs[:4], refs[4:11]
    positions, slots, ids, flat_gain, sems = refs[11:]
    copies = fetch(list(zip(sources, (positions, slots, ids, flat_gain))), sems)
    for copy in copies:
        copy.wait()
    gain[...] = flat_gain[...].reshape(gain.shape)
    lane = lax.axis_index("hd")
    block = positions.shape[1]

    def iota(shape, dim):
        return lax.broadcasted_iota(jnp.int32, shape, dim)

    eye = iota((block, block), 0) == iota((block, block), 1)
    reach = as_column(jnp.maximum(positions[...], 0).astype(f32), eye)
    past[...] = jnp.broadcast_to(reach, past.shape)
    column = iota((8, 128), 1)
    exponent = (column % 32).astype(f32) * (-2.0 / 64)
    inverse_freq = jnp.exp(exponent * np.float32(np.log(rope_base)))[:1, :]
    angles = reach * inverse_freq
    cosine[...] = jnp.cos(angles)
    turned = jnp.sin(angles)
    sine[...] = jnp.where(iota(angles.shape, 1) % 64 < 32, -turned, turned)

    tokens = ids.shape[1]
    cap = place.shape[0] // 2
    hit = named_experts(ids, 8)
    upto = (iota((tokens, tokens), 0) <= iota((tokens, tokens), 1)).astype(f32)
    rank = jnp.dot(hit, upto, preferred_element_type=f32) - 1.0
    slot = iota((2 * cap, tokens), 0).astype(f32)
    placed = jnp.zeros((2 * cap, tokens), f32)
    for live in range(2):
        order = jnp.where(lane == live, 0, cap).astype(f32)
        member = hit[live : live + 1, :] > 0.0
        placed = jnp.where(member & (slot == rank[live : live + 1, :] + order), 1.0, placed)
    place[...] = placed.astype(bf16)

    where = slots[...]
    owner = jnp.where(where >= 0, where // slots_dev, -1)
    owner_hit = (iota((groups, block), 0) == owner).astype(f32)
    before = (iota((block, block), 0) <= iota((block, block), 1)).astype(f32)
    running = jnp.dot(owner_hit, before, preferred_element_type=f32)
    owner_rank = jnp.sum(owner_hit * running, axis=0, keepdims=True) - 1.0
    capc = send.shape[0] // groups
    row = jnp.where(owner >= 0, owner * capc + owner_rank.astype(jnp.int32), -1)
    send[...] = (iota(send.shape, 0) == row).astype(bf16)
    inside = jnp.where(where >= 0, where % slots_dev, 0)
    high = as_column((inside // 64 + 1).astype(f32), eye)
    low = as_column((inside % 64).astype(f32), eye)
    spot = iota(tags.shape, 1)
    tags[...] = jnp.where(spot == 0, high, jnp.where(spot == 1, low, 0.0)).astype(bf16)


def prepare(groups, slots_dev, positions, slots, ids, gain):
    block, tokens = positions.shape[0], ids.shape[0]
    model = gain.shape[0]
    cap = tokens // 4
    capc = 2 * block // groups
    shapes = [
        ((block, 128), f32),
        ((block, 128), f32),
        ((block, 128), f32),
        ((2 * cap, tokens), bf16),
        ((groups * capc, block), bf16),
        ((block, 128), bf16),
        ((1, model), f32),
    ]
    sources = (positions[None], slots[None], ids.T, gain)
    return pl.pallas_call(
        functools.partial(prepare_kernel, groups, slots_dev),
        out_shape=tuple(jax.ShapeDtypeStruct(shape, kind) for shape, kind in shapes),
        in_specs=[ANY] * 4,
        out_specs=(VMEM,) * len(shapes),
        scratch_shapes=[
            pltpu.VMEM((1, block), jnp.int32),
            pltpu.VMEM((1, block), jnp.int32),
            pltpu.VMEM(ids.shape[::-1], jnp.int32),
            pltpu.VMEM((model,), f32),
            pltpu.SemaphoreType.DMA((4,)),
        ],
        compiler_params=PARAMS,
        cost_estimate=LITTLE,
        name="prepare",
    )(*[pltpu.with_memory_space_constraint(source, pltpu.HBM) for source in sources])


def project_kernel(
    own, other, gain, cosine, sine, w_query, w_keyval, q_out, kv_out, seam_out, raw, rows, sems
):
    count = own.shape[0]
    lane = lax.axis_index("hd")
    mine = pl.multiple_of(lane * count, count)
    theirs = pl.multiple_of((1 - lane) * count, count)
    copies = fetch([(own, raw.at[0]), (other, raw.at[1])], sems)
    cos_q, sin_q = cosine[...], sine[...]
    column = lax.broadcasted_iota(jnp.int32, cos_q.shape, 1)
    lower = column % 64 < 32
    cos_kv = jnp.where(column < 64, cos_q, 1.0)
    sin_kv = jnp.where(column < 64, sin_q, 0.0)
    for index, first in ((0, mine), (1, theirs)):
        copies[index].wait()
        rows[pl.ds(first, count), :] = normalized(raw[index].astype(f32), gain[...])
    width = 256
    for weights, out, cos, sin in ((w_keyval, kv_out, cos_kv, sin_kv), (w_query, q_out, cos_q, sin_q)):
        for first in range(0, weights.shape[1], width):
            made = jnp.dot(rows[...], weights[:, first : first + width], preferred_element_type=f32)
            for part in range(0, width, 128):
                here = made[:, part : part + 128]
                turned = jnp.where(lower, pltpu.roll(here, 96, 1), pltpu.roll(here, 32, 1))
                done = (here * cos + turned * sin).astype(bf16)
                out[:, first + part : first + part + 128] = done
                if out is kv_out:
                    seam_out[:, first + part : first + part + 128] = done[count:, :]


def project(own, other, gain, cosine, sine, w_query, flat_kv):
    count, width = own.shape
    made = w_query.shape[1] + flat_kv.shape[1]
    return pl.pallas_call(
        project_kernel,
        out_shape=(
            jax.ShapeDtypeStruct((2 * count, w_query.shape[1]), bf16),
            jax.ShapeDtypeStruct((2 * count, flat_kv.shape[1]), bf16),
            jax.ShapeDtypeStruct((count, flat_kv.shape[1]), bf16),
        ),
        in_specs=[ANY] * 2 + [VMEM] * 5,
        out_specs=(VMEM, VMEM, VMEM),
        scratch_shapes=[
            pltpu.VMEM((2, count, width), bf16),
            pltpu.VMEM((2 * count, width), bf16),
            pltpu.SemaphoreType.DMA((2,)),
        ],
        compiler_params=PARAMS,
        cost_estimate=takes(8),
        name="project",
    )(own, other, gain, cosine, sine, w_query, flat_kv)


def attend_rows_kernel(first, q, kv, seam, past, mixed, window, sem):
    count = q.shape[0] // 2
    if first == 0:
        copy = pltpu.make_async_copy(seam, window.at[pl.ds(0, count), :], sem)
        copy.start()
        window[count:, :] = kv[:count, :]
        copy.wait()
        keyed = window
    else:
        keyed = kv
    head = 64
    kv_heads = kv.shape[1] // (2 * head)
    per_kv = q.shape[1] // head // kv_heads
    shape = (count, 2 * count)
    row = lax.broadcasted_iota(jnp.int32, shape, 0) + count
    col = lax.broadcasted_iota(jnp.int32, shape, 1)
    reach = past[first : first + count, :1].astype(jnp.int32)
    visible = (col <= row) & (col >= row - reach)
    for kv_head in range(kv_heads):
        lanes = 2 * head * kv_head
        keys = keyed[:, lanes : lanes + head]
        values = keyed[:, lanes + head : lanes + 2 * head]
        for index in range(per_kv):
            at = (kv_head * per_kv + index) * head
            query = q[first : first + count, at : at + head]
            scores = lax.dot_general(query, keys, LAST_DIMS, preferred_element_type=f32)
            raised = jnp.where(visible, jnp.exp(scores * head ** (-0.5)), 0.0)
            probs = (raised / jnp.sum(raised, axis=-1, keepdims=True)).astype(bf16)
            made = jnp.dot(probs, values, preferred_element_type=f32)
            mixed[:, at : at + head] = made.astype(bf16)


def attend_late(q, kv, past):
    def kernel(q, kv, past, mixed):
        attend_rows_kernel(q.shape[0] // 2, q, kv, None, past, mixed, None, None)

    return pl.pallas_call(
        kernel,
        out_shape=jax.ShapeDtypeStruct((q.shape[0] // 2, q.shape[1]), bf16),
        in_specs=[VMEM] * 3,
        out_specs=VMEM,
        compiler_params=PARAMS,
        cost_estimate=takes(2),
        name="attend_late",
    )(q, kv, past)


def attend_early(q, kv, seam, past):
    return pl.pallas_call(
        functools.partial(attend_rows_kernel, 0),
        out_shape=jax.ShapeDtypeStruct((q.shape[0] // 2, q.shape[1]), bf16),
        in_specs=[VMEM, VMEM, ANY, VMEM],
        out_specs=VMEM,
        scratch_shapes=[pltpu.VMEM(kv.shape, bf16), pltpu.SemaphoreType.DMA],
        compiler_params=PARAMS,
        cost_estimate=takes(2),
        name="attend_early",
    )(q, kv, seam, past)


def outward_rows(flip, groups, unit_rows, early, late, parts, w_out, rows):
    place_parts(groups, parts, unit_rows, [(0, unit_rows, w_out, 0)])
    lane = lax.axis_index("hd")
    which = (1 - lane) if flip else lane

    @pl.when(which == 0)
    def _():
        rows[...] = early[...]

    @pl.when(which != 0)
    def _():
        rows[...] = late[...]

    return lax.dot_general(rows[...], w_out[...], LAST_DIMS, preferred_element_type=f32)


def send_kernel(groups, unit_rows, n_parts, early, late, *refs):
    parts, (out, w_out, rows) = refs[:n_parts], refs[n_parts:]
    out[...] = outward_rows(True, groups, unit_rows, early, late, parts, w_out, rows).astype(bf16)


def keep_kernel(groups, unit_rows, n_parts, early, late, tokens, *refs):
    parts, (out, w_out, rows) = refs[:n_parts], refs[n_parts:]
    made = outward_rows(False, groups, unit_rows, early, late, parts, w_out, rows)
    out[...] = tokens[...].astype(f32) + made


def outward_send(groups, early, late, parts, unit_rows):
    width, depth = groups * unit_rows, parts[0].shape[1]
    return pl.pallas_call(
        functools.partial(send_kernel, groups, unit_rows, len(parts)),
        out_shape=jax.ShapeDtypeStruct((early.shape[0], width), bf16),
        in_specs=[VMEM] * (2 + len(parts)),
        out_specs=VMEM,
        scratch_shapes=[pltpu.VMEM((width, depth), bf16), pltpu.VMEM(early.shape, bf16)],
        compiler_params=PARAMS,
        cost_estimate=reads(2 * width * depth),
        name="outward_send",
    )(early, late, *parts)


def outward_keep(groups, early, late, tokens, parts, unit_rows):
    width, depth = groups * unit_rows, parts[0].shape[1]
    return pl.pallas_call(
        functools.partial(keep_kernel, groups, unit_rows, len(parts)),
        out_shape=jax.ShapeDtypeStruct(tokens.shape, f32),
        in_specs=[VMEM] * (3 + len(parts)),
        out_specs=VMEM,
        scratch_shapes=[
            pltpu.VMEM((width, depth), bf16),
            pltpu.VMEM(early.shape, bf16),
        ],
        compiler_params=PARAMS,
        cost_estimate=reads(2 * width * depth),
        name="outward_keep",
    )(early, late, tokens, *parts)


def route_kernel(mine, arrived, flat_gain, place, residual, moe_in, sent, got, gain, sems, gain_sem):
    count = got.shape[0] // 4
    spans = [pl.ds(index * count, count) for index in range(4)]
    copies = fetch([(arrived.at[span, :], got.at[span, :]) for span in spans], sems)
    gain_copy = pltpu.make_async_copy(flat_gain, gain, gain_sem)
    gain_copy.start()
    gain_copy.wait()
    gains = gain[...].reshape(1, gain.shape[0])
    for span, copy in zip(spans, copies):
        copy.wait()
        added = (mine[span, :] + got[span, :].astype(f32)).astype(bf16)
        residual[span, :] = added
        moe_in[span, :] = normalized(added.astype(f32), gains)
    cap = sent.shape[0]
    rows = jnp.dot(place[cap:, :], moe_in[...], preferred_element_type=f32)
    sent[...] = rows.astype(bf16)


def route(mine, arrived, flat_gain, place):
    cap = place.shape[0] // 2
    return pl.pallas_call(
        route_kernel,
        out_shape=(
            jax.ShapeDtypeStruct(mine.shape, bf16),
            jax.ShapeDtypeStruct(mine.shape, bf16),
            jax.ShapeDtypeStruct((cap, mine.shape[1]), bf16),
        ),
        in_specs=[VMEM, ANY, ANY, VMEM],
        out_specs=(VMEM,) * 3,
        scratch_shapes=[
            pltpu.VMEM(mine.shape, bf16),
            pltpu.VMEM(flat_gain.shape, f32),
            pltpu.SemaphoreType.DMA((4,)),
            pltpu.SemaphoreType.DMA,
        ],
        compiler_params=PARAMS,
        cost_estimate=reads(16 << 20),
        name="route",
    )(mine, arrived, pltpu.with_memory_space_constraint(flat_gain, pltpu.HBM), place)


def expert_pieces(gate_up, down, up_rows, down_rows, width):
    pieces = [(i * up_rows, up_rows, gate_up, i * width) for i in range(2)]
    pieces += [
        (2 * up_rows + i * down_rows, down_rows, down, i * width) for i in range(down.shape[1] // width)
    ]
    return pieces, pieces[-1][0] + down_rows


def gate_kernel(groups, up_rows, down_rows, shards, moe_in, router_in, ids_in, place, *refs):
    parts, (gates, own, spread, gate_up, down, router, ids, sems, part_sems) = (
        refs[: len(shards)],
        refs[len(shards) :],
    )
    small = fetch([(router_in, router), (ids_in, ids)], sems)
    width = parts[0].shape[1]
    pieces, unit_rows = expert_pieces(gate_up, down, up_rows, down_rows, width)
    sources = ring_sources(groups, lax.axis_index("grp"))
    pairs = []
    for part, shard in zip(parts, shards):
        for unit in range(part.shape[0] // unit_rows):
            for first, rows, target, lane in pieces:
                at = pl.multiple_of(sources[shard + unit] * rows, rows)
                pairs.append(
                    (
                        part.at[pl.ds(unit * unit_rows + first, rows), :],
                        target.at[pl.ds(at, rows), pl.ds(lane, width)],
                    )
                )
    copies = fetch(pairs, part_sems)
    cap = own.shape[0]
    own[...] = jnp.dot(place[:cap, :], moe_in[...], preferred_element_type=f32).astype(bf16)
    tokens = ids.shape[1]
    row = lax.broadcasted_iota(jnp.int32, (tokens, tokens), 0)
    eye = (row == lax.broadcasted_iota(jnp.int32, (tokens, tokens), 1)).astype(f32)
    spread[...] = lax.dot_general(
        eye.astype(bf16), place[...], LAST_DIMS, preferred_element_type=f32
    ).astype(bf16)
    for copy in small:
        copy.wait()
    hit = named_experts(ids, router.shape[0])
    named = lax.dot_general(eye, hit, LAST_DIMS, preferred_element_type=f32)
    logits = lax.dot_general(moe_in[...], router[...], LAST_DIMS, preferred_element_type=f32)
    raised = jnp.where(named > 0, jnp.exp(logits), 0.0)
    gates[...] = raised / jnp.sum(raised, axis=-1, keepdims=True)
    for copy in copies:
        copy.wait()


def gate(groups, moe_in, router_t, ids_t, place, early, up_rows, down_rows):
    cap = place.shape[0] // 2
    tokens, model = moe_in.shape
    width = early[0][0].shape[1]
    units = 2 * len(early)
    far = [pltpu.with_memory_space_constraint(part, pltpu.HBM) for part in (router_t, ids_t)]
    return pl.pallas_call(
        functools.partial(gate_kernel, groups, up_rows, down_rows, [shard for _, shard in early]),
        out_shape=(
            jax.ShapeDtypeStruct((tokens, router_t.shape[0]), f32),
            jax.ShapeDtypeStruct((cap, model), bf16),
            jax.ShapeDtypeStruct(place.shape[::-1], bf16),
            jax.ShapeDtypeStruct((groups * up_rows, 2 * width), bf16),
            jax.ShapeDtypeStruct((groups * down_rows, model), bf16),
        ),
        in_specs=[VMEM, ANY, ANY, VMEM] + [ANY] * len(early),
        out_specs=(VMEM,) * 5,
        scratch_shapes=[
            pltpu.VMEM(router_t.shape, bf16),
            pltpu.VMEM(ids_t.shape, jnp.int32),
            pltpu.SemaphoreType.DMA((2,)),
            pltpu.SemaphoreType.DMA((units * (2 + model // width),)),
        ],
        compiler_params=PARAMS,
        cost_estimate=LITTLE,
        name="gate",
    )(moe_in, *far, place, *[part for part, _ in early])


def expert_kernel(groups, up_rows, down_rows, shards, own, other, gate_up_in, down_in, *refs):
    parts = refs[: len(shards)]
    own_out, other_out, gate_up, down, rows = refs[len(shards) :]
    width = parts[0].shape[1]
    count = own.shape[0]
    rows[:count, :] = own[...]
    rows[count:, :] = other[...]
    pieces, unit_rows = expert_pieces(gate_up, down, up_rows, down_rows, width)
    place_parts(groups, parts, unit_rows, pieces, shards)
    both = jnp.dot(rows[...], gate_up[...], preferred_element_type=f32)
    gate, up = both[:, :width], both[:, width:]
    hidden = (gate / (1.0 + jnp.exp(-gate)) * up).astype(bf16)
    made = jnp.dot(hidden, down[...], preferred_element_type=f32).astype(bf16)
    own_out[...] = made[:count, :]
    other_out[...] = made[count:, :]


def expert(groups, own, other, staged, late, up_rows, down_rows):
    count, model = own.shape
    width = late[0][0].shape[1]
    return pl.pallas_call(
        functools.partial(expert_kernel, groups, up_rows, down_rows, [shard for _, shard in late]),
        out_shape=(jax.ShapeDtypeStruct(own.shape, bf16),) * 2
        + tuple(jax.ShapeDtypeStruct(part.shape, bf16) for part in staged),
        in_specs=[VMEM] * (4 + len(late)),
        out_specs=(VMEM,) * 4,
        scratch_shapes=[pltpu.VMEM((2 * count, model), bf16)],
        input_output_aliases={2: 2, 3: 3},
        compiler_params=PARAMS,
        cost_estimate=pl.CostEstimate(flops=int(6.2 * 1.15e9), bytes_accessed=1, transcendentals=0),
        name="expert",
    )(own, other, *staged, *[part for part, _ in late])[:2]


def combine_kernel(residual, gates, spread, own, returned, out):
    lane = lax.axis_index("hd")
    count = own.shape[0]
    column = lax.broadcasted_iota(jnp.int32, gates.shape, 1)
    total = jnp.zeros(residual.shape, f32)
    for index, made in ((0, own), (1, returned)):
        live = lane if index == 0 else 1 - lane
        weight = jnp.sum(jnp.where(column == live, gates[...], 0.0), axis=-1, keepdims=True)
        picked = jnp.dot(
            spread[:, index * count : (index + 1) * count], made[...], preferred_element_type=f32
        )
        total += weight * picked
    out[...] = (residual[...].astype(f32) + total).astype(bf16)


def combine(residual, gates, spread, own, returned):
    return pl.pallas_call(
        combine_kernel,
        out_shape=jax.ShapeDtypeStruct(residual.shape, bf16),
        in_specs=[VMEM] * 5,
        out_specs=VMEM,
        compiler_params=PARAMS,
        cost_estimate=reads(6 * residual.shape[0] * residual.shape[1]),
        name="combine",
    )(residual, gates, spread, own, returned)


def bundle_kernel(send, kv, tags, result, out, sem):
    groups, rows, _ = out.shape
    heads = kv.shape[1] // 128
    capc = send.shape[0] // groups
    packed = jnp.dot(send[...], kv[...], preferred_element_type=f32).astype(bf16)
    tagged = jnp.dot(send[...], tags[...], preferred_element_type=f32)
    one = (lax.broadcasted_iota(jnp.int32, (16, 128), 0) == lax.broadcasted_iota(jnp.int32, (16, 128), 1))
    for owner in range(groups):
        mine = slice(owner * capc, (owner + 1) * capc)
        for head in range(heads):
            out[owner, head * capc : (head + 1) * capc, :] = packed[mine, head * 128 : (head + 1) * 128]
        wide = jnp.concatenate([tagged[mine, :], jnp.zeros((128 - capc, 128), f32)], axis=0)
        out[owner, heads * capc :, :] = lax.dot_general(
            one.astype(f32), wide, LAST_DIMS, preferred_element_type=f32
        ).astype(bf16)
    copy = pltpu.make_async_copy(out, result, sem)
    copy.start()
    copy.wait()


def bundle(groups, send, kv, tags):
    rows = send.shape[0] // groups * (kv.shape[1] // 128) + 16
    return pl.pallas_call(
        bundle_kernel,
        out_shape=pltpu.HBM((groups, rows, 128), bf16),
        in_specs=[VMEM] * 3,
        out_specs=HBM,
        scratch_shapes=[pltpu.VMEM((groups, rows, 128), bf16), pltpu.SemaphoreType.DMA],
        compiler_params=PARAMS,
        cost_estimate=LITTLE,
        name="bundle",
    )(send, kv, tags)


def write_kernel(heads, arrived, cache, out, rows, wide, known):
    groups, size, _ = arrived.shape
    slots = cache.shape[0] // heads
    capc = (size - 16) // heads
    high, low = [], []
    for source in range(groups):
        for head in range(heads):
            rows[source * capc : (source + 1) * capc, head * 128 : (head + 1) * 128] = arrived[
                source, head * capc : (head + 1) * capc, :
            ]
        numbers = arrived[source, heads * capc :, :].astype(f32)
        high.append(numbers[0:1, :capc])
        low.append(numbers[1:2, :capc])
    slot = jnp.concatenate(high, axis=1) * 64.0 + jnp.concatenate(low, axis=1) - 64.0
    row = lax.broadcasted_iota(jnp.int32, (slots, slot.shape[1]), 0).astype(f32)
    hit = (row == slot).astype(bf16)
    made = jnp.dot(hit, rows[...], preferred_element_type=f32)
    found = jnp.dot(hit, jnp.ones((slot.shape[1], 128), bf16), preferred_element_type=f32)
    for head in range(heads):
        wide[pl.ds(head, slots, heads), :] = made[:, head * 128 : (head + 1) * 128]
        known[pl.ds(head, slots, heads), :] = found
    old = cache[...].astype(f32)
    out[...] = jnp.where(known[...] > 0.0, wide[...], old).astype(bf16)


def write(arrived, cache):
    slots, heads, lanes = cache.shape
    capc = (arrived.shape[1] - 16) // heads
    flat = (slots * heads, lanes)
    written = pl.pallas_call(
        functools.partial(write_kernel, heads),
        out_shape=jax.ShapeDtypeStruct(flat, bf16),
        in_specs=[VMEM] * 2,
        out_specs=VMEM,
        scratch_shapes=[
            pltpu.VMEM((arrived.shape[0] * capc, heads * lanes), bf16),
            pltpu.VMEM(flat, f32),
            pltpu.VMEM(flat, f32),
        ],
        compiler_params=PARAMS,
        cost_estimate=reads(1 << 21),
        name="write",
    )(arrived, cache.reshape(flat))
    return written.reshape(cache.shape)


def two_lane_shards(
    tokens,
    positions,
    attn_gain,
    w_query,
    w_keyval,
    w_out,
    moe_gain,
    router,
    w_gate_up,
    w_down,
    expert_ids,
    cache_slot,
    kv_cache,
):
    groups = lax.axis_size("grp")
    tok_rows, model = tokens.shape
    block = positions.shape[0]
    kv_local, head2 = w_keyval.shape[1:]
    kv_width = kv_local * head2
    slots_dev = kv_cache.shape[0]
    swap = functools.partial(lax.ppermute, axis_name="hd", perm=[(0, 1), (1, 0)])

    together = lax.optimization_barrier

    other_tokens = swap(tokens)
    own = (w_gate_up[0], w_down[0], w_out.T)
    up_rows, down_rows = own[0].shape[0], own[1].shape[0]
    beside = [lax.ppermute(part, "grp", sibling_pairs(groups)) for part in own]
    expert_pair, out_pair = pack(own, beside)
    out_ring = Ring(out_pair, groups, lambda held, rows: held[:rows])
    out_ring.step()
    expert_ring = Ring(expert_pair, groups, cut)
    expert_ring.step()
    w_keyval, positions = together((w_keyval, positions, out_pair))[:2]
    flat_kv = w_keyval.reshape(model, kv_width)
    cosine, sine, past, place, send, tags, gain = prepare(
        groups, slots_dev, positions, cache_slot, expert_ids, attn_gain
    )
    cosine, flat_kv = out_ring.pin(cosine, flat_kv)
    out_ring.step()

    q, kv, tail = project(tokens, other_tokens, gain, cosine, sine, w_query, flat_kv)
    seam = lax.ppermute(tail, "grp", [(g, g + 1) for g in range(groups - 1)])
    late = attend_late(q, kv, past)
    late = out_ring.pin(late)
    out_ring.step()
    out_ring.share(2)
    seam, late = together((seam, late))
    seam = expert_ring.pin(seam)
    expert_ring.step()
    early = attend_early(q, kv, seam, past)
    early, out_ring.near = together((early, out_ring.near))
    early = out_ring.pin(early)
    out_ring.step()
    out_ring.share(3)
    early, kv, out_ring.near = together((early, kv, out_ring.near))
    outgoing = bundle(groups, send, kv, tags)
    early, outgoing = together((early, outgoing))
    early = out_ring.pin(early)
    early = expert_ring.pin(early)
    expert_ring.step()
    out_ring.share()
    sent = outward_send(groups, early, late, out_ring.parts(), out_ring.unit_rows)
    arrived = swap(sent)
    early = together((early, sent))[0]
    mine = outward_keep(groups, early, late, tokens, out_ring.parts(), out_ring.unit_rows)
    mine = expert_ring.pin(mine)
    expert_ring.share()
    expert_ring.step()
    outgoing = together((outgoing, sent))[0]
    arrived_cache = lax.all_to_all(outgoing, "grp", split_axis=0, concat_axis=0, tiled=True)
    arrived, mine = expert_ring.pin(arrived, mine)
    expert_ring.share()

    residual, moe_in, sent_rows = route(mine, arrived, moe_gain, place)
    landed = swap(sent_rows)
    parts_early, parts_late = expert_ring.split()
    gates, own_rows, spread, *staged = gate(
        groups, moe_in, router.T, expert_ids.T, place, parts_early, up_rows, down_rows
    )
    landed, own_rows = together((landed, own_rows))
    own_made, back = expert(groups, own_rows, landed, staged, parts_late, up_rows, down_rows)
    returned = swap(back)
    layer_out = combine(residual, gates, spread, own_made, returned)
    layer_out, arrived_cache = together((layer_out, arrived_cache))
    cache_after = write(arrived_cache, kv_cache)
    return (layer_out, cache_after)


def passed_along(value, axis, steps):
    count = lax.axis_size(axis)
    initial, last = (max(0, -steps), min(count, count - steps))
    return lax.ppermute(value, axis, [(source, source + steps) for source in range(initial, last)])


def rms_norm(row_set, norm_gain):
    floats = row_set.astype(jnp.float32)
    factor = lax.rsqrt(jnp.mean(floats * floats, axis=-1, keepdims=True) + norm_eps)
    return (floats * factor * norm_gain).astype(jnp.bfloat16)


def rotate(vectors, angle_pos):
    halves = vectors.shape[-1] // 2
    inverse_freq = rope_base ** (-2.0 * jnp.arange(halves, dtype=jnp.float32) / vectors.shape[-1])
    angles = angle_pos[:, None, None] * inverse_freq[None, None, :]
    cosine = jnp.cos(angles)
    sine_part = jnp.sin(angles)
    first_half = vectors[..., :halves]
    second_half = vectors[..., halves:]
    return jnp.concatenate(
        [
            first_half * cosine - second_half * sine_part,
            second_half * cosine + first_half * sine_part,
        ],
        axis=-1,
    )


def expert_rows(row_set, gate_up, down_rows):
    gate_and_up = jnp.dot(row_set, gate_up, preferred_element_type=jnp.float32)
    inner_width = gate_and_up.shape[1] // 2
    hidden = (jax.nn.silu(gate_and_up[:, :inner_width]) * gate_and_up[:, inner_width:]).astype(
        jnp.bfloat16
    )
    return jnp.dot(hidden, down_rows, preferred_element_type=jnp.float32).astype(jnp.bfloat16)


def attend_rows(query_blk, keys_blk, vals_blk, visible, scale_qk):
    scores = (
        jnp.einsum("qkgd,skd->kgqs", query_blk, keys_blk, preferred_element_type=jnp.float32)
        * scale_qk
    )
    weights_f = jnp.where(visible[None, None], jnp.exp(scores), 0.0)
    prob_bf = (weights_f / jnp.sum(weights_f, axis=-1, keepdims=True)).astype(jnp.bfloat16)
    return jnp.einsum("kgqs,skd->qkgd", prob_bf, vals_blk, preferred_element_type=jnp.float32)


def shards(
    tokens,
    positions,
    attn_gain,
    w_query,
    w_keyval,
    w_out,
    moe_gain,
    router,
    w_gate_up,
    w_down,
    expert_ids,
    cache_slot,
    kv_cache,
):
    lane_count = lax.axis_size("hd")
    group_count = lax.axis_size("grp")
    tok_rows = tokens.shape[0]
    model_width = tokens.shape[1]
    block_len = positions.shape[0]
    seg_most = block_len // 2
    head_dim = w_keyval.shape[2] // 2
    kv_local = w_keyval.shape[1]
    q_local = w_query.shape[1] // head_dim
    per_kv = q_local // kv_local
    expert_cap = tok_rows // 4
    normed = rms_norm(tokens, attn_gain)
    flat_kv = w_keyval.reshape(model_width, kv_local * 2 * head_dim)
    section = lax.all_gather(normed, "hd", axis=0, tiled=True)
    projected = jnp.concatenate(
        [
            jnp.dot(section, w_query, preferred_element_type=jnp.float32),
            jnp.dot(section, flat_kv, preferred_element_type=jnp.float32),
        ],
        axis=1,
    )
    angle_pos = jnp.maximum(positions, 0).astype(jnp.float32)
    queries = rotate(
        projected[:, : q_local * head_dim].reshape(block_len, q_local, head_dim), angle_pos
    ).astype(jnp.bfloat16)
    key_val = projected[:, q_local * head_dim :].reshape(block_len, kv_local, 2 * head_dim)
    rotated = rotate(key_val[:, :, :head_dim], angle_pos).astype(jnp.bfloat16)
    stored = jnp.concatenate([rotated, key_val[:, :, head_dim:].astype(jnp.bfloat16)], axis=2)
    seam_rows = passed_along(stored[block_len - seg_most :], "grp", 1)
    window = jnp.concatenate([seam_rows, stored], axis=0)
    scale_qk = head_dim ** (-0.5)
    local_rows = jnp.arange(block_len, dtype=jnp.int32)
    lowest = local_rows - jnp.maximum(positions, 0)
    pieces_out = []
    for q_block in range(2):
        first_row = q_block * seg_most
        rows_here = first_row + jnp.arange(seg_most, dtype=jnp.int32)
        cols_here = first_row - seg_most + jnp.arange(2 * seg_most, dtype=jnp.int32)
        low_here = lowest[first_row : first_row + seg_most]
        visible = (cols_here[None, :] >= low_here[:, None]) & (
            cols_here[None, :] <= rows_here[:, None]
        )
        query_blk = queries[first_row : first_row + seg_most].reshape(
            seg_most, kv_local, per_kv, head_dim
        )
        keys_blk = window[first_row : first_row + 2 * seg_most, :, :head_dim]
        vals_blk = window[first_row : first_row + 2 * seg_most, :, head_dim:]
        mixed_rows = attend_rows(query_blk, keys_blk, vals_blk, visible, scale_qk)
        pieces_out.append(mixed_rows.reshape(seg_most, q_local * head_dim).astype(jnp.bfloat16))
    attended = jnp.concatenate(pieces_out, axis=0)
    slots_dev = kv_cache.shape[0]
    capc = 2 * block_len // group_count
    live_slot = cache_slot >= 0
    owners = jnp.where(live_slot, cache_slot // slots_dev, group_count)
    owner_hit = (owners[:, None] == jnp.arange(group_count, dtype=jnp.int32)[None, :]).astype(
        jnp.bfloat16
    )
    lower_tri = (local_rows[:, None] >= local_rows[None, :]).astype(jnp.bfloat16)
    running = jnp.dot(lower_tri, owner_hit, preferred_element_type=jnp.float32)
    owner_rank = jnp.sum(running * owner_hit.astype(jnp.float32), axis=1).astype(jnp.int32) - 1
    send_rows = jnp.where(live_slot, owners * capc + owner_rank, group_count * capc)
    outgoing_cache = (
        jnp.zeros((group_count * capc, kv_local, 2 * head_dim), jnp.bfloat16)
        .at[send_rows]
        .set(stored, mode="drop")
    )
    outgoing_slots = (
        jnp.full((group_count * capc,), -1, jnp.int32)
        .at[send_rows]
        .set(cache_slot % slots_dev, mode="drop")
    )
    arrived, arrived_slots = (
        lax.all_to_all(
            outgoing_cache.reshape(group_count, capc, kv_local, 2 * head_dim),
            "grp",
            split_axis=0,
            concat_axis=0,
            tiled=True,
        ),
        lax.all_to_all(
            outgoing_slots.reshape(group_count, capc),
            "grp",
            split_axis=0,
            concat_axis=0,
            tiled=True,
        ),
    )
    flat_slots = arrived_slots.reshape(group_count * capc)
    write_rows = jnp.where(flat_slots >= 0, flat_slots, slots_dev).astype(jnp.int32)
    cache_after = kv_cache.at[write_rows].set(
        arrived.reshape(group_count * capc, kv_local, 2 * head_dim), mode="drop"
    )
    by_token = lax.all_to_all(attended, "hd", split_axis=0, concat_axis=1, tiled=True)
    attn_proj = jnp.dot(
        by_token,
        lax.all_gather(w_out, "grp", axis=1, tiled=True),
        preferred_element_type=jnp.float32,
    )
    residual = (tokens.astype(jnp.float32) + attn_proj).astype(jnp.bfloat16)
    moe_in = rms_norm(residual, moe_gain)
    logits = jnp.dot(moe_in, router, preferred_element_type=jnp.float32)
    expert_range = jnp.arange(router.shape[1], dtype=jnp.int32)
    matches_all = expert_ids[:, :, None] == expert_range[None, None, :]
    chosen = jnp.sum(jnp.where(matches_all, logits[:, None, :], 0.0), axis=2)
    raised = jnp.exp(chosen)
    gates = raised / jnp.sum(raised, axis=1, keepdims=True)
    live_range = jnp.arange(lane_count, dtype=jnp.int32)
    matches = expert_ids[:, :, None] == live_range[None, None, :]
    member = jnp.any(matches, axis=1)
    weighting = jnp.sum(jnp.where(matches, gates[:, :, None], 0.0), axis=1)
    ranking = jnp.cumsum(member.astype(jnp.int32), axis=0) - 1
    target = jnp.where(member, live_range[None, :] * expert_cap + ranking, -1)
    slot_range = jnp.arange(lane_count * expert_cap, dtype=jnp.int32)
    slot_hits = target[None, :, :] == slot_range[:, None, None]
    placing = jnp.any(slot_hits, axis=2).astype(jnp.bfloat16)
    outgoing = (
        jnp.dot(placing, moe_in, preferred_element_type=jnp.float32)
        .astype(jnp.bfloat16)
        .reshape(lane_count, expert_cap, model_width)
    )
    gate_up_all, down_all = (
        lax.all_gather(w_gate_up, "grp", axis=1, tiled=True),
        lax.all_gather(w_down, "grp", axis=1, tiled=True),
    )
    gate_up_mat = gate_up_all[0]
    down_mat = down_all[0]
    landed = lax.all_to_all(outgoing, "hd", split_axis=0, concat_axis=0, tiled=True)
    results = expert_rows(landed.reshape(-1, model_width), gate_up_mat, down_mat).reshape(landed.shape)
    returned = lax.all_to_all(results, "hd", split_axis=0, concat_axis=0, tiled=True)
    flat_returned = returned.reshape(-1, model_width)
    fetched = flat_returned[jnp.maximum(target, 0)]
    used_weight = jnp.where(member, weighting, 0.0)
    moe_total = jnp.sum(used_weight[:, :, None] * fetched.astype(jnp.float32), axis=1)
    layer_out = (residual.astype(jnp.float32) + moe_total).astype(jnp.bfloat16)
    return (layer_out, cache_after)


def solution(mesh):
    two_lanes = mesh.shape["hd"] == 2 and mesh.shape["grp"] % 8 == 0
    return jax.shard_map(
        two_lane_shards if two_lanes else shards,
        mesh=mesh,
        in_specs=(
            P(("grp", "hd"), None),
            P("grp"),
            P(),
            P(None, "hd"),
            P(None, "hd", None),
            P(None, "grp"),
            P(),
            P(),
            P("hd", "grp", None),
            P("hd", "grp", None),
            P(("grp", "hd"), None),
            P("grp"),
            P("grp", "hd", None),
        ),
        out_specs=(P(("grp", "hd"), None), P("grp", "hd", None)),
        check_vma=False,
    )
```

```python
import functools

import jax
import jax.numpy as jnp
import numpy as np
from jax import lax
from jax.experimental import pallas as pl
from jax.experimental.pallas import tpu as pltpu
from jax.sharding import PartitionSpec as P

norm_eps = 1e-05
rope_base = 10000.0
bf16 = jnp.bfloat16
f32 = jnp.float32
LAST_DIMS = (((1,), (1,)), ((), ()))


def ring_cycle(groups):
    rows = groups // 4
    return [2 * r for r in range(rows)] + [2 * r + 1 for r in reversed(range(rows))]


def ring_pairs(groups):
    cycle = ring_cycle(groups)
    count = len(cycle)
    pairs = []
    for place, pair in enumerate(cycle):
        pairs.append((2 * pair, 2 * cycle[(place + 1) % count]))
        pairs.append((2 * pair + 1, 2 * cycle[(place - 1) % count] + 1))
    return pairs


def sibling_pairs(groups):
    return [(g, g ^ 1) for g in range(groups)]


def ring_sources(groups, me):
    count = groups // 2
    rows = count // 2
    side, pair = me % 2, me // 2
    row, col = pair // 2, pair % 2
    place = jnp.where(col == 0, row, count - 1 - row)

    def block(core, steps):
        there = (place + (2 * core - 1) * steps + count) % count
        other = jnp.where(there < rows, 2 * there, 2 * (count - 1 - there) + 1)
        return [2 * other + core, 2 * other + 1 - core]

    full = (count - 1) // 2
    listed = [me, me + 1 - 2 * side]
    for core in (side, 1 - side):
        for steps in range(1, full + 1):
            listed += block(core, steps)
    return listed + [block(side, count // 2)[0], block(1 - side, count // 2)[0]]


class Ring:
    def __init__(self, pair, groups):
        self.across = functools.partial(lax.ppermute, axis_name="grp", perm=ring_pairs(groups))
        self.beside = functools.partial(lax.ppermute, axis_name="grp", perm=sibling_pairs(groups))
        self.full = (groups // 2 - 1) // 2
        self.unit_rows = pair.shape[0] // 2
        self.mine = [pair]
        self.near = []

    def step(self):
        held = self.mine[-1]
        if len(self.mine) > self.full:
            held = held[: self.unit_rows]
        self.mine.append(self.across(held))

    def pin(self, *others):
        done = lax.optimization_barrier((self.mine[-1],) + others)
        self.mine[-1] = done[0]
        return done[1:] if len(others) > 1 else done[1]

    def share(self, upto=None):
        for index in range(1 + len(self.near), 1 + (upto or len(self.mine) - 1)):
            self.near.append(self.beside(self.mine[index]))

    def parts(self):
        full = self.full
        return self.mine[: full + 1] + self.near[:full] + [self.mine[full + 1], self.near[full]]

    def split(self):
        full = self.full
        listed = [(part, 2 * index) for index, part in enumerate(self.parts()[:-1])]
        listed.append((self.near[full], 4 * full + 3))
        late = (full, 2 * full, 2 * full + 1, 2 * full + 2)
        return (
            [pair for index, pair in enumerate(listed) if index not in late],
            [listed[index] for index in late],
        )


def place_parts(groups, parts, unit_rows, pieces, shards=None):
    sources = ring_sources(groups, lax.axis_index("grp"))
    shard = 0
    for index, part in enumerate(parts):
        shard = shards[index] if shards else shard
        for unit in range(part.shape[0] // unit_rows):
            for first, rows, target, lane in pieces:
                at = pl.multiple_of(sources[shard] * rows, rows)
                start = unit * unit_rows + first
                target[pl.ds(at, rows), lane : lane + part.shape[1]] = part[start : start + rows, :]
            shard += 1


VMEM = pl.BlockSpec(memory_space=pltpu.VMEM)
ANY = pl.BlockSpec(memory_space=pl.ANY)
HBM = pl.BlockSpec(memory_space=pltpu.HBM)
PARAMS = pltpu.CompilerParams(vmem_limit_bytes=16 << 20)


LITTLE = pl.CostEstimate(flops=1, bytes_accessed=1, transcendentals=0)


def takes(us):
    return pl.CostEstimate(
        flops=int(us * 1.15e9), bytes_accessed=int(us * 8e6), transcendentals=0
    )


def reads(nbytes):
    return pl.CostEstimate(flops=1, bytes_accessed=nbytes, transcendentals=0)


def normalized(floats, gain):
    factor = lax.rsqrt(jnp.mean(floats * floats, axis=-1, keepdims=True) + norm_eps)
    return (floats * factor * gain).astype(bf16)


def fetch(pairs, sems):
    copies = []
    for index, (source, target) in enumerate(pairs):
        copies.append(pltpu.make_async_copy(source, target, sems.at[index]))
        copies[-1].start()
    return copies


def pack_kernel(*refs):
    sources, (expert_pair, out_pair, sems) = refs[:6], refs[6:]
    width = expert_pair.shape[1]
    lane = lax.axis_index("hd")
    first = pl.multiple_of(lane * out_pair.shape[1], out_pair.shape[1])
    pairs = []
    row = 0
    for index in range(2):
        up, down, w_out = sources[3 * index : 3 * index + 3]
        count = w_out.shape[0]
        pairs.append(
            (w_out.at[:, pl.ds(first, out_pair.shape[1])], out_pair.at[pl.ds(index * count, count), :])
        )
        for source in (up, down):
            for at in range(0, source.shape[1], width):
                pairs.append(
                    (source.at[:, pl.ds(at, width)], expert_pair.at[pl.ds(row, source.shape[0]), :])
                )
                row += source.shape[0]
    for copy in fetch(pairs, sems):
        copy.wait()


def pack(own, beside):
    own = [pltpu.with_memory_space_constraint(part, pltpu.HBM) for part in own]
    up, down, w_out_t = own
    width = up.shape[1] // 2
    pieces = [up.shape[1] // width, down.shape[1] // width]
    unit_rows = pieces[0] * up.shape[0] + pieces[1] * down.shape[0]
    return pl.pallas_call(
        pack_kernel,
        out_shape=(
            jax.ShapeDtypeStruct((2 * unit_rows, width), bf16),
            jax.ShapeDtypeStruct((2 * w_out_t.shape[0], w_out_t.shape[1] // 2), bf16),
        ),
        in_specs=[ANY] * 6,
        out_specs=(ANY, ANY),
        scratch_shapes=[pltpu.SemaphoreType.DMA((2 + 2 * sum(pieces),))],
        compiler_params=PARAMS,
        cost_estimate=LITTLE,
        name="pack",
    )(*own, *beside)


def as_column(row, eye):
    return jnp.sum(jnp.where(eye, row, 0.0), axis=1, keepdims=True)


def named_experts(ids, experts):
    tokens = ids.shape[1]
    expert = lax.broadcasted_iota(jnp.int32, (experts, tokens), 0)
    hit = jnp.zeros((experts, tokens), f32)
    for index in range(ids.shape[0]):
        hit = jnp.where(ids[index : index + 1, :] == expert, 1.0, hit)
    return hit


def prepare_kernel(groups, slots_dev, *refs):
    sources, (cosine, sine, past, place, send, tags, gain) = refs[:4], refs[4:11]
    positions, slots, ids, flat_gain, sems = refs[11:]
    copies = fetch(list(zip(sources, (positions, slots, ids, flat_gain))), sems)
    for copy in copies:
        copy.wait()
    gain[...] = flat_gain[...].reshape(gain.shape)
    lane = lax.axis_index("hd")
    block = positions.shape[1]

    def iota(shape, dim):
        return lax.broadcasted_iota(jnp.int32, shape, dim)

    eye = iota((block, block), 0) == iota((block, block), 1)
    reach = as_column(jnp.maximum(positions[...], 0).astype(f32), eye)
    past[...] = jnp.broadcast_to(reach, past.shape)
    column = iota((8, 128), 1)
    exponent = (column % 32).astype(f32) * (-2.0 / 64)
    inverse_freq = jnp.exp(exponent * np.float32(np.log(rope_base)))[:1, :]
    angles = reach * inverse_freq
    cosine[...] = jnp.cos(angles)
    turned = jnp.sin(angles)
    sine[...] = jnp.where(iota(angles.shape, 1) % 64 < 32, -turned, turned)

    tokens = ids.shape[1]
    cap = place.shape[0] // 2
    hit = named_experts(ids, 8)
    upto = (iota((tokens, tokens), 0) <= iota((tokens, tokens), 1)).astype(f32)
    rank = jnp.dot(hit, upto, preferred_element_type=f32) - 1.0
    slot = iota((2 * cap, tokens), 0).astype(f32)
    placed = jnp.zeros((2 * cap, tokens), f32)
    for live in range(2):
        order = jnp.where(lane == live, 0, cap).astype(f32)
        member = hit[live : live + 1, :] > 0.0
        placed = jnp.where(member & (slot == rank[live : live + 1, :] + order), 1.0, placed)
    place[...] = placed.astype(bf16)

    where = slots[...]
    owner = jnp.where(where >= 0, where // slots_dev, -1)
    owner_hit = (iota((groups, block), 0) == owner).astype(f32)
    before = (iota((block, block), 0) <= iota((block, block), 1)).astype(f32)
    running = jnp.dot(owner_hit, before, preferred_element_type=f32)
    owner_rank = jnp.sum(owner_hit * running, axis=0, keepdims=True) - 1.0
    capc = send.shape[0] // groups
    row = jnp.where(owner >= 0, owner * capc + owner_rank.astype(jnp.int32), -1)
    send[...] = (iota(send.shape, 0) == row).astype(bf16)
    inside = jnp.where(where >= 0, where % slots_dev, 0)
    high = as_column((inside // 64 + 1).astype(f32), eye)
    low = as_column((inside % 64).astype(f32), eye)
    spot = iota(tags.shape, 1)
    tags[...] = jnp.where(spot == 0, high, jnp.where(spot == 1, low, 0.0)).astype(bf16)


def prepare(groups, slots_dev, positions, slots, ids, gain):
    block, tokens = positions.shape[0], ids.shape[0]
    model = gain.shape[0]
    cap = tokens // 4
    capc = 2 * block // groups
    shapes = [
        ((block, 128), f32),
        ((block, 128), f32),
        ((block, 128), f32),
        ((2 * cap, tokens), bf16),
        ((groups * capc, block), bf16),
        ((block, 128), bf16),
        ((1, model), f32),
    ]
    sources = (positions[None], slots[None], ids.T, gain)
    return pl.pallas_call(
        functools.partial(prepare_kernel, groups, slots_dev),
        out_shape=tuple(jax.ShapeDtypeStruct(shape, kind) for shape, kind in shapes),
        in_specs=[ANY] * 4,
        out_specs=(VMEM,) * len(shapes),
        scratch_shapes=[
            pltpu.VMEM((1, block), jnp.int32),
            pltpu.VMEM((1, block), jnp.int32),
            pltpu.VMEM(ids.shape[::-1], jnp.int32),
            pltpu.VMEM((model,), f32),
            pltpu.SemaphoreType.DMA((4,)),
        ],
        compiler_params=PARAMS,
        cost_estimate=LITTLE,
        name="prepare",
    )(*[pltpu.with_memory_space_constraint(source, pltpu.HBM) for source in sources])


def project_kernel(
    own, other, gain, cosine, sine, w_query, w_keyval, q_out, kv_out, seam_out, raw, rows, sems
):
    count = own.shape[0]
    lane = lax.axis_index("hd")
    mine = pl.multiple_of(lane * count, count)
    theirs = pl.multiple_of((1 - lane) * count, count)
    copies = fetch([(own, raw.at[0]), (other, raw.at[1])], sems)
    cos_q, sin_q = cosine[...], sine[...]
    column = lax.broadcasted_iota(jnp.int32, cos_q.shape, 1)
    lower = column % 64 < 32
    cos_kv = jnp.where(column < 64, cos_q, 1.0)
    sin_kv = jnp.where(column < 64, sin_q, 0.0)
    for index, first in ((0, mine), (1, theirs)):
        copies[index].wait()
        rows[pl.ds(first, count), :] = normalized(raw[index].astype(f32), gain[...])
    width = 256
    for weights, out, cos, sin in ((w_keyval, kv_out, cos_kv, sin_kv), (w_query, q_out, cos_q, sin_q)):
        for first in range(0, weights.shape[1], width):
            made = jnp.dot(rows[...], weights[:, first : first + width], preferred_element_type=f32)
            for part in range(0, width, 128):
                here = made[:, part : part + 128]
                turned = jnp.where(lower, pltpu.roll(here, 96, 1), pltpu.roll(here, 32, 1))
                done = (here * cos + turned * sin).astype(bf16)
                out[:, first + part : first + part + 128] = done
                if out is kv_out:
                    seam_out[:, first + part : first + part + 128] = done[count:, :]


def project(own, other, gain, cosine, sine, w_query, flat_kv):
    count, width = own.shape
    made = w_query.shape[1] + flat_kv.shape[1]
    return pl.pallas_call(
        project_kernel,
        out_shape=(
            jax.ShapeDtypeStruct((2 * count, w_query.shape[1]), bf16),
            jax.ShapeDtypeStruct((2 * count, flat_kv.shape[1]), bf16),
            jax.ShapeDtypeStruct((count, flat_kv.shape[1]), bf16),
        ),
        in_specs=[ANY] * 2 + [VMEM] * 5,
        out_specs=(VMEM, VMEM, VMEM),
        scratch_shapes=[
            pltpu.VMEM((2, count, width), bf16),
            pltpu.VMEM((2 * count, width), bf16),
            pltpu.SemaphoreType.DMA((2,)),
        ],
        compiler_params=PARAMS,
        cost_estimate=takes(8),
        name="project",
    )(own, other, gain, cosine, sine, w_query, flat_kv)


def attend_rows_kernel(first, q, kv, seam, past, mixed, window, sem):
    count = q.shape[0] // 2
    if first == 0:
        copy = pltpu.make_async_copy(seam, window.at[pl.ds(0, count), :], sem)
        copy.start()
        window[count:, :] = kv[:count, :]
        copy.wait()
        keyed = window
    else:
        keyed = kv
    head = 64
    kv_heads = kv.shape[1] // (2 * head)
    per_kv = q.shape[1] // head // kv_heads
    shape = (count, 2 * count)
    row = lax.broadcasted_iota(jnp.int32, shape, 0) + count
    col = lax.broadcasted_iota(jnp.int32, shape, 1)
    reach = past[first : first + count, :1].astype(jnp.int32)
    visible = (col <= row) & (col >= row - reach)
    for kv_head in range(kv_heads):
        lanes = 2 * head * kv_head
        keys = keyed[:, lanes : lanes + head]
        values = keyed[:, lanes + head : lanes + 2 * head]
        for index in range(per_kv):
            at = (kv_head * per_kv + index) * head
            query = q[first : first + count, at : at + head]
            scores = lax.dot_general(query, keys, LAST_DIMS, preferred_element_type=f32)
            raised = jnp.where(visible, jnp.exp(scores * head ** (-0.5)), 0.0)
            probs = (raised / jnp.sum(raised, axis=-1, keepdims=True)).astype(bf16)
            made = jnp.dot(probs, values, preferred_element_type=f32)
            mixed[:, at : at + head] = made.astype(bf16)


def attend_late(q, kv, past):
    def kernel(q, kv, past, mixed):
        attend_rows_kernel(q.shape[0] // 2, q, kv, None, past, mixed, None, None)

    return pl.pallas_call(
        kernel,
        out_shape=jax.ShapeDtypeStruct((q.shape[0] // 2, q.shape[1]), bf16),
        in_specs=[VMEM] * 3,
        out_specs=VMEM,
        compiler_params=PARAMS,
        cost_estimate=takes(2),
        name="attend_late",
    )(q, kv, past)


def attend_early(q, kv, seam, past):
    return pl.pallas_call(
        functools.partial(attend_rows_kernel, 0),
        out_shape=jax.ShapeDtypeStruct((q.shape[0] // 2, q.shape[1]), bf16),
        in_specs=[VMEM, VMEM, ANY, VMEM],
        out_specs=VMEM,
        scratch_shapes=[pltpu.VMEM(kv.shape, bf16), pltpu.SemaphoreType.DMA],
        compiler_params=PARAMS,
        cost_estimate=takes(2),
        name="attend_early",
    )(q, kv, seam, past)


def outward_rows(flip, groups, unit_rows, early, late, parts, w_out, rows):
    place_parts(groups, parts, unit_rows, [(0, unit_rows, w_out, 0)])
    lane = lax.axis_index("hd")
    which = (1 - lane) if flip else lane

    @pl.when(which == 0)
    def _():
        rows[...] = early[...]

    @pl.when(which != 0)
    def _():
        rows[...] = late[...]

    return lax.dot_general(rows[...], w_out[...], LAST_DIMS, preferred_element_type=f32)


def send_kernel(groups, unit_rows, n_parts, early, late, *refs):
    parts, (out, w_out, rows) = refs[:n_parts], refs[n_parts:]
    out[...] = outward_rows(True, groups, unit_rows, early, late, parts, w_out, rows).astype(bf16)


def keep_kernel(groups, unit_rows, n_parts, early, late, tokens, *refs):
    parts, (out, w_out, rows) = refs[:n_parts], refs[n_parts:]
    made = outward_rows(False, groups, unit_rows, early, late, parts, w_out, rows)
    out[...] = tokens[...].astype(f32) + made


def outward_send(groups, early, late, parts, unit_rows):
    width, depth = groups * unit_rows, parts[0].shape[1]
    return pl.pallas_call(
        functools.partial(send_kernel, groups, unit_rows, len(parts)),
        out_shape=jax.ShapeDtypeStruct((early.shape[0], width), bf16),
        in_specs=[VMEM] * (2 + len(parts)),
        out_specs=VMEM,
        scratch_shapes=[pltpu.VMEM((width, depth), bf16), pltpu.VMEM(early.shape, bf16)],
        compiler_params=PARAMS,
        cost_estimate=reads(2 * width * depth),
        name="outward_send",
    )(early, late, *parts)


def outward_keep(groups, early, late, tokens, parts, unit_rows):
    width, depth = groups * unit_rows, parts[0].shape[1]
    return pl.pallas_call(
        functools.partial(keep_kernel, groups, unit_rows, len(parts)),
        out_shape=jax.ShapeDtypeStruct(tokens.shape, f32),
        in_specs=[VMEM] * (3 + len(parts)),
        out_specs=VMEM,
        scratch_shapes=[
            pltpu.VMEM((width, depth), bf16),
            pltpu.VMEM(early.shape, bf16),
        ],
        compiler_params=PARAMS,
        cost_estimate=reads(2 * width * depth),
        name="outward_keep",
    )(early, late, tokens, *parts)


def route_kernel(mine, arrived, flat_gain, place, residual, moe_in, sent, gain, gain_sem):
    copy = pltpu.make_async_copy(flat_gain, gain, gain_sem)
    copy.start()
    added = (mine[...] + arrived[...].astype(f32)).astype(bf16)
    residual[...] = added
    copy.wait()
    moe_in[...] = normalized(added.astype(f32), gain[...].reshape(1, gain.shape[0]))
    cap = sent.shape[0]
    rows = jnp.dot(place[cap:, :], moe_in[...], preferred_element_type=f32)
    sent[...] = rows.astype(bf16)


def route(mine, arrived, flat_gain, place):
    cap = place.shape[0] // 2
    return pl.pallas_call(
        route_kernel,
        out_shape=(
            jax.ShapeDtypeStruct(mine.shape, bf16),
            jax.ShapeDtypeStruct(mine.shape, bf16),
            jax.ShapeDtypeStruct((cap, mine.shape[1]), bf16),
        ),
        in_specs=[VMEM, VMEM, ANY, VMEM],
        out_specs=(VMEM,) * 3,
        scratch_shapes=[pltpu.VMEM(flat_gain.shape, f32), pltpu.SemaphoreType.DMA],
        compiler_params=PARAMS,
        cost_estimate=reads(16 << 20),
        name="route",
    )(mine, arrived, pltpu.with_memory_space_constraint(flat_gain, pltpu.HBM), place)


def expert_pieces(gate_up, down, up_rows, down_rows, width):
    pieces = [(i * up_rows, up_rows, gate_up, i * width) for i in range(2)]
    pieces += [
        (2 * up_rows + i * down_rows, down_rows, down, i * width) for i in range(down.shape[1] // width)
    ]
    return pieces, pieces[-1][0] + down_rows


def gate_kernel(groups, up_rows, down_rows, shards, moe_in, router_in, ids_in, place, *refs):
    parts, (gates, own, spread, gate_up, down, router, ids, sems, part_sems) = (
        refs[: len(shards)],
        refs[len(shards) :],
    )
    small = fetch([(router_in, router), (ids_in, ids)], sems)
    width = parts[0].shape[1]
    pieces, unit_rows = expert_pieces(gate_up, down, up_rows, down_rows, width)
    sources = ring_sources(groups, lax.axis_index("grp"))
    pairs = []
    for part, shard in zip(parts, shards):
        for unit in range(part.shape[0] // unit_rows):
            for first, rows, target, lane in pieces:
                at = pl.multiple_of(sources[shard + unit] * rows, rows)
                pairs.append(
                    (
                        part.at[pl.ds(unit * unit_rows + first, rows), :],
                        target.at[pl.ds(at, rows), pl.ds(lane, width)],
                    )
                )
    copies = fetch(pairs, part_sems)
    cap = own.shape[0]
    own[...] = jnp.dot(place[:cap, :], moe_in[...], preferred_element_type=f32).astype(bf16)
    tokens = ids.shape[1]
    row = lax.broadcasted_iota(jnp.int32, (tokens, tokens), 0)
    eye = (row == lax.broadcasted_iota(jnp.int32, (tokens, tokens), 1)).astype(f32)
    spread[...] = lax.dot_general(
        eye.astype(bf16), place[...], LAST_DIMS, preferred_element_type=f32
    ).astype(bf16)
    for copy in small:
        copy.wait()
    hit = named_experts(ids, router.shape[0])
    named = lax.dot_general(eye, hit, LAST_DIMS, preferred_element_type=f32)
    logits = lax.dot_general(moe_in[...], router[...], LAST_DIMS, preferred_element_type=f32)
    raised = jnp.where(named > 0, jnp.exp(logits), 0.0)
    gates[...] = raised / jnp.sum(raised, axis=-1, keepdims=True)
    for copy in copies:
        copy.wait()


def gate(groups, moe_in, router_t, ids_t, place, early, up_rows, down_rows):
    cap = place.shape[0] // 2
    tokens, model = moe_in.shape
    width = early[0][0].shape[1]
    units = 2 * len(early)
    far = [pltpu.with_memory_space_constraint(part, pltpu.HBM) for part in (router_t, ids_t)]
    return pl.pallas_call(
        functools.partial(gate_kernel, groups, up_rows, down_rows, [shard for _, shard in early]),
        out_shape=(
            jax.ShapeDtypeStruct((tokens, router_t.shape[0]), f32),
            jax.ShapeDtypeStruct((cap, model), bf16),
            jax.ShapeDtypeStruct(place.shape[::-1], bf16),
            jax.ShapeDtypeStruct((groups * up_rows, 2 * width), bf16),
            jax.ShapeDtypeStruct((groups * down_rows, model), bf16),
        ),
        in_specs=[VMEM, ANY, ANY, VMEM] + [ANY] * len(early),
        out_specs=(VMEM,) * 5,
        scratch_shapes=[
            pltpu.VMEM(router_t.shape, bf16),
            pltpu.VMEM(ids_t.shape, jnp.int32),
            pltpu.SemaphoreType.DMA((2,)),
            pltpu.SemaphoreType.DMA((units * (2 + model // width),)),
        ],
        compiler_params=PARAMS,
        cost_estimate=LITTLE,
        name="gate",
    )(moe_in, *far, place, *[part for part, _ in early])


def expert_kernel(groups, up_rows, down_rows, shards, own, other, gate_up_in, down_in, *refs):
    parts = refs[: len(shards)]
    own_out, other_out, gate_up, down, rows = refs[len(shards) :]
    width = parts[0].shape[1]
    count = own.shape[0]
    rows[:count, :] = own[...]
    rows[count:, :] = other[...]
    pieces, unit_rows = expert_pieces(gate_up, down, up_rows, down_rows, width)
    place_parts(groups, parts, unit_rows, pieces, shards)
    both = jnp.dot(rows[...], gate_up[...], preferred_element_type=f32)
    gate, up = both[:, :width], both[:, width:]
    hidden = (gate / (1.0 + jnp.exp(-gate)) * up).astype(bf16)
    made = jnp.dot(hidden, down[...], preferred_element_type=f32).astype(bf16)
    own_out[...] = made[:count, :]
    other_out[...] = made[count:, :]


def expert(groups, own, other, staged, late, up_rows, down_rows):
    count, model = own.shape
    width = late[0][0].shape[1]
    return pl.pallas_call(
        functools.partial(expert_kernel, groups, up_rows, down_rows, [shard for _, shard in late]),
        out_shape=(jax.ShapeDtypeStruct(own.shape, bf16),) * 2
        + tuple(jax.ShapeDtypeStruct(part.shape, bf16) for part in staged),
        in_specs=[VMEM] * (4 + len(late)),
        out_specs=(VMEM,) * 4,
        scratch_shapes=[pltpu.VMEM((2 * count, model), bf16)],
        input_output_aliases={2: 2, 3: 3},
        compiler_params=PARAMS,
        cost_estimate=pl.CostEstimate(flops=int(5.7 * 1.15e9), bytes_accessed=1, transcendentals=0),
        name="expert",
    )(own, other, *staged, *[part for part, _ in late])[:2]


def combine_kernel(residual, gates, spread, own, returned, out):
    lane = lax.axis_index("hd")
    count = own.shape[0]
    column = lax.broadcasted_iota(jnp.int32, gates.shape, 1)
    total = jnp.zeros(residual.shape, f32)
    for index, made in ((0, own), (1, returned)):
        live = lane if index == 0 else 1 - lane
        weight = jnp.sum(jnp.where(column == live, gates[...], 0.0), axis=-1, keepdims=True)
        picked = jnp.dot(
            spread[:, index * count : (index + 1) * count], made[...], preferred_element_type=f32
        )
        total += weight * picked
    out[...] = (residual[...].astype(f32) + total).astype(bf16)


def combine(residual, gates, spread, own, returned):
    return pl.pallas_call(
        combine_kernel,
        out_shape=jax.ShapeDtypeStruct(residual.shape, bf16),
        in_specs=[VMEM] * 5,
        out_specs=VMEM,
        compiler_params=PARAMS,
        cost_estimate=reads(6 * residual.shape[0] * residual.shape[1]),
        name="combine",
    )(residual, gates, spread, own, returned)


def bundle_kernel(send, kv, tags, result, out, sem):
    groups, rows, _ = out.shape
    heads = kv.shape[1] // 128
    capc = send.shape[0] // groups
    packed = jnp.dot(send[...], kv[...], preferred_element_type=f32).astype(bf16)
    tagged = jnp.dot(send[...], tags[...], preferred_element_type=f32)
    one = (lax.broadcasted_iota(jnp.int32, (16, 128), 0) == lax.broadcasted_iota(jnp.int32, (16, 128), 1))
    for owner in range(groups):
        mine = slice(owner * capc, (owner + 1) * capc)
        for head in range(heads):
            out[owner, head * capc : (head + 1) * capc, :] = packed[mine, head * 128 : (head + 1) * 128]
        wide = jnp.concatenate([tagged[mine, :], jnp.zeros((128 - capc, 128), f32)], axis=0)
        out[owner, heads * capc :, :] = lax.dot_general(
            one.astype(f32), wide, LAST_DIMS, preferred_element_type=f32
        ).astype(bf16)
    copy = pltpu.make_async_copy(out, result, sem)
    copy.start()
    copy.wait()


def bundle(groups, send, kv, tags):
    rows = send.shape[0] // groups * (kv.shape[1] // 128) + 16
    return pl.pallas_call(
        bundle_kernel,
        out_shape=pltpu.HBM((groups, rows, 128), bf16),
        in_specs=[VMEM] * 3,
        out_specs=HBM,
        scratch_shapes=[pltpu.VMEM((groups, rows, 128), bf16), pltpu.SemaphoreType.DMA],
        compiler_params=PARAMS,
        cost_estimate=LITTLE,
        name="bundle",
    )(send, kv, tags)


def write_kernel(heads, arrived, cache, out, rows, wide, known):
    groups, size, _ = arrived.shape
    slots = cache.shape[0] // heads
    capc = (size - 16) // heads
    high, low = [], []
    for source in range(groups):
        for head in range(heads):
            rows[source * capc : (source + 1) * capc, head * 128 : (head + 1) * 128] = arrived[
                source, head * capc : (head + 1) * capc, :
            ]
        numbers = arrived[source, heads * capc :, :].astype(f32)
        high.append(numbers[0:1, :capc])
        low.append(numbers[1:2, :capc])
    slot = jnp.concatenate(high, axis=1) * 64.0 + jnp.concatenate(low, axis=1) - 64.0
    row = lax.broadcasted_iota(jnp.int32, (slots, slot.shape[1]), 0).astype(f32)
    hit = (row == slot).astype(bf16)
    made = jnp.dot(hit, rows[...], preferred_element_type=f32)
    found = jnp.dot(hit, jnp.ones((slot.shape[1], 128), bf16), preferred_element_type=f32)
    for head in range(heads):
        wide[pl.ds(head, slots, heads), :] = made[:, head * 128 : (head + 1) * 128]
        known[pl.ds(head, slots, heads), :] = found
    old = cache[...].astype(f32)
    out[...] = jnp.where(known[...] > 0.0, wide[...], old).astype(bf16)


def write(arrived, cache):
    slots, heads, lanes = cache.shape
    capc = (arrived.shape[1] - 16) // heads
    flat = (slots * heads, lanes)
    written = pl.pallas_call(
        functools.partial(write_kernel, heads),
        out_shape=jax.ShapeDtypeStruct(flat, bf16),
        in_specs=[VMEM] * 2,
        out_specs=VMEM,
        scratch_shapes=[
            pltpu.VMEM((arrived.shape[0] * capc, heads * lanes), bf16),
            pltpu.VMEM(flat, f32),
            pltpu.VMEM(flat, f32),
        ],
        compiler_params=PARAMS,
        cost_estimate=reads(1 << 21),
        name="write",
    )(arrived, cache.reshape(flat))
    return written.reshape(cache.shape)


def two_lane_shards(
    tokens,
    positions,
    attn_gain,
    w_query,
    w_keyval,
    w_out,
    moe_gain,
    router,
    w_gate_up,
    w_down,
    expert_ids,
    cache_slot,
    kv_cache,
):
    groups = lax.axis_size("grp")
    tok_rows, model = tokens.shape
    block = positions.shape[0]
    kv_local, head2 = w_keyval.shape[1:]
    kv_width = kv_local * head2
    slots_dev = kv_cache.shape[0]
    swap = functools.partial(lax.ppermute, axis_name="hd", perm=[(0, 1), (1, 0)])

    together = lax.optimization_barrier

    other_tokens = swap(tokens)
    own = (w_gate_up[0], w_down[0], w_out.T)
    up_rows, down_rows = own[0].shape[0], own[1].shape[0]
    beside = [lax.ppermute(part, "grp", sibling_pairs(groups)) for part in own]
    expert_pair, out_pair = pack(own, beside)
    out_ring = Ring(out_pair, groups)
    out_ring.step()
    expert_ring = Ring(expert_pair, groups)
    expert_ring.step()
    w_keyval, positions = together((w_keyval, positions, out_pair))[:2]
    flat_kv = w_keyval.reshape(model, kv_width)
    cosine, sine, past, place, send, tags, gain = prepare(
        groups, slots_dev, positions, cache_slot, expert_ids, attn_gain
    )
    cosine, flat_kv = out_ring.pin(cosine, flat_kv)
    out_ring.step()

    q, kv, tail = project(tokens, other_tokens, gain, cosine, sine, w_query, flat_kv)
    seam = lax.ppermute(tail, "grp", [(g, g + 1) for g in range(groups - 1)])
    late = attend_late(q, kv, past)
    late = out_ring.pin(late)
    out_ring.step()
    out_ring.share(2)
    seam, late = together((seam, late))
    seam = expert_ring.pin(seam)
    expert_ring.step()
    early = attend_early(q, kv, seam, past)
    early, out_ring.near = together((early, out_ring.near))
    early = out_ring.pin(early)
    out_ring.step()
    out_ring.share(3)
    early, kv, out_ring.near = together((early, kv, out_ring.near))
    outgoing = bundle(groups, send, kv, tags)
    early, outgoing = together((early, outgoing))
    early = out_ring.pin(early)
    early = expert_ring.pin(early)
    expert_ring.step()
    out_ring.share()
    sent = outward_send(groups, early, late, out_ring.parts(), out_ring.unit_rows)
    arrived = swap(sent)
    early = together((early, sent))[0]
    mine = outward_keep(groups, early, late, tokens, out_ring.parts(), out_ring.unit_rows)
    mine = expert_ring.pin(mine)
    expert_ring.step()
    outgoing = together((outgoing, sent))[0]
    arrived_cache = lax.all_to_all(outgoing, "grp", split_axis=0, concat_axis=0, tiled=True)
    arrived, mine, expert_ring.mine[1:] = together((arrived, mine, expert_ring.mine[1:]))
    expert_ring.share()

    residual, moe_in, sent_rows = route(mine, arrived, moe_gain, place)
    landed = swap(sent_rows)
    parts_early, parts_late = expert_ring.split()
    gates, own_rows, spread, *staged = gate(
        groups, moe_in, router.T, expert_ids.T, place, parts_early, up_rows, down_rows
    )
    landed, own_rows = together((landed, own_rows))
    own_made, back = expert(groups, own_rows, landed, staged, parts_late, up_rows, down_rows)
    returned = swap(back)
    layer_out = combine(residual, gates, spread, own_made, returned)
    layer_out, arrived_cache = together((layer_out, arrived_cache))
    cache_after = write(arrived_cache, kv_cache)
    return (layer_out, cache_after)


def passed_along(value, axis, steps):
    count = lax.axis_size(axis)
    initial, last = (max(0, -steps), min(count, count - steps))
    return lax.ppermute(value, axis, [(source, source + steps) for source in range(initial, last)])


def rms_norm(row_set, norm_gain):
    floats = row_set.astype(jnp.float32)
    factor = lax.rsqrt(jnp.mean(floats * floats, axis=-1, keepdims=True) + norm_eps)
    return (floats * factor * norm_gain).astype(jnp.bfloat16)


def rotate(vectors, angle_pos):
    halves = vectors.shape[-1] // 2
    inverse_freq = rope_base ** (-2.0 * jnp.arange(halves, dtype=jnp.float32) / vectors.shape[-1])
    angles = angle_pos[:, None, None] * inverse_freq[None, None, :]
    cosine = jnp.cos(angles)
    sine_part = jnp.sin(angles)
    first_half = vectors[..., :halves]
    second_half = vectors[..., halves:]
    return jnp.concatenate(
        [
            first_half * cosine - second_half * sine_part,
            second_half * cosine + first_half * sine_part,
        ],
        axis=-1,
    )


def expert_rows(row_set, gate_up, down_rows):
    gate_and_up = jnp.dot(row_set, gate_up, preferred_element_type=jnp.float32)
    inner_width = gate_and_up.shape[1] // 2
    hidden = (jax.nn.silu(gate_and_up[:, :inner_width]) * gate_and_up[:, inner_width:]).astype(
        jnp.bfloat16
    )
    return jnp.dot(hidden, down_rows, preferred_element_type=jnp.float32).astype(jnp.bfloat16)


def attend_rows(query_blk, keys_blk, vals_blk, visible, scale_qk):
    scores = (
        jnp.einsum("qkgd,skd->kgqs", query_blk, keys_blk, preferred_element_type=jnp.float32)
        * scale_qk
    )
    weights_f = jnp.where(visible[None, None], jnp.exp(scores), 0.0)
    prob_bf = (weights_f / jnp.sum(weights_f, axis=-1, keepdims=True)).astype(jnp.bfloat16)
    return jnp.einsum("kgqs,skd->qkgd", prob_bf, vals_blk, preferred_element_type=jnp.float32)


def shards(
    tokens,
    positions,
    attn_gain,
    w_query,
    w_keyval,
    w_out,
    moe_gain,
    router,
    w_gate_up,
    w_down,
    expert_ids,
    cache_slot,
    kv_cache,
):
    lane_count = lax.axis_size("hd")
    group_count = lax.axis_size("grp")
    tok_rows = tokens.shape[0]
    model_width = tokens.shape[1]
    block_len = positions.shape[0]
    seg_most = block_len // 2
    head_dim = w_keyval.shape[2] // 2
    kv_local = w_keyval.shape[1]
    q_local = w_query.shape[1] // head_dim
    per_kv = q_local // kv_local
    expert_cap = tok_rows // 4
    normed = rms_norm(tokens, attn_gain)
    flat_kv = w_keyval.reshape(model_width, kv_local * 2 * head_dim)
    section = lax.all_gather(normed, "hd", axis=0, tiled=True)
    projected = jnp.concatenate(
        [
            jnp.dot(section, w_query, preferred_element_type=jnp.float32),
            jnp.dot(section, flat_kv, preferred_element_type=jnp.float32),
        ],
        axis=1,
    )
    angle_pos = jnp.maximum(positions, 0).astype(jnp.float32)
    queries = rotate(
        projected[:, : q_local * head_dim].reshape(block_len, q_local, head_dim), angle_pos
    ).astype(jnp.bfloat16)
    key_val = projected[:, q_local * head_dim :].reshape(block_len, kv_local, 2 * head_dim)
    rotated = rotate(key_val[:, :, :head_dim], angle_pos).astype(jnp.bfloat16)
    stored = jnp.concatenate([rotated, key_val[:, :, head_dim:].astype(jnp.bfloat16)], axis=2)
    seam_rows = passed_along(stored[block_len - seg_most :], "grp", 1)
    window = jnp.concatenate([seam_rows, stored], axis=0)
    scale_qk = head_dim ** (-0.5)
    local_rows = jnp.arange(block_len, dtype=jnp.int32)
    lowest = local_rows - jnp.maximum(positions, 0)
    pieces_out = []
    for q_block in range(2):
        first_row = q_block * seg_most
        rows_here = first_row + jnp.arange(seg_most, dtype=jnp.int32)
        cols_here = first_row - seg_most + jnp.arange(2 * seg_most, dtype=jnp.int32)
        low_here = lowest[first_row : first_row + seg_most]
        visible = (cols_here[None, :] >= low_here[:, None]) & (
            cols_here[None, :] <= rows_here[:, None]
        )
        query_blk = queries[first_row : first_row + seg_most].reshape(
            seg_most, kv_local, per_kv, head_dim
        )
        keys_blk = window[first_row : first_row + 2 * seg_most, :, :head_dim]
        vals_blk = window[first_row : first_row + 2 * seg_most, :, head_dim:]
        mixed_rows = attend_rows(query_blk, keys_blk, vals_blk, visible, scale_qk)
        pieces_out.append(mixed_rows.reshape(seg_most, q_local * head_dim).astype(jnp.bfloat16))
    attended = jnp.concatenate(pieces_out, axis=0)
    slots_dev = kv_cache.shape[0]
    capc = 2 * block_len // group_count
    live_slot = cache_slot >= 0
    owners = jnp.where(live_slot, cache_slot // slots_dev, group_count)
    owner_hit = (owners[:, None] == jnp.arange(group_count, dtype=jnp.int32)[None, :]).astype(
        jnp.bfloat16
    )
    lower_tri = (local_rows[:, None] >= local_rows[None, :]).astype(jnp.bfloat16)
    running = jnp.dot(lower_tri, owner_hit, preferred_element_type=jnp.float32)
    owner_rank = jnp.sum(running * owner_hit.astype(jnp.float32), axis=1).astype(jnp.int32) - 1
    send_rows = jnp.where(live_slot, owners * capc + owner_rank, group_count * capc)
    outgoing_cache = (
        jnp.zeros((group_count * capc, kv_local, 2 * head_dim), jnp.bfloat16)
        .at[send_rows]
        .set(stored, mode="drop")
    )
    outgoing_slots = (
        jnp.full((group_count * capc,), -1, jnp.int32)
        .at[send_rows]
        .set(cache_slot % slots_dev, mode="drop")
    )
    arrived, arrived_slots = (
        lax.all_to_all(
            outgoing_cache.reshape(group_count, capc, kv_local, 2 * head_dim),
            "grp",
            split_axis=0,
            concat_axis=0,
            tiled=True,
        ),
        lax.all_to_all(
            outgoing_slots.reshape(group_count, capc),
            "grp",
            split_axis=0,
            concat_axis=0,
            tiled=True,
        ),
    )
    flat_slots = arrived_slots.reshape(group_count * capc)
    write_rows = jnp.where(flat_slots >= 0, flat_slots, slots_dev).astype(jnp.int32)
    cache_after = kv_cache.at[write_rows].set(
        arrived.reshape(group_count * capc, kv_local, 2 * head_dim), mode="drop"
    )
    by_token = lax.all_to_all(attended, "hd", split_axis=0, concat_axis=1, tiled=True)
    attn_proj = jnp.dot(
        by_token,
        lax.all_gather(w_out, "grp", axis=1, tiled=True),
        preferred_element_type=jnp.float32,
    )
    residual = (tokens.astype(jnp.float32) + attn_proj).astype(jnp.bfloat16)
    moe_in = rms_norm(residual, moe_gain)
    logits = jnp.dot(moe_in, router, preferred_element_type=jnp.float32)
    expert_range = jnp.arange(router.shape[1], dtype=jnp.int32)
    matches_all = expert_ids[:, :, None] == expert_range[None, None, :]
    chosen = jnp.sum(jnp.where(matches_all, logits[:, None, :], 0.0), axis=2)
    raised = jnp.exp(chosen)
    gates = raised / jnp.sum(raised, axis=1, keepdims=True)
    live_range = jnp.arange(lane_count, dtype=jnp.int32)
    matches = expert_ids[:, :, None] == live_range[None, None, :]
    member = jnp.any(matches, axis=1)
    weighting = jnp.sum(jnp.where(matches, gates[:, :, None], 0.0), axis=1)
    ranking = jnp.cumsum(member.astype(jnp.int32), axis=0) - 1
    target = jnp.where(member, live_range[None, :] * expert_cap + ranking, -1)
    slot_range = jnp.arange(lane_count * expert_cap, dtype=jnp.int32)
    slot_hits = target[None, :, :] == slot_range[:, None, None]
    placing = jnp.any(slot_hits, axis=2).astype(jnp.bfloat16)
    outgoing = (
        jnp.dot(placing, moe_in, preferred_element_type=jnp.float32)
        .astype(jnp.bfloat16)
        .reshape(lane_count, expert_cap, model_width)
    )
    gate_up_all, down_all = (
        lax.all_gather(w_gate_up, "grp", axis=1, tiled=True),
        lax.all_gather(w_down, "grp", axis=1, tiled=True),
    )
    gate_up_mat = gate_up_all[0]
    down_mat = down_all[0]
    landed = lax.all_to_all(outgoing, "hd", split_axis=0, concat_axis=0, tiled=True)
    results = expert_rows(landed.reshape(-1, model_width), gate_up_mat, down_mat).reshape(landed.shape)
    returned = lax.all_to_all(results, "hd", split_axis=0, concat_axis=0, tiled=True)
    flat_returned = returned.reshape(-1, model_width)
    fetched = flat_returned[jnp.maximum(target, 0)]
    used_weight = jnp.where(member, weighting, 0.0)
    moe_total = jnp.sum(used_weight[:, :, None] * fetched.astype(jnp.float32), axis=1)
    layer_out = (residual.astype(jnp.float32) + moe_total).astype(jnp.bfloat16)
    return (layer_out, cache_after)


def solution(mesh):
    two_lanes = mesh.shape["hd"] == 2 and mesh.shape["grp"] % 8 == 0
    return jax.shard_map(
        two_lane_shards if two_lanes else shards,
        mesh=mesh,
        in_specs=(
            P(("grp", "hd"), None),
            P("grp"),
            P(),
            P(None, "hd"),
            P(None, "hd", None),
            P(None, "grp"),
            P(),
            P(),
            P("hd", "grp", None),
            P("hd", "grp", None),
            P(("grp", "hd"), None),
            P("grp"),
            P("grp", "hd", None),
        ),
        out_specs=(P(("grp", "hd"), None), P("grp", "hd", None)),
        check_vma=False,
    )
```

```python
import functools

import jax
import jax.numpy as jnp
import numpy as np
from jax import lax
from jax.experimental import pallas as pl
from jax.experimental.pallas import tpu as pltpu
from jax.sharding import PartitionSpec as P

norm_eps = 1e-05
rope_base = 10000.0
bf16 = jnp.bfloat16
f32 = jnp.float32
LAST_DIMS = (((1,), (1,)), ((), ()))


def ring_cycle(groups):
    rows = groups // 4
    return [2 * r for r in range(rows)] + [2 * r + 1 for r in reversed(range(rows))]


def ring_pairs(groups):
    cycle = ring_cycle(groups)
    count = len(cycle)
    pairs = []
    for place, pair in enumerate(cycle):
        pairs.append((2 * pair, 2 * cycle[(place + 1) % count]))
        pairs.append((2 * pair + 1, 2 * cycle[(place - 1) % count] + 1))
    return pairs


def sibling_pairs(groups):
    return [(g, g ^ 1) for g in range(groups)]


def ring_sources(groups, me):
    count = groups // 2
    rows = count // 2
    side, pair = me % 2, me // 2
    row, col = pair // 2, pair % 2
    place = jnp.where(col == 0, row, count - 1 - row)

    def block(core, steps):
        there = (place + (2 * core - 1) * steps + count) % count
        other = jnp.where(there < rows, 2 * there, 2 * (count - 1 - there) + 1)
        return [2 * other + core, 2 * other + 1 - core]

    full = (count - 1) // 2
    listed = [me, me + 1 - 2 * side]
    for core in (side, 1 - side):
        for steps in range(1, full + 1):
            listed += block(core, steps)
    return listed + [block(side, count // 2)[0], block(1 - side, count // 2)[0]]


class Ring:
    def __init__(self, pair, groups):
        self.across = functools.partial(lax.ppermute, axis_name="grp", perm=ring_pairs(groups))
        self.beside = functools.partial(lax.ppermute, axis_name="grp", perm=sibling_pairs(groups))
        self.full = (groups // 2 - 1) // 2
        self.unit_rows = pair.shape[0] // 2
        self.mine = [pair]
        self.near = []

    def step(self):
        held = self.mine[-1]
        if len(self.mine) > self.full:
            held = held[: self.unit_rows]
        self.mine.append(self.across(held))

    def pin(self, *others):
        done = lax.optimization_barrier((self.mine[-1],) + others)
        self.mine[-1] = done[0]
        return done[1:] if len(others) > 1 else done[1]

    def share(self, upto=None):
        for index in range(1 + len(self.near), 1 + (upto or len(self.mine) - 1)):
            self.near.append(self.beside(self.mine[index]))

    def parts(self):
        full = self.full
        return self.mine[: full + 1] + self.near[:full] + [self.mine[full + 1], self.near[full]]

    def split(self):
        full = self.full
        listed = [(part, 2 * index) for index, part in enumerate(self.parts()[:-1])]
        listed.append((self.near[full], 4 * full + 3))
        late = (full, 2 * full, 2 * full + 1, 2 * full + 2)
        return (
            [pair for index, pair in enumerate(listed) if index not in late],
            [listed[index] for index in late],
        )


def place_parts(groups, parts, unit_rows, pieces, shards=None):
    sources = ring_sources(groups, lax.axis_index("grp"))
    shard = 0
    for index, part in enumerate(parts):
        shard = shards[index] if shards else shard
        for unit in range(part.shape[0] // unit_rows):
            for first, rows, target, lane in pieces:
                at = pl.multiple_of(sources[shard] * rows, rows)
                start = unit * unit_rows + first
                target[pl.ds(at, rows), lane : lane + part.shape[1]] = part[start : start + rows, :]
            shard += 1


VMEM = pl.BlockSpec(memory_space=pltpu.VMEM)
ANY = pl.BlockSpec(memory_space=pl.ANY)
HBM = pl.BlockSpec(memory_space=pltpu.HBM)
PARAMS = pltpu.CompilerParams(vmem_limit_bytes=16 << 20)


LITTLE = pl.CostEstimate(flops=1, bytes_accessed=1, transcendentals=0)


def takes(us):
    return pl.CostEstimate(
        flops=int(us * 1.15e9), bytes_accessed=int(us * 8e6), transcendentals=0
    )


def reads(nbytes):
    return pl.CostEstimate(flops=1, bytes_accessed=nbytes, transcendentals=0)


def normalized(floats, gain):
    factor = lax.rsqrt(jnp.mean(floats * floats, axis=-1, keepdims=True) + norm_eps)
    return (floats * factor * gain).astype(bf16)


def fetch(pairs, sems):
    copies = []
    for index, (source, target) in enumerate(pairs):
        copies.append(pltpu.make_async_copy(source, target, sems.at[index]))
        copies[-1].start()
    return copies


def pack_kernel(*refs):
    sources, (expert_pair, out_pair, sems) = refs[:6], refs[6:]
    width = expert_pair.shape[1]
    lane = lax.axis_index("hd")
    first = pl.multiple_of(lane * out_pair.shape[1], out_pair.shape[1])
    pairs = []
    row = 0
    for index in range(2):
        up, down, w_out = sources[3 * index : 3 * index + 3]
        count = w_out.shape[0]
        pairs.append(
            (w_out.at[:, pl.ds(first, out_pair.shape[1])], out_pair.at[pl.ds(index * count, count), :])
        )
        for source in (up, down):
            for at in range(0, source.shape[1], width):
                pairs.append(
                    (source.at[:, pl.ds(at, width)], expert_pair.at[pl.ds(row, source.shape[0]), :])
                )
                row += source.shape[0]
    for copy in fetch(pairs, sems):
        copy.wait()


def pack(own, beside):
    own = [pltpu.with_memory_space_constraint(part, pltpu.HBM) for part in own]
    up, down, w_out_t = own
    width = up.shape[1] // 2
    pieces = [up.shape[1] // width, down.shape[1] // width]
    unit_rows = pieces[0] * up.shape[0] + pieces[1] * down.shape[0]
    return pl.pallas_call(
        pack_kernel,
        out_shape=(
            jax.ShapeDtypeStruct((2 * unit_rows, width), bf16),
            jax.ShapeDtypeStruct((2 * w_out_t.shape[0], w_out_t.shape[1] // 2), bf16),
        ),
        in_specs=[ANY] * 6,
        out_specs=(ANY, ANY),
        scratch_shapes=[pltpu.SemaphoreType.DMA((2 + 2 * sum(pieces),))],
        compiler_params=PARAMS,
        cost_estimate=LITTLE,
        name="pack",
    )(*own, *beside)


def as_column(row, eye):
    return jnp.sum(jnp.where(eye, row, 0.0), axis=1, keepdims=True)


def named_experts(ids, experts):
    tokens = ids.shape[1]
    expert = lax.broadcasted_iota(jnp.int32, (experts, tokens), 0)
    hit = jnp.zeros((experts, tokens), f32)
    for index in range(ids.shape[0]):
        hit = jnp.where(ids[index : index + 1, :] == expert, 1.0, hit)
    return hit


def prepare_kernel(groups, slots_dev, *refs):
    sources, (cosine, sine, past, place, send, tags, gain) = refs[:4], refs[4:11]
    positions, slots, ids, flat_gain, sems = refs[11:]
    copies = fetch(list(zip(sources, (positions, slots, ids, flat_gain))), sems)
    for copy in copies:
        copy.wait()
    gain[...] = flat_gain[...].reshape(gain.shape)
    lane = lax.axis_index("hd")
    block = positions.shape[1]

    def iota(shape, dim):
        return lax.broadcasted_iota(jnp.int32, shape, dim)

    eye = iota((block, block), 0) == iota((block, block), 1)
    reach = as_column(jnp.maximum(positions[...], 0).astype(f32), eye)
    past[...] = jnp.broadcast_to(reach, past.shape)
    column = iota((8, 128), 1)
    exponent = (column % 32).astype(f32) * (-2.0 / 64)
    inverse_freq = jnp.exp(exponent * np.float32(np.log(rope_base)))[:1, :]
    angles = reach * inverse_freq
    cosine[...] = jnp.cos(angles)
    turned = jnp.sin(angles)
    sine[...] = jnp.where(iota(angles.shape, 1) % 64 < 32, -turned, turned)

    tokens = ids.shape[1]
    cap = place.shape[0] // 2
    hit = named_experts(ids, 8)
    upto = (iota((tokens, tokens), 0) <= iota((tokens, tokens), 1)).astype(f32)
    rank = jnp.dot(hit, upto, preferred_element_type=f32) - 1.0
    slot = iota((2 * cap, tokens), 0).astype(f32)
    placed = jnp.zeros((2 * cap, tokens), f32)
    for live in range(2):
        order = jnp.where(lane == live, 0, cap).astype(f32)
        member = hit[live : live + 1, :] > 0.0
        placed = jnp.where(member & (slot == rank[live : live + 1, :] + order), 1.0, placed)
    place[...] = placed.astype(bf16)

    where = slots[...]
    owner = jnp.where(where >= 0, where // slots_dev, -1)
    owner_hit = (iota((groups, block), 0) == owner).astype(f32)
    before = (iota((block, block), 0) <= iota((block, block), 1)).astype(f32)
    running = jnp.dot(owner_hit, before, preferred_element_type=f32)
    owner_rank = jnp.sum(owner_hit * running, axis=0, keepdims=True) - 1.0
    capc = send.shape[0] // groups
    row = jnp.where(owner >= 0, owner * capc + owner_rank.astype(jnp.int32), -1)
    send[...] = (iota(send.shape, 0) == row).astype(bf16)
    inside = jnp.where(where >= 0, where % slots_dev, 0)
    high = as_column((inside // 64 + 1).astype(f32), eye)
    low = as_column((inside % 64).astype(f32), eye)
    spot = iota(tags.shape, 1)
    tags[...] = jnp.where(spot == 0, high, jnp.where(spot == 1, low, 0.0)).astype(bf16)


def prepare(groups, slots_dev, positions, slots, ids, gain):
    block, tokens = positions.shape[0], ids.shape[0]
    model = gain.shape[0]
    cap = tokens // 4
    capc = 2 * block // groups
    shapes = [
        ((block, 128), f32),
        ((block, 128), f32),
        ((block, 128), f32),
        ((2 * cap, tokens), bf16),
        ((groups * capc, block), bf16),
        ((block, 128), bf16),
        ((1, model), f32),
    ]
    sources = (positions[None], slots[None], ids.T, gain)
    return pl.pallas_call(
        functools.partial(prepare_kernel, groups, slots_dev),
        out_shape=tuple(jax.ShapeDtypeStruct(shape, kind) for shape, kind in shapes),
        in_specs=[ANY] * 4,
        out_specs=(VMEM,) * len(shapes),
        scratch_shapes=[
            pltpu.VMEM((1, block), jnp.int32),
            pltpu.VMEM((1, block), jnp.int32),
            pltpu.VMEM(ids.shape[::-1], jnp.int32),
            pltpu.VMEM((model,), f32),
            pltpu.SemaphoreType.DMA((4,)),
        ],
        compiler_params=PARAMS,
        cost_estimate=LITTLE,
        name="prepare",
    )(*[pltpu.with_memory_space_constraint(source, pltpu.HBM) for source in sources])


def project_kernel(
    own, other, gain, cosine, sine, w_query, w_keyval, q_out, kv_out, seam_out, raw, rows, sems
):
    count = own.shape[0]
    lane = lax.axis_index("hd")
    mine = pl.multiple_of(lane * count, count)
    theirs = pl.multiple_of((1 - lane) * count, count)
    copies = fetch([(own, raw.at[0]), (other, raw.at[1])], sems)
    cos_q, sin_q = cosine[...], sine[...]
    column = lax.broadcasted_iota(jnp.int32, cos_q.shape, 1)
    lower = column % 64 < 32
    cos_kv = jnp.where(column < 64, cos_q, 1.0)
    sin_kv = jnp.where(column < 64, sin_q, 0.0)
    for index, first in ((0, mine), (1, theirs)):
        copies[index].wait()
        rows[pl.ds(first, count), :] = normalized(raw[index].astype(f32), gain[...])
    width = 256
    for weights, out, cos, sin in ((w_keyval, kv_out, cos_kv, sin_kv), (w_query, q_out, cos_q, sin_q)):
        for first in range(0, weights.shape[1], width):
            made = jnp.dot(rows[...], weights[:, first : first + width], preferred_element_type=f32)
            for part in range(0, width, 128):
                here = made[:, part : part + 128]
                turned = jnp.where(lower, pltpu.roll(here, 96, 1), pltpu.roll(here, 32, 1))
                done = (here * cos + turned * sin).astype(bf16)
                out[:, first + part : first + part + 128] = done
                if out is kv_out:
                    seam_out[:, first + part : first + part + 128] = done[count:, :]


def project(own, other, gain, cosine, sine, w_query, flat_kv):
    count, width = own.shape
    made = w_query.shape[1] + flat_kv.shape[1]
    return pl.pallas_call(
        project_kernel,
        out_shape=(
            jax.ShapeDtypeStruct((2 * count, w_query.shape[1]), bf16),
            jax.ShapeDtypeStruct((2 * count, flat_kv.shape[1]), bf16),
            jax.ShapeDtypeStruct((count, flat_kv.shape[1]), bf16),
        ),
        in_specs=[ANY] * 2 + [VMEM] * 5,
        out_specs=(VMEM, VMEM, VMEM),
        scratch_shapes=[
            pltpu.VMEM((2, count, width), bf16),
            pltpu.VMEM((2 * count, width), bf16),
            pltpu.SemaphoreType.DMA((2,)),
        ],
        compiler_params=PARAMS,
        cost_estimate=takes(8),
        name="project",
    )(own, other, gain, cosine, sine, w_query, flat_kv)


def attend_rows_kernel(first, q, kv, seam, past, mixed, window, sem):
    count = q.shape[0] // 2
    if first == 0:
        copy = pltpu.make_async_copy(seam, window.at[pl.ds(0, count), :], sem)
        copy.start()
        window[count:, :] = kv[:count, :]
        copy.wait()
        keyed = window
    else:
        keyed = kv
    head = 64
    kv_heads = kv.shape[1] // (2 * head)
    per_kv = q.shape[1] // head // kv_heads
    shape = (count, 2 * count)
    row = lax.broadcasted_iota(jnp.int32, shape, 0) + count
    col = lax.broadcasted_iota(jnp.int32, shape, 1)
    reach = past[first : first + count, :1].astype(jnp.int32)
    visible = (col <= row) & (col >= row - reach)
    for kv_head in range(kv_heads):
        lanes = 2 * head * kv_head
        keys = keyed[:, lanes : lanes + head]
        values = keyed[:, lanes + head : lanes + 2 * head]
        for index in range(per_kv):
            at = (kv_head * per_kv + index) * head
            query = q[first : first + count, at : at + head]
            scores = lax.dot_general(query, keys, LAST_DIMS, preferred_element_type=f32)
            raised = jnp.where(visible, jnp.exp(scores * head ** (-0.5)), 0.0)
            probs = (raised / jnp.sum(raised, axis=-1, keepdims=True)).astype(bf16)
            made = jnp.dot(probs, values, preferred_element_type=f32)
            mixed[:, at : at + head] = made.astype(bf16)


def attend_late(q, kv, past):
    def kernel(q, kv, past, mixed):
        attend_rows_kernel(q.shape[0] // 2, q, kv, None, past, mixed, None, None)

    return pl.pallas_call(
        kernel,
        out_shape=jax.ShapeDtypeStruct((q.shape[0] // 2, q.shape[1]), bf16),
        in_specs=[VMEM] * 3,
        out_specs=VMEM,
        compiler_params=PARAMS,
        cost_estimate=takes(2),
        name="attend_late",
    )(q, kv, past)


def attend_early(q, kv, seam, past):
    return pl.pallas_call(
        functools.partial(attend_rows_kernel, 0),
        out_shape=jax.ShapeDtypeStruct((q.shape[0] // 2, q.shape[1]), bf16),
        in_specs=[VMEM, VMEM, ANY, VMEM],
        out_specs=VMEM,
        scratch_shapes=[pltpu.VMEM(kv.shape, bf16), pltpu.SemaphoreType.DMA],
        compiler_params=PARAMS,
        cost_estimate=takes(2),
        name="attend_early",
    )(q, kv, seam, past)


def outward_rows(flip, groups, unit_rows, early, late, parts, w_out, rows):
    place_parts(groups, parts, unit_rows, [(0, unit_rows, w_out, 0)])
    lane = lax.axis_index("hd")
    which = (1 - lane) if flip else lane

    @pl.when(which == 0)
    def _():
        rows[...] = early[...]

    @pl.when(which != 0)
    def _():
        rows[...] = late[...]

    return lax.dot_general(rows[...], w_out[...], LAST_DIMS, preferred_element_type=f32)


def send_kernel(groups, unit_rows, n_parts, early, late, *refs):
    parts, (out, w_out, rows) = refs[:n_parts], refs[n_parts:]
    out[...] = outward_rows(True, groups, unit_rows, early, late, parts, w_out, rows).astype(bf16)


def keep_kernel(groups, unit_rows, n_parts, early, late, tokens, *refs):
    parts, (out, w_out, rows) = refs[:n_parts], refs[n_parts:]
    made = outward_rows(False, groups, unit_rows, early, late, parts, w_out, rows)
    out[...] = tokens[...].astype(f32) + made


def outward_send(groups, early, late, parts, unit_rows):
    width, depth = groups * unit_rows, parts[0].shape[1]
    return pl.pallas_call(
        functools.partial(send_kernel, groups, unit_rows, len(parts)),
        out_shape=jax.ShapeDtypeStruct((early.shape[0], width), bf16),
        in_specs=[VMEM] * (2 + len(parts)),
        out_specs=VMEM,
        scratch_shapes=[pltpu.VMEM((width, depth), bf16), pltpu.VMEM(early.shape, bf16)],
        compiler_params=PARAMS,
        cost_estimate=reads(2 * width * depth),
        name="outward_send",
    )(early, late, *parts)


def outward_keep(groups, early, late, tokens, parts, unit_rows):
    width, depth = groups * unit_rows, parts[0].shape[1]
    return pl.pallas_call(
        functools.partial(keep_kernel, groups, unit_rows, len(parts)),
        out_shape=jax.ShapeDtypeStruct(tokens.shape, f32),
        in_specs=[VMEM] * (3 + len(parts)),
        out_specs=VMEM,
        scratch_shapes=[
            pltpu.VMEM((width, depth), bf16),
            pltpu.VMEM(early.shape, bf16),
        ],
        compiler_params=PARAMS,
        cost_estimate=reads(2 * width * depth),
        name="outward_keep",
    )(early, late, tokens, *parts)


def route_kernel(mine, arrived, flat_gain, place, residual, moe_in, sent, gain, gain_sem):
    copy = pltpu.make_async_copy(flat_gain, gain, gain_sem)
    copy.start()
    added = (mine[...] + arrived[...].astype(f32)).astype(bf16)
    residual[...] = added
    copy.wait()
    moe_in[...] = normalized(added.astype(f32), gain[...].reshape(1, gain.shape[0]))
    cap = sent.shape[0]
    rows = jnp.dot(place[cap:, :], moe_in[...], preferred_element_type=f32)
    sent[...] = rows.astype(bf16)


def route(mine, arrived, flat_gain, place):
    cap = place.shape[0] // 2
    return pl.pallas_call(
        route_kernel,
        out_shape=(
            jax.ShapeDtypeStruct(mine.shape, bf16),
            jax.ShapeDtypeStruct(mine.shape, bf16),
            jax.ShapeDtypeStruct((cap, mine.shape[1]), bf16),
        ),
        in_specs=[VMEM, VMEM, ANY, VMEM],
        out_specs=(VMEM,) * 3,
        scratch_shapes=[pltpu.VMEM(flat_gain.shape, f32), pltpu.SemaphoreType.DMA],
        compiler_params=PARAMS,
        cost_estimate=reads(16 << 20),
        name="route",
    )(mine, arrived, pltpu.with_memory_space_constraint(flat_gain, pltpu.HBM), place)


def expert_pieces(gate_up, down, up_rows, down_rows, width):
    pieces = [(i * up_rows, up_rows, gate_up, i * width) for i in range(2)]
    pieces += [
        (2 * up_rows + i * down_rows, down_rows, down, i * width) for i in range(down.shape[1] // width)
    ]
    return pieces, pieces[-1][0] + down_rows


def gate_kernel(groups, up_rows, down_rows, shards, moe_in, router_in, ids_in, place, *refs):
    parts, (gates, own, spread, gate_up, down, router, ids, sems, part_sems) = (
        refs[: len(shards)],
        refs[len(shards) :],
    )
    small = fetch([(router_in, router), (ids_in, ids)], sems)
    width = parts[0].shape[1]
    pieces, unit_rows = expert_pieces(gate_up, down, up_rows, down_rows, width)
    sources = ring_sources(groups, lax.axis_index("grp"))
    pairs = []
    for part, shard in zip(parts, shards):
        for unit in range(part.shape[0] // unit_rows):
            for first, rows, target, lane in pieces:
                at = pl.multiple_of(sources[shard + unit] * rows, rows)
                pairs.append(
                    (
                        part.at[pl.ds(unit * unit_rows + first, rows), :],
                        target.at[pl.ds(at, rows), pl.ds(lane, width)],
                    )
                )
    copies = fetch(pairs, part_sems)
    cap = own.shape[0]
    own[...] = jnp.dot(place[:cap, :], moe_in[...], preferred_element_type=f32).astype(bf16)
    tokens = ids.shape[1]
    row = lax.broadcasted_iota(jnp.int32, (tokens, tokens), 0)
    eye = (row == lax.broadcasted_iota(jnp.int32, (tokens, tokens), 1)).astype(f32)
    spread[...] = lax.dot_general(
        eye.astype(bf16), place[...], LAST_DIMS, preferred_element_type=f32
    ).astype(bf16)
    for copy in small:
        copy.wait()
    hit = named_experts(ids, router.shape[0])
    named = lax.dot_general(eye, hit, LAST_DIMS, preferred_element_type=f32)
    logits = lax.dot_general(moe_in[...], router[...], LAST_DIMS, preferred_element_type=f32)
    raised = jnp.where(named > 0, jnp.exp(logits), 0.0)
    gates[...] = raised / jnp.sum(raised, axis=-1, keepdims=True)
    for copy in copies:
        copy.wait()


def gate(groups, moe_in, router_t, ids_t, place, early, up_rows, down_rows):
    cap = place.shape[0] // 2
    tokens, model = moe_in.shape
    width = early[0][0].shape[1]
    units = 2 * len(early)
    far = [pltpu.with_memory_space_constraint(part, pltpu.HBM) for part in (router_t, ids_t)]
    return pl.pallas_call(
        functools.partial(gate_kernel, groups, up_rows, down_rows, [shard for _, shard in early]),
        out_shape=(
            jax.ShapeDtypeStruct((tokens, router_t.shape[0]), f32),
            jax.ShapeDtypeStruct((cap, model), bf16),
            jax.ShapeDtypeStruct(place.shape[::-1], bf16),
            jax.ShapeDtypeStruct((groups * up_rows, 2 * width), bf16),
            jax.ShapeDtypeStruct((groups * down_rows, model), bf16),
        ),
        in_specs=[VMEM, ANY, ANY, VMEM] + [ANY] * len(early),
        out_specs=(VMEM,) * 5,
        scratch_shapes=[
            pltpu.VMEM(router_t.shape, bf16),
            pltpu.VMEM(ids_t.shape, jnp.int32),
            pltpu.SemaphoreType.DMA((2,)),
            pltpu.SemaphoreType.DMA((units * (2 + model // width),)),
        ],
        compiler_params=PARAMS,
        cost_estimate=LITTLE,
        name="gate",
    )(moe_in, *far, place, *[part for part, _ in early])


def expert_kernel(groups, up_rows, down_rows, shards, own, other, gate_up_in, down_in, *refs):
    parts = refs[: len(shards)]
    own_out, other_out, gate_up, down, rows = refs[len(shards) :]
    width = parts[0].shape[1]
    count = own.shape[0]
    rows[:count, :] = own[...]
    rows[count:, :] = other[...]
    pieces, unit_rows = expert_pieces(gate_up, down, up_rows, down_rows, width)
    place_parts(groups, parts, unit_rows, pieces, shards)
    both = jnp.dot(rows[...], gate_up[...], preferred_element_type=f32)
    gate, up = both[:, :width], both[:, width:]
    hidden = (gate / (1.0 + jnp.exp(-gate)) * up).astype(bf16)
    made = jnp.dot(hidden, down[...], preferred_element_type=f32).astype(bf16)
    own_out[...] = made[:count, :]
    other_out[...] = made[count:, :]


def expert(groups, own, other, staged, late, up_rows, down_rows):
    count, model = own.shape
    width = late[0][0].shape[1]
    return pl.pallas_call(
        functools.partial(expert_kernel, groups, up_rows, down_rows, [shard for _, shard in late]),
        out_shape=(jax.ShapeDtypeStruct(own.shape, bf16),) * 2
        + tuple(jax.ShapeDtypeStruct(part.shape, bf16) for part in staged),
        in_specs=[VMEM] * (4 + len(late)),
        out_specs=(VMEM,) * 4,
        scratch_shapes=[pltpu.VMEM((2 * count, model), bf16)],
        input_output_aliases={2: 2, 3: 3},
        compiler_params=PARAMS,
        cost_estimate=pl.CostEstimate(flops=int(4.2 * 1.15e9), bytes_accessed=1, transcendentals=0),
        name="expert",
    )(own, other, *staged, *[part for part, _ in late])[:2]


def combine_kernel(residual, gates, spread, own, returned, out):
    lane = lax.axis_index("hd")
    count = own.shape[0]
    column = lax.broadcasted_iota(jnp.int32, gates.shape, 1)
    total = jnp.zeros(residual.shape, f32)
    for index, made in ((0, own), (1, returned)):
        live = lane if index == 0 else 1 - lane
        weight = jnp.sum(jnp.where(column == live, gates[...], 0.0), axis=-1, keepdims=True)
        picked = jnp.dot(
            spread[:, index * count : (index + 1) * count], made[...], preferred_element_type=f32
        )
        total += weight * picked
    out[...] = (residual[...].astype(f32) + total).astype(bf16)


def combine(residual, gates, spread, own, returned):
    return pl.pallas_call(
        combine_kernel,
        out_shape=jax.ShapeDtypeStruct(residual.shape, bf16),
        in_specs=[VMEM] * 5,
        out_specs=VMEM,
        compiler_params=PARAMS,
        cost_estimate=reads(6 * residual.shape[0] * residual.shape[1]),
        name="combine",
    )(residual, gates, spread, own, returned)


def bundle_kernel(send, kv, tags, result, out, sem):
    groups, rows, _ = out.shape
    heads = kv.shape[1] // 128
    capc = send.shape[0] // groups
    packed = jnp.dot(send[...], kv[...], preferred_element_type=f32).astype(bf16)
    tagged = jnp.dot(send[...], tags[...], preferred_element_type=f32)
    one = (lax.broadcasted_iota(jnp.int32, (16, 128), 0) == lax.broadcasted_iota(jnp.int32, (16, 128), 1))
    for owner in range(groups):
        mine = slice(owner * capc, (owner + 1) * capc)
        for head in range(heads):
            out[owner, head * capc : (head + 1) * capc, :] = packed[mine, head * 128 : (head + 1) * 128]
        wide = jnp.concatenate([tagged[mine, :], jnp.zeros((128 - capc, 128), f32)], axis=0)
        out[owner, heads * capc :, :] = lax.dot_general(
            one.astype(f32), wide, LAST_DIMS, preferred_element_type=f32
        ).astype(bf16)
    copy = pltpu.make_async_copy(out, result, sem)
    copy.start()
    copy.wait()


def bundle(groups, send, kv, tags):
    rows = send.shape[0] // groups * (kv.shape[1] // 128) + 16
    return pl.pallas_call(
        bundle_kernel,
        out_shape=pltpu.HBM((groups, rows, 128), bf16),
        in_specs=[VMEM] * 3,
        out_specs=HBM,
        scratch_shapes=[pltpu.VMEM((groups, rows, 128), bf16), pltpu.SemaphoreType.DMA],
        compiler_params=PARAMS,
        cost_estimate=LITTLE,
        name="bundle",
    )(send, kv, tags)


def write_kernel(heads, arrived, cache, out, rows, wide, known):
    groups, size, _ = arrived.shape
    slots = cache.shape[0] // heads
    capc = (size - 16) // heads
    high, low = [], []
    for source in range(groups):
        for head in range(heads):
            rows[source * capc : (source + 1) * capc, head * 128 : (head + 1) * 128] = arrived[
                source, head * capc : (head + 1) * capc, :
            ]
        numbers = arrived[source, heads * capc :, :].astype(f32)
        high.append(numbers[0:1, :capc])
        low.append(numbers[1:2, :capc])
    slot = jnp.concatenate(high, axis=1) * 64.0 + jnp.concatenate(low, axis=1) - 64.0
    row = lax.broadcasted_iota(jnp.int32, (slots, slot.shape[1]), 0).astype(f32)
    hit = (row == slot).astype(bf16)
    made = jnp.dot(hit, rows[...], preferred_element_type=f32)
    found = jnp.dot(hit, jnp.ones((slot.shape[1], 128), bf16), preferred_element_type=f32)
    for head in range(heads):
        wide[pl.ds(head, slots, heads), :] = made[:, head * 128 : (head + 1) * 128]
        known[pl.ds(head, slots, heads), :] = found
    old = cache[...].astype(f32)
    out[...] = jnp.where(known[...] > 0.0, wide[...], old).astype(bf16)


def write(arrived, cache):
    slots, heads, lanes = cache.shape
    capc = (arrived.shape[1] - 16) // heads
    flat = (slots * heads, lanes)
    written = pl.pallas_call(
        functools.partial(write_kernel, heads),
        out_shape=jax.ShapeDtypeStruct(flat, bf16),
        in_specs=[VMEM] * 2,
        out_specs=VMEM,
        scratch_shapes=[
            pltpu.VMEM((arrived.shape[0] * capc, heads * lanes), bf16),
            pltpu.VMEM(flat, f32),
            pltpu.VMEM(flat, f32),
        ],
        compiler_params=PARAMS,
        cost_estimate=reads(1 << 21),
        name="write",
    )(arrived, cache.reshape(flat))
    return written.reshape(cache.shape)


def two_lane_shards(
    tokens,
    positions,
    attn_gain,
    w_query,
    w_keyval,
    w_out,
    moe_gain,
    router,
    w_gate_up,
    w_down,
    expert_ids,
    cache_slot,
    kv_cache,
):
    groups = lax.axis_size("grp")
    tok_rows, model = tokens.shape
    block = positions.shape[0]
    kv_local, head2 = w_keyval.shape[1:]
    kv_width = kv_local * head2
    slots_dev = kv_cache.shape[0]
    swap = functools.partial(lax.ppermute, axis_name="hd", perm=[(0, 1), (1, 0)])

    together = lax.optimization_barrier

    other_tokens = swap(tokens)
    own = (w_gate_up[0], w_down[0], w_out.T)
    up_rows, down_rows = own[0].shape[0], own[1].shape[0]
    beside = [lax.ppermute(part, "grp", sibling_pairs(groups)) for part in own]
    expert_pair, out_pair = pack(own, beside)
    out_ring = Ring(out_pair, groups)
    out_ring.step()
    expert_ring = Ring(expert_pair, groups)
    expert_ring.step()
    w_keyval, positions = together((w_keyval, positions, out_pair))[:2]
    flat_kv = w_keyval.reshape(model, kv_width)
    cosine, sine, past, place, send, tags, gain = prepare(
        groups, slots_dev, positions, cache_slot, expert_ids, attn_gain
    )
    cosine, flat_kv = out_ring.pin(cosine, flat_kv)
    out_ring.step()

    q, kv, tail = project(tokens, other_tokens, gain, cosine, sine, w_query, flat_kv)
    seam = lax.ppermute(tail, "grp", [(g, g + 1) for g in range(groups - 1)])
    late = attend_late(q, kv, past)
    late = out_ring.pin(late)
    out_ring.step()
    out_ring.share(2)
    seam, late = together((seam, late))
    seam = expert_ring.pin(seam)
    expert_ring.step()
    early = attend_early(q, kv, seam, past)
    early, out_ring.near = together((early, out_ring.near))
    early = out_ring.pin(early)
    out_ring.step()
    out_ring.share(3)
    early, kv, out_ring.near = together((early, kv, out_ring.near))
    outgoing = bundle(groups, send, kv, tags)
    early, outgoing = together((early, outgoing))
    early = out_ring.pin(early)
    early = expert_ring.pin(early)
    expert_ring.step()
    out_ring.share()
    sent = outward_send(groups, early, late, out_ring.parts(), out_ring.unit_rows)
    arrived = swap(sent)
    early = together((early, sent))[0]
    mine = outward_keep(groups, early, late, tokens, out_ring.parts(), out_ring.unit_rows)
    mine = expert_ring.pin(mine)
    expert_ring.step()
    outgoing = together((outgoing, sent))[0]
    arrived_cache = lax.all_to_all(outgoing, "grp", split_axis=0, concat_axis=0, tiled=True)
    arrived, mine, expert_ring.mine[1:] = together((arrived, mine, expert_ring.mine[1:]))
    expert_ring.share()

    residual, moe_in, sent_rows = route(mine, arrived, moe_gain, place)
    landed = swap(sent_rows)
    parts_early, parts_late = expert_ring.split()
    gates, own_rows, spread, *staged = gate(
        groups, moe_in, router.T, expert_ids.T, place, parts_early, up_rows, down_rows
    )
    landed, own_rows = together((landed, own_rows))
    own_made, back = expert(groups, own_rows, landed, staged, parts_late, up_rows, down_rows)
    returned = swap(back)
    layer_out = combine(residual, gates, spread, own_made, returned)
    layer_out, arrived_cache = together((layer_out, arrived_cache))
    cache_after = write(arrived_cache, kv_cache)
    return (layer_out, cache_after)


def passed_along(value, axis, steps):
    count = lax.axis_size(axis)
    initial, last = (max(0, -steps), min(count, count - steps))
    return lax.ppermute(value, axis, [(source, source + steps) for source in range(initial, last)])


def rms_norm(row_set, norm_gain):
    floats = row_set.astype(jnp.float32)
    factor = lax.rsqrt(jnp.mean(floats * floats, axis=-1, keepdims=True) + norm_eps)
    return (floats * factor * norm_gain).astype(jnp.bfloat16)


def rotate(vectors, angle_pos):
    halves = vectors.shape[-1] // 2
    inverse_freq = rope_base ** (-2.0 * jnp.arange(halves, dtype=jnp.float32) / vectors.shape[-1])
    angles = angle_pos[:, None, None] * inverse_freq[None, None, :]
    cosine = jnp.cos(angles)
    sine_part = jnp.sin(angles)
    first_half = vectors[..., :halves]
    second_half = vectors[..., halves:]
    return jnp.concatenate(
        [
            first_half * cosine - second_half * sine_part,
            second_half * cosine + first_half * sine_part,
        ],
        axis=-1,
    )


def expert_rows(row_set, gate_up, down_rows):
    gate_and_up = jnp.dot(row_set, gate_up, preferred_element_type=jnp.float32)
    inner_width = gate_and_up.shape[1] // 2
    hidden = (jax.nn.silu(gate_and_up[:, :inner_width]) * gate_and_up[:, inner_width:]).astype(
        jnp.bfloat16
    )
    return jnp.dot(hidden, down_rows, preferred_element_type=jnp.float32).astype(jnp.bfloat16)


def attend_rows(query_blk, keys_blk, vals_blk, visible, scale_qk):
    scores = (
        jnp.einsum("qkgd,skd->kgqs", query_blk, keys_blk, preferred_element_type=jnp.float32)
        * scale_qk
    )
    weights_f = jnp.where(visible[None, None], jnp.exp(scores), 0.0)
    prob_bf = (weights_f / jnp.sum(weights_f, axis=-1, keepdims=True)).astype(jnp.bfloat16)
    return jnp.einsum("kgqs,skd->qkgd", prob_bf, vals_blk, preferred_element_type=jnp.float32)


def shards(
    tokens,
    positions,
    attn_gain,
    w_query,
    w_keyval,
    w_out,
    moe_gain,
    router,
    w_gate_up,
    w_down,
    expert_ids,
    cache_slot,
    kv_cache,
):
    lane_count = lax.axis_size("hd")
    group_count = lax.axis_size("grp")
    tok_rows = tokens.shape[0]
    model_width = tokens.shape[1]
    block_len = positions.shape[0]
    seg_most = block_len // 2
    head_dim = w_keyval.shape[2] // 2
    kv_local = w_keyval.shape[1]
    q_local = w_query.shape[1] // head_dim
    per_kv = q_local // kv_local
    expert_cap = tok_rows // 4
    normed = rms_norm(tokens, attn_gain)
    flat_kv = w_keyval.reshape(model_width, kv_local * 2 * head_dim)
    section = lax.all_gather(normed, "hd", axis=0, tiled=True)
    projected = jnp.concatenate(
        [
            jnp.dot(section, w_query, preferred_element_type=jnp.float32),
            jnp.dot(section, flat_kv, preferred_element_type=jnp.float32),
        ],
        axis=1,
    )
    angle_pos = jnp.maximum(positions, 0).astype(jnp.float32)
    queries = rotate(
        projected[:, : q_local * head_dim].reshape(block_len, q_local, head_dim), angle_pos
    ).astype(jnp.bfloat16)
    key_val = projected[:, q_local * head_dim :].reshape(block_len, kv_local, 2 * head_dim)
    rotated = rotate(key_val[:, :, :head_dim], angle_pos).astype(jnp.bfloat16)
    stored = jnp.concatenate([rotated, key_val[:, :, head_dim:].astype(jnp.bfloat16)], axis=2)
    seam_rows = passed_along(stored[block_len - seg_most :], "grp", 1)
    window = jnp.concatenate([seam_rows, stored], axis=0)
    scale_qk = head_dim ** (-0.5)
    local_rows = jnp.arange(block_len, dtype=jnp.int32)
    lowest = local_rows - jnp.maximum(positions, 0)
    pieces_out = []
    for q_block in range(2):
        first_row = q_block * seg_most
        rows_here = first_row + jnp.arange(seg_most, dtype=jnp.int32)
        cols_here = first_row - seg_most + jnp.arange(2 * seg_most, dtype=jnp.int32)
        low_here = lowest[first_row : first_row + seg_most]
        visible = (cols_here[None, :] >= low_here[:, None]) & (
            cols_here[None, :] <= rows_here[:, None]
        )
        query_blk = queries[first_row : first_row + seg_most].reshape(
            seg_most, kv_local, per_kv, head_dim
        )
        keys_blk = window[first_row : first_row + 2 * seg_most, :, :head_dim]
        vals_blk = window[first_row : first_row + 2 * seg_most, :, head_dim:]
        mixed_rows = attend_rows(query_blk, keys_blk, vals_blk, visible, scale_qk)
        pieces_out.append(mixed_rows.reshape(seg_most, q_local * head_dim).astype(jnp.bfloat16))
    attended = jnp.concatenate(pieces_out, axis=0)
    slots_dev = kv_cache.shape[0]
    capc = 2 * block_len // group_count
    live_slot = cache_slot >= 0
    owners = jnp.where(live_slot, cache_slot // slots_dev, group_count)
    owner_hit = (owners[:, None] == jnp.arange(group_count, dtype=jnp.int32)[None, :]).astype(
        jnp.bfloat16
    )
    lower_tri = (local_rows[:, None] >= local_rows[None, :]).astype(jnp.bfloat16)
    running = jnp.dot(lower_tri, owner_hit, preferred_element_type=jnp.float32)
    owner_rank = jnp.sum(running * owner_hit.astype(jnp.float32), axis=1).astype(jnp.int32) - 1
    send_rows = jnp.where(live_slot, owners * capc + owner_rank, group_count * capc)
    outgoing_cache = (
        jnp.zeros((group_count * capc, kv_local, 2 * head_dim), jnp.bfloat16)
        .at[send_rows]
        .set(stored, mode="drop")
    )
    outgoing_slots = (
        jnp.full((group_count * capc,), -1, jnp.int32)
        .at[send_rows]
        .set(cache_slot % slots_dev, mode="drop")
    )
    arrived, arrived_slots = (
        lax.all_to_all(
            outgoing_cache.reshape(group_count, capc, kv_local, 2 * head_dim),
            "grp",
            split_axis=0,
            concat_axis=0,
            tiled=True,
        ),
        lax.all_to_all(
            outgoing_slots.reshape(group_count, capc),
            "grp",
            split_axis=0,
            concat_axis=0,
            tiled=True,
        ),
    )
    flat_slots = arrived_slots.reshape(group_count * capc)
    write_rows = jnp.where(flat_slots >= 0, flat_slots, slots_dev).astype(jnp.int32)
    cache_after = kv_cache.at[write_rows].set(
        arrived.reshape(group_count * capc, kv_local, 2 * head_dim), mode="drop"
    )
    by_token = lax.all_to_all(attended, "hd", split_axis=0, concat_axis=1, tiled=True)
    attn_proj = jnp.dot(
        by_token,
        lax.all_gather(w_out, "grp", axis=1, tiled=True),
        preferred_element_type=jnp.float32,
    )
    residual = (tokens.astype(jnp.float32) + attn_proj).astype(jnp.bfloat16)
    moe_in = rms_norm(residual, moe_gain)
    logits = jnp.dot(moe_in, router, preferred_element_type=jnp.float32)
    expert_range = jnp.arange(router.shape[1], dtype=jnp.int32)
    matches_all = expert_ids[:, :, None] == expert_range[None, None, :]
    chosen = jnp.sum(jnp.where(matches_all, logits[:, None, :], 0.0), axis=2)
    raised = jnp.exp(chosen)
    gates = raised / jnp.sum(raised, axis=1, keepdims=True)
    live_range = jnp.arange(lane_count, dtype=jnp.int32)
    matches = expert_ids[:, :, None] == live_range[None, None, :]
    member = jnp.any(matches, axis=1)
    weighting = jnp.sum(jnp.where(matches, gates[:, :, None], 0.0), axis=1)
    ranking = jnp.cumsum(member.astype(jnp.int32), axis=0) - 1
    target = jnp.where(member, live_range[None, :] * expert_cap + ranking, -1)
    slot_range = jnp.arange(lane_count * expert_cap, dtype=jnp.int32)
    slot_hits = target[None, :, :] == slot_range[:, None, None]
    placing = jnp.any(slot_hits, axis=2).astype(jnp.bfloat16)
    outgoing = (
        jnp.dot(placing, moe_in, preferred_element_type=jnp.float32)
        .astype(jnp.bfloat16)
        .reshape(lane_count, expert_cap, model_width)
    )
    gate_up_all, down_all = (
        lax.all_gather(w_gate_up, "grp", axis=1, tiled=True),
        lax.all_gather(w_down, "grp", axis=1, tiled=True),
    )
    gate_up_mat = gate_up_all[0]
    down_mat = down_all[0]
    landed = lax.all_to_all(outgoing, "hd", split_axis=0, concat_axis=0, tiled=True)
    results = expert_rows(landed.reshape(-1, model_width), gate_up_mat, down_mat).reshape(landed.shape)
    returned = lax.all_to_all(results, "hd", split_axis=0, concat_axis=0, tiled=True)
    flat_returned = returned.reshape(-1, model_width)
    fetched = flat_returned[jnp.maximum(target, 0)]
    used_weight = jnp.where(member, weighting, 0.0)
    moe_total = jnp.sum(used_weight[:, :, None] * fetched.astype(jnp.float32), axis=1)
    layer_out = (residual.astype(jnp.float32) + moe_total).astype(jnp.bfloat16)
    return (layer_out, cache_after)


def solution(mesh):
    two_lanes = mesh.shape["hd"] == 2 and mesh.shape["grp"] % 8 == 0
    return jax.shard_map(
        two_lane_shards if two_lanes else shards,
        mesh=mesh,
        in_specs=(
            P(("grp", "hd"), None),
            P("grp"),
            P(),
            P(None, "hd"),
            P(None, "hd", None),
            P(None, "grp"),
            P(),
            P(),
            P("hd", "grp", None),
            P("hd", "grp", None),
            P(("grp", "hd"), None),
            P("grp"),
            P("grp", "hd", None),
        ),
        out_specs=(P(("grp", "hd"), None), P("grp", "hd", None)),
        check_vma=False,
    )
```

```python
import functools

import jax
import jax.numpy as jnp
import numpy as np
from jax import lax
from jax.experimental import pallas as pl
from jax.experimental.pallas import tpu as pltpu
from jax.sharding import PartitionSpec as P

norm_eps = 1e-05
rope_base = 10000.0
bf16 = jnp.bfloat16
f32 = jnp.float32
LAST_DIMS = (((1,), (1,)), ((), ()))


def ring_cycle(groups):
    rows = groups // 4
    return [2 * r for r in range(rows)] + [2 * r + 1 for r in reversed(range(rows))]


def ring_pairs(groups):
    cycle = ring_cycle(groups)
    count = len(cycle)
    pairs = []
    for place, pair in enumerate(cycle):
        pairs.append((2 * pair, 2 * cycle[(place + 1) % count]))
        pairs.append((2 * pair + 1, 2 * cycle[(place - 1) % count] + 1))
    return pairs


def sibling_pairs(groups):
    return [(g, g ^ 1) for g in range(groups)]


def ring_sources(groups, me):
    count = groups // 2
    rows = count // 2
    side, pair = me % 2, me // 2
    row, col = pair // 2, pair % 2
    place = jnp.where(col == 0, row, count - 1 - row)

    def block(core, steps):
        there = (place + (2 * core - 1) * steps + count) % count
        other = jnp.where(there < rows, 2 * there, 2 * (count - 1 - there) + 1)
        return [2 * other + core, 2 * other + 1 - core]

    full = (count - 1) // 2
    listed = [me, me + 1 - 2 * side]
    for core in (side, 1 - side):
        for steps in range(1, full + 1):
            listed += block(core, steps)
    return listed + [block(side, count // 2)[0], block(1 - side, count // 2)[0]]


class Ring:
    def __init__(self, pair, groups):
        self.across = functools.partial(lax.ppermute, axis_name="grp", perm=ring_pairs(groups))
        self.beside = functools.partial(lax.ppermute, axis_name="grp", perm=sibling_pairs(groups))
        self.full = (groups // 2 - 1) // 2
        self.unit_rows = pair.shape[0] // 2
        self.mine = [pair]
        self.near = []

    def step(self):
        held = self.mine[-1]
        if len(self.mine) > self.full:
            held = held[: self.unit_rows]
        self.mine.append(self.across(held))

    def pin(self, *others):
        done = lax.optimization_barrier((self.mine[-1],) + others)
        self.mine[-1] = done[0]
        return done[1:] if len(others) > 1 else done[1]

    def share(self, upto=None):
        for index in range(1 + len(self.near), 1 + (upto or len(self.mine) - 1)):
            self.near.append(self.beside(self.mine[index]))

    def parts(self):
        full = self.full
        return self.mine[: full + 1] + self.near[:full] + [self.mine[full + 1], self.near[full]]

    def split(self):
        full = self.full
        listed = [(part, 2 * index) for index, part in enumerate(self.parts()[:-1])]
        listed.append((self.near[full], 4 * full + 3))
        late = (full, 2 * full, 2 * full + 1, 2 * full + 2)
        return (
            [pair for index, pair in enumerate(listed) if index not in late],
            [listed[index] for index in late],
        )


def place_parts(groups, parts, unit_rows, pieces, shards=None):
    sources = ring_sources(groups, lax.axis_index("grp"))
    shard = 0
    for index, part in enumerate(parts):
        shard = shards[index] if shards else shard
        for unit in range(part.shape[0] // unit_rows):
            for first, rows, target, lane in pieces:
                at = pl.multiple_of(sources[shard] * rows, rows)
                start = unit * unit_rows + first
                target[pl.ds(at, rows), lane : lane + part.shape[1]] = part[start : start + rows, :]
            shard += 1


VMEM = pl.BlockSpec(memory_space=pltpu.VMEM)
ANY = pl.BlockSpec(memory_space=pl.ANY)
HBM = pl.BlockSpec(memory_space=pltpu.HBM)
PARAMS = pltpu.CompilerParams(vmem_limit_bytes=16 << 20)


LITTLE = pl.CostEstimate(flops=1, bytes_accessed=1, transcendentals=0)


def takes(us):
    return pl.CostEstimate(
        flops=int(us * 1.15e9), bytes_accessed=int(us * 8e6), transcendentals=0
    )


def reads(nbytes):
    return pl.CostEstimate(flops=1, bytes_accessed=nbytes, transcendentals=0)


def normalized(floats, gain):
    factor = lax.rsqrt(jnp.mean(floats * floats, axis=-1, keepdims=True) + norm_eps)
    return (floats * factor * gain).astype(bf16)


def fetch(pairs, sems):
    copies = []
    for index, (source, target) in enumerate(pairs):
        copies.append(pltpu.make_async_copy(source, target, sems.at[index]))
        copies[-1].start()
    return copies


def pack_kernel(*refs):
    sources, (expert_pair, out_pair, sems) = refs[:6], refs[6:]
    width = expert_pair.shape[1]
    lane = lax.axis_index("hd")
    first = pl.multiple_of(lane * out_pair.shape[1], out_pair.shape[1])
    pairs = []
    row = 0
    for index in range(2):
        up, down, w_out = sources[3 * index : 3 * index + 3]
        count = w_out.shape[0]
        pairs.append(
            (w_out.at[:, pl.ds(first, out_pair.shape[1])], out_pair.at[pl.ds(index * count, count), :])
        )
        for source in (up, down):
            for at in range(0, source.shape[1], width):
                pairs.append(
                    (source.at[:, pl.ds(at, width)], expert_pair.at[pl.ds(row, source.shape[0]), :])
                )
                row += source.shape[0]
    for copy in fetch(pairs, sems):
        copy.wait()


def pack(own, beside):
    own = [pltpu.with_memory_space_constraint(part, pltpu.HBM) for part in own]
    up, down, w_out_t = own
    width = up.shape[1] // 2
    pieces = [up.shape[1] // width, down.shape[1] // width]
    unit_rows = pieces[0] * up.shape[0] + pieces[1] * down.shape[0]
    return pl.pallas_call(
        pack_kernel,
        out_shape=(
            jax.ShapeDtypeStruct((2 * unit_rows, width), bf16),
            jax.ShapeDtypeStruct((2 * w_out_t.shape[0], w_out_t.shape[1] // 2), bf16),
        ),
        in_specs=[ANY] * 6,
        out_specs=(ANY, ANY),
        scratch_shapes=[pltpu.SemaphoreType.DMA((2 + 2 * sum(pieces),))],
        compiler_params=PARAMS,
        cost_estimate=LITTLE,
        name="pack",
    )(*own, *beside)


def as_column(row, eye):
    return jnp.sum(jnp.where(eye, row, 0.0), axis=1, keepdims=True)


def named_experts(ids, experts):
    tokens = ids.shape[1]
    expert = lax.broadcasted_iota(jnp.int32, (experts, tokens), 0)
    hit = jnp.zeros((experts, tokens), f32)
    for index in range(ids.shape[0]):
        hit = jnp.where(ids[index : index + 1, :] == expert, 1.0, hit)
    return hit


def prepare_kernel(groups, slots_dev, *refs):
    sources, (cosine, sine, past, place, send, tags, gain) = refs[:4], refs[4:11]
    positions, slots, ids, flat_gain, sems = refs[11:]
    copies = fetch(list(zip(sources, (positions, slots, ids, flat_gain))), sems)
    for copy in copies:
        copy.wait()
    gain[...] = flat_gain[...].reshape(gain.shape)
    lane = lax.axis_index("hd")
    block = positions.shape[1]

    def iota(shape, dim):
        return lax.broadcasted_iota(jnp.int32, shape, dim)

    eye = iota((block, block), 0) == iota((block, block), 1)
    reach = as_column(jnp.maximum(positions[...], 0).astype(f32), eye)
    past[...] = jnp.broadcast_to(reach, past.shape)
    column = iota((8, 128), 1)
    exponent = (column % 32).astype(f32) * (-2.0 / 64)
    inverse_freq = jnp.exp(exponent * np.float32(np.log(rope_base)))[:1, :]
    angles = reach * inverse_freq
    cosine[...] = jnp.cos(angles)
    turned = jnp.sin(angles)
    sine[...] = jnp.where(iota(angles.shape, 1) % 64 < 32, -turned, turned)

    tokens = ids.shape[1]
    cap = place.shape[0] // 2
    hit = named_experts(ids, 8)
    upto = (iota((tokens, tokens), 0) <= iota((tokens, tokens), 1)).astype(f32)
    rank = jnp.dot(hit, upto, preferred_element_type=f32) - 1.0
    slot = iota((2 * cap, tokens), 0).astype(f32)
    placed = jnp.zeros((2 * cap, tokens), f32)
    for live in range(2):
        order = jnp.where(lane == live, 0, cap).astype(f32)
        member = hit[live : live + 1, :] > 0.0
        placed = jnp.where(member & (slot == rank[live : live + 1, :] + order), 1.0, placed)
    place[...] = placed.astype(bf16)

    where = slots[...]
    owner = jnp.where(where >= 0, where // slots_dev, -1)
    owner_hit = (iota((groups, block), 0) == owner).astype(f32)
    before = (iota((block, block), 0) <= iota((block, block), 1)).astype(f32)
    running = jnp.dot(owner_hit, before, preferred_element_type=f32)
    owner_rank = jnp.sum(owner_hit * running, axis=0, keepdims=True) - 1.0
    capc = send.shape[0] // groups
    row = jnp.where(owner >= 0, owner * capc + owner_rank.astype(jnp.int32), -1)
    send[...] = (iota(send.shape, 0) == row).astype(bf16)
    inside = jnp.where(where >= 0, where % slots_dev, 0)
    high = as_column((inside // 64 + 1).astype(f32), eye)
    low = as_column((inside % 64).astype(f32), eye)
    spot = iota(tags.shape, 1)
    tags[...] = jnp.where(spot == 0, high, jnp.where(spot == 1, low, 0.0)).astype(bf16)


def prepare(groups, slots_dev, positions, slots, ids, gain):
    block, tokens = positions.shape[0], ids.shape[0]
    model = gain.shape[0]
    cap = tokens // 4
    capc = 2 * block // groups
    shapes = [
        ((block, 128), f32),
        ((block, 128), f32),
        ((block, 128), f32),
        ((2 * cap, tokens), bf16),
        ((groups * capc, block), bf16),
        ((block, 128), bf16),
        ((1, model), f32),
    ]
    sources = (positions[None], slots[None], ids.T, gain)
    return pl.pallas_call(
        functools.partial(prepare_kernel, groups, slots_dev),
        out_shape=tuple(jax.ShapeDtypeStruct(shape, kind) for shape, kind in shapes),
        in_specs=[ANY] * 4,
        out_specs=(VMEM,) * len(shapes),
        scratch_shapes=[
            pltpu.VMEM((1, block), jnp.int32),
            pltpu.VMEM((1, block), jnp.int32),
            pltpu.VMEM(ids.shape[::-1], jnp.int32),
            pltpu.VMEM((model,), f32),
            pltpu.SemaphoreType.DMA((4,)),
        ],
        compiler_params=PARAMS,
        cost_estimate=LITTLE,
        name="prepare",
    )(*[pltpu.with_memory_space_constraint(source, pltpu.HBM) for source in sources])


def project_kernel(
    own, other, gain, cosine, sine, w_query, w_keyval, q_out, kv_out, seam_out, raw, rows, sems
):
    count = own.shape[0]
    lane = lax.axis_index("hd")
    mine = pl.multiple_of(lane * count, count)
    theirs = pl.multiple_of((1 - lane) * count, count)
    copies = fetch([(own, raw.at[0]), (other, raw.at[1])], sems)
    cos_q, sin_q = cosine[...], sine[...]
    column = lax.broadcasted_iota(jnp.int32, cos_q.shape, 1)
    lower = column % 64 < 32
    cos_kv = jnp.where(column < 64, cos_q, 1.0)
    sin_kv = jnp.where(column < 64, sin_q, 0.0)
    for index, first in ((0, mine), (1, theirs)):
        copies[index].wait()
        rows[pl.ds(first, count), :] = normalized(raw[index].astype(f32), gain[...])
    width = 256
    for weights, out, cos, sin in ((w_keyval, kv_out, cos_kv, sin_kv), (w_query, q_out, cos_q, sin_q)):
        for first in range(0, weights.shape[1], width):
            made = jnp.dot(rows[...], weights[:, first : first + width], preferred_element_type=f32)
            for part in range(0, width, 128):
                here = made[:, part : part + 128]
                turned = jnp.where(lower, pltpu.roll(here, 96, 1), pltpu.roll(here, 32, 1))
                done = (here * cos + turned * sin).astype(bf16)
                out[:, first + part : first + part + 128] = done
                if out is kv_out:
                    seam_out[:, first + part : first + part + 128] = done[count:, :]


def project(own, other, gain, cosine, sine, w_query, flat_kv):
    count, width = own.shape
    made = w_query.shape[1] + flat_kv.shape[1]
    return pl.pallas_call(
        project_kernel,
        out_shape=(
            jax.ShapeDtypeStruct((2 * count, w_query.shape[1]), bf16),
            jax.ShapeDtypeStruct((2 * count, flat_kv.shape[1]), bf16),
            jax.ShapeDtypeStruct((count, flat_kv.shape[1]), bf16),
        ),
        in_specs=[ANY] * 2 + [VMEM] * 5,
        out_specs=(VMEM, VMEM, VMEM),
        scratch_shapes=[
            pltpu.VMEM((2, count, width), bf16),
            pltpu.VMEM((2 * count, width), bf16),
            pltpu.SemaphoreType.DMA((2,)),
        ],
        compiler_params=PARAMS,
        cost_estimate=takes(8),
        name="project",
    )(own, other, gain, cosine, sine, w_query, flat_kv)


def attend_rows_kernel(first, q, kv, seam, past, mixed, window, sem):
    count = q.shape[0] // 2
    if first == 0:
        copy = pltpu.make_async_copy(seam, window.at[pl.ds(0, count), :], sem)
        copy.start()
        window[count:, :] = kv[:count, :]
        copy.wait()
        keyed = window
    else:
        keyed = kv
    head = 64
    kv_heads = kv.shape[1] // (2 * head)
    per_kv = q.shape[1] // head // kv_heads
    shape = (count, 2 * count)
    row = lax.broadcasted_iota(jnp.int32, shape, 0) + count
    col = lax.broadcasted_iota(jnp.int32, shape, 1)
    reach = past[first : first + count, :1].astype(jnp.int32)
    visible = (col <= row) & (col >= row - reach)
    for kv_head in range(kv_heads):
        lanes = 2 * head * kv_head
        keys = keyed[:, lanes : lanes + head]
        values = keyed[:, lanes + head : lanes + 2 * head]
        for index in range(per_kv):
            at = (kv_head * per_kv + index) * head
            query = q[first : first + count, at : at + head]
            scores = lax.dot_general(query, keys, LAST_DIMS, preferred_element_type=f32)
            raised = jnp.where(visible, jnp.exp(scores * head ** (-0.5)), 0.0)
            probs = (raised / jnp.sum(raised, axis=-1, keepdims=True)).astype(bf16)
            made = jnp.dot(probs, values, preferred_element_type=f32)
            mixed[:, at : at + head] = made.astype(bf16)


def attend_late(q, kv, past):
    def kernel(q, kv, past, mixed):
        attend_rows_kernel(q.shape[0] // 2, q, kv, None, past, mixed, None, None)

    return pl.pallas_call(
        kernel,
        out_shape=jax.ShapeDtypeStruct((q.shape[0] // 2, q.shape[1]), bf16),
        in_specs=[VMEM] * 3,
        out_specs=VMEM,
        compiler_params=PARAMS,
        cost_estimate=takes(2),
        name="attend_late",
    )(q, kv, past)


def attend_early(q, kv, seam, past):
    return pl.pallas_call(
        functools.partial(attend_rows_kernel, 0),
        out_shape=jax.ShapeDtypeStruct((q.shape[0] // 2, q.shape[1]), bf16),
        in_specs=[VMEM, VMEM, ANY, VMEM],
        out_specs=VMEM,
        scratch_shapes=[pltpu.VMEM(kv.shape, bf16), pltpu.SemaphoreType.DMA],
        compiler_params=PARAMS,
        cost_estimate=takes(2),
        name="attend_early",
    )(q, kv, seam, past)


def outward_rows(flip, groups, unit_rows, early, late, parts, w_out, rows):
    place_parts(groups, parts, unit_rows, [(0, unit_rows, w_out, 0)])
    lane = lax.axis_index("hd")
    which = (1 - lane) if flip else lane

    @pl.when(which == 0)
    def _():
        rows[...] = early[...]

    @pl.when(which != 0)
    def _():
        rows[...] = late[...]

    return lax.dot_general(rows[...], w_out[...], LAST_DIMS, preferred_element_type=f32)


def send_kernel(groups, unit_rows, n_parts, early, late, *refs):
    parts, (out, w_out, rows) = refs[:n_parts], refs[n_parts:]
    out[...] = outward_rows(True, groups, unit_rows, early, late, parts, w_out, rows).astype(bf16)


def keep_kernel(groups, unit_rows, n_parts, early, late, tokens, *refs):
    parts, (out, w_out, rows) = refs[:n_parts], refs[n_parts:]
    made = outward_rows(False, groups, unit_rows, early, late, parts, w_out, rows)
    out[...] = tokens[...].astype(f32) + made


def outward_send(groups, early, late, parts, unit_rows):
    width, depth = groups * unit_rows, parts[0].shape[1]
    return pl.pallas_call(
        functools.partial(send_kernel, groups, unit_rows, len(parts)),
        out_shape=jax.ShapeDtypeStruct((early.shape[0], width), bf16),
        in_specs=[VMEM] * (2 + len(parts)),
        out_specs=VMEM,
        scratch_shapes=[pltpu.VMEM((width, depth), bf16), pltpu.VMEM(early.shape, bf16)],
        compiler_params=PARAMS,
        cost_estimate=reads(2 * width * depth),
        name="outward_send",
    )(early, late, *parts)


def outward_keep(groups, early, late, tokens, parts, unit_rows):
    width, depth = groups * unit_rows, parts[0].shape[1]
    return pl.pallas_call(
        functools.partial(keep_kernel, groups, unit_rows, len(parts)),
        out_shape=jax.ShapeDtypeStruct(tokens.shape, f32),
        in_specs=[VMEM] * (3 + len(parts)),
        out_specs=VMEM,
        scratch_shapes=[
            pltpu.VMEM((width, depth), bf16),
            pltpu.VMEM(early.shape, bf16),
        ],
        compiler_params=PARAMS,
        cost_estimate=reads(2 * width * depth),
        name="outward_keep",
    )(early, late, tokens, *parts)


def route_kernel(mine, arrived, flat_gain, place, residual, moe_in, sent, gain, gain_sem):
    copy = pltpu.make_async_copy(flat_gain, gain, gain_sem)
    copy.start()
    added = (mine[...] + arrived[...].astype(f32)).astype(bf16)
    residual[...] = added
    copy.wait()
    moe_in[...] = normalized(added.astype(f32), gain[...].reshape(1, gain.shape[0]))
    cap = sent.shape[0]
    rows = jnp.dot(place[cap:, :], moe_in[...], preferred_element_type=f32)
    sent[...] = rows.astype(bf16)


def route(mine, arrived, flat_gain, place):
    cap = place.shape[0] // 2
    return pl.pallas_call(
        route_kernel,
        out_shape=(
            jax.ShapeDtypeStruct(mine.shape, bf16),
            jax.ShapeDtypeStruct(mine.shape, bf16),
            jax.ShapeDtypeStruct((cap, mine.shape[1]), bf16),
        ),
        in_specs=[VMEM, VMEM, ANY, VMEM],
        out_specs=(VMEM,) * 3,
        scratch_shapes=[pltpu.VMEM(flat_gain.shape, f32), pltpu.SemaphoreType.DMA],
        compiler_params=PARAMS,
        cost_estimate=reads(16 << 20),
        name="route",
    )(mine, arrived, pltpu.with_memory_space_constraint(flat_gain, pltpu.HBM), place)


def expert_pieces(gate_up, down, up_rows, down_rows, width):
    pieces = [(i * up_rows, up_rows, gate_up, i * width) for i in range(2)]
    pieces += [
        (2 * up_rows + i * down_rows, down_rows, down, i * width) for i in range(down.shape[1] // width)
    ]
    return pieces, pieces[-1][0] + down_rows


def gate_kernel(groups, up_rows, down_rows, shards, moe_in, router_in, ids_in, place, *refs):
    parts, (gates, own, spread, gate_up, down, router, ids, sems, part_sems) = (
        refs[: len(shards)],
        refs[len(shards) :],
    )
    small = fetch([(router_in, router), (ids_in, ids)], sems)
    width = parts[0].shape[1]
    pieces, unit_rows = expert_pieces(gate_up, down, up_rows, down_rows, width)
    sources = ring_sources(groups, lax.axis_index("grp"))
    pairs = []
    for part, shard in zip(parts, shards):
        for unit in range(part.shape[0] // unit_rows):
            for first, rows, target, lane in pieces:
                at = pl.multiple_of(sources[shard + unit] * rows, rows)
                pairs.append(
                    (
                        part.at[pl.ds(unit * unit_rows + first, rows), :],
                        target.at[pl.ds(at, rows), pl.ds(lane, width)],
                    )
                )
    copies = fetch(pairs, part_sems)
    cap = own.shape[0]
    own[...] = jnp.dot(place[:cap, :], moe_in[...], preferred_element_type=f32).astype(bf16)
    tokens = ids.shape[1]
    row = lax.broadcasted_iota(jnp.int32, (tokens, tokens), 0)
    eye = (row == lax.broadcasted_iota(jnp.int32, (tokens, tokens), 1)).astype(f32)
    spread[...] = lax.dot_general(
        eye.astype(bf16), place[...], LAST_DIMS, preferred_element_type=f32
    ).astype(bf16)
    for copy in small:
        copy.wait()
    hit = named_experts(ids, router.shape[0])
    named = lax.dot_general(eye, hit, LAST_DIMS, preferred_element_type=f32)
    logits = lax.dot_general(moe_in[...], router[...], LAST_DIMS, preferred_element_type=f32)
    raised = jnp.where(named > 0, jnp.exp(logits), 0.0)
    gates[...] = raised / jnp.sum(raised, axis=-1, keepdims=True)
    for copy in copies:
        copy.wait()


def gate(groups, moe_in, router_t, ids_t, place, early, up_rows, down_rows):
    cap = place.shape[0] // 2
    tokens, model = moe_in.shape
    width = early[0][0].shape[1]
    units = 2 * len(early)
    far = [pltpu.with_memory_space_constraint(part, pltpu.HBM) for part in (router_t, ids_t)]
    return pl.pallas_call(
        functools.partial(gate_kernel, groups, up_rows, down_rows, [shard for _, shard in early]),
        out_shape=(
            jax.ShapeDtypeStruct((tokens, router_t.shape[0]), f32),
            jax.ShapeDtypeStruct((cap, model), bf16),
            jax.ShapeDtypeStruct(place.shape[::-1], bf16),
            jax.ShapeDtypeStruct((groups * up_rows, 2 * width), bf16),
            jax.ShapeDtypeStruct((groups * down_rows, model), bf16),
        ),
        in_specs=[VMEM, ANY, ANY, VMEM] + [ANY] * len(early),
        out_specs=(VMEM,) * 5,
        scratch_shapes=[
            pltpu.VMEM(router_t.shape, bf16),
            pltpu.VMEM(ids_t.shape, jnp.int32),
            pltpu.SemaphoreType.DMA((2,)),
            pltpu.SemaphoreType.DMA((units * (2 + model // width),)),
        ],
        compiler_params=PARAMS,
        cost_estimate=LITTLE,
        name="gate",
    )(moe_in, *far, place, *[part for part, _ in early])


def expert_kernel(groups, up_rows, down_rows, shards, own, other, gate_up_in, down_in, *refs):
    parts = refs[: len(shards)]
    own_out, other_out, gate_up, down, rows = refs[len(shards) :]
    width = parts[0].shape[1]
    count = own.shape[0]
    rows[:count, :] = own[...]
    rows[count:, :] = other[...]
    pieces, unit_rows = expert_pieces(gate_up, down, up_rows, down_rows, width)
    place_parts(groups, parts, unit_rows, pieces, shards)
    both = jnp.dot(rows[...], gate_up[...], preferred_element_type=f32)
    gate, up = both[:, :width], both[:, width:]
    hidden = (gate / (1.0 + jnp.exp(-gate)) * up).astype(bf16)
    made = jnp.dot(hidden, down[...], preferred_element_type=f32).astype(bf16)
    own_out[...] = made[:count, :]
    other_out[...] = made[count:, :]


def expert(groups, own, other, staged, late, up_rows, down_rows):
    count, model = own.shape
    width = late[0][0].shape[1]
    return pl.pallas_call(
        functools.partial(expert_kernel, groups, up_rows, down_rows, [shard for _, shard in late]),
        out_shape=(jax.ShapeDtypeStruct(own.shape, bf16),) * 2
        + tuple(jax.ShapeDtypeStruct(part.shape, bf16) for part in staged),
        in_specs=[VMEM] * (4 + len(late)),
        out_specs=(VMEM,) * 4,
        scratch_shapes=[pltpu.VMEM((2 * count, model), bf16)],
        input_output_aliases={2: 2, 3: 3},
        compiler_params=PARAMS,
        cost_estimate=pl.CostEstimate(flops=int(2.2 * 1.15e9), bytes_accessed=1, transcendentals=0),
        name="expert",
    )(own, other, *staged, *[part for part, _ in late])[:2]


def combine_kernel(residual, gates, spread, own, returned, out):
    lane = lax.axis_index("hd")
    count = own.shape[0]
    column = lax.broadcasted_iota(jnp.int32, gates.shape, 1)
    total = jnp.zeros(residual.shape, f32)
    for index, made in ((0, own), (1, returned)):
        live = lane if index == 0 else 1 - lane
        weight = jnp.sum(jnp.where(column == live, gates[...], 0.0), axis=-1, keepdims=True)
        picked = jnp.dot(
            spread[:, index * count : (index + 1) * count], made[...], preferred_element_type=f32
        )
        total += weight * picked
    out[...] = (residual[...].astype(f32) + total).astype(bf16)


def combine(residual, gates, spread, own, returned):
    return pl.pallas_call(
        combine_kernel,
        out_shape=jax.ShapeDtypeStruct(residual.shape, bf16),
        in_specs=[VMEM] * 5,
        out_specs=VMEM,
        compiler_params=PARAMS,
        cost_estimate=reads(6 * residual.shape[0] * residual.shape[1]),
        name="combine",
    )(residual, gates, spread, own, returned)


def bundle_kernel(send, kv, tags, result, out, sem):
    groups, rows, _ = out.shape
    heads = kv.shape[1] // 128
    capc = send.shape[0] // groups
    packed = jnp.dot(send[...], kv[...], preferred_element_type=f32).astype(bf16)
    tagged = jnp.dot(send[...], tags[...], preferred_element_type=f32)
    one = (lax.broadcasted_iota(jnp.int32, (16, 128), 0) == lax.broadcasted_iota(jnp.int32, (16, 128), 1))
    for owner in range(groups):
        mine = slice(owner * capc, (owner + 1) * capc)
        for head in range(heads):
            out[owner, head * capc : (head + 1) * capc, :] = packed[mine, head * 128 : (head + 1) * 128]
        wide = jnp.concatenate([tagged[mine, :], jnp.zeros((128 - capc, 128), f32)], axis=0)
        out[owner, heads * capc :, :] = lax.dot_general(
            one.astype(f32), wide, LAST_DIMS, preferred_element_type=f32
        ).astype(bf16)
    copy = pltpu.make_async_copy(out, result, sem)
    copy.start()
    copy.wait()


def bundle(groups, send, kv, tags):
    rows = send.shape[0] // groups * (kv.shape[1] // 128) + 16
    return pl.pallas_call(
        bundle_kernel,
        out_shape=pltpu.HBM((groups, rows, 128), bf16),
        in_specs=[VMEM] * 3,
        out_specs=HBM,
        scratch_shapes=[pltpu.VMEM((groups, rows, 128), bf16), pltpu.SemaphoreType.DMA],
        compiler_params=PARAMS,
        cost_estimate=LITTLE,
        name="bundle",
    )(send, kv, tags)


def write_kernel(heads, arrived, cache, out, rows, wide, known):
    groups, size, _ = arrived.shape
    slots = cache.shape[0] // heads
    capc = (size - 16) // heads
    high, low = [], []
    for source in range(groups):
        for head in range(heads):
            rows[source * capc : (source + 1) * capc, head * 128 : (head + 1) * 128] = arrived[
                source, head * capc : (head + 1) * capc, :
            ]
        numbers = arrived[source, heads * capc :, :].astype(f32)
        high.append(numbers[0:1, :capc])
        low.append(numbers[1:2, :capc])
    slot = jnp.concatenate(high, axis=1) * 64.0 + jnp.concatenate(low, axis=1) - 64.0
    row = lax.broadcasted_iota(jnp.int32, (slots, slot.shape[1]), 0).astype(f32)
    hit = (row == slot).astype(bf16)
    made = jnp.dot(hit, rows[...], preferred_element_type=f32)
    found = jnp.dot(hit, jnp.ones((slot.shape[1], 128), bf16), preferred_element_type=f32)
    for head in range(heads):
        wide[pl.ds(head, slots, heads), :] = made[:, head * 128 : (head + 1) * 128]
        known[pl.ds(head, slots, heads), :] = found
    old = cache[...].astype(f32)
    out[...] = jnp.where(known[...] > 0.0, wide[...], old).astype(bf16)


def write(arrived, cache):
    slots, heads, lanes = cache.shape
    capc = (arrived.shape[1] - 16) // heads
    flat = (slots * heads, lanes)
    written = pl.pallas_call(
        functools.partial(write_kernel, heads),
        out_shape=jax.ShapeDtypeStruct(flat, bf16),
        in_specs=[VMEM] * 2,
        out_specs=VMEM,
        scratch_shapes=[
            pltpu.VMEM((arrived.shape[0] * capc, heads * lanes), bf16),
            pltpu.VMEM(flat, f32),
            pltpu.VMEM(flat, f32),
        ],
        compiler_params=PARAMS,
        cost_estimate=reads(1 << 21),
        name="write",
    )(arrived, cache.reshape(flat))
    return written.reshape(cache.shape)


def two_lane_shards(
    tokens,
    positions,
    attn_gain,
    w_query,
    w_keyval,
    w_out,
    moe_gain,
    router,
    w_gate_up,
    w_down,
    expert_ids,
    cache_slot,
    kv_cache,
):
    groups = lax.axis_size("grp")
    tok_rows, model = tokens.shape
    block = positions.shape[0]
    kv_local, head2 = w_keyval.shape[1:]
    kv_width = kv_local * head2
    slots_dev = kv_cache.shape[0]
    swap = functools.partial(lax.ppermute, axis_name="hd", perm=[(0, 1), (1, 0)])

    together = lax.optimization_barrier

    other_tokens = swap(tokens)
    own = (w_gate_up[0], w_down[0], w_out.T)
    up_rows, down_rows = own[0].shape[0], own[1].shape[0]
    beside = [lax.ppermute(part, "grp", sibling_pairs(groups)) for part in own]
    expert_pair, out_pair = pack(own, beside)
    out_ring = Ring(out_pair, groups)
    out_ring.step()
    expert_ring = Ring(expert_pair, groups)
    expert_ring.step()
    w_keyval, positions = together((w_keyval, positions, out_pair))[:2]
    flat_kv = w_keyval.reshape(model, kv_width)
    cosine, sine, past, place, send, tags, gain = prepare(
        groups, slots_dev, positions, cache_slot, expert_ids, attn_gain
    )
    cosine, flat_kv = out_ring.pin(cosine, flat_kv)
    out_ring.step()

    q, kv, tail = project(tokens, other_tokens, gain, cosine, sine, w_query, flat_kv)
    seam = lax.ppermute(tail, "grp", [(g, g + 1) for g in range(groups - 1)])
    late = attend_late(q, kv, past)
    late = out_ring.pin(late)
    out_ring.step()
    out_ring.share(2)
    seam, late = together((seam, late))
    seam = expert_ring.pin(seam)
    expert_ring.step()
    early = attend_early(q, kv, seam, past)
    early, out_ring.near = together((early, out_ring.near))
    early = out_ring.pin(early)
    out_ring.step()
    out_ring.share(3)
    early, kv, out_ring.near = together((early, kv, out_ring.near))
    outgoing = bundle(groups, send, kv, tags)
    early, outgoing = together((early, outgoing))
    early = out_ring.pin(early)
    early = expert_ring.pin(early)
    expert_ring.step()
    out_ring.share()
    sent = outward_send(groups, early, late, out_ring.parts(), out_ring.unit_rows)
    arrived = swap(sent)
    early = together((early, sent))[0]
    mine = outward_keep(groups, early, late, tokens, out_ring.parts(), out_ring.unit_rows)
    mine = expert_ring.pin(mine)
    expert_ring.step()
    outgoing = together((outgoing, sent))[0]
    arrived_cache = lax.all_to_all(outgoing, "grp", split_axis=0, concat_axis=0, tiled=True)
    arrived, mine, expert_ring.mine[1:] = together((arrived, mine, expert_ring.mine[1:]))
    expert_ring.share()

    residual, moe_in, sent_rows = route(mine, arrived, moe_gain, place)
    landed = swap(sent_rows)
    parts_early, parts_late = expert_ring.split()
    gates, own_rows, spread, *staged = gate(
        groups, moe_in, router.T, expert_ids.T, place, parts_early, up_rows, down_rows
    )
    landed, own_rows = together((landed, own_rows))
    own_made, back = expert(groups, own_rows, landed, staged, parts_late, up_rows, down_rows)
    returned = swap(back)
    layer_out = combine(residual, gates, spread, own_made, returned)
    layer_out, arrived_cache = together((layer_out, arrived_cache))
    cache_after = write(arrived_cache, kv_cache)
    return (layer_out, cache_after)


def passed_along(value, axis, steps):
    count = lax.axis_size(axis)
    initial, last = (max(0, -steps), min(count, count - steps))
    return lax.ppermute(value, axis, [(source, source + steps) for source in range(initial, last)])


def rms_norm(row_set, norm_gain):
    floats = row_set.astype(jnp.float32)
    factor = lax.rsqrt(jnp.mean(floats * floats, axis=-1, keepdims=True) + norm_eps)
    return (floats * factor * norm_gain).astype(jnp.bfloat16)


def rotate(vectors, angle_pos):
    halves = vectors.shape[-1] // 2
    inverse_freq = rope_base ** (-2.0 * jnp.arange(halves, dtype=jnp.float32) / vectors.shape[-1])
    angles = angle_pos[:, None, None] * inverse_freq[None, None, :]
    cosine = jnp.cos(angles)
    sine_part = jnp.sin(angles)
    first_half = vectors[..., :halves]
    second_half = vectors[..., halves:]
    return jnp.concatenate(
        [
            first_half * cosine - second_half * sine_part,
            second_half * cosine + first_half * sine_part,
        ],
        axis=-1,
    )


def expert_rows(row_set, gate_up, down_rows):
    gate_and_up = jnp.dot(row_set, gate_up, preferred_element_type=jnp.float32)
    inner_width = gate_and_up.shape[1] // 2
    hidden = (jax.nn.silu(gate_and_up[:, :inner_width]) * gate_and_up[:, inner_width:]).astype(
        jnp.bfloat16
    )
    return jnp.dot(hidden, down_rows, preferred_element_type=jnp.float32).astype(jnp.bfloat16)


def attend_rows(query_blk, keys_blk, vals_blk, visible, scale_qk):
    scores = (
        jnp.einsum("qkgd,skd->kgqs", query_blk, keys_blk, preferred_element_type=jnp.float32)
        * scale_qk
    )
    weights_f = jnp.where(visible[None, None], jnp.exp(scores), 0.0)
    prob_bf = (weights_f / jnp.sum(weights_f, axis=-1, keepdims=True)).astype(jnp.bfloat16)
    return jnp.einsum("kgqs,skd->qkgd", prob_bf, vals_blk, preferred_element_type=jnp.float32)


def shards(
    tokens,
    positions,
    attn_gain,
    w_query,
    w_keyval,
    w_out,
    moe_gain,
    router,
    w_gate_up,
    w_down,
    expert_ids,
    cache_slot,
    kv_cache,
):
    lane_count = lax.axis_size("hd")
    group_count = lax.axis_size("grp")
    tok_rows = tokens.shape[0]
    model_width = tokens.shape[1]
    block_len = positions.shape[0]
    seg_most = block_len // 2
    head_dim = w_keyval.shape[2] // 2
    kv_local = w_keyval.shape[1]
    q_local = w_query.shape[1] // head_dim
    per_kv = q_local // kv_local
    expert_cap = tok_rows // 4
    normed = rms_norm(tokens, attn_gain)
    flat_kv = w_keyval.reshape(model_width, kv_local * 2 * head_dim)
    section = lax.all_gather(normed, "hd", axis=0, tiled=True)
    projected = jnp.concatenate(
        [
            jnp.dot(section, w_query, preferred_element_type=jnp.float32),
            jnp.dot(section, flat_kv, preferred_element_type=jnp.float32),
        ],
        axis=1,
    )
    angle_pos = jnp.maximum(positions, 0).astype(jnp.float32)
    queries = rotate(
        projected[:, : q_local * head_dim].reshape(block_len, q_local, head_dim), angle_pos
    ).astype(jnp.bfloat16)
    key_val = projected[:, q_local * head_dim :].reshape(block_len, kv_local, 2 * head_dim)
    rotated = rotate(key_val[:, :, :head_dim], angle_pos).astype(jnp.bfloat16)
    stored = jnp.concatenate([rotated, key_val[:, :, head_dim:].astype(jnp.bfloat16)], axis=2)
    seam_rows = passed_along(stored[block_len - seg_most :], "grp", 1)
    window = jnp.concatenate([seam_rows, stored], axis=0)
    scale_qk = head_dim ** (-0.5)
    local_rows = jnp.arange(block_len, dtype=jnp.int32)
    lowest = local_rows - jnp.maximum(positions, 0)
    pieces_out = []
    for q_block in range(2):
        first_row = q_block * seg_most
        rows_here = first_row + jnp.arange(seg_most, dtype=jnp.int32)
        cols_here = first_row - seg_most + jnp.arange(2 * seg_most, dtype=jnp.int32)
        low_here = lowest[first_row : first_row + seg_most]
        visible = (cols_here[None, :] >= low_here[:, None]) & (
            cols_here[None, :] <= rows_here[:, None]
        )
        query_blk = queries[first_row : first_row + seg_most].reshape(
            seg_most, kv_local, per_kv, head_dim
        )
        keys_blk = window[first_row : first_row + 2 * seg_most, :, :head_dim]
        vals_blk = window[first_row : first_row + 2 * seg_most, :, head_dim:]
        mixed_rows = attend_rows(query_blk, keys_blk, vals_blk, visible, scale_qk)
        pieces_out.append(mixed_rows.reshape(seg_most, q_local * head_dim).astype(jnp.bfloat16))
    attended = jnp.concatenate(pieces_out, axis=0)
    slots_dev = kv_cache.shape[0]
    capc = 2 * block_len // group_count
    live_slot = cache_slot >= 0
    owners = jnp.where(live_slot, cache_slot // slots_dev, group_count)
    owner_hit = (owners[:, None] == jnp.arange(group_count, dtype=jnp.int32)[None, :]).astype(
        jnp.bfloat16
    )
    lower_tri = (local_rows[:, None] >= local_rows[None, :]).astype(jnp.bfloat16)
    running = jnp.dot(lower_tri, owner_hit, preferred_element_type=jnp.float32)
    owner_rank = jnp.sum(running * owner_hit.astype(jnp.float32), axis=1).astype(jnp.int32) - 1
    send_rows = jnp.where(live_slot, owners * capc + owner_rank, group_count * capc)
    outgoing_cache = (
        jnp.zeros((group_count * capc, kv_local, 2 * head_dim), jnp.bfloat16)
        .at[send_rows]
        .set(stored, mode="drop")
    )
    outgoing_slots = (
        jnp.full((group_count * capc,), -1, jnp.int32)
        .at[send_rows]
        .set(cache_slot % slots_dev, mode="drop")
    )
    arrived, arrived_slots = (
        lax.all_to_all(
            outgoing_cache.reshape(group_count, capc, kv_local, 2 * head_dim),
            "grp",
            split_axis=0,
            concat_axis=0,
            tiled=True,
        ),
        lax.all_to_all(
            outgoing_slots.reshape(group_count, capc),
            "grp",
            split_axis=0,
            concat_axis=0,
            tiled=True,
        ),
    )
    flat_slots = arrived_slots.reshape(group_count * capc)
    write_rows = jnp.where(flat_slots >= 0, flat_slots, slots_dev).astype(jnp.int32)
    cache_after = kv_cache.at[write_rows].set(
        arrived.reshape(group_count * capc, kv_local, 2 * head_dim), mode="drop"
    )
    by_token = lax.all_to_all(attended, "hd", split_axis=0, concat_axis=1, tiled=True)
    attn_proj = jnp.dot(
        by_token,
        lax.all_gather(w_out, "grp", axis=1, tiled=True),
        preferred_element_type=jnp.float32,
    )
    residual = (tokens.astype(jnp.float32) + attn_proj).astype(jnp.bfloat16)
    moe_in = rms_norm(residual, moe_gain)
    logits = jnp.dot(moe_in, router, preferred_element_type=jnp.float32)
    expert_range = jnp.arange(router.shape[1], dtype=jnp.int32)
    matches_all = expert_ids[:, :, None] == expert_range[None, None, :]
    chosen = jnp.sum(jnp.where(matches_all, logits[:, None, :], 0.0), axis=2)
    raised = jnp.exp(chosen)
    gates = raised / jnp.sum(raised, axis=1, keepdims=True)
    live_range = jnp.arange(lane_count, dtype=jnp.int32)
    matches = expert_ids[:, :, None] == live_range[None, None, :]
    member = jnp.any(matches, axis=1)
    weighting = jnp.sum(jnp.where(matches, gates[:, :, None], 0.0), axis=1)
    ranking = jnp.cumsum(member.astype(jnp.int32), axis=0) - 1
    target = jnp.where(member, live_range[None, :] * expert_cap + ranking, -1)
    slot_range = jnp.arange(lane_count * expert_cap, dtype=jnp.int32)
    slot_hits = target[None, :, :] == slot_range[:, None, None]
    placing = jnp.any(slot_hits, axis=2).astype(jnp.bfloat16)
    outgoing = (
        jnp.dot(placing, moe_in, preferred_element_type=jnp.float32)
        .astype(jnp.bfloat16)
        .reshape(lane_count, expert_cap, model_width)
    )
    gate_up_all, down_all = (
        lax.all_gather(w_gate_up, "grp", axis=1, tiled=True),
        lax.all_gather(w_down, "grp", axis=1, tiled=True),
    )
    gate_up_mat = gate_up_all[0]
    down_mat = down_all[0]
    landed = lax.all_to_all(outgoing, "hd", split_axis=0, concat_axis=0, tiled=True)
    results = expert_rows(landed.reshape(-1, model_width), gate_up_mat, down_mat).reshape(landed.shape)
    returned = lax.all_to_all(results, "hd", split_axis=0, concat_axis=0, tiled=True)
    flat_returned = returned.reshape(-1, model_width)
    fetched = flat_returned[jnp.maximum(target, 0)]
    used_weight = jnp.where(member, weighting, 0.0)
    moe_total = jnp.sum(used_weight[:, :, None] * fetched.astype(jnp.float32), axis=1)
    layer_out = (residual.astype(jnp.float32) + moe_total).astype(jnp.bfloat16)
    return (layer_out, cache_after)


def solution(mesh):
    two_lanes = mesh.shape["hd"] == 2 and mesh.shape["grp"] % 8 == 0
    return jax.shard_map(
        two_lane_shards if two_lanes else shards,
        mesh=mesh,
        in_specs=(
            P(("grp", "hd"), None),
            P("grp"),
            P(),
            P(None, "hd"),
            P(None, "hd", None),
            P(None, "grp"),
            P(),
            P(),
            P("hd", "grp", None),
            P("hd", "grp", None),
            P(("grp", "hd"), None),
            P("grp"),
            P("grp", "hd", None),
        ),
        out_specs=(P(("grp", "hd"), None), P("grp", "hd", None)),
        check_vma=False,
    )
```

```python
import functools

import jax
import jax.numpy as jnp
import numpy as np
from jax import lax
from jax.experimental import pallas as pl
from jax.experimental.pallas import tpu as pltpu
from jax.sharding import PartitionSpec as P

norm_eps = 1e-05
rope_base = 10000.0
bf16 = jnp.bfloat16
f32 = jnp.float32
LAST_DIMS = (((1,), (1,)), ((), ()))


def ring_cycle(groups):
    rows = groups // 4
    return [2 * r for r in range(rows)] + [2 * r + 1 for r in reversed(range(rows))]


def ring_pairs(groups):
    cycle = ring_cycle(groups)
    count = len(cycle)
    pairs = []
    for place, pair in enumerate(cycle):
        pairs.append((2 * pair, 2 * cycle[(place + 1) % count]))
        pairs.append((2 * pair + 1, 2 * cycle[(place - 1) % count] + 1))
    return pairs


def sibling_pairs(groups):
    return [(g, g ^ 1) for g in range(groups)]


def ring_sources(groups, me):
    count = groups // 2
    rows = count // 2
    side, pair = me % 2, me // 2
    row, col = pair // 2, pair % 2
    place = jnp.where(col == 0, row, count - 1 - row)

    def block(core, steps):
        there = (place + (2 * core - 1) * steps + count) % count
        other = jnp.where(there < rows, 2 * there, 2 * (count - 1 - there) + 1)
        return [2 * other + core, 2 * other + 1 - core]

    full = (count - 1) // 2
    listed = [me, me + 1 - 2 * side]
    for core in (side, 1 - side):
        for steps in range(1, full + 1):
            listed += block(core, steps)
    return listed + [block(side, count // 2)[0], block(1 - side, count // 2)[0]]


class Ring:
    def __init__(self, pair, groups):
        self.across = functools.partial(lax.ppermute, axis_name="grp", perm=ring_pairs(groups))
        self.beside = functools.partial(lax.ppermute, axis_name="grp", perm=sibling_pairs(groups))
        self.full = (groups // 2 - 1) // 2
        self.unit_rows = pair.shape[0] // 2
        self.mine = [pair]
        self.near = []

    def step(self):
        held = self.mine[-1]
        if len(self.mine) > self.full:
            held = held[: self.unit_rows]
        self.mine.append(self.across(held))

    def pin(self, *others):
        done = lax.optimization_barrier((self.mine[-1],) + others)
        self.mine[-1] = done[0]
        return done[1:] if len(others) > 1 else done[1]

    def share(self, upto=None):
        for index in range(1 + len(self.near), 1 + (upto or len(self.mine) - 1)):
            self.near.append(self.beside(self.mine[index]))

    def parts(self):
        full = self.full
        return self.mine[: full + 1] + self.near[:full] + [self.mine[full + 1], self.near[full]]


def place_parts(groups, parts, unit_rows, pieces):
    sources = ring_sources(groups, lax.axis_index("grp"))
    shard = 0
    for part in parts:
        for unit in range(part.shape[0] // unit_rows):
            for first, rows, target, lane in pieces:
                at = pl.multiple_of(sources[shard] * rows, rows)
                start = unit * unit_rows + first
                target[pl.ds(at, rows), lane : lane + part.shape[1]] = part[start : start + rows, :]
            shard += 1


VMEM = pl.BlockSpec(memory_space=pltpu.VMEM)
ANY = pl.BlockSpec(memory_space=pl.ANY)
HBM = pl.BlockSpec(memory_space=pltpu.HBM)
PARAMS = pltpu.CompilerParams(vmem_limit_bytes=16 << 20)


LITTLE = pl.CostEstimate(flops=1, bytes_accessed=1, transcendentals=0)


def takes(us):
    return pl.CostEstimate(
        flops=int(us * 1.15e9), bytes_accessed=int(us * 8e6), transcendentals=0
    )


def reads(nbytes):
    return pl.CostEstimate(flops=1, bytes_accessed=nbytes, transcendentals=0)


def normalized(floats, gain):
    factor = lax.rsqrt(jnp.mean(floats * floats, axis=-1, keepdims=True) + norm_eps)
    return (floats * factor * gain).astype(bf16)


def fetch(pairs, sems):
    copies = []
    for index, (source, target) in enumerate(pairs):
        copies.append(pltpu.make_async_copy(source, target, sems.at[index]))
        copies[-1].start()
    return copies


def pack_kernel(*refs):
    sources, (expert_pair, out_pair, sems) = refs[:6], refs[6:]
    width = expert_pair.shape[1]
    lane = lax.axis_index("hd")
    first = pl.multiple_of(lane * out_pair.shape[1], out_pair.shape[1])
    pairs = []
    row = 0
    for index in range(2):
        up, down, w_out = sources[3 * index : 3 * index + 3]
        count = w_out.shape[0]
        pairs.append(
            (w_out.at[:, pl.ds(first, out_pair.shape[1])], out_pair.at[pl.ds(index * count, count), :])
        )
        for source in (up, down):
            for at in range(0, source.shape[1], width):
                pairs.append(
                    (source.at[:, pl.ds(at, width)], expert_pair.at[pl.ds(row, source.shape[0]), :])
                )
                row += source.shape[0]
    for copy in fetch(pairs, sems):
        copy.wait()


def pack(own, beside):
    own = [pltpu.with_memory_space_constraint(part, pltpu.HBM) for part in own]
    up, down, w_out_t = own
    width = up.shape[1] // 2
    pieces = [up.shape[1] // width, down.shape[1] // width]
    unit_rows = pieces[0] * up.shape[0] + pieces[1] * down.shape[0]
    return pl.pallas_call(
        pack_kernel,
        out_shape=(
            jax.ShapeDtypeStruct((2 * unit_rows, width), bf16),
            jax.ShapeDtypeStruct((2 * w_out_t.shape[0], w_out_t.shape[1] // 2), bf16),
        ),
        in_specs=[ANY] * 6,
        out_specs=(ANY, ANY),
        scratch_shapes=[pltpu.SemaphoreType.DMA((2 + 2 * sum(pieces),))],
        compiler_params=PARAMS,
        cost_estimate=LITTLE,
        name="pack",
    )(*own, *beside)


def as_column(row, eye):
    return jnp.sum(jnp.where(eye, row, 0.0), axis=1, keepdims=True)


def named_experts(ids, experts):
    tokens = ids.shape[1]
    expert = lax.broadcasted_iota(jnp.int32, (experts, tokens), 0)
    hit = jnp.zeros((experts, tokens), f32)
    for index in range(ids.shape[0]):
        hit = jnp.where(ids[index : index + 1, :] == expert, 1.0, hit)
    return hit


def prepare_kernel(groups, slots_dev, *refs):
    sources, (cosine, sine, past, place, send, tags, gain) = refs[:4], refs[4:11]
    positions, slots, ids, flat_gain, sems = refs[11:]
    copies = fetch(list(zip(sources, (positions, slots, ids, flat_gain))), sems)
    for copy in copies:
        copy.wait()
    gain[...] = flat_gain[...].reshape(gain.shape)
    lane = lax.axis_index("hd")
    block = positions.shape[1]

    def iota(shape, dim):
        return lax.broadcasted_iota(jnp.int32, shape, dim)

    eye = iota((block, block), 0) == iota((block, block), 1)
    reach = as_column(jnp.maximum(positions[...], 0).astype(f32), eye)
    past[...] = jnp.broadcast_to(reach, past.shape)
    column = iota((8, 128), 1)
    exponent = (column % 32).astype(f32) * (-2.0 / 64)
    inverse_freq = jnp.exp(exponent * np.float32(np.log(rope_base)))[:1, :]
    angles = reach * inverse_freq
    cosine[...] = jnp.cos(angles)
    turned = jnp.sin(angles)
    sine[...] = jnp.where(iota(angles.shape, 1) % 64 < 32, -turned, turned)

    tokens = ids.shape[1]
    cap = place.shape[0] // 2
    hit = named_experts(ids, 8)
    upto = (iota((tokens, tokens), 0) <= iota((tokens, tokens), 1)).astype(f32)
    rank = jnp.dot(hit, upto, preferred_element_type=f32) - 1.0
    slot = iota((2 * cap, tokens), 0).astype(f32)
    placed = jnp.zeros((2 * cap, tokens), f32)
    for live in range(2):
        order = jnp.where(lane == live, 0, cap).astype(f32)
        member = hit[live : live + 1, :] > 0.0
        placed = jnp.where(member & (slot == rank[live : live + 1, :] + order), 1.0, placed)
    place[...] = placed.astype(bf16)

    where = slots[...]
    owner = jnp.where(where >= 0, where // slots_dev, -1)
    owner_hit = (iota((groups, block), 0) == owner).astype(f32)
    before = (iota((block, block), 0) <= iota((block, block), 1)).astype(f32)
    running = jnp.dot(owner_hit, before, preferred_element_type=f32)
    owner_rank = jnp.sum(owner_hit * running, axis=0, keepdims=True) - 1.0
    capc = send.shape[0] // groups
    row = jnp.where(owner >= 0, owner * capc + owner_rank.astype(jnp.int32), -1)
    send[...] = (iota(send.shape, 0) == row).astype(bf16)
    inside = jnp.where(where >= 0, where % slots_dev, 0)
    high = as_column((inside // 64 + 1).astype(f32), eye)
    low = as_column((inside % 64).astype(f32), eye)
    spot = iota(tags.shape, 1)
    tags[...] = jnp.where(spot == 0, high, jnp.where(spot == 1, low, 0.0)).astype(bf16)


def prepare(groups, slots_dev, positions, slots, ids, gain):
    block, tokens = positions.shape[0], ids.shape[0]
    model = gain.shape[0]
    cap = tokens // 4
    capc = 2 * block // groups
    shapes = [
        ((block, 128), f32),
        ((block, 128), f32),
        ((block, 128), f32),
        ((2 * cap, tokens), bf16),
        ((groups * capc, block), bf16),
        ((block, 128), bf16),
        ((1, model), f32),
    ]
    sources = (positions[None], slots[None], ids.T, gain)
    return pl.pallas_call(
        functools.partial(prepare_kernel, groups, slots_dev),
        out_shape=tuple(jax.ShapeDtypeStruct(shape, kind) for shape, kind in shapes),
        in_specs=[ANY] * 4,
        out_specs=(VMEM,) * len(shapes),
        scratch_shapes=[
            pltpu.VMEM((1, block), jnp.int32),
            pltpu.VMEM((1, block), jnp.int32),
            pltpu.VMEM(ids.shape[::-1], jnp.int32),
            pltpu.VMEM((model,), f32),
            pltpu.SemaphoreType.DMA((4,)),
        ],
        compiler_params=PARAMS,
        cost_estimate=LITTLE,
        name="prepare",
    )(*[pltpu.with_memory_space_constraint(source, pltpu.HBM) for source in sources])


def project_kernel(
    own, other, gain, cosine, sine, w_query, w_keyval, q_out, kv_out, seam_out, raw, rows, sems
):
    count = own.shape[0]
    lane = lax.axis_index("hd")
    mine = pl.multiple_of(lane * count, count)
    theirs = pl.multiple_of((1 - lane) * count, count)
    copies = fetch([(own, raw.at[0]), (other, raw.at[1])], sems)
    cos_q, sin_q = cosine[...], sine[...]
    column = lax.broadcasted_iota(jnp.int32, cos_q.shape, 1)
    lower = column % 64 < 32
    cos_kv = jnp.where(column < 64, cos_q, 1.0)
    sin_kv = jnp.where(column < 64, sin_q, 0.0)
    for index, first in ((0, mine), (1, theirs)):
        copies[index].wait()
        rows[pl.ds(first, count), :] = normalized(raw[index].astype(f32), gain[...])
    width = 256
    for weights, out, cos, sin in ((w_keyval, kv_out, cos_kv, sin_kv), (w_query, q_out, cos_q, sin_q)):
        for first in range(0, weights.shape[1], width):
            made = jnp.dot(rows[...], weights[:, first : first + width], preferred_element_type=f32)
            for part in range(0, width, 128):
                here = made[:, part : part + 128]
                turned = jnp.where(lower, pltpu.roll(here, 96, 1), pltpu.roll(here, 32, 1))
                done = (here * cos + turned * sin).astype(bf16)
                out[:, first + part : first + part + 128] = done
                if out is kv_out:
                    seam_out[:, first + part : first + part + 128] = done[count:, :]


def project(own, other, gain, cosine, sine, w_query, flat_kv):
    count, width = own.shape
    made = w_query.shape[1] + flat_kv.shape[1]
    return pl.pallas_call(
        project_kernel,
        out_shape=(
            jax.ShapeDtypeStruct((2 * count, w_query.shape[1]), bf16),
            jax.ShapeDtypeStruct((2 * count, flat_kv.shape[1]), bf16),
            jax.ShapeDtypeStruct((count, flat_kv.shape[1]), bf16),
        ),
        in_specs=[ANY] * 2 + [VMEM] * 5,
        out_specs=(VMEM, VMEM, VMEM),
        scratch_shapes=[
            pltpu.VMEM((2, count, width), bf16),
            pltpu.VMEM((2 * count, width), bf16),
            pltpu.SemaphoreType.DMA((2,)),
        ],
        compiler_params=PARAMS,
        cost_estimate=takes(8),
        name="project",
    )(own, other, gain, cosine, sine, w_query, flat_kv)


def attend_rows_kernel(first, q, kv, seam, past, mixed, window, sem):
    count = q.shape[0] // 2
    if first == 0:
        copy = pltpu.make_async_copy(seam, window.at[pl.ds(0, count), :], sem)
        copy.start()
        window[count:, :] = kv[:count, :]
        copy.wait()
        keyed = window
    else:
        keyed = kv
    head = 64
    kv_heads = kv.shape[1] // (2 * head)
    per_kv = q.shape[1] // head // kv_heads
    shape = (count, 2 * count)
    row = lax.broadcasted_iota(jnp.int32, shape, 0) + count
    col = lax.broadcasted_iota(jnp.int32, shape, 1)
    reach = past[first : first + count, :1].astype(jnp.int32)
    visible = (col <= row) & (col >= row - reach)
    for kv_head in range(kv_heads):
        lanes = 2 * head * kv_head
        keys = keyed[:, lanes : lanes + head]
        values = keyed[:, lanes + head : lanes + 2 * head]
        for index in range(per_kv):
            at = (kv_head * per_kv + index) * head
            query = q[first : first + count, at : at + head]
            scores = lax.dot_general(query, keys, LAST_DIMS, preferred_element_type=f32)
            raised = jnp.where(visible, jnp.exp(scores * head ** (-0.5)), 0.0)
            probs = (raised / jnp.sum(raised, axis=-1, keepdims=True)).astype(bf16)
            made = jnp.dot(probs, values, preferred_element_type=f32)
            mixed[:, at : at + head] = made.astype(bf16)


def attend_late(q, kv, past):
    def kernel(q, kv, past, mixed):
        attend_rows_kernel(q.shape[0] // 2, q, kv, None, past, mixed, None, None)

    return pl.pallas_call(
        kernel,
        out_shape=jax.ShapeDtypeStruct((q.shape[0] // 2, q.shape[1]), bf16),
        in_specs=[VMEM] * 3,
        out_specs=VMEM,
        compiler_params=PARAMS,
        cost_estimate=takes(2),
        name="attend_late",
    )(q, kv, past)


def attend_early(q, kv, seam, past):
    return pl.pallas_call(
        functools.partial(attend_rows_kernel, 0),
        out_shape=jax.ShapeDtypeStruct((q.shape[0] // 2, q.shape[1]), bf16),
        in_specs=[VMEM, VMEM, ANY, VMEM],
        out_specs=VMEM,
        scratch_shapes=[pltpu.VMEM(kv.shape, bf16), pltpu.SemaphoreType.DMA],
        compiler_params=PARAMS,
        cost_estimate=takes(2),
        name="attend_early",
    )(q, kv, seam, past)


def outward_rows(flip, groups, unit_rows, early, late, parts, w_out, rows):
    place_parts(groups, parts, unit_rows, [(0, unit_rows, w_out, 0)])
    lane = lax.axis_index("hd")
    which = (1 - lane) if flip else lane

    @pl.when(which == 0)
    def _():
        rows[...] = early[...]

    @pl.when(which != 0)
    def _():
        rows[...] = late[...]

    return lax.dot_general(rows[...], w_out[...], LAST_DIMS, preferred_element_type=f32)


def send_kernel(groups, unit_rows, n_parts, early, late, *refs):
    parts, (out, w_out, rows) = refs[:n_parts], refs[n_parts:]
    out[...] = outward_rows(True, groups, unit_rows, early, late, parts, w_out, rows).astype(bf16)


def keep_kernel(groups, unit_rows, n_parts, early, late, tokens, flat_gain, *refs):
    parts, (out, gain, w_out, rows) = refs[:n_parts], refs[n_parts:]
    gain[...] = flat_gain[...].reshape(gain.shape)
    made = outward_rows(False, groups, unit_rows, early, late, parts, w_out, rows)
    out[...] = tokens[...].astype(f32) + made


def outward_send(groups, early, late, parts, unit_rows):
    width, depth = groups * unit_rows, parts[0].shape[1]
    return pl.pallas_call(
        functools.partial(send_kernel, groups, unit_rows, len(parts)),
        out_shape=jax.ShapeDtypeStruct((early.shape[0], width), bf16),
        in_specs=[VMEM] * (2 + len(parts)),
        out_specs=VMEM,
        scratch_shapes=[pltpu.VMEM((width, depth), bf16), pltpu.VMEM(early.shape, bf16)],
        compiler_params=PARAMS,
        cost_estimate=reads(2 * width * depth),
        name="outward_send",
    )(early, late, *parts)


def outward_keep(groups, early, late, tokens, gain, parts, unit_rows):
    width, depth = groups * unit_rows, parts[0].shape[1]
    return pl.pallas_call(
        functools.partial(keep_kernel, groups, unit_rows, len(parts)),
        out_shape=(
            jax.ShapeDtypeStruct(tokens.shape, f32),
            jax.ShapeDtypeStruct((1, width), f32),
        ),
        in_specs=[VMEM] * (4 + len(parts)),
        out_specs=(VMEM, VMEM),
        scratch_shapes=[
            pltpu.VMEM((width, depth), bf16),
            pltpu.VMEM(early.shape, bf16),
        ],
        compiler_params=PARAMS,
        cost_estimate=reads(2 * width * depth),
        name="outward_keep",
    )(early, late, tokens, gain, *parts)


def route_kernel(mine, arrived, gain, place, residual, moe_in, sent):
    added = (mine[...] + arrived[...].astype(f32)).astype(bf16)
    residual[...] = added
    moe_in[...] = normalized(added.astype(f32), gain[...])
    cap = sent.shape[0]
    rows = jnp.dot(place[cap:, :], moe_in[...], preferred_element_type=f32)
    sent[...] = rows.astype(bf16)


def route(mine, arrived, gain, place):
    cap = place.shape[0] // 2
    return pl.pallas_call(
        route_kernel,
        out_shape=(
            jax.ShapeDtypeStruct(mine.shape, bf16),
            jax.ShapeDtypeStruct(mine.shape, bf16),
            jax.ShapeDtypeStruct((cap, mine.shape[1]), bf16),
        ),
        in_specs=[VMEM] * 4,
        out_specs=(VMEM,) * 3,
        compiler_params=PARAMS,
        cost_estimate=reads(10 * mine.shape[0] * mine.shape[1]),
        name="route",
    )(mine, arrived, gain, place)


def gate_kernel(moe_in, router, ids, place, gates, own, spread):
    cap = own.shape[0]
    own[...] = jnp.dot(place[:cap, :], moe_in[...], preferred_element_type=f32).astype(bf16)
    hit = named_experts(ids, router.shape[0])
    tokens = ids.shape[1]
    row = lax.broadcasted_iota(jnp.int32, (tokens, tokens), 0)
    eye = (row == lax.broadcasted_iota(jnp.int32, (tokens, tokens), 1)).astype(f32)
    named = lax.dot_general(eye, hit, LAST_DIMS, preferred_element_type=f32)
    spread[...] = lax.dot_general(
        eye.astype(bf16), place[...], LAST_DIMS, preferred_element_type=f32
    ).astype(bf16)
    logits = lax.dot_general(moe_in[...], router[...], LAST_DIMS, preferred_element_type=f32)
    raised = jnp.where(named > 0, jnp.exp(logits), 0.0)
    gates[...] = raised / jnp.sum(raised, axis=-1, keepdims=True)


def gate(moe_in, router_t, ids_t, place):
    cap = place.shape[0] // 2
    return pl.pallas_call(
        gate_kernel,
        out_shape=(
            jax.ShapeDtypeStruct((moe_in.shape[0], router_t.shape[0]), f32),
            jax.ShapeDtypeStruct((cap, moe_in.shape[1]), bf16),
            jax.ShapeDtypeStruct(place.shape[::-1], bf16),
        ),
        in_specs=[VMEM] * 4,
        out_specs=(VMEM,) * 3,
        compiler_params=PARAMS,
        cost_estimate=LITTLE,
        name="gate",
    )(moe_in, router_t, ids_t, place)


def expert_kernel(groups, up_rows, down_rows, n_parts, own, other, *refs):
    parts = refs[:n_parts]
    own_out, other_out, rows, gate_up, down = refs[n_parts:]
    width = parts[0].shape[1]
    count = own.shape[0]
    rows[:count, :] = own[...]
    rows[count:, :] = other[...]
    pieces = [(i * up_rows, up_rows, gate_up, i * width) for i in range(2)]
    pieces += [
        (2 * up_rows + i * down_rows, down_rows, down, i * width) for i in range(down.shape[1] // width)
    ]
    unit_rows = pieces[-1][0] + down_rows
    place_parts(groups, parts, unit_rows, pieces)
    both = jnp.dot(rows[...], gate_up[...], preferred_element_type=f32)
    gate, up = both[:, :width], both[:, width:]
    hidden = (gate / (1.0 + jnp.exp(-gate)) * up).astype(bf16)
    made = jnp.dot(hidden, down[...], preferred_element_type=f32).astype(bf16)
    own_out[...] = made[:count, :]
    other_out[...] = made[count:, :]


def expert(groups, own, other, parts, up_rows, down_rows):
    count, model = own.shape
    width = parts[0].shape[1]
    return pl.pallas_call(
        functools.partial(expert_kernel, groups, up_rows, down_rows, len(parts)),
        out_shape=(jax.ShapeDtypeStruct(own.shape, bf16),) * 2,
        in_specs=[VMEM] * (2 + len(parts)),
        out_specs=(VMEM, VMEM),
        scratch_shapes=[
            pltpu.VMEM((2 * count, model), bf16),
            pltpu.VMEM((groups * up_rows, 2 * width), bf16),
            pltpu.VMEM((groups * down_rows, model), bf16),
        ],
        compiler_params=PARAMS,
        cost_estimate=takes(4.0),
        name="expert",
    )(own, other, *parts)


def combine_kernel(residual, gates, spread, own, returned, out):
    lane = lax.axis_index("hd")
    count = own.shape[0]
    column = lax.broadcasted_iota(jnp.int32, gates.shape, 1)
    total = jnp.zeros(residual.shape, f32)
    for index, made in ((0, own), (1, returned)):
        live = lane if index == 0 else 1 - lane
        weight = jnp.sum(jnp.where(column == live, gates[...], 0.0), axis=-1, keepdims=True)
        picked = jnp.dot(
            spread[:, index * count : (index + 1) * count], made[...], preferred_element_type=f32
        )
        total += weight * picked
    out[...] = (residual[...].astype(f32) + total).astype(bf16)


def combine(residual, gates, spread, own, returned):
    return pl.pallas_call(
        combine_kernel,
        out_shape=jax.ShapeDtypeStruct(residual.shape, bf16),
        in_specs=[VMEM] * 5,
        out_specs=VMEM,
        compiler_params=PARAMS,
        cost_estimate=reads(6 * residual.shape[0] * residual.shape[1]),
        name="combine",
    )(residual, gates, spread, own, returned)


def bundle_kernel(send, kv, tags, result, out, sem):
    groups, rows, _ = out.shape
    heads = kv.shape[1] // 128
    capc = send.shape[0] // groups
    packed = jnp.dot(send[...], kv[...], preferred_element_type=f32).astype(bf16)
    tagged = jnp.dot(send[...], tags[...], preferred_element_type=f32)
    one = (lax.broadcasted_iota(jnp.int32, (16, 128), 0) == lax.broadcasted_iota(jnp.int32, (16, 128), 1))
    for owner in range(groups):
        mine = slice(owner * capc, (owner + 1) * capc)
        for head in range(heads):
            out[owner, head * capc : (head + 1) * capc, :] = packed[mine, head * 128 : (head + 1) * 128]
        wide = jnp.concatenate([tagged[mine, :], jnp.zeros((128 - capc, 128), f32)], axis=0)
        out[owner, heads * capc :, :] = lax.dot_general(
            one.astype(f32), wide, LAST_DIMS, preferred_element_type=f32
        ).astype(bf16)
    copy = pltpu.make_async_copy(out, result, sem)
    copy.start()
    copy.wait()


def bundle(groups, send, kv, tags):
    rows = send.shape[0] // groups * (kv.shape[1] // 128) + 16
    return pl.pallas_call(
        bundle_kernel,
        out_shape=pltpu.HBM((groups, rows, 128), bf16),
        in_specs=[VMEM] * 3,
        out_specs=HBM,
        scratch_shapes=[pltpu.VMEM((groups, rows, 128), bf16), pltpu.SemaphoreType.DMA],
        compiler_params=PARAMS,
        cost_estimate=LITTLE,
        name="bundle",
    )(send, kv, tags)


def write_kernel(heads, arrived, cache, out, rows, wide, known):
    groups, size, _ = arrived.shape
    slots = cache.shape[0] // heads
    capc = (size - 16) // heads
    high, low = [], []
    for source in range(groups):
        for head in range(heads):
            rows[source * capc : (source + 1) * capc, head * 128 : (head + 1) * 128] = arrived[
                source, head * capc : (head + 1) * capc, :
            ]
        numbers = arrived[source, heads * capc :, :].astype(f32)
        high.append(numbers[0:1, :capc])
        low.append(numbers[1:2, :capc])
    slot = jnp.concatenate(high, axis=1) * 64.0 + jnp.concatenate(low, axis=1) - 64.0
    row = lax.broadcasted_iota(jnp.int32, (slots, slot.shape[1]), 0).astype(f32)
    hit = (row == slot).astype(bf16)
    made = jnp.dot(hit, rows[...], preferred_element_type=f32)
    found = jnp.dot(hit, jnp.ones((slot.shape[1], 128), bf16), preferred_element_type=f32)
    for head in range(heads):
        wide[pl.ds(head, slots, heads), :] = made[:, head * 128 : (head + 1) * 128]
        known[pl.ds(head, slots, heads), :] = found
    old = cache[...].astype(f32)
    out[...] = jnp.where(known[...] > 0.0, wide[...], old).astype(bf16)


def write(arrived, cache):
    slots, heads, lanes = cache.shape
    capc = (arrived.shape[1] - 16) // heads
    flat = (slots * heads, lanes)
    written = pl.pallas_call(
        functools.partial(write_kernel, heads),
        out_shape=jax.ShapeDtypeStruct(flat, bf16),
        in_specs=[VMEM] * 2,
        out_specs=VMEM,
        scratch_shapes=[
            pltpu.VMEM((arrived.shape[0] * capc, heads * lanes), bf16),
            pltpu.VMEM(flat, f32),
            pltpu.VMEM(flat, f32),
        ],
        compiler_params=PARAMS,
        cost_estimate=reads(1 << 21),
        name="write",
    )(arrived, cache.reshape(flat))
    return written.reshape(cache.shape)


def two_lane_shards(
    tokens,
    positions,
    attn_gain,
    w_query,
    w_keyval,
    w_out,
    moe_gain,
    router,
    w_gate_up,
    w_down,
    expert_ids,
    cache_slot,
    kv_cache,
):
    groups = lax.axis_size("grp")
    tok_rows, model = tokens.shape
    block = positions.shape[0]
    kv_local, head2 = w_keyval.shape[1:]
    kv_width = kv_local * head2
    slots_dev = kv_cache.shape[0]
    swap = functools.partial(lax.ppermute, axis_name="hd", perm=[(0, 1), (1, 0)])

    together = lax.optimization_barrier

    other_tokens = swap(tokens)
    own = (w_gate_up[0], w_down[0], w_out.T)
    up_rows, down_rows = own[0].shape[0], own[1].shape[0]
    beside = [lax.ppermute(part, "grp", sibling_pairs(groups)) for part in own]
    expert_pair, out_pair = pack(own, beside)
    out_ring = Ring(out_pair, groups)
    out_ring.step()
    expert_ring = Ring(expert_pair, groups)
    expert_ring.step()
    w_keyval, positions = together((w_keyval, positions, out_pair))[:2]
    flat_kv = w_keyval.reshape(model, kv_width)
    cosine, sine, past, place, send, tags, gain = prepare(
        groups, slots_dev, positions, cache_slot, expert_ids, attn_gain
    )
    other_tokens, cosine, flat_kv = out_ring.pin(other_tokens, cosine, flat_kv)
    out_ring.step()

    q, kv, tail = project(tokens, other_tokens, gain, cosine, sine, w_query, flat_kv)
    seam = lax.ppermute(tail, "grp", [(g, g + 1) for g in range(groups - 1)])
    q = out_ring.pin(q)
    out_ring.step()
    out_ring.share(2)
    late = attend_late(q, kv, past)
    seam, late = together((seam, late))
    seam = expert_ring.pin(seam)
    expert_ring.step()
    early = attend_early(q, kv, seam, past)
    early, out_ring.near = together((early, out_ring.near))
    early = out_ring.pin(early)
    out_ring.step()
    out_ring.share(3)
    early, kv, out_ring.near = together((early, kv, out_ring.near))
    outgoing = bundle(groups, send, kv, tags)
    early, outgoing = together((early, outgoing))
    early = out_ring.pin(early)
    early = expert_ring.pin(early)
    expert_ring.step()
    out_ring.share()
    sent = outward_send(groups, early, late, out_ring.parts(), out_ring.unit_rows)
    arrived = swap(sent)
    early = together((early, sent))[0]
    mine, late_gain = outward_keep(
        groups, early, late, tokens, moe_gain, out_ring.parts(), out_ring.unit_rows
    )
    late_gain = expert_ring.pin(late_gain)
    expert_ring.share()
    expert_ring.step()
    outgoing = together((outgoing, sent))[0]
    arrived_cache = lax.all_to_all(outgoing, "grp", split_axis=0, concat_axis=0, tiled=True)

    residual, moe_in, sent_rows = route(mine, arrived, late_gain, place)
    landed = swap(sent_rows)
    gates, own_rows, spread = gate(moe_in, router.T, expert_ids.T, place)
    landed, own_rows = expert_ring.pin(landed, own_rows)
    expert_ring.share()
    own_made, back = expert(
        groups, own_rows, landed, expert_ring.parts(), up_rows, down_rows
    )
    returned = swap(back)
    layer_out = combine(residual, gates, spread, own_made, returned)
    layer_out, arrived_cache = together((layer_out, arrived_cache))
    cache_after = write(arrived_cache, kv_cache)
    return (layer_out, cache_after)


def passed_along(value, axis, steps):
    count = lax.axis_size(axis)
    initial, last = (max(0, -steps), min(count, count - steps))
    return lax.ppermute(value, axis, [(source, source + steps) for source in range(initial, last)])


def rms_norm(row_set, norm_gain):
    floats = row_set.astype(jnp.float32)
    factor = lax.rsqrt(jnp.mean(floats * floats, axis=-1, keepdims=True) + norm_eps)
    return (floats * factor * norm_gain).astype(jnp.bfloat16)


def rotate(vectors, angle_pos):
    halves = vectors.shape[-1] // 2
    inverse_freq = rope_base ** (-2.0 * jnp.arange(halves, dtype=jnp.float32) / vectors.shape[-1])
    angles = angle_pos[:, None, None] * inverse_freq[None, None, :]
    cosine = jnp.cos(angles)
    sine_part = jnp.sin(angles)
    first_half = vectors[..., :halves]
    second_half = vectors[..., halves:]
    return jnp.concatenate(
        [
            first_half * cosine - second_half * sine_part,
            second_half * cosine + first_half * sine_part,
        ],
        axis=-1,
    )


def expert_rows(row_set, gate_up, down_rows):
    gate_and_up = jnp.dot(row_set, gate_up, preferred_element_type=jnp.float32)
    inner_width = gate_and_up.shape[1] // 2
    hidden = (jax.nn.silu(gate_and_up[:, :inner_width]) * gate_and_up[:, inner_width:]).astype(
        jnp.bfloat16
    )
    return jnp.dot(hidden, down_rows, preferred_element_type=jnp.float32).astype(jnp.bfloat16)


def attend_rows(query_blk, keys_blk, vals_blk, visible, scale_qk):
    scores = (
        jnp.einsum("qkgd,skd->kgqs", query_blk, keys_blk, preferred_element_type=jnp.float32)
        * scale_qk
    )
    weights_f = jnp.where(visible[None, None], jnp.exp(scores), 0.0)
    prob_bf = (weights_f / jnp.sum(weights_f, axis=-1, keepdims=True)).astype(jnp.bfloat16)
    return jnp.einsum("kgqs,skd->qkgd", prob_bf, vals_blk, preferred_element_type=jnp.float32)


def shards(
    tokens,
    positions,
    attn_gain,
    w_query,
    w_keyval,
    w_out,
    moe_gain,
    router,
    w_gate_up,
    w_down,
    expert_ids,
    cache_slot,
    kv_cache,
):
    lane_count = lax.axis_size("hd")
    group_count = lax.axis_size("grp")
    tok_rows = tokens.shape[0]
    model_width = tokens.shape[1]
    block_len = positions.shape[0]
    seg_most = block_len // 2
    head_dim = w_keyval.shape[2] // 2
    kv_local = w_keyval.shape[1]
    q_local = w_query.shape[1] // head_dim
    per_kv = q_local // kv_local
    expert_cap = tok_rows // 4
    normed = rms_norm(tokens, attn_gain)
    flat_kv = w_keyval.reshape(model_width, kv_local * 2 * head_dim)
    section = lax.all_gather(normed, "hd", axis=0, tiled=True)
    projected = jnp.concatenate(
        [
            jnp.dot(section, w_query, preferred_element_type=jnp.float32),
            jnp.dot(section, flat_kv, preferred_element_type=jnp.float32),
        ],
        axis=1,
    )
    angle_pos = jnp.maximum(positions, 0).astype(jnp.float32)
    queries = rotate(
        projected[:, : q_local * head_dim].reshape(block_len, q_local, head_dim), angle_pos
    ).astype(jnp.bfloat16)
    key_val = projected[:, q_local * head_dim :].reshape(block_len, kv_local, 2 * head_dim)
    rotated = rotate(key_val[:, :, :head_dim], angle_pos).astype(jnp.bfloat16)
    stored = jnp.concatenate([rotated, key_val[:, :, head_dim:].astype(jnp.bfloat16)], axis=2)
    seam_rows = passed_along(stored[block_len - seg_most :], "grp", 1)
    window = jnp.concatenate([seam_rows, stored], axis=0)
    scale_qk = head_dim ** (-0.5)
    local_rows = jnp.arange(block_len, dtype=jnp.int32)
    lowest = local_rows - jnp.maximum(positions, 0)
    pieces_out = []
    for q_block in range(2):
        first_row = q_block * seg_most
        rows_here = first_row + jnp.arange(seg_most, dtype=jnp.int32)
        cols_here = first_row - seg_most + jnp.arange(2 * seg_most, dtype=jnp.int32)
        low_here = lowest[first_row : first_row + seg_most]
        visible = (cols_here[None, :] >= low_here[:, None]) & (
            cols_here[None, :] <= rows_here[:, None]
        )
        query_blk = queries[first_row : first_row + seg_most].reshape(
            seg_most, kv_local, per_kv, head_dim
        )
        keys_blk = window[first_row : first_row + 2 * seg_most, :, :head_dim]
        vals_blk = window[first_row : first_row + 2 * seg_most, :, head_dim:]
        mixed_rows = attend_rows(query_blk, keys_blk, vals_blk, visible, scale_qk)
        pieces_out.append(mixed_rows.reshape(seg_most, q_local * head_dim).astype(jnp.bfloat16))
    attended = jnp.concatenate(pieces_out, axis=0)
    slots_dev = kv_cache.shape[0]
    capc = 2 * block_len // group_count
    live_slot = cache_slot >= 0
    owners = jnp.where(live_slot, cache_slot // slots_dev, group_count)
    owner_hit = (owners[:, None] == jnp.arange(group_count, dtype=jnp.int32)[None, :]).astype(
        jnp.bfloat16
    )
    lower_tri = (local_rows[:, None] >= local_rows[None, :]).astype(jnp.bfloat16)
    running = jnp.dot(lower_tri, owner_hit, preferred_element_type=jnp.float32)
    owner_rank = jnp.sum(running * owner_hit.astype(jnp.float32), axis=1).astype(jnp.int32) - 1
    send_rows = jnp.where(live_slot, owners * capc + owner_rank, group_count * capc)
    outgoing_cache = (
        jnp.zeros((group_count * capc, kv_local, 2 * head_dim), jnp.bfloat16)
        .at[send_rows]
        .set(stored, mode="drop")
    )
    outgoing_slots = (
        jnp.full((group_count * capc,), -1, jnp.int32)
        .at[send_rows]
        .set(cache_slot % slots_dev, mode="drop")
    )
    arrived, arrived_slots = (
        lax.all_to_all(
            outgoing_cache.reshape(group_count, capc, kv_local, 2 * head_dim),
            "grp",
            split_axis=0,
            concat_axis=0,
            tiled=True,
        ),
        lax.all_to_all(
            outgoing_slots.reshape(group_count, capc),
            "grp",
            split_axis=0,
            concat_axis=0,
            tiled=True,
        ),
    )
    flat_slots = arrived_slots.reshape(group_count * capc)
    write_rows = jnp.where(flat_slots >= 0, flat_slots, slots_dev).astype(jnp.int32)
    cache_after = kv_cache.at[write_rows].set(
        arrived.reshape(group_count * capc, kv_local, 2 * head_dim), mode="drop"
    )
    by_token = lax.all_to_all(attended, "hd", split_axis=0, concat_axis=1, tiled=True)
    attn_proj = jnp.dot(
        by_token,
        lax.all_gather(w_out, "grp", axis=1, tiled=True),
        preferred_element_type=jnp.float32,
    )
    residual = (tokens.astype(jnp.float32) + attn_proj).astype(jnp.bfloat16)
    moe_in = rms_norm(residual, moe_gain)
    logits = jnp.dot(moe_in, router, preferred_element_type=jnp.float32)
    expert_range = jnp.arange(router.shape[1], dtype=jnp.int32)
    matches_all = expert_ids[:, :, None] == expert_range[None, None, :]
    chosen = jnp.sum(jnp.where(matches_all, logits[:, None, :], 0.0), axis=2)
    raised = jnp.exp(chosen)
    gates = raised / jnp.sum(raised, axis=1, keepdims=True)
    live_range = jnp.arange(lane_count, dtype=jnp.int32)
    matches = expert_ids[:, :, None] == live_range[None, None, :]
    member = jnp.any(matches, axis=1)
    weighting = jnp.sum(jnp.where(matches, gates[:, :, None], 0.0), axis=1)
    ranking = jnp.cumsum(member.astype(jnp.int32), axis=0) - 1
    target = jnp.where(member, live_range[None, :] * expert_cap + ranking, -1)
    slot_range = jnp.arange(lane_count * expert_cap, dtype=jnp.int32)
    slot_hits = target[None, :, :] == slot_range[:, None, None]
    placing = jnp.any(slot_hits, axis=2).astype(jnp.bfloat16)
    outgoing = (
        jnp.dot(placing, moe_in, preferred_element_type=jnp.float32)
        .astype(jnp.bfloat16)
        .reshape(lane_count, expert_cap, model_width)
    )
    gate_up_all, down_all = (
        lax.all_gather(w_gate_up, "grp", axis=1, tiled=True),
        lax.all_gather(w_down, "grp", axis=1, tiled=True),
    )
    gate_up_mat = gate_up_all[0]
    down_mat = down_all[0]
    landed = lax.all_to_all(outgoing, "hd", split_axis=0, concat_axis=0, tiled=True)
    results = expert_rows(landed.reshape(-1, model_width), gate_up_mat, down_mat).reshape(landed.shape)
    returned = lax.all_to_all(results, "hd", split_axis=0, concat_axis=0, tiled=True)
    flat_returned = returned.reshape(-1, model_width)
    fetched = flat_returned[jnp.maximum(target, 0)]
    used_weight = jnp.where(member, weighting, 0.0)
    moe_total = jnp.sum(used_weight[:, :, None] * fetched.astype(jnp.float32), axis=1)
    layer_out = (residual.astype(jnp.float32) + moe_total).astype(jnp.bfloat16)
    return (layer_out, cache_after)


def solution(mesh):
    two_lanes = mesh.shape["hd"] == 2 and mesh.shape["grp"] % 8 == 0
    return jax.shard_map(
        two_lane_shards if two_lanes else shards,
        mesh=mesh,
        in_specs=(
            P(("grp", "hd"), None),
            P("grp"),
            P(),
            P(None, "hd"),
            P(None, "hd", None),
            P(None, "grp"),
            P(),
            P(),
            P("hd", "grp", None),
            P("hd", "grp", None),
            P(("grp", "hd"), None),
            P("grp"),
            P("grp", "hd", None),
        ),
        out_specs=(P(("grp", "hd"), None), P("grp", "hd", None)),
        check_vma=False,
    )
```

```python
import functools

import jax
import jax.numpy as jnp
import numpy as np
from jax import lax
from jax.experimental import pallas as pl
from jax.experimental.pallas import tpu as pltpu
from jax.sharding import PartitionSpec as P

norm_eps = 1e-05
rope_base = 10000.0
bf16 = jnp.bfloat16
f32 = jnp.float32
LAST_DIMS = (((1,), (1,)), ((), ()))


def ring_cycle(groups):
    rows = groups // 4
    return [2 * r for r in range(rows)] + [2 * r + 1 for r in reversed(range(rows))]


def ring_pairs(groups):
    cycle = ring_cycle(groups)
    count = len(cycle)
    pairs = []
    for place, pair in enumerate(cycle):
        pairs.append((2 * pair, 2 * cycle[(place + 1) % count]))
        pairs.append((2 * pair + 1, 2 * cycle[(place - 1) % count] + 1))
    return pairs


def sibling_pairs(groups):
    return [(g, g ^ 1) for g in range(groups)]


def ring_sources(groups, me):
    count = groups // 2
    rows = count // 2
    side, pair = me % 2, me // 2
    row, col = pair // 2, pair % 2
    place = jnp.where(col == 0, row, count - 1 - row)

    def block(core, steps):
        there = (place + (2 * core - 1) * steps + count) % count
        other = jnp.where(there < rows, 2 * there, 2 * (count - 1 - there) + 1)
        return [2 * other + core, 2 * other + 1 - core]

    full = (count - 1) // 2
    listed = [me, me + 1 - 2 * side]
    for core in (side, 1 - side):
        for steps in range(1, full + 1):
            listed += block(core, steps)
    return listed + [block(side, count // 2)[0], block(1 - side, count // 2)[0]]


class Ring:
    def __init__(self, pair, groups):
        self.across = functools.partial(lax.ppermute, axis_name="grp", perm=ring_pairs(groups))
        self.beside = functools.partial(lax.ppermute, axis_name="grp", perm=sibling_pairs(groups))
        self.full = (groups // 2 - 1) // 2
        self.unit_rows = pair.shape[0] // 2
        self.mine = [pair]
        self.near = []

    def step(self):
        held = self.mine[-1]
        if len(self.mine) > self.full:
            held = held[: self.unit_rows]
        self.mine.append(self.across(held))

    def pin(self, *others):
        done = lax.optimization_barrier((self.mine[-1],) + others)
        self.mine[-1] = done[0]
        return done[1:] if len(others) > 1 else done[1]

    def share(self, upto=None):
        for index in range(1 + len(self.near), 1 + (upto or len(self.mine) - 1)):
            self.near.append(self.beside(self.mine[index]))

    def parts(self):
        full = self.full
        return self.mine[: full + 1] + self.near[:full] + [self.mine[full + 1], self.near[full]]


def place_parts(groups, parts, unit_rows, pieces):
    sources = ring_sources(groups, lax.axis_index("grp"))
    shard = 0
    for part in parts:
        for unit in range(part.shape[0] // unit_rows):
            for first, rows, target, lane in pieces:
                at = pl.multiple_of(sources[shard] * rows, rows)
                start = unit * unit_rows + first
                target[pl.ds(at, rows), lane : lane + part.shape[1]] = part[start : start + rows, :]
            shard += 1


VMEM = pl.BlockSpec(memory_space=pltpu.VMEM)
ANY = pl.BlockSpec(memory_space=pl.ANY)
HBM = pl.BlockSpec(memory_space=pltpu.HBM)
PARAMS = pltpu.CompilerParams(vmem_limit_bytes=16 << 20)


LITTLE = pl.CostEstimate(flops=1, bytes_accessed=1, transcendentals=0)


def takes(us):
    return pl.CostEstimate(
        flops=int(us * 1.15e9), bytes_accessed=int(us * 8e6), transcendentals=0
    )


def reads(nbytes):
    return pl.CostEstimate(flops=1, bytes_accessed=nbytes, transcendentals=0)


def normalized(floats, gain):
    factor = lax.rsqrt(jnp.mean(floats * floats, axis=-1, keepdims=True) + norm_eps)
    return (floats * factor * gain).astype(bf16)


def fetch(pairs, sems):
    copies = []
    for index, (source, target) in enumerate(pairs):
        copies.append(pltpu.make_async_copy(source, target, sems.at[index]))
        copies[-1].start()
    return copies


def pack_kernel(*refs):
    sources, (expert_pair, out_pair, sems) = refs[:6], refs[6:]
    width = expert_pair.shape[1]
    lane = lax.axis_index("hd")
    first = pl.multiple_of(lane * out_pair.shape[1], out_pair.shape[1])
    pairs = []
    row = 0
    for index in range(2):
        up, down, w_out = sources[3 * index : 3 * index + 3]
        count = w_out.shape[0]
        pairs.append(
            (w_out.at[:, pl.ds(first, out_pair.shape[1])], out_pair.at[pl.ds(index * count, count), :])
        )
        for source in (up, down):
            for at in range(0, source.shape[1], width):
                pairs.append(
                    (source.at[:, pl.ds(at, width)], expert_pair.at[pl.ds(row, source.shape[0]), :])
                )
                row += source.shape[0]
    for copy in fetch(pairs, sems):
        copy.wait()


def pack(own, beside):
    own = [pltpu.with_memory_space_constraint(part, pltpu.HBM) for part in own]
    up, down, w_out_t = own
    width = up.shape[1] // 2
    pieces = [up.shape[1] // width, down.shape[1] // width]
    unit_rows = pieces[0] * up.shape[0] + pieces[1] * down.shape[0]
    return pl.pallas_call(
        pack_kernel,
        out_shape=(
            jax.ShapeDtypeStruct((2 * unit_rows, width), bf16),
            jax.ShapeDtypeStruct((2 * w_out_t.shape[0], w_out_t.shape[1] // 2), bf16),
        ),
        in_specs=[ANY] * 6,
        out_specs=(ANY, ANY),
        scratch_shapes=[pltpu.SemaphoreType.DMA((2 + 2 * sum(pieces),))],
        compiler_params=PARAMS,
        cost_estimate=LITTLE,
        name="pack",
    )(*own, *beside)


def as_column(row, eye):
    return jnp.sum(jnp.where(eye, row, 0.0), axis=1, keepdims=True)


def named_experts(ids, experts):
    tokens = ids.shape[1]
    expert = lax.broadcasted_iota(jnp.int32, (experts, tokens), 0)
    hit = jnp.zeros((experts, tokens), f32)
    for index in range(ids.shape[0]):
        hit = jnp.where(ids[index : index + 1, :] == expert, 1.0, hit)
    return hit


def prepare_kernel(groups, slots_dev, *refs):
    sources, (cosine, sine, past, place, send, tags, gain) = refs[:4], refs[4:11]
    positions, slots, ids, flat_gain, sems = refs[11:]
    copies = fetch(list(zip(sources, (positions, slots, ids, flat_gain))), sems)
    for copy in copies:
        copy.wait()
    gain[...] = flat_gain[...].reshape(gain.shape)
    lane = lax.axis_index("hd")
    block = positions.shape[1]

    def iota(shape, dim):
        return lax.broadcasted_iota(jnp.int32, shape, dim)

    eye = iota((block, block), 0) == iota((block, block), 1)
    reach = as_column(jnp.maximum(positions[...], 0).astype(f32), eye)
    past[...] = jnp.broadcast_to(reach, past.shape)
    column = iota((8, 128), 1)
    exponent = (column % 32).astype(f32) * (-2.0 / 64)
    inverse_freq = jnp.exp(exponent * np.float32(np.log(rope_base)))[:1, :]
    angles = reach * inverse_freq
    cosine[...] = jnp.cos(angles)
    turned = jnp.sin(angles)
    sine[...] = jnp.where(iota(angles.shape, 1) % 64 < 32, -turned, turned)

    tokens = ids.shape[1]
    cap = place.shape[0] // 2
    hit = named_experts(ids, 8)
    upto = (iota((tokens, tokens), 0) <= iota((tokens, tokens), 1)).astype(f32)
    rank = jnp.dot(hit, upto, preferred_element_type=f32) - 1.0
    slot = iota((2 * cap, tokens), 0).astype(f32)
    placed = jnp.zeros((2 * cap, tokens), f32)
    for live in range(2):
        order = jnp.where(lane == live, 0, cap).astype(f32)
        member = hit[live : live + 1, :] > 0.0
        placed = jnp.where(member & (slot == rank[live : live + 1, :] + order), 1.0, placed)
    place[...] = placed.astype(bf16)

    where = slots[...]
    owner = jnp.where(where >= 0, where // slots_dev, -1)
    owner_hit = (iota((groups, block), 0) == owner).astype(f32)
    before = (iota((block, block), 0) <= iota((block, block), 1)).astype(f32)
    running = jnp.dot(owner_hit, before, preferred_element_type=f32)
    owner_rank = jnp.sum(owner_hit * running, axis=0, keepdims=True) - 1.0
    capc = send.shape[0] // groups
    row = jnp.where(owner >= 0, owner * capc + owner_rank.astype(jnp.int32), -1)
    send[...] = (iota(send.shape, 0) == row).astype(bf16)
    inside = jnp.where(where >= 0, where % slots_dev, 0)
    high = as_column((inside // 64 + 1).astype(f32), eye)
    low = as_column((inside % 64).astype(f32), eye)
    spot = iota(tags.shape, 1)
    tags[...] = jnp.where(spot == 0, high, jnp.where(spot == 1, low, 0.0)).astype(bf16)


def prepare(groups, slots_dev, positions, slots, ids, gain):
    block, tokens = positions.shape[0], ids.shape[0]
    model = gain.shape[0]
    cap = tokens // 4
    capc = 2 * block // groups
    shapes = [
        ((block, 128), f32),
        ((block, 128), f32),
        ((block, 128), f32),
        ((2 * cap, tokens), bf16),
        ((groups * capc, block), bf16),
        ((block, 128), bf16),
        ((1, model), f32),
    ]
    sources = (positions[None], slots[None], ids.T, gain)
    return pl.pallas_call(
        functools.partial(prepare_kernel, groups, slots_dev),
        out_shape=tuple(jax.ShapeDtypeStruct(shape, kind) for shape, kind in shapes),
        in_specs=[ANY] * 4,
        out_specs=(VMEM,) * len(shapes),
        scratch_shapes=[
            pltpu.VMEM((1, block), jnp.int32),
            pltpu.VMEM((1, block), jnp.int32),
            pltpu.VMEM(ids.shape[::-1], jnp.int32),
            pltpu.VMEM((model,), f32),
            pltpu.SemaphoreType.DMA((4,)),
        ],
        compiler_params=PARAMS,
        cost_estimate=LITTLE,
        name="prepare",
    )(*[pltpu.with_memory_space_constraint(source, pltpu.HBM) for source in sources])


def project_kernel(
    own, other, gain, cosine, sine, w_query, w_keyval, q_out, kv_out, seam_out, raw, rows, sems
):
    count = own.shape[0]
    lane = lax.axis_index("hd")
    mine = pl.multiple_of(lane * count, count)
    theirs = pl.multiple_of((1 - lane) * count, count)
    copies = fetch([(own, raw.at[0]), (other, raw.at[1])], sems)
    cos_q, sin_q = cosine[...], sine[...]
    column = lax.broadcasted_iota(jnp.int32, cos_q.shape, 1)
    lower = column % 64 < 32
    cos_kv = jnp.where(column < 64, cos_q, 1.0)
    sin_kv = jnp.where(column < 64, sin_q, 0.0)
    for index, first in ((0, mine), (1, theirs)):
        copies[index].wait()
        rows[pl.ds(first, count), :] = normalized(raw[index].astype(f32), gain[...])
    width = 256
    for weights, out, cos, sin in ((w_keyval, kv_out, cos_kv, sin_kv), (w_query, q_out, cos_q, sin_q)):
        for first in range(0, weights.shape[1], width):
            made = jnp.dot(rows[...], weights[:, first : first + width], preferred_element_type=f32)
            for part in range(0, width, 128):
                here = made[:, part : part + 128]
                turned = jnp.where(lower, pltpu.roll(here, 96, 1), pltpu.roll(here, 32, 1))
                done = (here * cos + turned * sin).astype(bf16)
                out[:, first + part : first + part + 128] = done
                if out is kv_out:
                    seam_out[:, first + part : first + part + 128] = done[count:, :]


def project(own, other, gain, cosine, sine, w_query, flat_kv):
    count, width = own.shape
    made = w_query.shape[1] + flat_kv.shape[1]
    return pl.pallas_call(
        project_kernel,
        out_shape=(
            jax.ShapeDtypeStruct((2 * count, w_query.shape[1]), bf16),
            jax.ShapeDtypeStruct((2 * count, flat_kv.shape[1]), bf16),
            jax.ShapeDtypeStruct((count, flat_kv.shape[1]), bf16),
        ),
        in_specs=[ANY] * 2 + [VMEM] * 5,
        out_specs=(VMEM, VMEM, VMEM),
        scratch_shapes=[
            pltpu.VMEM((2, count, width), bf16),
            pltpu.VMEM((2 * count, width), bf16),
            pltpu.SemaphoreType.DMA((2,)),
        ],
        compiler_params=PARAMS,
        cost_estimate=takes(8),
        name="project",
    )(own, other, gain, cosine, sine, w_query, flat_kv)


def attend_rows_kernel(first, q, kv, seam, past, mixed, window, sem):
    count = q.shape[0] // 2
    if first == 0:
        copy = pltpu.make_async_copy(seam, window.at[pl.ds(0, count), :], sem)
        copy.start()
        window[count:, :] = kv[:count, :]
        copy.wait()
        keyed = window
    else:
        keyed = kv
    head = 64
    kv_heads = kv.shape[1] // (2 * head)
    per_kv = q.shape[1] // head // kv_heads
    shape = (count, 2 * count)
    row = lax.broadcasted_iota(jnp.int32, shape, 0) + count
    col = lax.broadcasted_iota(jnp.int32, shape, 1)
    reach = past[first : first + count, :1].astype(jnp.int32)
    visible = (col <= row) & (col >= row - reach)
    for kv_head in range(kv_heads):
        lanes = 2 * head * kv_head
        keys = keyed[:, lanes : lanes + head]
        values = keyed[:, lanes + head : lanes + 2 * head]
        for index in range(per_kv):
            at = (kv_head * per_kv + index) * head
            query = q[first : first + count, at : at + head]
            scores = lax.dot_general(query, keys, LAST_DIMS, preferred_element_type=f32)
            raised = jnp.where(visible, jnp.exp(scores * head ** (-0.5)), 0.0)
            probs = (raised / jnp.sum(raised, axis=-1, keepdims=True)).astype(bf16)
            made = jnp.dot(probs, values, preferred_element_type=f32)
            mixed[:, at : at + head] = made.astype(bf16)


def attend_late(q, kv, past):
    def kernel(q, kv, past, mixed):
        attend_rows_kernel(q.shape[0] // 2, q, kv, None, past, mixed, None, None)

    return pl.pallas_call(
        kernel,
        out_shape=jax.ShapeDtypeStruct((q.shape[0] // 2, q.shape[1]), bf16),
        in_specs=[VMEM] * 3,
        out_specs=VMEM,
        compiler_params=PARAMS,
        cost_estimate=takes(2),
        name="attend_late",
    )(q, kv, past)


def attend_early(q, kv, seam, past):
    return pl.pallas_call(
        functools.partial(attend_rows_kernel, 0),
        out_shape=jax.ShapeDtypeStruct((q.shape[0] // 2, q.shape[1]), bf16),
        in_specs=[VMEM, VMEM, ANY, VMEM],
        out_specs=VMEM,
        scratch_shapes=[pltpu.VMEM(kv.shape, bf16), pltpu.SemaphoreType.DMA],
        compiler_params=PARAMS,
        cost_estimate=takes(2),
        name="attend_early",
    )(q, kv, seam, past)


def outward_rows(flip, groups, unit_rows, early, late, parts, w_out, rows):
    place_parts(groups, parts, unit_rows, [(0, unit_rows, w_out, 0)])
    lane = lax.axis_index("hd")
    which = (1 - lane) if flip else lane

    @pl.when(which == 0)
    def _():
        rows[...] = early[...]

    @pl.when(which != 0)
    def _():
        rows[...] = late[...]

    return lax.dot_general(rows[...], w_out[...], LAST_DIMS, preferred_element_type=f32)


def send_kernel(groups, unit_rows, n_parts, early, late, *refs):
    parts, (out, w_out, rows) = refs[:n_parts], refs[n_parts:]
    out[...] = outward_rows(True, groups, unit_rows, early, late, parts, w_out, rows).astype(bf16)


def keep_kernel(groups, unit_rows, n_parts, early, late, tokens, flat_gain, *refs):
    parts, (out, gain, w_out, rows) = refs[:n_parts], refs[n_parts:]
    gain[...] = flat_gain[...].reshape(gain.shape)
    made = outward_rows(False, groups, unit_rows, early, late, parts, w_out, rows)
    out[...] = tokens[...].astype(f32) + made


def outward_send(groups, early, late, parts, unit_rows):
    width, depth = groups * unit_rows, parts[0].shape[1]
    return pl.pallas_call(
        functools.partial(send_kernel, groups, unit_rows, len(parts)),
        out_shape=jax.ShapeDtypeStruct((early.shape[0], width), bf16),
        in_specs=[VMEM] * (2 + len(parts)),
        out_specs=VMEM,
        scratch_shapes=[pltpu.VMEM((width, depth), bf16), pltpu.VMEM(early.shape, bf16)],
        compiler_params=PARAMS,
        cost_estimate=reads(2 * width * depth),
        name="outward_send",
    )(early, late, *parts)


def outward_keep(groups, early, late, tokens, gain, parts, unit_rows):
    width, depth = groups * unit_rows, parts[0].shape[1]
    return pl.pallas_call(
        functools.partial(keep_kernel, groups, unit_rows, len(parts)),
        out_shape=(
            jax.ShapeDtypeStruct(tokens.shape, f32),
            jax.ShapeDtypeStruct((1, width), f32),
        ),
        in_specs=[VMEM] * (4 + len(parts)),
        out_specs=(VMEM, VMEM),
        scratch_shapes=[
            pltpu.VMEM((width, depth), bf16),
            pltpu.VMEM(early.shape, bf16),
        ],
        compiler_params=PARAMS,
        cost_estimate=reads(2 * width * depth),
        name="outward_keep",
    )(early, late, tokens, gain, *parts)


def route_kernel(mine, arrived, gain, place, residual, moe_in, sent):
    added = (mine[...] + arrived[...].astype(f32)).astype(bf16)
    residual[...] = added
    moe_in[...] = normalized(added.astype(f32), gain[...])
    cap = sent.shape[0]
    rows = jnp.dot(place[cap:, :], moe_in[...], preferred_element_type=f32)
    sent[...] = rows.astype(bf16)


def route(mine, arrived, gain, place):
    cap = place.shape[0] // 2
    return pl.pallas_call(
        route_kernel,
        out_shape=(
            jax.ShapeDtypeStruct(mine.shape, bf16),
            jax.ShapeDtypeStruct(mine.shape, bf16),
            jax.ShapeDtypeStruct((cap, mine.shape[1]), bf16),
        ),
        in_specs=[VMEM] * 4,
        out_specs=(VMEM,) * 3,
        compiler_params=PARAMS,
        cost_estimate=reads(10 * mine.shape[0] * mine.shape[1]),
        name="route",
    )(mine, arrived, gain, place)


def gate_kernel(moe_in, router, ids, place, gates, own, spread):
    cap = own.shape[0]
    own[...] = jnp.dot(place[:cap, :], moe_in[...], preferred_element_type=f32).astype(bf16)
    hit = named_experts(ids, router.shape[0])
    tokens = ids.shape[1]
    row = lax.broadcasted_iota(jnp.int32, (tokens, tokens), 0)
    eye = (row == lax.broadcasted_iota(jnp.int32, (tokens, tokens), 1)).astype(f32)
    named = lax.dot_general(eye, hit, LAST_DIMS, preferred_element_type=f32)
    spread[...] = lax.dot_general(
        eye.astype(bf16), place[...], LAST_DIMS, preferred_element_type=f32
    ).astype(bf16)
    logits = lax.dot_general(moe_in[...], router[...], LAST_DIMS, preferred_element_type=f32)
    raised = jnp.where(named > 0, jnp.exp(logits), 0.0)
    gates[...] = raised / jnp.sum(raised, axis=-1, keepdims=True)


def gate(moe_in, router_t, ids_t, place):
    cap = place.shape[0] // 2
    return pl.pallas_call(
        gate_kernel,
        out_shape=(
            jax.ShapeDtypeStruct((moe_in.shape[0], router_t.shape[0]), f32),
            jax.ShapeDtypeStruct((cap, moe_in.shape[1]), bf16),
            jax.ShapeDtypeStruct(place.shape[::-1], bf16),
        ),
        in_specs=[VMEM] * 4,
        out_specs=(VMEM,) * 3,
        compiler_params=PARAMS,
        cost_estimate=LITTLE,
        name="gate",
    )(moe_in, router_t, ids_t, place)


def expert_kernel(groups, up_rows, down_rows, n_parts, own, other, *refs):
    parts = refs[:n_parts]
    own_out, other_out, rows, gate_up, down = refs[n_parts:]
    width = parts[0].shape[1]
    count = own.shape[0]
    rows[:count, :] = own[...]
    rows[count:, :] = other[...]
    pieces = [(i * up_rows, up_rows, gate_up, i * width) for i in range(2)]
    pieces += [
        (2 * up_rows + i * down_rows, down_rows, down, i * width) for i in range(down.shape[1] // width)
    ]
    unit_rows = pieces[-1][0] + down_rows
    place_parts(groups, parts, unit_rows, pieces)
    both = jnp.dot(rows[...], gate_up[...], preferred_element_type=f32)
    gate, up = both[:, :width], both[:, width:]
    hidden = (gate / (1.0 + jnp.exp(-gate)) * up).astype(bf16)
    made = jnp.dot(hidden, down[...], preferred_element_type=f32).astype(bf16)
    own_out[...] = made[:count, :]
    other_out[...] = made[count:, :]


def expert(groups, own, other, parts, up_rows, down_rows):
    count, model = own.shape
    width = parts[0].shape[1]
    return pl.pallas_call(
        functools.partial(expert_kernel, groups, up_rows, down_rows, len(parts)),
        out_shape=(jax.ShapeDtypeStruct(own.shape, bf16),) * 2,
        in_specs=[VMEM] * (2 + len(parts)),
        out_specs=(VMEM, VMEM),
        scratch_shapes=[
            pltpu.VMEM((2 * count, model), bf16),
            pltpu.VMEM((groups * up_rows, 2 * width), bf16),
            pltpu.VMEM((groups * down_rows, model), bf16),
        ],
        compiler_params=PARAMS,
        cost_estimate=takes(2.6),
        name="expert",
    )(own, other, *parts)


def combine_kernel(residual, gates, spread, own, returned, out):
    lane = lax.axis_index("hd")
    count = own.shape[0]
    column = lax.broadcasted_iota(jnp.int32, gates.shape, 1)
    total = jnp.zeros(residual.shape, f32)
    for index, made in ((0, own), (1, returned)):
        live = lane if index == 0 else 1 - lane
        weight = jnp.sum(jnp.where(column == live, gates[...], 0.0), axis=-1, keepdims=True)
        picked = jnp.dot(
            spread[:, index * count : (index + 1) * count], made[...], preferred_element_type=f32
        )
        total += weight * picked
    out[...] = (residual[...].astype(f32) + total).astype(bf16)


def combine(residual, gates, spread, own, returned):
    return pl.pallas_call(
        combine_kernel,
        out_shape=jax.ShapeDtypeStruct(residual.shape, bf16),
        in_specs=[VMEM] * 5,
        out_specs=VMEM,
        compiler_params=PARAMS,
        cost_estimate=reads(6 * residual.shape[0] * residual.shape[1]),
        name="combine",
    )(residual, gates, spread, own, returned)


def bundle_kernel(send, kv, tags, result, out, sem):
    groups, rows, _ = out.shape
    heads = kv.shape[1] // 128
    capc = send.shape[0] // groups
    packed = jnp.dot(send[...], kv[...], preferred_element_type=f32).astype(bf16)
    tagged = jnp.dot(send[...], tags[...], preferred_element_type=f32)
    one = (lax.broadcasted_iota(jnp.int32, (16, 128), 0) == lax.broadcasted_iota(jnp.int32, (16, 128), 1))
    for owner in range(groups):
        mine = slice(owner * capc, (owner + 1) * capc)
        for head in range(heads):
            out[owner, head * capc : (head + 1) * capc, :] = packed[mine, head * 128 : (head + 1) * 128]
        wide = jnp.concatenate([tagged[mine, :], jnp.zeros((128 - capc, 128), f32)], axis=0)
        out[owner, heads * capc :, :] = lax.dot_general(
            one.astype(f32), wide, LAST_DIMS, preferred_element_type=f32
        ).astype(bf16)
    copy = pltpu.make_async_copy(out, result, sem)
    copy.start()
    copy.wait()


def bundle(groups, send, kv, tags):
    rows = send.shape[0] // groups * (kv.shape[1] // 128) + 16
    return pl.pallas_call(
        bundle_kernel,
        out_shape=pltpu.HBM((groups, rows, 128), bf16),
        in_specs=[VMEM] * 3,
        out_specs=HBM,
        scratch_shapes=[pltpu.VMEM((groups, rows, 128), bf16), pltpu.SemaphoreType.DMA],
        compiler_params=PARAMS,
        cost_estimate=LITTLE,
        name="bundle",
    )(send, kv, tags)


def write_kernel(heads, arrived, cache, out, rows, wide, known):
    groups, size, _ = arrived.shape
    slots = cache.shape[0] // heads
    capc = (size - 16) // heads
    high, low = [], []
    for source in range(groups):
        for head in range(heads):
            rows[source * capc : (source + 1) * capc, head * 128 : (head + 1) * 128] = arrived[
                source, head * capc : (head + 1) * capc, :
            ]
        numbers = arrived[source, heads * capc :, :].astype(f32)
        high.append(numbers[0:1, :capc])
        low.append(numbers[1:2, :capc])
    slot = jnp.concatenate(high, axis=1) * 64.0 + jnp.concatenate(low, axis=1) - 64.0
    row = lax.broadcasted_iota(jnp.int32, (slots, slot.shape[1]), 0).astype(f32)
    hit = (row == slot).astype(bf16)
    made = jnp.dot(hit, rows[...], preferred_element_type=f32)
    found = jnp.dot(hit, jnp.ones((slot.shape[1], 128), bf16), preferred_element_type=f32)
    for head in range(heads):
        wide[pl.ds(head, slots, heads), :] = made[:, head * 128 : (head + 1) * 128]
        known[pl.ds(head, slots, heads), :] = found
    old = cache[...].astype(f32)
    out[...] = jnp.where(known[...] > 0.0, wide[...], old).astype(bf16)


def write(arrived, cache):
    slots, heads, lanes = cache.shape
    capc = (arrived.shape[1] - 16) // heads
    flat = (slots * heads, lanes)
    written = pl.pallas_call(
        functools.partial(write_kernel, heads),
        out_shape=jax.ShapeDtypeStruct(flat, bf16),
        in_specs=[VMEM] * 2,
        out_specs=VMEM,
        scratch_shapes=[
            pltpu.VMEM((arrived.shape[0] * capc, heads * lanes), bf16),
            pltpu.VMEM(flat, f32),
            pltpu.VMEM(flat, f32),
        ],
        compiler_params=PARAMS,
        cost_estimate=reads(1 << 21),
        name="write",
    )(arrived, cache.reshape(flat))
    return written.reshape(cache.shape)


def two_lane_shards(
    tokens,
    positions,
    attn_gain,
    w_query,
    w_keyval,
    w_out,
    moe_gain,
    router,
    w_gate_up,
    w_down,
    expert_ids,
    cache_slot,
    kv_cache,
):
    groups = lax.axis_size("grp")
    tok_rows, model = tokens.shape
    block = positions.shape[0]
    kv_local, head2 = w_keyval.shape[1:]
    kv_width = kv_local * head2
    slots_dev = kv_cache.shape[0]
    swap = functools.partial(lax.ppermute, axis_name="hd", perm=[(0, 1), (1, 0)])

    together = lax.optimization_barrier

    other_tokens = swap(tokens)
    own = (w_gate_up[0], w_down[0], w_out.T)
    up_rows, down_rows = own[0].shape[0], own[1].shape[0]
    beside = [lax.ppermute(part, "grp", sibling_pairs(groups)) for part in own]
    expert_pair, out_pair = pack(own, beside)
    out_ring = Ring(out_pair, groups)
    out_ring.step()
    expert_ring = Ring(expert_pair, groups)
    expert_ring.step()
    w_keyval, positions = together((w_keyval, positions, out_pair))[:2]
    flat_kv = w_keyval.reshape(model, kv_width)
    cosine, sine, past, place, send, tags, gain = prepare(
        groups, slots_dev, positions, cache_slot, expert_ids, attn_gain
    )
    other_tokens, cosine, flat_kv = out_ring.pin(other_tokens, cosine, flat_kv)
    out_ring.step()

    q, kv, tail = project(tokens, other_tokens, gain, cosine, sine, w_query, flat_kv)
    seam = lax.ppermute(tail, "grp", [(g, g + 1) for g in range(groups - 1)])
    q = out_ring.pin(q)
    out_ring.step()
    out_ring.share(2)
    late = attend_late(q, kv, past)
    seam, late = together((seam, late))
    seam = expert_ring.pin(seam)
    expert_ring.step()
    early = attend_early(q, kv, seam, past)
    early, out_ring.near = together((early, out_ring.near))
    early = out_ring.pin(early)
    out_ring.step()
    out_ring.share(3)
    early, kv, out_ring.near = together((early, kv, out_ring.near))
    outgoing = bundle(groups, send, kv, tags)
    early, outgoing = together((early, outgoing))
    early = out_ring.pin(early)
    early = expert_ring.pin(early)
    expert_ring.step()
    out_ring.share()
    sent = outward_send(groups, early, late, out_ring.parts(), out_ring.unit_rows)
    arrived = swap(sent)
    early = together((early, sent))[0]
    mine, late_gain = outward_keep(
        groups, early, late, tokens, moe_gain, out_ring.parts(), out_ring.unit_rows
    )
    late_gain = expert_ring.pin(late_gain)
    expert_ring.share()
    expert_ring.step()
    outgoing = together((outgoing, sent))[0]
    arrived_cache = lax.all_to_all(outgoing, "grp", split_axis=0, concat_axis=0, tiled=True)

    residual, moe_in, sent_rows = route(mine, arrived, late_gain, place)
    landed = swap(sent_rows)
    gates, own_rows, spread = gate(moe_in, router.T, expert_ids.T, place)
    own_rows = expert_ring.pin(own_rows)
    expert_ring.share()
    landed, own_rows = together((landed, own_rows))
    own_made, back = expert(
        groups, own_rows, landed, expert_ring.parts(), up_rows, down_rows
    )
    returned = swap(back)
    layer_out = combine(residual, gates, spread, own_made, returned)
    layer_out, arrived_cache = together((layer_out, arrived_cache))
    cache_after = write(arrived_cache, kv_cache)
    return (layer_out, cache_after)


def passed_along(value, axis, steps):
    count = lax.axis_size(axis)
    initial, last = (max(0, -steps), min(count, count - steps))
    return lax.ppermute(value, axis, [(source, source + steps) for source in range(initial, last)])


def rms_norm(row_set, norm_gain):
    floats = row_set.astype(jnp.float32)
    factor = lax.rsqrt(jnp.mean(floats * floats, axis=-1, keepdims=True) + norm_eps)
    return (floats * factor * norm_gain).astype(jnp.bfloat16)


def rotate(vectors, angle_pos):
    halves = vectors.shape[-1] // 2
    inverse_freq = rope_base ** (-2.0 * jnp.arange(halves, dtype=jnp.float32) / vectors.shape[-1])
    angles = angle_pos[:, None, None] * inverse_freq[None, None, :]
    cosine = jnp.cos(angles)
    sine_part = jnp.sin(angles)
    first_half = vectors[..., :halves]
    second_half = vectors[..., halves:]
    return jnp.concatenate(
        [
            first_half * cosine - second_half * sine_part,
            second_half * cosine + first_half * sine_part,
        ],
        axis=-1,
    )


def expert_rows(row_set, gate_up, down_rows):
    gate_and_up = jnp.dot(row_set, gate_up, preferred_element_type=jnp.float32)
    inner_width = gate_and_up.shape[1] // 2
    hidden = (jax.nn.silu(gate_and_up[:, :inner_width]) * gate_and_up[:, inner_width:]).astype(
        jnp.bfloat16
    )
    return jnp.dot(hidden, down_rows, preferred_element_type=jnp.float32).astype(jnp.bfloat16)


def attend_rows(query_blk, keys_blk, vals_blk, visible, scale_qk):
    scores = (
        jnp.einsum("qkgd,skd->kgqs", query_blk, keys_blk, preferred_element_type=jnp.float32)
        * scale_qk
    )
    weights_f = jnp.where(visible[None, None], jnp.exp(scores), 0.0)
    prob_bf = (weights_f / jnp.sum(weights_f, axis=-1, keepdims=True)).astype(jnp.bfloat16)
    return jnp.einsum("kgqs,skd->qkgd", prob_bf, vals_blk, preferred_element_type=jnp.float32)


def shards(
    tokens,
    positions,
    attn_gain,
    w_query,
    w_keyval,
    w_out,
    moe_gain,
    router,
    w_gate_up,
    w_down,
    expert_ids,
    cache_slot,
    kv_cache,
):
    lane_count = lax.axis_size("hd")
    group_count = lax.axis_size("grp")
    tok_rows = tokens.shape[0]
    model_width = tokens.shape[1]
    block_len = positions.shape[0]
    seg_most = block_len // 2
    head_dim = w_keyval.shape[2] // 2
    kv_local = w_keyval.shape[1]
    q_local = w_query.shape[1] // head_dim
    per_kv = q_local // kv_local
    expert_cap = tok_rows // 4
    normed = rms_norm(tokens, attn_gain)
    flat_kv = w_keyval.reshape(model_width, kv_local * 2 * head_dim)
    section = lax.all_gather(normed, "hd", axis=0, tiled=True)
    projected = jnp.concatenate(
        [
            jnp.dot(section, w_query, preferred_element_type=jnp.float32),
            jnp.dot(section, flat_kv, preferred_element_type=jnp.float32),
        ],
        axis=1,
    )
    angle_pos = jnp.maximum(positions, 0).astype(jnp.float32)
    queries = rotate(
        projected[:, : q_local * head_dim].reshape(block_len, q_local, head_dim), angle_pos
    ).astype(jnp.bfloat16)
    key_val = projected[:, q_local * head_dim :].reshape(block_len, kv_local, 2 * head_dim)
    rotated = rotate(key_val[:, :, :head_dim], angle_pos).astype(jnp.bfloat16)
    stored = jnp.concatenate([rotated, key_val[:, :, head_dim:].astype(jnp.bfloat16)], axis=2)
    seam_rows = passed_along(stored[block_len - seg_most :], "grp", 1)
    window = jnp.concatenate([seam_rows, stored], axis=0)
    scale_qk = head_dim ** (-0.5)
    local_rows = jnp.arange(block_len, dtype=jnp.int32)
    lowest = local_rows - jnp.maximum(positions, 0)
    pieces_out = []
    for q_block in range(2):
        first_row = q_block * seg_most
        rows_here = first_row + jnp.arange(seg_most, dtype=jnp.int32)
        cols_here = first_row - seg_most + jnp.arange(2 * seg_most, dtype=jnp.int32)
        low_here = lowest[first_row : first_row + seg_most]
        visible = (cols_here[None, :] >= low_here[:, None]) & (
            cols_here[None, :] <= rows_here[:, None]
        )
        query_blk = queries[first_row : first_row + seg_most].reshape(
            seg_most, kv_local, per_kv, head_dim
        )
        keys_blk = window[first_row : first_row + 2 * seg_most, :, :head_dim]
        vals_blk = window[first_row : first_row + 2 * seg_most, :, head_dim:]
        mixed_rows = attend_rows(query_blk, keys_blk, vals_blk, visible, scale_qk)
        pieces_out.append(mixed_rows.reshape(seg_most, q_local * head_dim).astype(jnp.bfloat16))
    attended = jnp.concatenate(pieces_out, axis=0)
    slots_dev = kv_cache.shape[0]
    capc = 2 * block_len // group_count
    live_slot = cache_slot >= 0
    owners = jnp.where(live_slot, cache_slot // slots_dev, group_count)
    owner_hit = (owners[:, None] == jnp.arange(group_count, dtype=jnp.int32)[None, :]).astype(
        jnp.bfloat16
    )
    lower_tri = (local_rows[:, None] >= local_rows[None, :]).astype(jnp.bfloat16)
    running = jnp.dot(lower_tri, owner_hit, preferred_element_type=jnp.float32)
    owner_rank = jnp.sum(running * owner_hit.astype(jnp.float32), axis=1).astype(jnp.int32) - 1
    send_rows = jnp.where(live_slot, owners * capc + owner_rank, group_count * capc)
    outgoing_cache = (
        jnp.zeros((group_count * capc, kv_local, 2 * head_dim), jnp.bfloat16)
        .at[send_rows]
        .set(stored, mode="drop")
    )
    outgoing_slots = (
        jnp.full((group_count * capc,), -1, jnp.int32)
        .at[send_rows]
        .set(cache_slot % slots_dev, mode="drop")
    )
    arrived, arrived_slots = (
        lax.all_to_all(
            outgoing_cache.reshape(group_count, capc, kv_local, 2 * head_dim),
            "grp",
            split_axis=0,
            concat_axis=0,
            tiled=True,
        ),
        lax.all_to_all(
            outgoing_slots.reshape(group_count, capc),
            "grp",
            split_axis=0,
            concat_axis=0,
            tiled=True,
        ),
    )
    flat_slots = arrived_slots.reshape(group_count * capc)
    write_rows = jnp.where(flat_slots >= 0, flat_slots, slots_dev).astype(jnp.int32)
    cache_after = kv_cache.at[write_rows].set(
        arrived.reshape(group_count * capc, kv_local, 2 * head_dim), mode="drop"
    )
    by_token = lax.all_to_all(attended, "hd", split_axis=0, concat_axis=1, tiled=True)
    attn_proj = jnp.dot(
        by_token,
        lax.all_gather(w_out, "grp", axis=1, tiled=True),
        preferred_element_type=jnp.float32,
    )
    residual = (tokens.astype(jnp.float32) + attn_proj).astype(jnp.bfloat16)
    moe_in = rms_norm(residual, moe_gain)
    logits = jnp.dot(moe_in, router, preferred_element_type=jnp.float32)
    expert_range = jnp.arange(router.shape[1], dtype=jnp.int32)
    matches_all = expert_ids[:, :, None] == expert_range[None, None, :]
    chosen = jnp.sum(jnp.where(matches_all, logits[:, None, :], 0.0), axis=2)
    raised = jnp.exp(chosen)
    gates = raised / jnp.sum(raised, axis=1, keepdims=True)
    live_range = jnp.arange(lane_count, dtype=jnp.int32)
    matches = expert_ids[:, :, None] == live_range[None, None, :]
    member = jnp.any(matches, axis=1)
    weighting = jnp.sum(jnp.where(matches, gates[:, :, None], 0.0), axis=1)
    ranking = jnp.cumsum(member.astype(jnp.int32), axis=0) - 1
    target = jnp.where(member, live_range[None, :] * expert_cap + ranking, -1)
    slot_range = jnp.arange(lane_count * expert_cap, dtype=jnp.int32)
    slot_hits = target[None, :, :] == slot_range[:, None, None]
    placing = jnp.any(slot_hits, axis=2).astype(jnp.bfloat16)
    outgoing = (
        jnp.dot(placing, moe_in, preferred_element_type=jnp.float32)
        .astype(jnp.bfloat16)
        .reshape(lane_count, expert_cap, model_width)
    )
    gate_up_all, down_all = (
        lax.all_gather(w_gate_up, "grp", axis=1, tiled=True),
        lax.all_gather(w_down, "grp", axis=1, tiled=True),
    )
    gate_up_mat = gate_up_all[0]
    down_mat = down_all[0]
    landed = lax.all_to_all(outgoing, "hd", split_axis=0, concat_axis=0, tiled=True)
    results = expert_rows(landed.reshape(-1, model_width), gate_up_mat, down_mat).reshape(landed.shape)
    returned = lax.all_to_all(results, "hd", split_axis=0, concat_axis=0, tiled=True)
    flat_returned = returned.reshape(-1, model_width)
    fetched = flat_returned[jnp.maximum(target, 0)]
    used_weight = jnp.where(member, weighting, 0.0)
    moe_total = jnp.sum(used_weight[:, :, None] * fetched.astype(jnp.float32), axis=1)
    layer_out = (residual.astype(jnp.float32) + moe_total).astype(jnp.bfloat16)
    return (layer_out, cache_after)


def solution(mesh):
    two_lanes = mesh.shape["hd"] == 2 and mesh.shape["grp"] % 8 == 0
    return jax.shard_map(
        two_lane_shards if two_lanes else shards,
        mesh=mesh,
        in_specs=(
            P(("grp", "hd"), None),
            P("grp"),
            P(),
            P(None, "hd"),
            P(None, "hd", None),
            P(None, "grp"),
            P(),
            P(),
            P("hd", "grp", None),
            P("hd", "grp", None),
            P(("grp", "hd"), None),
            P("grp"),
            P("grp", "hd", None),
        ),
        out_specs=(P(("grp", "hd"), None), P("grp", "hd", None)),
        check_vma=False,
    )
```
